32 devices in a mesh: chan: 4 (over x, core), tm: 8 (over z, y).
Axes of the slice: x: 2, y: 2, z: 4, core: 2. Of those that a mesh axis runs over, the one named last changes fastest.
Arguments:
- ref_signal: float32 [2, 16384], P(None, 'tm'), may hold values from -40 to 40
- surveillance: float32 [2, 256, 16384], P(None, 'chan', 'tm'), may hold values from -2000 to 2000
- steering: float32 [2, 64, 256], P(None, None, 'chan'), may hold values from -0.5 to 0.5
Outputs:
- range_doppler: float32 [64, 2, 256, 256], P('chan', None, 'tm')
The draws below stay inside these ranges and needn't reach their ends.
All inputs are finite; a program needn't handle non-finite values.
Results may differ from the reference program's by a relative error of at most 0.0003.
Values sent between devices are 32-bit elements; how exact they have to be, the bound alone decides.
No kernel may reach another device: no remote copies, remote signals or barrier semaphores. Data moves between devices by JAX's collectives and lax.ppermute only.
A program may use at most 64 MiB of HBM per device.

```python
import math
import jax
import jax.numpy as jnp
from jax import lax

CHANNELS = 256
BEAMS = 64
LAGS = 256
DOPPLER = 256
TAPS = 64
BLOCK_LEN = 256
SAMPLES = 16384


def make_signals(key):
    base_key = jax.random.fold_in(key, 4242)
    keys = jax.random.split(base_key, 5)
    base = jnp.clip(jax.random.normal(keys[0], (2, SAMPLES), jnp.float32), -5.0, 5.0) * math.sqrt(0.5)
    fades = jnp.exp(jax.random.uniform(keys[1], (SAMPLES // 32,), jnp.float32, 0.0, math.log(3.2)))
    fading = jnp.repeat(fades, 32)
    ramp = jnp.arange(SAMPLES, dtype=jnp.float32) / SAMPLES
    trend = 1.0 + 0.75 * ramp
    ref_signal = base * fading * trend
    reach = max(TAPS // 4, 1)
    clutter_taps = jnp.clip(jax.random.normal(keys[2], (2, CHANNELS, reach), jnp.float32), -4.0, 4.0) * (1.5 / math.sqrt(reach))
    clutter_real = jnp.zeros((CHANNELS, SAMPLES), jnp.float32)
    clutter_imag = jnp.zeros((CHANNELS, SAMPLES), jnp.float32)
    for delay in range(reach):
        shifted = jnp.pad(ref_signal, ((0, 0), (delay, 0)))[:, :SAMPLES]
        tap_real = clutter_taps[0, :, delay:delay + 1]
        tap_imag = clutter_taps[1, :, delay:delay + 1]
        clutter_real = clutter_real + tap_real * shifted[0][None, :] - tap_imag * shifted[1][None, :]
        clutter_imag = clutter_imag + tap_real * shifted[1][None, :] + tap_imag * shifted[0][None, :]
    levels = jnp.exp(jax.random.uniform(keys[3], (CHANNELS, 1), jnp.float32, 0.0, math.log(3.2)))
    noise = jnp.clip(jax.random.normal(keys[4], (2, CHANNELS, SAMPLES), jnp.float32), -5.0, 5.0) * math.sqrt(0.5)
    surveillance = jnp.stack([clutter_real, clutter_imag], 0) + noise * levels[None, :, :]
    return (ref_signal, surveillance)


def draw_ref_signal(key, part):
    return make_signals(key)[0]


def draw_surveillance(key, part):
    return make_signals(key)[1]


def spiked(result, stream_key, source, target, blocks, factor):
    def block_of(dim):
        return (jnp.arange(result.shape[dim]) // (result.shape[dim] // blocks)).reshape((-1,) + (1,) * (result.ndim - 1 - dim))

    near = jax.random.permutation(stream_key, blocks)[block_of(target)]
    other_side = (block_of(target) + blocks // 2) % blocks
    return jnp.where((block_of(source) == near) | (block_of(source) == other_side), factor * result, result)


def block_levels(rng, dims, shards, smallest, high):
    def one(position, blocks):
        steps = jax.random.uniform(jax.random.fold_in(jax.random.fold_in(rng, 6), position), (blocks,), jnp.float32, smallest / len(shards), high / len(shards))
        return jnp.repeat(jnp.exp(steps), dims[position] // blocks).reshape((-1,) + (1,) * (len(dims) - position - 1))

    level = one(*shards[0])
    for cut in shards[1:]:
        level = level * one(*cut)
    return level


def noise_with(rng, extent, spread, bound, cuts, heavy, kind=jnp.bfloat16):
    array = spread * jax.random.normal(rng, extent, jnp.float32)
    if cuts:
        array = array * block_levels(rng, extent, cuts, -0.22, 0.18)
    return jnp.clip(spiked(array, jax.random.fold_in(rng, 3), *heavy), -bound, bound).astype(kind)


def setup_inputs(seed: int = 0) -> dict:
    streams_of = jax.random.split(jax.random.key(seed), 4)
    return {
        "ref_signal": draw_ref_signal(jax.random.fold_in(streams_of[3], 71), 0),
        "surveillance": draw_surveillance(jax.random.fold_in(streams_of[3], 71), 0),
        "steering": noise_with(streams_of[2], (2, BEAMS, CHANNELS), CHANNELS ** -0.5, 0.5, ((2, 4),), (2, 1, 4, 2.0), jnp.float32),
    }


def lag_window(ref_ext, offset):
    window = lax.dynamic_slice_in_dim(ref_ext, offset, BLOCK_LEN + LAGS, 1)
    positions = (jnp.arange(BLOCK_LEN)[None, :] - jnp.arange(LAGS)[:, None] + LAGS).astype(jnp.int32)
    return window[:, positions]

def reference(ref_signal, surveillance, steering):
    highest = lax.Precision.HIGHEST
    blocks_all = SAMPLES // BLOCK_LEN
    ref_ext = jnp.concatenate([jnp.zeros((2, LAGS), jnp.float32), ref_signal], axis=1)
    survey = surveillance.reshape(2 * CHANNELS, SAMPLES)
    block_ids = jnp.arange(blocks_all, dtype=jnp.int32)

    def statistics(carry, block_idx):
        offset = (block_idx * BLOCK_LEN).astype(jnp.int32)
        basis = lag_window(ref_ext, offset)[:, :TAPS, :].reshape(2 * TAPS, BLOCK_LEN)
        portion = lax.dynamic_slice_in_dim(survey, offset, BLOCK_LEN, 1)
        gram_sum = carry[0] + jnp.dot(basis, basis.T, precision=highest)
        cross_sum = carry[1] + jnp.dot(basis, portion.T, precision=highest)
        return ((gram_sum, cross_sum), None)
    start_carry = (jnp.zeros((2 * TAPS, 2 * TAPS), jnp.float32), jnp.zeros((2 * TAPS, 2 * CHANNELS), jnp.float32))
    (gram_sum, cross_sum), _ = lax.scan(statistics, start_carry, block_ids)
    g_real = gram_sum[:TAPS, :TAPS] + gram_sum[TAPS:, TAPS:]
    g_imag = gram_sum[:TAPS, TAPS:] - gram_sum[TAPS:, :TAPS]
    system = jnp.concatenate([jnp.concatenate([g_real, -g_imag], 1), jnp.concatenate([g_imag, g_real], 1)], 0)
    b_real = cross_sum[:TAPS, :CHANNELS] + cross_sum[TAPS:, CHANNELS:]
    b_imag = cross_sum[:TAPS, CHANNELS:] - cross_sum[TAPS:, :CHANNELS]
    solved = jnp.linalg.solve(system, jnp.concatenate([b_real, b_imag], 0))
    a_real = solved[:TAPS].T
    a_imag = solved[TAPS:].T
    mixing = jnp.concatenate([jnp.concatenate([a_real, -a_imag], 1), jnp.concatenate([a_imag, a_real], 1)], 0)

    def cleanse(carry, block_idx):
        offset = (block_idx * BLOCK_LEN).astype(jnp.int32)
        basis = lag_window(ref_ext, offset)[:, :TAPS, :].reshape(2 * TAPS, BLOCK_LEN)
        portion = lax.dynamic_slice_in_dim(survey, offset, BLOCK_LEN, 1)
        return (carry, portion - jnp.dot(mixing, basis, precision=highest))
    _, cleaned_blocks = lax.scan(cleanse, None, block_ids)
    cleaned = cleaned_blocks.transpose(1, 0, 2).reshape(2 * CHANNELS, SAMPLES)
    w_real = steering[0]
    w_imag = steering[1]
    w_big = jnp.concatenate([jnp.concatenate([w_real, -w_imag], 1), jnp.concatenate([w_imag, w_real], 1)], 0)
    beams = jnp.dot(w_big, cleaned, precision=highest)

    def correlate(carry, block_idx):
        offset = (block_idx * BLOCK_LEN).astype(jnp.int32)
        lag_rows = lag_window(ref_ext, offset).reshape(2 * LAGS, BLOCK_LEN)
        segment = lax.dynamic_slice_in_dim(beams, offset, BLOCK_LEN, 1)
        product = jnp.dot(segment, lag_rows.T, precision=highest).reshape(2, BEAMS, 2, LAGS)
        real_part = product[0, :, 0] + product[1, :, 1]
        imag_part = product[1, :, 0] - product[0, :, 1]
        return (carry, jnp.stack([real_part, imag_part], 0))
    _, lagged = lax.scan(correlate, None, block_ids)
    spectrum = jnp.fft.fft(lax.complex(lagged[:, 0], lagged[:, 1]), n=DOPPLER, axis=0)
    stacked = jnp.stack([jnp.real(spectrum), jnp.imag(spectrum)], 0)
    scale = 0.125 / math.sqrt(SAMPLES)
    return stacked.transpose(2, 0, 3, 1) * scale
```

```python
import functools
import math

import jax
import jax.numpy as jnp
import numpy as np
from jax import lax
from jax.experimental import pallas as pl
from jax.experimental.pallas import tpu as pltpu
from jax.sharding import PartitionSpec as P

LAGS = 256
DOPPLER = 256
TAPS = 64
BLOCK_LEN = 256
LANES = 128
SUBLANES = 8

HIGHEST = lax.Precision.HIGHEST
VMEM_BYTES = 48 * 1024 * 1024


def params():
    return pltpu.CompilerParams(vmem_limit_bytes=VMEM_BYTES)


def halves(x):
    high = x.astype(jnp.bfloat16)
    return high, (x - high.astype(jnp.float32)).astype(jnp.bfloat16)


def dot_nt(a, b, precision=None):
    return lax.dot_general(
        a, b, (((1,), (1,)), ((), ())), precision=precision, preferred_element_type=jnp.float32
    )


def row_sign(shape):
    rows = lax.broadcasted_iota(jnp.int32, shape, 0)
    return jnp.where(rows % SUBLANES < SUBLANES // 2, 1.0, -1.0).astype(jnp.float32)


def lane_sign(shape):
    lanes = lax.broadcasted_iota(jnp.int32, shape, 1)
    return jnp.where(lanes % LANES < LANES // 2, 1.0, -1.0).astype(jnp.float32)


def swap_groups(rows, groups):
    width = LANES // groups
    lane_group = lax.broadcasted_iota(jnp.int32, rows[0].shape, 1) // width
    outs = []
    for j in range(groups):
        out = rows[j]
        for i in range(groups):
            if i != j:
                moved = pltpu.roll(rows[i], (width * (i - j)) % LANES, 1)
                out = jnp.where(lane_group == i, moved, out)
        outs.append(out)
    return outs


def beam_kernel(chan_count, beams_local, w_ref, s_ref, even_ref, odd_ref):
    me = lax.axis_index("chan")
    half = SUBLANES // 2
    sub = lax.broadcasted_iota(jnp.int32, (SUBLANES, w_ref.shape[2]), 0)
    top = sub < half
    parts = []
    for parity in range(2):
        rows = []
        for e in range(parity, chan_count, 2):
            base = (me ^ e) * beams_local
            for tile in range(beams_local // SUBLANES):
                start = pl.multiple_of(base + tile * SUBLANES, SUBLANES)
                wr = w_ref[0, pl.ds(start, SUBLANES), :]
                wi = w_ref[1, pl.ds(start, SUBLANES), :]
                wr_s = pltpu.roll(wr, half, 0)
                wi_s = pltpu.roll(wi, half, 0)
                first = [jnp.where(top, wr, wi_s), jnp.where(top, -wi, wr_s)]
                second = [jnp.where(top, wr_s, wi), jnp.where(top, -wi_s, wr)]
                rows.append(jnp.concatenate(first, 1))
                rows.append(jnp.concatenate(second, 1))
        parts.append(jnp.concatenate(rows, 0))
    weights = jnp.concatenate(parts, 0)
    product = jnp.dot(
        weights, s_ref[...], precision=HIGHEST, preferred_element_type=jnp.float32
    )
    mid = product.shape[0] // 2
    even_ref[...] = product[:mid]
    odd_ref[...] = product[mid:]


def beam_call(steering, survey, chan_count, beams_local):
    depth, length = survey.shape
    rows = chan_count * beams_local
    steps = 4
    width = length // steps
    out = jax.ShapeDtypeStruct((rows, length), jnp.float32)
    return pl.pallas_call(
        functools.partial(beam_kernel, chan_count, beams_local),
        grid=(steps,),
        in_specs=[
            pl.BlockSpec(steering.shape, lambda i: (0, 0, 0)),
            pl.BlockSpec((depth, width), lambda i: (0, i)),
        ],
        out_specs=[pl.BlockSpec((rows, width), lambda i: (0, i))] * 2,
        out_shape=[out, out],
        compiler_params=params(),
        cost_estimate=pl.CostEstimate(
            flops=4 * rows * depth * length, bytes_accessed=4 * length * (depth + 2 * rows), transcendentals=0
        ),
        name="beams",
    )(steering, survey)


def table_kernel(ref_ref, out_ref):
    me = lax.axis_index("tm")
    length = ref_ref.shape[2]
    before = jnp.maximum(me - 1, 0)
    edge = ref_ref[before, :, length - 2 * LANES :]
    edge = jnp.where(me > 0, edge, jnp.zeros_like(edge))
    span = jnp.concatenate([edge, ref_ref[me]], 1)
    for c in range(2):
        tiled = jnp.broadcast_to(span[c : c + 1], (LANES, span.shape[1]))
        shifted = pltpu.roll(tiled, 0, 1, stride=1, stride_axis=0)[:, LANES:]
        high, low = halves(shifted)
        out_ref[0, c] = high
        out_ref[1, c] = low


def table_call(ref_all):
    length = ref_all.shape[2]
    shape = (2, 2, LANES, LANES + length)
    return pl.pallas_call(
        table_kernel,
        out_shape=jax.ShapeDtypeStruct(shape, jnp.bfloat16),
        compiler_params=params(),
        cost_estimate=pl.CostEstimate(
            flops=8 * math.prod(shape), bytes_accessed=2 * math.prod(shape), transcendentals=0
        ),
        name="shifted_reference",
    )(ref_all)


def lag_kernel(groups, owners, *refs):
    *y_refs, table_ref, out_ref = refs
    y = y_refs[0][...]
    for y_ref in y_refs[1:]:
        y = y + y_ref[...]
    rows, length = y.shape
    blocks = length // BLOCK_LEN
    turned = jnp.concatenate(
        [pltpu.roll(y[r : r + SUBLANES], SUBLANES // 2, 0) for r in range(0, rows, SUBLANES)], 0
    )
    turned = turned * row_sign(turned.shape)
    y_high, y_low = halves(y)
    t_high, t_low = halves(turned)
    both = jnp.concatenate([y_high, y_low], 0)
    turned_both = jnp.concatenate([t_high, t_low], 0)
    taps_sum = None
    for q in range(blocks):
        near = slice(q * BLOCK_LEN + LANES, q * BLOCK_LEN + LANES + BLOCK_LEN)
        far = slice(q * BLOCK_LEN, (q + 1) * BLOCK_LEN)
        cols = slice(q * BLOCK_LEN, (q + 1) * BLOCK_LEN)
        tables = []
        for h in range(2):
            tables.append(
                jnp.concatenate(
                    [
                        jnp.concatenate([table_ref[h, 0, :, near], table_ref[h, 1, :, near]], 1),
                        jnp.concatenate([table_ref[h, 0, :, far], table_ref[h, 1, :, far]], 1),
                    ],
                    0,
                )
            )
        lhs = jnp.concatenate([both[:, cols], turned_both[:, cols]], 1)
        by_high = dot_nt(lhs, tables[0])
        by_low = dot_nt(lhs[:rows], tables[1])
        product = by_high[:rows] + (by_high[rows:] + by_low)
        taps = product[:, :LANES]
        taps_sum = taps if taps_sum is None else taps_sum + taps
        for h in range(LAGS // LANES):
            lanes = slice(h * LANES, (h + 1) * LANES)
            tiles = [product[r : r + SUBLANES, lanes] for r in range(0, rows, SUBLANES)]
            for j, tile in enumerate(swap_groups(tiles, groups)):
                out_ref[h * groups + j, q] = tile
    left = lax.broadcasted_iota(jnp.int32, (SUBLANES, LANES), 1) < TAPS
    packed = []
    for i in range(groups // 2):
        a = taps_sum[i * SUBLANES : (i + 1) * SUBLANES]
        other = i + groups // 2
        b = taps_sum[other * SUBLANES : (other + 1) * SUBLANES]
        packed.append(jnp.where(left, a, pltpu.roll(b, LANES - TAPS, 1)))
    for owner in range(owners):
        for i, tile in enumerate(packed):
            out_ref[owner, blocks + i] = tile


def lag_call(ys, table, groups, owners):
    rows, length = ys[0].shape
    blocks = length // BLOCK_LEN
    shape = (owners, blocks + groups // 2, SUBLANES, LANES)
    return pl.pallas_call(
        functools.partial(lag_kernel, groups, owners),
        out_shape=jax.ShapeDtypeStruct(shape, jnp.float32),
        compiler_params=params(),
        cost_estimate=pl.CostEstimate(
            flops=12 * rows * LAGS * 2 * length,
            bytes_accessed=4 * math.prod(shape) + 2 * math.prod(table.shape),
            transcendentals=0,
        ),
        name="lag_products",
    )(*ys, table)


def complex_inverse(a):
    size = a.shape[0]
    lanes = lax.broadcasted_iota(jnp.int32, (1, 2 * size), 1)
    rows = lax.broadcasted_iota(jnp.int32, (size, 1), 0)
    all_lanes = lax.broadcasted_iota(jnp.int32, a.shape, 1)
    all_rows = lax.broadcasted_iota(jnp.int32, a.shape, 0)
    sign = -lane_sign((1, 2 * size))
    for j in range(size):
        col_r = a[:, j : j + 1]
        col_i = a[:, size + j : size + j + 1]
        row = a[j : j + 1]
        pivot = 1.0 / a[j : j + 1, j : j + 1]
        row = jnp.where(lanes == j, 1.0, jnp.where(lanes == size + j, 0.0, row))
        turned = pltpu.roll(row, size, 1) * sign
        row = row * pivot
        turned = turned * pivot
        col_r = jnp.where(rows == j, 0.0, col_r)
        col_i = jnp.where(rows == j, 0.0, col_i)
        kept = jnp.where((all_lanes == j) | (all_lanes == size + j), 0.0, a)
        kept = jnp.where(all_rows == j, row, kept)
        a = kept - (col_r * row + col_i * turned)
    return a


def own_kernel(lags_local, ref_ref, out_ref, span_ref, late_ref):
    owners, _, length = ref_ref.shape
    samples = owners * length
    blocks = samples // BLOCK_LEN
    first_lag = lax.axis_index("tm") * lags_local
    span_ref[:, :BLOCK_LEN] = jnp.zeros((2, BLOCK_LEN), jnp.float32)
    span_ref[:, BLOCK_LEN + samples :] = jnp.zeros((2, BLOCK_LEN), jnp.float32)
    for t in range(owners):
        span_ref[:, BLOCK_LEN + t * length : BLOCK_LEN + (t + 1) * length] = ref_ref[t]
    late_ref[...] = pltpu.roll(span_ref[...], first_lag, 1)

    def shifted(window, count):
        tiled = jnp.broadcast_to(window, (count, window.shape[1]))
        return pltpu.roll(tiled, 0, 1, stride=1, stride_axis=0)[:, LANES : LANES + BLOCK_LEN]

    def taps_of(window):
        return jnp.concatenate(
            [shifted(window[c : c + 1, BLOCK_LEN - LANES :], TAPS) for c in range(2)], 0
        )

    turn = lane_sign((lags_local, LANES))

    def step(q, total):
        lanes = pl.ds(pl.multiple_of(q * BLOCK_LEN, BLOCK_LEN), 2 * BLOCK_LEN)
        window, late = span_ref[:, lanes], late_ref[:, lanes]
        taps_high, taps_low = halves(taps_of(window))
        lag_rows = [shifted(late[c : c + 1, BLOCK_LEN - LANES :], lags_local) for c in range(2)]
        pad = jnp.zeros((2 * SUBLANES - 2, BLOCK_LEN), jnp.float32)
        lag_rows = jnp.concatenate(lag_rows + [window[:, BLOCK_LEN:], pad], 0)
        lags_high, lags_low = halves(lag_rows)
        product = dot_nt(
            jnp.concatenate([lags_high, lags_low], 0), jnp.concatenate([taps_high, taps_low], 0)
        )
        count = lag_rows.shape[0]
        product = product[:count, :LANES] + (product[:count, LANES:] + product[count:, :LANES])
        by_real = product[:lags_local]
        by_imag = product[lags_local : 2 * lags_local]
        rows = pl.ds(pl.multiple_of(q * lags_local, lags_local), lags_local)
        out_ref[rows, :] = by_real + turn * pltpu.roll(by_imag, TAPS, 1)
        return total + product[2 * lags_local : 2 * lags_local + SUBLANES]

    total = lax.fori_loop(0, blocks, step, jnp.zeros((SUBLANES, LANES), jnp.float32))

    line = total[0:1] + lane_sign((1, LANES)) * pltpu.roll(total[1:2], TAPS, 1)
    low = lax.broadcasted_iota(jnp.int32, (1, LANES), 1) < TAPS
    line_r = jnp.where(low, line, 0.0)
    line_i = jnp.where(low, pltpu.roll(line, TAPS, 1), 0.0)
    above = lax.broadcasted_iota(jnp.int32, (TAPS, TAPS), 1) > lax.broadcasted_iota(jnp.int32, (TAPS, TAPS), 0)
    equal = lax.broadcasted_iota(jnp.int32, (TAPS, TAPS), 1) == lax.broadcasted_iota(jnp.int32, (TAPS, TAPS), 0)

    def upper(x):
        spread = pltpu.roll(jnp.broadcast_to(x, (TAPS, LANES)), 0, 1, stride=1, stride_axis=0)
        return spread[:, :TAPS]

    up_r = upper(line_r)
    up_i = jnp.where(above, upper(line_i), 0.0)
    strict_r = jnp.where(above, up_r, 0.0)
    diag_r = jnp.where(equal, up_r, 0.0)
    gram_r = strict_r + strict_r.T + diag_r
    gram_i = up_i - up_i.T
    tail = taps_of(span_ref[:, samples:])
    tails = dot_nt(tail, tail, HIGHEST)
    gram_r = gram_r - (tails[:TAPS, :TAPS] + tails[TAPS:, TAPS:])
    gram_i = gram_i - (tails[:TAPS, TAPS:] - tails[TAPS:, :TAPS])

    inverse = complex_inverse(jnp.concatenate([gram_r, gram_i], 1))
    lower = -lane_sign(inverse.shape) * pltpu.roll(inverse, TAPS, 1)
    solver = jnp.concatenate([inverse, lower], 0)
    out_ref[...] = jnp.dot(
        out_ref[...], solver, precision=HIGHEST, preferred_element_type=jnp.float32
    )


def own_call(ref_all, lags_local):
    owners, _, length = ref_all.shape
    samples = owners * length
    blocks = samples // BLOCK_LEN
    shape = (blocks * lags_local, 2 * TAPS)
    return pl.pallas_call(
        functools.partial(own_kernel, lags_local),
        out_shape=jax.ShapeDtypeStruct(shape, jnp.float32),
        scratch_shapes=[pltpu.VMEM((2, samples + 2 * BLOCK_LEN), jnp.float32)] * 2,
        compiler_params=params(),
        cost_estimate=pl.CostEstimate(
            flops=12 * samples * 2 * TAPS * 4 * lags_local, bytes_accessed=4 * math.prod(shape), transcendentals=0
        ),
        name="reference_products",
    )(ref_all)


def doppler_table(block_count, scale):
    phase = (np.arange(block_count)[:, None] * np.arange(DOPPLER)[None, :] % DOPPLER) * (2.0 * math.pi / DOPPLER)
    cosine, sine = np.cos(phase), np.sin(phase)
    upper = np.concatenate([cosine, -sine], 1)
    lower = np.concatenate([sine, cosine], 1)
    return (np.concatenate([upper, lower], 0) * scale).astype(np.float32)


def map_kernel(groups, got_ref, own_ref, wave_ref, out_ref, held_ref):
    owners, pieces = got_ref.shape[:2]
    blocks = pieces - groups // 2
    lags_local = LANES // groups
    total = owners * blocks
    left = lax.broadcasted_iota(jnp.int32, (SUBLANES, LANES), 1) < TAPS
    sign = row_sign((SUBLANES, LANES))
    rows = [None] * groups
    for i in range(groups // 2):
        tile = got_ref[0, blocks + i]
        for owner in range(1, owners):
            tile = tile + got_ref[owner, blocks + i]
        swapped = pltpu.roll(tile, TAPS, 1)
        for part, here, there in ((i, tile, swapped), (i + groups // 2, swapped, tile)):
            other = -sign * pltpu.roll(there, SUBLANES // 2, 0)
            rows[part] = jnp.where(left, here, other)
    cross = jnp.concatenate(rows, 0)
    clutter = dot_nt(cross, own_ref[...], HIGHEST)
    for q in range(0, total, groups):
        lanes = slice(q * lags_local, q * lags_local + LANES)
        tiles = [clutter[r : r + SUBLANES, lanes] for r in range(0, groups * SUBLANES, SUBLANES)]
        for j, tile in enumerate(swap_groups(tiles, groups)):
            at = q + j
            held_ref[at * SUBLANES : (at + 1) * SUBLANES, :] = got_ref[at // blocks, at % blocks] - tile
    half = SUBLANES // 2
    wave = wave_ref[...]
    for g in range(half):
        parts = [held_ref[pl.ds(c * half + g, total, stride=SUBLANES), :] for c in range(2)]
        lagged = jnp.concatenate(parts, 0).T
        spectrum = jnp.dot(lagged, wave, precision=HIGHEST, preferred_element_type=jnp.float32)
        for i in range(groups):
            for c in range(2):
                out_ref[half * i + g, c] = spectrum[
                    i * lags_local : (i + 1) * lags_local, c * DOPPLER : (c + 1) * DOPPLER
                ]


def map_call(got, own, wave, groups, beams_local):
    owners, pieces = got.shape[:2]
    total = owners * (pieces - groups // 2)
    lags_local = LANES // groups
    shape = (beams_local, 2, lags_local, DOPPLER)
    return pl.pallas_call(
        functools.partial(map_kernel, groups),
        out_shape=jax.ShapeDtypeStruct(shape, jnp.float32),
        scratch_shapes=[pltpu.VMEM((total * SUBLANES, LANES), jnp.float32)],
        compiler_params=params(),
        cost_estimate=pl.CostEstimate(
            flops=12 * math.prod(shape) * total, bytes_accessed=4 * math.prod(shape), transcendentals=0
        ),
        name="range_doppler",
    )(got, own, wave)


def swap(x, axis, by):
    pairs = [(i, i ^ by) for i in range(lax.axis_size(axis))]
    return lax.ppermute(x, axis, pairs)


def tiled_device(ref_signal, surveillance, steering):
    chan_count, tm_count = lax.axis_size("chan"), lax.axis_size("tm")
    channels, length = surveillance.shape[1:]
    beams_local = steering.shape[1] // chan_count
    lags_local = LAGS // tm_count
    groups = LANES // lags_local
    samples = length * tm_count

    ref_all = lax.all_to_all(
        jnp.broadcast_to(ref_signal[None], (tm_count,) + ref_signal.shape), "tm", 0, 0, tiled=True
    )
    even, odd = beam_call(steering, surveillance.reshape(2 * channels, length), chan_count, beams_local)
    rows = 2 * beams_local
    parts = [even.reshape(chan_count // 2, rows, length), swap(odd, "chan", 1).reshape(chan_count // 2, rows, length)]
    by = 2
    while by < chan_count:
        sent = parts[0][1::2]
        for part in parts[1:]:
            sent = sent + part[1::2]
        parts = [part[::2] for part in parts] + [swap(sent, "chan", by)]
        by *= 2
    table = table_call(ref_all)
    pieces = lag_call([part[0] for part in parts], table, groups, tm_count)
    got = lax.all_to_all(pieces, "tm", 0, 0, tiled=True)
    own = own_call(ref_all, lags_local)
    wave = doppler_table(samples // BLOCK_LEN, 0.125 / math.sqrt(samples))
    return map_call(got, own, jnp.asarray(wave), groups, beams_local)


def lag_table(ref_ext, offset, lags):
    window = lax.dynamic_slice_in_dim(ref_ext, offset, BLOCK_LEN + LAGS, 1)
    span = BLOCK_LEN + LAGS
    tiled = jnp.tile(jnp.pad(window, ((0, 0), (0, 1))), (1, lags))[:, : lags * span]
    return tiled.reshape(2, lags, span)[:, :, LAGS:]


def times_conj(a, b):
    real = jnp.einsum("...t,lt->...l", a[..., 0, :], b[0], precision=HIGHEST) + jnp.einsum(
        "...t,lt->...l", a[..., 1, :], b[1], precision=HIGHEST
    )
    imag = jnp.einsum("...t,lt->...l", a[..., 1, :], b[0], precision=HIGHEST) - jnp.einsum(
        "...t,lt->...l", a[..., 0, :], b[1], precision=HIGHEST
    )
    return jnp.stack([real, imag], -2)


def plain_device(ref_signal, surveillance, steering):
    chan_count, tm_count = lax.axis_size("chan"), lax.axis_size("tm")
    length = surveillance.shape[2]
    beams = steering.shape[1]
    lags_local = LAGS // tm_count
    samples = length * tm_count
    local_blocks = length // BLOCK_LEN
    here = lax.axis_index("tm")

    w_real, w_imag = steering
    real = jnp.dot(w_real, surveillance[0], precision=HIGHEST) - jnp.dot(w_imag, surveillance[1], precision=HIGHEST)
    imag = jnp.dot(w_imag, surveillance[0], precision=HIGHEST) + jnp.dot(w_real, surveillance[1], precision=HIGHEST)
    beam = lax.psum_scatter(jnp.stack([real, imag], 1), "chan", scatter_dimension=0, tiled=True)
    ref_all = lax.all_gather(ref_signal, "tm", axis=1, tiled=True)
    ref_ext = jnp.pad(ref_all, ((0, 0), (LAGS, 0)))

    def beam_step(carry, q):
        offset = q * BLOCK_LEN
        table = lag_table(ref_ext, here * length + offset, LAGS)
        segment = lax.dynamic_slice_in_dim(beam, offset, BLOCK_LEN, 2)
        return carry, times_conj(segment, table)

    _, products = lax.scan(beam_step, None, jnp.arange(local_blocks, dtype=jnp.int32))
    cross = lax.psum(products[..., :TAPS].sum(0), "tm")
    got = lax.all_to_all(products, "tm", 3, 0, tiled=True)

    def own_step(gram, q):
        offset = q * BLOCK_LEN
        table = lag_table(ref_ext, offset, LAGS)
        taps = table[:, :TAPS].transpose(1, 0, 2)
        mine = lax.dynamic_slice_in_dim(table, here * lags_local, lags_local, 1)
        return gram + times_conj(taps, table[:, :TAPS]), times_conj(taps, mine)

    start = jnp.zeros((TAPS, 2, TAPS), jnp.float32)
    gram, own = lax.scan(own_step, start, jnp.arange(samples // BLOCK_LEN, dtype=jnp.int32))
    g_real, g_imag = gram[:, 0].T, gram[:, 1].T
    system = jnp.concatenate([jnp.concatenate([g_real, -g_imag], 1), jnp.concatenate([g_imag, g_real], 1)], 0)
    right = jnp.concatenate([cross[:, 0].T, cross[:, 1].T], 0)
    solved = jax.scipy.linalg.cho_solve((jnp.linalg.cholesky(system), True), right)
    b_real, b_imag = solved[:TAPS].T, solved[TAPS:].T
    mixing = jnp.concatenate([jnp.stack([b_real, b_imag], 1), jnp.stack([-b_imag, b_real], 1)], 2)
    stacked = jnp.concatenate([own[:, :, 0], own[:, :, 1]], 1)
    lagged = got - jnp.einsum("mck,qkl->qmcl", mixing, stacked, precision=HIGHEST)
    wave = jnp.asarray(doppler_table(samples // BLOCK_LEN, 0.125 / math.sqrt(samples)))
    wave = wave.reshape(2, samples // BLOCK_LEN, 2, DOPPLER)
    return jnp.einsum("qmcl,cqdk->mdlk", lagged, wave, precision=HIGHEST)


def on_device(ref_signal, surveillance, steering):
    chan_count, tm_count = lax.axis_size("chan"), lax.axis_size("tm")
    beams_local = steering.shape[1] // chan_count
    lags_local = LAGS // tm_count
    fills = (
        LANES % lags_local == 0
        and lags_local % (2 * SUBLANES) == 0
        and beams_local * lags_local == LANES * SUBLANES // 2
        and chan_count > 1
        and chan_count & (chan_count - 1) == 0
        and 2 * surveillance.shape[1] % LANES == 0
        and surveillance.shape[2] % (4 * BLOCK_LEN) == 0
    )
    device = tiled_device if fills else plain_device
    return device(ref_signal, surveillance, steering)


def solution(mesh):
    placed = (P(None, "tm"), P(None, "chan", "tm"), P(None, None, "chan"))
    return jax.shard_map(
        on_device,
        mesh=mesh,
        in_specs=placed,
        out_specs=P("chan", None, "tm", None),
        check_vma=False,
    )
```

```python
import functools
import math

import jax
import jax.numpy as jnp
import numpy as np
from jax import lax
from jax.experimental import pallas as pl
from jax.experimental.pallas import tpu as pltpu
from jax.sharding import PartitionSpec as P

LAGS = 256
DOPPLER = 256
TAPS = 64
BLOCK_LEN = 256
LANES = 128
SUBLANES = 8

HIGHEST = lax.Precision.HIGHEST
VMEM_BYTES = 48 * 1024 * 1024


def params():
    return pltpu.CompilerParams(vmem_limit_bytes=VMEM_BYTES)


def halves(x):
    high = x.astype(jnp.bfloat16)
    return high, (x - high.astype(jnp.float32)).astype(jnp.bfloat16)


def dot_nt(a, b, precision=None):
    return lax.dot_general(
        a, b, (((1,), (1,)), ((), ())), precision=precision, preferred_element_type=jnp.float32
    )


def row_sign(shape):
    rows = lax.broadcasted_iota(jnp.int32, shape, 0)
    return jnp.where(rows % SUBLANES < SUBLANES // 2, 1.0, -1.0).astype(jnp.float32)


def lane_sign(shape):
    lanes = lax.broadcasted_iota(jnp.int32, shape, 1)
    return jnp.where(lanes % LANES < LANES // 2, 1.0, -1.0).astype(jnp.float32)


def swap_groups(rows, groups):
    width = LANES // groups
    lane_group = lax.broadcasted_iota(jnp.int32, rows[0].shape, 1) // width
    outs = []
    for j in range(groups):
        out = rows[j]
        for i in range(groups):
            if i != j:
                moved = pltpu.roll(rows[i], (width * (i - j)) % LANES, 1)
                out = jnp.where(lane_group == i, moved, out)
        outs.append(out)
    return outs


def beam_kernel(chan_count, beams_local, w_ref, s_ref, even_ref, odd_ref):
    me = lax.axis_index("chan")
    half = SUBLANES // 2
    sub = lax.broadcasted_iota(jnp.int32, (SUBLANES, w_ref.shape[2]), 0)
    top = sub < half
    parts = []
    for parity in range(2):
        rows = []
        for e in range(parity, chan_count, 2):
            base = (me ^ e) * beams_local
            for tile in range(beams_local // SUBLANES):
                start = pl.multiple_of(base + tile * SUBLANES, SUBLANES)
                wr = w_ref[0, pl.ds(start, SUBLANES), :]
                wi = w_ref[1, pl.ds(start, SUBLANES), :]
                wr_s = pltpu.roll(wr, half, 0)
                wi_s = pltpu.roll(wi, half, 0)
                first = [jnp.where(top, wr, wi_s), jnp.where(top, -wi, wr_s)]
                second = [jnp.where(top, wr_s, wi), jnp.where(top, -wi_s, wr)]
                rows.append(jnp.concatenate(first, 1))
                rows.append(jnp.concatenate(second, 1))
        parts.append(jnp.concatenate(rows, 0))
    weights = jnp.concatenate(parts, 0)
    product = jnp.dot(
        weights, s_ref[...], precision=HIGHEST, preferred_element_type=jnp.float32
    )
    mid = product.shape[0] // 2
    even_ref[...] = product[:mid]
    odd_ref[...] = product[mid:]


def beam_call(steering, survey, chan_count, beams_local):
    depth, length = survey.shape
    rows = chan_count * beams_local
    steps = 4
    width = length // steps
    out = jax.ShapeDtypeStruct((rows, length), jnp.float32)
    return pl.pallas_call(
        functools.partial(beam_kernel, chan_count, beams_local),
        grid=(steps,),
        in_specs=[
            pl.BlockSpec(steering.shape, lambda i: (0, 0, 0)),
            pl.BlockSpec((depth, width), lambda i: (0, i)),
        ],
        out_specs=[pl.BlockSpec((rows, width), lambda i: (0, i))] * 2,
        out_shape=[out, out],
        compiler_params=params(),
        cost_estimate=pl.CostEstimate(
            flops=4 * rows * depth * length, bytes_accessed=4 * length * (depth + 2 * rows), transcendentals=0
        ),
        name="beams",
    )(steering, survey)


def table_kernel(edge_ref, ref_ref, out_ref):
    span = jnp.concatenate([edge_ref[...], ref_ref[...]], 1)
    for c in range(2):
        tiled = jnp.broadcast_to(span[c : c + 1], (LANES, span.shape[1]))
        shifted = pltpu.roll(tiled, 0, 1, stride=1, stride_axis=0)[:, LANES:]
        high, low = halves(shifted)
        out_ref[0, c] = high
        out_ref[1, c] = low


def table_call(edge, ref):
    shape = (2, 2, LANES, LANES + ref.shape[1])
    return pl.pallas_call(
        table_kernel,
        out_shape=jax.ShapeDtypeStruct(shape, jnp.bfloat16),
        compiler_params=params(),
        cost_estimate=pl.CostEstimate(
            flops=8 * math.prod(shape), bytes_accessed=2 * math.prod(shape), transcendentals=0
        ),
        name="shifted_reference",
    )(edge, ref)


def lag_kernel(groups, owners, *refs):
    y_refs = refs[: -(owners + 2)]
    table_ref = refs[-(owners + 2)]
    out_refs = refs[-(owners + 1) : -1]
    held_ref = refs[-1]
    me = lax.axis_index("tm")
    y = y_refs[0][...]
    for y_ref in y_refs[1:]:
        y = y + y_ref[...]
    rows, length = y.shape
    blocks = length // BLOCK_LEN
    turned = jnp.concatenate(
        [pltpu.roll(y[r : r + SUBLANES], SUBLANES // 2, 0) for r in range(0, rows, SUBLANES)], 0
    )
    turned = turned * row_sign(turned.shape)
    y_high, y_low = halves(y)
    t_high, t_low = halves(turned)
    both = jnp.concatenate([y_high, y_low], 0)
    turned_both = jnp.concatenate([t_high, t_low], 0)
    taps_sum = None
    for q in range(blocks):
        near = slice(q * BLOCK_LEN + LANES, q * BLOCK_LEN + LANES + BLOCK_LEN)
        far = slice(q * BLOCK_LEN, (q + 1) * BLOCK_LEN)
        cols = slice(q * BLOCK_LEN, (q + 1) * BLOCK_LEN)
        tables = []
        for h in range(2):
            tables.append(
                jnp.concatenate(
                    [
                        jnp.concatenate([table_ref[h, 0, :, near], table_ref[h, 1, :, near]], 1),
                        jnp.concatenate([table_ref[h, 0, :, far], table_ref[h, 1, :, far]], 1),
                    ],
                    0,
                )
            )
        lhs = jnp.concatenate([both[:, cols], turned_both[:, cols]], 1)
        by_high = dot_nt(lhs, tables[0])
        by_low = dot_nt(lhs[:rows], tables[1])
        product = by_high[:rows] + (by_high[rows:] + by_low)
        taps = product[:, :LANES]
        taps_sum = taps if taps_sum is None else taps_sum + taps
        for h in range(LAGS // LANES):
            lanes = slice(h * LANES, (h + 1) * LANES)
            tiles = [product[r : r + SUBLANES, lanes] for r in range(0, rows, SUBLANES)]
            for j, tile in enumerate(swap_groups(tiles, groups)):
                held_ref[h * groups + j, q] = tile
    left = lax.broadcasted_iota(jnp.int32, (SUBLANES, LANES), 1) < TAPS
    for i in range(groups // 2):
        a = taps_sum[i * SUBLANES : (i + 1) * SUBLANES]
        other = i + groups // 2
        b = taps_sum[other * SUBLANES : (other + 1) * SUBLANES]
        tile = jnp.where(left, a, pltpu.roll(b, LANES - TAPS, 1))
        for out_ref in out_refs:
            out_ref[blocks + i] = tile
    for e, out_ref in enumerate(out_refs):
        out_ref[:blocks] = held_ref[me ^ e]


def lag_call(ys, table, groups, owners):
    rows, length = ys[0].shape
    blocks = length // BLOCK_LEN
    shape = (blocks + groups // 2, SUBLANES, LANES)
    return pl.pallas_call(
        functools.partial(lag_kernel, groups, owners),
        out_shape=[jax.ShapeDtypeStruct(shape, jnp.float32)] * owners,
        scratch_shapes=[pltpu.VMEM((owners, blocks, SUBLANES, LANES), jnp.float32)],
        compiler_params=params(),
        cost_estimate=pl.CostEstimate(
            flops=12 * rows * LAGS * 2 * length,
            bytes_accessed=4 * owners * math.prod(shape) + 2 * math.prod(table.shape),
            transcendentals=0,
        ),
        name="lag_products",
    )(*ys, table)


SHARES = 2
BATCH = 4


def own_kernel(lags_local, *refs):
    *part_refs, out_ref, tail_ref, span_ref, late_ref = refs
    me = lax.axis_index("tm")
    length = part_refs[0].shape[2]
    owners = sum(part_ref.shape[0] for part_ref in part_refs)
    samples = owners * length
    blocks = samples // BLOCK_LEN // SHARES
    first_block = lax.rem(lax.axis_index("chan"), SHARES) * blocks
    span_ref[:, :BLOCK_LEN] = jnp.zeros((2, BLOCK_LEN), jnp.float32)
    span_ref[:, BLOCK_LEN + samples :] = jnp.zeros((2, BLOCK_LEN), jnp.float32)
    e = 0
    for part_ref in part_refs:
        for i in range(part_ref.shape[0]):
            start = pl.multiple_of((me ^ e) * length + BLOCK_LEN, BLOCK_LEN)
            span_ref[:, pl.ds(start, length)] = part_ref[i]
            e += 1
    late_ref[...] = pltpu.roll(span_ref[...], me * lags_local, 1)

    def shifted(window, count):
        tiled = jnp.broadcast_to(window, (count, window.shape[1]))
        return pltpu.roll(tiled, 0, 1, stride=1, stride_axis=0)[:, LANES:]

    def pair_of(window, count):
        return jnp.concatenate([shifted(window[c : c + 1], count) for c in range(2)], 0)

    turn = lane_sign((lags_local, LANES))

    def step(n, total):
        start = pl.multiple_of((first_block + n * BATCH) * BLOCK_LEN, BLOCK_LEN) + BLOCK_LEN - LANES
        lanes = pl.ds(pl.multiple_of(start, LANES), BATCH * BLOCK_LEN + LANES)
        window, late = span_ref[:, lanes], late_ref[:, lanes]
        taps_high, taps_low = halves(pair_of(window, TAPS))
        pad = jnp.zeros((2 * SUBLANES - 2, BATCH * BLOCK_LEN), jnp.float32)
        lag_rows = jnp.concatenate([pair_of(late, lags_local), window[:, LANES:], pad], 0)
        lags_high, lags_low = halves(lag_rows)
        taps = jnp.concatenate([taps_high, taps_low], 0)
        lags = jnp.concatenate([lags_high, lags_low], 0)
        count = lag_rows.shape[0]
        for b in range(BATCH):
            cols = slice(b * BLOCK_LEN, (b + 1) * BLOCK_LEN)
            product = dot_nt(lags[:, cols], taps[:, cols])
            product = product[:count, :LANES] + (product[:count, LANES:] + product[count:, :LANES])
            by_real = product[:lags_local]
            by_imag = product[lags_local : 2 * lags_local]
            rows = pl.ds(pl.multiple_of((n * BATCH + b) * lags_local, lags_local), lags_local)
            out_ref[rows, :] = by_real + turn * pltpu.roll(by_imag, TAPS, 1)
            total = total + product[2 * lags_local : 2 * lags_local + SUBLANES]
        return total

    total = lax.fori_loop(0, blocks // BATCH, step, jnp.zeros((SUBLANES, LANES), jnp.float32))
    out_ref[blocks * lags_local :, :] = total
    tail = pair_of(span_ref[:, samples + BLOCK_LEN - LANES :], TAPS)
    tail_ref[...] = dot_nt(tail, tail, HIGHEST)


def own_call(parts, lags_local):
    length = parts[0].shape[2]
    samples = length * sum(part.shape[0] for part in parts)
    rows = samples // BLOCK_LEN // SHARES * lags_local
    return pl.pallas_call(
        functools.partial(own_kernel, lags_local),
        out_shape=[
            jax.ShapeDtypeStruct((rows + SUBLANES, 2 * TAPS), jnp.float32),
            jax.ShapeDtypeStruct((2 * TAPS, 2 * TAPS), jnp.float32),
        ],
        scratch_shapes=[pltpu.VMEM((2, samples + 2 * BLOCK_LEN), jnp.float32)] * 2,
        compiler_params=params(),
        cost_estimate=pl.CostEstimate(
            flops=24 * rows * BLOCK_LEN * 2 * TAPS, bytes_accessed=4 * rows * 2 * TAPS, transcendentals=0
        ),
        name="reference_products",
    )(*parts)


def as_factor(a):
    return jnp.concatenate([a, -lane_sign(a.shape) * pltpu.roll(a, a.shape[0], 1)], 0)


def dot_split(a, b):
    (a_high, a_low), (b_high, b_low) = a, b
    left = jnp.concatenate([a_high, a_low], 1)
    right = jnp.concatenate([b_high, b_high], 0)
    return jnp.dot(left, right, preferred_element_type=jnp.float32) + jnp.dot(
        a_high, b_low, preferred_element_type=jnp.float32
    )


def solver_kernel(mine_ref, other_ref, tail_ref, gram_ref, solver_ref):
    total = mine_ref[...] + other_ref[...]
    line = total[0:1] + lane_sign((1, LANES)) * pltpu.roll(total[1:2], TAPS, 1)
    low = lax.broadcasted_iota(jnp.int32, (1, LANES), 1) < TAPS
    line_r = jnp.where(low, line, 0.0)
    line_i = jnp.where(low, pltpu.roll(line, TAPS, 1), 0.0)
    cols = lax.broadcasted_iota(jnp.int32, (TAPS, TAPS), 1)
    rows = lax.broadcasted_iota(jnp.int32, (TAPS, TAPS), 0)
    above = cols > rows

    def upper(x):
        spread = pltpu.roll(jnp.broadcast_to(x, (TAPS, LANES)), 0, 1, stride=1, stride_axis=0)
        return spread[:, :TAPS]

    up_r = upper(line_r)
    up_i = jnp.where(above, upper(line_i), 0.0)
    strict_r = jnp.where(above, up_r, 0.0)
    diag_r = jnp.where(cols == rows, up_r, 0.0)
    tails = tail_ref[...]
    gram_r = strict_r + strict_r.T + diag_r - (tails[:TAPS, :TAPS] + tails[TAPS:, TAPS:])
    gram_i = up_i - up_i.T - (tails[:TAPS, TAPS:] - tails[TAPS:, :TAPS])
    gram = jnp.concatenate([gram_r, gram_i], 1)
    gram_factor = as_factor(gram)
    gram_ref[...] = gram_factor
    gram_halves = halves(gram_factor)
    one = (
        lax.broadcasted_iota(jnp.int32, gram.shape, 0) == lax.broadcasted_iota(jnp.int32, gram.shape, 1)
    ).astype(jnp.float32)
    bound = jnp.max(jnp.sum(jnp.abs(gram), axis=1, keepdims=True), axis=0, keepdims=True)

    def again(state):
        count, left, _ = state
        return (count < 60) & (left > 1e-3)

    def newton(state):
        count, _, x = state
        x_halves = halves(x)
        seen = dot_split(x_halves, gram_halves)
        left = jnp.max(jnp.abs(seen - one))
        x = 2.0 * x - dot_split(halves(seen), halves(as_factor(x)))
        return count + 1, left, x

    start = (jnp.int32(0), jnp.float32(1.0), one * (1.0 / bound))
    _, _, inverse = lax.while_loop(again, newton, start)
    solver_ref[...] = as_factor(inverse)


def solver_call(mine, other, tail):
    last = mine.shape[0] // SUBLANES - 1
    line = pl.BlockSpec((SUBLANES, LANES), lambda i: (last, 0))
    whole = pl.BlockSpec(tail.shape, lambda i: (0, 0))
    return pl.pallas_call(
        solver_kernel,
        grid=(1,),
        in_specs=[line, line, whole],
        out_specs=[whole, whole],
        out_shape=[jax.ShapeDtypeStruct(tail.shape, jnp.float32)] * 2,
        compiler_params=params(),
        cost_estimate=pl.CostEstimate(flops=500_000_000, bytes_accessed=200_000, transcendentals=0),
        name="gram_inverse",
    )(mine, other, tail)


def doppler_table(block_count, scale):
    phase = (np.arange(block_count)[:, None] * np.arange(DOPPLER)[None, :] % DOPPLER) * (2.0 * math.pi / DOPPLER)
    cosine, sine = np.cos(phase), np.sin(phase)
    upper = np.concatenate([cosine, -sine], 1)
    lower = np.concatenate([sine, cosine], 1)
    return (np.concatenate([upper, lower], 0) * scale).astype(np.float32)


def map_kernel(groups, owners, *refs):
    got_refs = refs[:owners]
    mine_ref, other_ref, gram_ref, solver_ref, wave_ref, out_ref, got_ref, held_ref = refs[owners:]
    me = lax.axis_index("tm")
    blocks = got_refs[0].shape[0] - groups // 2
    lags_local = LANES // groups
    total = owners * blocks
    left = lax.broadcasted_iota(jnp.int32, (SUBLANES, LANES), 1) < TAPS
    sign = row_sign((SUBLANES, LANES))
    for e, ref in enumerate(got_refs):
        start = pl.multiple_of((me ^ e) * blocks * SUBLANES, SUBLANES)
        got_ref[pl.ds(start, blocks * SUBLANES), :] = ref[:blocks].reshape(blocks * SUBLANES, LANES)
    rows = [None] * groups
    for i in range(groups // 2):
        tile = got_refs[0][blocks + i]
        for ref in got_refs[1:]:
            tile = tile + ref[blocks + i]
        swapped = pltpu.roll(tile, TAPS, 1)
        for part, here, there in ((i, tile, swapped), (i + groups // 2, swapped, tile)):
            other = -sign * pltpu.roll(there, SUBLANES // 2, 0)
            rows[part] = jnp.where(left, here, other)
    cross = jnp.concatenate(rows, 0)
    solver = solver_ref[...]
    taps = jnp.dot(cross, solver, precision=HIGHEST, preferred_element_type=jnp.float32)
    rest = cross - jnp.dot(taps, gram_ref[...], precision=HIGHEST, preferred_element_type=jnp.float32)
    taps = taps + jnp.dot(rest, solver, precision=HIGHEST, preferred_element_type=jnp.float32)
    taps_high, taps_low = halves(taps)
    taps_both = jnp.concatenate([taps_high, taps_low], 1)
    share = lax.rem(lax.axis_index("chan"), SHARES)
    share_blocks = total // SHARES
    for which, own_ref in enumerate((mine_ref, other_ref)):
        first = (share ^ which) * share_blocks
        for q in range(0, share_blocks, 2 * groups):
            own_high, own_low = halves(own_ref[q * lags_local : (q + 2 * groups) * lags_local, :])
            clutter = dot_nt(taps_both, jnp.concatenate([own_high, own_high], 1)) + dot_nt(taps_high, own_low)
            for h in range(2):
                lanes = slice(h * LANES, (h + 1) * LANES)
                tiles = [clutter[r : r + SUBLANES, lanes] for r in range(0, groups * SUBLANES, SUBLANES)]
                tiles = jnp.concatenate(swap_groups(tiles, groups), 0)
                at = pl.multiple_of((first + q + h * groups) * SUBLANES, groups * SUBLANES)
                at = pl.ds(at, groups * SUBLANES)
                held_ref[at, :] = got_ref[at, :] - tiles
    half = SUBLANES // 2
    wave = (wave_ref[0], wave_ref[1])
    for g in range(half):
        parts = [held_ref[pl.ds(c * half + g, total, stride=SUBLANES), :] for c in range(2)]
        spectrum = dot_split(halves(jnp.concatenate(parts, 0).T), wave)
        for i in range(groups):
            for c in range(2):
                out_ref[half * i + g, c] = spectrum[
                    i * lags_local : (i + 1) * lags_local, c * DOPPLER : (c + 1) * DOPPLER
                ]


def map_call(got, mine, other, gram, solver, wave, groups, beams_local):
    owners = len(got)
    total = owners * (got[0].shape[0] - groups // 2)
    lags_local = LANES // groups
    shape = (beams_local, 2, lags_local, DOPPLER)
    return pl.pallas_call(
        functools.partial(map_kernel, groups, owners),
        out_shape=jax.ShapeDtypeStruct(shape, jnp.float32),
        scratch_shapes=[pltpu.VMEM((total * SUBLANES, LANES), jnp.float32)] * 2,
        compiler_params=params(),
        cost_estimate=pl.CostEstimate(
            flops=12 * math.prod(shape) * total, bytes_accessed=4 * math.prod(shape), transcendentals=0
        ),
        name="range_doppler",
    )(*got, mine, other, gram, solver, wave)


def swap(x, axis, by):
    pairs = [(i, i ^ by) for i in range(lax.axis_size(axis))]
    return lax.ppermute(x, axis, pairs)


def tiled_device(ref_signal, surveillance, steering):
    chan_count, tm_count = lax.axis_size("chan"), lax.axis_size("tm")
    channels, length = surveillance.shape[1:]
    beams_local = steering.shape[1] // chan_count
    lags_local = LAGS // tm_count
    groups = LANES // lags_local
    samples = length * tm_count

    edge = lax.ppermute(
        ref_signal[:, length - 2 * LANES :], "tm", [(i, i + 1) for i in range(tm_count - 1)]
    )
    ref_parts = [ref_signal[None]]
    by = 1
    while by < tm_count:
        ref_parts.append(swap(jnp.concatenate(ref_parts, 0), "tm", by))
        by *= 2

    even, odd = beam_call(steering, surveillance.reshape(2 * channels, length), chan_count, beams_local)
    rows = 2 * beams_local
    parts = [even.reshape(chan_count // 2, rows, length), swap(odd, "chan", 1).reshape(chan_count // 2, rows, length)]
    by = 2
    while by < chan_count:
        sent = parts[0][1::2]
        for part in parts[1:]:
            sent = sent + part[1::2]
        parts = [part[::2] for part in parts] + [swap(sent, "chan", by)]
        by *= 2
    table = table_call(edge, ref_signal)
    pieces = lag_call([part[0] for part in parts], table, groups, tm_count)
    got = [pieces[0]] + [swap(piece, "tm", e) for e, piece in enumerate(pieces) if e]
    mine, tail = own_call(ref_parts, lags_local)
    other = swap(mine, "chan", 1)
    gram, solver = solver_call(mine, other, tail)
    wave = doppler_table(samples // BLOCK_LEN, 0.125 / math.sqrt(samples))
    high = wave.astype(jnp.bfloat16)
    wave = np.stack([high, (wave - high.astype(np.float32)).astype(jnp.bfloat16)])
    return map_call(got, mine, other, gram, solver, jnp.asarray(wave), groups, beams_local)


def lag_table(ref_ext, offset, lags):
    window = lax.dynamic_slice_in_dim(ref_ext, offset, BLOCK_LEN + LAGS, 1)
    span = BLOCK_LEN + LAGS
    tiled = jnp.tile(jnp.pad(window, ((0, 0), (0, 1))), (1, lags))[:, : lags * span]
    return tiled.reshape(2, lags, span)[:, :, LAGS:]


def times_conj(a, b):
    real = jnp.einsum("...t,lt->...l", a[..., 0, :], b[0], precision=HIGHEST) + jnp.einsum(
        "...t,lt->...l", a[..., 1, :], b[1], precision=HIGHEST
    )
    imag = jnp.einsum("...t,lt->...l", a[..., 1, :], b[0], precision=HIGHEST) - jnp.einsum(
        "...t,lt->...l", a[..., 0, :], b[1], precision=HIGHEST
    )
    return jnp.stack([real, imag], -2)


def plain_device(ref_signal, surveillance, steering):
    chan_count, tm_count = lax.axis_size("chan"), lax.axis_size("tm")
    length = surveillance.shape[2]
    beams = steering.shape[1]
    lags_local = LAGS // tm_count
    samples = length * tm_count
    local_blocks = length // BLOCK_LEN
    here = lax.axis_index("tm")

    w_real, w_imag = steering
    real = jnp.dot(w_real, surveillance[0], precision=HIGHEST) - jnp.dot(w_imag, surveillance[1], precision=HIGHEST)
    imag = jnp.dot(w_imag, surveillance[0], precision=HIGHEST) + jnp.dot(w_real, surveillance[1], precision=HIGHEST)
    beam = lax.psum_scatter(jnp.stack([real, imag], 1), "chan", scatter_dimension=0, tiled=True)
    ref_all = lax.all_gather(ref_signal, "tm", axis=1, tiled=True)
    ref_ext = jnp.pad(ref_all, ((0, 0), (LAGS, 0)))

    def beam_step(carry, q):
        offset = q * BLOCK_LEN
        table = lag_table(ref_ext, here * length + offset, LAGS)
        segment = lax.dynamic_slice_in_dim(beam, offset, BLOCK_LEN, 2)
        return carry, times_conj(segment, table)

    _, products = lax.scan(beam_step, None, jnp.arange(local_blocks, dtype=jnp.int32))
    cross = lax.psum(products[..., :TAPS].sum(0), "tm")
    got = lax.all_to_all(products, "tm", 3, 0, tiled=True)

    def own_step(gram, q):
        offset = q * BLOCK_LEN
        table = lag_table(ref_ext, offset, LAGS)
        taps = table[:, :TAPS].transpose(1, 0, 2)
        mine = lax.dynamic_slice_in_dim(table, here * lags_local, lags_local, 1)
        return gram + times_conj(taps, table[:, :TAPS]), times_conj(taps, mine)

    start = jnp.zeros((TAPS, 2, TAPS), jnp.float32)
    gram, own = lax.scan(own_step, start, jnp.arange(samples // BLOCK_LEN, dtype=jnp.int32))
    g_real, g_imag = gram[:, 0].T, gram[:, 1].T
    system = jnp.concatenate([jnp.concatenate([g_real, -g_imag], 1), jnp.concatenate([g_imag, g_real], 1)], 0)
    right = jnp.concatenate([cross[:, 0].T, cross[:, 1].T], 0)
    solved = jax.scipy.linalg.cho_solve((jnp.linalg.cholesky(system), True), right)
    b_real, b_imag = solved[:TAPS].T, solved[TAPS:].T
    mixing = jnp.concatenate([jnp.stack([b_real, b_imag], 1), jnp.stack([-b_imag, b_real], 1)], 2)
    stacked = jnp.concatenate([own[:, :, 0], own[:, :, 1]], 1)
    lagged = got - jnp.einsum("mck,qkl->qmcl", mixing, stacked, precision=HIGHEST)
    wave = jnp.asarray(doppler_table(samples // BLOCK_LEN, 0.125 / math.sqrt(samples)))
    wave = wave.reshape(2, samples // BLOCK_LEN, 2, DOPPLER)
    return jnp.einsum("qmcl,cqdk->mdlk", lagged, wave, precision=HIGHEST)


def on_device(ref_signal, surveillance, steering):
    chan_count, tm_count = lax.axis_size("chan"), lax.axis_size("tm")
    beams_local = steering.shape[1] // chan_count
    lags_local = LAGS // tm_count
    fills = (
        LANES % lags_local == 0
        and lags_local % (2 * SUBLANES) == 0
        and beams_local * lags_local == LANES * SUBLANES // 2
        and chan_count > 1
        and chan_count & (chan_count - 1) == 0
        and tm_count & (tm_count - 1) == 0
        and 2 * surveillance.shape[1] % LANES == 0
        and surveillance.shape[2] % (4 * BLOCK_LEN) == 0
    )
    device = tiled_device if fills else plain_device
    return device(ref_signal, surveillance, steering)


def solution(mesh):
    placed = (P(None, "tm"), P(None, "chan", "tm"), P(None, None, "chan"))
    return jax.shard_map(
        on_device,
        mesh=mesh,
        in_specs=placed,
        out_specs=P("chan", None, "tm", None),
        check_vma=False,
    )
```

```python
import functools
import math

import jax
import jax.numpy as jnp
import numpy as np
from jax import lax
from jax.experimental import pallas as pl
from jax.experimental.pallas import tpu as pltpu
from jax.sharding import PartitionSpec as P

LAGS = 256
DOPPLER = 256
TAPS = 64
BLOCK_LEN = 256
LANES = 128
SUBLANES = 8

HIGHEST = lax.Precision.HIGHEST
VMEM_BYTES = 48 * 1024 * 1024


def params():
    return pltpu.CompilerParams(vmem_limit_bytes=VMEM_BYTES)


def halves(x):
    high = x.astype(jnp.bfloat16)
    return high, (x - high.astype(jnp.float32)).astype(jnp.bfloat16)


def dot_nt(a, b, precision=None):
    return lax.dot_general(
        a, b, (((1,), (1,)), ((), ())), precision=precision, preferred_element_type=jnp.float32
    )


def dot_split(a, b):
    (a_high, a_low), (b_high, b_low) = a, b
    left = jnp.concatenate([a_high, a_low], 1)
    right = jnp.concatenate([b_high, b_high], 0)
    return jnp.dot(left, right, preferred_element_type=jnp.float32) + jnp.dot(
        a_high, b_low, preferred_element_type=jnp.float32
    )


def row_sign(shape):
    rows = lax.broadcasted_iota(jnp.int32, shape, 0)
    return jnp.where(rows % SUBLANES < SUBLANES // 2, 1.0, -1.0).astype(jnp.float32)


def lane_sign(shape):
    lanes = lax.broadcasted_iota(jnp.int32, shape, 1)
    return jnp.where(lanes % LANES < LANES // 2, 1.0, -1.0).astype(jnp.float32)


def swap_groups(rows, groups):
    width = LANES // groups
    lane_group = lax.broadcasted_iota(jnp.int32, rows[0].shape, 1) // width
    outs = []
    for j in range(groups):
        out = rows[j]
        for i in range(groups):
            if i != j:
                moved = pltpu.roll(rows[i], (width * (i - j)) % LANES, 1)
                out = jnp.where(lane_group == i, moved, out)
        outs.append(out)
    return outs


def beam_kernel(parity, chan_count, beams_local, w_ref, s_ref, out_ref):
    me = lax.axis_index("chan")
    half = SUBLANES // 2
    sub = lax.broadcasted_iota(jnp.int32, (SUBLANES, w_ref.shape[2]), 0)
    top = sub < half
    rows = []
    for e in range(parity, chan_count, 2):
        base = (me ^ e) * beams_local
        for tile in range(beams_local // SUBLANES):
            start = pl.multiple_of(base + tile * SUBLANES, SUBLANES)
            wr = w_ref[0, pl.ds(start, SUBLANES), :]
            wi = w_ref[1, pl.ds(start, SUBLANES), :]
            wr_s = pltpu.roll(wr, half, 0)
            wi_s = pltpu.roll(wi, half, 0)
            first = [jnp.where(top, wr, wi_s), jnp.where(top, -wi, wr_s)]
            second = [jnp.where(top, wr_s, wi), jnp.where(top, -wi_s, wr)]
            rows.append(jnp.concatenate(first, 1))
            rows.append(jnp.concatenate(second, 1))
    weights = jnp.concatenate(rows, 0)
    out_ref[...] = dot_split(halves(weights), halves(s_ref[...]))


def beam_call(steering, survey, parity, chan_count, beams_local):
    depth, length = survey.shape
    rows = chan_count * beams_local
    steps = 4
    width = length // steps
    return pl.pallas_call(
        functools.partial(beam_kernel, parity, chan_count, beams_local),
        grid=(steps,),
        in_specs=[
            pl.BlockSpec(steering.shape, lambda i: (0, 0, 0)),
            pl.BlockSpec((depth, width), lambda i: (0, i)),
        ],
        out_specs=pl.BlockSpec((rows, width), lambda i: (0, i)),
        out_shape=jax.ShapeDtypeStruct((rows, length), jnp.float32),
        compiler_params=pltpu.CompilerParams(vmem_limit_bytes=60 * 1024 * 1024),
        cost_estimate=pl.CostEstimate(
            flops=6 * rows * depth * length, bytes_accessed=4 * length * (depth + rows), transcendentals=0
        ),
        name="beams_kept" if parity == 0 else "beams_sent",
    )(steering, survey)


def table_kernel(ref_ref, out_ref):
    me = lax.axis_index("tm")
    edge = ref_ref[jnp.maximum(me - 1, 0), :, ref_ref.shape[2] - 2 * LANES :]
    edge = jnp.where(me > 0, edge, jnp.zeros_like(edge))
    span = jnp.concatenate([edge, ref_ref[me]], 1)
    for c in range(2):
        tiled = jnp.broadcast_to(span[c : c + 1], (LANES, span.shape[1]))
        shifted = pltpu.roll(tiled, 0, 1, stride=1, stride_axis=0)[:, LANES:]
        high, low = halves(shifted)
        out_ref[0, c] = high
        out_ref[1, c] = low


def table_call(ref_all):
    shape = (2, 2, LANES, LANES + ref_all.shape[2])
    return pl.pallas_call(
        table_kernel,
        out_shape=jax.ShapeDtypeStruct(shape, jnp.bfloat16),
        compiler_params=params(),
        cost_estimate=pl.CostEstimate(
            flops=8 * math.prod(shape), bytes_accessed=2 * math.prod(shape), transcendentals=0
        ),
        name="shifted_reference",
    )(ref_all)


def lag_kernel(groups, owners, *refs):
    *y_refs, table_ref, out_ref = refs
    y = y_refs[0][...]
    for y_ref in y_refs[1:]:
        y = y + y_ref[...]
    rows, length = y.shape
    blocks = length // BLOCK_LEN
    turned = jnp.concatenate(
        [pltpu.roll(y[r : r + SUBLANES], SUBLANES // 2, 0) for r in range(0, rows, SUBLANES)], 0
    )
    turned = turned * row_sign(turned.shape)
    y_high, y_low = halves(y)
    t_high, t_low = halves(turned)
    both = jnp.concatenate([y_high, y_low], 0)
    turned_both = jnp.concatenate([t_high, t_low], 0)
    taps_sum = None
    for q in range(blocks):
        near = slice(q * BLOCK_LEN + LANES, q * BLOCK_LEN + LANES + BLOCK_LEN)
        far = slice(q * BLOCK_LEN, (q + 1) * BLOCK_LEN)
        cols = slice(q * BLOCK_LEN, (q + 1) * BLOCK_LEN)
        tables = []
        for h in range(2):
            tables.append(
                jnp.concatenate(
                    [
                        jnp.concatenate([table_ref[h, 0, :, near], table_ref[h, 1, :, near]], 1),
                        jnp.concatenate([table_ref[h, 0, :, far], table_ref[h, 1, :, far]], 1),
                    ],
                    0,
                )
            )
        lhs = jnp.concatenate([both[:, cols], turned_both[:, cols]], 1)
        by_high = dot_nt(lhs, tables[0])
        by_low = dot_nt(lhs[:rows], tables[1])
        product = by_high[:rows] + (by_high[rows:] + by_low)
        taps = product[:, :LANES]
        taps_sum = taps if taps_sum is None else taps_sum + taps
        for h in range(LAGS // LANES):
            lanes = slice(h * LANES, (h + 1) * LANES)
            tiles = [product[r : r + SUBLANES, lanes] for r in range(0, rows, SUBLANES)]
            for j, tile in enumerate(swap_groups(tiles, groups)):
                out_ref[h * groups + j, q] = tile
    left = lax.broadcasted_iota(jnp.int32, (SUBLANES, LANES), 1) < TAPS
    for i in range(groups // 2):
        a = taps_sum[i * SUBLANES : (i + 1) * SUBLANES]
        other = i + groups // 2
        b = taps_sum[other * SUBLANES : (other + 1) * SUBLANES]
        tile = jnp.where(left, a, pltpu.roll(b, LANES - TAPS, 1))
        for owner in range(owners):
            out_ref[owner, blocks + i] = tile


def lag_call(ys, table, groups, owners):
    rows, length = ys[0].shape
    blocks = length // BLOCK_LEN
    shape = (owners, blocks + groups // 2, SUBLANES, LANES)
    return pl.pallas_call(
        functools.partial(lag_kernel, groups, owners),
        out_shape=jax.ShapeDtypeStruct(shape, jnp.float32),
        compiler_params=params(),
        cost_estimate=pl.CostEstimate(
            flops=12 * rows * LAGS * 2 * length,
            bytes_accessed=4 * math.prod(shape) + 2 * math.prod(table.shape),
            transcendentals=0,
        ),
        name="lag_products",
    )(*ys, table)


SHARES = 2
BATCH = 4


def own_kernel(lags_local, ref_ref, out_ref, tail_ref, span_ref, late_ref):
    me = lax.axis_index("tm")
    owners, _, length = ref_ref.shape
    samples = owners * length
    blocks = samples // BLOCK_LEN // SHARES
    first_block = lax.rem(lax.axis_index("chan"), SHARES) * blocks
    span_ref[:, :BLOCK_LEN] = jnp.zeros((2, BLOCK_LEN), jnp.float32)
    span_ref[:, BLOCK_LEN + samples :] = jnp.zeros((2, BLOCK_LEN), jnp.float32)
    for t in range(owners):
        span_ref[:, BLOCK_LEN + t * length : BLOCK_LEN + (t + 1) * length] = ref_ref[t]
    late_ref[...] = pltpu.roll(span_ref[...], me * lags_local, 1)

    def shifted(window, count):
        tiled = jnp.broadcast_to(window, (count, window.shape[1]))
        return pltpu.roll(tiled, 0, 1, stride=1, stride_axis=0)[:, LANES:]

    def pair_of(window, count):
        return jnp.concatenate([shifted(window[c : c + 1], count) for c in range(2)], 0)

    turn = lane_sign((lags_local, LANES))

    def step(n, total):
        start = pl.multiple_of((first_block + n * BATCH) * BLOCK_LEN, BLOCK_LEN) + BLOCK_LEN - LANES
        lanes = pl.ds(pl.multiple_of(start, LANES), BATCH * BLOCK_LEN + LANES)
        window, late = span_ref[:, lanes], late_ref[:, lanes]
        taps_high, taps_low = halves(pair_of(window, TAPS))
        pad = jnp.zeros((2 * SUBLANES - 2, BATCH * BLOCK_LEN), jnp.float32)
        lag_rows = jnp.concatenate([pair_of(late, lags_local), window[:, LANES:], pad], 0)
        lags_high, lags_low = halves(lag_rows)
        taps = jnp.concatenate([taps_high, taps_low], 0)
        lags = jnp.concatenate([lags_high, lags_low], 0)
        count = lag_rows.shape[0]
        for b in range(BATCH):
            cols = slice(b * BLOCK_LEN, (b + 1) * BLOCK_LEN)
            product = dot_nt(lags[:, cols], taps[:, cols])
            product = product[:count, :LANES] + (product[:count, LANES:] + product[count:, :LANES])
            by_real = product[:lags_local]
            by_imag = product[lags_local : 2 * lags_local]
            rows = pl.ds(pl.multiple_of((n * BATCH + b) * lags_local, lags_local), lags_local)
            out_ref[rows, :] = by_real + turn * pltpu.roll(by_imag, TAPS, 1)
            total = total + product[2 * lags_local : 2 * lags_local + SUBLANES]
        return total

    total = lax.fori_loop(0, blocks // BATCH, step, jnp.zeros((SUBLANES, LANES), jnp.float32))
    out_ref[blocks * lags_local :, :] = total
    tail = pair_of(span_ref[:, samples + BLOCK_LEN - LANES :], TAPS)
    tail_ref[...] = dot_nt(tail, tail, HIGHEST)


def own_call(ref_all, lags_local):
    samples = ref_all.shape[0] * ref_all.shape[2]
    rows = samples // BLOCK_LEN // SHARES * lags_local
    return pl.pallas_call(
        functools.partial(own_kernel, lags_local),
        out_shape=[
            jax.ShapeDtypeStruct((rows + SUBLANES, 2 * TAPS), jnp.float32),
            jax.ShapeDtypeStruct((2 * TAPS, 2 * TAPS), jnp.float32),
        ],
        scratch_shapes=[pltpu.VMEM((2, samples + 2 * BLOCK_LEN), jnp.float32)] * 2,
        compiler_params=params(),
        cost_estimate=pl.CostEstimate(
            flops=24 * rows * BLOCK_LEN * 2 * TAPS, bytes_accessed=4 * rows * 2 * TAPS, transcendentals=0
        ),
        name="reference_products",
    )(ref_all)


def as_factor(a):
    return jnp.concatenate([a, -lane_sign(a.shape) * pltpu.roll(a, a.shape[0], 1)], 0)


def solver_kernel(mine_ref, other_ref, tail_ref, gram_ref, solver_ref):
    total = mine_ref[...] + other_ref[...]
    line = total[0:1] + lane_sign((1, LANES)) * pltpu.roll(total[1:2], TAPS, 1)
    low = lax.broadcasted_iota(jnp.int32, (1, LANES), 1) < TAPS
    line_r = jnp.where(low, line, 0.0)
    line_i = jnp.where(low, pltpu.roll(line, TAPS, 1), 0.0)
    cols = lax.broadcasted_iota(jnp.int32, (TAPS, TAPS), 1)
    rows = lax.broadcasted_iota(jnp.int32, (TAPS, TAPS), 0)
    above = cols > rows

    def upper(x):
        spread = pltpu.roll(jnp.broadcast_to(x, (TAPS, LANES)), 0, 1, stride=1, stride_axis=0)
        return spread[:, :TAPS]

    up_r = upper(line_r)
    up_i = jnp.where(above, upper(line_i), 0.0)
    strict_r = jnp.where(above, up_r, 0.0)
    diag_r = jnp.where(cols == rows, up_r, 0.0)
    tails = tail_ref[...]
    gram_r = strict_r + strict_r.T + diag_r - (tails[:TAPS, :TAPS] + tails[TAPS:, TAPS:])
    gram_i = up_i - up_i.T - (tails[:TAPS, TAPS:] - tails[TAPS:, :TAPS])
    gram = jnp.concatenate([gram_r, gram_i], 1)
    gram_factor = as_factor(gram)
    gram_ref[...] = gram_factor
    gram_halves = halves(gram_factor)
    one = (
        lax.broadcasted_iota(jnp.int32, gram.shape, 0) == lax.broadcasted_iota(jnp.int32, gram.shape, 1)
    ).astype(jnp.float32)
    bound = jnp.max(jnp.sum(jnp.abs(gram), axis=1, keepdims=True), axis=0, keepdims=True)

    def again(state):
        count, left, _ = state
        return (count < 60) & (left > 1e-3)

    def newton(state):
        count, _, x = state
        x_halves = halves(x)
        seen = dot_split(x_halves, gram_halves)
        left = jnp.max(jnp.abs(seen - one))
        x = 2.0 * x - dot_split(halves(seen), halves(as_factor(x)))
        return count + 1, left, x

    start = (jnp.int32(0), jnp.float32(1.0), one * (1.0 / bound))
    _, _, inverse = lax.while_loop(again, newton, start)
    solver_ref[...] = as_factor(inverse)


def solver_call(mine, other, tail):
    last = mine.shape[0] // SUBLANES - 1
    line = pl.BlockSpec((SUBLANES, LANES), lambda i: (last, 0))
    whole = pl.BlockSpec(tail.shape, lambda i: (0, 0))
    return pl.pallas_call(
        solver_kernel,
        grid=(1,),
        in_specs=[line, line, whole],
        out_specs=[whole, whole],
        out_shape=[jax.ShapeDtypeStruct(tail.shape, jnp.float32)] * 2,
        compiler_params=params(),
        cost_estimate=pl.CostEstimate(flops=500_000_000, bytes_accessed=200_000, transcendentals=0),
        name="gram_inverse",
    )(mine, other, tail)


def doppler_table(block_count, scale):
    phase = (np.arange(block_count)[:, None] * np.arange(DOPPLER)[None, :] % DOPPLER) * (2.0 * math.pi / DOPPLER)
    cosine, sine = np.cos(phase), np.sin(phase)
    upper = np.concatenate([cosine, -sine], 1)
    lower = np.concatenate([sine, cosine], 1)
    return (np.concatenate([upper, lower], 0) * scale).astype(np.float32)


def map_kernel(groups, got_ref, mine_ref, other_ref, gram_ref, solver_ref, wave_ref, out_ref, held_ref):
    owners, pieces = got_ref.shape[:2]
    blocks = pieces - groups // 2
    lags_local = LANES // groups
    total = owners * blocks
    left = lax.broadcasted_iota(jnp.int32, (SUBLANES, LANES), 1) < TAPS
    sign = row_sign((SUBLANES, LANES))
    rows = [None] * groups
    for i in range(groups // 2):
        tile = got_ref[0, blocks + i]
        for owner in range(1, owners):
            tile = tile + got_ref[owner, blocks + i]
        swapped = pltpu.roll(tile, TAPS, 1)
        for part, here, there in ((i, tile, swapped), (i + groups // 2, swapped, tile)):
            other = -sign * pltpu.roll(there, SUBLANES // 2, 0)
            rows[part] = jnp.where(left, here, other)
    cross = jnp.concatenate(rows, 0)
    solver = solver_ref[...]
    taps = jnp.dot(cross, solver, precision=HIGHEST, preferred_element_type=jnp.float32)
    rest = cross - jnp.dot(taps, gram_ref[...], precision=HIGHEST, preferred_element_type=jnp.float32)
    taps = taps + jnp.dot(rest, solver, precision=HIGHEST, preferred_element_type=jnp.float32)
    taps_high, taps_low = halves(taps)
    taps_both = jnp.concatenate([taps_high, taps_low], 1)
    share = lax.rem(lax.axis_index("chan"), SHARES)
    share_blocks = total // SHARES
    for which, own_ref in enumerate((mine_ref, other_ref)):
        first = (share ^ which) * share_blocks
        for q in range(0, share_blocks, 2 * groups):
            own_high, own_low = halves(own_ref[q * lags_local : (q + 2 * groups) * lags_local, :])
            clutter = dot_nt(taps_both, jnp.concatenate([own_high, own_high], 1)) + dot_nt(taps_high, own_low)
            for h in range(2):
                lanes = slice(h * LANES, (h + 1) * LANES)
                tiles = [clutter[r : r + SUBLANES, lanes] for r in range(0, groups * SUBLANES, SUBLANES)]
                for j, tile in enumerate(swap_groups(tiles, groups)):
                    at = first + q + h * groups + j
                    here = pl.ds(pl.multiple_of(at * SUBLANES, SUBLANES), SUBLANES)
                    held_ref[here, :] = got_ref[at // blocks, at % blocks] - tile
    half = SUBLANES // 2
    wave = (wave_ref[0], wave_ref[1])
    for g in range(half):
        parts = [held_ref[pl.ds(c * half + g, total, stride=SUBLANES), :] for c in range(2)]
        spectrum = dot_split(halves(jnp.concatenate(parts, 0).T), wave)
        for i in range(groups):
            for c in range(2):
                out_ref[half * i + g, c] = spectrum[
                    i * lags_local : (i + 1) * lags_local, c * DOPPLER : (c + 1) * DOPPLER
                ]


def map_call(got, mine, other, gram, solver, wave, groups, beams_local):
    total = got.shape[0] * (got.shape[1] - groups // 2)
    lags_local = LANES // groups
    shape = (beams_local, 2, lags_local, DOPPLER)
    return pl.pallas_call(
        functools.partial(map_kernel, groups),
        out_shape=jax.ShapeDtypeStruct(shape, jnp.float32),
        scratch_shapes=[pltpu.VMEM((total * SUBLANES, LANES), jnp.float32)],
        compiler_params=params(),
        cost_estimate=pl.CostEstimate(
            flops=12 * math.prod(shape) * total, bytes_accessed=4 * math.prod(shape), transcendentals=0
        ),
        name="range_doppler",
    )(got, mine, other, gram, solver, wave)


def swap(x, axis, by):
    pairs = [(i, i ^ by) for i in range(lax.axis_size(axis))]
    return lax.ppermute(x, axis, pairs)


def tiled_device(ref_signal, surveillance, steering):
    chan_count, tm_count = lax.axis_size("chan"), lax.axis_size("tm")
    channels, length = surveillance.shape[1:]
    beams_local = steering.shape[1] // chan_count
    lags_local = LAGS // tm_count
    groups = LANES // lags_local
    samples = length * tm_count

    ref_all = lax.all_to_all(
        jnp.broadcast_to(ref_signal[None], (tm_count,) + ref_signal.shape), "tm", 0, 0, tiled=True
    )
    survey = surveillance.reshape(2 * channels, length)
    rows = 2 * beams_local
    shape = (chan_count // 2, rows, length)
    moved = swap(beam_call(steering, survey, 1, chan_count, beams_local), "chan", 1)
    parts = [beam_call(steering, survey, 0, chan_count, beams_local).reshape(shape), moved.reshape(shape)]
    by = 2
    while by < chan_count:
        sent = parts[0][1::2]
        for part in parts[1:]:
            sent = sent + part[1::2]
        ref_all, sent = lax.optimization_barrier((ref_all, sent))
        parts = [part[::2] for part in parts] + [swap(sent, "chan", by)]
        by *= 2
    mine, tail = own_call(ref_all, lags_local)
    table = table_call(ref_all)
    pieces = lag_call([part[0] for part in parts], table, groups, tm_count)
    got = lax.all_to_all(pieces, "tm", 0, 0, tiled=True)
    other = swap(mine, "chan", 1)
    gram, solver = solver_call(mine, other, tail)
    wave = doppler_table(samples // BLOCK_LEN, 0.125 / math.sqrt(samples))
    high = wave.astype(jnp.bfloat16)
    wave = np.stack([high, (wave - high.astype(np.float32)).astype(jnp.bfloat16)])
    return map_call(got, mine, other, gram, solver, jnp.asarray(wave), groups, beams_local)


def lag_table(ref_ext, offset, lags):
    window = lax.dynamic_slice_in_dim(ref_ext, offset, BLOCK_LEN + LAGS, 1)
    span = BLOCK_LEN + LAGS
    tiled = jnp.tile(jnp.pad(window, ((0, 0), (0, 1))), (1, lags))[:, : lags * span]
    return tiled.reshape(2, lags, span)[:, :, LAGS:]


def times_conj(a, b):
    real = jnp.einsum("...t,lt->...l", a[..., 0, :], b[0], precision=HIGHEST) + jnp.einsum(
        "...t,lt->...l", a[..., 1, :], b[1], precision=HIGHEST
    )
    imag = jnp.einsum("...t,lt->...l", a[..., 1, :], b[0], precision=HIGHEST) - jnp.einsum(
        "...t,lt->...l", a[..., 0, :], b[1], precision=HIGHEST
    )
    return jnp.stack([real, imag], -2)


def plain_device(ref_signal, surveillance, steering):
    chan_count, tm_count = lax.axis_size("chan"), lax.axis_size("tm")
    length = surveillance.shape[2]
    beams = steering.shape[1]
    lags_local = LAGS // tm_count
    samples = length * tm_count
    local_blocks = length // BLOCK_LEN
    here = lax.axis_index("tm")

    w_real, w_imag = steering
    real = jnp.dot(w_real, surveillance[0], precision=HIGHEST) - jnp.dot(w_imag, surveillance[1], precision=HIGHEST)
    imag = jnp.dot(w_imag, surveillance[0], precision=HIGHEST) + jnp.dot(w_real, surveillance[1], precision=HIGHEST)
    beam = lax.psum_scatter(jnp.stack([real, imag], 1), "chan", scatter_dimension=0, tiled=True)
    ref_all = lax.all_gather(ref_signal, "tm", axis=1, tiled=True)
    ref_ext = jnp.pad(ref_all, ((0, 0), (LAGS, 0)))

    def beam_step(carry, q):
        offset = q * BLOCK_LEN
        table = lag_table(ref_ext, here * length + offset, LAGS)
        segment = lax.dynamic_slice_in_dim(beam, offset, BLOCK_LEN, 2)
        return carry, times_conj(segment, table)

    _, products = lax.scan(beam_step, None, jnp.arange(local_blocks, dtype=jnp.int32))
    cross = lax.psum(products[..., :TAPS].sum(0), "tm")
    got = lax.all_to_all(products, "tm", 3, 0, tiled=True)

    def own_step(gram, q):
        offset = q * BLOCK_LEN
        table = lag_table(ref_ext, offset, LAGS)
        taps = table[:, :TAPS].transpose(1, 0, 2)
        mine = lax.dynamic_slice_in_dim(table, here * lags_local, lags_local, 1)
        return gram + times_conj(taps, table[:, :TAPS]), times_conj(taps, mine)

    start = jnp.zeros((TAPS, 2, TAPS), jnp.float32)
    gram, own = lax.scan(own_step, start, jnp.arange(samples // BLOCK_LEN, dtype=jnp.int32))
    g_real, g_imag = gram[:, 0].T, gram[:, 1].T
    system = jnp.concatenate([jnp.concatenate([g_real, -g_imag], 1), jnp.concatenate([g_imag, g_real], 1)], 0)
    right = jnp.concatenate([cross[:, 0].T, cross[:, 1].T], 0)
    solved = jax.scipy.linalg.cho_solve((jnp.linalg.cholesky(system), True), right)
    b_real, b_imag = solved[:TAPS].T, solved[TAPS:].T
    mixing = jnp.concatenate([jnp.stack([b_real, b_imag], 1), jnp.stack([-b_imag, b_real], 1)], 2)
    stacked = jnp.concatenate([own[:, :, 0], own[:, :, 1]], 1)
    lagged = got - jnp.einsum("mck,qkl->qmcl", mixing, stacked, precision=HIGHEST)
    wave = jnp.asarray(doppler_table(samples // BLOCK_LEN, 0.125 / math.sqrt(samples)))
    wave = wave.reshape(2, samples // BLOCK_LEN, 2, DOPPLER)
    return jnp.einsum("qmcl,cqdk->mdlk", lagged, wave, precision=HIGHEST)


def on_device(ref_signal, surveillance, steering):
    chan_count, tm_count = lax.axis_size("chan"), lax.axis_size("tm")
    beams_local = steering.shape[1] // chan_count
    lags_local = LAGS // tm_count
    fills = (
        LANES % lags_local == 0
        and lags_local % (2 * SUBLANES) == 0
        and beams_local * lags_local == LANES * SUBLANES // 2
        and chan_count > 1
        and chan_count & (chan_count - 1) == 0
        and tm_count & (tm_count - 1) == 0
        and 2 * surveillance.shape[1] % LANES == 0
        and surveillance.shape[2] % (4 * BLOCK_LEN) == 0
    )
    device = tiled_device if fills else plain_device
    return device(ref_signal, surveillance, steering)


def solution(mesh):
    placed = (P(None, "tm"), P(None, "chan", "tm"), P(None, None, "chan"))
    return jax.shard_map(
        on_device,
        mesh=mesh,
        in_specs=placed,
        out_specs=P("chan", None, "tm", None),
        check_vma=False,
    )
```

```python
import functools
import math

import jax
import jax.numpy as jnp
import numpy as np
from jax import lax
from jax.experimental import pallas as pl
from jax.experimental.pallas import tpu as pltpu
from jax.sharding import PartitionSpec as P

LAGS = 256
DOPPLER = 256
TAPS = 64
BLOCK_LEN = 256
LANES = 128
SUBLANES = 8

HIGHEST = lax.Precision.HIGHEST
VMEM_BYTES = 48 * 1024 * 1024


def params():
    return pltpu.CompilerParams(vmem_limit_bytes=VMEM_BYTES)


def halves(x):
    high = x.astype(jnp.bfloat16)
    return high, (x - high.astype(jnp.float32)).astype(jnp.bfloat16)


def dot_nt(a, b, precision=None):
    return lax.dot_general(
        a, b, (((1,), (1,)), ((), ())), precision=precision, preferred_element_type=jnp.float32
    )


def dot_split(a, b):
    (a_high, a_low), (b_high, b_low) = a, b
    left = jnp.concatenate([a_high, a_low], 1)
    right = jnp.concatenate([b_high, b_high], 0)
    return jnp.dot(left, right, preferred_element_type=jnp.float32) + jnp.dot(
        a_high, b_low, preferred_element_type=jnp.float32
    )


def row_sign(shape):
    rows = lax.broadcasted_iota(jnp.int32, shape, 0)
    return jnp.where(rows % SUBLANES < SUBLANES // 2, 1.0, -1.0).astype(jnp.float32)


def lane_sign(shape):
    lanes = lax.broadcasted_iota(jnp.int32, shape, 1)
    return jnp.where(lanes % LANES < LANES // 2, 1.0, -1.0).astype(jnp.float32)


def swap_groups(rows, groups):
    width = LANES // groups
    lane_group = lax.broadcasted_iota(jnp.int32, rows[0].shape, 1) // width
    outs = []
    for j in range(groups):
        out = rows[j]
        for i in range(groups):
            if i != j:
                moved = pltpu.roll(rows[i], (width * (i - j)) % LANES, 1)
                out = jnp.where(lane_group == i, moved, out)
        outs.append(out)
    return outs


CHUNKS = 4


def beam_kernel(
    chan_count, beams_local, w_hbm, s_hbm, ref_hbm, kept_ref, sent_ref, spread_hbm, w_ref, s_ref, w_sem, s_sem, ref_sem
):
    me = lax.axis_index("chan")
    depth, length = s_hbm.shape
    width = length // CHUNKS
    w_copy = pltpu.make_async_copy(w_hbm, w_ref, w_sem)
    w_copy.start()
    s_copies = []
    for n in range(CHUNKS):
        cols = pl.ds(n * width, width)
        s_copies.append(pltpu.make_async_copy(s_hbm.at[:, cols], s_ref.at[:, cols], s_sem.at[n]))
        s_copies[n].start()
    ref_copies = []
    for n in range(spread_hbm.shape[0]):
        ref_copies.append(pltpu.make_async_copy(ref_hbm, spread_hbm.at[n], ref_sem.at[n]))
        ref_copies[n].start()
    half = SUBLANES // 2
    sub = lax.broadcasted_iota(jnp.int32, (SUBLANES, w_hbm.shape[2]), 0)
    top = sub < half
    w_copy.wait()
    rows = []
    for parity in range(2):
        for e in range(parity, chan_count, 2):
            base = (me ^ e) * beams_local
            for tile in range(beams_local // SUBLANES):
                start = pl.multiple_of(base + tile * SUBLANES, SUBLANES)
                wr = w_ref[0, pl.ds(start, SUBLANES), :]
                wi = w_ref[1, pl.ds(start, SUBLANES), :]
                wr_s = pltpu.roll(wr, half, 0)
                wi_s = pltpu.roll(wi, half, 0)
                first = [jnp.where(top, wr, wi_s), jnp.where(top, -wi, wr_s)]
                second = [jnp.where(top, wr_s, wi), jnp.where(top, -wi_s, wr)]
                rows.append(jnp.concatenate(first, 1))
                rows.append(jnp.concatenate(second, 1))
    weights = halves(jnp.concatenate(rows, 0))
    mid = weights[0].shape[0] // 2
    for n in range(CHUNKS):
        cols = slice(n * width, (n + 1) * width)
        s_copies[n].wait()
        product = dot_split(weights, halves(s_ref[:, cols]))
        kept_ref[:, cols] = product[:mid]
        sent_ref[:, cols] = product[mid:]
    for copy in ref_copies:
        copy.wait()


def beam_call(steering, survey, ref, owners, chan_count, beams_local):
    depth, length = survey.shape
    rows = chan_count * beams_local
    out = jax.ShapeDtypeStruct((rows, length), jnp.float32)
    hbm = pl.BlockSpec(memory_space=pltpu.HBM)
    vmem = pl.BlockSpec(memory_space=pltpu.VMEM)
    return pl.pallas_call(
        functools.partial(beam_kernel, chan_count, beams_local),
        in_specs=[hbm, hbm, hbm],
        out_specs=[vmem, vmem, hbm],
        out_shape=[out, out, jax.ShapeDtypeStruct((owners,) + ref.shape, jnp.float32)],
        scratch_shapes=[
            pltpu.VMEM(steering.shape, jnp.float32),
            pltpu.VMEM(survey.shape, jnp.float32),
            pltpu.SemaphoreType.DMA,
            pltpu.SemaphoreType.DMA((CHUNKS,)),
            pltpu.SemaphoreType.DMA((owners,)),
        ],
        compiler_params=params(),
        cost_estimate=pl.CostEstimate(
            flops=12 * rows * depth * length, bytes_accessed=4 * length * (depth + 2 * rows), transcendentals=0
        ),
        name="beams",
    )(*(pltpu.with_memory_space_constraint(x, pltpu.HBM) for x in (steering, survey, ref)))


def table_kernel(ref_ref, out_ref):
    me = lax.axis_index("tm")
    edge = ref_ref[jnp.maximum(me - 1, 0), :, ref_ref.shape[2] - 2 * LANES :]
    edge = jnp.where(me > 0, edge, jnp.zeros_like(edge))
    span = jnp.concatenate([edge, ref_ref[me]], 1)
    for c in range(2):
        tiled = jnp.broadcast_to(span[c : c + 1], (LANES, span.shape[1]))
        shifted = pltpu.roll(tiled, 0, 1, stride=1, stride_axis=0)[:, LANES:]
        high, low = halves(shifted)
        out_ref[0, c] = high
        out_ref[1, c] = low


def table_call(ref_all):
    shape = (2, 2, LANES, LANES + ref_all.shape[2])
    return pl.pallas_call(
        table_kernel,
        out_shape=jax.ShapeDtypeStruct(shape, jnp.bfloat16),
        compiler_params=params(),
        cost_estimate=pl.CostEstimate(
            flops=8 * math.prod(shape), bytes_accessed=2 * math.prod(shape), transcendentals=0
        ),
        name="shifted_reference",
    )(ref_all)


def lag_kernel(groups, owners, *refs):
    *y_refs, table_ref, out_hbm, out_ref, out_sem = refs
    copies = []

    def send(first, count):
        part = (slice(None), pl.ds(first, count))
        copies.append(pltpu.make_async_copy(out_ref.at[part], out_hbm.at[part], out_sem.at[len(copies)]))
        copies[-1].start()

    y = y_refs[0][...]
    for y_ref in y_refs[1:]:
        y = y + y_ref[...]
    rows, length = y.shape
    blocks = length // BLOCK_LEN
    turned = jnp.concatenate(
        [pltpu.roll(y[r : r + SUBLANES], SUBLANES // 2, 0) for r in range(0, rows, SUBLANES)], 0
    )
    turned = turned * row_sign(turned.shape)
    y_high, y_low = halves(y)
    t_high, t_low = halves(turned)
    both = jnp.concatenate([y_high, y_low], 0)
    turned_both = jnp.concatenate([t_high, t_low], 0)
    taps_sum = None
    for q in range(blocks):
        near = slice(q * BLOCK_LEN + LANES, q * BLOCK_LEN + LANES + BLOCK_LEN)
        far = slice(q * BLOCK_LEN, (q + 1) * BLOCK_LEN)
        cols = slice(q * BLOCK_LEN, (q + 1) * BLOCK_LEN)
        tables = []
        for h in range(2):
            tables.append(
                jnp.concatenate(
                    [
                        jnp.concatenate([table_ref[h, 0, :, near], table_ref[h, 1, :, near]], 1),
                        jnp.concatenate([table_ref[h, 0, :, far], table_ref[h, 1, :, far]], 1),
                    ],
                    0,
                )
            )
        lhs = jnp.concatenate([both[:, cols], turned_both[:, cols]], 1)
        by_high = dot_nt(lhs, tables[0])
        by_low = dot_nt(lhs[:rows], tables[1])
        product = by_high[:rows] + (by_high[rows:] + by_low)
        taps = product[:, :LANES]
        taps_sum = taps if taps_sum is None else taps_sum + taps
        for h in range(LAGS // LANES):
            lanes = slice(h * LANES, (h + 1) * LANES)
            tiles = [product[r : r + SUBLANES, lanes] for r in range(0, rows, SUBLANES)]
            for j, tile in enumerate(swap_groups(tiles, groups)):
                out_ref[h * groups + j, q] = tile
        if q % 2:
            send(q - 1, 2)
    left = lax.broadcasted_iota(jnp.int32, (SUBLANES, LANES), 1) < TAPS
    for i in range(groups // 2):
        a = taps_sum[i * SUBLANES : (i + 1) * SUBLANES]
        other = i + groups // 2
        b = taps_sum[other * SUBLANES : (other + 1) * SUBLANES]
        tile = jnp.where(left, a, pltpu.roll(b, LANES - TAPS, 1))
        for owner in range(owners):
            out_ref[owner, blocks + i] = tile
    send(blocks, groups // 2)
    for copy in copies:
        copy.wait()


def lag_call(ys, table, groups, owners):
    rows, length = ys[0].shape
    blocks = length // BLOCK_LEN
    shape = (owners, blocks + groups // 2, SUBLANES, LANES)
    return pl.pallas_call(
        functools.partial(lag_kernel, groups, owners),
        in_specs=[pl.BlockSpec(memory_space=pltpu.VMEM)] * (len(ys) + 1),
        out_specs=pl.BlockSpec(memory_space=pltpu.HBM),
        out_shape=jax.ShapeDtypeStruct(shape, jnp.float32),
        scratch_shapes=[pltpu.VMEM(shape, jnp.float32), pltpu.SemaphoreType.DMA((blocks // 2 + 1,))],
        compiler_params=params(),
        cost_estimate=pl.CostEstimate(
            flops=12 * rows * LAGS * 2 * length,
            bytes_accessed=4 * math.prod(shape) + 2 * math.prod(table.shape),
            transcendentals=0,
        ),
        name="lag_products",
    )(*ys, table)


SHARES = 2
BATCH = 4


def own_kernel(lags_local, ref_ref, out_ref, tail_ref, span_ref, late_ref):
    me = lax.axis_index("tm")
    owners, _, length = ref_ref.shape
    samples = owners * length
    blocks = samples // BLOCK_LEN // SHARES
    first_block = lax.rem(lax.axis_index("chan"), SHARES) * blocks
    span_ref[:, :BLOCK_LEN] = jnp.zeros((2, BLOCK_LEN), jnp.float32)
    span_ref[:, BLOCK_LEN + samples :] = jnp.zeros((2, BLOCK_LEN), jnp.float32)
    for t in range(owners):
        span_ref[:, BLOCK_LEN + t * length : BLOCK_LEN + (t + 1) * length] = ref_ref[t]
    late_ref[...] = pltpu.roll(span_ref[...], me * lags_local, 1)

    def shifted(window, count):
        tiled = jnp.broadcast_to(window, (count, window.shape[1]))
        return pltpu.roll(tiled, 0, 1, stride=1, stride_axis=0)[:, LANES:]

    def pair_of(window, count):
        return jnp.concatenate([shifted(window[c : c + 1], count) for c in range(2)], 0)

    turn = lane_sign((lags_local, LANES))

    def step(n, total):
        start = pl.multiple_of((first_block + n * BATCH) * BLOCK_LEN, BLOCK_LEN) + BLOCK_LEN - LANES
        lanes = pl.ds(pl.multiple_of(start, LANES), BATCH * BLOCK_LEN + LANES)
        window, late = span_ref[:, lanes], late_ref[:, lanes]
        taps_high, taps_low = halves(pair_of(window, TAPS))
        pad = jnp.zeros((2 * SUBLANES - 2, BATCH * BLOCK_LEN), jnp.float32)
        lag_rows = jnp.concatenate([pair_of(late, lags_local), window[:, LANES:], pad], 0)
        lags_high, lags_low = halves(lag_rows)
        taps = jnp.concatenate([taps_high, taps_low], 0)
        lags = jnp.concatenate([lags_high, lags_low], 0)
        count = lag_rows.shape[0]
        for b in range(BATCH):
            cols = slice(b * BLOCK_LEN, (b + 1) * BLOCK_LEN)
            product = dot_nt(lags[:, cols], taps[:, cols])
            product = product[:count, :LANES] + (product[:count, LANES:] + product[count:, :LANES])
            by_real = product[:lags_local]
            by_imag = product[lags_local : 2 * lags_local]
            rows = pl.ds(pl.multiple_of((n * BATCH + b) * lags_local, lags_local), lags_local)
            out_ref[rows, :] = by_real + turn * pltpu.roll(by_imag, TAPS, 1)
            total = total + product[2 * lags_local : 2 * lags_local + SUBLANES]
        return total

    total = lax.fori_loop(0, blocks // BATCH, step, jnp.zeros((SUBLANES, LANES), jnp.float32))
    out_ref[blocks * lags_local :, :] = total
    tail = pair_of(span_ref[:, samples + BLOCK_LEN - LANES :], TAPS)
    tail_ref[...] = dot_nt(tail, tail, HIGHEST)


def own_call(ref_all, lags_local):
    samples = ref_all.shape[0] * ref_all.shape[2]
    rows = samples // BLOCK_LEN // SHARES * lags_local
    return pl.pallas_call(
        functools.partial(own_kernel, lags_local),
        out_shape=[
            jax.ShapeDtypeStruct((rows + SUBLANES, 2 * TAPS), jnp.float32),
            jax.ShapeDtypeStruct((2 * TAPS, 2 * TAPS), jnp.float32),
        ],
        scratch_shapes=[pltpu.VMEM((2, samples + 2 * BLOCK_LEN), jnp.float32)] * 2,
        compiler_params=params(),
        cost_estimate=pl.CostEstimate(
            flops=24 * rows * BLOCK_LEN * 2 * TAPS, bytes_accessed=4 * rows * 2 * TAPS, transcendentals=0
        ),
        name="reference_products",
    )(ref_all)


def as_factor(a):
    return jnp.concatenate([a, -lane_sign(a.shape) * pltpu.roll(a, a.shape[0], 1)], 0)


def solver_kernel(mine_ref, other_ref, tail_ref, gram_ref, solver_ref):
    total = mine_ref[...] + other_ref[...]
    line = total[0:1] + lane_sign((1, LANES)) * pltpu.roll(total[1:2], TAPS, 1)
    low = lax.broadcasted_iota(jnp.int32, (1, LANES), 1) < TAPS
    line_r = jnp.where(low, line, 0.0)
    line_i = jnp.where(low, pltpu.roll(line, TAPS, 1), 0.0)
    cols = lax.broadcasted_iota(jnp.int32, (TAPS, TAPS), 1)
    rows = lax.broadcasted_iota(jnp.int32, (TAPS, TAPS), 0)
    above = cols > rows

    def upper(x):
        spread = pltpu.roll(jnp.broadcast_to(x, (TAPS, LANES)), 0, 1, stride=1, stride_axis=0)
        return spread[:, :TAPS]

    up_r = upper(line_r)
    up_i = jnp.where(above, upper(line_i), 0.0)
    strict_r = jnp.where(above, up_r, 0.0)
    diag_r = jnp.where(cols == rows, up_r, 0.0)
    tails = tail_ref[...]
    gram_r = strict_r + strict_r.T + diag_r - (tails[:TAPS, :TAPS] + tails[TAPS:, TAPS:])
    gram_i = up_i - up_i.T - (tails[:TAPS, TAPS:] - tails[TAPS:, :TAPS])
    gram = jnp.concatenate([gram_r, gram_i], 1)
    gram_factor = as_factor(gram)
    gram_ref[...] = gram_factor
    gram_halves = halves(gram_factor)
    one = (
        lax.broadcasted_iota(jnp.int32, gram.shape, 0) == lax.broadcasted_iota(jnp.int32, gram.shape, 1)
    ).astype(jnp.float32)
    bound = jnp.max(jnp.sum(jnp.abs(gram), axis=1, keepdims=True), axis=0, keepdims=True)

    def again(state):
        count, left, _ = state
        return (count < 60) & (left > 1e-3)

    def newton(state):
        count, _, x = state
        x_halves = halves(x)
        seen = dot_split(x_halves, gram_halves)
        left = jnp.max(jnp.abs(seen - one))
        x = 2.0 * x - dot_split(halves(seen), halves(as_factor(x)))
        return count + 1, left, x

    start = (jnp.int32(0), jnp.float32(1.0), one * (1.0 / bound))
    _, _, inverse = lax.while_loop(again, newton, start)
    solver_ref[...] = as_factor(inverse)


def solver_call(mine, other, tail):
    last = mine.shape[0] // SUBLANES - 1
    line = pl.BlockSpec((SUBLANES, LANES), lambda i: (last, 0))
    whole = pl.BlockSpec(tail.shape, lambda i: (0, 0))
    return pl.pallas_call(
        solver_kernel,
        grid=(1,),
        in_specs=[line, line, whole],
        out_specs=[whole, whole],
        out_shape=[jax.ShapeDtypeStruct(tail.shape, jnp.float32)] * 2,
        compiler_params=params(),
        cost_estimate=pl.CostEstimate(flops=500_000_000, bytes_accessed=200_000, transcendentals=0),
        name="gram_inverse",
    )(mine, other, tail)


def doppler_table(block_count, scale):
    phase = (np.arange(block_count)[:, None] * np.arange(DOPPLER)[None, :] % DOPPLER) * (2.0 * math.pi / DOPPLER)
    cosine, sine = np.cos(phase), np.sin(phase)
    upper = np.concatenate([cosine, -sine], 1)
    lower = np.concatenate([sine, cosine], 1)
    return (np.concatenate([upper, lower], 0) * scale).astype(np.float32)


def map_kernel(groups, got_ref, mine_ref, other_ref, gram_ref, solver_ref, wave_ref, out_hbm, held_ref, out_ref, out_sem):
    owners, pieces = got_ref.shape[:2]
    blocks = pieces - groups // 2
    lags_local = LANES // groups
    total = owners * blocks
    left = lax.broadcasted_iota(jnp.int32, (SUBLANES, LANES), 1) < TAPS
    sign = row_sign((SUBLANES, LANES))
    rows = [None] * groups
    for i in range(groups // 2):
        tile = got_ref[0, blocks + i]
        for owner in range(1, owners):
            tile = tile + got_ref[owner, blocks + i]
        swapped = pltpu.roll(tile, TAPS, 1)
        for part, here, there in ((i, tile, swapped), (i + groups // 2, swapped, tile)):
            other = -sign * pltpu.roll(there, SUBLANES // 2, 0)
            rows[part] = jnp.where(left, here, other)
    cross = jnp.concatenate(rows, 0)
    solver = solver_ref[...]
    taps = jnp.dot(cross, solver, precision=HIGHEST, preferred_element_type=jnp.float32)
    rest = cross - jnp.dot(taps, gram_ref[...], precision=HIGHEST, preferred_element_type=jnp.float32)
    taps = taps + jnp.dot(rest, solver, precision=HIGHEST, preferred_element_type=jnp.float32)
    taps_high, taps_low = halves(taps)
    taps_both = jnp.concatenate([taps_high, taps_low], 1)
    share = lax.rem(lax.axis_index("chan"), SHARES)
    share_blocks = total // SHARES
    for which, own_ref in enumerate((mine_ref, other_ref)):
        first = (share ^ which) * share_blocks
        for q in range(0, share_blocks, 2 * groups):
            own_high, own_low = halves(own_ref[q * lags_local : (q + 2 * groups) * lags_local, :])
            clutter = dot_nt(taps_both, jnp.concatenate([own_high, own_high], 1)) + dot_nt(taps_high, own_low)
            for h in range(2):
                lanes = slice(h * LANES, (h + 1) * LANES)
                tiles = [clutter[r : r + SUBLANES, lanes] for r in range(0, groups * SUBLANES, SUBLANES)]
                for j, tile in enumerate(swap_groups(tiles, groups)):
                    at = first + q + h * groups + j
                    here = pl.ds(pl.multiple_of(at * SUBLANES, SUBLANES), SUBLANES)
                    held_ref[here, :] = got_ref[at // blocks, at % blocks] - tile
    half = SUBLANES // 2
    wave = (wave_ref[0], wave_ref[1])
    copies = []
    for g in range(half):
        parts = [held_ref[pl.ds(c * half + g, total, stride=SUBLANES), :] for c in range(2)]
        spectrum = dot_split(halves(jnp.concatenate(parts, 0).T), wave)
        for i in range(groups):
            beam = half * i + g
            for c in range(2):
                out_ref[beam, c] = spectrum[i * lags_local : (i + 1) * lags_local, c * DOPPLER : (c + 1) * DOPPLER]
            copies.append(pltpu.make_async_copy(out_ref.at[beam], out_hbm.at[beam], out_sem.at[beam]))
            copies[-1].start()
    for copy in copies:
        copy.wait()


def map_call(got, mine, other, gram, solver, wave, groups, beams_local):
    total = got.shape[0] * (got.shape[1] - groups // 2)
    lags_local = LANES // groups
    shape = (beams_local, 2, lags_local, DOPPLER)
    return pl.pallas_call(
        functools.partial(map_kernel, groups),
        in_specs=[pl.BlockSpec(memory_space=pltpu.VMEM)] * 6,
        out_specs=pl.BlockSpec(memory_space=pltpu.HBM),
        out_shape=jax.ShapeDtypeStruct(shape, jnp.float32),
        scratch_shapes=[
            pltpu.VMEM((total * SUBLANES, LANES), jnp.float32),
            pltpu.VMEM(shape, jnp.float32),
            pltpu.SemaphoreType.DMA((beams_local,)),
        ],
        compiler_params=params(),
        cost_estimate=pl.CostEstimate(
            flops=12 * math.prod(shape) * total, bytes_accessed=4 * math.prod(shape), transcendentals=0
        ),
        name="range_doppler",
    )(got, mine, other, gram, solver, wave)


def swap(x, axis, by):
    pairs = [(i, i ^ by) for i in range(lax.axis_size(axis))]
    return lax.ppermute(x, axis, pairs)


def tiled_device(ref_signal, surveillance, steering):
    chan_count, tm_count = lax.axis_size("chan"), lax.axis_size("tm")
    channels, length = surveillance.shape[1:]
    beams_local = steering.shape[1] // chan_count
    lags_local = LAGS // tm_count
    groups = LANES // lags_local
    samples = length * tm_count

    survey = surveillance.reshape(2 * channels, length)
    kept, moved, spread = beam_call(steering, survey, ref_signal, tm_count, chan_count, beams_local)
    shape = (chan_count // 2, 2 * beams_local, length)
    parts = [kept.reshape(shape), swap(moved, "chan", 1).reshape(shape)]
    by = 2
    while by < chan_count:
        sent = parts[0][1::2]
        for part in parts[1:]:
            sent = sent + part[1::2]
        spread, sent = lax.optimization_barrier((spread, sent))
        parts = [part[::2] for part in parts] + [swap(sent, "chan", by)]
        by *= 2
    ref_all = lax.all_to_all(spread, "tm", 0, 0, tiled=True)
    table = table_call(ref_all)
    pieces = lag_call([part[0] for part in parts], table, groups, tm_count)
    ref_all, pieces = lax.optimization_barrier((ref_all, pieces))
    got = lax.all_to_all(pieces, "tm", 0, 0, tiled=True)
    mine, tail = own_call(ref_all, lags_local)
    other = swap(mine, "chan", 1)
    gram, solver = solver_call(mine, other, tail)
    wave = doppler_table(samples // BLOCK_LEN, 0.125 / math.sqrt(samples))
    high = wave.astype(jnp.bfloat16)
    wave = np.stack([high, (wave - high.astype(np.float32)).astype(jnp.bfloat16)])
    return map_call(got, mine, other, gram, solver, jnp.asarray(wave), groups, beams_local)


def lag_table(ref_ext, offset, lags):
    window = lax.dynamic_slice_in_dim(ref_ext, offset, BLOCK_LEN + LAGS, 1)
    span = BLOCK_LEN + LAGS
    tiled = jnp.tile(jnp.pad(window, ((0, 0), (0, 1))), (1, lags))[:, : lags * span]
    return tiled.reshape(2, lags, span)[:, :, LAGS:]


def times_conj(a, b):
    real = jnp.einsum("...t,lt->...l", a[..., 0, :], b[0], precision=HIGHEST) + jnp.einsum(
        "...t,lt->...l", a[..., 1, :], b[1], precision=HIGHEST
    )
    imag = jnp.einsum("...t,lt->...l", a[..., 1, :], b[0], precision=HIGHEST) - jnp.einsum(
        "...t,lt->...l", a[..., 0, :], b[1], precision=HIGHEST
    )
    return jnp.stack([real, imag], -2)


def plain_device(ref_signal, surveillance, steering):
    chan_count, tm_count = lax.axis_size("chan"), lax.axis_size("tm")
    length = surveillance.shape[2]
    beams = steering.shape[1]
    lags_local = LAGS // tm_count
    samples = length * tm_count
    local_blocks = length // BLOCK_LEN
    here = lax.axis_index("tm")

    w_real, w_imag = steering
    real = jnp.dot(w_real, surveillance[0], precision=HIGHEST) - jnp.dot(w_imag, surveillance[1], precision=HIGHEST)
    imag = jnp.dot(w_imag, surveillance[0], precision=HIGHEST) + jnp.dot(w_real, surveillance[1], precision=HIGHEST)
    beam = lax.psum_scatter(jnp.stack([real, imag], 1), "chan", scatter_dimension=0, tiled=True)
    ref_all = lax.all_gather(ref_signal, "tm", axis=1, tiled=True)
    ref_ext = jnp.pad(ref_all, ((0, 0), (LAGS, 0)))

    def beam_step(carry, q):
        offset = q * BLOCK_LEN
        table = lag_table(ref_ext, here * length + offset, LAGS)
        segment = lax.dynamic_slice_in_dim(beam, offset, BLOCK_LEN, 2)
        return carry, times_conj(segment, table)

    _, products = lax.scan(beam_step, None, jnp.arange(local_blocks, dtype=jnp.int32))
    cross = lax.psum(products[..., :TAPS].sum(0), "tm")
    got = lax.all_to_all(products, "tm", 3, 0, tiled=True)

    def own_step(gram, q):
        offset = q * BLOCK_LEN
        table = lag_table(ref_ext, offset, LAGS)
        taps = table[:, :TAPS].transpose(1, 0, 2)
        mine = lax.dynamic_slice_in_dim(table, here * lags_local, lags_local, 1)
        return gram + times_conj(taps, table[:, :TAPS]), times_conj(taps, mine)

    start = jnp.zeros((TAPS, 2, TAPS), jnp.float32)
    gram, own = lax.scan(own_step, start, jnp.arange(samples // BLOCK_LEN, dtype=jnp.int32))
    g_real, g_imag = gram[:, 0].T, gram[:, 1].T
    system = jnp.concatenate([jnp.concatenate([g_real, -g_imag], 1), jnp.concatenate([g_imag, g_real], 1)], 0)
    right = jnp.concatenate([cross[:, 0].T, cross[:, 1].T], 0)
    solved = jax.scipy.linalg.cho_solve((jnp.linalg.cholesky(system), True), right)
    b_real, b_imag = solved[:TAPS].T, solved[TAPS:].T
    mixing = jnp.concatenate([jnp.stack([b_real, b_imag], 1), jnp.stack([-b_imag, b_real], 1)], 2)
    stacked = jnp.concatenate([own[:, :, 0], own[:, :, 1]], 1)
    lagged = got - jnp.einsum("mck,qkl->qmcl", mixing, stacked, precision=HIGHEST)
    wave = jnp.asarray(doppler_table(samples // BLOCK_LEN, 0.125 / math.sqrt(samples)))
    wave = wave.reshape(2, samples // BLOCK_LEN, 2, DOPPLER)
    return jnp.einsum("qmcl,cqdk->mdlk", lagged, wave, precision=HIGHEST)


def on_device(ref_signal, surveillance, steering):
    chan_count, tm_count = lax.axis_size("chan"), lax.axis_size("tm")
    beams_local = steering.shape[1] // chan_count
    lags_local = LAGS // tm_count
    fills = (
        LANES % lags_local == 0
        and lags_local % (2 * SUBLANES) == 0
        and beams_local * lags_local == LANES * SUBLANES // 2
        and chan_count > 1
        and chan_count & (chan_count - 1) == 0
        and tm_count & (tm_count - 1) == 0
        and 2 * surveillance.shape[1] % LANES == 0
        and surveillance.shape[2] % (4 * BLOCK_LEN) == 0
    )
    device = tiled_device if fills else plain_device
    return device(ref_signal, surveillance, steering)


def solution(mesh):
    placed = (P(None, "tm"), P(None, "chan", "tm"), P(None, None, "chan"))
    return jax.shard_map(
        on_device,
        mesh=mesh,
        in_specs=placed,
        out_specs=P("chan", None, "tm", None),
        check_vma=False,
    )
```

```python
import functools
import math

import jax
import jax.numpy as jnp
import numpy as np
from jax import lax
from jax.experimental import pallas as pl
from jax.experimental.pallas import tpu as pltpu
from jax.sharding import PartitionSpec as P

LAGS = 256
DOPPLER = 256
TAPS = 64
BLOCK_LEN = 256
LANES = 128
SUBLANES = 8

HIGHEST = lax.Precision.HIGHEST
VMEM_BYTES = 48 * 1024 * 1024


def params():
    return pltpu.CompilerParams(vmem_limit_bytes=VMEM_BYTES)


def halves(x):
    high = x.astype(jnp.bfloat16)
    return high, (x - high.astype(jnp.float32)).astype(jnp.bfloat16)


def dot_nt(a, b, precision=None):
    return lax.dot_general(
        a, b, (((1,), (1,)), ((), ())), precision=precision, preferred_element_type=jnp.float32
    )


def dot_split(a, b):
    (a_high, a_low), (b_high, b_low) = a, b
    left = jnp.concatenate([a_high, a_low], 1)
    right = jnp.concatenate([b_high, b_high], 0)
    return jnp.dot(left, right, preferred_element_type=jnp.float32) + jnp.dot(
        a_high, b_low, preferred_element_type=jnp.float32
    )


def row_sign(shape):
    rows = lax.broadcasted_iota(jnp.int32, shape, 0)
    return jnp.where(rows % SUBLANES < SUBLANES // 2, 1.0, -1.0).astype(jnp.float32)


def lane_sign(shape):
    lanes = lax.broadcasted_iota(jnp.int32, shape, 1)
    return jnp.where(lanes % LANES < LANES // 2, 1.0, -1.0).astype(jnp.float32)


def swap_groups(rows, groups):
    width = LANES // groups
    lane_group = lax.broadcasted_iota(jnp.int32, rows[0].shape, 1) // width
    outs = []
    for j in range(groups):
        out = rows[j]
        for i in range(groups):
            if i != j:
                moved = pltpu.roll(rows[i], (width * (i - j)) % LANES, 1)
                out = jnp.where(lane_group == i, moved, out)
        outs.append(out)
    return outs


CHUNKS = 4


def beam_kernel(
    chan_count, beams_local, w_hbm, s_hbm, ref_hbm, kept_ref, sent_ref, tiles_ref, w_ref, s_ref, ref_ref, w_sem, s_sem, ref_sem
):
    me = lax.axis_index("chan")
    depth, length = s_hbm.shape
    width = length // CHUNKS
    w_copy = pltpu.make_async_copy(w_hbm, w_ref, w_sem)
    w_copy.start()
    s_copies = []
    for n in range(CHUNKS):
        cols = pl.ds(n * width, width)
        s_copies.append(pltpu.make_async_copy(s_hbm.at[:, cols], s_ref.at[:, cols], s_sem.at[n]))
        s_copies[n].start()
    ref_copy = pltpu.make_async_copy(ref_hbm, ref_ref, ref_sem)
    ref_copy.start()
    half = SUBLANES // 2
    sub = lax.broadcasted_iota(jnp.int32, (SUBLANES, w_hbm.shape[2]), 0)
    top = sub < half
    w_copy.wait()
    rows = []
    for parity in range(2):
        for e in range(parity, chan_count, 2):
            base = (me ^ e) * beams_local
            for tile in range(beams_local // SUBLANES):
                start = pl.multiple_of(base + tile * SUBLANES, SUBLANES)
                wr = w_ref[0, pl.ds(start, SUBLANES), :]
                wi = w_ref[1, pl.ds(start, SUBLANES), :]
                wr_s = pltpu.roll(wr, half, 0)
                wi_s = pltpu.roll(wi, half, 0)
                first = [jnp.where(top, wr, wi_s), jnp.where(top, -wi, wr_s)]
                second = [jnp.where(top, wr_s, wi), jnp.where(top, -wi_s, wr)]
                rows.append(jnp.concatenate(first, 1))
                rows.append(jnp.concatenate(second, 1))
    weights = halves(jnp.concatenate(rows, 0))
    mid = weights[0].shape[0] // 2
    for n in range(CHUNKS):
        cols = slice(n * width, (n + 1) * width)
        s_copies[n].wait()
        product = dot_split(weights, halves(s_ref[:, cols]))
        kept_ref[:, cols] = product[:mid]
        sent_ref[:, cols] = product[mid:]
    ref_copy.wait()
    for c in range(2):
        for n in range(length // LANES):
            tiles_ref[0, c, n : n + 1, :] = ref_ref[c : c + 1, n * LANES : (n + 1) * LANES]


def beam_call(steering, survey, ref, chan_count, beams_local):
    depth, length = survey.shape
    rows = chan_count * beams_local
    out = jax.ShapeDtypeStruct((rows, length), jnp.float32)
    hbm = pl.BlockSpec(memory_space=pltpu.HBM)
    vmem = pl.BlockSpec(memory_space=pltpu.VMEM)
    return pl.pallas_call(
        functools.partial(beam_kernel, chan_count, beams_local),
        in_specs=[hbm, hbm, hbm],
        out_specs=[vmem, vmem, vmem],
        out_shape=[out, out, jax.ShapeDtypeStruct((1, 2, length // LANES, LANES), jnp.float32)],
        scratch_shapes=[
            pltpu.VMEM(steering.shape, jnp.float32),
            pltpu.VMEM(survey.shape, jnp.float32),
            pltpu.VMEM(ref.shape, jnp.float32),
            pltpu.SemaphoreType.DMA,
            pltpu.SemaphoreType.DMA((CHUNKS,)),
            pltpu.SemaphoreType.DMA,
        ],
        compiler_params=params(),
        cost_estimate=pl.CostEstimate(
            flops=12 * rows * depth * length, bytes_accessed=4 * length * (depth + 2 * rows), transcendentals=0
        ),
        name="beams",
    )(*(pltpu.with_memory_space_constraint(x, pltpu.HBM) for x in (steering, survey, ref)))


def table_kernel(*refs):
    *part_refs, out_ref = refs
    me = lax.axis_index("tm")
    own = part_refs[0][0]
    rows = own.shape[1]
    edge = jnp.zeros((2, 2, LANES), jnp.float32)
    for n, part_ref in enumerate(part_refs[1:], 1):
        last = part_ref[part_ref.shape[0] - 1, :, rows - 2 :, :]
        edge = jnp.where((me > 0) & ((me ^ (me - 1)) == 2**n - 1), last, edge)
    for c in range(2):
        line = [edge[c, n : n + 1] for n in range(2)] + [own[c, n : n + 1] for n in range(rows)]
        line = jnp.concatenate(line, 1)
        for g in range(0, LANES, 2 * SUBLANES):
            tiled = jnp.broadcast_to(line, (2 * SUBLANES, line.shape[1]))
            high, low = halves(pltpu.roll(tiled, g, 1, stride=1, stride_axis=0)[:, LANES:])
            out_ref[0, c, g : g + 2 * SUBLANES] = high
            out_ref[1, c, g : g + 2 * SUBLANES] = low


def table_call(parts):
    shape = (2, 2, LANES, LANES * (parts[0].shape[2] + 1))
    return pl.pallas_call(
        table_kernel,
        out_shape=jax.ShapeDtypeStruct(shape, jnp.bfloat16),
        compiler_params=params(),
        cost_estimate=pl.CostEstimate(
            flops=8 * math.prod(shape), bytes_accessed=2 * math.prod(shape), transcendentals=0
        ),
        name="shifted_reference",
    )(*parts)


def lag_kernel(groups, owners, *refs):
    *y_refs, table_ref, out_hbm, out_ref, out_sem = refs
    copies = []

    def send(first, count):
        part = (slice(None), pl.ds(first, count))
        copies.append(pltpu.make_async_copy(out_ref.at[part], out_hbm.at[part], out_sem.at[len(copies)]))
        copies[-1].start()

    y = y_refs[0][...]
    for y_ref in y_refs[1:]:
        y = y + y_ref[...]
    rows, length = y.shape
    blocks = length // BLOCK_LEN
    turned = jnp.concatenate(
        [pltpu.roll(y[r : r + SUBLANES], SUBLANES // 2, 0) for r in range(0, rows, SUBLANES)], 0
    )
    turned = turned * row_sign(turned.shape)
    y_high, y_low = halves(y)
    t_high, t_low = halves(turned)
    both = jnp.concatenate([y_high, y_low], 0)
    turned_both = jnp.concatenate([t_high, t_low], 0)
    taps_sum = None
    for q in range(blocks):
        near = slice(q * BLOCK_LEN + LANES, q * BLOCK_LEN + LANES + BLOCK_LEN)
        far = slice(q * BLOCK_LEN, (q + 1) * BLOCK_LEN)
        cols = slice(q * BLOCK_LEN, (q + 1) * BLOCK_LEN)
        tables = []
        for h in range(2):
            tables.append(
                jnp.concatenate(
                    [
                        jnp.concatenate([table_ref[h, 0, :, near], table_ref[h, 1, :, near]], 1),
                        jnp.concatenate([table_ref[h, 0, :, far], table_ref[h, 1, :, far]], 1),
                    ],
                    0,
                )
            )
        lhs = jnp.concatenate([both[:, cols], turned_both[:, cols]], 1)
        by_high = dot_nt(lhs, tables[0])
        by_low = dot_nt(lhs[:rows], tables[1])
        product = by_high[:rows] + (by_high[rows:] + by_low)
        taps = product[:, :LANES]
        taps_sum = taps if taps_sum is None else taps_sum + taps
        for h in range(LAGS // LANES):
            lanes = slice(h * LANES, (h + 1) * LANES)
            tiles = [product[r : r + SUBLANES, lanes] for r in range(0, rows, SUBLANES)]
            for j, tile in enumerate(swap_groups(tiles, groups)):
                out_ref[h * groups + j, q] = tile
        if q % 2:
            send(q - 1, 2)
    left = lax.broadcasted_iota(jnp.int32, (SUBLANES, LANES), 1) < TAPS
    for i in range(groups // 2):
        a = taps_sum[i * SUBLANES : (i + 1) * SUBLANES]
        other = i + groups // 2
        b = taps_sum[other * SUBLANES : (other + 1) * SUBLANES]
        tile = jnp.where(left, a, pltpu.roll(b, LANES - TAPS, 1))
        for owner in range(owners):
            out_ref[owner, blocks + i] = tile
    send(blocks, groups // 2)
    for copy in copies:
        copy.wait()


def lag_call(ys, table, groups, owners):
    rows, length = ys[0].shape
    blocks = length // BLOCK_LEN
    shape = (owners, blocks + groups // 2, SUBLANES, LANES)
    return pl.pallas_call(
        functools.partial(lag_kernel, groups, owners),
        in_specs=[pl.BlockSpec(memory_space=pltpu.VMEM)] * (len(ys) + 1),
        out_specs=pl.BlockSpec(memory_space=pltpu.HBM),
        out_shape=jax.ShapeDtypeStruct(shape, jnp.float32),
        scratch_shapes=[pltpu.VMEM(shape, jnp.float32), pltpu.SemaphoreType.DMA((blocks // 2 + 1,))],
        compiler_params=params(),
        cost_estimate=pl.CostEstimate(
            flops=12 * rows * LAGS * 2 * length,
            bytes_accessed=4 * math.prod(shape) + 2 * math.prod(table.shape),
            transcendentals=0,
        ),
        name="lag_products",
    )(*ys, table)


BATCH = 4
EDGE = 2


def own_kernel(lags_local, *refs):
    *part_refs, out_ref, line_ref, tail_ref, span_ref, late_ref, taps_a, lags_a, taps_b, lags_b = refs
    me = lax.axis_index("tm")
    part_rows = part_refs[0].shape[2]
    owners = sum(part_ref.shape[0] for part_ref in part_refs)
    samples = owners * part_rows * LANES
    steps = samples // BLOCK_LEN // BATCH
    total_rows = span_ref.shape[1]
    block_rows = BLOCK_LEN // LANES

    span_ref[...] = jnp.zeros_like(span_ref)
    e = 0
    for part_ref in part_refs:
        for i in range(part_ref.shape[0]):
            span_ref[:, pl.ds(EDGE + (me ^ e) * part_rows, part_rows), :] = part_ref[i]
            e += 1
    late_rows = (me * lags_local) // LANES
    late_lanes = lax.rem(me * lags_local, LANES)
    turned = [pltpu.roll(span_ref[c], late_lanes, 1) for c in range(2)]
    before = [pltpu.roll(x, 1, 0) for x in turned]
    lanes = lax.broadcasted_iota(jnp.int32, (total_rows, LANES), 1)
    for c in range(2):
        late_ref[c] = pltpu.roll(jnp.where(lanes < late_lanes, before[c], turned[c]), late_rows, 0)

    def line_of(ref, c, first, count):
        return jnp.concatenate([ref[c, pl.ds(first + n, 1), :] for n in range(count)], 1)

    def shifted(line, by):
        tiled = jnp.broadcast_to(line, (2 * SUBLANES, line.shape[1]))
        return pltpu.roll(tiled, by, 1, stride=1, stride_axis=0)[:, LANES:]

    def keep(ref, row, value):
        high, low = halves(value)
        half = ref.shape[0] // 2
        ref[row : row + 2 * SUBLANES, :] = high
        ref[half + row : half + row + 2 * SUBLANES, :] = low

    def build(n, taps_ref, lags_ref):
        first = EDGE - 1 + n * BATCH * block_rows
        count = BATCH * block_rows + 1
        lines = [line_of(span_ref, c, first, count) for c in range(2)]
        for c in range(2):
            for g in range(0, TAPS, 2 * SUBLANES):
                keep(taps_ref, c * TAPS + g, shifted(lines[c], g))
            late = line_of(late_ref, c, first, count)
            for g in range(0, lags_local, 2 * SUBLANES):
                keep(lags_ref, c * lags_local + g, shifted(late, g))
        pad = jnp.zeros((2 * SUBLANES - 2, BATCH * BLOCK_LEN), jnp.float32)
        keep(lags_ref, 2 * lags_local, jnp.concatenate([line[:, LANES:] for line in lines] + [pad], 0))

    turn = lane_sign((lags_local, LANES))

    def use(n, taps_ref, lags_ref):
        count = lags_ref.shape[0] // 2
        for b in range(BATCH):
            cols = slice(b * BLOCK_LEN, (b + 1) * BLOCK_LEN)
            product = dot_nt(lags_ref[:, cols], taps_ref[:, cols])
            product = product[:count, :LANES] + (product[:count, LANES:] + product[count:, :LANES])
            by_real = product[:lags_local]
            by_imag = product[lags_local : 2 * lags_local]
            rows = pl.ds(pl.multiple_of((n * BATCH + b) * lags_local, lags_local), lags_local)
            high, low = halves(by_real + turn * pltpu.roll(by_imag, TAPS, 1))
            out_ref[0, rows, :] = high
            out_ref[1, rows, :] = low
            line_ref[...] += product[2 * lags_local : 2 * lags_local + SUBLANES]

    line_ref[...] = jnp.zeros_like(line_ref)
    build(0, taps_a, lags_a)

    def pair(m, carry):
        build(2 * m + 1, taps_b, lags_b)
        use(2 * m, taps_a, lags_a)
        build(jnp.minimum(2 * m + 2, steps - 1), taps_a, lags_a)
        use(2 * m + 1, taps_b, lags_b)
        return carry

    lax.fori_loop(0, steps // 2, pair, 0)
    tail = []
    for c in range(2):
        line = line_of(span_ref, c, EDGE + owners * part_rows - 1, 2)
        tail += [shifted(line, g) for g in range(0, TAPS, 2 * SUBLANES)]
    tail = jnp.concatenate(tail, 0)
    tail_ref[...] = dot_nt(tail, tail, HIGHEST)


def own_call(parts, lags_local):
    part_rows = parts[0].shape[2]
    span_rows = part_rows * sum(part.shape[0] for part in parts)
    rows = span_rows * LANES // BLOCK_LEN * lags_local
    held_rows = -(-(span_rows + 2 * EDGE) // SUBLANES) * SUBLANES
    width = BATCH * BLOCK_LEN
    taps = pltpu.VMEM((4 * TAPS, width), jnp.bfloat16)
    lags = pltpu.VMEM((4 * lags_local + 4 * SUBLANES, width), jnp.bfloat16)
    span = pltpu.VMEM((2, held_rows, LANES), jnp.float32)
    return pl.pallas_call(
        functools.partial(own_kernel, lags_local),
        out_shape=[
            jax.ShapeDtypeStruct((2, rows, 2 * TAPS), jnp.bfloat16),
            jax.ShapeDtypeStruct((SUBLANES, 2 * TAPS), jnp.float32),
            jax.ShapeDtypeStruct((2 * TAPS, 2 * TAPS), jnp.float32),
        ],
        scratch_shapes=[span, span, taps, lags, taps, lags],
        compiler_params=params(),
        cost_estimate=pl.CostEstimate(
            flops=24 * rows * BLOCK_LEN * 2 * TAPS, bytes_accessed=4 * rows * 2 * TAPS, transcendentals=0
        ),
        name="reference_products",
    )(*parts)


def as_factor(a):
    return jnp.concatenate([a, -lane_sign(a.shape) * pltpu.roll(a, a.shape[0], 1)], 0)


def solver_kernel(line_ref, tail_ref, gram_ref, solver_ref):
    total = line_ref[...]
    line = total[0:1] + lane_sign((1, LANES)) * pltpu.roll(total[1:2], TAPS, 1)
    low = lax.broadcasted_iota(jnp.int32, (1, LANES), 1) < TAPS
    line_r = jnp.where(low, line, 0.0)
    line_i = jnp.where(low, pltpu.roll(line, TAPS, 1), 0.0)
    cols = lax.broadcasted_iota(jnp.int32, (TAPS, TAPS), 1)
    rows = lax.broadcasted_iota(jnp.int32, (TAPS, TAPS), 0)
    above = cols > rows

    def upper(x):
        spread = pltpu.roll(jnp.broadcast_to(x, (TAPS, LANES)), 0, 1, stride=1, stride_axis=0)
        return spread[:, :TAPS]

    up_r = upper(line_r)
    up_i = jnp.where(above, upper(line_i), 0.0)
    strict_r = jnp.where(above, up_r, 0.0)
    diag_r = jnp.where(cols == rows, up_r, 0.0)
    tails = tail_ref[...]
    gram_r = strict_r + strict_r.T + diag_r - (tails[:TAPS, :TAPS] + tails[TAPS:, TAPS:])
    gram_i = up_i - up_i.T - (tails[:TAPS, TAPS:] - tails[TAPS:, :TAPS])
    gram = jnp.concatenate([gram_r, gram_i], 1)
    gram_halves = halves(as_factor(gram))
    gram_ref[0], gram_ref[1] = gram_halves
    one = (
        lax.broadcasted_iota(jnp.int32, gram.shape, 0) == lax.broadcasted_iota(jnp.int32, gram.shape, 1)
    ).astype(jnp.float32)
    bound = jnp.max(jnp.sum(jnp.abs(gram), axis=1, keepdims=True), axis=0, keepdims=True)

    def again(state):
        count, left, _ = state
        return (count < 60) & (left > 1e-3)

    def newton(state):
        count, _, x = state
        x_halves = halves(x)
        seen = dot_split(x_halves, gram_halves)
        left = jnp.max(jnp.abs(seen - one))
        x = 2.0 * x - dot_split(halves(seen), halves(as_factor(x)))
        return count + 1, left, x

    start = (jnp.int32(0), jnp.float32(1.0), one * (1.0 / bound))
    _, _, inverse = lax.while_loop(again, newton, start)
    solver_ref[0], solver_ref[1] = halves(as_factor(inverse))


def solver_call(line, tail):
    out = jax.ShapeDtypeStruct((2,) + tail.shape, jnp.bfloat16)
    return pl.pallas_call(
        solver_kernel,
        out_shape=[out, out],
        compiler_params=params(),
        cost_estimate=pl.CostEstimate(flops=500_000_000, bytes_accessed=200_000, transcendentals=0),
        name="gram_inverse",
    )(line, tail)


def doppler_table(block_count, scale):
    phase = (np.arange(block_count)[:, None] * np.arange(DOPPLER)[None, :] % DOPPLER) * (2.0 * math.pi / DOPPLER)
    cosine, sine = np.cos(phase), np.sin(phase)
    upper = np.concatenate([cosine, -sine], 1)
    lower = np.concatenate([sine, cosine], 1)
    return (np.concatenate([upper, lower], 0) * scale).astype(np.float32)


def map_kernel(groups, got_ref, own_ref, gram_ref, solver_ref, wave_ref, out_hbm, held_ref, out_ref, out_sem):
    owners, pieces = got_ref.shape[:2]
    blocks = pieces - groups // 2
    lags_local = LANES // groups
    total = owners * blocks
    left = lax.broadcasted_iota(jnp.int32, (SUBLANES, LANES), 1) < TAPS
    sign = row_sign((SUBLANES, LANES))
    rows = [None] * groups
    for i in range(groups // 2):
        tile = got_ref[0, blocks + i]
        for owner in range(1, owners):
            tile = tile + got_ref[owner, blocks + i]
        swapped = pltpu.roll(tile, TAPS, 1)
        for part, here, there in ((i, tile, swapped), (i + groups // 2, swapped, tile)):
            other = -sign * pltpu.roll(there, SUBLANES // 2, 0)
            rows[part] = jnp.where(left, here, other)
    cross = jnp.concatenate(rows, 0)
    solver = (solver_ref[0], solver_ref[1])
    taps = dot_split(halves(cross), solver)
    rest = cross - dot_split(halves(taps), (gram_ref[0], gram_ref[1]))
    taps = taps + dot_split(halves(rest), solver)
    taps_high, taps_low = halves(taps)
    taps_both = jnp.concatenate([taps_high, taps_low], 1)
    for q in range(0, total, 2 * groups):
        own = slice(q * lags_local, (q + 2 * groups) * lags_local)
        own_high = own_ref[0, own, :]
        clutter = dot_nt(taps_both, jnp.concatenate([own_high, own_high], 1)) + dot_nt(taps_high, own_ref[1, own, :])
        for h in range(2):
            lanes = slice(h * LANES, (h + 1) * LANES)
            tiles = [clutter[r : r + SUBLANES, lanes] for r in range(0, groups * SUBLANES, SUBLANES)]
            for j, tile in enumerate(swap_groups(tiles, groups)):
                at = q + h * groups + j
                held_ref[at * SUBLANES : (at + 1) * SUBLANES, :] = got_ref[at // blocks, at % blocks] - tile
    half = SUBLANES // 2
    wave = (wave_ref[0], wave_ref[1])
    copies = []
    for g in range(half):
        parts = [held_ref[pl.ds(c * half + g, total, stride=SUBLANES), :] for c in range(2)]
        spectrum = dot_split(halves(jnp.concatenate(parts, 0).T), wave)
        for i in range(groups):
            beam = half * i + g
            for c in range(2):
                out_ref[beam, c] = spectrum[i * lags_local : (i + 1) * lags_local, c * DOPPLER : (c + 1) * DOPPLER]
            copies.append(pltpu.make_async_copy(out_ref.at[beam], out_hbm.at[beam], out_sem.at[beam]))
            copies[-1].start()
    for copy in copies:
        copy.wait()


def map_call(got, own, gram, solver, wave, groups, beams_local):
    total = got.shape[0] * (got.shape[1] - groups // 2)
    lags_local = LANES // groups
    shape = (beams_local, 2, lags_local, DOPPLER)
    return pl.pallas_call(
        functools.partial(map_kernel, groups),
        in_specs=[pl.BlockSpec(memory_space=pltpu.VMEM)] * 5,
        out_specs=pl.BlockSpec(memory_space=pltpu.HBM),
        out_shape=jax.ShapeDtypeStruct(shape, jnp.float32),
        scratch_shapes=[
            pltpu.VMEM((total * SUBLANES, LANES), jnp.float32),
            pltpu.VMEM(shape, jnp.float32),
            pltpu.SemaphoreType.DMA((beams_local,)),
        ],
        compiler_params=params(),
        cost_estimate=pl.CostEstimate(
            flops=12 * math.prod(shape) * total, bytes_accessed=4 * math.prod(shape), transcendentals=0
        ),
        name="range_doppler",
    )(got, own, gram, solver, wave)


def swap(x, axis, by):
    pairs = [(i, i ^ by) for i in range(lax.axis_size(axis))]
    return lax.ppermute(x, axis, pairs)


def tiled_device(ref_signal, surveillance, steering):
    chan_count, tm_count = lax.axis_size("chan"), lax.axis_size("tm")
    channels, length = surveillance.shape[1:]
    beams_local = steering.shape[1] // chan_count
    lags_local = LAGS // tm_count
    groups = LANES // lags_local
    samples = length * tm_count

    survey = surveillance.reshape(2 * channels, length)
    kept, moved, tiles = beam_call(steering, survey, ref_signal, chan_count, beams_local)
    shape = (chan_count // 2, 2 * beams_local, length)
    parts = [kept.reshape(shape), swap(moved, "chan", 1).reshape(shape)]
    near = swap(tiles, "tm", 1)
    by = 2
    while by < chan_count:
        sent = parts[0][1::2]
        for part in parts[1:]:
            sent = sent + part[1::2]
        tiles, sent = lax.optimization_barrier((tiles, sent))
        parts = [part[::2] for part in parts] + [swap(sent, "chan", by)]
        by *= 2
    ref_parts = [tiles, near]
    by = 2
    while by < tm_count:
        ref_parts.append(swap(jnp.concatenate(ref_parts, 0), "tm", by))
        by *= 2
    table = table_call(ref_parts)
    pieces = lag_call([part[0] for part in parts], table, groups, tm_count)
    got = lax.all_to_all(pieces, "tm", 0, 0, tiled=True)
    own, line, tail = own_call(ref_parts, lags_local)
    gram, solver = solver_call(line, tail)
    wave = doppler_table(samples // BLOCK_LEN, 0.125 / math.sqrt(samples))
    high = wave.astype(jnp.bfloat16)
    wave = np.stack([high, (wave - high.astype(np.float32)).astype(jnp.bfloat16)])
    return map_call(got, own, gram, solver, jnp.asarray(wave), groups, beams_local)


def lag_table(ref_ext, offset, lags):
    window = lax.dynamic_slice_in_dim(ref_ext, offset, BLOCK_LEN + LAGS, 1)
    span = BLOCK_LEN + LAGS
    tiled = jnp.tile(jnp.pad(window, ((0, 0), (0, 1))), (1, lags))[:, : lags * span]
    return tiled.reshape(2, lags, span)[:, :, LAGS:]


def times_conj(a, b):
    real = jnp.einsum("...t,lt->...l", a[..., 0, :], b[0], precision=HIGHEST) + jnp.einsum(
        "...t,lt->...l", a[..., 1, :], b[1], precision=HIGHEST
    )
    imag = jnp.einsum("...t,lt->...l", a[..., 1, :], b[0], precision=HIGHEST) - jnp.einsum(
        "...t,lt->...l", a[..., 0, :], b[1], precision=HIGHEST
    )
    return jnp.stack([real, imag], -2)


def plain_device(ref_signal, surveillance, steering):
    chan_count, tm_count = lax.axis_size("chan"), lax.axis_size("tm")
    length = surveillance.shape[2]
    beams = steering.shape[1]
    lags_local = LAGS // tm_count
    samples = length * tm_count
    local_blocks = length // BLOCK_LEN
    here = lax.axis_index("tm")

    w_real, w_imag = steering
    real = jnp.dot(w_real, surveillance[0], precision=HIGHEST) - jnp.dot(w_imag, surveillance[1], precision=HIGHEST)
    imag = jnp.dot(w_imag, surveillance[0], precision=HIGHEST) + jnp.dot(w_real, surveillance[1], precision=HIGHEST)
    beam = lax.psum_scatter(jnp.stack([real, imag], 1), "chan", scatter_dimension=0, tiled=True)
    ref_all = lax.all_gather(ref_signal, "tm", axis=1, tiled=True)
    ref_ext = jnp.pad(ref_all, ((0, 0), (LAGS, 0)))

    def beam_step(carry, q):
        offset = q * BLOCK_LEN
        table = lag_table(ref_ext, here * length + offset, LAGS)
        segment = lax.dynamic_slice_in_dim(beam, offset, BLOCK_LEN, 2)
        return carry, times_conj(segment, table)

    _, products = lax.scan(beam_step, None, jnp.arange(local_blocks, dtype=jnp.int32))
    cross = lax.psum(products[..., :TAPS].sum(0), "tm")
    got = lax.all_to_all(products, "tm", 3, 0, tiled=True)

    def own_step(gram, q):
        offset = q * BLOCK_LEN
        table = lag_table(ref_ext, offset, LAGS)
        taps = table[:, :TAPS].transpose(1, 0, 2)
        mine = lax.dynamic_slice_in_dim(table, here * lags_local, lags_local, 1)
        return gram + times_conj(taps, table[:, :TAPS]), times_conj(taps, mine)

    start = jnp.zeros((TAPS, 2, TAPS), jnp.float32)
    gram, own = lax.scan(own_step, start, jnp.arange(samples // BLOCK_LEN, dtype=jnp.int32))
    g_real, g_imag = gram[:, 0].T, gram[:, 1].T
    system = jnp.concatenate([jnp.concatenate([g_real, -g_imag], 1), jnp.concatenate([g_imag, g_real], 1)], 0)
    right = jnp.concatenate([cross[:, 0].T, cross[:, 1].T], 0)
    solved = jax.scipy.linalg.cho_solve((jnp.linalg.cholesky(system), True), right)
    b_real, b_imag = solved[:TAPS].T, solved[TAPS:].T
    mixing = jnp.concatenate([jnp.stack([b_real, b_imag], 1), jnp.stack([-b_imag, b_real], 1)], 2)
    stacked = jnp.concatenate([own[:, :, 0], own[:, :, 1]], 1)
    lagged = got - jnp.einsum("mck,qkl->qmcl", mixing, stacked, precision=HIGHEST)
    wave = jnp.asarray(doppler_table(samples // BLOCK_LEN, 0.125 / math.sqrt(samples)))
    wave = wave.reshape(2, samples // BLOCK_LEN, 2, DOPPLER)
    return jnp.einsum("qmcl,cqdk->mdlk", lagged, wave, precision=HIGHEST)


def on_device(ref_signal, surveillance, steering):
    chan_count, tm_count = lax.axis_size("chan"), lax.axis_size("tm")
    beams_local = steering.shape[1] // chan_count
    lags_local = LAGS // tm_count
    fills = (
        LANES % lags_local == 0
        and lags_local % (2 * SUBLANES) == 0
        and beams_local * lags_local == LANES * SUBLANES // 2
        and chan_count > 1
        and chan_count & (chan_count - 1) == 0
        and tm_count > 1
        and tm_count & (tm_count - 1) == 0
        and 2 * surveillance.shape[1] % LANES == 0
        and surveillance.shape[2] % (2 * BATCH * BLOCK_LEN) == 0
    )
    device = tiled_device if fills else plain_device
    return device(ref_signal, surveillance, steering)


def solution(mesh):
    placed = (P(None, "tm"), P(None, "chan", "tm"), P(None, None, "chan"))
    return jax.shard_map(
        on_device,
        mesh=mesh,
        in_specs=placed,
        out_specs=P("chan", None, "tm", None),
        check_vma=False,
    )
```

```python
import functools
import math

import jax
import jax.numpy as jnp
import numpy as np
from jax import lax
from jax.experimental import pallas as pl
from jax.experimental.pallas import tpu as pltpu
from jax.sharding import PartitionSpec as P

LAGS = 256
DOPPLER = 256
TAPS = 64
BLOCK_LEN = 256
LANES = 128
SUBLANES = 8

HIGHEST = lax.Precision.HIGHEST
VMEM_BYTES = 48 * 1024 * 1024


def params():
    return pltpu.CompilerParams(vmem_limit_bytes=VMEM_BYTES)


def halves(x):
    high = x.astype(jnp.bfloat16)
    return high, (x - high.astype(jnp.float32)).astype(jnp.bfloat16)


def dot_nt(a, b, precision=None):
    return lax.dot_general(
        a, b, (((1,), (1,)), ((), ())), precision=precision, preferred_element_type=jnp.float32
    )


def dot_split(a, b):
    (a_high, a_low), (b_high, b_low) = a, b
    left = jnp.concatenate([a_high, a_low], 1)
    right = jnp.concatenate([b_high, b_high], 0)
    return jnp.dot(left, right, preferred_element_type=jnp.float32) + jnp.dot(
        a_high, b_low, preferred_element_type=jnp.float32
    )


def row_sign(shape):
    rows = lax.broadcasted_iota(jnp.int32, shape, 0)
    return jnp.where(rows % SUBLANES < SUBLANES // 2, 1.0, -1.0).astype(jnp.float32)


def lane_sign(shape):
    lanes = lax.broadcasted_iota(jnp.int32, shape, 1)
    return jnp.where(lanes % LANES < LANES // 2, 1.0, -1.0).astype(jnp.float32)


def swap_groups(rows, groups):
    width = LANES // groups
    lane_group = lax.broadcasted_iota(jnp.int32, rows[0].shape, 1) // width
    outs = []
    for j in range(groups):
        out = rows[j]
        for i in range(groups):
            if i != j:
                moved = pltpu.roll(rows[i], (width * (i - j)) % LANES, 1)
                out = jnp.where(lane_group == i, moved, out)
        outs.append(out)
    return outs


CHUNKS = 4


def beam_kernel(
    chan_count, beams_local, w_hbm, s_hbm, ref_hbm, kept_ref, sent_ref, tiles_ref, w_ref, s_ref, ref_ref, w_sem, s_sem, ref_sem
):
    me = lax.axis_index("chan")
    depth, length = s_hbm.shape
    width = length // CHUNKS
    w_copy = pltpu.make_async_copy(w_hbm, w_ref, w_sem)
    w_copy.start()
    s_copies = []
    for n in range(CHUNKS):
        cols = pl.ds(n * width, width)
        s_copies.append(pltpu.make_async_copy(s_hbm.at[:, cols], s_ref.at[:, cols], s_sem.at[n]))
        s_copies[n].start()
    ref_copy = pltpu.make_async_copy(ref_hbm, ref_ref, ref_sem)
    ref_copy.start()
    half = SUBLANES // 2
    sub = lax.broadcasted_iota(jnp.int32, (SUBLANES, w_hbm.shape[2]), 0)
    top = sub < half
    w_copy.wait()
    rows = []
    for parity in range(2):
        for e in range(parity, chan_count, 2):
            base = (me ^ e) * beams_local
            for tile in range(beams_local // SUBLANES):
                start = pl.multiple_of(base + tile * SUBLANES, SUBLANES)
                wr = w_ref[0, pl.ds(start, SUBLANES), :]
                wi = w_ref[1, pl.ds(start, SUBLANES), :]
                wr_s = pltpu.roll(wr, half, 0)
                wi_s = pltpu.roll(wi, half, 0)
                first = [jnp.where(top, wr, wi_s), jnp.where(top, -wi, wr_s)]
                second = [jnp.where(top, wr_s, wi), jnp.where(top, -wi_s, wr)]
                rows.append(jnp.concatenate(first, 1))
                rows.append(jnp.concatenate(second, 1))
    weights = halves(jnp.concatenate(rows, 0))
    mid = weights[0].shape[0] // 2
    for n in range(CHUNKS):
        cols = slice(n * width, (n + 1) * width)
        s_copies[n].wait()
        product = dot_split(weights, halves(s_ref[:, cols]))
        kept_ref[:, cols] = product[:mid]
        sent_ref[:, cols] = product[mid:]
    ref_copy.wait()
    for c in range(2):
        for n in range(length // LANES):
            tiles_ref[0, c, n : n + 1, :] = ref_ref[c : c + 1, n * LANES : (n + 1) * LANES]


def beam_call(steering, survey, ref, chan_count, beams_local):
    depth, length = survey.shape
    rows = chan_count * beams_local
    out = jax.ShapeDtypeStruct((rows, length), jnp.float32)
    hbm = pl.BlockSpec(memory_space=pltpu.HBM)
    vmem = pl.BlockSpec(memory_space=pltpu.VMEM)
    return pl.pallas_call(
        functools.partial(beam_kernel, chan_count, beams_local),
        in_specs=[hbm, hbm, hbm],
        out_specs=[vmem, vmem, vmem],
        out_shape=[out, out, jax.ShapeDtypeStruct((1, 2, length // LANES, LANES), jnp.float32)],
        scratch_shapes=[
            pltpu.VMEM(steering.shape, jnp.float32),
            pltpu.VMEM(survey.shape, jnp.float32),
            pltpu.VMEM(ref.shape, jnp.float32),
            pltpu.SemaphoreType.DMA,
            pltpu.SemaphoreType.DMA((CHUNKS,)),
            pltpu.SemaphoreType.DMA,
        ],
        compiler_params=params(),
        cost_estimate=pl.CostEstimate(
            flops=12 * rows * depth * length, bytes_accessed=4 * length * (depth + 2 * rows), transcendentals=0
        ),
        name="beams",
    )(*(pltpu.with_memory_space_constraint(x, pltpu.HBM) for x in (steering, survey, ref)))


def pair_kernel(tiles_ref, near_ref, out_ref):
    out_ref[0] = tiles_ref[0]
    for c in range(2):
        for n in range(tiles_ref.shape[2]):
            out_ref[1, c, n : n + 1, :] = near_ref[c : c + 1, n * LANES : (n + 1) * LANES]


def pair_call(tiles, near):
    return pl.pallas_call(
        pair_kernel,
        out_shape=jax.ShapeDtypeStruct((2,) + tiles.shape[1:], jnp.float32),
        compiler_params=params(),
        cost_estimate=pl.CostEstimate(flops=0, bytes_accessed=16 * near.size, transcendentals=0),
        name="reference_pair",
    )(tiles, near)


def table_kernel(*refs):
    *part_refs, out_ref = refs
    me = lax.axis_index("tm")
    own = part_refs[0][0]
    rows = own.shape[1]
    edge = jnp.zeros((2, 2, LANES), jnp.float32)
    for n, part_ref in enumerate(part_refs):
        edge = jnp.where((me > 0) & ((me ^ (me - 1)) == 2 * n + 1), part_ref[1, :, rows - 2 :, :], edge)
    for c in range(2):
        line = [edge[c, n : n + 1] for n in range(2)] + [own[c, n : n + 1] for n in range(rows)]
        line = jnp.concatenate(line, 1)
        for g in range(0, LANES, 2 * SUBLANES):
            tiled = jnp.broadcast_to(line, (2 * SUBLANES, line.shape[1]))
            high, low = halves(pltpu.roll(tiled, g, 1, stride=1, stride_axis=0)[:, LANES:])
            out_ref[0, c, g : g + 2 * SUBLANES] = high
            out_ref[1, c, g : g + 2 * SUBLANES] = low


def table_call(parts):
    shape = (2, 2, LANES, LANES * (parts[0].shape[2] + 1))
    return pl.pallas_call(
        table_kernel,
        out_shape=jax.ShapeDtypeStruct(shape, jnp.bfloat16),
        compiler_params=params(),
        cost_estimate=pl.CostEstimate(
            flops=8 * math.prod(shape), bytes_accessed=2 * math.prod(shape), transcendentals=0
        ),
        name="shifted_reference",
    )(*parts)


def lag_kernel(groups, owners, *refs):
    *y_refs, table_ref, out_hbm, out_ref, out_sem = refs
    copies = []

    def send(first, count):
        part = (slice(None), pl.ds(first, count))
        copies.append(pltpu.make_async_copy(out_ref.at[part], out_hbm.at[part], out_sem.at[len(copies)]))
        copies[-1].start()

    y = y_refs[0][...]
    for y_ref in y_refs[1:]:
        y = y + y_ref[...]
    rows, length = y.shape
    blocks = length // BLOCK_LEN
    turned = jnp.concatenate(
        [pltpu.roll(y[r : r + SUBLANES], SUBLANES // 2, 0) for r in range(0, rows, SUBLANES)], 0
    )
    turned = turned * row_sign(turned.shape)
    y_high, y_low = halves(y)
    t_high, t_low = halves(turned)
    both = jnp.concatenate([y_high, y_low], 0)
    turned_both = jnp.concatenate([t_high, t_low], 0)
    taps_sum = None
    for q in range(blocks):
        near = slice(q * BLOCK_LEN + LANES, q * BLOCK_LEN + LANES + BLOCK_LEN)
        far = slice(q * BLOCK_LEN, (q + 1) * BLOCK_LEN)
        cols = slice(q * BLOCK_LEN, (q + 1) * BLOCK_LEN)
        tables = []
        for h in range(2):
            tables.append(
                jnp.concatenate(
                    [
                        jnp.concatenate([table_ref[h, 0, :, near], table_ref[h, 1, :, near]], 1),
                        jnp.concatenate([table_ref[h, 0, :, far], table_ref[h, 1, :, far]], 1),
                    ],
                    0,
                )
            )
        lhs = jnp.concatenate([both[:, cols], turned_both[:, cols]], 1)
        by_high = dot_nt(lhs, tables[0])
        by_low = dot_nt(lhs[:rows], tables[1])
        product = by_high[:rows] + (by_high[rows:] + by_low)
        taps = product[:, :LANES]
        taps_sum = taps if taps_sum is None else taps_sum + taps
        for h in range(LAGS // LANES):
            lanes = slice(h * LANES, (h + 1) * LANES)
            tiles = [product[r : r + SUBLANES, lanes] for r in range(0, rows, SUBLANES)]
            for j, tile in enumerate(swap_groups(tiles, groups)):
                out_ref[h * groups + j, q] = tile
        if q % 2:
            send(q - 1, 2)
    left = lax.broadcasted_iota(jnp.int32, (SUBLANES, LANES), 1) < TAPS
    for i in range(groups // 2):
        a = taps_sum[i * SUBLANES : (i + 1) * SUBLANES]
        other = i + groups // 2
        b = taps_sum[other * SUBLANES : (other + 1) * SUBLANES]
        tile = jnp.where(left, a, pltpu.roll(b, LANES - TAPS, 1))
        for owner in range(owners):
            out_ref[owner, blocks + i] = tile
    send(blocks, groups // 2)
    for copy in copies:
        copy.wait()


def lag_call(ys, table, groups, owners):
    rows, length = ys[0].shape
    blocks = length // BLOCK_LEN
    shape = (owners, blocks + groups // 2, SUBLANES, LANES)
    return pl.pallas_call(
        functools.partial(lag_kernel, groups, owners),
        in_specs=[pl.BlockSpec(memory_space=pltpu.VMEM)] * (len(ys) + 1),
        out_specs=pl.BlockSpec(memory_space=pltpu.HBM),
        out_shape=jax.ShapeDtypeStruct(shape, jnp.float32),
        scratch_shapes=[pltpu.VMEM(shape, jnp.float32), pltpu.SemaphoreType.DMA((blocks // 2 + 1,))],
        compiler_params=params(),
        cost_estimate=pl.CostEstimate(
            flops=12 * rows * LAGS * 2 * length,
            bytes_accessed=4 * math.prod(shape) + 2 * math.prod(table.shape),
            transcendentals=0,
        ),
        name="lag_products",
    )(*ys, table)


BATCH = 4
EDGE = 2


def own_kernel(lags_local, *refs):
    *part_refs, out_ref, line_ref, tail_ref, span_ref, late_ref, taps_a, lags_a, taps_b, lags_b = refs
    me = lax.axis_index("tm")
    part_rows = part_refs[0].shape[2]
    owners = sum(part_ref.shape[0] for part_ref in part_refs)
    samples = owners * part_rows * LANES
    steps = samples // BLOCK_LEN // BATCH
    total_rows = span_ref.shape[1]
    block_rows = BLOCK_LEN // LANES

    span_ref[...] = jnp.zeros_like(span_ref)
    e = 0
    for part_ref in part_refs:
        for i in range(part_ref.shape[0]):
            span_ref[:, pl.ds(EDGE + (me ^ e) * part_rows, part_rows), :] = part_ref[i]
            e += 1
    late_rows = (me * lags_local) // LANES
    late_lanes = lax.rem(me * lags_local, LANES)
    turned = [pltpu.roll(span_ref[c], late_lanes, 1) for c in range(2)]
    before = [pltpu.roll(x, 1, 0) for x in turned]
    lanes = lax.broadcasted_iota(jnp.int32, (total_rows, LANES), 1)
    for c in range(2):
        late_ref[c] = pltpu.roll(jnp.where(lanes < late_lanes, before[c], turned[c]), late_rows, 0)

    def line_of(ref, c, first, count):
        return jnp.concatenate([ref[c, pl.ds(first + n, 1), :] for n in range(count)], 1)

    def shifted(line, by):
        tiled = jnp.broadcast_to(line, (2 * SUBLANES, line.shape[1]))
        return pltpu.roll(tiled, by, 1, stride=1, stride_axis=0)[:, LANES:]

    def keep(ref, row, value):
        high, low = halves(value)
        half = ref.shape[0] // 2
        ref[row : row + 2 * SUBLANES, :] = high
        ref[half + row : half + row + 2 * SUBLANES, :] = low

    def build(n, taps_ref, lags_ref):
        first = EDGE - 1 + n * BATCH * block_rows
        count = BATCH * block_rows + 1
        lines = [line_of(span_ref, c, first, count) for c in range(2)]
        for c in range(2):
            for g in range(0, TAPS, 2 * SUBLANES):
                keep(taps_ref, c * TAPS + g, shifted(lines[c], g))
            late = line_of(late_ref, c, first, count)
            for g in range(0, lags_local, 2 * SUBLANES):
                keep(lags_ref, c * lags_local + g, shifted(late, g))
        pad = jnp.zeros((2 * SUBLANES - 2, BATCH * BLOCK_LEN), jnp.float32)
        keep(lags_ref, 2 * lags_local, jnp.concatenate([line[:, LANES:] for line in lines] + [pad], 0))

    turn = lane_sign((lags_local, LANES))

    def use(n, taps_ref, lags_ref):
        count = lags_ref.shape[0] // 2
        for b in range(BATCH):
            cols = slice(b * BLOCK_LEN, (b + 1) * BLOCK_LEN)
            product = dot_nt(lags_ref[:, cols], taps_ref[:, cols])
            product = product[:count, :LANES] + (product[:count, LANES:] + product[count:, :LANES])
            by_real = product[:lags_local]
            by_imag = product[lags_local : 2 * lags_local]
            rows = pl.ds(pl.multiple_of((n * BATCH + b) * lags_local, lags_local), lags_local)
            high, low = halves(by_real + turn * pltpu.roll(by_imag, TAPS, 1))
            out_ref[0, rows, :] = high
            out_ref[1, rows, :] = low
            line_ref[...] += product[2 * lags_local : 2 * lags_local + SUBLANES]

    line_ref[...] = jnp.zeros_like(line_ref)
    build(0, taps_a, lags_a)

    def pair(m, carry):
        build(2 * m + 1, taps_b, lags_b)
        use(2 * m, taps_a, lags_a)
        build(jnp.minimum(2 * m + 2, steps - 1), taps_a, lags_a)
        use(2 * m + 1, taps_b, lags_b)
        return carry

    lax.fori_loop(0, steps // 2, pair, 0)
    tail = []
    for c in range(2):
        line = line_of(span_ref, c, EDGE + owners * part_rows - 1, 2)
        tail += [shifted(line, g) for g in range(0, TAPS, 2 * SUBLANES)]
    tail = jnp.concatenate(tail, 0)
    tail_ref[...] = dot_nt(tail, tail, HIGHEST)


def own_call(parts, lags_local):
    part_rows = parts[0].shape[2]
    span_rows = part_rows * sum(part.shape[0] for part in parts)
    rows = span_rows * LANES // BLOCK_LEN * lags_local
    held_rows = -(-(span_rows + 2 * EDGE) // SUBLANES) * SUBLANES
    width = BATCH * BLOCK_LEN
    taps = pltpu.VMEM((4 * TAPS, width), jnp.bfloat16)
    lags = pltpu.VMEM((4 * lags_local + 4 * SUBLANES, width), jnp.bfloat16)
    span = pltpu.VMEM((2, held_rows, LANES), jnp.float32)
    return pl.pallas_call(
        functools.partial(own_kernel, lags_local),
        out_shape=[
            jax.ShapeDtypeStruct((2, rows, 2 * TAPS), jnp.bfloat16),
            jax.ShapeDtypeStruct((SUBLANES, 2 * TAPS), jnp.float32),
            jax.ShapeDtypeStruct((2 * TAPS, 2 * TAPS), jnp.float32),
        ],
        scratch_shapes=[span, span, taps, lags, taps, lags],
        compiler_params=params(),
        cost_estimate=pl.CostEstimate(
            flops=24 * rows * BLOCK_LEN * 2 * TAPS, bytes_accessed=4 * rows * 2 * TAPS, transcendentals=0
        ),
        name="reference_products",
    )(*parts)


def as_factor(a):
    return jnp.concatenate([a, -lane_sign(a.shape) * pltpu.roll(a, a.shape[0], 1)], 0)


def solver_kernel(line_ref, tail_ref, gram_ref, solver_ref):
    total = line_ref[...]
    line = total[0:1] + lane_sign((1, LANES)) * pltpu.roll(total[1:2], TAPS, 1)
    low = lax.broadcasted_iota(jnp.int32, (1, LANES), 1) < TAPS
    line_r = jnp.where(low, line, 0.0)
    line_i = jnp.where(low, pltpu.roll(line, TAPS, 1), 0.0)
    cols = lax.broadcasted_iota(jnp.int32, (TAPS, TAPS), 1)
    rows = lax.broadcasted_iota(jnp.int32, (TAPS, TAPS), 0)
    above = cols > rows

    def upper(x):
        spread = pltpu.roll(jnp.broadcast_to(x, (TAPS, LANES)), 0, 1, stride=1, stride_axis=0)
        return spread[:, :TAPS]

    up_r = upper(line_r)
    up_i = jnp.where(above, upper(line_i), 0.0)
    strict_r = jnp.where(above, up_r, 0.0)
    diag_r = jnp.where(cols == rows, up_r, 0.0)
    tails = tail_ref[...]
    gram_r = strict_r + strict_r.T + diag_r - (tails[:TAPS, :TAPS] + tails[TAPS:, TAPS:])
    gram_i = up_i - up_i.T - (tails[:TAPS, TAPS:] - tails[TAPS:, :TAPS])
    gram = jnp.concatenate([gram_r, gram_i], 1)
    gram_halves = halves(as_factor(gram))
    gram_ref[0], gram_ref[1] = gram_halves
    one = (
        lax.broadcasted_iota(jnp.int32, gram.shape, 0) == lax.broadcasted_iota(jnp.int32, gram.shape, 1)
    ).astype(jnp.float32)
    bound = jnp.max(jnp.sum(jnp.abs(gram), axis=1, keepdims=True), axis=0, keepdims=True)

    def again(state):
        count, left, _ = state
        return (count < 60) & (left > 1e-3)

    def newton(state):
        count, _, x = state
        x_halves = halves(x)
        seen = dot_split(x_halves, gram_halves)
        left = jnp.max(jnp.abs(seen - one))
        x = 2.0 * x - dot_split(halves(seen), halves(as_factor(x)))
        return count + 1, left, x

    start = (jnp.int32(0), jnp.float32(1.0), one * (1.0 / bound))
    _, _, inverse = lax.while_loop(again, newton, start)
    solver_ref[0], solver_ref[1] = halves(as_factor(inverse))


def solver_call(line, tail):
    out = jax.ShapeDtypeStruct((2,) + tail.shape, jnp.bfloat16)
    return pl.pallas_call(
        solver_kernel,
        out_shape=[out, out],
        compiler_params=params(),
        cost_estimate=pl.CostEstimate(flops=500_000_000, bytes_accessed=200_000, transcendentals=0),
        name="gram_inverse",
    )(line, tail)


def doppler_table(block_count, scale):
    phase = (np.arange(block_count)[:, None] * np.arange(DOPPLER)[None, :] % DOPPLER) * (2.0 * math.pi / DOPPLER)
    cosine, sine = np.cos(phase), np.sin(phase)
    upper = np.concatenate([cosine, -sine], 1)
    lower = np.concatenate([sine, cosine], 1)
    return (np.concatenate([upper, lower], 0) * scale).astype(np.float32)


def map_kernel(groups, got_ref, own_ref, gram_ref, solver_ref, wave_ref, out_hbm, held_ref, out_ref, out_sem):
    owners, pieces = got_ref.shape[:2]
    blocks = pieces - groups // 2
    lags_local = LANES // groups
    total = owners * blocks
    left = lax.broadcasted_iota(jnp.int32, (SUBLANES, LANES), 1) < TAPS
    sign = row_sign((SUBLANES, LANES))
    rows = [None] * groups
    for i in range(groups // 2):
        tile = got_ref[0, blocks + i]
        for owner in range(1, owners):
            tile = tile + got_ref[owner, blocks + i]
        swapped = pltpu.roll(tile, TAPS, 1)
        for part, here, there in ((i, tile, swapped), (i + groups // 2, swapped, tile)):
            other = -sign * pltpu.roll(there, SUBLANES // 2, 0)
            rows[part] = jnp.where(left, here, other)
    cross = jnp.concatenate(rows, 0)
    solver = (solver_ref[0], solver_ref[1])
    taps = dot_split(halves(cross), solver)
    rest = cross - dot_split(halves(taps), (gram_ref[0], gram_ref[1]))
    taps = taps + dot_split(halves(rest), solver)
    taps_high, taps_low = halves(taps)
    taps_both = jnp.concatenate([taps_high, taps_low], 1)
    for q in range(0, total, 2 * groups):
        own = slice(q * lags_local, (q + 2 * groups) * lags_local)
        own_high = own_ref[0, own, :]
        clutter = dot_nt(taps_both, jnp.concatenate([own_high, own_high], 1)) + dot_nt(taps_high, own_ref[1, own, :])
        for h in range(2):
            lanes = slice(h * LANES, (h + 1) * LANES)
            tiles = [clutter[r : r + SUBLANES, lanes] for r in range(0, groups * SUBLANES, SUBLANES)]
            for j, tile in enumerate(swap_groups(tiles, groups)):
                at = q + h * groups + j
                held_ref[at * SUBLANES : (at + 1) * SUBLANES, :] = got_ref[at // blocks, at % blocks] - tile
    half = SUBLANES // 2
    wave = (wave_ref[0], wave_ref[1])
    copies = []
    for g in range(half):
        parts = [held_ref[pl.ds(c * half + g, total, stride=SUBLANES), :] for c in range(2)]
        spectrum = dot_split(halves(jnp.concatenate(parts, 0).T), wave)
        for i in range(groups):
            beam = half * i + g
            for c in range(2):
                out_ref[beam, c] = spectrum[i * lags_local : (i + 1) * lags_local, c * DOPPLER : (c + 1) * DOPPLER]
            copies.append(pltpu.make_async_copy(out_ref.at[beam], out_hbm.at[beam], out_sem.at[beam]))
            copies[-1].start()
    for copy in copies:
        copy.wait()


def map_call(got, own, gram, solver, wave, groups, beams_local):
    total = got.shape[0] * (got.shape[1] - groups // 2)
    lags_local = LANES // groups
    shape = (beams_local, 2, lags_local, DOPPLER)
    return pl.pallas_call(
        functools.partial(map_kernel, groups),
        in_specs=[pl.BlockSpec(memory_space=pltpu.VMEM)] * 5,
        out_specs=pl.BlockSpec(memory_space=pltpu.HBM),
        out_shape=jax.ShapeDtypeStruct(shape, jnp.float32),
        scratch_shapes=[
            pltpu.VMEM((total * SUBLANES, LANES), jnp.float32),
            pltpu.VMEM(shape, jnp.float32),
            pltpu.SemaphoreType.DMA((beams_local,)),
        ],
        compiler_params=params(),
        cost_estimate=pl.CostEstimate(
            flops=12 * math.prod(shape) * total, bytes_accessed=4 * math.prod(shape), transcendentals=0
        ),
        name="range_doppler",
    )(got, own, gram, solver, wave)


def swap(x, axis, by):
    pairs = [(i, i ^ by) for i in range(lax.axis_size(axis))]
    return lax.ppermute(x, axis, pairs)


def tiled_device(ref_signal, surveillance, steering):
    chan_count, tm_count = lax.axis_size("chan"), lax.axis_size("tm")
    channels, length = surveillance.shape[1:]
    beams_local = steering.shape[1] // chan_count
    lags_local = LAGS // tm_count
    groups = LANES // lags_local
    samples = length * tm_count

    survey = surveillance.reshape(2 * channels, length)
    near = swap(ref_signal, "tm", 1)
    kept, moved, tiles = beam_call(steering, survey, ref_signal, chan_count, beams_local)
    shape = (chan_count // 2, 2 * beams_local, length)
    parts = [kept.reshape(shape), swap(moved, "chan", 1).reshape(shape)]
    pair = pair_call(tiles, near)
    by = 2
    while by < chan_count:
        sent = parts[0][1::2]
        for part in parts[1:]:
            sent = sent + part[1::2]
        pair, sent = lax.optimization_barrier((pair, sent))
        parts = [part[::2] for part in parts] + [swap(sent, "chan", by)]
        by *= 2
    ref_parts = [pair] + [swap(pair, "tm", by) for by in range(2, tm_count, 2)]
    table = table_call(ref_parts)
    pieces = lag_call([part[0] for part in parts], table, groups, tm_count)
    got = lax.all_to_all(pieces, "tm", 0, 0, tiled=True)
    own, line, tail = own_call(ref_parts, lags_local)
    gram, solver = solver_call(line, tail)
    wave = doppler_table(samples // BLOCK_LEN, 0.125 / math.sqrt(samples))
    high = wave.astype(jnp.bfloat16)
    wave = np.stack([high, (wave - high.astype(np.float32)).astype(jnp.bfloat16)])
    return map_call(got, own, gram, solver, jnp.asarray(wave), groups, beams_local)


def lag_table(ref_ext, offset, lags):
    window = lax.dynamic_slice_in_dim(ref_ext, offset, BLOCK_LEN + LAGS, 1)
    span = BLOCK_LEN + LAGS
    tiled = jnp.tile(jnp.pad(window, ((0, 0), (0, 1))), (1, lags))[:, : lags * span]
    return tiled.reshape(2, lags, span)[:, :, LAGS:]


def times_conj(a, b):
    real = jnp.einsum("...t,lt->...l", a[..., 0, :], b[0], precision=HIGHEST) + jnp.einsum(
        "...t,lt->...l", a[..., 1, :], b[1], precision=HIGHEST
    )
    imag = jnp.einsum("...t,lt->...l", a[..., 1, :], b[0], precision=HIGHEST) - jnp.einsum(
        "...t,lt->...l", a[..., 0, :], b[1], precision=HIGHEST
    )
    return jnp.stack([real, imag], -2)


def plain_device(ref_signal, surveillance, steering):
    chan_count, tm_count = lax.axis_size("chan"), lax.axis_size("tm")
    length = surveillance.shape[2]
    beams = steering.shape[1]
    lags_local = LAGS // tm_count
    samples = length * tm_count
    local_blocks = length // BLOCK_LEN
    here = lax.axis_index("tm")

    w_real, w_imag = steering
    real = jnp.dot(w_real, surveillance[0], precision=HIGHEST) - jnp.dot(w_imag, surveillance[1], precision=HIGHEST)
    imag = jnp.dot(w_imag, surveillance[0], precision=HIGHEST) + jnp.dot(w_real, surveillance[1], precision=HIGHEST)
    beam = lax.psum_scatter(jnp.stack([real, imag], 1), "chan", scatter_dimension=0, tiled=True)
    ref_all = lax.all_gather(ref_signal, "tm", axis=1, tiled=True)
    ref_ext = jnp.pad(ref_all, ((0, 0), (LAGS, 0)))

    def beam_step(carry, q):
        offset = q * BLOCK_LEN
        table = lag_table(ref_ext, here * length + offset, LAGS)
        segment = lax.dynamic_slice_in_dim(beam, offset, BLOCK_LEN, 2)
        return carry, times_conj(segment, table)

    _, products = lax.scan(beam_step, None, jnp.arange(local_blocks, dtype=jnp.int32))
    cross = lax.psum(products[..., :TAPS].sum(0), "tm")
    got = lax.all_to_all(products, "tm", 3, 0, tiled=True)

    def own_step(gram, q):
        offset = q * BLOCK_LEN
        table = lag_table(ref_ext, offset, LAGS)
        taps = table[:, :TAPS].transpose(1, 0, 2)
        mine = lax.dynamic_slice_in_dim(table, here * lags_local, lags_local, 1)
        return gram + times_conj(taps, table[:, :TAPS]), times_conj(taps, mine)

    start = jnp.zeros((TAPS, 2, TAPS), jnp.float32)
    gram, own = lax.scan(own_step, start, jnp.arange(samples // BLOCK_LEN, dtype=jnp.int32))
    g_real, g_imag = gram[:, 0].T, gram[:, 1].T
    system = jnp.concatenate([jnp.concatenate([g_real, -g_imag], 1), jnp.concatenate([g_imag, g_real], 1)], 0)
    right = jnp.concatenate([cross[:, 0].T, cross[:, 1].T], 0)
    solved = jax.scipy.linalg.cho_solve((jnp.linalg.cholesky(system), True), right)
    b_real, b_imag = solved[:TAPS].T, solved[TAPS:].T
    mixing = jnp.concatenate([jnp.stack([b_real, b_imag], 1), jnp.stack([-b_imag, b_real], 1)], 2)
    stacked = jnp.concatenate([own[:, :, 0], own[:, :, 1]], 1)
    lagged = got - jnp.einsum("mck,qkl->qmcl", mixing, stacked, precision=HIGHEST)
    wave = jnp.asarray(doppler_table(samples // BLOCK_LEN, 0.125 / math.sqrt(samples)))
    wave = wave.reshape(2, samples // BLOCK_LEN, 2, DOPPLER)
    return jnp.einsum("qmcl,cqdk->mdlk", lagged, wave, precision=HIGHEST)


def on_device(ref_signal, surveillance, steering):
    chan_count, tm_count = lax.axis_size("chan"), lax.axis_size("tm")
    beams_local = steering.shape[1] // chan_count
    lags_local = LAGS // tm_count
    fills = (
        LANES % lags_local == 0
        and lags_local % (2 * SUBLANES) == 0
        and beams_local * lags_local == LANES * SUBLANES // 2
        and chan_count > 1
        and chan_count & (chan_count - 1) == 0
        and tm_count > 1
        and tm_count & (tm_count - 1) == 0
        and 2 * surveillance.shape[1] % LANES == 0
        and surveillance.shape[2] % (2 * BATCH * BLOCK_LEN) == 0
    )
    device = tiled_device if fills else plain_device
    return device(ref_signal, surveillance, steering)


def solution(mesh):
    placed = (P(None, "tm"), P(None, "chan", "tm"), P(None, None, "chan"))
    return jax.shard_map(
        on_device,
        mesh=mesh,
        in_specs=placed,
        out_specs=P("chan", None, "tm", None),
        check_vma=False,
    )
```

```python
import functools
import math

import jax
import jax.numpy as jnp
import numpy as np
from jax import lax
from jax.experimental import pallas as pl
from jax.experimental.pallas import tpu as pltpu
from jax.sharding import PartitionSpec as P

LAGS = 256
DOPPLER = 256
TAPS = 64
BLOCK_LEN = 256
LANES = 128
SUBLANES = 8

HIGHEST = lax.Precision.HIGHEST
VMEM_BYTES = 48 * 1024 * 1024


def params():
    return pltpu.CompilerParams(vmem_limit_bytes=VMEM_BYTES)


def halves(x):
    high = x.astype(jnp.bfloat16)
    return high, (x - high.astype(jnp.float32)).astype(jnp.bfloat16)


def dot_nt(a, b, precision=None):
    return lax.dot_general(
        a, b, (((1,), (1,)), ((), ())), precision=precision, preferred_element_type=jnp.float32
    )


def dot_split(a, b):
    (a_high, a_low), (b_high, b_low) = a, b
    left = jnp.concatenate([a_high, a_low], 1)
    right = jnp.concatenate([b_high, b_high], 0)
    return jnp.dot(left, right, preferred_element_type=jnp.float32) + jnp.dot(
        a_high, b_low, preferred_element_type=jnp.float32
    )


def row_sign(shape):
    rows = lax.broadcasted_iota(jnp.int32, shape, 0)
    return jnp.where(rows % SUBLANES < SUBLANES // 2, 1.0, -1.0).astype(jnp.float32)


def lane_sign(shape):
    lanes = lax.broadcasted_iota(jnp.int32, shape, 1)
    return jnp.where(lanes % LANES < LANES // 2, 1.0, -1.0).astype(jnp.float32)


def swap_groups(rows, groups):
    width = LANES // groups
    lane_group = lax.broadcasted_iota(jnp.int32, rows[0].shape, 1) // width
    outs = []
    for j in range(groups):
        out = rows[j]
        for i in range(groups):
            if i != j:
                moved = pltpu.roll(rows[i], (width * (i - j)) % LANES, 1)
                out = jnp.where(lane_group == i, moved, out)
        outs.append(out)
    return outs


CHUNKS = 4


def beam_sent_kernel(chan_count, beams_local, w_hbm, s_hbm, sent_ref, split_ref, kept_w_ref, w_ref, s_ref, w_sem, s_sem):
    me = lax.axis_index("chan")
    depth, length = s_hbm.shape
    width = length // CHUNKS
    w_copy = pltpu.make_async_copy(w_hbm, w_ref, w_sem)
    w_copy.start()
    s_copies = []
    for n in range(CHUNKS):
        cols = pl.ds(n * width, width)
        s_copies.append(pltpu.make_async_copy(s_hbm.at[:, cols], s_ref.at[:, cols], s_sem.at[n]))
        s_copies[n].start()
    half = SUBLANES // 2
    sub = lax.broadcasted_iota(jnp.int32, (SUBLANES, w_hbm.shape[2]), 0)
    top = sub < half

    def weights(parity):
        rows = []
        for e in range(parity, chan_count, 2):
            base = (me ^ e) * beams_local
            for tile in range(beams_local // SUBLANES):
                start = pl.multiple_of(base + tile * SUBLANES, SUBLANES)
                wr = w_ref[0, pl.ds(start, SUBLANES), :]
                wi = w_ref[1, pl.ds(start, SUBLANES), :]
                wr_s = pltpu.roll(wr, half, 0)
                wi_s = pltpu.roll(wi, half, 0)
                first = [jnp.where(top, wr, wi_s), jnp.where(top, -wi, wr_s)]
                second = [jnp.where(top, wr_s, wi), jnp.where(top, -wi_s, wr)]
                rows.append(jnp.concatenate(first, 1))
                rows.append(jnp.concatenate(second, 1))
        return halves(jnp.concatenate(rows, 0))

    w_copy.wait()
    kept_w_ref[0], kept_w_ref[1] = weights(0)
    sent_w = weights(1)
    for n in range(CHUNKS):
        cols = slice(n * width, (n + 1) * width)
        s_copies[n].wait()
        samples = halves(s_ref[:, cols])
        split_ref[0, :, cols], split_ref[1, :, cols] = samples
        sent_ref[:, cols] = dot_split(sent_w, samples)


def beam_sent_call(steering, survey, chan_count, beams_local):
    depth, length = survey.shape
    rows = chan_count * beams_local
    hbm = pl.BlockSpec(memory_space=pltpu.HBM)
    return pl.pallas_call(
        functools.partial(beam_sent_kernel, chan_count, beams_local),
        in_specs=[hbm, hbm],
        out_specs=[pl.BlockSpec(memory_space=pltpu.VMEM)] * 3,
        out_shape=[
            jax.ShapeDtypeStruct((rows, length), jnp.float32),
            jax.ShapeDtypeStruct((2, depth, length), jnp.bfloat16),
            jax.ShapeDtypeStruct((2, rows, depth), jnp.bfloat16),
        ],
        scratch_shapes=[
            pltpu.VMEM(steering.shape, jnp.float32),
            pltpu.VMEM(survey.shape, jnp.float32),
            pltpu.SemaphoreType.DMA,
            pltpu.SemaphoreType.DMA((CHUNKS,)),
        ],
        compiler_params=params(),
        cost_estimate=pl.CostEstimate(
            flops=6 * rows * depth * length, bytes_accessed=4 * length * (depth + 2 * rows), transcendentals=0
        ),
        name="beams_sent",
    )(*(pltpu.with_memory_space_constraint(x, pltpu.HBM) for x in (steering, survey)))


def beam_kept_kernel(split_ref, w_ref, ref_hbm, kept_ref, tiles_ref, ref_ref, ref_sem):
    ref_copy = pltpu.make_async_copy(ref_hbm, ref_ref, ref_sem)
    ref_copy.start()
    length = split_ref.shape[2]
    width = length // CHUNKS
    for n in range(CHUNKS):
        cols = slice(n * width, (n + 1) * width)
        kept_ref[:, cols] = dot_split((w_ref[0], w_ref[1]), (split_ref[0, :, cols], split_ref[1, :, cols]))
    ref_copy.wait()
    for c in range(2):
        for n in range(length // LANES):
            cols = slice(n * LANES, (n + 1) * LANES)
            tiles_ref[c, n : n + 1, :] = ref_ref[c : c + 1, cols]


def beam_kept_call(split, weights, ref):
    depth, length = split.shape[1:]
    rows = weights.shape[1]
    vmem = pl.BlockSpec(memory_space=pltpu.VMEM)
    return pl.pallas_call(
        beam_kept_kernel,
        in_specs=[vmem, vmem, pl.BlockSpec(memory_space=pltpu.HBM)],
        out_specs=[vmem, vmem],
        out_shape=[
            jax.ShapeDtypeStruct((rows, length), jnp.float32),
            jax.ShapeDtypeStruct((2, length // LANES, LANES), jnp.float32),
        ],
        scratch_shapes=[pltpu.VMEM(ref.shape, jnp.float32), pltpu.SemaphoreType.DMA],
        compiler_params=params(),
        cost_estimate=pl.CostEstimate(
            flops=6 * rows * depth * length, bytes_accessed=4 * length * (depth + rows), transcendentals=0
        ),
        name="beams_kept",
    )(split, weights, pltpu.with_memory_space_constraint(ref, pltpu.HBM))


def pair_kernel(tiles_ref, near_ref, out_ref):
    out_ref[0] = tiles_ref[...]
    for c in range(2):
        for n in range(tiles_ref.shape[1]):
            out_ref[1, c, n : n + 1, :] = near_ref[c : c + 1, n * LANES : (n + 1) * LANES]


def pair_call(tiles, near):
    return pl.pallas_call(
        pair_kernel,
        out_shape=jax.ShapeDtypeStruct((2,) + tiles.shape, jnp.float32),
        compiler_params=params(),
        cost_estimate=pl.CostEstimate(flops=0, bytes_accessed=16 * near.size, transcendentals=0),
        name="reference_pair",
    )(tiles, near)


def table_kernel(*refs):
    *part_refs, out_ref = refs
    me = lax.axis_index("tm")
    own = part_refs[0][0]
    rows = own.shape[1]
    edge = jnp.zeros((2, 2, LANES), jnp.float32)
    for n, part_ref in enumerate(part_refs):
        edge = jnp.where((me > 0) & ((me ^ (me - 1)) == 2 * n + 1), part_ref[1, :, rows - 2 :, :], edge)
    for c in range(2):
        line = [edge[c, n : n + 1] for n in range(2)] + [own[c, n : n + 1] for n in range(rows)]
        line = jnp.concatenate(line, 1)
        for g in range(0, LANES, 2 * SUBLANES):
            tiled = jnp.broadcast_to(line, (2 * SUBLANES, line.shape[1]))
            high, low = halves(pltpu.roll(tiled, g, 1, stride=1, stride_axis=0)[:, LANES:])
            out_ref[0, c, g : g + 2 * SUBLANES] = high
            out_ref[1, c, g : g + 2 * SUBLANES] = low


def table_call(parts):
    shape = (2, 2, LANES, LANES * (parts[0].shape[2] + 1))
    return pl.pallas_call(
        table_kernel,
        out_shape=jax.ShapeDtypeStruct(shape, jnp.bfloat16),
        compiler_params=params(),
        cost_estimate=pl.CostEstimate(
            flops=8 * math.prod(shape), bytes_accessed=2 * math.prod(shape), transcendentals=0
        ),
        name="shifted_reference",
    )(*parts)


def lag_kernel(groups, owners, *refs):
    *y_refs, table_ref, out_hbm, out_ref, out_sem = refs
    copies = []

    def send(first, count):
        part = (slice(None), pl.ds(first, count))
        copies.append(pltpu.make_async_copy(out_ref.at[part], out_hbm.at[part], out_sem.at[len(copies)]))
        copies[-1].start()

    y = y_refs[0][...]
    for y_ref in y_refs[1:]:
        y = y + y_ref[...]
    rows, length = y.shape
    blocks = length // BLOCK_LEN
    turned = jnp.concatenate(
        [pltpu.roll(y[r : r + SUBLANES], SUBLANES // 2, 0) for r in range(0, rows, SUBLANES)], 0
    )
    turned = turned * row_sign(turned.shape)
    y_high, y_low = halves(y)
    t_high, t_low = halves(turned)
    both = jnp.concatenate([y_high, y_low], 0)
    turned_both = jnp.concatenate([t_high, t_low], 0)
    taps_sum = None
    for q in range(blocks):
        near = slice(q * BLOCK_LEN + LANES, q * BLOCK_LEN + LANES + BLOCK_LEN)
        far = slice(q * BLOCK_LEN, (q + 1) * BLOCK_LEN)
        cols = slice(q * BLOCK_LEN, (q + 1) * BLOCK_LEN)
        tables = []
        for h in range(2):
            tables.append(
                jnp.concatenate(
                    [
                        jnp.concatenate([table_ref[h, 0, :, near], table_ref[h, 1, :, near]], 1),
                        jnp.concatenate([table_ref[h, 0, :, far], table_ref[h, 1, :, far]], 1),
                    ],
                    0,
                )
            )
        lhs = jnp.concatenate([both[:, cols], turned_both[:, cols]], 1)
        by_high = dot_nt(lhs, tables[0])
        by_low = dot_nt(lhs[:rows], tables[1])
        product = by_high[:rows] + (by_high[rows:] + by_low)
        taps = product[:, :LANES]
        taps_sum = taps if taps_sum is None else taps_sum + taps
        for h in range(LAGS // LANES):
            lanes = slice(h * LANES, (h + 1) * LANES)
            tiles = [product[r : r + SUBLANES, lanes] for r in range(0, rows, SUBLANES)]
            for j, tile in enumerate(swap_groups(tiles, groups)):
                out_ref[h * groups + j, q] = tile
        if q % 2:
            send(q - 1, 2)
    left = lax.broadcasted_iota(jnp.int32, (SUBLANES, LANES), 1) < TAPS
    for i in range(groups // 2):
        a = taps_sum[i * SUBLANES : (i + 1) * SUBLANES]
        other = i + groups // 2
        b = taps_sum[other * SUBLANES : (other + 1) * SUBLANES]
        tile = jnp.where(left, a, pltpu.roll(b, LANES - TAPS, 1))
        for owner in range(owners):
            out_ref[owner, blocks + i] = tile
    send(blocks, groups // 2)
    for copy in copies:
        copy.wait()


def lag_call(ys, table, groups, owners):
    rows, length = ys[0].shape
    blocks = length // BLOCK_LEN
    shape = (owners, blocks + groups // 2, SUBLANES, LANES)
    return pl.pallas_call(
        functools.partial(lag_kernel, groups, owners),
        in_specs=[pl.BlockSpec(memory_space=pltpu.VMEM)] * (len(ys) + 1),
        out_specs=pl.BlockSpec(memory_space=pltpu.HBM),
        out_shape=jax.ShapeDtypeStruct(shape, jnp.float32),
        scratch_shapes=[pltpu.VMEM(shape, jnp.float32), pltpu.SemaphoreType.DMA((blocks // 2 + 1,))],
        compiler_params=params(),
        cost_estimate=pl.CostEstimate(
            flops=12 * rows * LAGS * 2 * length,
            bytes_accessed=4 * math.prod(shape) + 2 * math.prod(table.shape),
            transcendentals=0,
        ),
        name="lag_products",
    )(*ys, table)


BATCH = 4
EDGE = 2


def own_kernel(lags_local, *refs):
    *part_refs, out_ref, line_ref, tail_ref, span_ref, late_ref, taps_a, lags_a, taps_b, lags_b = refs
    me = lax.axis_index("tm")
    part_rows = part_refs[0].shape[2]
    owners = sum(part_ref.shape[0] for part_ref in part_refs)
    samples = owners * part_rows * LANES
    steps = samples // BLOCK_LEN // BATCH
    total_rows = span_ref.shape[1]
    block_rows = BLOCK_LEN // LANES

    span_ref[...] = jnp.zeros_like(span_ref)
    e = 0
    for part_ref in part_refs:
        for i in range(part_ref.shape[0]):
            span_ref[:, pl.ds(EDGE + (me ^ e) * part_rows, part_rows), :] = part_ref[i]
            e += 1
    late_rows = (me * lags_local) // LANES
    late_lanes = lax.rem(me * lags_local, LANES)
    turned = [pltpu.roll(span_ref[c], late_lanes, 1) for c in range(2)]
    before = [pltpu.roll(x, 1, 0) for x in turned]
    lanes = lax.broadcasted_iota(jnp.int32, (total_rows, LANES), 1)
    for c in range(2):
        late_ref[c] = pltpu.roll(jnp.where(lanes < late_lanes, before[c], turned[c]), late_rows, 0)

    def line_of(ref, c, first, count):
        return jnp.concatenate([ref[c, pl.ds(first + n, 1), :] for n in range(count)], 1)

    def shifted(line, by):
        tiled = jnp.broadcast_to(line, (2 * SUBLANES, line.shape[1]))
        return pltpu.roll(tiled, by, 1, stride=1, stride_axis=0)[:, LANES:]

    def keep(ref, row, value):
        high, low = halves(value)
        half = ref.shape[0] // 2
        ref[row : row + 2 * SUBLANES, :] = high
        ref[half + row : half + row + 2 * SUBLANES, :] = low

    def build(n, taps_ref, lags_ref):
        first = EDGE - 1 + n * BATCH * block_rows
        count = BATCH * block_rows + 1
        lines = [line_of(span_ref, c, first, count) for c in range(2)]
        for c in range(2):
            for g in range(0, TAPS, 2 * SUBLANES):
                keep(taps_ref, c * TAPS + g, shifted(lines[c], g))
            late = line_of(late_ref, c, first, count)
            for g in range(0, lags_local, 2 * SUBLANES):
                keep(lags_ref, c * lags_local + g, shifted(late, g))
        pad = jnp.zeros((2 * SUBLANES - 2, BATCH * BLOCK_LEN), jnp.float32)
        keep(lags_ref, 2 * lags_local, jnp.concatenate([line[:, LANES:] for line in lines] + [pad], 0))

    turn = lane_sign((lags_local, LANES))

    def use(n, taps_ref, lags_ref):
        count = lags_ref.shape[0] // 2
        for b in range(BATCH):
            cols = slice(b * BLOCK_LEN, (b + 1) * BLOCK_LEN)
            product = dot_nt(lags_ref[:, cols], taps_ref[:, cols])
            product = product[:count, :LANES] + (product[:count, LANES:] + product[count:, :LANES])
            by_real = product[:lags_local]
            by_imag = product[lags_local : 2 * lags_local]
            rows = pl.ds(pl.multiple_of((n * BATCH + b) * lags_local, lags_local), lags_local)
            high, low = halves(by_real + turn * pltpu.roll(by_imag, TAPS, 1))
            out_ref[0, rows, :] = high
            out_ref[1, rows, :] = low
            line_ref[...] += product[2 * lags_local : 2 * lags_local + SUBLANES]

    line_ref[...] = jnp.zeros_like(line_ref)
    build(0, taps_a, lags_a)

    def pair(m, carry):
        build(2 * m + 1, taps_b, lags_b)
        use(2 * m, taps_a, lags_a)
        build(jnp.minimum(2 * m + 2, steps - 1), taps_a, lags_a)
        use(2 * m + 1, taps_b, lags_b)
        return carry

    lax.fori_loop(0, steps // 2, pair, 0)
    tail = []
    for c in range(2):
        line = line_of(span_ref, c, EDGE + owners * part_rows - 1, 2)
        tail += [shifted(line, g) for g in range(0, TAPS, 2 * SUBLANES)]
    tail = jnp.concatenate(tail, 0)
    tail_ref[...] = dot_nt(tail, tail, HIGHEST)


def own_call(parts, lags_local):
    part_rows = parts[0].shape[2]
    span_rows = part_rows * sum(part.shape[0] for part in parts)
    rows = span_rows * LANES // BLOCK_LEN * lags_local
    held_rows = -(-(span_rows + 2 * EDGE) // SUBLANES) * SUBLANES
    width = BATCH * BLOCK_LEN
    taps = pltpu.VMEM((4 * TAPS, width), jnp.bfloat16)
    lags = pltpu.VMEM((4 * lags_local + 4 * SUBLANES, width), jnp.bfloat16)
    span = pltpu.VMEM((2, held_rows, LANES), jnp.float32)
    return pl.pallas_call(
        functools.partial(own_kernel, lags_local),
        out_shape=[
            jax.ShapeDtypeStruct((2, rows, 2 * TAPS), jnp.bfloat16),
            jax.ShapeDtypeStruct((SUBLANES, 2 * TAPS), jnp.float32),
            jax.ShapeDtypeStruct((2 * TAPS, 2 * TAPS), jnp.float32),
        ],
        scratch_shapes=[span, span, taps, lags, taps, lags],
        compiler_params=params(),
        cost_estimate=pl.CostEstimate(
            flops=24 * rows * BLOCK_LEN * 2 * TAPS, bytes_accessed=4 * rows * 2 * TAPS, transcendentals=0
        ),
        name="reference_products",
    )(*parts)


def as_factor(a):
    return jnp.concatenate([a, -lane_sign(a.shape) * pltpu.roll(a, a.shape[0], 1)], 0)


def solver_kernel(line_ref, tail_ref, gram_ref, solver_ref):
    total = line_ref[...]
    line = total[0:1] + lane_sign((1, LANES)) * pltpu.roll(total[1:2], TAPS, 1)
    low = lax.broadcasted_iota(jnp.int32, (1, LANES), 1) < TAPS
    line_r = jnp.where(low, line, 0.0)
    line_i = jnp.where(low, pltpu.roll(line, TAPS, 1), 0.0)
    cols = lax.broadcasted_iota(jnp.int32, (TAPS, TAPS), 1)
    rows = lax.broadcasted_iota(jnp.int32, (TAPS, TAPS), 0)
    above = cols > rows

    def upper(x):
        spread = pltpu.roll(jnp.broadcast_to(x, (TAPS, LANES)), 0, 1, stride=1, stride_axis=0)
        return spread[:, :TAPS]

    up_r = upper(line_r)
    up_i = jnp.where(above, upper(line_i), 0.0)
    strict_r = jnp.where(above, up_r, 0.0)
    diag_r = jnp.where(cols == rows, up_r, 0.0)
    tails = tail_ref[...]
    gram_r = strict_r + strict_r.T + diag_r - (tails[:TAPS, :TAPS] + tails[TAPS:, TAPS:])
    gram_i = up_i - up_i.T - (tails[:TAPS, TAPS:] - tails[TAPS:, :TAPS])
    gram = jnp.concatenate([gram_r, gram_i], 1)
    gram_halves = halves(as_factor(gram))
    gram_ref[0], gram_ref[1] = gram_halves
    one = (
        lax.broadcasted_iota(jnp.int32, gram.shape, 0) == lax.broadcasted_iota(jnp.int32, gram.shape, 1)
    ).astype(jnp.float32)
    bound = jnp.max(jnp.sum(jnp.abs(gram), axis=1, keepdims=True), axis=0, keepdims=True)

    def again(state):
        count, left, _ = state
        return (count < 60) & (left > 1e-3)

    def newton(state):
        count, _, x = state
        x_halves = halves(x)
        seen = dot_split(x_halves, gram_halves)
        left = jnp.max(jnp.abs(seen - one))
        x = 2.0 * x - dot_split(halves(seen), halves(as_factor(x)))
        return count + 1, left, x

    start = (jnp.int32(0), jnp.float32(1.0), one * (1.0 / bound))
    _, _, inverse = lax.while_loop(again, newton, start)
    solver_ref[0], solver_ref[1] = halves(as_factor(inverse))


def solver_call(line, tail):
    out = jax.ShapeDtypeStruct((2,) + tail.shape, jnp.bfloat16)
    return pl.pallas_call(
        solver_kernel,
        out_shape=[out, out],
        compiler_params=params(),
        cost_estimate=pl.CostEstimate(flops=500_000_000, bytes_accessed=200_000, transcendentals=0),
        name="gram_inverse",
    )(line, tail)


def doppler_table(block_count, scale):
    phase = (np.arange(block_count)[:, None] * np.arange(DOPPLER)[None, :] % DOPPLER) * (2.0 * math.pi / DOPPLER)
    cosine, sine = np.cos(phase), np.sin(phase)
    upper = np.concatenate([cosine, -sine], 1)
    lower = np.concatenate([sine, cosine], 1)
    return (np.concatenate([upper, lower], 0) * scale).astype(np.float32)


def map_kernel(groups, got_ref, own_ref, gram_ref, solver_ref, wave_ref, out_hbm, held_ref, out_ref, out_sem):
    owners, pieces = got_ref.shape[:2]
    blocks = pieces - groups // 2
    lags_local = LANES // groups
    total = owners * blocks
    left = lax.broadcasted_iota(jnp.int32, (SUBLANES, LANES), 1) < TAPS
    sign = row_sign((SUBLANES, LANES))
    rows = [None] * groups
    for i in range(groups // 2):
        tile = got_ref[0, blocks + i]
        for owner in range(1, owners):
            tile = tile + got_ref[owner, blocks + i]
        swapped = pltpu.roll(tile, TAPS, 1)
        for part, here, there in ((i, tile, swapped), (i + groups // 2, swapped, tile)):
            other = -sign * pltpu.roll(there, SUBLANES // 2, 0)
            rows[part] = jnp.where(left, here, other)
    cross = jnp.concatenate(rows, 0)
    solver = (solver_ref[0], solver_ref[1])
    taps = dot_split(halves(cross), solver)
    rest = cross - dot_split(halves(taps), (gram_ref[0], gram_ref[1]))
    taps = taps + dot_split(halves(rest), solver)
    taps_high, taps_low = halves(taps)
    taps_both = jnp.concatenate([taps_high, taps_low], 1)
    for q in range(0, total, 2 * groups):
        own = slice(q * lags_local, (q + 2 * groups) * lags_local)
        own_high = own_ref[0, own, :]
        clutter = dot_nt(taps_both, jnp.concatenate([own_high, own_high], 1)) + dot_nt(taps_high, own_ref[1, own, :])
        for h in range(2):
            lanes = slice(h * LANES, (h + 1) * LANES)
            tiles = [clutter[r : r + SUBLANES, lanes] for r in range(0, groups * SUBLANES, SUBLANES)]
            for j, tile in enumerate(swap_groups(tiles, groups)):
                at = q + h * groups + j
                held_ref[at * SUBLANES : (at + 1) * SUBLANES, :] = got_ref[at // blocks, at % blocks] - tile
    half = SUBLANES // 2
    wave = (wave_ref[0], wave_ref[1])
    copies = []
    for g in range(half):
        parts = [held_ref[pl.ds(c * half + g, total, stride=SUBLANES), :] for c in range(2)]
        spectrum = dot_split(halves(jnp.concatenate(parts, 0).T), wave)
        for i in range(groups):
            beam = half * i + g
            for c in range(2):
                out_ref[beam, c] = spectrum[i * lags_local : (i + 1) * lags_local, c * DOPPLER : (c + 1) * DOPPLER]
            copies.append(pltpu.make_async_copy(out_ref.at[beam], out_hbm.at[beam], out_sem.at[beam]))
            copies[-1].start()
    for copy in copies:
        copy.wait()


def map_call(got, own, gram, solver, wave, groups, beams_local):
    total = got.shape[0] * (got.shape[1] - groups // 2)
    lags_local = LANES // groups
    shape = (beams_local, 2, lags_local, DOPPLER)
    return pl.pallas_call(
        functools.partial(map_kernel, groups),
        in_specs=[pl.BlockSpec(memory_space=pltpu.VMEM)] * 5,
        out_specs=pl.BlockSpec(memory_space=pltpu.HBM),
        out_shape=jax.ShapeDtypeStruct(shape, jnp.float32),
        scratch_shapes=[
            pltpu.VMEM((total * SUBLANES, LANES), jnp.float32),
            pltpu.VMEM(shape, jnp.float32),
            pltpu.SemaphoreType.DMA((beams_local,)),
        ],
        compiler_params=params(),
        cost_estimate=pl.CostEstimate(
            flops=12 * math.prod(shape) * total, bytes_accessed=4 * math.prod(shape), transcendentals=0
        ),
        name="range_doppler",
    )(got, own, gram, solver, wave)


def swap(x, axis, by):
    pairs = [(i, i ^ by) for i in range(lax.axis_size(axis))]
    return lax.ppermute(x, axis, pairs)


def tiled_device(ref_signal, surveillance, steering):
    chan_count, tm_count = lax.axis_size("chan"), lax.axis_size("tm")
    channels, length = surveillance.shape[1:]
    beams_local = steering.shape[1] // chan_count
    lags_local = LAGS // tm_count
    groups = LANES // lags_local
    samples = length * tm_count

    survey = surveillance.reshape(2 * channels, length)
    near = swap(ref_signal, "tm", 1)
    moved, split, weights = beam_sent_call(steering, survey, chan_count, beams_local)
    shape = (chan_count // 2, 2 * beams_local, length)
    moved = swap(moved, "chan", 1)
    kept, tiles = beam_kept_call(split, weights, ref_signal)
    near, moved = lax.optimization_barrier((near, moved))
    parts = [kept.reshape(shape), moved.reshape(shape)]
    by = 2
    while by < chan_count:
        sent = parts[0][1::2]
        for part in parts[1:]:
            sent = sent + part[1::2]
        tiles, sent = lax.optimization_barrier((tiles, sent))
        parts = [part[::2] for part in parts] + [swap(sent, "chan", by)]
        by *= 2
    pair = pair_call(tiles, near)
    ref_parts = [pair] + [swap(pair, "tm", by) for by in range(2, tm_count, 2)]
    table = table_call(ref_parts)
    pieces = lag_call([part[0] for part in parts], table, groups, tm_count)
    got = lax.all_to_all(pieces, "tm", 0, 0, tiled=True)
    own, line, tail = own_call(ref_parts, lags_local)
    gram, solver = solver_call(line, tail)
    wave = doppler_table(samples // BLOCK_LEN, 0.125 / math.sqrt(samples))
    high = wave.astype(jnp.bfloat16)
    wave = np.stack([high, (wave - high.astype(np.float32)).astype(jnp.bfloat16)])
    return map_call(got, own, gram, solver, jnp.asarray(wave), groups, beams_local)


def lag_table(ref_ext, offset, lags):
    window = lax.dynamic_slice_in_dim(ref_ext, offset, BLOCK_LEN + LAGS, 1)
    span = BLOCK_LEN + LAGS
    tiled = jnp.tile(jnp.pad(window, ((0, 0), (0, 1))), (1, lags))[:, : lags * span]
    return tiled.reshape(2, lags, span)[:, :, LAGS:]


def times_conj(a, b):
    real = jnp.einsum("...t,lt->...l", a[..., 0, :], b[0], precision=HIGHEST) + jnp.einsum(
        "...t,lt->...l", a[..., 1, :], b[1], precision=HIGHEST
    )
    imag = jnp.einsum("...t,lt->...l", a[..., 1, :], b[0], precision=HIGHEST) - jnp.einsum(
        "...t,lt->...l", a[..., 0, :], b[1], precision=HIGHEST
    )
    return jnp.stack([real, imag], -2)


def plain_device(ref_signal, surveillance, steering):
    chan_count, tm_count = lax.axis_size("chan"), lax.axis_size("tm")
    length = surveillance.shape[2]
    beams = steering.shape[1]
    lags_local = LAGS // tm_count
    samples = length * tm_count
    local_blocks = length // BLOCK_LEN
    here = lax.axis_index("tm")

    w_real, w_imag = steering
    real = jnp.dot(w_real, surveillance[0], precision=HIGHEST) - jnp.dot(w_imag, surveillance[1], precision=HIGHEST)
    imag = jnp.dot(w_imag, surveillance[0], precision=HIGHEST) + jnp.dot(w_real, surveillance[1], precision=HIGHEST)
    beam = lax.psum_scatter(jnp.stack([real, imag], 1), "chan", scatter_dimension=0, tiled=True)
    ref_all = lax.all_gather(ref_signal, "tm", axis=1, tiled=True)
    ref_ext = jnp.pad(ref_all, ((0, 0), (LAGS, 0)))

    def beam_step(carry, q):
        offset = q * BLOCK_LEN
        table = lag_table(ref_ext, here * length + offset, LAGS)
        segment = lax.dynamic_slice_in_dim(beam, offset, BLOCK_LEN, 2)
        return carry, times_conj(segment, table)

    _, products = lax.scan(beam_step, None, jnp.arange(local_blocks, dtype=jnp.int32))
    cross = lax.psum(products[..., :TAPS].sum(0), "tm")
    got = lax.all_to_all(products, "tm", 3, 0, tiled=True)

    def own_step(gram, q):
        offset = q * BLOCK_LEN
        table = lag_table(ref_ext, offset, LAGS)
        taps = table[:, :TAPS].transpose(1, 0, 2)
        mine = lax.dynamic_slice_in_dim(table, here * lags_local, lags_local, 1)
        return gram + times_conj(taps, table[:, :TAPS]), times_conj(taps, mine)

    start = jnp.zeros((TAPS, 2, TAPS), jnp.float32)
    gram, own = lax.scan(own_step, start, jnp.arange(samples // BLOCK_LEN, dtype=jnp.int32))
    g_real, g_imag = gram[:, 0].T, gram[:, 1].T
    system = jnp.concatenate([jnp.concatenate([g_real, -g_imag], 1), jnp.concatenate([g_imag, g_real], 1)], 0)
    right = jnp.concatenate([cross[:, 0].T, cross[:, 1].T], 0)
    solved = jax.scipy.linalg.cho_solve((jnp.linalg.cholesky(system), True), right)
    b_real, b_imag = solved[:TAPS].T, solved[TAPS:].T
    mixing = jnp.concatenate([jnp.stack([b_real, b_imag], 1), jnp.stack([-b_imag, b_real], 1)], 2)
    stacked = jnp.concatenate([own[:, :, 0], own[:, :, 1]], 1)
    lagged = got - jnp.einsum("mck,qkl->qmcl", mixing, stacked, precision=HIGHEST)
    wave = jnp.asarray(doppler_table(samples // BLOCK_LEN, 0.125 / math.sqrt(samples)))
    wave = wave.reshape(2, samples // BLOCK_LEN, 2, DOPPLER)
    return jnp.einsum("qmcl,cqdk->mdlk", lagged, wave, precision=HIGHEST)


def on_device(ref_signal, surveillance, steering):
    chan_count, tm_count = lax.axis_size("chan"), lax.axis_size("tm")
    beams_local = steering.shape[1] // chan_count
    lags_local = LAGS // tm_count
    fills = (
        LANES % lags_local == 0
        and lags_local % (2 * SUBLANES) == 0
        and beams_local * lags_local == LANES * SUBLANES // 2
        and chan_count > 1
        and chan_count & (chan_count - 1) == 0
        and tm_count > 1
        and tm_count & (tm_count - 1) == 0
        and 2 * surveillance.shape[1] % LANES == 0
        and surveillance.shape[2] % (2 * BATCH * BLOCK_LEN) == 0
    )
    device = tiled_device if fills else plain_device
    return device(ref_signal, surveillance, steering)


def solution(mesh):
    placed = (P(None, "tm"), P(None, "chan", "tm"), P(None, None, "chan"))
    return jax.shard_map(
        on_device,
        mesh=mesh,
        in_specs=placed,
        out_specs=P("chan", None, "tm", None),
        check_vma=False,
    )
```

```python
import functools
import math

import jax
import jax.numpy as jnp
import numpy as np
from jax import lax
from jax.experimental import pallas as pl
from jax.experimental.pallas import tpu as pltpu
from jax.sharding import PartitionSpec as P

LAGS = 256
DOPPLER = 256
TAPS = 64
BLOCK_LEN = 256
LANES = 128
SUBLANES = 8
EDGE = 2

HIGHEST = lax.Precision.HIGHEST
VMEM_BYTES = 48 * 1024 * 1024


def params():
    return pltpu.CompilerParams(vmem_limit_bytes=VMEM_BYTES)


def halves(x):
    high = x.astype(jnp.bfloat16)
    return high, (x - high.astype(jnp.float32)).astype(jnp.bfloat16)


def dot_nt(a, b, precision=None):
    return lax.dot_general(
        a, b, (((1,), (1,)), ((), ())), precision=precision, preferred_element_type=jnp.float32
    )


def dot_split(a, b):
    (a_high, a_low), (b_high, b_low) = a, b
    left = jnp.concatenate([a_high, a_low], 1)
    right = jnp.concatenate([b_high, b_high], 0)
    return jnp.dot(left, right, preferred_element_type=jnp.float32) + jnp.dot(
        a_high, b_low, preferred_element_type=jnp.float32
    )


def row_sign(shape):
    rows = lax.broadcasted_iota(jnp.int32, shape, 0)
    return jnp.where(rows % SUBLANES < SUBLANES // 2, 1.0, -1.0).astype(jnp.float32)


def lane_sign(shape):
    lanes = lax.broadcasted_iota(jnp.int32, shape, 1)
    return jnp.where(lanes % LANES < LANES // 2, 1.0, -1.0).astype(jnp.float32)


def swap_groups(rows, groups):
    width = LANES // groups
    lane_group = lax.broadcasted_iota(jnp.int32, rows[0].shape, 1) // width
    outs = []
    for j in range(groups):
        out = rows[j]
        for i in range(groups):
            if i != j:
                moved = pltpu.roll(rows[i], (width * (i - j)) % LANES, 1)
                out = jnp.where(lane_group == i, moved, out)
        outs.append(out)
    return outs


SPANS = 2
CHUNKS = 2


def beam_first_kernel(
    chan_count, beams_local, w_hbm, s_hbm, kept_ref, sent_ref, later_ref, weights_ref, w_ref, s_ref, w_sem, s_sem, later_sem
):
    me = lax.axis_index("chan")
    span = s_ref.shape[1]
    width = span // CHUNKS
    w_copy = pltpu.make_async_copy(w_hbm, w_ref, w_sem)
    w_copy.start()
    s_copies = []
    for n in range(CHUNKS):
        cols = pl.ds(n * width, width)
        s_copies.append(pltpu.make_async_copy(s_hbm.at[:, cols], s_ref.at[:, cols], s_sem.at[n]))
        s_copies[n].start()
    later_copy = pltpu.make_async_copy(s_hbm.at[:, pl.ds(span, later_ref.shape[1])], later_ref, later_sem)
    later_copy.start()
    half = SUBLANES // 2
    sub = lax.broadcasted_iota(jnp.int32, (SUBLANES, w_hbm.shape[2]), 0)
    top = sub < half
    w_copy.wait()
    rows = []
    for parity in range(2):
        for e in range(parity, chan_count, 2):
            base = (me ^ e) * beams_local
            for tile in range(beams_local // SUBLANES):
                start = pl.multiple_of(base + tile * SUBLANES, SUBLANES)
                wr = w_ref[0, pl.ds(start, SUBLANES), :]
                wi = w_ref[1, pl.ds(start, SUBLANES), :]
                wr_s = pltpu.roll(wr, half, 0)
                wi_s = pltpu.roll(wi, half, 0)
                first = [jnp.where(top, wr, wi_s), jnp.where(top, -wi, wr_s)]
                second = [jnp.where(top, wr_s, wi), jnp.where(top, -wi_s, wr)]
                rows.append(jnp.concatenate(first, 1))
                rows.append(jnp.concatenate(second, 1))
    weights = halves(jnp.concatenate(rows, 0))
    weights_ref[0], weights_ref[1] = weights
    mid = weights[0].shape[0] // 2
    for n in range(CHUNKS):
        cols = slice(n * width, (n + 1) * width)
        s_copies[n].wait()
        product = dot_split(weights, halves(s_ref[:, cols]))
        kept_ref[:, cols] = product[:mid]
        sent_ref[:, cols] = product[mid:]
    later_copy.wait()


def beam_first_call(steering, survey, chan_count, beams_local):
    depth, length = survey.shape
    span = length // SPANS
    rows = chan_count * beams_local
    out = jax.ShapeDtypeStruct((rows, span), jnp.float32)
    hbm = pl.BlockSpec(memory_space=pltpu.HBM)
    return pl.pallas_call(
        functools.partial(beam_first_kernel, chan_count, beams_local),
        in_specs=[hbm, hbm],
        out_specs=[pl.BlockSpec(memory_space=pltpu.VMEM)] * 4,
        out_shape=[
            out,
            out,
            jax.ShapeDtypeStruct((depth, length - span), jnp.float32),
            jax.ShapeDtypeStruct((2, 2 * rows, depth), jnp.bfloat16),
        ],
        scratch_shapes=[
            pltpu.VMEM(steering.shape, jnp.float32),
            pltpu.VMEM((depth, span), jnp.float32),
            pltpu.SemaphoreType.DMA,
            pltpu.SemaphoreType.DMA((CHUNKS,)),
            pltpu.SemaphoreType.DMA,
        ],
        compiler_params=params(),
        cost_estimate=pl.CostEstimate(
            flops=12 * rows * depth * span, bytes_accessed=4 * length * (depth + rows), transcendentals=0
        ),
        name="beams_first",
    )(*(pltpu.with_memory_space_constraint(x, pltpu.HBM) for x in (steering, survey)))


def beam_later_kernel(later_ref, weights_ref, ref_hbm, kept_ref, sent_ref, tiles_ref, edge_ref, ref_ref, ref_sem):
    ref_copy = pltpu.make_async_copy(ref_hbm, ref_ref, ref_sem)
    ref_copy.start()
    product = dot_split((weights_ref[0], weights_ref[1]), halves(later_ref[...]))
    mid = product.shape[0] // 2
    kept_ref[...] = product[:mid]
    sent_ref[...] = product[mid:]
    ref_copy.wait()
    edge_ref[...] = jnp.zeros_like(edge_ref)
    count = tiles_ref.shape[1]
    for c in range(2):
        for n in range(count):
            row = ref_ref[c : c + 1, n * LANES : (n + 1) * LANES]
            tiles_ref[c, n : n + 1, :] = row
            if n >= count - EDGE:
                at = SUBLANES * c + n + EDGE - count
                edge_ref[at : at + 1, :] = row


def beam_later_call(later, weights, ref):
    depth, span = later.shape
    rows = weights.shape[1] // 2
    vmem = pl.BlockSpec(memory_space=pltpu.VMEM)
    out = jax.ShapeDtypeStruct((rows, span), jnp.float32)
    return pl.pallas_call(
        beam_later_kernel,
        in_specs=[vmem, vmem, pl.BlockSpec(memory_space=pltpu.HBM)],
        out_specs=[vmem] * 4,
        out_shape=[
            out,
            out,
            jax.ShapeDtypeStruct((2, ref.shape[1] // LANES, LANES), jnp.float32),
            jax.ShapeDtypeStruct((2 * SUBLANES, LANES), jnp.float32),
        ],
        scratch_shapes=[pltpu.VMEM(ref.shape, jnp.float32), pltpu.SemaphoreType.DMA],
        compiler_params=params(),
        cost_estimate=pl.CostEstimate(
            flops=12 * rows * depth * span, bytes_accessed=4 * span * (depth + 2 * rows), transcendentals=0
        ),
        name="beams_later",
    )(later, weights, pltpu.with_memory_space_constraint(ref, pltpu.HBM))


def pair_kernel(tiles_ref, near_ref, _, out_ref):
    out_ref[0] = tiles_ref[...]
    for c in range(2):
        for n in range(tiles_ref.shape[1]):
            out_ref[1, c, n : n + 1, :] = near_ref[c : c + 1, n * LANES : (n + 1) * LANES]


def pair_call(tiles, near, after):
    vmem = pl.BlockSpec(memory_space=pltpu.VMEM)
    return pl.pallas_call(
        pair_kernel,
        in_specs=[vmem, vmem, pl.BlockSpec(memory_space=pl.ANY)],
        out_shape=jax.ShapeDtypeStruct((2,) + tiles.shape, jnp.float32),
        compiler_params=params(),
        cost_estimate=pl.CostEstimate(flops=0, bytes_accessed=16 * near.size, transcendentals=0),
        name="reference_pair",
    )(tiles, near, after)


def table_kernel(edge_ref, tiles_ref, out_ref):
    rows = tiles_ref.shape[1]
    for c in range(2):
        line = [edge_ref[SUBLANES * c + n : SUBLANES * c + n + 1, :] for n in range(EDGE)]
        line = jnp.concatenate(line + [tiles_ref[c, n : n + 1, :] for n in range(rows)], 1)
        for g in range(0, LANES, 2 * SUBLANES):
            tiled = jnp.broadcast_to(line, (2 * SUBLANES, line.shape[1]))
            high, low = halves(pltpu.roll(tiled, g, 1, stride=1, stride_axis=0)[:, LANES:])
            out_ref[0, c, g : g + 2 * SUBLANES] = high
            out_ref[1, c, g : g + 2 * SUBLANES] = low


def table_call(edge, tiles):
    shape = (2, 2, LANES, LANES * (tiles.shape[1] + 1))
    return pl.pallas_call(
        table_kernel,
        out_shape=jax.ShapeDtypeStruct(shape, jnp.bfloat16),
        compiler_params=params(),
        cost_estimate=pl.CostEstimate(
            flops=8 * math.prod(shape), bytes_accessed=2 * math.prod(shape), transcendentals=0
        ),
        name="shifted_reference",
    )(edge, tiles)


def lag_kernel(groups, part_count, first, blocks, *refs):
    y_refs, table_ref, refs = refs[:part_count], refs[part_count], refs[part_count + 1 :]
    if first:
        before_ref, _, *refs = refs
    out_hbm, after_ref, out_ref, out_sem = refs
    copies = []

    def send(start, count):
        part = (slice(None), pl.ds(start, count))
        copies.append(pltpu.make_async_copy(out_ref.at[part], out_hbm.at[part], out_sem.at[len(copies)]))
        copies[-1].start()

    y = y_refs[0][...]
    for y_ref in y_refs[1:]:
        y = y + y_ref[...]
    rows, length = y.shape
    count = length // BLOCK_LEN
    turned = jnp.concatenate(
        [pltpu.roll(y[r : r + SUBLANES], SUBLANES // 2, 0) for r in range(0, rows, SUBLANES)], 0
    )
    turned = turned * row_sign(turned.shape)
    y_high, y_low = halves(y)
    t_high, t_low = halves(turned)
    both = jnp.concatenate([y_high, y_low], 0)
    turned_both = jnp.concatenate([t_high, t_low], 0)
    taps_sum = before_ref[...] if first else None
    for n in range(count):
        q = first + n
        near = slice(q * BLOCK_LEN + LANES, q * BLOCK_LEN + LANES + BLOCK_LEN)
        far = slice(q * BLOCK_LEN, (q + 1) * BLOCK_LEN)
        cols = slice(n * BLOCK_LEN, (n + 1) * BLOCK_LEN)
        tables = []
        for h in range(2):
            tables.append(
                jnp.concatenate(
                    [
                        jnp.concatenate([table_ref[h, 0, :, near], table_ref[h, 1, :, near]], 1),
                        jnp.concatenate([table_ref[h, 0, :, far], table_ref[h, 1, :, far]], 1),
                    ],
                    0,
                )
            )
        lhs = jnp.concatenate([both[:, cols], turned_both[:, cols]], 1)
        by_high = dot_nt(lhs, tables[0])
        by_low = dot_nt(lhs[:rows], tables[1])
        product = by_high[:rows] + (by_high[rows:] + by_low)
        taps = product[:, :LANES]
        taps_sum = taps if taps_sum is None else taps_sum + taps
        for h in range(LAGS // LANES):
            lanes = slice(h * LANES, (h + 1) * LANES)
            tiles = [product[r : r + SUBLANES, lanes] for r in range(0, rows, SUBLANES)]
            for j, tile in enumerate(swap_groups(tiles, groups)):
                out_ref[h * groups + j, q] = tile
        if n % 2:
            send(q - 1, 2)
    after_ref[...] = taps_sum
    if first + count == blocks:
        left = lax.broadcasted_iota(jnp.int32, (SUBLANES, LANES), 1) < TAPS
        for i in range(groups // 2):
            a = taps_sum[i * SUBLANES : (i + 1) * SUBLANES]
            other = i + groups // 2
            b = taps_sum[other * SUBLANES : (other + 1) * SUBLANES]
            tile = jnp.where(left, a, pltpu.roll(b, LANES - TAPS, 1))
            for owner in range(out_ref.shape[0]):
                out_ref[owner, blocks + i] = tile
        send(blocks, groups // 2)
    for copy in copies:
        copy.wait()


def lag_call(ys, table, groups, owners, first, blocks, before=None):
    rows, length = ys[0].shape
    shape = (owners, blocks + groups // 2, SUBLANES, LANES)
    vmem, hbm = pl.BlockSpec(memory_space=pltpu.VMEM), pl.BlockSpec(memory_space=pltpu.HBM)
    operands = [*ys, table]
    in_specs = [vmem] * len(operands)
    aliases = {}
    if before is not None:
        pieces, taps_sum = before
        operands += [taps_sum, pieces]
        in_specs += [vmem, hbm]
        aliases = {len(operands) - 1: 0}
    return pl.pallas_call(
        functools.partial(lag_kernel, groups, len(ys), first, blocks),
        in_specs=in_specs,
        out_specs=[hbm, vmem],
        out_shape=[jax.ShapeDtypeStruct(shape, jnp.float32), jax.ShapeDtypeStruct((rows, LANES), jnp.float32)],
        input_output_aliases=aliases,
        scratch_shapes=[
            pltpu.VMEM(shape, jnp.float32),
            pltpu.SemaphoreType.DMA((length // BLOCK_LEN // 2 + 1,)),
        ],
        compiler_params=params(),
        cost_estimate=pl.CostEstimate(
            flops=12 * rows * LAGS * 2 * length,
            bytes_accessed=4 * math.prod(shape) + 2 * math.prod(table.shape),
            transcendentals=0,
        ),
        name="lag_products",
    )(*operands)


BATCH = 4


def own_kernel(lags_local, *refs):
    *part_refs, _, out_ref, line_ref, tail_ref, span_ref, late_ref, taps_a, lags_a, taps_b, lags_b = refs
    me = lax.axis_index("tm")
    part_rows = part_refs[0].shape[2]
    owners = sum(part_ref.shape[0] for part_ref in part_refs)
    samples = owners * part_rows * LANES
    steps = samples // BLOCK_LEN // BATCH
    total_rows = span_ref.shape[1]
    block_rows = BLOCK_LEN // LANES

    span_ref[...] = jnp.zeros_like(span_ref)
    e = 0
    for part_ref in part_refs:
        for i in range(part_ref.shape[0]):
            span_ref[:, pl.ds(EDGE + (me ^ e) * part_rows, part_rows), :] = part_ref[i]
            e += 1
    late_rows = (me * lags_local) // LANES
    late_lanes = lax.rem(me * lags_local, LANES)
    turned = [pltpu.roll(span_ref[c], late_lanes, 1) for c in range(2)]
    before = [pltpu.roll(x, 1, 0) for x in turned]
    lanes = lax.broadcasted_iota(jnp.int32, (total_rows, LANES), 1)
    for c in range(2):
        late_ref[c] = pltpu.roll(jnp.where(lanes < late_lanes, before[c], turned[c]), late_rows, 0)

    def line_of(ref, c, first, count):
        return jnp.concatenate([ref[c, pl.ds(first + n, 1), :] for n in range(count)], 1)

    def shifted(line, by):
        tiled = jnp.broadcast_to(line, (2 * SUBLANES, line.shape[1]))
        return pltpu.roll(tiled, by, 1, stride=1, stride_axis=0)[:, LANES:]

    def keep(ref, row, value):
        high, low = halves(value)
        half = ref.shape[0] // 2
        ref[row : row + 2 * SUBLANES, :] = high
        ref[half + row : half + row + 2 * SUBLANES, :] = low

    def build(n, taps_ref, lags_ref):
        first = EDGE - 1 + n * BATCH * block_rows
        count = BATCH * block_rows + 1
        lines = [line_of(span_ref, c, first, count) for c in range(2)]
        for c in range(2):
            for g in range(0, TAPS, 2 * SUBLANES):
                keep(taps_ref, c * TAPS + g, shifted(lines[c], g))
            late = line_of(late_ref, c, first, count)
            for g in range(0, lags_local, 2 * SUBLANES):
                keep(lags_ref, c * lags_local + g, shifted(late, g))
        pad = jnp.zeros((2 * SUBLANES - 2, BATCH * BLOCK_LEN), jnp.float32)
        keep(lags_ref, 2 * lags_local, jnp.concatenate([line[:, LANES:] for line in lines] + [pad], 0))

    turn = lane_sign((lags_local, LANES))

    def use(n, taps_ref, lags_ref):
        count = lags_ref.shape[0] // 2
        for b in range(BATCH):
            cols = slice(b * BLOCK_LEN, (b + 1) * BLOCK_LEN)
            product = dot_nt(lags_ref[:, cols], taps_ref[:, cols])
            product = product[:count, :LANES] + (product[:count, LANES:] + product[count:, :LANES])
            by_real = product[:lags_local]
            by_imag = product[lags_local : 2 * lags_local]
            rows = pl.ds(pl.multiple_of((n * BATCH + b) * lags_local, lags_local), lags_local)
            high, low = halves(by_real + turn * pltpu.roll(by_imag, TAPS, 1))
            out_ref[0, rows, :] = high
            out_ref[1, rows, :] = low
            line_ref[...] += product[2 * lags_local : 2 * lags_local + SUBLANES]

    line_ref[...] = jnp.zeros_like(line_ref)
    build(0, taps_a, lags_a)

    def pair(m, carry):
        build(2 * m + 1, taps_b, lags_b)
        use(2 * m, taps_a, lags_a)
        build(jnp.minimum(2 * m + 2, steps - 1), taps_a, lags_a)
        use(2 * m + 1, taps_b, lags_b)
        return carry

    lax.fori_loop(0, steps // 2, pair, 0)
    tail = []
    for c in range(2):
        line = line_of(span_ref, c, EDGE + owners * part_rows - 1, 2)
        tail += [shifted(line, g) for g in range(0, TAPS, 2 * SUBLANES)]
    tail = jnp.concatenate(tail, 0)
    tail_ref[...] = dot_nt(tail, tail, HIGHEST)


def own_call(parts, lags_local, after):
    part_rows = parts[0].shape[2]
    span_rows = part_rows * sum(part.shape[0] for part in parts)
    rows = span_rows * LANES // BLOCK_LEN * lags_local
    held_rows = -(-(span_rows + 2 * EDGE) // SUBLANES) * SUBLANES
    width = BATCH * BLOCK_LEN
    taps = pltpu.VMEM((4 * TAPS, width), jnp.bfloat16)
    lags = pltpu.VMEM((4 * lags_local + 4 * SUBLANES, width), jnp.bfloat16)
    span = pltpu.VMEM((2, held_rows, LANES), jnp.float32)
    return pl.pallas_call(
        functools.partial(own_kernel, lags_local),
        in_specs=[pl.BlockSpec(memory_space=pltpu.VMEM)] * len(parts) + [pl.BlockSpec(memory_space=pl.ANY)],
        out_shape=[
            jax.ShapeDtypeStruct((2, rows, 2 * TAPS), jnp.bfloat16),
            jax.ShapeDtypeStruct((SUBLANES, 2 * TAPS), jnp.float32),
            jax.ShapeDtypeStruct((2 * TAPS, 2 * TAPS), jnp.float32),
        ],
        scratch_shapes=[span, span, taps, lags, taps, lags],
        compiler_params=params(),
        cost_estimate=pl.CostEstimate(
            flops=24 * rows * BLOCK_LEN * 2 * TAPS, bytes_accessed=4 * rows * 2 * TAPS, transcendentals=0
        ),
        name="reference_products",
    )(*parts, after)


def as_factor(a):
    return jnp.concatenate([a, -lane_sign(a.shape) * pltpu.roll(a, a.shape[0], 1)], 0)


def solver_kernel(line_ref, tail_ref, gram_ref, solver_ref):
    total = line_ref[...]
    line = total[0:1] + lane_sign((1, LANES)) * pltpu.roll(total[1:2], TAPS, 1)
    low = lax.broadcasted_iota(jnp.int32, (1, LANES), 1) < TAPS
    line_r = jnp.where(low, line, 0.0)
    line_i = jnp.where(low, pltpu.roll(line, TAPS, 1), 0.0)
    cols = lax.broadcasted_iota(jnp.int32, (TAPS, TAPS), 1)
    rows = lax.broadcasted_iota(jnp.int32, (TAPS, TAPS), 0)
    above = cols > rows

    def upper(x):
        spread = pltpu.roll(jnp.broadcast_to(x, (TAPS, LANES)), 0, 1, stride=1, stride_axis=0)
        return spread[:, :TAPS]

    up_r = upper(line_r)
    up_i = jnp.where(above, upper(line_i), 0.0)
    strict_r = jnp.where(above, up_r, 0.0)
    diag_r = jnp.where(cols == rows, up_r, 0.0)
    tails = tail_ref[...]
    gram_r = strict_r + strict_r.T + diag_r - (tails[:TAPS, :TAPS] + tails[TAPS:, TAPS:])
    gram_i = up_i - up_i.T - (tails[:TAPS, TAPS:] - tails[TAPS:, :TAPS])
    gram = jnp.concatenate([gram_r, gram_i], 1)
    gram_halves = halves(as_factor(gram))
    gram_ref[0], gram_ref[1] = gram_halves
    one = (
        lax.broadcasted_iota(jnp.int32, gram.shape, 0) == lax.broadcasted_iota(jnp.int32, gram.shape, 1)
    ).astype(jnp.float32)
    bound = jnp.max(jnp.sum(jnp.abs(gram), axis=1, keepdims=True), axis=0, keepdims=True)

    def again(state):
        count, left, _ = state
        return (count < 60) & (left > 1e-3)

    def newton(state):
        count, _, x = state
        x_halves = halves(x)
        seen = dot_split(x_halves, gram_halves)
        left = jnp.max(jnp.abs(seen - one))
        x = 2.0 * x - dot_split(halves(seen), halves(as_factor(x)))
        return count + 1, left, x

    start = (jnp.int32(0), jnp.float32(1.0), one * (1.0 / bound))
    _, _, inverse = lax.while_loop(again, newton, start)
    solver_ref[0], solver_ref[1] = halves(as_factor(inverse))


def solver_call(line, tail):
    out = jax.ShapeDtypeStruct((2,) + tail.shape, jnp.bfloat16)
    return pl.pallas_call(
        solver_kernel,
        out_shape=[out, out],
        compiler_params=params(),
        cost_estimate=pl.CostEstimate(flops=500_000_000, bytes_accessed=200_000, transcendentals=0),
        name="gram_inverse",
    )(line, tail)


def doppler_table(block_count, scale):
    phase = (np.arange(block_count)[:, None] * np.arange(DOPPLER)[None, :] % DOPPLER) * (2.0 * math.pi / DOPPLER)
    cosine, sine = np.cos(phase), np.sin(phase)
    upper = np.concatenate([cosine, -sine], 1)
    lower = np.concatenate([sine, cosine], 1)
    return (np.concatenate([upper, lower], 0) * scale).astype(np.float32)


def map_kernel(groups, got_ref, own_ref, gram_ref, solver_ref, wave_ref, out_hbm, held_ref, out_ref, out_sem):
    owners, pieces = got_ref.shape[:2]
    blocks = pieces - groups // 2
    lags_local = LANES // groups
    total = owners * blocks
    left = lax.broadcasted_iota(jnp.int32, (SUBLANES, LANES), 1) < TAPS
    sign = row_sign((SUBLANES, LANES))
    rows = [None] * groups
    for i in range(groups // 2):
        tile = got_ref[0, blocks + i]
        for owner in range(1, owners):
            tile = tile + got_ref[owner, blocks + i]
        swapped = pltpu.roll(tile, TAPS, 1)
        for part, here, there in ((i, tile, swapped), (i + groups // 2, swapped, tile)):
            other = -sign * pltpu.roll(there, SUBLANES // 2, 0)
            rows[part] = jnp.where(left, here, other)
    cross = jnp.concatenate(rows, 0)
    solver = (solver_ref[0], solver_ref[1])
    taps = dot_split(halves(cross), solver)
    rest = cross - dot_split(halves(taps), (gram_ref[0], gram_ref[1]))
    taps = taps + dot_split(halves(rest), solver)
    taps_high, taps_low = halves(taps)
    taps_both = jnp.concatenate([taps_high, taps_low], 1)
    for q in range(0, total, 2 * groups):
        own = slice(q * lags_local, (q + 2 * groups) * lags_local)
        own_high = own_ref[0, own, :]
        clutter = dot_nt(taps_both, jnp.concatenate([own_high, own_high], 1)) + dot_nt(taps_high, own_ref[1, own, :])
        for h in range(2):
            lanes = slice(h * LANES, (h + 1) * LANES)
            tiles = [clutter[r : r + SUBLANES, lanes] for r in range(0, groups * SUBLANES, SUBLANES)]
            for j, tile in enumerate(swap_groups(tiles, groups)):
                at = q + h * groups + j
                held_ref[at * SUBLANES : (at + 1) * SUBLANES, :] = got_ref[at // blocks, at % blocks] - tile
    half = SUBLANES // 2
    wave = (wave_ref[0], wave_ref[1])
    copies = []
    for g in range(half):
        parts = [held_ref[pl.ds(c * half + g, total, stride=SUBLANES), :] for c in range(2)]
        spectrum = dot_split(halves(jnp.concatenate(parts, 0).T), wave)
        for i in range(groups):
            beam = half * i + g
            for c in range(2):
                out_ref[beam, c] = spectrum[i * lags_local : (i + 1) * lags_local, c * DOPPLER : (c + 1) * DOPPLER]
            copies.append(pltpu.make_async_copy(out_ref.at[beam], out_hbm.at[beam], out_sem.at[beam]))
            copies[-1].start()
    for copy in copies:
        copy.wait()


def map_call(got, own, gram, solver, wave, groups, beams_local):
    total = got.shape[0] * (got.shape[1] - groups // 2)
    lags_local = LANES // groups
    shape = (beams_local, 2, lags_local, DOPPLER)
    return pl.pallas_call(
        functools.partial(map_kernel, groups),
        in_specs=[pl.BlockSpec(memory_space=pltpu.VMEM)] * 5,
        out_specs=pl.BlockSpec(memory_space=pltpu.HBM),
        out_shape=jax.ShapeDtypeStruct(shape, jnp.float32),
        scratch_shapes=[
            pltpu.VMEM((total * SUBLANES, LANES), jnp.float32),
            pltpu.VMEM(shape, jnp.float32),
            pltpu.SemaphoreType.DMA((beams_local,)),
        ],
        compiler_params=params(),
        cost_estimate=pl.CostEstimate(
            flops=12 * math.prod(shape) * total, bytes_accessed=4 * math.prod(shape), transcendentals=0
        ),
        name="range_doppler",
    )(got, own, gram, solver, wave)


def swap(x, axis, by):
    pairs = [(i, i ^ by) for i in range(lax.axis_size(axis))]
    return lax.ppermute(x, axis, pairs)


def tiled_device(ref_signal, surveillance, steering):
    chan_count, tm_count = lax.axis_size("chan"), lax.axis_size("tm")
    channels, length = surveillance.shape[1:]
    beams_local = steering.shape[1] // chan_count
    lags_local = LAGS // tm_count
    groups = LANES // lags_local
    samples = length * tm_count

    survey = surveillance.reshape(2 * channels, length)
    near = swap(ref_signal, "tm", 1)
    kept_first, sent_first, later, weights = beam_first_call(steering, survey, chan_count, beams_local)
    kept_later, sent_later, tiles, edge = beam_later_call(later, weights, ref_signal)
    edge = lax.ppermute(edge, "tm", [(i, i + 1) for i in range(tm_count - 1)])
    shape = (chan_count // 2, 2 * beams_local, length // SPANS)
    spans = []
    for kept, moved in ((kept_first, sent_first), (kept_later, sent_later)):
        parts = [kept.reshape(shape), swap(moved, "chan", 1).reshape(shape)]
        by = 2
        while by < chan_count:
            sent = parts[0][1::2]
            for part in parts[1:]:
                sent = sent + part[1::2]
            parts = [part[::2] for part in parts] + [swap(sent, "chan", by)]
            by *= 2
        spans.append([part[0] for part in parts])
    pair = pair_call(tiles, near, sent)
    ref_parts = [pair] + [swap(pair, "tm", by) for by in range(2, tm_count, 2)]
    table = table_call(edge, tiles)
    blocks = length // BLOCK_LEN
    before = lag_call(spans[0], table, groups, tm_count, 0, blocks)
    pieces, taps_sum = lag_call(spans[1], table, groups, tm_count, blocks // SPANS, blocks, before)
    got = lax.all_to_all(pieces, "tm", 0, 0, tiled=True)
    own, line, tail = own_call(ref_parts, lags_local, taps_sum)
    gram, solver = solver_call(line, tail)
    wave = doppler_table(samples // BLOCK_LEN, 0.125 / math.sqrt(samples))
    high = wave.astype(jnp.bfloat16)
    wave = np.stack([high, (wave - high.astype(np.float32)).astype(jnp.bfloat16)])
    return map_call(got, own, gram, solver, jnp.asarray(wave), groups, beams_local)


def lag_table(ref_ext, offset, lags):
    window = lax.dynamic_slice_in_dim(ref_ext, offset, BLOCK_LEN + LAGS, 1)
    span = BLOCK_LEN + LAGS
    tiled = jnp.tile(jnp.pad(window, ((0, 0), (0, 1))), (1, lags))[:, : lags * span]
    return tiled.reshape(2, lags, span)[:, :, LAGS:]


def times_conj(a, b):
    real = jnp.einsum("...t,lt->...l", a[..., 0, :], b[0], precision=HIGHEST) + jnp.einsum(
        "...t,lt->...l", a[..., 1, :], b[1], precision=HIGHEST
    )
    imag = jnp.einsum("...t,lt->...l", a[..., 1, :], b[0], precision=HIGHEST) - jnp.einsum(
        "...t,lt->...l", a[..., 0, :], b[1], precision=HIGHEST
    )
    return jnp.stack([real, imag], -2)


def plain_device(ref_signal, surveillance, steering):
    chan_count, tm_count = lax.axis_size("chan"), lax.axis_size("tm")
    length = surveillance.shape[2]
    beams = steering.shape[1]
    lags_local = LAGS // tm_count
    samples = length * tm_count
    local_blocks = length // BLOCK_LEN
    here = lax.axis_index("tm")

    w_real, w_imag = steering
    real = jnp.dot(w_real, surveillance[0], precision=HIGHEST) - jnp.dot(w_imag, surveillance[1], precision=HIGHEST)
    imag = jnp.dot(w_imag, surveillance[0], precision=HIGHEST) + jnp.dot(w_real, surveillance[1], precision=HIGHEST)
    beam = lax.psum_scatter(jnp.stack([real, imag], 1), "chan", scatter_dimension=0, tiled=True)
    ref_all = lax.all_gather(ref_signal, "tm", axis=1, tiled=True)
    ref_ext = jnp.pad(ref_all, ((0, 0), (LAGS, 0)))

    def beam_step(carry, q):
        offset = q * BLOCK_LEN
        table = lag_table(ref_ext, here * length + offset, LAGS)
        segment = lax.dynamic_slice_in_dim(beam, offset, BLOCK_LEN, 2)
        return carry, times_conj(segment, table)

    _, products = lax.scan(beam_step, None, jnp.arange(local_blocks, dtype=jnp.int32))
    cross = lax.psum(products[..., :TAPS].sum(0), "tm")
    got = lax.all_to_all(products, "tm", 3, 0, tiled=True)

    def own_step(gram, q):
        offset = q * BLOCK_LEN
        table = lag_table(ref_ext, offset, LAGS)
        taps = table[:, :TAPS].transpose(1, 0, 2)
        mine = lax.dynamic_slice_in_dim(table, here * lags_local, lags_local, 1)
        return gram + times_conj(taps, table[:, :TAPS]), times_conj(taps, mine)

    start = jnp.zeros((TAPS, 2, TAPS), jnp.float32)
    gram, own = lax.scan(own_step, start, jnp.arange(samples // BLOCK_LEN, dtype=jnp.int32))
    g_real, g_imag = gram[:, 0].T, gram[:, 1].T
    system = jnp.concatenate([jnp.concatenate([g_real, -g_imag], 1), jnp.concatenate([g_imag, g_real], 1)], 0)
    right = jnp.concatenate([cross[:, 0].T, cross[:, 1].T], 0)
    solved = jax.scipy.linalg.cho_solve((jnp.linalg.cholesky(system), True), right)
    b_real, b_imag = solved[:TAPS].T, solved[TAPS:].T
    mixing = jnp.concatenate([jnp.stack([b_real, b_imag], 1), jnp.stack([-b_imag, b_real], 1)], 2)
    stacked = jnp.concatenate([own[:, :, 0], own[:, :, 1]], 1)
    lagged = got - jnp.einsum("mck,qkl->qmcl", mixing, stacked, precision=HIGHEST)
    wave = jnp.asarray(doppler_table(samples // BLOCK_LEN, 0.125 / math.sqrt(samples)))
    wave = wave.reshape(2, samples // BLOCK_LEN, 2, DOPPLER)
    return jnp.einsum("qmcl,cqdk->mdlk", lagged, wave, precision=HIGHEST)


def on_device(ref_signal, surveillance, steering):
    chan_count, tm_count = lax.axis_size("chan"), lax.axis_size("tm")
    beams_local = steering.shape[1] // chan_count
    lags_local = LAGS // tm_count
    fills = (
        LANES % lags_local == 0
        and lags_local % (2 * SUBLANES) == 0
        and beams_local * lags_local == LANES * SUBLANES // 2
        and chan_count > 1
        and chan_count & (chan_count - 1) == 0
        and tm_count > 1
        and tm_count & (tm_count - 1) == 0
        and 2 * surveillance.shape[1] % LANES == 0
        and surveillance.shape[2] % (2 * BATCH * BLOCK_LEN) == 0
    )
    device = tiled_device if fills else plain_device
    return device(ref_signal, surveillance, steering)


def solution(mesh):
    placed = (P(None, "tm"), P(None, "chan", "tm"), P(None, None, "chan"))
    return jax.shard_map(
        on_device,
        mesh=mesh,
        in_specs=placed,
        out_specs=P("chan", None, "tm", None),
        check_vma=False,
    )
```

```python
import functools
import math

import jax
import jax.numpy as jnp
import numpy as np
from jax import lax
from jax.experimental import pallas as pl
from jax.experimental.pallas import tpu as pltpu
from jax.sharding import PartitionSpec as P

LAGS = 256
DOPPLER = 256
TAPS = 64
BLOCK_LEN = 256
LANES = 128
SUBLANES = 8
EDGE = 2

HIGHEST = lax.Precision.HIGHEST
VMEM_BYTES = 48 * 1024 * 1024


def params():
    return pltpu.CompilerParams(vmem_limit_bytes=VMEM_BYTES)


def cost(us):
    return pl.CostEstimate(flops=int(us * 1.15e9), bytes_accessed=0, transcendentals=0)


def halves(x):
    high = x.astype(jnp.bfloat16)
    return high, (x - high.astype(jnp.float32)).astype(jnp.bfloat16)


def dot_nt(a, b, precision=None):
    return lax.dot_general(
        a, b, (((1,), (1,)), ((), ())), precision=precision, preferred_element_type=jnp.float32
    )


def dot_split(a, b):
    (a_high, a_low), (b_high, b_low) = a, b
    left = jnp.concatenate([a_high, a_low], 1)
    right = jnp.concatenate([b_high, b_high], 0)
    return jnp.dot(left, right, preferred_element_type=jnp.float32) + jnp.dot(
        a_high, b_low, preferred_element_type=jnp.float32
    )


def row_sign(shape):
    rows = lax.broadcasted_iota(jnp.int32, shape, 0)
    return jnp.where(rows % SUBLANES < SUBLANES // 2, 1.0, -1.0).astype(jnp.float32)


def lane_sign(shape):
    lanes = lax.broadcasted_iota(jnp.int32, shape, 1)
    return jnp.where(lanes % LANES < LANES // 2, 1.0, -1.0).astype(jnp.float32)


def swap_groups(rows, groups):
    width = LANES // groups
    lane_group = lax.broadcasted_iota(jnp.int32, rows[0].shape, 1) // width
    outs = []
    for j in range(groups):
        out = rows[j]
        for i in range(groups):
            if i != j:
                moved = pltpu.roll(rows[i], (width * (i - j)) % LANES, 1)
                out = jnp.where(lane_group == i, moved, out)
        outs.append(out)
    return outs


SPANS = 2
CHUNKS = 2


def beam_first_kernel(
    chan_count, beams_local, w_hbm, s_hbm, kept_ref, sent_ref, later_ref, weights_ref, w_ref, s_ref, w_sem, s_sem, later_sem
):
    me = lax.axis_index("chan")
    span = s_ref.shape[1]
    width = span // CHUNKS
    w_copy = pltpu.make_async_copy(w_hbm, w_ref, w_sem)
    w_copy.start()
    s_copies = []
    for n in range(CHUNKS):
        cols = pl.ds(n * width, width)
        s_copies.append(pltpu.make_async_copy(s_hbm.at[:, cols], s_ref.at[:, cols], s_sem.at[n]))
        s_copies[n].start()
    later_copy = pltpu.make_async_copy(s_hbm.at[:, pl.ds(span, later_ref.shape[1])], later_ref, later_sem)
    later_copy.start()
    half = SUBLANES // 2
    sub = lax.broadcasted_iota(jnp.int32, (SUBLANES, w_hbm.shape[2]), 0)
    top = sub < half
    w_copy.wait()
    rows = []
    for parity in range(2):
        for e in range(parity, chan_count, 2):
            base = (me ^ e) * beams_local
            for tile in range(beams_local // SUBLANES):
                start = pl.multiple_of(base + tile * SUBLANES, SUBLANES)
                wr = w_ref[0, pl.ds(start, SUBLANES), :]
                wi = w_ref[1, pl.ds(start, SUBLANES), :]
                wr_s = pltpu.roll(wr, half, 0)
                wi_s = pltpu.roll(wi, half, 0)
                first = [jnp.where(top, wr, wi_s), jnp.where(top, -wi, wr_s)]
                second = [jnp.where(top, wr_s, wi), jnp.where(top, -wi_s, wr)]
                rows.append(jnp.concatenate(first, 1))
                rows.append(jnp.concatenate(second, 1))
    weights = halves(jnp.concatenate(rows, 0))
    weights_ref[0], weights_ref[1] = weights
    mid = weights[0].shape[0] // 2
    for n in range(CHUNKS):
        cols = slice(n * width, (n + 1) * width)
        s_copies[n].wait()
        product = dot_split(weights, halves(s_ref[:, cols]))
        kept_ref[:, cols] = product[:mid]
        sent_ref[:, cols] = product[mid:]
    later_copy.wait()


def beam_first_call(steering, survey, chan_count, beams_local):
    depth, length = survey.shape
    span = length // SPANS
    rows = chan_count * beams_local
    out = jax.ShapeDtypeStruct((rows, span), jnp.float32)
    hbm = pl.BlockSpec(memory_space=pltpu.HBM)
    return pl.pallas_call(
        functools.partial(beam_first_kernel, chan_count, beams_local),
        in_specs=[hbm, hbm],
        out_specs=[pl.BlockSpec(memory_space=pltpu.VMEM)] * 4,
        out_shape=[
            out,
            out,
            jax.ShapeDtypeStruct((depth, length - span), jnp.float32),
            jax.ShapeDtypeStruct((2, 2 * rows, depth), jnp.bfloat16),
        ],
        scratch_shapes=[
            pltpu.VMEM(steering.shape, jnp.float32),
            pltpu.VMEM((depth, span), jnp.float32),
            pltpu.SemaphoreType.DMA,
            pltpu.SemaphoreType.DMA((CHUNKS,)),
            pltpu.SemaphoreType.DMA,
        ],
        compiler_params=params(),
        cost_estimate=cost(1.5),
        name="beams_first",
    )(*(pltpu.with_memory_space_constraint(x, pltpu.HBM) for x in (steering, survey)))


def beam_later_kernel(later_ref, weights_ref, ref_hbm, kept_ref, sent_ref, tiles_ref, edge_ref, ref_ref, ref_sem):
    ref_copy = pltpu.make_async_copy(ref_hbm, ref_ref, ref_sem)
    ref_copy.start()
    product = dot_split((weights_ref[0], weights_ref[1]), halves(later_ref[...]))
    mid = product.shape[0] // 2
    kept_ref[...] = product[:mid]
    sent_ref[...] = product[mid:]
    ref_copy.wait()
    edge_ref[...] = jnp.zeros_like(edge_ref)
    count = tiles_ref.shape[1]
    for c in range(2):
        for n in range(count):
            row = ref_ref[c : c + 1, n * LANES : (n + 1) * LANES]
            tiles_ref[c, n : n + 1, :] = row
            if n >= count - EDGE:
                at = SUBLANES * c + n + EDGE - count
                edge_ref[at : at + 1, :] = row


def beam_later_call(later, weights, ref):
    depth, span = later.shape
    rows = weights.shape[1] // 2
    vmem = pl.BlockSpec(memory_space=pltpu.VMEM)
    out = jax.ShapeDtypeStruct((rows, span), jnp.float32)
    return pl.pallas_call(
        beam_later_kernel,
        in_specs=[vmem, vmem, pl.BlockSpec(memory_space=pltpu.HBM)],
        out_specs=[vmem] * 4,
        out_shape=[
            out,
            out,
            jax.ShapeDtypeStruct((2, ref.shape[1] // LANES, LANES), jnp.float32),
            jax.ShapeDtypeStruct((2 * SUBLANES, LANES), jnp.float32),
        ],
        scratch_shapes=[pltpu.VMEM(ref.shape, jnp.float32), pltpu.SemaphoreType.DMA],
        compiler_params=params(),
        cost_estimate=cost(0.9),
        name="beams_later",
    )(later, weights, pltpu.with_memory_space_constraint(ref, pltpu.HBM))


def sum_kernel(count, *refs):
    kept_ref, sent_ref = refs[-2:]
    for n in range(kept_ref.shape[0]):
        for offset, out_ref in ((0, kept_ref), (1, sent_ref)):
            total = refs[0][2 * n + offset]
            for ref in refs[1:count]:
                total = total + ref[2 * n + offset]
            out_ref[n] = total


def sum_call(parts, after):
    shape = (parts[0].shape[0] // 2,) + parts[0].shape[1:]
    out = jax.ShapeDtypeStruct(shape, jnp.float32)
    vmem = pl.BlockSpec(memory_space=pltpu.VMEM)
    return pl.pallas_call(
        functools.partial(sum_kernel, len(parts)),
        in_specs=[vmem] * len(parts) + [pl.BlockSpec(memory_space=pl.ANY)] * len(after),
        out_specs=[vmem, vmem],
        out_shape=[out, out],
        compiler_params=params(),
        cost_estimate=cost(0.1),
        name="halves_summed",
    )(*parts, *after)


def pair_kernel(tiles_ref, near_ref, _, out_ref):
    out_ref[0] = tiles_ref[...]
    out_ref[1] = near_ref[...]


def pair_call(tiles, near, after):
    vmem = pl.BlockSpec(memory_space=pltpu.VMEM)
    return pl.pallas_call(
        pair_kernel,
        in_specs=[vmem, vmem, pl.BlockSpec(memory_space=pl.ANY)],
        out_shape=jax.ShapeDtypeStruct((2,) + tiles.shape, jnp.float32),
        compiler_params=params(),
        cost_estimate=cost(0.1),
        name="reference_pair",
    )(tiles, near, after)


def table_kernel(edge_ref, tiles_ref, out_ref):
    rows = tiles_ref.shape[1]
    for c in range(2):
        line = [edge_ref[SUBLANES * c + n : SUBLANES * c + n + 1, :] for n in range(EDGE)]
        line = jnp.concatenate(line + [tiles_ref[c, n : n + 1, :] for n in range(rows)], 1)
        for g in range(0, LANES, 2 * SUBLANES):
            tiled = jnp.broadcast_to(line, (2 * SUBLANES, line.shape[1]))
            high, low = halves(pltpu.roll(tiled, g, 1, stride=1, stride_axis=0)[:, LANES:])
            out_ref[0, c, g : g + 2 * SUBLANES] = high
            out_ref[1, c, g : g + 2 * SUBLANES] = low


def table_call(edge, tiles):
    shape = (2, 2, LANES, LANES * (tiles.shape[1] + 1))
    return pl.pallas_call(
        table_kernel,
        out_shape=jax.ShapeDtypeStruct(shape, jnp.bfloat16),
        compiler_params=params(),
        cost_estimate=cost(0.7),
        name="shifted_reference",
    )(edge, tiles)


def lag_kernel(groups, spans, *refs):
    *y_refs, table_ref, _, out_hbm, out_ref, out_sem = refs
    copies = []

    def send(start, count):
        part = (slice(None), pl.ds(start, count))
        copies.append(pltpu.make_async_copy(out_ref.at[part], out_hbm.at[part], out_sem.at[len(copies)]))
        copies[-1].start()

    count = len(y_refs) // spans
    parts = []
    for n in range(spans):
        part = y_refs[n * count][...]
        for y_ref in y_refs[n * count + 1 : (n + 1) * count]:
            part = part + y_ref[...]
        parts.append(part)
    y = jnp.concatenate(parts, 1)
    rows, length = y.shape
    blocks = length // BLOCK_LEN
    turned = jnp.concatenate(
        [pltpu.roll(y[r : r + SUBLANES], SUBLANES // 2, 0) for r in range(0, rows, SUBLANES)], 0
    )
    turned = turned * row_sign(turned.shape)
    y_high, y_low = halves(y)
    t_high, t_low = halves(turned)
    both = jnp.concatenate([y_high, y_low], 0)
    turned_both = jnp.concatenate([t_high, t_low], 0)
    taps_sum = None
    for q in range(blocks):
        near = slice(q * BLOCK_LEN + LANES, q * BLOCK_LEN + LANES + BLOCK_LEN)
        far = slice(q * BLOCK_LEN, (q + 1) * BLOCK_LEN)
        cols = slice(q * BLOCK_LEN, (q + 1) * BLOCK_LEN)
        tables = []
        for h in range(2):
            tables.append(
                jnp.concatenate(
                    [
                        jnp.concatenate([table_ref[h, 0, :, near], table_ref[h, 1, :, near]], 1),
                        jnp.concatenate([table_ref[h, 0, :, far], table_ref[h, 1, :, far]], 1),
                    ],
                    0,
                )
            )
        lhs = jnp.concatenate([both[:, cols], turned_both[:, cols]], 1)
        by_high = dot_nt(lhs, tables[0])
        by_low = dot_nt(lhs[:rows], tables[1])
        product = by_high[:rows] + (by_high[rows:] + by_low)
        taps = product[:, :LANES]
        taps_sum = taps if taps_sum is None else taps_sum + taps
        for h in range(LAGS // LANES):
            lanes = slice(h * LANES, (h + 1) * LANES)
            tiles = [product[r : r + SUBLANES, lanes] for r in range(0, rows, SUBLANES)]
            for j, tile in enumerate(swap_groups(tiles, groups)):
                out_ref[h * groups + j, q] = tile
        if q % 2:
            send(q - 1, 2)
    left = lax.broadcasted_iota(jnp.int32, (SUBLANES, LANES), 1) < TAPS
    for i in range(groups // 2):
        a = taps_sum[i * SUBLANES : (i + 1) * SUBLANES]
        other = i + groups // 2
        b = taps_sum[other * SUBLANES : (other + 1) * SUBLANES]
        tile = jnp.where(left, a, pltpu.roll(b, LANES - TAPS, 1))
        for owner in range(out_ref.shape[0]):
            out_ref[owner, blocks + i] = tile
    send(blocks, groups // 2)
    for copy in copies:
        copy.wait()


def lag_call(ys, spans, table, after, groups, owners):
    blocks = spans * ys[0].shape[1] // BLOCK_LEN
    shape = (owners, blocks + groups // 2, SUBLANES, LANES)
    vmem = pl.BlockSpec(memory_space=pltpu.VMEM)
    return pl.pallas_call(
        functools.partial(lag_kernel, groups, spans),
        in_specs=[vmem] * (len(ys) + 1) + [pl.BlockSpec(memory_space=pl.ANY)],
        out_specs=pl.BlockSpec(memory_space=pltpu.HBM),
        out_shape=jax.ShapeDtypeStruct(shape, jnp.float32),
        scratch_shapes=[pltpu.VMEM(shape, jnp.float32), pltpu.SemaphoreType.DMA((blocks // 2 + 1,))],
        compiler_params=params(),
        cost_estimate=cost(2.1),
        name="lag_products",
    )(*ys, table, after)


BATCH = 4


def own_kernel(lags_local, *refs):
    *part_refs, _, out_ref, line_ref, tail_ref, span_ref, late_ref, taps_a, lags_a, taps_b, lags_b = refs
    me = lax.axis_index("tm")
    part_rows = part_refs[0].shape[2]
    owners = sum(part_ref.shape[0] for part_ref in part_refs)
    samples = owners * part_rows * LANES
    steps = samples // BLOCK_LEN // BATCH
    total_rows = span_ref.shape[1]
    block_rows = BLOCK_LEN // LANES

    span_ref[...] = jnp.zeros_like(span_ref)
    e = 0
    for part_ref in part_refs:
        for i in range(part_ref.shape[0]):
            span_ref[:, pl.ds(EDGE + (me ^ e) * part_rows, part_rows), :] = part_ref[i]
            e += 1
    late_rows = (me * lags_local) // LANES
    late_lanes = lax.rem(me * lags_local, LANES)
    turned = [pltpu.roll(span_ref[c], late_lanes, 1) for c in range(2)]
    before = [pltpu.roll(x, 1, 0) for x in turned]
    lanes = lax.broadcasted_iota(jnp.int32, (total_rows, LANES), 1)
    for c in range(2):
        late_ref[c] = pltpu.roll(jnp.where(lanes < late_lanes, before[c], turned[c]), late_rows, 0)

    def line_of(ref, c, first, count):
        return jnp.concatenate([ref[c, pl.ds(first + n, 1), :] for n in range(count)], 1)

    def shifted(line, by):
        tiled = jnp.broadcast_to(line, (2 * SUBLANES, line.shape[1]))
        return pltpu.roll(tiled, by, 1, stride=1, stride_axis=0)[:, LANES:]

    def keep(ref, row, value):
        high, low = halves(value)
        half = ref.shape[0] // 2
        ref[row : row + 2 * SUBLANES, :] = high
        ref[half + row : half + row + 2 * SUBLANES, :] = low

    def build(n, taps_ref, lags_ref):
        first = EDGE - 1 + n * BATCH * block_rows
        count = BATCH * block_rows + 1
        lines = [line_of(span_ref, c, first, count) for c in range(2)]
        for c in range(2):
            for g in range(0, TAPS, 2 * SUBLANES):
                keep(taps_ref, c * TAPS + g, shifted(lines[c], g))
            late = line_of(late_ref, c, first, count)
            for g in range(0, lags_local, 2 * SUBLANES):
                keep(lags_ref, c * lags_local + g, shifted(late, g))
        pad = jnp.zeros((2 * SUBLANES - 2, BATCH * BLOCK_LEN), jnp.float32)
        keep(lags_ref, 2 * lags_local, jnp.concatenate([line[:, LANES:] for line in lines] + [pad], 0))

    turn = lane_sign((lags_local, LANES))

    def use(n, taps_ref, lags_ref):
        count = lags_ref.shape[0] // 2
        for b in range(BATCH):
            cols = slice(b * BLOCK_LEN, (b + 1) * BLOCK_LEN)
            product = dot_nt(lags_ref[:, cols], taps_ref[:, cols])
            product = product[:count, :LANES] + (product[:count, LANES:] + product[count:, :LANES])
            by_real = product[:lags_local]
            by_imag = product[lags_local : 2 * lags_local]
            rows = pl.ds(pl.multiple_of((n * BATCH + b) * lags_local, lags_local), lags_local)
            high, low = halves(by_real + turn * pltpu.roll(by_imag, TAPS, 1))
            out_ref[0, rows, :] = high
            out_ref[1, rows, :] = low
            line_ref[...] += product[2 * lags_local : 2 * lags_local + SUBLANES]

    line_ref[...] = jnp.zeros_like(line_ref)
    build(0, taps_a, lags_a)

    def pair(m, carry):
        build(2 * m + 1, taps_b, lags_b)
        use(2 * m, taps_a, lags_a)
        build(jnp.minimum(2 * m + 2, steps - 1), taps_a, lags_a)
        use(2 * m + 1, taps_b, lags_b)
        return carry

    lax.fori_loop(0, steps // 2, pair, 0)
    tail = []
    for c in range(2):
        line = line_of(span_ref, c, EDGE + owners * part_rows - 1, 2)
        tail += [shifted(line, g) for g in range(0, TAPS, 2 * SUBLANES)]
    tail = jnp.concatenate(tail, 0)
    tail_ref[...] = dot_nt(tail, tail, HIGHEST)


def own_call(parts, lags_local, after):
    part_rows = parts[0].shape[2]
    span_rows = part_rows * sum(part.shape[0] for part in parts)
    rows = span_rows * LANES // BLOCK_LEN * lags_local
    held_rows = -(-(span_rows + 2 * EDGE) // SUBLANES) * SUBLANES
    width = BATCH * BLOCK_LEN
    taps = pltpu.VMEM((4 * TAPS, width), jnp.bfloat16)
    lags = pltpu.VMEM((4 * lags_local + 4 * SUBLANES, width), jnp.bfloat16)
    span = pltpu.VMEM((2, held_rows, LANES), jnp.float32)
    return pl.pallas_call(
        functools.partial(own_kernel, lags_local),
        in_specs=[pl.BlockSpec(memory_space=pltpu.VMEM)] * len(parts) + [pl.BlockSpec(memory_space=pl.ANY)],
        out_shape=[
            jax.ShapeDtypeStruct((2, rows, 2 * TAPS), jnp.bfloat16),
            jax.ShapeDtypeStruct((SUBLANES, 2 * TAPS), jnp.float32),
            jax.ShapeDtypeStruct((2 * TAPS, 2 * TAPS), jnp.float32),
        ],
        scratch_shapes=[span, span, taps, lags, taps, lags],
        compiler_params=params(),
        cost_estimate=cost(6.2),
        name="reference_products",
    )(*parts, after)


def as_factor(a):
    return jnp.concatenate([a, -lane_sign(a.shape) * pltpu.roll(a, a.shape[0], 1)], 0)


def solver_kernel(line_ref, tail_ref, gram_ref, solver_ref):
    total = line_ref[...]
    line = total[0:1] + lane_sign((1, LANES)) * pltpu.roll(total[1:2], TAPS, 1)
    low = lax.broadcasted_iota(jnp.int32, (1, LANES), 1) < TAPS
    line_r = jnp.where(low, line, 0.0)
    line_i = jnp.where(low, pltpu.roll(line, TAPS, 1), 0.0)
    cols = lax.broadcasted_iota(jnp.int32, (TAPS, TAPS), 1)
    rows = lax.broadcasted_iota(jnp.int32, (TAPS, TAPS), 0)
    above = cols > rows

    def upper(x):
        spread = pltpu.roll(jnp.broadcast_to(x, (TAPS, LANES)), 0, 1, stride=1, stride_axis=0)
        return spread[:, :TAPS]

    up_r = upper(line_r)
    up_i = jnp.where(above, upper(line_i), 0.0)
    strict_r = jnp.where(above, up_r, 0.0)
    diag_r = jnp.where(cols == rows, up_r, 0.0)
    tails = tail_ref[...]
    gram_r = strict_r + strict_r.T + diag_r - (tails[:TAPS, :TAPS] + tails[TAPS:, TAPS:])
    gram_i = up_i - up_i.T - (tails[:TAPS, TAPS:] - tails[TAPS:, :TAPS])
    gram = jnp.concatenate([gram_r, gram_i], 1)
    gram_halves = halves(as_factor(gram))
    gram_ref[0], gram_ref[1] = gram_halves
    one = (
        lax.broadcasted_iota(jnp.int32, gram.shape, 0) == lax.broadcasted_iota(jnp.int32, gram.shape, 1)
    ).astype(jnp.float32)
    bound = jnp.max(jnp.sum(jnp.abs(gram), axis=1, keepdims=True), axis=0, keepdims=True)

    def again(state):
        count, left, _ = state
        return (count < 60) & (left > 1e-3)

    def newton(state):
        count, _, x = state
        x_halves = halves(x)
        seen = dot_split(x_halves, gram_halves)
        left = jnp.max(jnp.abs(seen - one))
        x = 2.0 * x - dot_split(halves(seen), halves(as_factor(x)))
        return count + 1, left, x

    start = (jnp.int32(0), jnp.float32(1.0), one * (1.0 / bound))
    _, _, inverse = lax.while_loop(again, newton, start)
    solver_ref[0], solver_ref[1] = halves(as_factor(inverse))


def solver_call(line, tail):
    out = jax.ShapeDtypeStruct((2,) + tail.shape, jnp.bfloat16)
    return pl.pallas_call(
        solver_kernel,
        out_shape=[out, out],
        compiler_params=params(),
        cost_estimate=cost(2.0),
        name="gram_inverse",
    )(line, tail)


def doppler_table(block_count, scale):
    phase = (np.arange(block_count)[:, None] * np.arange(DOPPLER)[None, :] % DOPPLER) * (2.0 * math.pi / DOPPLER)
    cosine, sine = np.cos(phase), np.sin(phase)
    upper = np.concatenate([cosine, -sine], 1)
    lower = np.concatenate([sine, cosine], 1)
    return (np.concatenate([upper, lower], 0) * scale).astype(np.float32)


def map_kernel(groups, got_ref, own_ref, gram_ref, solver_ref, wave_ref, out_hbm, held_ref, out_ref, out_sem):
    owners, pieces = got_ref.shape[:2]
    blocks = pieces - groups // 2
    lags_local = LANES // groups
    total = owners * blocks
    left = lax.broadcasted_iota(jnp.int32, (SUBLANES, LANES), 1) < TAPS
    sign = row_sign((SUBLANES, LANES))
    rows = [None] * groups
    for i in range(groups // 2):
        tile = got_ref[0, blocks + i]
        for owner in range(1, owners):
            tile = tile + got_ref[owner, blocks + i]
        swapped = pltpu.roll(tile, TAPS, 1)
        for part, here, there in ((i, tile, swapped), (i + groups // 2, swapped, tile)):
            other = -sign * pltpu.roll(there, SUBLANES // 2, 0)
            rows[part] = jnp.where(left, here, other)
    cross = jnp.concatenate(rows, 0)
    solver = (solver_ref[0], solver_ref[1])
    taps = dot_split(halves(cross), solver)
    rest = cross - dot_split(halves(taps), (gram_ref[0], gram_ref[1]))
    taps = taps + dot_split(halves(rest), solver)
    taps_high, taps_low = halves(taps)
    taps_both = jnp.concatenate([taps_high, taps_low], 1)
    for q in range(0, total, 2 * groups):
        own = slice(q * lags_local, (q + 2 * groups) * lags_local)
        own_high = own_ref[0, own, :]
        clutter = dot_nt(taps_both, jnp.concatenate([own_high, own_high], 1)) + dot_nt(taps_high, own_ref[1, own, :])
        for h in range(2):
            lanes = slice(h * LANES, (h + 1) * LANES)
            tiles = [clutter[r : r + SUBLANES, lanes] for r in range(0, groups * SUBLANES, SUBLANES)]
            for j, tile in enumerate(swap_groups(tiles, groups)):
                at = q + h * groups + j
                held_ref[at * SUBLANES : (at + 1) * SUBLANES, :] = got_ref[at // blocks, at % blocks] - tile
    half = SUBLANES // 2
    wave = (wave_ref[0], wave_ref[1])
    copies = []
    for g in range(half):
        parts = [held_ref[pl.ds(c * half + g, total, stride=SUBLANES), :] for c in range(2)]
        spectrum = dot_split(halves(jnp.concatenate(parts, 0).T), wave)
        for i in range(groups):
            beam = half * i + g
            for c in range(2):
                out_ref[beam, c] = spectrum[i * lags_local : (i + 1) * lags_local, c * DOPPLER : (c + 1) * DOPPLER]
            copies.append(pltpu.make_async_copy(out_ref.at[beam], out_hbm.at[beam], out_sem.at[beam]))
            copies[-1].start()
    for copy in copies:
        copy.wait()


def map_call(got, own, gram, solver, wave, groups, beams_local):
    total = got.shape[0] * (got.shape[1] - groups // 2)
    lags_local = LANES // groups
    shape = (beams_local, 2, lags_local, DOPPLER)
    return pl.pallas_call(
        functools.partial(map_kernel, groups),
        in_specs=[pl.BlockSpec(memory_space=pltpu.VMEM)] * 5,
        out_specs=pl.BlockSpec(memory_space=pltpu.HBM),
        out_shape=jax.ShapeDtypeStruct(shape, jnp.float32),
        scratch_shapes=[
            pltpu.VMEM((total * SUBLANES, LANES), jnp.float32),
            pltpu.VMEM(shape, jnp.float32),
            pltpu.SemaphoreType.DMA((beams_local,)),
        ],
        compiler_params=params(),
        cost_estimate=cost(2.5),
        name="range_doppler",
    )(got, own, gram, solver, wave)


def swap(x, axis, by):
    pairs = [(i, i ^ by) for i in range(lax.axis_size(axis))]
    return lax.ppermute(x, axis, pairs)


def tiled_device(ref_signal, surveillance, steering):
    chan_count, tm_count = lax.axis_size("chan"), lax.axis_size("tm")
    channels, length = surveillance.shape[1:]
    beams_local = steering.shape[1] // chan_count
    lags_local = LAGS // tm_count
    groups = LANES // lags_local
    samples = length * tm_count

    survey = surveillance.reshape(2 * channels, length)
    kept_first, sent_first, later, weights = beam_first_call(steering, survey, chan_count, beams_local)
    kept_later, sent_later, tiles, edge = beam_later_call(later, weights, ref_signal)
    near = swap(tiles, "tm", 1)
    edge = lax.ppermute(edge, "tm", [(i, i + 1) for i in range(tm_count - 1)])
    shape = (chan_count // 2, 2 * beams_local, length // SPANS)
    ys = []
    after = []
    for kept, moved in ((kept_first, sent_first), (kept_later, sent_later)):
        kept, sent = kept.reshape(shape), swap(moved, "chan", 1).reshape(shape)
        by = 2
        while by < chan_count:
            kept, moved = sum_call([kept, sent], after)
            sent = swap(moved, "chan", by)
            by *= 2
        after = [near, edge]
        ys += [kept[0], sent[0]]
    pair = pair_call(tiles, near, moved)
    ref_parts = [pair] + [swap(pair, "tm", by) for by in range(2, tm_count, 2)]
    table = table_call(edge, tiles)
    pieces = lag_call(ys, SPANS, table, pair, groups, tm_count)
    got = lax.all_to_all(pieces, "tm", 0, 0, tiled=True)
    own, line, tail = own_call(ref_parts, lags_local, pieces)
    gram, solver = solver_call(line, tail)
    wave = doppler_table(samples // BLOCK_LEN, 0.125 / math.sqrt(samples))
    high = wave.astype(jnp.bfloat16)
    wave = np.stack([high, (wave - high.astype(np.float32)).astype(jnp.bfloat16)])
    return map_call(got, own, gram, solver, jnp.asarray(wave), groups, beams_local)


def lag_table(ref_ext, offset, lags):
    window = lax.dynamic_slice_in_dim(ref_ext, offset, BLOCK_LEN + LAGS, 1)
    span = BLOCK_LEN + LAGS
    tiled = jnp.tile(jnp.pad(window, ((0, 0), (0, 1))), (1, lags))[:, : lags * span]
    return tiled.reshape(2, lags, span)[:, :, LAGS:]


def times_conj(a, b):
    real = jnp.einsum("...t,lt->...l", a[..., 0, :], b[0], precision=HIGHEST) + jnp.einsum(
        "...t,lt->...l", a[..., 1, :], b[1], precision=HIGHEST
    )
    imag = jnp.einsum("...t,lt->...l", a[..., 1, :], b[0], precision=HIGHEST) - jnp.einsum(
        "...t,lt->...l", a[..., 0, :], b[1], precision=HIGHEST
    )
    return jnp.stack([real, imag], -2)


def plain_device(ref_signal, surveillance, steering):
    chan_count, tm_count = lax.axis_size("chan"), lax.axis_size("tm")
    length = surveillance.shape[2]
    beams = steering.shape[1]
    lags_local = LAGS // tm_count
    samples = length * tm_count
    local_blocks = length // BLOCK_LEN
    here = lax.axis_index("tm")

    w_real, w_imag = steering
    real = jnp.dot(w_real, surveillance[0], precision=HIGHEST) - jnp.dot(w_imag, surveillance[1], precision=HIGHEST)
    imag = jnp.dot(w_imag, surveillance[0], precision=HIGHEST) + jnp.dot(w_real, surveillance[1], precision=HIGHEST)
    beam = lax.psum_scatter(jnp.stack([real, imag], 1), "chan", scatter_dimension=0, tiled=True)
    ref_all = lax.all_gather(ref_signal, "tm", axis=1, tiled=True)
    ref_ext = jnp.pad(ref_all, ((0, 0), (LAGS, 0)))

    def beam_step(carry, q):
        offset = q * BLOCK_LEN
        table = lag_table(ref_ext, here * length + offset, LAGS)
        segment = lax.dynamic_slice_in_dim(beam, offset, BLOCK_LEN, 2)
        return carry, times_conj(segment, table)

    _, products = lax.scan(beam_step, None, jnp.arange(local_blocks, dtype=jnp.int32))
    cross = lax.psum(products[..., :TAPS].sum(0), "tm")
    got = lax.all_to_all(products, "tm", 3, 0, tiled=True)

    def own_step(gram, q):
        offset = q * BLOCK_LEN
        table = lag_table(ref_ext, offset, LAGS)
        taps = table[:, :TAPS].transpose(1, 0, 2)
        mine = lax.dynamic_slice_in_dim(table, here * lags_local, lags_local, 1)
        return gram + times_conj(taps, table[:, :TAPS]), times_conj(taps, mine)

    start = jnp.zeros((TAPS, 2, TAPS), jnp.float32)
    gram, own = lax.scan(own_step, start, jnp.arange(samples // BLOCK_LEN, dtype=jnp.int32))
    g_real, g_imag = gram[:, 0].T, gram[:, 1].T
    system = jnp.concatenate([jnp.concatenate([g_real, -g_imag], 1), jnp.concatenate([g_imag, g_real], 1)], 0)
    right = jnp.concatenate([cross[:, 0].T, cross[:, 1].T], 0)
    solved = jax.scipy.linalg.cho_solve((jnp.linalg.cholesky(system), True), right)
    b_real, b_imag = solved[:TAPS].T, solved[TAPS:].T
    mixing = jnp.concatenate([jnp.stack([b_real, b_imag], 1), jnp.stack([-b_imag, b_real], 1)], 2)
    stacked = jnp.concatenate([own[:, :, 0], own[:, :, 1]], 1)
    lagged = got - jnp.einsum("mck,qkl->qmcl", mixing, stacked, precision=HIGHEST)
    wave = jnp.asarray(doppler_table(samples // BLOCK_LEN, 0.125 / math.sqrt(samples)))
    wave = wave.reshape(2, samples // BLOCK_LEN, 2, DOPPLER)
    return jnp.einsum("qmcl,cqdk->mdlk", lagged, wave, precision=HIGHEST)


def on_device(ref_signal, surveillance, steering):
    chan_count, tm_count = lax.axis_size("chan"), lax.axis_size("tm")
    beams_local = steering.shape[1] // chan_count
    lags_local = LAGS // tm_count
    fills = (
        LANES % lags_local == 0
        and lags_local % (2 * SUBLANES) == 0
        and beams_local * lags_local == LANES * SUBLANES // 2
        and chan_count > 1
        and chan_count & (chan_count - 1) == 0
        and tm_count > 1
        and tm_count & (tm_count - 1) == 0
        and 2 * surveillance.shape[1] % LANES == 0
        and surveillance.shape[2] % (2 * BATCH * BLOCK_LEN) == 0
    )
    device = tiled_device if fills else plain_device
    return device(ref_signal, surveillance, steering)


def solution(mesh):
    placed = (P(None, "tm"), P(None, "chan", "tm"), P(None, None, "chan"))
    return jax.shard_map(
        on_device,
        mesh=mesh,
        in_specs=placed,
        out_specs=P("chan", None, "tm", None),
        check_vma=False,
    )
```

```python
import functools
import math

import jax
import jax.numpy as jnp
import numpy as np
from jax import lax
from jax.experimental import pallas as pl
from jax.experimental.pallas import tpu as pltpu
from jax.sharding import PartitionSpec as P

LAGS = 256
DOPPLER = 256
TAPS = 64
BLOCK_LEN = 256
LANES = 128
SUBLANES = 8
EDGE = 2

HIGHEST = lax.Precision.HIGHEST
VMEM_BYTES = 48 * 1024 * 1024


def params():
    return pltpu.CompilerParams(vmem_limit_bytes=VMEM_BYTES)


def cost(us):
    return pl.CostEstimate(flops=int(us * 1.15e9), bytes_accessed=0, transcendentals=0)


def halves(x):
    high = x.astype(jnp.bfloat16)
    return high, (x - high.astype(jnp.float32)).astype(jnp.bfloat16)


def dot_nt(a, b, precision=None):
    return lax.dot_general(
        a, b, (((1,), (1,)), ((), ())), precision=precision, preferred_element_type=jnp.float32
    )


def dot_split(a, b):
    (a_high, a_low), (b_high, b_low) = a, b
    left = jnp.concatenate([a_high, a_low], 1)
    right = jnp.concatenate([b_high, b_high], 0)
    return jnp.dot(left, right, preferred_element_type=jnp.float32) + jnp.dot(
        a_high, b_low, preferred_element_type=jnp.float32
    )


def row_sign(shape):
    rows = lax.broadcasted_iota(jnp.int32, shape, 0)
    return jnp.where(rows % SUBLANES < SUBLANES // 2, 1.0, -1.0).astype(jnp.float32)


def lane_sign(shape):
    lanes = lax.broadcasted_iota(jnp.int32, shape, 1)
    return jnp.where(lanes % LANES < LANES // 2, 1.0, -1.0).astype(jnp.float32)


def swap_groups(rows, groups):
    width = LANES // groups
    lane_group = lax.broadcasted_iota(jnp.int32, rows[0].shape, 1) // width
    outs = []
    for j in range(groups):
        out = rows[j]
        for i in range(groups):
            if i != j:
                moved = pltpu.roll(rows[i], (width * (i - j)) % LANES, 1)
                out = jnp.where(lane_group == i, moved, out)
        outs.append(out)
    return outs


CHUNKS = 4


def beam_kernel(
    chan_count, beams_local, w_hbm, s_hbm, ref_hbm, kept_ref, sent_ref, tiles_ref, edge_ref, spread_hbm,
    w_ref, s_ref, ref_ref, w_sem, s_sem, ref_sem, spread_sem,
):
    me = lax.axis_index("chan")
    length = s_hbm.shape[1]
    width = length // CHUNKS
    w_copy = pltpu.make_async_copy(w_hbm, w_ref, w_sem)
    w_copy.start()
    ref_copy = pltpu.make_async_copy(ref_hbm, ref_ref, ref_sem)
    ref_copy.start()
    s_copies = []
    for n in range(CHUNKS):
        cols = pl.ds(n * width, width)
        s_copies.append(pltpu.make_async_copy(s_hbm.at[:, cols], s_ref.at[:, cols], s_sem.at[n]))
        s_copies[n].start()
    half = SUBLANES // 2
    sub = lax.broadcasted_iota(jnp.int32, (SUBLANES, w_hbm.shape[2]), 0)
    top = sub < half
    w_copy.wait()
    rows = []
    for parity in range(2):
        for e in range(parity, chan_count, 2):
            base = (me ^ e) * beams_local
            for tile in range(beams_local // SUBLANES):
                start = pl.multiple_of(base + tile * SUBLANES, SUBLANES)
                wr = w_ref[0, pl.ds(start, SUBLANES), :]
                wi = w_ref[1, pl.ds(start, SUBLANES), :]
                wr_s = pltpu.roll(wr, half, 0)
                wi_s = pltpu.roll(wi, half, 0)
                first = [jnp.where(top, wr, wi_s), jnp.where(top, -wi, wr_s)]
                second = [jnp.where(top, wr_s, wi), jnp.where(top, -wi_s, wr)]
                rows.append(jnp.concatenate(first, 1))
                rows.append(jnp.concatenate(second, 1))
    weights = halves(jnp.concatenate(rows, 0))
    ref_copy.wait()
    edge_ref[...] = jnp.zeros_like(edge_ref)
    count = tiles_ref.shape[1]
    for c in range(2):
        for n in range(count):
            row = ref_ref[c : c + 1, n * LANES : (n + 1) * LANES]
            tiles_ref[c, n : n + 1, :] = row
            if n >= count - EDGE:
                at = SUBLANES * c + n + EDGE - count
                edge_ref[at : at + 1, :] = row
    copies = []
    for n in range(spread_hbm.shape[0]):
        copies.append(pltpu.make_async_copy(tiles_ref, spread_hbm.at[n], spread_sem.at[n]))
        copies[n].start()
    mid = weights[0].shape[0] // 2
    for n in range(CHUNKS):
        cols = slice(n * width, (n + 1) * width)
        s_copies[n].wait()
        product = dot_split(weights, halves(s_ref[:, cols]))
        kept_ref[:, cols] = product[:mid]
        sent_ref[:, cols] = product[mid:]
    for copy in copies:
        copy.wait()


def beam_call(steering, survey, ref, owners, chan_count, beams_local):
    depth, length = survey.shape
    rows = chan_count * beams_local
    tiles = (2, length // LANES, LANES)
    out = jax.ShapeDtypeStruct((rows, length), jnp.float32)
    hbm, vmem = pl.BlockSpec(memory_space=pltpu.HBM), pl.BlockSpec(memory_space=pltpu.VMEM)
    return pl.pallas_call(
        functools.partial(beam_kernel, chan_count, beams_local),
        in_specs=[hbm] * 3,
        out_specs=[vmem] * 4 + [hbm],
        out_shape=[
            out,
            out,
            jax.ShapeDtypeStruct(tiles, jnp.float32),
            jax.ShapeDtypeStruct((2 * SUBLANES, LANES), jnp.float32),
            jax.ShapeDtypeStruct((owners,) + tiles, jnp.float32),
        ],
        scratch_shapes=[
            pltpu.VMEM(steering.shape, jnp.float32),
            pltpu.VMEM(survey.shape, jnp.float32),
            pltpu.VMEM(ref.shape, jnp.float32),
            pltpu.SemaphoreType.DMA,
            pltpu.SemaphoreType.DMA((CHUNKS,)),
            pltpu.SemaphoreType.DMA,
            pltpu.SemaphoreType.DMA((owners,)),
        ],
        compiler_params=params(),
        cost_estimate=cost(2.2),
        name="beams",
    )(*(pltpu.with_memory_space_constraint(x, pltpu.HBM) for x in (steering, survey, ref)))


def hold_kernel(*refs):
    del refs


def hold_call(x, *after):
    return pl.pallas_call(
        hold_kernel,
        in_specs=[pl.BlockSpec(memory_space=pltpu.HBM)] + [pl.BlockSpec(memory_space=pl.ANY)] * len(after),
        out_specs=pl.BlockSpec(memory_space=pltpu.HBM),
        out_shape=jax.ShapeDtypeStruct(x.shape, x.dtype),
        input_output_aliases={0: 0},
        compiler_params=params(),
        cost_estimate=cost(0.1),
        name="reference_held",
    )(x, *after)


def sum_kernel(count, *refs):
    kept_ref, sent_ref = refs[-2:]
    for n in range(kept_ref.shape[0]):
        for offset, out_ref in ((0, kept_ref), (1, sent_ref)):
            total = refs[0][2 * n + offset]
            for ref in refs[1:count]:
                total = total + ref[2 * n + offset]
            out_ref[n] = total


def sum_call(parts):
    shape = (parts[0].shape[0] // 2,) + parts[0].shape[1:]
    out = jax.ShapeDtypeStruct(shape, jnp.float32)
    vmem = pl.BlockSpec(memory_space=pltpu.VMEM)
    return pl.pallas_call(
        functools.partial(sum_kernel, len(parts)),
        in_specs=[vmem] * len(parts),
        out_specs=[vmem, vmem],
        out_shape=[out, out],
        compiler_params=params(),
        cost_estimate=cost(0.1),
        name="halves_summed",
    )(*parts)


def table_kernel(edge_ref, tiles_ref, out_ref):
    rows = tiles_ref.shape[1]
    for c in range(2):
        line = [edge_ref[SUBLANES * c + n : SUBLANES * c + n + 1, :] for n in range(EDGE)]
        line = jnp.concatenate(line + [tiles_ref[c, n : n + 1, :] for n in range(rows)], 1)
        for g in range(0, LANES, 2 * SUBLANES):
            tiled = jnp.broadcast_to(line, (2 * SUBLANES, line.shape[1]))
            high, low = halves(pltpu.roll(tiled, g, 1, stride=1, stride_axis=0)[:, LANES:])
            out_ref[0, c, g : g + 2 * SUBLANES] = high
            out_ref[1, c, g : g + 2 * SUBLANES] = low


def table_call(edge, tiles):
    shape = (2, 2, LANES, LANES * (tiles.shape[1] + 1))
    return pl.pallas_call(
        table_kernel,
        out_shape=jax.ShapeDtypeStruct(shape, jnp.bfloat16),
        compiler_params=params(),
        cost_estimate=cost(0.7),
        name="shifted_reference",
    )(edge, tiles)


def lag_kernel(groups, *refs):
    *y_refs, table_ref, _, out_hbm, out_ref, out_sem = refs
    copies = []

    def send(start, count):
        part = (slice(None), pl.ds(start, count))
        copies.append(pltpu.make_async_copy(out_ref.at[part], out_hbm.at[part], out_sem.at[len(copies)]))
        copies[-1].start()

    y = y_refs[0][...]
    for y_ref in y_refs[1:]:
        y = y + y_ref[...]
    rows, length = y.shape
    blocks = length // BLOCK_LEN
    turned = jnp.concatenate(
        [pltpu.roll(y[r : r + SUBLANES], SUBLANES // 2, 0) for r in range(0, rows, SUBLANES)], 0
    )
    turned = turned * row_sign(turned.shape)
    y_high, y_low = halves(y)
    t_high, t_low = halves(turned)
    both = jnp.concatenate([y_high, y_low], 0)
    turned_both = jnp.concatenate([t_high, t_low], 0)
    taps_sum = None
    for q in range(blocks):
        near = slice(q * BLOCK_LEN + LANES, q * BLOCK_LEN + LANES + BLOCK_LEN)
        far = slice(q * BLOCK_LEN, (q + 1) * BLOCK_LEN)
        cols = slice(q * BLOCK_LEN, (q + 1) * BLOCK_LEN)
        tables = []
        for h in range(2):
            tables.append(
                jnp.concatenate(
                    [
                        jnp.concatenate([table_ref[h, 0, :, near], table_ref[h, 1, :, near]], 1),
                        jnp.concatenate([table_ref[h, 0, :, far], table_ref[h, 1, :, far]], 1),
                    ],
                    0,
                )
            )
        lhs = jnp.concatenate([both[:, cols], turned_both[:, cols]], 1)
        by_high = dot_nt(lhs, tables[0])
        by_low = dot_nt(lhs[:rows], tables[1])
        product = by_high[:rows] + (by_high[rows:] + by_low)
        taps = product[:, :LANES]
        taps_sum = taps if taps_sum is None else taps_sum + taps
        for h in range(LAGS // LANES):
            lanes = slice(h * LANES, (h + 1) * LANES)
            tiles = [product[r : r + SUBLANES, lanes] for r in range(0, rows, SUBLANES)]
            for j, tile in enumerate(swap_groups(tiles, groups)):
                out_ref[h * groups + j, q] = tile
        if q % 2:
            send(q - 1, 2)
    left = lax.broadcasted_iota(jnp.int32, (SUBLANES, LANES), 1) < TAPS
    for i in range(groups // 2):
        a = taps_sum[i * SUBLANES : (i + 1) * SUBLANES]
        other = i + groups // 2
        b = taps_sum[other * SUBLANES : (other + 1) * SUBLANES]
        tile = jnp.where(left, a, pltpu.roll(b, LANES - TAPS, 1))
        for owner in range(out_ref.shape[0]):
            out_ref[owner, blocks + i] = tile
    send(blocks, groups // 2)
    for copy in copies:
        copy.wait()


def lag_call(ys, table, after, groups, owners):
    blocks = ys[0].shape[1] // BLOCK_LEN
    shape = (owners, blocks + groups // 2, SUBLANES, LANES)
    vmem = pl.BlockSpec(memory_space=pltpu.VMEM)
    return pl.pallas_call(
        functools.partial(lag_kernel, groups),
        in_specs=[vmem] * (len(ys) + 1) + [pl.BlockSpec(memory_space=pl.ANY)],
        out_specs=pl.BlockSpec(memory_space=pltpu.HBM),
        out_shape=jax.ShapeDtypeStruct(shape, jnp.float32),
        scratch_shapes=[pltpu.VMEM(shape, jnp.float32), pltpu.SemaphoreType.DMA((blocks // 2 + 1,))],
        compiler_params=params(),
        cost_estimate=cost(2.1),
        name="lag_products",
    )(*ys, table, after)


BATCH = 4


def own_kernel(lags_local, *refs):
    ref_ref, _, out_ref, line_ref, tail_ref, span_ref, late_ref, taps_a, lags_a, taps_b, lags_b = refs
    me = lax.axis_index("tm")
    owners, _, part_rows, _ = ref_ref.shape
    samples = owners * part_rows * LANES
    steps = samples // BLOCK_LEN // BATCH
    total_rows = span_ref.shape[1]
    block_rows = BLOCK_LEN // LANES

    span_ref[...] = jnp.zeros_like(span_ref)
    for t in range(owners):
        span_ref[:, EDGE + t * part_rows : EDGE + (t + 1) * part_rows, :] = ref_ref[t]
    late_rows = (me * lags_local) // LANES
    late_lanes = lax.rem(me * lags_local, LANES)
    turned = [pltpu.roll(span_ref[c], late_lanes, 1) for c in range(2)]
    before = [pltpu.roll(x, 1, 0) for x in turned]
    lanes = lax.broadcasted_iota(jnp.int32, (total_rows, LANES), 1)
    for c in range(2):
        late_ref[c] = pltpu.roll(jnp.where(lanes < late_lanes, before[c], turned[c]), late_rows, 0)

    def line_of(ref, c, first, count):
        return jnp.concatenate([ref[c, pl.ds(first + n, 1), :] for n in range(count)], 1)

    def shifted(line, by):
        tiled = jnp.broadcast_to(line, (2 * SUBLANES, line.shape[1]))
        return pltpu.roll(tiled, by, 1, stride=1, stride_axis=0)[:, LANES:]

    def keep(ref, row, value):
        high, low = halves(value)
        half = ref.shape[0] // 2
        ref[row : row + 2 * SUBLANES, :] = high
        ref[half + row : half + row + 2 * SUBLANES, :] = low

    def build(n, taps_ref, lags_ref):
        first = EDGE - 1 + n * BATCH * block_rows
        count = BATCH * block_rows + 1
        lines = [line_of(span_ref, c, first, count) for c in range(2)]
        for c in range(2):
            for g in range(0, TAPS, 2 * SUBLANES):
                keep(taps_ref, c * TAPS + g, shifted(lines[c], g))
            late = line_of(late_ref, c, first, count)
            for g in range(0, lags_local, 2 * SUBLANES):
                keep(lags_ref, c * lags_local + g, shifted(late, g))
        pad = jnp.zeros((2 * SUBLANES - 2, BATCH * BLOCK_LEN), jnp.float32)
        keep(lags_ref, 2 * lags_local, jnp.concatenate([line[:, LANES:] for line in lines] + [pad], 0))

    turn = lane_sign((lags_local, LANES))

    def use(n, taps_ref, lags_ref):
        count = lags_ref.shape[0] // 2
        for b in range(BATCH):
            cols = slice(b * BLOCK_LEN, (b + 1) * BLOCK_LEN)
            product = dot_nt(lags_ref[:, cols], taps_ref[:, cols])
            product = product[:count, :LANES] + (product[:count, LANES:] + product[count:, :LANES])
            by_real = product[:lags_local]
            by_imag = product[lags_local : 2 * lags_local]
            rows = pl.ds(pl.multiple_of((n * BATCH + b) * lags_local, lags_local), lags_local)
            high, low = halves(by_real + turn * pltpu.roll(by_imag, TAPS, 1))
            out_ref[0, rows, :] = high
            out_ref[1, rows, :] = low
            line_ref[...] += product[2 * lags_local : 2 * lags_local + SUBLANES]

    line_ref[...] = jnp.zeros_like(line_ref)
    build(0, taps_a, lags_a)

    def pair(m, carry):
        build(2 * m + 1, taps_b, lags_b)
        use(2 * m, taps_a, lags_a)
        build(jnp.minimum(2 * m + 2, steps - 1), taps_a, lags_a)
        use(2 * m + 1, taps_b, lags_b)
        return carry

    lax.fori_loop(0, steps // 2, pair, 0)
    tail = []
    for c in range(2):
        line = line_of(span_ref, c, EDGE + owners * part_rows - 1, 2)
        tail += [shifted(line, g) for g in range(0, TAPS, 2 * SUBLANES)]
    tail = jnp.concatenate(tail, 0)
    tail_ref[...] = dot_nt(tail, tail, HIGHEST)


def own_call(ref_all, lags_local, after):
    span_rows = ref_all.shape[0] * ref_all.shape[2]
    rows = span_rows * LANES // BLOCK_LEN * lags_local
    held_rows = -(-(span_rows + 2 * EDGE) // SUBLANES) * SUBLANES
    width = BATCH * BLOCK_LEN
    taps = pltpu.VMEM((4 * TAPS, width), jnp.bfloat16)
    lags = pltpu.VMEM((4 * lags_local + 4 * SUBLANES, width), jnp.bfloat16)
    span = pltpu.VMEM((2, held_rows, LANES), jnp.float32)
    return pl.pallas_call(
        functools.partial(own_kernel, lags_local),
        in_specs=[pl.BlockSpec(memory_space=pltpu.VMEM), pl.BlockSpec(memory_space=pl.ANY)],
        out_shape=[
            jax.ShapeDtypeStruct((2, rows, 2 * TAPS), jnp.bfloat16),
            jax.ShapeDtypeStruct((SUBLANES, 2 * TAPS), jnp.float32),
            jax.ShapeDtypeStruct((2 * TAPS, 2 * TAPS), jnp.float32),
        ],
        scratch_shapes=[span, span, taps, lags, taps, lags],
        compiler_params=params(),
        cost_estimate=cost(6.2),
        name="reference_products",
    )(ref_all, after)


def as_factor(a):
    return jnp.concatenate([a, -lane_sign(a.shape) * pltpu.roll(a, a.shape[0], 1)], 0)


def solver_kernel(line_ref, tail_ref, gram_ref, solver_ref):
    total = line_ref[...]
    line = total[0:1] + lane_sign((1, LANES)) * pltpu.roll(total[1:2], TAPS, 1)
    low = lax.broadcasted_iota(jnp.int32, (1, LANES), 1) < TAPS
    line_r = jnp.where(low, line, 0.0)
    line_i = jnp.where(low, pltpu.roll(line, TAPS, 1), 0.0)
    cols = lax.broadcasted_iota(jnp.int32, (TAPS, TAPS), 1)
    rows = lax.broadcasted_iota(jnp.int32, (TAPS, TAPS), 0)
    above = cols > rows

    def upper(x):
        spread = pltpu.roll(jnp.broadcast_to(x, (TAPS, LANES)), 0, 1, stride=1, stride_axis=0)
        return spread[:, :TAPS]

    up_r = upper(line_r)
    up_i = jnp.where(above, upper(line_i), 0.0)
    strict_r = jnp.where(above, up_r, 0.0)
    diag_r = jnp.where(cols == rows, up_r, 0.0)
    tails = tail_ref[...]
    gram_r = strict_r + strict_r.T + diag_r - (tails[:TAPS, :TAPS] + tails[TAPS:, TAPS:])
    gram_i = up_i - up_i.T - (tails[:TAPS, TAPS:] - tails[TAPS:, :TAPS])
    gram = jnp.concatenate([gram_r, gram_i], 1)
    gram_halves = halves(as_factor(gram))
    gram_ref[0], gram_ref[1] = gram_halves
    one = (
        lax.broadcasted_iota(jnp.int32, gram.shape, 0) == lax.broadcasted_iota(jnp.int32, gram.shape, 1)
    ).astype(jnp.float32)
    bound = jnp.max(jnp.sum(jnp.abs(gram), axis=1, keepdims=True), axis=0, keepdims=True)

    def again(state):
        count, left, _ = state
        return (count < 60) & (left > 1e-3)

    def newton(state):
        count, _, x = state
        x_halves = halves(x)
        seen = dot_split(x_halves, gram_halves)
        left = jnp.max(jnp.abs(seen - one))
        x = 2.0 * x - dot_split(halves(seen), halves(as_factor(x)))
        return count + 1, left, x

    start = (jnp.int32(0), jnp.float32(1.0), one * (1.0 / bound))
    _, _, inverse = lax.while_loop(again, newton, start)
    solver_ref[0], solver_ref[1] = halves(as_factor(inverse))


def solver_call(line, tail):
    out = jax.ShapeDtypeStruct((2,) + tail.shape, jnp.bfloat16)
    return pl.pallas_call(
        solver_kernel,
        out_shape=[out, out],
        compiler_params=params(),
        cost_estimate=cost(2.0),
        name="gram_inverse",
    )(line, tail)


def doppler_table(block_count, scale):
    phase = (np.arange(block_count)[:, None] * np.arange(DOPPLER)[None, :] % DOPPLER) * (2.0 * math.pi / DOPPLER)
    cosine, sine = np.cos(phase), np.sin(phase)
    upper = np.concatenate([cosine, -sine], 1)
    lower = np.concatenate([sine, cosine], 1)
    return (np.concatenate([upper, lower], 0) * scale).astype(np.float32)


def map_kernel(groups, got_ref, own_ref, gram_ref, solver_ref, wave_ref, out_hbm, held_ref, out_ref, out_sem):
    owners, pieces = got_ref.shape[:2]
    blocks = pieces - groups // 2
    lags_local = LANES // groups
    total = owners * blocks
    left = lax.broadcasted_iota(jnp.int32, (SUBLANES, LANES), 1) < TAPS
    sign = row_sign((SUBLANES, LANES))
    rows = [None] * groups
    for i in range(groups // 2):
        tile = got_ref[0, blocks + i]
        for owner in range(1, owners):
            tile = tile + got_ref[owner, blocks + i]
        swapped = pltpu.roll(tile, TAPS, 1)
        for part, here, there in ((i, tile, swapped), (i + groups // 2, swapped, tile)):
            other = -sign * pltpu.roll(there, SUBLANES // 2, 0)
            rows[part] = jnp.where(left, here, other)
    cross = jnp.concatenate(rows, 0)
    solver = (solver_ref[0], solver_ref[1])
    taps = dot_split(halves(cross), solver)
    rest = cross - dot_split(halves(taps), (gram_ref[0], gram_ref[1]))
    taps = taps + dot_split(halves(rest), solver)
    taps_high, taps_low = halves(taps)
    taps_both = jnp.concatenate([taps_high, taps_low], 1)
    for q in range(0, total, 2 * groups):
        own = slice(q * lags_local, (q + 2 * groups) * lags_local)
        own_high = own_ref[0, own, :]
        clutter = dot_nt(taps_both, jnp.concatenate([own_high, own_high], 1)) + dot_nt(taps_high, own_ref[1, own, :])
        for h in range(2):
            lanes = slice(h * LANES, (h + 1) * LANES)
            tiles = [clutter[r : r + SUBLANES, lanes] for r in range(0, groups * SUBLANES, SUBLANES)]
            for j, tile in enumerate(swap_groups(tiles, groups)):
                at = q + h * groups + j
                held_ref[at * SUBLANES : (at + 1) * SUBLANES, :] = got_ref[at // blocks, at % blocks] - tile
    half = SUBLANES // 2
    wave = (wave_ref[0], wave_ref[1])
    copies = []
    for g in range(half):
        parts = [held_ref[pl.ds(c * half + g, total, stride=SUBLANES), :] for c in range(2)]
        spectrum = dot_split(halves(jnp.concatenate(parts, 0).T), wave)
        for i in range(groups):
            beam = half * i + g
            for c in range(2):
                out_ref[beam, c] = spectrum[i * lags_local : (i + 1) * lags_local, c * DOPPLER : (c + 1) * DOPPLER]
            copies.append(pltpu.make_async_copy(out_ref.at[beam], out_hbm.at[beam], out_sem.at[beam]))
            copies[-1].start()
    for copy in copies:
        copy.wait()


def map_call(got, own, gram, solver, wave, groups, beams_local):
    total = got.shape[0] * (got.shape[1] - groups // 2)
    lags_local = LANES // groups
    shape = (beams_local, 2, lags_local, DOPPLER)
    return pl.pallas_call(
        functools.partial(map_kernel, groups),
        in_specs=[pl.BlockSpec(memory_space=pltpu.VMEM)] * 5,
        out_specs=pl.BlockSpec(memory_space=pltpu.HBM),
        out_shape=jax.ShapeDtypeStruct(shape, jnp.float32),
        scratch_shapes=[
            pltpu.VMEM((total * SUBLANES, LANES), jnp.float32),
            pltpu.VMEM(shape, jnp.float32),
            pltpu.SemaphoreType.DMA((beams_local,)),
        ],
        compiler_params=params(),
        cost_estimate=cost(2.5),
        name="range_doppler",
    )(got, own, gram, solver, wave)


def swap(x, axis, by):
    pairs = [(i, i ^ by) for i in range(lax.axis_size(axis))]
    return lax.ppermute(x, axis, pairs)


def tiled_device(ref_signal, surveillance, steering):
    chan_count, tm_count = lax.axis_size("chan"), lax.axis_size("tm")
    channels, length = surveillance.shape[1:]
    beams_local = steering.shape[1] // chan_count
    lags_local = LAGS // tm_count
    groups = LANES // lags_local
    samples = length * tm_count

    survey = surveillance.reshape(2 * channels, length)
    kept, moved, tiles, edge, spread = beam_call(steering, survey, ref_signal, tm_count, chan_count, beams_local)
    edge = lax.ppermute(edge, "tm", [(i, i + 1) for i in range(tm_count - 1)])
    shape = (chan_count // 2, 2 * beams_local, length)
    kept, got = kept.reshape(shape), swap(moved, "chan", 1).reshape(shape)
    by = 2
    while by < chan_count:
        kept, moved = sum_call([kept, got])
        got = swap(moved, "chan", by)
        by *= 2
    spread = hold_call(spread, moved, edge)
    ref_all = lax.all_to_all(spread, "tm", 0, 0, tiled=True)
    table = table_call(edge, tiles)
    pieces = lag_call([kept[0], got[0]], table, spread, groups, tm_count)
    got = lax.all_to_all(pieces, "tm", 0, 0, tiled=True)
    own, line, tail = own_call(ref_all, lags_local, pieces)
    gram, solver = solver_call(line, tail)
    wave = doppler_table(samples // BLOCK_LEN, 0.125 / math.sqrt(samples))
    high = wave.astype(jnp.bfloat16)
    wave = np.stack([high, (wave - high.astype(np.float32)).astype(jnp.bfloat16)])
    return map_call(got, own, gram, solver, jnp.asarray(wave), groups, beams_local)


def lag_table(ref_ext, offset, lags):
    window = lax.dynamic_slice_in_dim(ref_ext, offset, BLOCK_LEN + LAGS, 1)
    span = BLOCK_LEN + LAGS
    tiled = jnp.tile(jnp.pad(window, ((0, 0), (0, 1))), (1, lags))[:, : lags * span]
    return tiled.reshape(2, lags, span)[:, :, LAGS:]


def times_conj(a, b):
    real = jnp.einsum("...t,lt->...l", a[..., 0, :], b[0], precision=HIGHEST) + jnp.einsum(
        "...t,lt->...l", a[..., 1, :], b[1], precision=HIGHEST
    )
    imag = jnp.einsum("...t,lt->...l", a[..., 1, :], b[0], precision=HIGHEST) - jnp.einsum(
        "...t,lt->...l", a[..., 0, :], b[1], precision=HIGHEST
    )
    return jnp.stack([real, imag], -2)


def plain_device(ref_signal, surveillance, steering):
    chan_count, tm_count = lax.axis_size("chan"), lax.axis_size("tm")
    length = surveillance.shape[2]
    beams = steering.shape[1]
    lags_local = LAGS // tm_count
    samples = length * tm_count
    local_blocks = length // BLOCK_LEN
    here = lax.axis_index("tm")

    w_real, w_imag = steering
    real = jnp.dot(w_real, surveillance[0], precision=HIGHEST) - jnp.dot(w_imag, surveillance[1], precision=HIGHEST)
    imag = jnp.dot(w_imag, surveillance[0], precision=HIGHEST) + jnp.dot(w_real, surveillance[1], precision=HIGHEST)
    beam = lax.psum_scatter(jnp.stack([real, imag], 1), "chan", scatter_dimension=0, tiled=True)
    ref_all = lax.all_gather(ref_signal, "tm", axis=1, tiled=True)
    ref_ext = jnp.pad(ref_all, ((0, 0), (LAGS, 0)))

    def beam_step(carry, q):
        offset = q * BLOCK_LEN
        table = lag_table(ref_ext, here * length + offset, LAGS)
        segment = lax.dynamic_slice_in_dim(beam, offset, BLOCK_LEN, 2)
        return carry, times_conj(segment, table)

    _, products = lax.scan(beam_step, None, jnp.arange(local_blocks, dtype=jnp.int32))
    cross = lax.psum(products[..., :TAPS].sum(0), "tm")
    got = lax.all_to_all(products, "tm", 3, 0, tiled=True)

    def own_step(gram, q):
        offset = q * BLOCK_LEN
        table = lag_table(ref_ext, offset, LAGS)
        taps = table[:, :TAPS].transpose(1, 0, 2)
        mine = lax.dynamic_slice_in_dim(table, here * lags_local, lags_local, 1)
        return gram + times_conj(taps, table[:, :TAPS]), times_conj(taps, mine)

    start = jnp.zeros((TAPS, 2, TAPS), jnp.float32)
    gram, own = lax.scan(own_step, start, jnp.arange(samples // BLOCK_LEN, dtype=jnp.int32))
    g_real, g_imag = gram[:, 0].T, gram[:, 1].T
    system = jnp.concatenate([jnp.concatenate([g_real, -g_imag], 1), jnp.concatenate([g_imag, g_real], 1)], 0)
    right = jnp.concatenate([cross[:, 0].T, cross[:, 1].T], 0)
    solved = jax.scipy.linalg.cho_solve((jnp.linalg.cholesky(system), True), right)
    b_real, b_imag = solved[:TAPS].T, solved[TAPS:].T
    mixing = jnp.concatenate([jnp.stack([b_real, b_imag], 1), jnp.stack([-b_imag, b_real], 1)], 2)
    stacked = jnp.concatenate([own[:, :, 0], own[:, :, 1]], 1)
    lagged = got - jnp.einsum("mck,qkl->qmcl", mixing, stacked, precision=HIGHEST)
    wave = jnp.asarray(doppler_table(samples // BLOCK_LEN, 0.125 / math.sqrt(samples)))
    wave = wave.reshape(2, samples // BLOCK_LEN, 2, DOPPLER)
    return jnp.einsum("qmcl,cqdk->mdlk", lagged, wave, precision=HIGHEST)


def on_device(ref_signal, surveillance, steering):
    chan_count, tm_count = lax.axis_size("chan"), lax.axis_size("tm")
    beams_local = steering.shape[1] // chan_count
    lags_local = LAGS // tm_count
    fills = (
        LANES % lags_local == 0
        and lags_local % (2 * SUBLANES) == 0
        and beams_local * lags_local == LANES * SUBLANES // 2
        and chan_count > 1
        and chan_count & (chan_count - 1) == 0
        and tm_count > 1
        and tm_count & (tm_count - 1) == 0
        and 2 * surveillance.shape[1] % LANES == 0
        and surveillance.shape[2] % (2 * BATCH * BLOCK_LEN) == 0
    )
    device = tiled_device if fills else plain_device
    return device(ref_signal, surveillance, steering)


def solution(mesh):
    placed = (P(None, "tm"), P(None, "chan", "tm"), P(None, None, "chan"))
    return jax.shard_map(
        on_device,
        mesh=mesh,
        in_specs=placed,
        out_specs=P("chan", None, "tm", None),
        check_vma=False,
    )
```

```python
import functools
import math

import jax
import jax.numpy as jnp
import numpy as np
from jax import lax
from jax.experimental import pallas as pl
from jax.experimental.pallas import tpu as pltpu
from jax.sharding import PartitionSpec as P

LAGS = 256
DOPPLER = 256
TAPS = 64
BLOCK_LEN = 256
LANES = 128
SUBLANES = 8
EDGE = 2

HIGHEST = lax.Precision.HIGHEST
VMEM_BYTES = 48 * 1024 * 1024


def params():
    return pltpu.CompilerParams(vmem_limit_bytes=VMEM_BYTES)


def cost(us):
    return pl.CostEstimate(flops=int(us * 1.15e9), bytes_accessed=0, transcendentals=0)


def halves(x):
    high = x.astype(jnp.bfloat16)
    return high, (x - high.astype(jnp.float32)).astype(jnp.bfloat16)


def dot_nt(a, b, precision=None):
    return lax.dot_general(
        a, b, (((1,), (1,)), ((), ())), precision=precision, preferred_element_type=jnp.float32
    )


def dot_split(a, b):
    (a_high, a_low), (b_high, b_low) = a, b
    left = jnp.concatenate([a_high, a_low], 1)
    right = jnp.concatenate([b_high, b_high], 0)
    return jnp.dot(left, right, preferred_element_type=jnp.float32) + jnp.dot(
        a_high, b_low, preferred_element_type=jnp.float32
    )


def row_sign(shape):
    rows = lax.broadcasted_iota(jnp.int32, shape, 0)
    return jnp.where(rows % SUBLANES < SUBLANES // 2, 1.0, -1.0).astype(jnp.float32)


def lane_sign(shape):
    lanes = lax.broadcasted_iota(jnp.int32, shape, 1)
    return jnp.where(lanes % LANES < LANES // 2, 1.0, -1.0).astype(jnp.float32)


def swap_groups(rows, groups):
    width = LANES // groups
    lane_group = lax.broadcasted_iota(jnp.int32, rows[0].shape, 1) // width
    outs = []
    for j in range(groups):
        out = rows[j]
        for i in range(groups):
            if i != j:
                moved = pltpu.roll(rows[i], (width * (i - j)) % LANES, 1)
                out = jnp.where(lane_group == i, moved, out)
        outs.append(out)
    return outs


CHUNKS = 4


def beam_kernel(
    chan_count, beams_local, w_hbm, s_hbm, ref_hbm, kept_ref, sent_ref, tiles_ref, edge_ref,
    w_ref, s_ref, ref_ref, w_sem, s_sem, ref_sem,
):
    me = lax.axis_index("chan")
    length = s_hbm.shape[1]
    width = length // CHUNKS
    w_copy = pltpu.make_async_copy(w_hbm, w_ref, w_sem)
    w_copy.start()
    ref_copy = pltpu.make_async_copy(ref_hbm, ref_ref, ref_sem)
    ref_copy.start()
    s_copies = []
    for n in range(CHUNKS):
        cols = pl.ds(n * width, width)
        s_copies.append(pltpu.make_async_copy(s_hbm.at[:, cols], s_ref.at[:, cols], s_sem.at[n]))
        s_copies[n].start()
    half = SUBLANES // 2
    sub = lax.broadcasted_iota(jnp.int32, (SUBLANES, w_hbm.shape[2]), 0)
    top = sub < half
    w_copy.wait()
    rows = []
    for parity in range(2):
        for e in range(parity, chan_count, 2):
            base = (me ^ e) * beams_local
            for tile in range(beams_local // SUBLANES):
                start = pl.multiple_of(base + tile * SUBLANES, SUBLANES)
                wr = w_ref[0, pl.ds(start, SUBLANES), :]
                wi = w_ref[1, pl.ds(start, SUBLANES), :]
                wr_s = pltpu.roll(wr, half, 0)
                wi_s = pltpu.roll(wi, half, 0)
                first = [jnp.where(top, wr, wi_s), jnp.where(top, -wi, wr_s)]
                second = [jnp.where(top, wr_s, wi), jnp.where(top, -wi_s, wr)]
                rows.append(jnp.concatenate(first, 1))
                rows.append(jnp.concatenate(second, 1))
    weights = halves(jnp.concatenate(rows, 0))
    ref_copy.wait()
    edge_ref[...] = jnp.zeros_like(edge_ref)
    count = tiles_ref.shape[1]
    for c in range(2):
        for n in range(count):
            row = ref_ref[c : c + 1, n * LANES : (n + 1) * LANES]
            tiles_ref[c, n : n + 1, :] = row
            if n >= count - EDGE:
                at = SUBLANES * c + n + EDGE - count
                edge_ref[at : at + 1, :] = row
    mid = weights[0].shape[0] // 2
    for n in range(CHUNKS):
        cols = slice(n * width, (n + 1) * width)
        s_copies[n].wait()
        product = dot_split(weights, halves(s_ref[:, cols]))
        kept_ref[:, cols] = product[:mid]
        sent_ref[:, cols] = product[mid:]


def beam_call(steering, survey, ref, chan_count, beams_local):
    depth, length = survey.shape
    rows = chan_count * beams_local
    tiles = (2, length // LANES, LANES)
    out = jax.ShapeDtypeStruct((rows, length), jnp.float32)
    hbm, vmem = pl.BlockSpec(memory_space=pltpu.HBM), pl.BlockSpec(memory_space=pltpu.VMEM)
    return pl.pallas_call(
        functools.partial(beam_kernel, chan_count, beams_local),
        in_specs=[hbm] * 3,
        out_specs=[vmem] * 4,
        out_shape=[
            out,
            out,
            jax.ShapeDtypeStruct(tiles, jnp.float32),
            jax.ShapeDtypeStruct((2 * SUBLANES, LANES), jnp.float32),
        ],
        scratch_shapes=[
            pltpu.VMEM(steering.shape, jnp.float32),
            pltpu.VMEM(survey.shape, jnp.float32),
            pltpu.VMEM(ref.shape, jnp.float32),
            pltpu.SemaphoreType.DMA,
            pltpu.SemaphoreType.DMA((CHUNKS,)),
            pltpu.SemaphoreType.DMA,
        ],
        compiler_params=params(),
        cost_estimate=cost(2.2),
        name="beams",
    )(*(pltpu.with_memory_space_constraint(x, pltpu.HBM) for x in (steering, survey, ref)))


def sum_kernel(count, *refs):
    kept_ref, sent_ref = refs[-2:]
    for n in range(kept_ref.shape[0]):
        for offset, out_ref in ((0, kept_ref), (1, sent_ref)):
            total = refs[0][2 * n + offset]
            for ref in refs[1:count]:
                total = total + ref[2 * n + offset]
            out_ref[n] = total


def sum_call(parts):
    shape = (parts[0].shape[0] // 2,) + parts[0].shape[1:]
    out = jax.ShapeDtypeStruct(shape, jnp.float32)
    vmem = pl.BlockSpec(memory_space=pltpu.VMEM)
    return pl.pallas_call(
        functools.partial(sum_kernel, len(parts)),
        in_specs=[vmem] * len(parts),
        out_specs=[vmem, vmem],
        out_shape=[out, out],
        compiler_params=params(),
        cost_estimate=cost(0.1),
        name="halves_summed",
    )(*parts)


def join_kernel(first_ref, second_ref, *refs):
    out_ref = refs[-1]
    count = first_ref.shape[0]
    out_ref[:count] = first_ref[...]
    out_ref[count:] = second_ref[...]


def join_call(first, second, *after):
    vmem = pl.BlockSpec(memory_space=pltpu.VMEM)
    return pl.pallas_call(
        join_kernel,
        in_specs=[vmem, vmem] + [pl.BlockSpec(memory_space=pl.ANY)] * len(after),
        out_shape=jax.ShapeDtypeStruct((2 * first.shape[0],) + first.shape[1:], jnp.float32),
        compiler_params=params(),
        cost_estimate=cost(1.0),
        name="reference_joined",
    )(first, second, *after)


def table_kernel(edge_ref, tiles_ref, *refs):
    *round_refs, out_ref = refs
    me = lax.axis_index("tm")
    rows = tiles_ref.shape[1]
    for c in range(2):
        before = edge_ref[SUBLANES * c : SUBLANES * c + EDGE, :]
        for n, round_ref in enumerate(round_refs):
            last = round_ref[round_ref.shape[0] - 1, c, rows - EDGE :, :]
            before = jnp.where((me > 0) & ((me ^ (me - 1)) == 2 ** (n + 1) - 1), last, before)
        line = [before[n : n + 1] for n in range(EDGE)]
        line = jnp.concatenate(line + [tiles_ref[c, n : n + 1, :] for n in range(rows)], 1)
        for g in range(0, LANES, 2 * SUBLANES):
            tiled = jnp.broadcast_to(line, (2 * SUBLANES, line.shape[1]))
            high, low = halves(pltpu.roll(tiled, g, 1, stride=1, stride_axis=0)[:, LANES:])
            out_ref[0, c, g : g + 2 * SUBLANES] = high
            out_ref[1, c, g : g + 2 * SUBLANES] = low


def table_call(edge, tiles, rounds):
    shape = (2, 2, LANES, LANES * (tiles.shape[1] + 1))
    return pl.pallas_call(
        table_kernel,
        out_shape=jax.ShapeDtypeStruct(shape, jnp.bfloat16),
        compiler_params=params(),
        cost_estimate=cost(0.7),
        name="shifted_reference",
    )(edge, tiles, *rounds)


def lag_kernel(groups, *refs):
    *y_refs, table_ref, _, out_hbm, out_ref, out_sem = refs
    copies = []

    def send(start, count):
        part = (slice(None), pl.ds(start, count))
        copies.append(pltpu.make_async_copy(out_ref.at[part], out_hbm.at[part], out_sem.at[len(copies)]))
        copies[-1].start()

    y = y_refs[0][...]
    for y_ref in y_refs[1:]:
        y = y + y_ref[...]
    rows, length = y.shape
    blocks = length // BLOCK_LEN
    turned = jnp.concatenate(
        [pltpu.roll(y[r : r + SUBLANES], SUBLANES // 2, 0) for r in range(0, rows, SUBLANES)], 0
    )
    turned = turned * row_sign(turned.shape)
    y_high, y_low = halves(y)
    t_high, t_low = halves(turned)
    both = jnp.concatenate([y_high, y_low], 0)
    turned_both = jnp.concatenate([t_high, t_low], 0)
    taps_sum = None
    for q in range(blocks):
        near = slice(q * BLOCK_LEN + LANES, q * BLOCK_LEN + LANES + BLOCK_LEN)
        far = slice(q * BLOCK_LEN, (q + 1) * BLOCK_LEN)
        cols = slice(q * BLOCK_LEN, (q + 1) * BLOCK_LEN)
        tables = []
        for h in range(2):
            tables.append(
                jnp.concatenate(
                    [
                        jnp.concatenate([table_ref[h, 0, :, near], table_ref[h, 1, :, near]], 1),
                        jnp.concatenate([table_ref[h, 0, :, far], table_ref[h, 1, :, far]], 1),
                    ],
                    0,
                )
            )
        lhs = jnp.concatenate([both[:, cols], turned_both[:, cols]], 1)
        by_high = dot_nt(lhs, tables[0])
        by_low = dot_nt(lhs[:rows], tables[1])
        product = by_high[:rows] + (by_high[rows:] + by_low)
        taps = product[:, :LANES]
        taps_sum = taps if taps_sum is None else taps_sum + taps
        for h in range(LAGS // LANES):
            lanes = slice(h * LANES, (h + 1) * LANES)
            tiles = [product[r : r + SUBLANES, lanes] for r in range(0, rows, SUBLANES)]
            for j, tile in enumerate(swap_groups(tiles, groups)):
                out_ref[h * groups + j, q] = tile
        if q % 2:
            send(q - 1, 2)
    left = lax.broadcasted_iota(jnp.int32, (SUBLANES, LANES), 1) < TAPS
    for i in range(groups // 2):
        a = taps_sum[i * SUBLANES : (i + 1) * SUBLANES]
        other = i + groups // 2
        b = taps_sum[other * SUBLANES : (other + 1) * SUBLANES]
        tile = jnp.where(left, a, pltpu.roll(b, LANES - TAPS, 1))
        for owner in range(out_ref.shape[0]):
            out_ref[owner, blocks + i] = tile
    send(blocks, groups // 2)
    for copy in copies:
        copy.wait()


def lag_call(ys, table, after, groups, owners):
    blocks = ys[0].shape[1] // BLOCK_LEN
    shape = (owners, blocks + groups // 2, SUBLANES, LANES)
    vmem = pl.BlockSpec(memory_space=pltpu.VMEM)
    return pl.pallas_call(
        functools.partial(lag_kernel, groups),
        in_specs=[vmem] * (len(ys) + 1) + [pl.BlockSpec(memory_space=pl.ANY)],
        out_specs=pl.BlockSpec(memory_space=pltpu.HBM),
        out_shape=jax.ShapeDtypeStruct(shape, jnp.float32),
        scratch_shapes=[pltpu.VMEM(shape, jnp.float32), pltpu.SemaphoreType.DMA((blocks // 2 + 1,))],
        compiler_params=params(),
        cost_estimate=cost(2.1),
        name="lag_products",
    )(*ys, table, after)


BATCH = 4


def own_kernel(lags_local, *refs):
    *part_refs, _, out_ref, line_ref, tail_ref, span_ref, late_ref, taps_a, lags_a, taps_b, lags_b = refs
    me = lax.axis_index("tm")
    part_rows = part_refs[0].shape[2]
    owners = sum(part_ref.shape[0] for part_ref in part_refs)
    samples = owners * part_rows * LANES
    steps = samples // BLOCK_LEN // BATCH
    total_rows = span_ref.shape[1]
    block_rows = BLOCK_LEN // LANES

    span_ref[...] = jnp.zeros_like(span_ref)
    e = 0
    for part_ref in part_refs:
        for i in range(part_ref.shape[0]):
            span_ref[:, pl.ds(EDGE + (me ^ e) * part_rows, part_rows), :] = part_ref[i]
            e += 1
    late_rows = (me * lags_local) // LANES
    late_lanes = lax.rem(me * lags_local, LANES)
    turned = [pltpu.roll(span_ref[c], late_lanes, 1) for c in range(2)]
    before = [pltpu.roll(x, 1, 0) for x in turned]
    lanes = lax.broadcasted_iota(jnp.int32, (total_rows, LANES), 1)
    for c in range(2):
        late_ref[c] = pltpu.roll(jnp.where(lanes < late_lanes, before[c], turned[c]), late_rows, 0)

    def line_of(ref, c, first, count):
        return jnp.concatenate([ref[c, pl.ds(first + n, 1), :] for n in range(count)], 1)

    def shifted(line, by):
        tiled = jnp.broadcast_to(line, (2 * SUBLANES, line.shape[1]))
        return pltpu.roll(tiled, by, 1, stride=1, stride_axis=0)[:, LANES:]

    def keep(ref, row, value):
        high, low = halves(value)
        half = ref.shape[0] // 2
        ref[row : row + 2 * SUBLANES, :] = high
        ref[half + row : half + row + 2 * SUBLANES, :] = low

    def build(n, taps_ref, lags_ref):
        first = EDGE - 1 + n * BATCH * block_rows
        count = BATCH * block_rows + 1
        lines = [line_of(span_ref, c, first, count) for c in range(2)]
        for c in range(2):
            for g in range(0, TAPS, 2 * SUBLANES):
                keep(taps_ref, c * TAPS + g, shifted(lines[c], g))
            late = line_of(late_ref, c, first, count)
            for g in range(0, lags_local, 2 * SUBLANES):
                keep(lags_ref, c * lags_local + g, shifted(late, g))
        pad = jnp.zeros((2 * SUBLANES - 2, BATCH * BLOCK_LEN), jnp.float32)
        keep(lags_ref, 2 * lags_local, jnp.concatenate([line[:, LANES:] for line in lines] + [pad], 0))

    turn = lane_sign((lags_local, LANES))

    def use(n, taps_ref, lags_ref):
        count = lags_ref.shape[0] // 2
        for b in range(BATCH):
            cols = slice(b * BLOCK_LEN, (b + 1) * BLOCK_LEN)
            product = dot_nt(lags_ref[:, cols], taps_ref[:, cols])
            product = product[:count, :LANES] + (product[:count, LANES:] + product[count:, :LANES])
            by_real = product[:lags_local]
            by_imag = product[lags_local : 2 * lags_local]
            rows = pl.ds(pl.multiple_of((n * BATCH + b) * lags_local, lags_local), lags_local)
            high, low = halves(by_real + turn * pltpu.roll(by_imag, TAPS, 1))
            out_ref[0, rows, :] = high
            out_ref[1, rows, :] = low
            line_ref[...] += product[2 * lags_local : 2 * lags_local + SUBLANES]

    line_ref[...] = jnp.zeros_like(line_ref)
    build(0, taps_a, lags_a)

    def pair(m, carry):
        build(2 * m + 1, taps_b, lags_b)
        use(2 * m, taps_a, lags_a)
        build(jnp.minimum(2 * m + 2, steps - 1), taps_a, lags_a)
        use(2 * m + 1, taps_b, lags_b)
        return carry

    lax.fori_loop(0, steps // 2, pair, 0)
    tail = []
    for c in range(2):
        line = line_of(span_ref, c, EDGE + owners * part_rows - 1, 2)
        tail += [shifted(line, g) for g in range(0, TAPS, 2 * SUBLANES)]
    tail = jnp.concatenate(tail, 0)
    tail_ref[...] = dot_nt(tail, tail, HIGHEST)


def own_call(parts, lags_local, after):
    part_rows = parts[0].shape[2]
    span_rows = part_rows * sum(part.shape[0] for part in parts)
    rows = span_rows * LANES // BLOCK_LEN * lags_local
    held_rows = -(-(span_rows + 2 * EDGE) // SUBLANES) * SUBLANES
    width = BATCH * BLOCK_LEN
    taps = pltpu.VMEM((4 * TAPS, width), jnp.bfloat16)
    lags = pltpu.VMEM((4 * lags_local + 4 * SUBLANES, width), jnp.bfloat16)
    span = pltpu.VMEM((2, held_rows, LANES), jnp.float32)
    return pl.pallas_call(
        functools.partial(own_kernel, lags_local),
        in_specs=[pl.BlockSpec(memory_space=pltpu.VMEM)] * len(parts) + [pl.BlockSpec(memory_space=pl.ANY)],
        out_shape=[
            jax.ShapeDtypeStruct((2, rows, 2 * TAPS), jnp.bfloat16),
            jax.ShapeDtypeStruct((SUBLANES, 2 * TAPS), jnp.float32),
            jax.ShapeDtypeStruct((2 * TAPS, 2 * TAPS), jnp.float32),
        ],
        scratch_shapes=[span, span, taps, lags, taps, lags],
        compiler_params=params(),
        cost_estimate=cost(6.2),
        name="reference_products",
    )(*parts, after)


def as_factor(a):
    return jnp.concatenate([a, -lane_sign(a.shape) * pltpu.roll(a, a.shape[0], 1)], 0)


def solver_kernel(line_ref, tail_ref, gram_ref, solver_ref):
    total = line_ref[...]
    line = total[0:1] + lane_sign((1, LANES)) * pltpu.roll(total[1:2], TAPS, 1)
    low = lax.broadcasted_iota(jnp.int32, (1, LANES), 1) < TAPS
    line_r = jnp.where(low, line, 0.0)
    line_i = jnp.where(low, pltpu.roll(line, TAPS, 1), 0.0)
    cols = lax.broadcasted_iota(jnp.int32, (TAPS, TAPS), 1)
    rows = lax.broadcasted_iota(jnp.int32, (TAPS, TAPS), 0)
    above = cols > rows

    def upper(x):
        spread = pltpu.roll(jnp.broadcast_to(x, (TAPS, LANES)), 0, 1, stride=1, stride_axis=0)
        return spread[:, :TAPS]

    up_r = upper(line_r)
    up_i = jnp.where(above, upper(line_i), 0.0)
    strict_r = jnp.where(above, up_r, 0.0)
    diag_r = jnp.where(cols == rows, up_r, 0.0)
    tails = tail_ref[...]
    gram_r = strict_r + strict_r.T + diag_r - (tails[:TAPS, :TAPS] + tails[TAPS:, TAPS:])
    gram_i = up_i - up_i.T - (tails[:TAPS, TAPS:] - tails[TAPS:, :TAPS])
    gram = jnp.concatenate([gram_r, gram_i], 1)
    gram_halves = halves(as_factor(gram))
    gram_ref[0], gram_ref[1] = gram_halves
    one = (
        lax.broadcasted_iota(jnp.int32, gram.shape, 0) == lax.broadcasted_iota(jnp.int32, gram.shape, 1)
    ).astype(jnp.float32)
    bound = jnp.max(jnp.sum(jnp.abs(gram), axis=1, keepdims=True), axis=0, keepdims=True)

    def again(state):
        count, left, _ = state
        return (count < 60) & (left > 1e-3)

    def newton(state):
        count, _, x = state
        x_halves = halves(x)
        seen = dot_split(x_halves, gram_halves)
        left = jnp.max(jnp.abs(seen - one))
        x = 2.0 * x - dot_split(halves(seen), halves(as_factor(x)))
        return count + 1, left, x

    start = (jnp.int32(0), jnp.float32(1.0), one * (1.0 / bound))
    _, _, inverse = lax.while_loop(again, newton, start)
    solver_ref[0], solver_ref[1] = halves(as_factor(inverse))


def solver_call(line, tail):
    out = jax.ShapeDtypeStruct((2,) + tail.shape, jnp.bfloat16)
    return pl.pallas_call(
        solver_kernel,
        out_shape=[out, out],
        compiler_params=params(),
        cost_estimate=cost(2.0),
        name="gram_inverse",
    )(line, tail)


def doppler_table(block_count, scale):
    phase = (np.arange(block_count)[:, None] * np.arange(DOPPLER)[None, :] % DOPPLER) * (2.0 * math.pi / DOPPLER)
    cosine, sine = np.cos(phase), np.sin(phase)
    upper = np.concatenate([cosine, -sine], 1)
    lower = np.concatenate([sine, cosine], 1)
    return (np.concatenate([upper, lower], 0) * scale).astype(np.float32)


def map_kernel(groups, got_ref, own_ref, gram_ref, solver_ref, wave_ref, out_hbm, held_ref, out_ref, out_sem):
    owners, pieces = got_ref.shape[:2]
    blocks = pieces - groups // 2
    lags_local = LANES // groups
    total = owners * blocks
    left = lax.broadcasted_iota(jnp.int32, (SUBLANES, LANES), 1) < TAPS
    sign = row_sign((SUBLANES, LANES))
    rows = [None] * groups
    for i in range(groups // 2):
        tile = got_ref[0, blocks + i]
        for owner in range(1, owners):
            tile = tile + got_ref[owner, blocks + i]
        swapped = pltpu.roll(tile, TAPS, 1)
        for part, here, there in ((i, tile, swapped), (i + groups // 2, swapped, tile)):
            other = -sign * pltpu.roll(there, SUBLANES // 2, 0)
            rows[part] = jnp.where(left, here, other)
    cross = jnp.concatenate(rows, 0)
    solver = (solver_ref[0], solver_ref[1])
    taps = dot_split(halves(cross), solver)
    rest = cross - dot_split(halves(taps), (gram_ref[0], gram_ref[1]))
    taps = taps + dot_split(halves(rest), solver)
    taps_high, taps_low = halves(taps)
    taps_both = jnp.concatenate([taps_high, taps_low], 1)
    for q in range(0, total, 2 * groups):
        own = slice(q * lags_local, (q + 2 * groups) * lags_local)
        own_high = own_ref[0, own, :]
        clutter = dot_nt(taps_both, jnp.concatenate([own_high, own_high], 1)) + dot_nt(taps_high, own_ref[1, own, :])
        for h in range(2):
            lanes = slice(h * LANES, (h + 1) * LANES)
            tiles = [clutter[r : r + SUBLANES, lanes] for r in range(0, groups * SUBLANES, SUBLANES)]
            for j, tile in enumerate(swap_groups(tiles, groups)):
                at = q + h * groups + j
                held_ref[at * SUBLANES : (at + 1) * SUBLANES, :] = got_ref[at // blocks, at % blocks] - tile
    half = SUBLANES // 2
    wave = (wave_ref[0], wave_ref[1])
    copies = []
    for g in range(half):
        parts = [held_ref[pl.ds(c * half + g, total, stride=SUBLANES), :] for c in range(2)]
        spectrum = dot_split(halves(jnp.concatenate(parts, 0).T), wave)
        for i in range(groups):
            beam = half * i + g
            for c in range(2):
                out_ref[beam, c] = spectrum[i * lags_local : (i + 1) * lags_local, c * DOPPLER : (c + 1) * DOPPLER]
            copies.append(pltpu.make_async_copy(out_ref.at[beam], out_hbm.at[beam], out_sem.at[beam]))
            copies[-1].start()
    for copy in copies:
        copy.wait()


def map_call(got, own, gram, solver, wave, groups, beams_local):
    total = got.shape[0] * (got.shape[1] - groups // 2)
    lags_local = LANES // groups
    shape = (beams_local, 2, lags_local, DOPPLER)
    return pl.pallas_call(
        functools.partial(map_kernel, groups),
        in_specs=[pl.BlockSpec(memory_space=pltpu.VMEM)] * 5,
        out_specs=pl.BlockSpec(memory_space=pltpu.HBM),
        out_shape=jax.ShapeDtypeStruct(shape, jnp.float32),
        scratch_shapes=[
            pltpu.VMEM((total * SUBLANES, LANES), jnp.float32),
            pltpu.VMEM(shape, jnp.float32),
            pltpu.SemaphoreType.DMA((beams_local,)),
        ],
        compiler_params=params(),
        cost_estimate=cost(2.5),
        name="range_doppler",
    )(got, own, gram, solver, wave)


def swap(x, axis, by):
    pairs = [(i, i ^ by) for i in range(lax.axis_size(axis))]
    return lax.ppermute(x, axis, pairs)


def tiled_device(ref_signal, surveillance, steering):
    chan_count, tm_count = lax.axis_size("chan"), lax.axis_size("tm")
    channels, length = surveillance.shape[1:]
    beams_local = steering.shape[1] // chan_count
    lags_local = LAGS // tm_count
    groups = LANES // lags_local
    samples = length * tm_count

    survey = surveillance.reshape(2 * channels, length)
    kept, moved, tiles, edge = beam_call(steering, survey, ref_signal, chan_count, beams_local)
    early = 1 if tm_count < 4 else 2
    edge = lax.ppermute(
        edge, "tm", [(i, i + 1) for i in range(tm_count - 1) if i ^ (i + 1) >= 1 << early]
    )
    near = swap(tiles[None], "tm", 1)
    shape = (chan_count // 2, 2 * beams_local, length)
    kept, got = kept.reshape(shape), swap(moved, "chan", 1).reshape(shape)
    by = 2
    while by < chan_count:
        kept, moved = sum_call([kept, got])
        got = swap(moved, "chan", by)
        by *= 2
    rounds = [near]
    joined = join_call(tiles[None], near, moved)
    while joined.shape[0] < tm_count:
        rounds.append(swap(joined, "tm", joined.shape[0]))
        if joined.shape[0] * 2 == tm_count:
            break
        joined = join_call(joined, rounds[-1])
    table = table_call(edge, tiles, rounds[:early])
    pieces = lag_call([kept[0], got[0]], table, joined, groups, tm_count)
    got = lax.all_to_all(pieces, "tm", 0, 0, tiled=True)
    own, line, tail = own_call([tiles[None]] + rounds, lags_local, pieces)
    gram, solver = solver_call(line, tail)
    wave = doppler_table(samples // BLOCK_LEN, 0.125 / math.sqrt(samples))
    high = wave.astype(jnp.bfloat16)
    wave = np.stack([high, (wave - high.astype(np.float32)).astype(jnp.bfloat16)])
    return map_call(got, own, gram, solver, jnp.asarray(wave), groups, beams_local)


def lag_table(ref_ext, offset, lags):
    window = lax.dynamic_slice_in_dim(ref_ext, offset, BLOCK_LEN + LAGS, 1)
    span = BLOCK_LEN + LAGS
    tiled = jnp.tile(jnp.pad(window, ((0, 0), (0, 1))), (1, lags))[:, : lags * span]
    return tiled.reshape(2, lags, span)[:, :, LAGS:]


def times_conj(a, b):
    real = jnp.einsum("...t,lt->...l", a[..., 0, :], b[0], precision=HIGHEST) + jnp.einsum(
        "...t,lt->...l", a[..., 1, :], b[1], precision=HIGHEST
    )
    imag = jnp.einsum("...t,lt->...l", a[..., 1, :], b[0], precision=HIGHEST) - jnp.einsum(
        "...t,lt->...l", a[..., 0, :], b[1], precision=HIGHEST
    )
    return jnp.stack([real, imag], -2)


def plain_device(ref_signal, surveillance, steering):
    chan_count, tm_count = lax.axis_size("chan"), lax.axis_size("tm")
    length = surveillance.shape[2]
    beams = steering.shape[1]
    lags_local = LAGS // tm_count
    samples = length * tm_count
    local_blocks = length // BLOCK_LEN
    here = lax.axis_index("tm")

    w_real, w_imag = steering
    real = jnp.dot(w_real, surveillance[0], precision=HIGHEST) - jnp.dot(w_imag, surveillance[1], precision=HIGHEST)
    imag = jnp.dot(w_imag, surveillance[0], precision=HIGHEST) + jnp.dot(w_real, surveillance[1], precision=HIGHEST)
    beam = lax.psum_scatter(jnp.stack([real, imag], 1), "chan", scatter_dimension=0, tiled=True)
    ref_all = lax.all_gather(ref_signal, "tm", axis=1, tiled=True)
    ref_ext = jnp.pad(ref_all, ((0, 0), (LAGS, 0)))

    def beam_step(carry, q):
        offset = q * BLOCK_LEN
        table = lag_table(ref_ext, here * length + offset, LAGS)
        segment = lax.dynamic_slice_in_dim(beam, offset, BLOCK_LEN, 2)
        return carry, times_conj(segment, table)

    _, products = lax.scan(beam_step, None, jnp.arange(local_blocks, dtype=jnp.int32))
    cross = lax.psum(products[..., :TAPS].sum(0), "tm")
    got = lax.all_to_all(products, "tm", 3, 0, tiled=True)

    def own_step(gram, q):
        offset = q * BLOCK_LEN
        table = lag_table(ref_ext, offset, LAGS)
        taps = table[:, :TAPS].transpose(1, 0, 2)
        mine = lax.dynamic_slice_in_dim(table, here * lags_local, lags_local, 1)
        return gram + times_conj(taps, table[:, :TAPS]), times_conj(taps, mine)

    start = jnp.zeros((TAPS, 2, TAPS), jnp.float32)
    gram, own = lax.scan(own_step, start, jnp.arange(samples // BLOCK_LEN, dtype=jnp.int32))
    g_real, g_imag = gram[:, 0].T, gram[:, 1].T
    system = jnp.concatenate([jnp.concatenate([g_real, -g_imag], 1), jnp.concatenate([g_imag, g_real], 1)], 0)
    right = jnp.concatenate([cross[:, 0].T, cross[:, 1].T], 0)
    solved = jax.scipy.linalg.cho_solve((jnp.linalg.cholesky(system), True), right)
    b_real, b_imag = solved[:TAPS].T, solved[TAPS:].T
    mixing = jnp.concatenate([jnp.stack([b_real, b_imag], 1), jnp.stack([-b_imag, b_real], 1)], 2)
    stacked = jnp.concatenate([own[:, :, 0], own[:, :, 1]], 1)
    lagged = got - jnp.einsum("mck,qkl->qmcl", mixing, stacked, precision=HIGHEST)
    wave = jnp.asarray(doppler_table(samples // BLOCK_LEN, 0.125 / math.sqrt(samples)))
    wave = wave.reshape(2, samples // BLOCK_LEN, 2, DOPPLER)
    return jnp.einsum("qmcl,cqdk->mdlk", lagged, wave, precision=HIGHEST)


def on_device(ref_signal, surveillance, steering):
    chan_count, tm_count = lax.axis_size("chan"), lax.axis_size("tm")
    beams_local = steering.shape[1] // chan_count
    lags_local = LAGS // tm_count
    fills = (
        LANES % lags_local == 0
        and lags_local % (2 * SUBLANES) == 0
        and beams_local * lags_local == LANES * SUBLANES // 2
        and chan_count > 1
        and chan_count & (chan_count - 1) == 0
        and tm_count > 1
        and tm_count & (tm_count - 1) == 0
        and 2 * surveillance.shape[1] % LANES == 0
        and surveillance.shape[2] % (2 * BATCH * BLOCK_LEN) == 0
    )
    device = tiled_device if fills else plain_device
    return device(ref_signal, surveillance, steering)


def solution(mesh):
    placed = (P(None, "tm"), P(None, "chan", "tm"), P(None, None, "chan"))
    return jax.shard_map(
        on_device,
        mesh=mesh,
        in_specs=placed,
        out_specs=P("chan", None, "tm", None),
        check_vma=False,
    )
```

```python
import functools
import math

import jax
import jax.numpy as jnp
import numpy as np
from jax import lax
from jax.experimental import pallas as pl
from jax.experimental.pallas import tpu as pltpu
from jax.sharding import PartitionSpec as P

LAGS = 256
DOPPLER = 256
TAPS = 64
BLOCK_LEN = 256
LANES = 128
SUBLANES = 8
EDGE = 2

HIGHEST = lax.Precision.HIGHEST
VMEM_BYTES = 48 * 1024 * 1024


def params():
    return pltpu.CompilerParams(vmem_limit_bytes=VMEM_BYTES)


def cost(us):
    return pl.CostEstimate(flops=int(us * 1.15e9), bytes_accessed=0, transcendentals=0)


def halves(x):
    high = x.astype(jnp.bfloat16)
    return high, (x - high.astype(jnp.float32)).astype(jnp.bfloat16)


def dot_nt(a, b, precision=None):
    return lax.dot_general(
        a, b, (((1,), (1,)), ((), ())), precision=precision, preferred_element_type=jnp.float32
    )


def dot_split(a, b):
    (a_high, a_low), (b_high, b_low) = a, b
    left = jnp.concatenate([a_high, a_low], 1)
    right = jnp.concatenate([b_high, b_high], 0)
    return jnp.dot(left, right, preferred_element_type=jnp.float32) + jnp.dot(
        a_high, b_low, preferred_element_type=jnp.float32
    )


def row_sign(shape):
    rows = lax.broadcasted_iota(jnp.int32, shape, 0)
    return jnp.where(rows % SUBLANES < SUBLANES // 2, 1.0, -1.0).astype(jnp.float32)


def lane_sign(shape):
    lanes = lax.broadcasted_iota(jnp.int32, shape, 1)
    return jnp.where(lanes % LANES < LANES // 2, 1.0, -1.0).astype(jnp.float32)


def swap_groups(rows, groups):
    width = LANES // groups
    lane_group = lax.broadcasted_iota(jnp.int32, rows[0].shape, 1) // width
    outs = []
    for j in range(groups):
        out = rows[j]
        for i in range(groups):
            if i != j:
                moved = pltpu.roll(rows[i], (width * (i - j)) % LANES, 1)
                out = jnp.where(lane_group == i, moved, out)
        outs.append(out)
    return outs


CHUNKS = 4


def beam_kernel(
    chan_count, beams_local, w_hbm, s_hbm, ref_hbm, kept_ref, sent_ref, tiles_ref,
    w_ref, s_ref, ref_ref, w_sem, s_sem, ref_sem,
):
    me = lax.axis_index("chan")
    length = s_hbm.shape[1]
    width = length // CHUNKS
    w_copy = pltpu.make_async_copy(w_hbm, w_ref, w_sem)
    w_copy.start()
    ref_copy = pltpu.make_async_copy(ref_hbm, ref_ref, ref_sem)
    ref_copy.start()
    s_copies = []
    for n in range(CHUNKS):
        cols = pl.ds(n * width, width)
        s_copies.append(pltpu.make_async_copy(s_hbm.at[:, cols], s_ref.at[:, cols], s_sem.at[n]))
        s_copies[n].start()
    half = SUBLANES // 2
    sub = lax.broadcasted_iota(jnp.int32, (SUBLANES, w_hbm.shape[2]), 0)
    top = sub < half
    w_copy.wait()
    rows = []
    for parity in range(2):
        for e in range(parity, chan_count, 2):
            base = (me ^ e) * beams_local
            for tile in range(beams_local // SUBLANES):
                start = pl.multiple_of(base + tile * SUBLANES, SUBLANES)
                wr = w_ref[0, pl.ds(start, SUBLANES), :]
                wi = w_ref[1, pl.ds(start, SUBLANES), :]
                wr_s = pltpu.roll(wr, half, 0)
                wi_s = pltpu.roll(wi, half, 0)
                first = [jnp.where(top, wr, wi_s), jnp.where(top, -wi, wr_s)]
                second = [jnp.where(top, wr_s, wi), jnp.where(top, -wi_s, wr)]
                rows.append(jnp.concatenate(first, 1))
                rows.append(jnp.concatenate(second, 1))
    weights = halves(jnp.concatenate(rows, 0))
    ref_copy.wait()
    for c in range(2):
        for n in range(tiles_ref.shape[1]):
            tiles_ref[c, n : n + 1, :] = ref_ref[c : c + 1, n * LANES : (n + 1) * LANES]
    mid = weights[0].shape[0] // 2
    for n in range(CHUNKS):
        cols = slice(n * width, (n + 1) * width)
        s_copies[n].wait()
        product = dot_split(weights, halves(s_ref[:, cols]))
        kept_ref[:, cols] = product[:mid]
        sent_ref[:, cols] = product[mid:]


def beam_call(steering, survey, ref, chan_count, beams_local):
    depth, length = survey.shape
    rows = chan_count * beams_local
    tiles = (2, length // LANES, LANES)
    out = jax.ShapeDtypeStruct((rows, length), jnp.float32)
    hbm, vmem = pl.BlockSpec(memory_space=pltpu.HBM), pl.BlockSpec(memory_space=pltpu.VMEM)
    return pl.pallas_call(
        functools.partial(beam_kernel, chan_count, beams_local),
        in_specs=[hbm] * 3,
        out_specs=[vmem] * 3,
        out_shape=[
            out,
            out,
            jax.ShapeDtypeStruct(tiles, jnp.float32),
        ],
        scratch_shapes=[
            pltpu.VMEM(steering.shape, jnp.float32),
            pltpu.VMEM(survey.shape, jnp.float32),
            pltpu.VMEM(ref.shape, jnp.float32),
            pltpu.SemaphoreType.DMA,
            pltpu.SemaphoreType.DMA((CHUNKS,)),
            pltpu.SemaphoreType.DMA,
        ],
        compiler_params=params(),
        cost_estimate=cost(2.2),
        name="beams",
    )(*(pltpu.with_memory_space_constraint(x, pltpu.HBM) for x in (steering, survey, ref)))


def sum_kernel(count, *refs):
    kept_ref, sent_ref = refs[-2:]
    for n in range(kept_ref.shape[0]):
        for offset, out_ref in ((0, kept_ref), (1, sent_ref)):
            total = refs[0][2 * n + offset]
            for ref in refs[1:count]:
                total = total + ref[2 * n + offset]
            out_ref[n] = total


def sum_call(parts):
    shape = (parts[0].shape[0] // 2,) + parts[0].shape[1:]
    out = jax.ShapeDtypeStruct(shape, jnp.float32)
    vmem = pl.BlockSpec(memory_space=pltpu.VMEM)
    return pl.pallas_call(
        functools.partial(sum_kernel, len(parts)),
        in_specs=[vmem] * len(parts),
        out_specs=[vmem, vmem],
        out_shape=[out, out],
        compiler_params=params(),
        cost_estimate=cost(0.1),
        name="halves_summed",
    )(*parts)


def join_kernel(first_ref, second_ref, *refs):
    out_ref = refs[-1]
    count = first_ref.shape[0]
    out_ref[:count] = first_ref[...]
    out_ref[count:] = second_ref[...]


def join_call(first, second, *after):
    vmem = pl.BlockSpec(memory_space=pltpu.VMEM)
    return pl.pallas_call(
        join_kernel,
        in_specs=[vmem, vmem] + [pl.BlockSpec(memory_space=pl.ANY)] * len(after),
        out_shape=jax.ShapeDtypeStruct((2 * first.shape[0],) + first.shape[1:], jnp.float32),
        compiler_params=params(),
        cost_estimate=cost(1.0),
        name="reference_joined",
    )(first, second, *after)


def edge_kernel(blocks_ref, out_ref):
    rows = blocks_ref.shape[2]
    out_ref[...] = jnp.zeros_like(out_ref)
    for c in range(2):
        out_ref[SUBLANES * c : SUBLANES * c + EDGE, :] = blocks_ref[0, c, rows - EDGE :, :]


def edge_call(blocks):
    return pl.pallas_call(
        edge_kernel,
        out_shape=jax.ShapeDtypeStruct((2 * SUBLANES, LANES), jnp.float32),
        compiler_params=params(),
        cost_estimate=cost(0.1),
        name="reference_edge",
    )(blocks)


def spread_line(line, keep):
    for g in range(0, LANES, 2 * SUBLANES):
        tiled = jnp.broadcast_to(line, (2 * SUBLANES, line.shape[1]))
        for h, value in enumerate(halves(pltpu.roll(tiled, g, 1, stride=1, stride_axis=0)[:, LANES:])):
            keep(h, g, value)


def table_kernel(tiles_ref, out_ref):
    for c in range(2):
        line = jnp.concatenate([tiles_ref[c, n : n + 1, :] for n in range(tiles_ref.shape[1])], 1)

        def keep(h, g, value):
            out_ref[h, c, g : g + 2 * SUBLANES] = value

        spread_line(line, keep)


def table_call(tiles):
    shape = (2, 2, LANES, LANES * (tiles.shape[1] - 1))
    return pl.pallas_call(
        table_kernel,
        out_shape=jax.ShapeDtypeStruct(shape, jnp.bfloat16),
        compiler_params=params(),
        cost_estimate=cost(0.7),
        name="shifted_reference",
    )(tiles)


def lag_kernel(groups, part_count, *refs):
    y_refs, refs = refs[:part_count], refs[part_count:]
    table_ref, edge_ref, tiles_ref, *round_refs, _, out_hbm, out_ref, out_sem, first_ref = refs
    copies = []

    me = lax.axis_index("tm")
    for c in range(2):
        before = edge_ref[SUBLANES * c : SUBLANES * c + EDGE, :]
        for n, round_ref in enumerate(round_refs):
            last = round_ref[round_ref.shape[0] - 1, c, round_ref.shape[2] - EDGE :, :]
            before = jnp.where((me > 0) & ((me ^ (me - 1)) == 2 ** (n + 1) - 1), last, before)
        line = jnp.concatenate([before[n : n + 1] for n in range(EDGE)] + [tiles_ref[c, 0:1, :]], 1)

        def keep(h, g, value):
            first_ref[h, c, g : g + 2 * SUBLANES] = value

        spread_line(line, keep)

    def tiles_at(h, c, start):
        known = first_ref.shape[3]
        if start >= known:
            return table_ref[h, c, :, start - known : start - known + BLOCK_LEN]
        if start + BLOCK_LEN <= known:
            return first_ref[h, c, :, start : start + BLOCK_LEN]
        rest = start + BLOCK_LEN - known
        return jnp.concatenate([first_ref[h, c, :, start:], table_ref[h, c, :, :rest]], 1)

    def send(start, count):
        part = (slice(None), pl.ds(start, count))
        copies.append(pltpu.make_async_copy(out_ref.at[part], out_hbm.at[part], out_sem.at[len(copies)]))
        copies[-1].start()

    y = y_refs[0][...]
    for y_ref in y_refs[1:]:
        y = y + y_ref[...]
    rows, length = y.shape
    blocks = length // BLOCK_LEN
    turned = jnp.concatenate(
        [pltpu.roll(y[r : r + SUBLANES], SUBLANES // 2, 0) for r in range(0, rows, SUBLANES)], 0
    )
    turned = turned * row_sign(turned.shape)
    y_high, y_low = halves(y)
    t_high, t_low = halves(turned)
    both = jnp.concatenate([y_high, y_low], 0)
    turned_both = jnp.concatenate([t_high, t_low], 0)
    taps_sum = None
    for q in range(blocks):
        cols = slice(q * BLOCK_LEN, (q + 1) * BLOCK_LEN)
        tables = []
        for h in range(2):
            rows_of = []
            for start in (q * BLOCK_LEN + LANES, q * BLOCK_LEN):
                rows_of.append(jnp.concatenate([tiles_at(h, c, start) for c in range(2)], 1))
            tables.append(jnp.concatenate(rows_of, 0))
        lhs = jnp.concatenate([both[:, cols], turned_both[:, cols]], 1)
        by_high = dot_nt(lhs, tables[0])
        by_low = dot_nt(lhs[:rows], tables[1])
        product = by_high[:rows] + (by_high[rows:] + by_low)
        taps = product[:, :LANES]
        taps_sum = taps if taps_sum is None else taps_sum + taps
        for h in range(LAGS // LANES):
            lanes = slice(h * LANES, (h + 1) * LANES)
            tiles = [product[r : r + SUBLANES, lanes] for r in range(0, rows, SUBLANES)]
            for j, tile in enumerate(swap_groups(tiles, groups)):
                out_ref[h * groups + j, q] = tile
        if q % 2:
            send(q - 1, 2)
    left = lax.broadcasted_iota(jnp.int32, (SUBLANES, LANES), 1) < TAPS
    for i in range(groups // 2):
        a = taps_sum[i * SUBLANES : (i + 1) * SUBLANES]
        other = i + groups // 2
        b = taps_sum[other * SUBLANES : (other + 1) * SUBLANES]
        tile = jnp.where(left, a, pltpu.roll(b, LANES - TAPS, 1))
        for owner in range(out_ref.shape[0]):
            out_ref[owner, blocks + i] = tile
    send(blocks, groups // 2)
    for copy in copies:
        copy.wait()


def lag_call(ys, table, edge, tiles, rounds, after, groups, owners):
    blocks = ys[0].shape[1] // BLOCK_LEN
    shape = (owners, blocks + groups // 2, SUBLANES, LANES)
    vmem = pl.BlockSpec(memory_space=pltpu.VMEM)
    return pl.pallas_call(
        functools.partial(lag_kernel, groups, len(ys)),
        in_specs=[vmem] * (len(ys) + 3 + len(rounds)) + [pl.BlockSpec(memory_space=pl.ANY)],
        out_specs=pl.BlockSpec(memory_space=pltpu.HBM),
        out_shape=jax.ShapeDtypeStruct(shape, jnp.float32),
        scratch_shapes=[
            pltpu.VMEM(shape, jnp.float32),
            pltpu.SemaphoreType.DMA((blocks // 2 + 1,)),
            pltpu.VMEM((2, 2, LANES, 2 * LANES), jnp.bfloat16),
        ],
        compiler_params=params(),
        cost_estimate=cost(2.1),
        name="lag_products",
    )(*ys, table, edge, tiles, *rounds, after)


BATCH = 4


def own_kernel(lags_local, *refs):
    *part_refs, _, out_ref, line_ref, tail_ref, span_ref, late_ref, taps_a, lags_a, taps_b, lags_b = refs
    me = lax.axis_index("tm")
    part_rows = part_refs[0].shape[2]
    owners = sum(part_ref.shape[0] for part_ref in part_refs)
    samples = owners * part_rows * LANES
    steps = samples // BLOCK_LEN // BATCH
    total_rows = span_ref.shape[1]
    block_rows = BLOCK_LEN // LANES

    span_ref[...] = jnp.zeros_like(span_ref)
    e = 0
    for part_ref in part_refs:
        for i in range(part_ref.shape[0]):
            span_ref[:, pl.ds(EDGE + (me ^ e) * part_rows, part_rows), :] = part_ref[i]
            e += 1
    late_rows = (me * lags_local) // LANES
    late_lanes = lax.rem(me * lags_local, LANES)
    turned = [pltpu.roll(span_ref[c], late_lanes, 1) for c in range(2)]
    before = [pltpu.roll(x, 1, 0) for x in turned]
    lanes = lax.broadcasted_iota(jnp.int32, (total_rows, LANES), 1)
    for c in range(2):
        late_ref[c] = pltpu.roll(jnp.where(lanes < late_lanes, before[c], turned[c]), late_rows, 0)

    def line_of(ref, c, first, count):
        return jnp.concatenate([ref[c, pl.ds(first + n, 1), :] for n in range(count)], 1)

    def shifted(line, by):
        tiled = jnp.broadcast_to(line, (2 * SUBLANES, line.shape[1]))
        return pltpu.roll(tiled, by, 1, stride=1, stride_axis=0)[:, LANES:]

    def keep(ref, row, value):
        high, low = halves(value)
        half = ref.shape[0] // 2
        ref[row : row + 2 * SUBLANES, :] = high
        ref[half + row : half + row + 2 * SUBLANES, :] = low

    def build(n, taps_ref, lags_ref):
        first = EDGE - 1 + n * BATCH * block_rows
        count = BATCH * block_rows + 1
        lines = [line_of(span_ref, c, first, count) for c in range(2)]
        for c in range(2):
            for g in range(0, TAPS, 2 * SUBLANES):
                keep(taps_ref, c * TAPS + g, shifted(lines[c], g))
            late = line_of(late_ref, c, first, count)
            for g in range(0, lags_local, 2 * SUBLANES):
                keep(lags_ref, c * lags_local + g, shifted(late, g))
        pad = jnp.zeros((2 * SUBLANES - 2, BATCH * BLOCK_LEN), jnp.float32)
        keep(lags_ref, 2 * lags_local, jnp.concatenate([line[:, LANES:] for line in lines] + [pad], 0))

    turn = lane_sign((lags_local, LANES))

    def use(n, taps_ref, lags_ref):
        count = lags_ref.shape[0] // 2
        for b in range(BATCH):
            cols = slice(b * BLOCK_LEN, (b + 1) * BLOCK_LEN)
            product = dot_nt(lags_ref[:, cols], taps_ref[:, cols])
            product = product[:count, :LANES] + (product[:count, LANES:] + product[count:, :LANES])
            by_real = product[:lags_local]
            by_imag = product[lags_local : 2 * lags_local]
            rows = pl.ds(pl.multiple_of((n * BATCH + b) * lags_local, lags_local), lags_local)
            high, low = halves(by_real + turn * pltpu.roll(by_imag, TAPS, 1))
            out_ref[0, rows, :] = high
            out_ref[1, rows, :] = low
            line_ref[...] += product[2 * lags_local : 2 * lags_local + SUBLANES]

    line_ref[...] = jnp.zeros_like(line_ref)
    build(0, taps_a, lags_a)

    def pair(m, carry):
        build(2 * m + 1, taps_b, lags_b)
        use(2 * m, taps_a, lags_a)
        build(jnp.minimum(2 * m + 2, steps - 1), taps_a, lags_a)
        use(2 * m + 1, taps_b, lags_b)
        return carry

    lax.fori_loop(0, steps // 2, pair, 0)
    tail = []
    for c in range(2):
        line = line_of(span_ref, c, EDGE + owners * part_rows - 1, 2)
        tail += [shifted(line, g) for g in range(0, TAPS, 2 * SUBLANES)]
    tail = jnp.concatenate(tail, 0)
    tail_ref[...] = dot_nt(tail, tail, HIGHEST)


def own_call(parts, lags_local, after):
    part_rows = parts[0].shape[2]
    span_rows = part_rows * sum(part.shape[0] for part in parts)
    rows = span_rows * LANES // BLOCK_LEN * lags_local
    held_rows = -(-(span_rows + 2 * EDGE) // SUBLANES) * SUBLANES
    width = BATCH * BLOCK_LEN
    taps = pltpu.VMEM((4 * TAPS, width), jnp.bfloat16)
    lags = pltpu.VMEM((4 * lags_local + 4 * SUBLANES, width), jnp.bfloat16)
    span = pltpu.VMEM((2, held_rows, LANES), jnp.float32)
    return pl.pallas_call(
        functools.partial(own_kernel, lags_local),
        in_specs=[pl.BlockSpec(memory_space=pltpu.VMEM)] * len(parts) + [pl.BlockSpec(memory_space=pl.ANY)],
        out_shape=[
            jax.ShapeDtypeStruct((2, rows, 2 * TAPS), jnp.bfloat16),
            jax.ShapeDtypeStruct((SUBLANES, 2 * TAPS), jnp.float32),
            jax.ShapeDtypeStruct((2 * TAPS, 2 * TAPS), jnp.float32),
        ],
        scratch_shapes=[span, span, taps, lags, taps, lags],
        compiler_params=params(),
        cost_estimate=cost(6.2),
        name="reference_products",
    )(*parts, after)


def as_factor(a):
    return jnp.concatenate([a, -lane_sign(a.shape) * pltpu.roll(a, a.shape[0], 1)], 0)


def solver_kernel(line_ref, tail_ref, gram_ref, solver_ref):
    total = line_ref[...]
    line = total[0:1] + lane_sign((1, LANES)) * pltpu.roll(total[1:2], TAPS, 1)
    low = lax.broadcasted_iota(jnp.int32, (1, LANES), 1) < TAPS
    line_r = jnp.where(low, line, 0.0)
    line_i = jnp.where(low, pltpu.roll(line, TAPS, 1), 0.0)
    cols = lax.broadcasted_iota(jnp.int32, (TAPS, TAPS), 1)
    rows = lax.broadcasted_iota(jnp.int32, (TAPS, TAPS), 0)
    above = cols > rows

    def upper(x):
        spread = pltpu.roll(jnp.broadcast_to(x, (TAPS, LANES)), 0, 1, stride=1, stride_axis=0)
        return spread[:, :TAPS]

    up_r = upper(line_r)
    up_i = jnp.where(above, upper(line_i), 0.0)
    strict_r = jnp.where(above, up_r, 0.0)
    diag_r = jnp.where(cols == rows, up_r, 0.0)
    tails = tail_ref[...]
    gram_r = strict_r + strict_r.T + diag_r - (tails[:TAPS, :TAPS] + tails[TAPS:, TAPS:])
    gram_i = up_i - up_i.T - (tails[:TAPS, TAPS:] - tails[TAPS:, :TAPS])
    gram = jnp.concatenate([gram_r, gram_i], 1)
    gram_halves = halves(as_factor(gram))
    gram_ref[0], gram_ref[1] = gram_halves
    one = (
        lax.broadcasted_iota(jnp.int32, gram.shape, 0) == lax.broadcasted_iota(jnp.int32, gram.shape, 1)
    ).astype(jnp.float32)
    bound = jnp.max(jnp.sum(jnp.abs(gram), axis=1, keepdims=True), axis=0, keepdims=True)

    def again(state):
        count, left, _ = state
        return (count < 60) & (left > 1e-3)

    def newton(state):
        count, _, x = state
        x_halves = halves(x)
        seen = dot_split(x_halves, gram_halves)
        left = jnp.max(jnp.abs(seen - one))
        x = 2.0 * x - dot_split(halves(seen), halves(as_factor(x)))
        return count + 1, left, x

    start = (jnp.int32(0), jnp.float32(1.0), one * (1.0 / bound))
    _, _, inverse = lax.while_loop(again, newton, start)
    solver_ref[0], solver_ref[1] = halves(as_factor(inverse))


def solver_call(line, tail):
    out = jax.ShapeDtypeStruct((2,) + tail.shape, jnp.bfloat16)
    return pl.pallas_call(
        solver_kernel,
        out_shape=[out, out],
        compiler_params=params(),
        cost_estimate=cost(2.0),
        name="gram_inverse",
    )(line, tail)


def doppler_table(block_count, scale):
    phase = (np.arange(block_count)[:, None] * np.arange(DOPPLER)[None, :] % DOPPLER) * (2.0 * math.pi / DOPPLER)
    cosine, sine = np.cos(phase), np.sin(phase)
    upper = np.concatenate([cosine, -sine], 1)
    lower = np.concatenate([sine, cosine], 1)
    return (np.concatenate([upper, lower], 0) * scale).astype(np.float32)


def map_kernel(groups, got_ref, own_ref, gram_ref, solver_ref, wave_ref, out_hbm, held_ref, out_ref, out_sem):
    owners, pieces = got_ref.shape[:2]
    blocks = pieces - groups // 2
    lags_local = LANES // groups
    total = owners * blocks
    left = lax.broadcasted_iota(jnp.int32, (SUBLANES, LANES), 1) < TAPS
    sign = row_sign((SUBLANES, LANES))
    rows = [None] * groups
    for i in range(groups // 2):
        tile = got_ref[0, blocks + i]
        for owner in range(1, owners):
            tile = tile + got_ref[owner, blocks + i]
        swapped = pltpu.roll(tile, TAPS, 1)
        for part, here, there in ((i, tile, swapped), (i + groups // 2, swapped, tile)):
            other = -sign * pltpu.roll(there, SUBLANES // 2, 0)
            rows[part] = jnp.where(left, here, other)
    cross = jnp.concatenate(rows, 0)
    solver = (solver_ref[0], solver_ref[1])
    taps = dot_split(halves(cross), solver)
    rest = cross - dot_split(halves(taps), (gram_ref[0], gram_ref[1]))
    taps = taps + dot_split(halves(rest), solver)
    taps_high, taps_low = halves(taps)
    taps_both = jnp.concatenate([taps_high, taps_low], 1)
    for q in range(0, total, 2 * groups):
        own = slice(q * lags_local, (q + 2 * groups) * lags_local)
        own_high = own_ref[0, own, :]
        clutter = dot_nt(taps_both, jnp.concatenate([own_high, own_high], 1)) + dot_nt(taps_high, own_ref[1, own, :])
        for h in range(2):
            lanes = slice(h * LANES, (h + 1) * LANES)
            tiles = [clutter[r : r + SUBLANES, lanes] for r in range(0, groups * SUBLANES, SUBLANES)]
            for j, tile in enumerate(swap_groups(tiles, groups)):
                at = q + h * groups + j
                held_ref[at * SUBLANES : (at + 1) * SUBLANES, :] = got_ref[at // blocks, at % blocks] - tile
    half = SUBLANES // 2
    wave = (wave_ref[0], wave_ref[1])
    copies = []
    for first in range(0, half, 2):
        lagged = []
        for g in (first, first + 1):
            parts = [held_ref[pl.ds(c * half + g, total, stride=SUBLANES), :] for c in range(2)]
            lagged.append(jnp.concatenate(parts, 0).T)
        spectrum = dot_split(halves(jnp.concatenate(lagged, 0)), wave)
        for n in range(2 * groups):
            beam = half * (n % groups) + first + n // groups
            for c in range(2):
                out_ref[beam, c] = spectrum[n * lags_local : (n + 1) * lags_local, c * DOPPLER : (c + 1) * DOPPLER]
            copies.append(pltpu.make_async_copy(out_ref.at[beam], out_hbm.at[beam], out_sem.at[beam]))
            copies[-1].start()
    for copy in copies:
        copy.wait()


def map_call(got, own, gram, solver, wave, groups, beams_local):
    total = got.shape[0] * (got.shape[1] - groups // 2)
    lags_local = LANES // groups
    shape = (beams_local, 2, lags_local, DOPPLER)
    return pl.pallas_call(
        functools.partial(map_kernel, groups),
        in_specs=[pl.BlockSpec(memory_space=pltpu.VMEM)] * 5,
        out_specs=pl.BlockSpec(memory_space=pltpu.HBM),
        out_shape=jax.ShapeDtypeStruct(shape, jnp.float32),
        scratch_shapes=[
            pltpu.VMEM((total * SUBLANES, LANES), jnp.float32),
            pltpu.VMEM(shape, jnp.float32),
            pltpu.SemaphoreType.DMA((beams_local,)),
        ],
        compiler_params=params(),
        cost_estimate=cost(2.5),
        name="range_doppler",
    )(got, own, gram, solver, wave)


def swap(x, axis, by):
    pairs = [(i, i ^ by) for i in range(lax.axis_size(axis))]
    return lax.ppermute(x, axis, pairs)


def tiled_device(ref_signal, surveillance, steering):
    chan_count, tm_count = lax.axis_size("chan"), lax.axis_size("tm")
    channels, length = surveillance.shape[1:]
    beams_local = steering.shape[1] // chan_count
    lags_local = LAGS // tm_count
    groups = LANES // lags_local
    samples = length * tm_count

    survey = surveillance.reshape(2 * channels, length)
    kept, moved, tiles = beam_call(steering, survey, ref_signal, chan_count, beams_local)
    near = swap(tiles[None], "tm", 1)
    shape = (chan_count // 2, 2 * beams_local, length)
    kept, got = kept.reshape(shape), swap(moved, "chan", 1).reshape(shape)
    by = 2
    while by < chan_count:
        kept, moved = sum_call([kept, got])
        got = swap(moved, "chan", by)
        by *= 2
    rounds = [near]
    joined = join_call(tiles[None], near, moved)
    early = 1 if tm_count < 4 else 2
    edge = lax.ppermute(
        edge_call(joined), "tm", [(i, i + 1) for i in range(tm_count - 1) if i ^ (i + 1) >= 1 << early]
    )
    while joined.shape[0] < tm_count:
        rounds.append(swap(joined, "tm", joined.shape[0]))
        if joined.shape[0] * 2 == tm_count:
            break
        joined = join_call(joined, rounds[-1])
    table = table_call(tiles)
    pieces = lag_call([kept[0], got[0]], table, edge, tiles, rounds[:early], joined, groups, tm_count)
    got = lax.all_to_all(pieces, "tm", 0, 0, tiled=True)
    own, line, tail = own_call([tiles[None]] + rounds, lags_local, pieces)
    gram, solver = solver_call(line, tail)
    wave = doppler_table(samples // BLOCK_LEN, 0.125 / math.sqrt(samples))
    high = wave.astype(jnp.bfloat16)
    wave = np.stack([high, (wave - high.astype(np.float32)).astype(jnp.bfloat16)])
    return map_call(got, own, gram, solver, jnp.asarray(wave), groups, beams_local)


def lag_table(ref_ext, offset, lags):
    window = lax.dynamic_slice_in_dim(ref_ext, offset, BLOCK_LEN + LAGS, 1)
    span = BLOCK_LEN + LAGS
    tiled = jnp.tile(jnp.pad(window, ((0, 0), (0, 1))), (1, lags))[:, : lags * span]
    return tiled.reshape(2, lags, span)[:, :, LAGS:]


def times_conj(a, b):
    real = jnp.einsum("...t,lt->...l", a[..., 0, :], b[0], precision=HIGHEST) + jnp.einsum(
        "...t,lt->...l", a[..., 1, :], b[1], precision=HIGHEST
    )
    imag = jnp.einsum("...t,lt->...l", a[..., 1, :], b[0], precision=HIGHEST) - jnp.einsum(
        "...t,lt->...l", a[..., 0, :], b[1], precision=HIGHEST
    )
    return jnp.stack([real, imag], -2)


def plain_device(ref_signal, surveillance, steering):
    chan_count, tm_count = lax.axis_size("chan"), lax.axis_size("tm")
    length = surveillance.shape[2]
    beams = steering.shape[1]
    lags_local = LAGS // tm_count
    samples = length * tm_count
    local_blocks = length // BLOCK_LEN
    here = lax.axis_index("tm")

    w_real, w_imag = steering
    real = jnp.dot(w_real, surveillance[0], precision=HIGHEST) - jnp.dot(w_imag, surveillance[1], precision=HIGHEST)
    imag = jnp.dot(w_imag, surveillance[0], precision=HIGHEST) + jnp.dot(w_real, surveillance[1], precision=HIGHEST)
    beam = lax.psum_scatter(jnp.stack([real, imag], 1), "chan", scatter_dimension=0, tiled=True)
    ref_all = lax.all_gather(ref_signal, "tm", axis=1, tiled=True)
    ref_ext = jnp.pad(ref_all, ((0, 0), (LAGS, 0)))

    def beam_step(carry, q):
        offset = q * BLOCK_LEN
        table = lag_table(ref_ext, here * length + offset, LAGS)
        segment = lax.dynamic_slice_in_dim(beam, offset, BLOCK_LEN, 2)
        return carry, times_conj(segment, table)

    _, products = lax.scan(beam_step, None, jnp.arange(local_blocks, dtype=jnp.int32))
    cross = lax.psum(products[..., :TAPS].sum(0), "tm")
    got = lax.all_to_all(products, "tm", 3, 0, tiled=True)

    def own_step(gram, q):
        offset = q * BLOCK_LEN
        table = lag_table(ref_ext, offset, LAGS)
        taps = table[:, :TAPS].transpose(1, 0, 2)
        mine = lax.dynamic_slice_in_dim(table, here * lags_local, lags_local, 1)
        return gram + times_conj(taps, table[:, :TAPS]), times_conj(taps, mine)

    start = jnp.zeros((TAPS, 2, TAPS), jnp.float32)
    gram, own = lax.scan(own_step, start, jnp.arange(samples // BLOCK_LEN, dtype=jnp.int32))
    g_real, g_imag = gram[:, 0].T, gram[:, 1].T
    system = jnp.concatenate([jnp.concatenate([g_real, -g_imag], 1), jnp.concatenate([g_imag, g_real], 1)], 0)
    right = jnp.concatenate([cross[:, 0].T, cross[:, 1].T], 0)
    solved = jax.scipy.linalg.cho_solve((jnp.linalg.cholesky(system), True), right)
    b_real, b_imag = solved[:TAPS].T, solved[TAPS:].T
    mixing = jnp.concatenate([jnp.stack([b_real, b_imag], 1), jnp.stack([-b_imag, b_real], 1)], 2)
    stacked = jnp.concatenate([own[:, :, 0], own[:, :, 1]], 1)
    lagged = got - jnp.einsum("mck,qkl->qmcl", mixing, stacked, precision=HIGHEST)
    wave = jnp.asarray(doppler_table(samples // BLOCK_LEN, 0.125 / math.sqrt(samples)))
    wave = wave.reshape(2, samples // BLOCK_LEN, 2, DOPPLER)
    return jnp.einsum("qmcl,cqdk->mdlk", lagged, wave, precision=HIGHEST)


def on_device(ref_signal, surveillance, steering):
    chan_count, tm_count = lax.axis_size("chan"), lax.axis_size("tm")
    beams_local = steering.shape[1] // chan_count
    lags_local = LAGS // tm_count
    fills = (
        LANES % lags_local == 0
        and lags_local % (2 * SUBLANES) == 0
        and beams_local * lags_local == LANES * SUBLANES // 2
        and chan_count > 1
        and chan_count & (chan_count - 1) == 0
        and tm_count > 1
        and tm_count & (tm_count - 1) == 0
        and 2 * surveillance.shape[1] % LANES == 0
        and surveillance.shape[2] % (2 * BATCH * BLOCK_LEN) == 0
    )
    device = tiled_device if fills else plain_device
    return device(ref_signal, surveillance, steering)


def solution(mesh):
    placed = (P(None, "tm"), P(None, "chan", "tm"), P(None, None, "chan"))
    return jax.shard_map(
        on_device,
        mesh=mesh,
        in_specs=placed,
        out_specs=P("chan", None, "tm", None),
        check_vma=False,
    )
```

```python
import functools
import math

import jax
import jax.numpy as jnp
import numpy as np
from jax import lax
from jax.experimental import pallas as pl
from jax.experimental.pallas import tpu as pltpu
from jax.sharding import PartitionSpec as P

LAGS = 256
DOPPLER = 256
TAPS = 64
BLOCK_LEN = 256
LANES = 128
SUBLANES = 8
EDGE = 2

HIGHEST = lax.Precision.HIGHEST
VMEM_BYTES = 48 * 1024 * 1024


def params():
    return pltpu.CompilerParams(vmem_limit_bytes=VMEM_BYTES)


def cost(us):
    return pl.CostEstimate(flops=int(us * 1.15e9), bytes_accessed=0, transcendentals=0)


def halves(x):
    high = x.astype(jnp.bfloat16)
    return high, (x - high.astype(jnp.float32)).astype(jnp.bfloat16)


def dot_nt(a, b, precision=None):
    return lax.dot_general(
        a, b, (((1,), (1,)), ((), ())), precision=precision, preferred_element_type=jnp.float32
    )


def dot_split(a, b):
    (a_high, a_low), (b_high, b_low) = a, b
    left = jnp.concatenate([a_high, a_low], 1)
    right = jnp.concatenate([b_high, b_high], 0)
    return jnp.dot(left, right, preferred_element_type=jnp.float32) + jnp.dot(
        a_high, b_low, preferred_element_type=jnp.float32
    )


def row_sign(shape):
    rows = lax.broadcasted_iota(jnp.int32, shape, 0)
    return jnp.where(rows % SUBLANES < SUBLANES // 2, 1.0, -1.0).astype(jnp.float32)


def lane_sign(shape):
    lanes = lax.broadcasted_iota(jnp.int32, shape, 1)
    return jnp.where(lanes % LANES < LANES // 2, 1.0, -1.0).astype(jnp.float32)


def swap_groups(rows, groups):
    width = LANES // groups
    lane_group = lax.broadcasted_iota(jnp.int32, rows[0].shape, 1) // width
    outs = []
    for j in range(groups):
        out = rows[j]
        for i in range(groups):
            if i != j:
                moved = pltpu.roll(rows[i], (width * (i - j)) % LANES, 1)
                out = jnp.where(lane_group == i, moved, out)
        outs.append(out)
    return outs


CHUNKS = 4


def beam_kernel(
    chan_count, beams_local, w_hbm, s_hbm, ref_hbm, kept_ref, sent_ref, tiles_ref,
    w_ref, s_ref, ref_ref, w_sem, s_sem, ref_sem,
):
    me = lax.axis_index("chan")
    length = s_hbm.shape[1]
    width = length // CHUNKS
    w_copy = pltpu.make_async_copy(w_hbm, w_ref, w_sem)
    w_copy.start()
    ref_copy = pltpu.make_async_copy(ref_hbm, ref_ref, ref_sem)
    ref_copy.start()
    s_copies = []
    for n in range(CHUNKS):
        cols = pl.ds(n * width, width)
        s_copies.append(pltpu.make_async_copy(s_hbm.at[:, cols], s_ref.at[:, cols], s_sem.at[n]))
        s_copies[n].start()
    half = SUBLANES // 2
    sub = lax.broadcasted_iota(jnp.int32, (SUBLANES, w_hbm.shape[2]), 0)
    top = sub < half
    w_copy.wait()
    rows = []
    for parity in range(2):
        for e in range(parity, chan_count, 2):
            base = (me ^ e) * beams_local
            for tile in range(beams_local // SUBLANES):
                start = pl.multiple_of(base + tile * SUBLANES, SUBLANES)
                wr = w_ref[0, pl.ds(start, SUBLANES), :]
                wi = w_ref[1, pl.ds(start, SUBLANES), :]
                wr_s = pltpu.roll(wr, half, 0)
                wi_s = pltpu.roll(wi, half, 0)
                first = [jnp.where(top, wr, wi_s), jnp.where(top, -wi, wr_s)]
                second = [jnp.where(top, wr_s, wi), jnp.where(top, -wi_s, wr)]
                rows.append(jnp.concatenate(first, 1))
                rows.append(jnp.concatenate(second, 1))
    weights = halves(jnp.concatenate(rows, 0))
    ref_copy.wait()
    for c in range(2):
        for n in range(tiles_ref.shape[1]):
            tiles_ref[c, n : n + 1, :] = ref_ref[c : c + 1, n * LANES : (n + 1) * LANES]
    mid = weights[0].shape[0] // 2
    for n in range(CHUNKS):
        cols = slice(n * width, (n + 1) * width)
        s_copies[n].wait()
        product = dot_split(weights, halves(s_ref[:, cols]))
        kept_ref[:, cols] = product[:mid]
        sent_ref[:, cols] = product[mid:]


def beam_call(steering, survey, ref, chan_count, beams_local):
    depth, length = survey.shape
    rows = chan_count * beams_local
    tiles = (2, length // LANES, LANES)
    out = jax.ShapeDtypeStruct((rows, length), jnp.float32)
    hbm, vmem = pl.BlockSpec(memory_space=pltpu.HBM), pl.BlockSpec(memory_space=pltpu.VMEM)
    return pl.pallas_call(
        functools.partial(beam_kernel, chan_count, beams_local),
        in_specs=[hbm] * 3,
        out_specs=[vmem] * 3,
        out_shape=[
            out,
            out,
            jax.ShapeDtypeStruct(tiles, jnp.float32),
        ],
        scratch_shapes=[
            pltpu.VMEM(steering.shape, jnp.float32),
            pltpu.VMEM(survey.shape, jnp.float32),
            pltpu.VMEM(ref.shape, jnp.float32),
            pltpu.SemaphoreType.DMA,
            pltpu.SemaphoreType.DMA((CHUNKS,)),
            pltpu.SemaphoreType.DMA,
        ],
        compiler_params=params(),
        cost_estimate=cost(2.2),
        name="beams",
    )(*(pltpu.with_memory_space_constraint(x, pltpu.HBM) for x in (steering, survey, ref)))


def sum_kernel(count, *refs):
    kept_ref, sent_ref = refs[-2:]
    for n in range(kept_ref.shape[0]):
        for offset, out_ref in ((0, kept_ref), (1, sent_ref)):
            total = refs[0][2 * n + offset]
            for ref in refs[1:count]:
                total = total + ref[2 * n + offset]
            out_ref[n] = total


def sum_call(parts):
    shape = (parts[0].shape[0] // 2,) + parts[0].shape[1:]
    out = jax.ShapeDtypeStruct(shape, jnp.float32)
    vmem = pl.BlockSpec(memory_space=pltpu.VMEM)
    return pl.pallas_call(
        functools.partial(sum_kernel, len(parts)),
        in_specs=[vmem] * len(parts),
        out_specs=[vmem, vmem],
        out_shape=[out, out],
        compiler_params=params(),
        cost_estimate=cost(0.1),
        name="halves_summed",
    )(*parts)


def join_kernel(first_ref, second_ref, *refs):
    out_ref = refs[-1]
    count = first_ref.shape[0]
    out_ref[:count] = first_ref[...]
    out_ref[count:] = second_ref[...]


def join_call(first, second, *after):
    vmem = pl.BlockSpec(memory_space=pltpu.VMEM)
    return pl.pallas_call(
        join_kernel,
        in_specs=[vmem, vmem] + [pl.BlockSpec(memory_space=pl.ANY)] * len(after),
        out_shape=jax.ShapeDtypeStruct((2 * first.shape[0],) + first.shape[1:], jnp.float32),
        compiler_params=params(),
        cost_estimate=cost(1.0),
        name="reference_joined",
    )(first, second, *after)


def edge_kernel(blocks_ref, out_ref):
    rows = blocks_ref.shape[2]
    out_ref[...] = jnp.zeros_like(out_ref)
    for c in range(2):
        out_ref[SUBLANES * c : SUBLANES * c + EDGE, :] = blocks_ref[0, c, rows - EDGE :, :]


def edge_call(blocks):
    return pl.pallas_call(
        edge_kernel,
        out_shape=jax.ShapeDtypeStruct((2 * SUBLANES, LANES), jnp.float32),
        compiler_params=params(),
        cost_estimate=cost(0.1),
        name="reference_edge",
    )(blocks)


def spread_line(line, keep):
    for g in range(0, LANES, 2 * SUBLANES):
        tiled = jnp.broadcast_to(line, (2 * SUBLANES, line.shape[1]))
        for h, value in enumerate(halves(pltpu.roll(tiled, g, 1, stride=1, stride_axis=0)[:, LANES:])):
            keep(h, g, value)


def table_kernel(tiles_ref, out_ref):
    for c in range(2):
        line = jnp.concatenate([tiles_ref[c, n : n + 1, :] for n in range(tiles_ref.shape[1])], 1)

        def keep(h, g, value):
            out_ref[h, c, g : g + 2 * SUBLANES] = value

        spread_line(line, keep)


def table_call(tiles):
    shape = (2, 2, LANES, LANES * (tiles.shape[1] - 1))
    return pl.pallas_call(
        table_kernel,
        out_shape=jax.ShapeDtypeStruct(shape, jnp.bfloat16),
        compiler_params=params(),
        cost_estimate=cost(0.7),
        name="shifted_reference",
    )(tiles)


def lag_kernel(groups, part_count, *refs):
    y_refs, refs = refs[:part_count], refs[part_count:]
    table_ref, edge_ref, tiles_ref, *round_refs, _, out_hbm, out_ref, out_sem, first_ref = refs
    copies = []

    me = lax.axis_index("tm")
    for c in range(2):
        before = edge_ref[SUBLANES * c : SUBLANES * c + EDGE, :]
        for n, round_ref in enumerate(round_refs):
            last = round_ref[round_ref.shape[0] - 1, c, round_ref.shape[2] - EDGE :, :]
            before = jnp.where((me > 0) & ((me ^ (me - 1)) == 2 ** (n + 1) - 1), last, before)
        line = jnp.concatenate([before[n : n + 1] for n in range(EDGE)] + [tiles_ref[c, 0:1, :]], 1)

        def keep(h, g, value):
            first_ref[h, c, g : g + 2 * SUBLANES] = value

        spread_line(line, keep)

    def tiles_at(h, c, start):
        known = first_ref.shape[3]
        if start >= known:
            return table_ref[h, c, :, start - known : start - known + BLOCK_LEN]
        if start + BLOCK_LEN <= known:
            return first_ref[h, c, :, start : start + BLOCK_LEN]
        rest = start + BLOCK_LEN - known
        return jnp.concatenate([first_ref[h, c, :, start:], table_ref[h, c, :, :rest]], 1)

    def send(start, count):
        part = (slice(None), pl.ds(start, count))
        copies.append(pltpu.make_async_copy(out_ref.at[part], out_hbm.at[part], out_sem.at[len(copies)]))
        copies[-1].start()

    y = y_refs[0][...]
    for y_ref in y_refs[1:]:
        y = y + y_ref[...]
    rows, length = y.shape
    blocks = length // BLOCK_LEN
    turned = jnp.concatenate(
        [pltpu.roll(y[r : r + SUBLANES], SUBLANES // 2, 0) for r in range(0, rows, SUBLANES)], 0
    )
    turned = turned * row_sign(turned.shape)
    y_high, y_low = halves(y)
    t_high, t_low = halves(turned)
    both = jnp.concatenate([y_high, y_low], 0)
    turned_both = jnp.concatenate([t_high, t_low], 0)
    taps_sum = None
    for q in range(blocks):
        cols = slice(q * BLOCK_LEN, (q + 1) * BLOCK_LEN)
        tables = []
        for h in range(2):
            rows_of = []
            for start in (q * BLOCK_LEN + LANES, q * BLOCK_LEN):
                rows_of.append(jnp.concatenate([tiles_at(h, c, start) for c in range(2)], 1))
            tables.append(jnp.concatenate(rows_of, 0))
        lhs = jnp.concatenate([both[:, cols], turned_both[:, cols]], 1)
        by_high = dot_nt(lhs, tables[0])
        by_low = dot_nt(lhs[:rows], tables[1])
        product = by_high[:rows] + (by_high[rows:] + by_low)
        taps = product[:, :LANES]
        taps_sum = taps if taps_sum is None else taps_sum + taps
        for h in range(LAGS // LANES):
            lanes = slice(h * LANES, (h + 1) * LANES)
            tiles = [product[r : r + SUBLANES, lanes] for r in range(0, rows, SUBLANES)]
            for j, tile in enumerate(swap_groups(tiles, groups)):
                out_ref[h * groups + j, q] = tile
        if q % 2:
            send(q - 1, 2)
    left = lax.broadcasted_iota(jnp.int32, (SUBLANES, LANES), 1) < TAPS
    for i in range(groups // 2):
        a = taps_sum[i * SUBLANES : (i + 1) * SUBLANES]
        other = i + groups // 2
        b = taps_sum[other * SUBLANES : (other + 1) * SUBLANES]
        tile = jnp.where(left, a, pltpu.roll(b, LANES - TAPS, 1))
        for owner in range(out_ref.shape[0]):
            out_ref[owner, blocks + i] = tile
    send(blocks, groups // 2)
    for copy in copies:
        copy.wait()


def lag_call(ys, table, edge, tiles, rounds, after, groups, owners):
    blocks = ys[0].shape[1] // BLOCK_LEN
    shape = (owners, blocks + groups // 2, SUBLANES, LANES)
    vmem = pl.BlockSpec(memory_space=pltpu.VMEM)
    return pl.pallas_call(
        functools.partial(lag_kernel, groups, len(ys)),
        in_specs=[vmem] * (len(ys) + 3 + len(rounds)) + [pl.BlockSpec(memory_space=pl.ANY)],
        out_specs=pl.BlockSpec(memory_space=pltpu.HBM),
        out_shape=jax.ShapeDtypeStruct(shape, jnp.float32),
        scratch_shapes=[
            pltpu.VMEM(shape, jnp.float32),
            pltpu.SemaphoreType.DMA((blocks // 2 + 1,)),
            pltpu.VMEM((2, 2, LANES, 2 * LANES), jnp.bfloat16),
        ],
        compiler_params=params(),
        cost_estimate=cost(2.1),
        name="lag_products",
    )(*ys, table, edge, tiles, *rounds, after)


BATCH = 4


def own_kernel(lags_local, *refs):
    *part_refs, _, out_ref, line_ref, tail_ref, span_ref, late_ref, taps_a, lags_a, taps_b, lags_b = refs
    me = lax.axis_index("tm")
    part_rows = part_refs[0].shape[2]
    owners = sum(part_ref.shape[0] for part_ref in part_refs)
    samples = owners * part_rows * LANES
    steps = samples // BLOCK_LEN // BATCH
    total_rows = span_ref.shape[1]
    block_rows = BLOCK_LEN // LANES

    span_ref[...] = jnp.zeros_like(span_ref)
    e = 0
    for part_ref in part_refs:
        for i in range(part_ref.shape[0]):
            span_ref[:, pl.ds(EDGE + (me ^ e) * part_rows, part_rows), :] = part_ref[i]
            e += 1
    late_rows = (me * lags_local) // LANES
    late_lanes = lax.rem(me * lags_local, LANES)
    turned = [pltpu.roll(span_ref[c], late_lanes, 1) for c in range(2)]
    before = [pltpu.roll(x, 1, 0) for x in turned]
    lanes = lax.broadcasted_iota(jnp.int32, (total_rows, LANES), 1)
    for c in range(2):
        late_ref[c] = pltpu.roll(jnp.where(lanes < late_lanes, before[c], turned[c]), late_rows, 0)

    def line_of(ref, c, first, count):
        return jnp.concatenate([ref[c, pl.ds(first + n, 1), :] for n in range(count)], 1)

    def shifted(line, by):
        tiled = jnp.broadcast_to(line, (2 * SUBLANES, line.shape[1]))
        return pltpu.roll(tiled, by, 1, stride=1, stride_axis=0)[:, LANES:]

    def keep(ref, row, value):
        high, low = halves(value)
        half = ref.shape[0] // 2
        ref[row : row + 2 * SUBLANES, :] = high
        ref[half + row : half + row + 2 * SUBLANES, :] = low

    def build(n, taps_ref, lags_ref):
        first = EDGE - 1 + n * BATCH * block_rows
        count = BATCH * block_rows + 1
        lines = [line_of(span_ref, c, first, count) for c in range(2)]
        for c in range(2):
            for g in range(0, TAPS, 2 * SUBLANES):
                keep(taps_ref, c * TAPS + g, shifted(lines[c], g))
            late = line_of(late_ref, c, first, count)
            for g in range(0, lags_local, 2 * SUBLANES):
                keep(lags_ref, c * lags_local + g, shifted(late, g))
        pad = jnp.zeros((2 * SUBLANES - 2, BATCH * BLOCK_LEN), jnp.float32)
        keep(lags_ref, 2 * lags_local, jnp.concatenate([line[:, LANES:] for line in lines] + [pad], 0))

    turn = lane_sign((lags_local, LANES))

    def use(n, taps_ref, lags_ref):
        count = lags_ref.shape[0] // 2
        for b in range(BATCH):
            cols = slice(b * BLOCK_LEN, (b + 1) * BLOCK_LEN)
            product = dot_nt(lags_ref[:, cols], taps_ref[:, cols])
            product = product[:count, :LANES] + (product[:count, LANES:] + product[count:, :LANES])
            by_real = product[:lags_local]
            by_imag = product[lags_local : 2 * lags_local]
            rows = pl.ds(pl.multiple_of((n * BATCH + b) * lags_local, lags_local), lags_local)
            high, low = halves(by_real + turn * pltpu.roll(by_imag, TAPS, 1))
            out_ref[0, rows, :] = high
            out_ref[1, rows, :] = low
            line_ref[...] += product[2 * lags_local : 2 * lags_local + SUBLANES]

    line_ref[...] = jnp.zeros_like(line_ref)
    build(0, taps_a, lags_a)

    def pair(m, carry):
        build(2 * m + 1, taps_b, lags_b)
        use(2 * m, taps_a, lags_a)
        build(jnp.minimum(2 * m + 2, steps - 1), taps_a, lags_a)
        use(2 * m + 1, taps_b, lags_b)
        return carry

    lax.fori_loop(0, steps // 2, pair, 0)
    tail = []
    for c in range(2):
        line = line_of(span_ref, c, EDGE + owners * part_rows - 1, 2)
        tail += [shifted(line, g) for g in range(0, TAPS, 2 * SUBLANES)]
    tail = jnp.concatenate(tail, 0)
    tail_ref[...] = dot_nt(tail, tail, HIGHEST)


def own_call(parts, lags_local, after):
    part_rows = parts[0].shape[2]
    span_rows = part_rows * sum(part.shape[0] for part in parts)
    rows = span_rows * LANES // BLOCK_LEN * lags_local
    held_rows = -(-(span_rows + 2 * EDGE) // SUBLANES) * SUBLANES
    width = BATCH * BLOCK_LEN
    taps = pltpu.VMEM((4 * TAPS, width), jnp.bfloat16)
    lags = pltpu.VMEM((4 * lags_local + 4 * SUBLANES, width), jnp.bfloat16)
    span = pltpu.VMEM((2, held_rows, LANES), jnp.float32)
    return pl.pallas_call(
        functools.partial(own_kernel, lags_local),
        in_specs=[pl.BlockSpec(memory_space=pltpu.VMEM)] * len(parts) + [pl.BlockSpec(memory_space=pl.ANY)],
        out_shape=[
            jax.ShapeDtypeStruct((2, rows, 2 * TAPS), jnp.bfloat16),
            jax.ShapeDtypeStruct((SUBLANES, 2 * TAPS), jnp.float32),
            jax.ShapeDtypeStruct((2 * TAPS, 2 * TAPS), jnp.float32),
        ],
        scratch_shapes=[span, span, taps, lags, taps, lags],
        compiler_params=params(),
        cost_estimate=cost(6.2),
        name="reference_products",
    )(*parts, after)


def as_factor(a):
    return jnp.concatenate([a, -lane_sign(a.shape) * pltpu.roll(a, a.shape[0], 1)], 0)


def solver_kernel(line_ref, tail_ref, solver_ref):
    total = line_ref[...]
    line = total[0:1] + lane_sign((1, LANES)) * pltpu.roll(total[1:2], TAPS, 1)
    low = lax.broadcasted_iota(jnp.int32, (1, LANES), 1) < TAPS
    line_r = jnp.where(low, line, 0.0)
    line_i = jnp.where(low, pltpu.roll(line, TAPS, 1), 0.0)
    cols = lax.broadcasted_iota(jnp.int32, (TAPS, TAPS), 1)
    rows = lax.broadcasted_iota(jnp.int32, (TAPS, TAPS), 0)
    above = cols > rows

    def upper(x):
        spread = pltpu.roll(jnp.broadcast_to(x, (TAPS, LANES)), 0, 1, stride=1, stride_axis=0)
        return spread[:, :TAPS]

    up_r = upper(line_r)
    up_i = jnp.where(above, upper(line_i), 0.0)
    strict_r = jnp.where(above, up_r, 0.0)
    diag_r = jnp.where(cols == rows, up_r, 0.0)
    tails = tail_ref[...]
    gram_r = strict_r + strict_r.T + diag_r - (tails[:TAPS, :TAPS] + tails[TAPS:, TAPS:])
    gram_i = up_i - up_i.T - (tails[:TAPS, TAPS:] - tails[TAPS:, :TAPS])
    gram = jnp.concatenate([gram_r, gram_i], 1)
    gram_factor = as_factor(gram)
    gram_halves = halves(gram_factor)
    one = (
        lax.broadcasted_iota(jnp.int32, gram.shape, 0) == lax.broadcasted_iota(jnp.int32, gram.shape, 1)
    ).astype(jnp.float32)
    bound = jnp.max(jnp.sum(jnp.abs(gram), axis=1, keepdims=True), axis=0, keepdims=True)

    def again(state):
        count, left, _ = state
        return (count < 60) & (left > 1e-3)

    def newton(state):
        count, _, x = state
        x_halves = halves(x)
        seen = dot_split(x_halves, gram_halves)
        left = jnp.max(jnp.abs(seen - one))
        x = 2.0 * x - dot_split(halves(seen), halves(as_factor(x)))
        return count + 1, left, x

    start = (jnp.int32(0), jnp.float32(1.0), one * (1.0 / bound))
    _, _, inverse = lax.while_loop(again, newton, start)
    seen = jnp.dot(inverse, gram_factor, precision=HIGHEST, preferred_element_type=jnp.float32)
    inverse = inverse + jnp.dot(
        one - seen, as_factor(inverse), precision=HIGHEST, preferred_element_type=jnp.float32
    )
    solver_ref[...] = as_factor(inverse)


def solver_call(line, tail):
    return pl.pallas_call(
        solver_kernel,
        out_shape=jax.ShapeDtypeStruct(tail.shape, jnp.float32),
        compiler_params=params(),
        cost_estimate=cost(2.0),
        name="gram_inverse",
    )(line, tail)


def doppler_table(block_count, scale):
    phase = (np.arange(block_count)[:, None] * np.arange(DOPPLER)[None, :] % DOPPLER) * (2.0 * math.pi / DOPPLER)
    cosine, sine = np.cos(phase), np.sin(phase)
    upper = np.concatenate([cosine, -sine], 1)
    lower = np.concatenate([sine, cosine], 1)
    return (np.concatenate([upper, lower], 0) * scale).astype(np.float32)


def map_kernel(groups, got_ref, own_ref, solver_ref, wave_ref, out_hbm, held_ref, out_ref, out_sem):
    owners, pieces = got_ref.shape[:2]
    blocks = pieces - groups // 2
    lags_local = LANES // groups
    total = owners * blocks
    left = lax.broadcasted_iota(jnp.int32, (SUBLANES, LANES), 1) < TAPS
    sign = row_sign((SUBLANES, LANES))
    rows = [None] * groups
    for i in range(groups // 2):
        tile = got_ref[0, blocks + i]
        for owner in range(1, owners):
            tile = tile + got_ref[owner, blocks + i]
        swapped = pltpu.roll(tile, TAPS, 1)
        for part, here, there in ((i, tile, swapped), (i + groups // 2, swapped, tile)):
            other = -sign * pltpu.roll(there, SUBLANES // 2, 0)
            rows[part] = jnp.where(left, here, other)
    cross = jnp.concatenate(rows, 0)
    taps = jnp.dot(cross, solver_ref[...], precision=HIGHEST, preferred_element_type=jnp.float32)
    taps_high, taps_low = halves(taps)
    taps_both = jnp.concatenate([taps_high, taps_low], 1)
    for q in range(0, total, 2 * groups):
        own = slice(q * lags_local, (q + 2 * groups) * lags_local)
        own_high = own_ref[0, own, :]
        clutter = dot_nt(taps_both, jnp.concatenate([own_high, own_high], 1)) + dot_nt(taps_high, own_ref[1, own, :])
        for h in range(2):
            lanes = slice(h * LANES, (h + 1) * LANES)
            tiles = [clutter[r : r + SUBLANES, lanes] for r in range(0, groups * SUBLANES, SUBLANES)]
            for j, tile in enumerate(swap_groups(tiles, groups)):
                at = q + h * groups + j
                held_ref[at * SUBLANES : (at + 1) * SUBLANES, :] = got_ref[at // blocks, at % blocks] - tile
    half = SUBLANES // 2
    wave = (wave_ref[0], wave_ref[1])
    copies = []
    for first in range(0, half, 2):
        lagged = []
        for g in (first, first + 1):
            parts = [held_ref[pl.ds(c * half + g, total, stride=SUBLANES), :] for c in range(2)]
            lagged.append(jnp.concatenate(parts, 0).T)
        spectrum = dot_split(halves(jnp.concatenate(lagged, 0)), wave)
        for n in range(2 * groups):
            beam = half * (n % groups) + first + n // groups
            for c in range(2):
                out_ref[beam, c] = spectrum[n * lags_local : (n + 1) * lags_local, c * DOPPLER : (c + 1) * DOPPLER]
            copies.append(pltpu.make_async_copy(out_ref.at[beam], out_hbm.at[beam], out_sem.at[beam]))
            copies[-1].start()
    for copy in copies:
        copy.wait()


def map_call(got, own, solver, wave, groups, beams_local):
    total = got.shape[0] * (got.shape[1] - groups // 2)
    lags_local = LANES // groups
    shape = (beams_local, 2, lags_local, DOPPLER)
    return pl.pallas_call(
        functools.partial(map_kernel, groups),
        in_specs=[pl.BlockSpec(memory_space=pltpu.VMEM)] * 4,
        out_specs=pl.BlockSpec(memory_space=pltpu.HBM),
        out_shape=jax.ShapeDtypeStruct(shape, jnp.float32),
        scratch_shapes=[
            pltpu.VMEM((total * SUBLANES, LANES), jnp.float32),
            pltpu.VMEM(shape, jnp.float32),
            pltpu.SemaphoreType.DMA((beams_local,)),
        ],
        compiler_params=params(),
        cost_estimate=cost(2.5),
        name="range_doppler",
    )(got, own, solver, wave)


def swap(x, axis, by):
    pairs = [(i, i ^ by) for i in range(lax.axis_size(axis))]
    return lax.ppermute(x, axis, pairs)


def tiled_device(ref_signal, surveillance, steering):
    chan_count, tm_count = lax.axis_size("chan"), lax.axis_size("tm")
    channels, length = surveillance.shape[1:]
    beams_local = steering.shape[1] // chan_count
    lags_local = LAGS // tm_count
    groups = LANES // lags_local
    samples = length * tm_count

    survey = surveillance.reshape(2 * channels, length)
    kept, moved, tiles = beam_call(steering, survey, ref_signal, chan_count, beams_local)
    near = swap(tiles[None], "tm", 1)
    early = 1 if tm_count < 4 else 2
    edge = lax.ppermute(
        edge_call(tiles[None]), "tm", [(i, i + 1) for i in range(tm_count - 1) if i ^ (i + 1) >= 1 << early]
    )
    shape = (chan_count // 2, 2 * beams_local, length)
    kept, got = kept.reshape(shape), swap(moved, "chan", 1).reshape(shape)
    by = 2
    while by < chan_count:
        kept, moved = sum_call([kept, got])
        got = swap(moved, "chan", by)
        by *= 2
    rounds = [near]
    joined = join_call(tiles[None], near, moved, edge)
    while joined.shape[0] < tm_count:
        rounds.append(swap(joined, "tm", joined.shape[0]))
        if joined.shape[0] * 2 == tm_count:
            break
        joined = join_call(joined, rounds[-1])
    table = table_call(tiles)
    pieces = lag_call([kept[0], got[0]], table, edge, tiles, rounds[:early], joined, groups, tm_count)
    got = lax.all_to_all(pieces, "tm", 0, 0, tiled=True)
    own, line, tail = own_call([tiles[None]] + rounds, lags_local, pieces)
    solver = solver_call(line, tail)
    wave = doppler_table(samples // BLOCK_LEN, 0.125 / math.sqrt(samples))
    high = wave.astype(jnp.bfloat16)
    wave = np.stack([high, (wave - high.astype(np.float32)).astype(jnp.bfloat16)])
    return map_call(got, own, solver, jnp.asarray(wave), groups, beams_local)


def lag_table(ref_ext, offset, lags):
    window = lax.dynamic_slice_in_dim(ref_ext, offset, BLOCK_LEN + LAGS, 1)
    span = BLOCK_LEN + LAGS
    tiled = jnp.tile(jnp.pad(window, ((0, 0), (0, 1))), (1, lags))[:, : lags * span]
    return tiled.reshape(2, lags, span)[:, :, LAGS:]


def times_conj(a, b):
    real = jnp.einsum("...t,lt->...l", a[..., 0, :], b[0], precision=HIGHEST) + jnp.einsum(
        "...t,lt->...l", a[..., 1, :], b[1], precision=HIGHEST
    )
    imag = jnp.einsum("...t,lt->...l", a[..., 1, :], b[0], precision=HIGHEST) - jnp.einsum(
        "...t,lt->...l", a[..., 0, :], b[1], precision=HIGHEST
    )
    return jnp.stack([real, imag], -2)


def plain_device(ref_signal, surveillance, steering):
    chan_count, tm_count = lax.axis_size("chan"), lax.axis_size("tm")
    length = surveillance.shape[2]
    beams = steering.shape[1]
    lags_local = LAGS // tm_count
    samples = length * tm_count
    local_blocks = length // BLOCK_LEN
    here = lax.axis_index("tm")

    w_real, w_imag = steering
    real = jnp.dot(w_real, surveillance[0], precision=HIGHEST) - jnp.dot(w_imag, surveillance[1], precision=HIGHEST)
    imag = jnp.dot(w_imag, surveillance[0], precision=HIGHEST) + jnp.dot(w_real, surveillance[1], precision=HIGHEST)
    beam = lax.psum_scatter(jnp.stack([real, imag], 1), "chan", scatter_dimension=0, tiled=True)
    ref_all = lax.all_gather(ref_signal, "tm", axis=1, tiled=True)
    ref_ext = jnp.pad(ref_all, ((0, 0), (LAGS, 0)))

    def beam_step(carry, q):
        offset = q * BLOCK_LEN
        table = lag_table(ref_ext, here * length + offset, LAGS)
        segment = lax.dynamic_slice_in_dim(beam, offset, BLOCK_LEN, 2)
        return carry, times_conj(segment, table)

    _, products = lax.scan(beam_step, None, jnp.arange(local_blocks, dtype=jnp.int32))
    cross = lax.psum(products[..., :TAPS].sum(0), "tm")
    got = lax.all_to_all(products, "tm", 3, 0, tiled=True)

    def own_step(gram, q):
        offset = q * BLOCK_LEN
        table = lag_table(ref_ext, offset, LAGS)
        taps = table[:, :TAPS].transpose(1, 0, 2)
        mine = lax.dynamic_slice_in_dim(table, here * lags_local, lags_local, 1)
        return gram + times_conj(taps, table[:, :TAPS]), times_conj(taps, mine)

    start = jnp.zeros((TAPS, 2, TAPS), jnp.float32)
    gram, own = lax.scan(own_step, start, jnp.arange(samples // BLOCK_LEN, dtype=jnp.int32))
    g_real, g_imag = gram[:, 0].T, gram[:, 1].T
    system = jnp.concatenate([jnp.concatenate([g_real, -g_imag], 1), jnp.concatenate([g_imag, g_real], 1)], 0)
    right = jnp.concatenate([cross[:, 0].T, cross[:, 1].T], 0)
    solved = jax.scipy.linalg.cho_solve((jnp.linalg.cholesky(system), True), right)
    b_real, b_imag = solved[:TAPS].T, solved[TAPS:].T
    mixing = jnp.concatenate([jnp.stack([b_real, b_imag], 1), jnp.stack([-b_imag, b_real], 1)], 2)
    stacked = jnp.concatenate([own[:, :, 0], own[:, :, 1]], 1)
    lagged = got - jnp.einsum("mck,qkl->qmcl", mixing, stacked, precision=HIGHEST)
    wave = jnp.asarray(doppler_table(samples // BLOCK_LEN, 0.125 / math.sqrt(samples)))
    wave = wave.reshape(2, samples // BLOCK_LEN, 2, DOPPLER)
    return jnp.einsum("qmcl,cqdk->mdlk", lagged, wave, precision=HIGHEST)


def on_device(ref_signal, surveillance, steering):
    chan_count, tm_count = lax.axis_size("chan"), lax.axis_size("tm")
    beams_local = steering.shape[1] // chan_count
    lags_local = LAGS // tm_count
    fills = (
        LANES % lags_local == 0
        and lags_local % (2 * SUBLANES) == 0
        and beams_local * lags_local == LANES * SUBLANES // 2
        and chan_count > 1
        and chan_count & (chan_count - 1) == 0
        and tm_count > 1
        and tm_count & (tm_count - 1) == 0
        and 2 * surveillance.shape[1] % LANES == 0
        and surveillance.shape[2] % (2 * BATCH * BLOCK_LEN) == 0
    )
    device = tiled_device if fills else plain_device
    return device(ref_signal, surveillance, steering)


def solution(mesh):
    placed = (P(None, "tm"), P(None, "chan", "tm"), P(None, None, "chan"))
    return jax.shard_map(
        on_device,
        mesh=mesh,
        in_specs=placed,
        out_specs=P("chan", None, "tm", None),
        check_vma=False,
    )
```

```python
import functools
import math

import jax
import jax.numpy as jnp
import numpy as np
from jax import lax
from jax.experimental import pallas as pl
from jax.experimental.pallas import tpu as pltpu
from jax.sharding import PartitionSpec as P

LAGS = 256
DOPPLER = 256
TAPS = 64
BLOCK_LEN = 256
LANES = 128
SUBLANES = 8
EDGE = 2

HIGHEST = lax.Precision.HIGHEST
VMEM_BYTES = 48 * 1024 * 1024


def params():
    return pltpu.CompilerParams(vmem_limit_bytes=VMEM_BYTES)


def cost(us):
    return pl.CostEstimate(flops=int(us * 1.15e9), bytes_accessed=0, transcendentals=0)


def halves(x):
    high = x.astype(jnp.bfloat16)
    return high, (x - high.astype(jnp.float32)).astype(jnp.bfloat16)


def dot_nt(a, b, precision=None):
    return lax.dot_general(
        a, b, (((1,), (1,)), ((), ())), precision=precision, preferred_element_type=jnp.float32
    )


def dot_split(a, b):
    (a_high, a_low), (b_high, b_low) = a, b
    left = jnp.concatenate([a_high, a_low], 1)
    right = jnp.concatenate([b_high, b_high], 0)
    return jnp.dot(left, right, preferred_element_type=jnp.float32) + jnp.dot(
        a_high, b_low, preferred_element_type=jnp.float32
    )


def row_sign(shape):
    rows = lax.broadcasted_iota(jnp.int32, shape, 0)
    return jnp.where(rows % SUBLANES < SUBLANES // 2, 1.0, -1.0).astype(jnp.float32)


def lane_sign(shape):
    lanes = lax.broadcasted_iota(jnp.int32, shape, 1)
    return jnp.where(lanes % LANES < LANES // 2, 1.0, -1.0).astype(jnp.float32)


def swap_groups(rows, groups):
    width = LANES // groups
    lane_group = lax.broadcasted_iota(jnp.int32, rows[0].shape, 1) // width
    outs = []
    for j in range(groups):
        out = rows[j]
        for i in range(groups):
            if i != j:
                moved = pltpu.roll(rows[i], (width * (i - j)) % LANES, 1)
                out = jnp.where(lane_group == i, moved, out)
        outs.append(out)
    return outs


CHUNKS = 4


def beam_kernel(
    chan_count, beams_local, w_hbm, s_hbm, ref_hbm, kept_ref, sent_ref, tiles_ref,
    w_ref, s_ref, ref_ref, w_sem, s_sem, ref_sem,
):
    me = lax.axis_index("chan")
    length = s_hbm.shape[1]
    width = length // CHUNKS
    w_copy = pltpu.make_async_copy(w_hbm, w_ref, w_sem)
    w_copy.start()
    ref_copy = pltpu.make_async_copy(ref_hbm, ref_ref, ref_sem)
    ref_copy.start()
    s_copies = []
    for n in range(CHUNKS):
        cols = pl.ds(n * width, width)
        s_copies.append(pltpu.make_async_copy(s_hbm.at[:, cols], s_ref.at[:, cols], s_sem.at[n]))
        s_copies[n].start()
    half = SUBLANES // 2
    sub = lax.broadcasted_iota(jnp.int32, (SUBLANES, w_hbm.shape[2]), 0)
    top = sub < half
    w_copy.wait()
    rows = []
    for parity in range(2):
        for e in range(parity, chan_count, 2):
            base = (me ^ e) * beams_local
            for tile in range(beams_local // SUBLANES):
                start = pl.multiple_of(base + tile * SUBLANES, SUBLANES)
                wr = w_ref[0, pl.ds(start, SUBLANES), :]
                wi = w_ref[1, pl.ds(start, SUBLANES), :]
                wr_s = pltpu.roll(wr, half, 0)
                wi_s = pltpu.roll(wi, half, 0)
                first = [jnp.where(top, wr, wi_s), jnp.where(top, -wi, wr_s)]
                second = [jnp.where(top, wr_s, wi), jnp.where(top, -wi_s, wr)]
                rows.append(jnp.concatenate(first, 1))
                rows.append(jnp.concatenate(second, 1))
    weights = halves(jnp.concatenate(rows, 0))
    ref_copy.wait()
    for c in range(2):
        for n in range(tiles_ref.shape[1]):
            tiles_ref[c, n : n + 1, :] = ref_ref[c : c + 1, n * LANES : (n + 1) * LANES]
    mid = weights[0].shape[0] // 2
    for n in range(CHUNKS):
        cols = slice(n * width, (n + 1) * width)
        s_copies[n].wait()
        product = dot_split(weights, halves(s_ref[:, cols]))
        kept_ref[:, cols] = product[:mid]
        sent_ref[:, cols] = product[mid:]


def beam_call(steering, survey, ref, chan_count, beams_local):
    depth, length = survey.shape
    rows = chan_count * beams_local
    tiles = (2, length // LANES, LANES)
    out = jax.ShapeDtypeStruct((rows, length), jnp.float32)
    hbm, vmem = pl.BlockSpec(memory_space=pltpu.HBM), pl.BlockSpec(memory_space=pltpu.VMEM)
    return pl.pallas_call(
        functools.partial(beam_kernel, chan_count, beams_local),
        in_specs=[hbm] * 3,
        out_specs=[vmem] * 3,
        out_shape=[
            out,
            out,
            jax.ShapeDtypeStruct(tiles, jnp.float32),
        ],
        scratch_shapes=[
            pltpu.VMEM(steering.shape, jnp.float32),
            pltpu.VMEM(survey.shape, jnp.float32),
            pltpu.VMEM(ref.shape, jnp.float32),
            pltpu.SemaphoreType.DMA,
            pltpu.SemaphoreType.DMA((CHUNKS,)),
            pltpu.SemaphoreType.DMA,
        ],
        compiler_params=params(),
        cost_estimate=cost(2.2),
        name="beams",
    )(*(pltpu.with_memory_space_constraint(x, pltpu.HBM) for x in (steering, survey, ref)))


def sum_kernel(count, *refs):
    kept_ref, sent_ref = refs[-2:]
    for n in range(kept_ref.shape[0]):
        for offset, out_ref in ((0, kept_ref), (1, sent_ref)):
            total = refs[0][2 * n + offset]
            for ref in refs[1:count]:
                total = total + ref[2 * n + offset]
            out_ref[n] = total


def sum_call(parts):
    shape = (parts[0].shape[0] // 2,) + parts[0].shape[1:]
    out = jax.ShapeDtypeStruct(shape, jnp.float32)
    vmem = pl.BlockSpec(memory_space=pltpu.VMEM)
    return pl.pallas_call(
        functools.partial(sum_kernel, len(parts)),
        in_specs=[vmem] * len(parts),
        out_specs=[vmem, vmem],
        out_shape=[out, out],
        compiler_params=params(),
        cost_estimate=cost(0.1),
        name="halves_summed",
    )(*parts)


def join_kernel(first_ref, second_ref, *refs):
    out_ref = refs[-1]
    count = first_ref.shape[0]
    out_ref[:count] = first_ref[...]
    out_ref[count:] = second_ref[...]


def join_call(first, second, *after):
    vmem = pl.BlockSpec(memory_space=pltpu.VMEM)
    return pl.pallas_call(
        join_kernel,
        in_specs=[vmem, vmem] + [pl.BlockSpec(memory_space=pl.ANY)] * len(after),
        out_shape=jax.ShapeDtypeStruct((2 * first.shape[0],) + first.shape[1:], jnp.float32),
        compiler_params=params(),
        cost_estimate=cost(1.0),
        name="reference_joined",
    )(first, second, *after)


def spread_line(line, keep):
    for g in range(0, LANES, 2 * SUBLANES):
        tiled = jnp.broadcast_to(line, (2 * SUBLANES, line.shape[1]))
        for h, value in enumerate(halves(pltpu.roll(tiled, g, 1, stride=1, stride_axis=0)[:, LANES:])):
            keep(h, g, value)


def table_kernel(tiles_ref, out_ref):
    for c in range(2):
        line = jnp.concatenate([tiles_ref[c, n : n + 1, :] for n in range(tiles_ref.shape[1])], 1)

        def keep(h, g, value):
            out_ref[h, c, g : g + 2 * SUBLANES] = value

        spread_line(line, keep)


def table_call(tiles):
    shape = (2, 2, LANES, LANES * (tiles.shape[1] - 1))
    return pl.pallas_call(
        table_kernel,
        out_shape=jax.ShapeDtypeStruct(shape, jnp.bfloat16),
        compiler_params=params(),
        cost_estimate=cost(0.7),
        name="shifted_reference",
    )(tiles)


def lag_kernel(groups, part_count, *refs):
    y_refs, refs = refs[:part_count], refs[part_count:]
    table_ref, tiles_ref, *round_refs, _, out_hbm, out_ref, out_sem, first_ref = refs
    copies = []

    me = lax.axis_index("tm")
    for c in range(2):
        tails = [ref[ref.shape[0] - 1, c, ref.shape[2] - EDGE :, :] for ref in round_refs]
        before = jnp.where(me % 2 == 1, tails[0], jnp.where(me > 0, tails[-1], 0.0))
        line = jnp.concatenate([before[n : n + 1] for n in range(EDGE)] + [tiles_ref[c, 0:1, :]], 1)

        def keep(h, g, value):
            first_ref[h, c, g : g + 2 * SUBLANES] = value

        spread_line(line, keep)

    def tiles_at(h, c, start):
        known = first_ref.shape[3]
        if start >= known:
            return table_ref[h, c, :, start - known : start - known + BLOCK_LEN]
        if start + BLOCK_LEN <= known:
            return first_ref[h, c, :, start : start + BLOCK_LEN]
        rest = start + BLOCK_LEN - known
        return jnp.concatenate([first_ref[h, c, :, start:], table_ref[h, c, :, :rest]], 1)

    def send(start, count):
        part = (slice(None), pl.ds(start, count))
        copies.append(pltpu.make_async_copy(out_ref.at[part], out_hbm.at[part], out_sem.at[len(copies)]))
        copies[-1].start()

    y = y_refs[0][...]
    for y_ref in y_refs[1:]:
        y = y + y_ref[...]
    rows, length = y.shape
    blocks = length // BLOCK_LEN
    turned = jnp.concatenate(
        [pltpu.roll(y[r : r + SUBLANES], SUBLANES // 2, 0) for r in range(0, rows, SUBLANES)], 0
    )
    turned = turned * row_sign(turned.shape)
    y_high, y_low = halves(y)
    t_high, t_low = halves(turned)
    both = jnp.concatenate([y_high, y_low], 0)
    turned_both = jnp.concatenate([t_high, t_low], 0)
    taps_sum = None
    for q in range(blocks):
        cols = slice(q * BLOCK_LEN, (q + 1) * BLOCK_LEN)
        tables = []
        for h in range(2):
            rows_of = []
            for start in (q * BLOCK_LEN + LANES, q * BLOCK_LEN):
                rows_of.append(jnp.concatenate([tiles_at(h, c, start) for c in range(2)], 1))
            tables.append(jnp.concatenate(rows_of, 0))
        lhs = jnp.concatenate([both[:, cols], turned_both[:, cols]], 1)
        by_high = dot_nt(lhs, tables[0])
        by_low = dot_nt(lhs[:rows], tables[1])
        product = by_high[:rows] + (by_high[rows:] + by_low)
        taps = product[:, :LANES]
        taps_sum = taps if taps_sum is None else taps_sum + taps
        for h in range(LAGS // LANES):
            lanes = slice(h * LANES, (h + 1) * LANES)
            tiles = [product[r : r + SUBLANES, lanes] for r in range(0, rows, SUBLANES)]
            for j, tile in enumerate(swap_groups(tiles, groups)):
                out_ref[h * groups + j, q] = tile
        if q % 2:
            send(q - 1, 2)
    left = lax.broadcasted_iota(jnp.int32, (SUBLANES, LANES), 1) < TAPS
    for i in range(groups // 2):
        a = taps_sum[i * SUBLANES : (i + 1) * SUBLANES]
        other = i + groups // 2
        b = taps_sum[other * SUBLANES : (other + 1) * SUBLANES]
        tile = jnp.where(left, a, pltpu.roll(b, LANES - TAPS, 1))
        for owner in range(out_ref.shape[0]):
            out_ref[owner, blocks + i] = tile
    send(blocks, groups // 2)
    for copy in copies:
        copy.wait()


def lag_call(ys, table, tiles, rounds, after, groups, owners):
    blocks = ys[0].shape[1] // BLOCK_LEN
    shape = (owners, blocks + groups // 2, SUBLANES, LANES)
    vmem = pl.BlockSpec(memory_space=pltpu.VMEM)
    return pl.pallas_call(
        functools.partial(lag_kernel, groups, len(ys)),
        in_specs=[vmem] * (len(ys) + 2 + len(rounds)) + [pl.BlockSpec(memory_space=pl.ANY)],
        out_specs=pl.BlockSpec(memory_space=pltpu.HBM),
        out_shape=jax.ShapeDtypeStruct(shape, jnp.float32),
        scratch_shapes=[
            pltpu.VMEM(shape, jnp.float32),
            pltpu.SemaphoreType.DMA((blocks // 2 + 1,)),
            pltpu.VMEM((2, 2, LANES, 2 * LANES), jnp.bfloat16),
        ],
        compiler_params=params(),
        cost_estimate=cost(2.1),
        name="lag_products",
    )(*ys, table, tiles, *rounds, after)


BATCH = 4


def own_kernel(lags_local, *refs):
    *part_refs, _, out_ref, line_ref, tail_ref, span_ref, late_ref, taps_a, lags_a, taps_b, lags_b = refs
    me = lax.axis_index("tm")
    part_rows = part_refs[0].shape[2]
    owners = sum(part_ref.shape[0] for part_ref in part_refs)
    samples = owners * part_rows * LANES
    steps = samples // BLOCK_LEN // BATCH
    total_rows = span_ref.shape[1]
    block_rows = BLOCK_LEN // LANES

    span_ref[...] = jnp.zeros_like(span_ref)
    n = 0
    for part_ref in part_refs:
        for i in range(part_ref.shape[0]):
            block = lax.rem(me - (n // 2) * 2 + owners, owners) ^ (n % 2)
            span_ref[:, pl.ds(EDGE + block * part_rows, part_rows), :] = part_ref[i]
            n += 1
    late_rows = (me * lags_local) // LANES
    late_lanes = lax.rem(me * lags_local, LANES)
    turned = [pltpu.roll(span_ref[c], late_lanes, 1) for c in range(2)]
    before = [pltpu.roll(x, 1, 0) for x in turned]
    lanes = lax.broadcasted_iota(jnp.int32, (total_rows, LANES), 1)
    for c in range(2):
        late_ref[c] = pltpu.roll(jnp.where(lanes < late_lanes, before[c], turned[c]), late_rows, 0)

    def line_of(ref, c, first, count):
        return jnp.concatenate([ref[c, pl.ds(first + n, 1), :] for n in range(count)], 1)

    def shifted(line, by):
        tiled = jnp.broadcast_to(line, (2 * SUBLANES, line.shape[1]))
        return pltpu.roll(tiled, by, 1, stride=1, stride_axis=0)[:, LANES:]

    def keep(ref, row, value):
        high, low = halves(value)
        half = ref.shape[0] // 2
        ref[row : row + 2 * SUBLANES, :] = high
        ref[half + row : half + row + 2 * SUBLANES, :] = low

    def build(n, taps_ref, lags_ref):
        first = EDGE - 1 + n * BATCH * block_rows
        count = BATCH * block_rows + 1
        lines = [line_of(span_ref, c, first, count) for c in range(2)]
        for c in range(2):
            for g in range(0, TAPS, 2 * SUBLANES):
                keep(taps_ref, c * TAPS + g, shifted(lines[c], g))
            late = line_of(late_ref, c, first, count)
            for g in range(0, lags_local, 2 * SUBLANES):
                keep(lags_ref, c * lags_local + g, shifted(late, g))
        pad = jnp.zeros((2 * SUBLANES - 2, BATCH * BLOCK_LEN), jnp.float32)
        keep(lags_ref, 2 * lags_local, jnp.concatenate([line[:, LANES:] for line in lines] + [pad], 0))

    turn = lane_sign((lags_local, LANES))

    def use(n, taps_ref, lags_ref):
        count = lags_ref.shape[0] // 2
        for b in range(BATCH):
            cols = slice(b * BLOCK_LEN, (b + 1) * BLOCK_LEN)
            product = dot_nt(lags_ref[:, cols], taps_ref[:, cols])
            product = product[:count, :LANES] + (product[:count, LANES:] + product[count:, :LANES])
            by_real = product[:lags_local]
            by_imag = product[lags_local : 2 * lags_local]
            rows = pl.ds(pl.multiple_of((n * BATCH + b) * lags_local, lags_local), lags_local)
            high, low = halves(by_real + turn * pltpu.roll(by_imag, TAPS, 1))
            out_ref[0, rows, :] = high
            out_ref[1, rows, :] = low
            line_ref[...] += product[2 * lags_local : 2 * lags_local + SUBLANES]

    line_ref[...] = jnp.zeros_like(line_ref)
    build(0, taps_a, lags_a)

    def pair(m, carry):
        build(2 * m + 1, taps_b, lags_b)
        use(2 * m, taps_a, lags_a)
        build(jnp.minimum(2 * m + 2, steps - 1), taps_a, lags_a)
        use(2 * m + 1, taps_b, lags_b)
        return carry

    lax.fori_loop(0, steps // 2, pair, 0)
    tail = []
    for c in range(2):
        line = line_of(span_ref, c, EDGE + owners * part_rows - 1, 2)
        tail += [shifted(line, g) for g in range(0, TAPS, 2 * SUBLANES)]
    tail = jnp.concatenate(tail, 0)
    tail_ref[...] = dot_nt(tail, tail, HIGHEST)


def own_call(parts, lags_local, after):
    part_rows = parts[0].shape[2]
    span_rows = part_rows * sum(part.shape[0] for part in parts)
    rows = span_rows * LANES // BLOCK_LEN * lags_local
    held_rows = -(-(span_rows + 2 * EDGE) // SUBLANES) * SUBLANES
    width = BATCH * BLOCK_LEN
    taps = pltpu.VMEM((4 * TAPS, width), jnp.bfloat16)
    lags = pltpu.VMEM((4 * lags_local + 4 * SUBLANES, width), jnp.bfloat16)
    span = pltpu.VMEM((2, held_rows, LANES), jnp.float32)
    return pl.pallas_call(
        functools.partial(own_kernel, lags_local),
        in_specs=[pl.BlockSpec(memory_space=pltpu.VMEM)] * len(parts) + [pl.BlockSpec(memory_space=pl.ANY)],
        out_shape=[
            jax.ShapeDtypeStruct((2, rows, 2 * TAPS), jnp.bfloat16),
            jax.ShapeDtypeStruct((SUBLANES, 2 * TAPS), jnp.float32),
            jax.ShapeDtypeStruct((2 * TAPS, 2 * TAPS), jnp.float32),
        ],
        scratch_shapes=[span, span, taps, lags, taps, lags],
        compiler_params=params(),
        cost_estimate=cost(6.2),
        name="reference_products",
    )(*parts, after)


def as_factor(a):
    return jnp.concatenate([a, -lane_sign(a.shape) * pltpu.roll(a, a.shape[0], 1)], 0)


def solver_kernel(line_ref, tail_ref, gram_ref, solver_ref):
    total = line_ref[...]
    line = total[0:1] + lane_sign((1, LANES)) * pltpu.roll(total[1:2], TAPS, 1)
    low = lax.broadcasted_iota(jnp.int32, (1, LANES), 1) < TAPS
    line_r = jnp.where(low, line, 0.0)
    line_i = jnp.where(low, pltpu.roll(line, TAPS, 1), 0.0)
    cols = lax.broadcasted_iota(jnp.int32, (TAPS, TAPS), 1)
    rows = lax.broadcasted_iota(jnp.int32, (TAPS, TAPS), 0)
    above = cols > rows

    def upper(x):
        spread = pltpu.roll(jnp.broadcast_to(x, (TAPS, LANES)), 0, 1, stride=1, stride_axis=0)
        return spread[:, :TAPS]

    up_r = upper(line_r)
    up_i = jnp.where(above, upper(line_i), 0.0)
    strict_r = jnp.where(above, up_r, 0.0)
    diag_r = jnp.where(cols == rows, up_r, 0.0)
    tails = tail_ref[...]
    gram_r = strict_r + strict_r.T + diag_r - (tails[:TAPS, :TAPS] + tails[TAPS:, TAPS:])
    gram_i = up_i - up_i.T - (tails[:TAPS, TAPS:] - tails[TAPS:, :TAPS])
    gram = jnp.concatenate([gram_r, gram_i], 1)
    gram_halves = halves(as_factor(gram))
    gram_ref[0], gram_ref[1] = gram_halves
    one = (
        lax.broadcasted_iota(jnp.int32, gram.shape, 0) == lax.broadcasted_iota(jnp.int32, gram.shape, 1)
    ).astype(jnp.float32)
    bound = jnp.max(jnp.sum(jnp.abs(gram), axis=1, keepdims=True), axis=0, keepdims=True)

    def again(state):
        count, left, _ = state
        return (count < 60) & (left > 1e-3)

    def newton(state):
        count, _, x = state
        x_halves = halves(x)
        seen = dot_split(x_halves, gram_halves)
        left = jnp.max(jnp.abs(seen - one))
        x = 2.0 * x - dot_split(halves(seen), halves(as_factor(x)))
        return count + 1, left, x

    start = (jnp.int32(0), jnp.float32(1.0), one * (1.0 / bound))
    _, _, inverse = lax.while_loop(again, newton, start)
    solver_ref[0], solver_ref[1] = halves(as_factor(inverse))


def solver_call(line, tail):
    out = jax.ShapeDtypeStruct((2,) + tail.shape, jnp.bfloat16)
    return pl.pallas_call(
        solver_kernel,
        out_shape=[out, out],
        compiler_params=params(),
        cost_estimate=cost(2.0),
        name="gram_inverse",
    )(line, tail)


def doppler_table(block_count, scale):
    phase = (np.arange(block_count)[:, None] * np.arange(DOPPLER)[None, :] % DOPPLER) * (2.0 * math.pi / DOPPLER)
    cosine, sine = np.cos(phase), np.sin(phase)
    upper = np.concatenate([cosine, -sine], 1)
    lower = np.concatenate([sine, cosine], 1)
    return (np.concatenate([upper, lower], 0) * scale).astype(np.float32)


def map_kernel(groups, got_ref, own_ref, gram_ref, solver_ref, wave_ref, out_hbm, held_ref, out_ref, out_sem):
    owners, pieces = got_ref.shape[:2]
    blocks = pieces - groups // 2
    lags_local = LANES // groups
    total = owners * blocks
    left = lax.broadcasted_iota(jnp.int32, (SUBLANES, LANES), 1) < TAPS
    sign = row_sign((SUBLANES, LANES))
    rows = [None] * groups
    for i in range(groups // 2):
        tile = got_ref[0, blocks + i]
        for owner in range(1, owners):
            tile = tile + got_ref[owner, blocks + i]
        swapped = pltpu.roll(tile, TAPS, 1)
        for part, here, there in ((i, tile, swapped), (i + groups // 2, swapped, tile)):
            other = -sign * pltpu.roll(there, SUBLANES // 2, 0)
            rows[part] = jnp.where(left, here, other)
    cross = jnp.concatenate(rows, 0)
    solver = (solver_ref[0], solver_ref[1])
    taps = dot_split(halves(cross), solver)
    rest = cross - dot_split(halves(taps), (gram_ref[0], gram_ref[1]))
    taps = taps + dot_split(halves(rest), solver)
    taps_high, taps_low = halves(taps)
    taps_both = jnp.concatenate([taps_high, taps_low], 1)
    for q in range(0, total, 2 * groups):
        own = slice(q * lags_local, (q + 2 * groups) * lags_local)
        own_high = own_ref[0, own, :]
        clutter = dot_nt(taps_both, jnp.concatenate([own_high, own_high], 1)) + dot_nt(taps_high, own_ref[1, own, :])
        for h in range(2):
            lanes = slice(h * LANES, (h + 1) * LANES)
            tiles = [clutter[r : r + SUBLANES, lanes] for r in range(0, groups * SUBLANES, SUBLANES)]
            for j, tile in enumerate(swap_groups(tiles, groups)):
                at = q + h * groups + j
                held_ref[at * SUBLANES : (at + 1) * SUBLANES, :] = got_ref[at // blocks, at % blocks] - tile
    half = SUBLANES // 2
    wave = (wave_ref[0], wave_ref[1])
    copies = []
    for first in range(0, half, 2):
        lagged = []
        for g in (first, first + 1):
            parts = [held_ref[pl.ds(c * half + g, total, stride=SUBLANES), :] for c in range(2)]
            lagged.append(jnp.concatenate(parts, 0).T)
        spectrum = dot_split(halves(jnp.concatenate(lagged, 0)), wave)
        for n in range(2 * groups):
            beam = half * (n % groups) + first + n // groups
            for c in range(2):
                out_ref[beam, c] = spectrum[n * lags_local : (n + 1) * lags_local, c * DOPPLER : (c + 1) * DOPPLER]
            copies.append(pltpu.make_async_copy(out_ref.at[beam], out_hbm.at[beam], out_sem.at[beam]))
            copies[-1].start()
    for copy in copies:
        copy.wait()


def map_call(got, own, gram, solver, wave, groups, beams_local):
    total = got.shape[0] * (got.shape[1] - groups // 2)
    lags_local = LANES // groups
    shape = (beams_local, 2, lags_local, DOPPLER)
    return pl.pallas_call(
        functools.partial(map_kernel, groups),
        in_specs=[pl.BlockSpec(memory_space=pltpu.VMEM)] * 5,
        out_specs=pl.BlockSpec(memory_space=pltpu.HBM),
        out_shape=jax.ShapeDtypeStruct(shape, jnp.float32),
        scratch_shapes=[
            pltpu.VMEM((total * SUBLANES, LANES), jnp.float32),
            pltpu.VMEM(shape, jnp.float32),
            pltpu.SemaphoreType.DMA((beams_local,)),
        ],
        compiler_params=params(),
        cost_estimate=cost(2.5),
        name="range_doppler",
    )(got, own, gram, solver, wave)


def swap(x, axis, by):
    pairs = [(i, i ^ by) for i in range(lax.axis_size(axis))]
    return lax.ppermute(x, axis, pairs)


def tiled_device(ref_signal, surveillance, steering):
    chan_count, tm_count = lax.axis_size("chan"), lax.axis_size("tm")
    channels, length = surveillance.shape[1:]
    beams_local = steering.shape[1] // chan_count
    lags_local = LAGS // tm_count
    groups = LANES // lags_local
    samples = length * tm_count

    survey = surveillance.reshape(2 * channels, length)
    kept, moved, tiles = beam_call(steering, survey, ref_signal, chan_count, beams_local)
    near = swap(tiles[None], "tm", 1)
    shape = (chan_count // 2, 2 * beams_local, length)
    kept, got = kept.reshape(shape), swap(moved, "chan", 1).reshape(shape)
    by = 2
    while by < chan_count:
        kept, moved = sum_call([kept, got])
        got = swap(moved, "chan", by)
        by *= 2
    rounds = [near]
    joined = join_call(tiles[None], near, moved)
    while True:
        count = joined.shape[0]
        rounds.append(lax.ppermute(joined, "tm", [(i, (i + count) % tm_count) for i in range(tm_count)]))
        if count * 2 == tm_count:
            break
        joined = join_call(joined, rounds[-1])
    table = table_call(tiles)
    pieces = lag_call([kept[0], got[0]], table, tiles, rounds[:2], joined, groups, tm_count)
    got = lax.all_to_all(pieces, "tm", 0, 0, tiled=True)
    own, line, tail = own_call([tiles[None]] + rounds, lags_local, pieces)
    gram, solver = solver_call(line, tail)
    wave = doppler_table(samples // BLOCK_LEN, 0.125 / math.sqrt(samples))
    high = wave.astype(jnp.bfloat16)
    wave = np.stack([high, (wave - high.astype(np.float32)).astype(jnp.bfloat16)])
    return map_call(got, own, gram, solver, jnp.asarray(wave), groups, beams_local)


def lag_table(ref_ext, offset, lags):
    window = lax.dynamic_slice_in_dim(ref_ext, offset, BLOCK_LEN + LAGS, 1)
    span = BLOCK_LEN + LAGS
    tiled = jnp.tile(jnp.pad(window, ((0, 0), (0, 1))), (1, lags))[:, : lags * span]
    return tiled.reshape(2, lags, span)[:, :, LAGS:]


def times_conj(a, b):
    real = jnp.einsum("...t,lt->...l", a[..., 0, :], b[0], precision=HIGHEST) + jnp.einsum(
        "...t,lt->...l", a[..., 1, :], b[1], precision=HIGHEST
    )
    imag = jnp.einsum("...t,lt->...l", a[..., 1, :], b[0], precision=HIGHEST) - jnp.einsum(
        "...t,lt->...l", a[..., 0, :], b[1], precision=HIGHEST
    )
    return jnp.stack([real, imag], -2)


def plain_device(ref_signal, surveillance, steering):
    chan_count, tm_count = lax.axis_size("chan"), lax.axis_size("tm")
    length = surveillance.shape[2]
    beams = steering.shape[1]
    lags_local = LAGS // tm_count
    samples = length * tm_count
    local_blocks = length // BLOCK_LEN
    here = lax.axis_index("tm")

    w_real, w_imag = steering
    real = jnp.dot(w_real, surveillance[0], precision=HIGHEST) - jnp.dot(w_imag, surveillance[1], precision=HIGHEST)
    imag = jnp.dot(w_imag, surveillance[0], precision=HIGHEST) + jnp.dot(w_real, surveillance[1], precision=HIGHEST)
    beam = lax.psum_scatter(jnp.stack([real, imag], 1), "chan", scatter_dimension=0, tiled=True)
    ref_all = lax.all_gather(ref_signal, "tm", axis=1, tiled=True)
    ref_ext = jnp.pad(ref_all, ((0, 0), (LAGS, 0)))

    def beam_step(carry, q):
        offset = q * BLOCK_LEN
        table = lag_table(ref_ext, here * length + offset, LAGS)
        segment = lax.dynamic_slice_in_dim(beam, offset, BLOCK_LEN, 2)
        return carry, times_conj(segment, table)

    _, products = lax.scan(beam_step, None, jnp.arange(local_blocks, dtype=jnp.int32))
    cross = lax.psum(products[..., :TAPS].sum(0), "tm")
    got = lax.all_to_all(products, "tm", 3, 0, tiled=True)

    def own_step(gram, q):
        offset = q * BLOCK_LEN
        table = lag_table(ref_ext, offset, LAGS)
        taps = table[:, :TAPS].transpose(1, 0, 2)
        mine = lax.dynamic_slice_in_dim(table, here * lags_local, lags_local, 1)
        return gram + times_conj(taps, table[:, :TAPS]), times_conj(taps, mine)

    start = jnp.zeros((TAPS, 2, TAPS), jnp.float32)
    gram, own = lax.scan(own_step, start, jnp.arange(samples // BLOCK_LEN, dtype=jnp.int32))
    g_real, g_imag = gram[:, 0].T, gram[:, 1].T
    system = jnp.concatenate([jnp.concatenate([g_real, -g_imag], 1), jnp.concatenate([g_imag, g_real], 1)], 0)
    right = jnp.concatenate([cross[:, 0].T, cross[:, 1].T], 0)
    solved = jax.scipy.linalg.cho_solve((jnp.linalg.cholesky(system), True), right)
    b_real, b_imag = solved[:TAPS].T, solved[TAPS:].T
    mixing = jnp.concatenate([jnp.stack([b_real, b_imag], 1), jnp.stack([-b_imag, b_real], 1)], 2)
    stacked = jnp.concatenate([own[:, :, 0], own[:, :, 1]], 1)
    lagged = got - jnp.einsum("mck,qkl->qmcl", mixing, stacked, precision=HIGHEST)
    wave = jnp.asarray(doppler_table(samples // BLOCK_LEN, 0.125 / math.sqrt(samples)))
    wave = wave.reshape(2, samples // BLOCK_LEN, 2, DOPPLER)
    return jnp.einsum("qmcl,cqdk->mdlk", lagged, wave, precision=HIGHEST)


def on_device(ref_signal, surveillance, steering):
    chan_count, tm_count = lax.axis_size("chan"), lax.axis_size("tm")
    beams_local = steering.shape[1] // chan_count
    lags_local = LAGS // tm_count
    fills = (
        LANES % lags_local == 0
        and lags_local % (2 * SUBLANES) == 0
        and beams_local * lags_local == LANES * SUBLANES // 2
        and chan_count > 1
        and chan_count & (chan_count - 1) == 0
        and tm_count > 2
        and tm_count & (tm_count - 1) == 0
        and 2 * surveillance.shape[1] % LANES == 0
        and surveillance.shape[2] % (2 * BATCH * BLOCK_LEN) == 0
    )
    device = tiled_device if fills else plain_device
    return device(ref_signal, surveillance, steering)


def solution(mesh):
    placed = (P(None, "tm"), P(None, "chan", "tm"), P(None, None, "chan"))
    return jax.shard_map(
        on_device,
        mesh=mesh,
        in_specs=placed,
        out_specs=P("chan", None, "tm", None),
        check_vma=False,
    )
```

```python
import functools
import math

import jax
import jax.numpy as jnp
import numpy as np
from jax import lax
from jax.experimental import pallas as pl
from jax.experimental.pallas import tpu as pltpu
from jax.sharding import PartitionSpec as P

LAGS = 256
DOPPLER = 256
TAPS = 64
BLOCK_LEN = 256
LANES = 128
SUBLANES = 8
EDGE = 2

HIGHEST = lax.Precision.HIGHEST
VMEM_BYTES = 48 * 1024 * 1024


def params():
    return pltpu.CompilerParams(vmem_limit_bytes=VMEM_BYTES)


def cost(us):
    return pl.CostEstimate(flops=int(us * 1.15e9), bytes_accessed=0, transcendentals=0)


def halves(x):
    high = x.astype(jnp.bfloat16)
    return high, (x - high.astype(jnp.float32)).astype(jnp.bfloat16)


def dot_nt(a, b, precision=None):
    return lax.dot_general(
        a, b, (((1,), (1,)), ((), ())), precision=precision, preferred_element_type=jnp.float32
    )


def dot_split(a, b):
    (a_high, a_low), (b_high, b_low) = a, b
    left = jnp.concatenate([a_high, a_low], 1)
    right = jnp.concatenate([b_high, b_high], 0)
    return jnp.dot(left, right, preferred_element_type=jnp.float32) + jnp.dot(
        a_high, b_low, preferred_element_type=jnp.float32
    )


def row_sign(shape):
    rows = lax.broadcasted_iota(jnp.int32, shape, 0)
    return jnp.where(rows % SUBLANES < SUBLANES // 2, 1.0, -1.0).astype(jnp.float32)


def lane_sign(shape):
    lanes = lax.broadcasted_iota(jnp.int32, shape, 1)
    return jnp.where(lanes % LANES < LANES // 2, 1.0, -1.0).astype(jnp.float32)


def swap_groups(rows, groups):
    width = LANES // groups
    lane_group = lax.broadcasted_iota(jnp.int32, rows[0].shape, 1) // width
    outs = []
    for j in range(groups):
        out = rows[j]
        for i in range(groups):
            if i != j:
                moved = pltpu.roll(rows[i], (width * (i - j)) % LANES, 1)
                out = jnp.where(lane_group == i, moved, out)
        outs.append(out)
    return outs


CHUNKS = 4


def beam_kernel(
    chan_count, beams_local, w_hbm, s_hbm, ref_hbm, kept_ref, sent_ref, tiles_ref,
    w_ref, s_ref, ref_ref, w_sem, s_sem, ref_sem,
):
    me = lax.axis_index("chan")
    length = s_hbm.shape[1]
    width = length // CHUNKS
    w_copy = pltpu.make_async_copy(w_hbm, w_ref, w_sem)
    w_copy.start()
    ref_copy = pltpu.make_async_copy(ref_hbm, ref_ref, ref_sem)
    ref_copy.start()
    s_copies = []
    for n in range(CHUNKS):
        cols = pl.ds(n * width, width)
        s_copies.append(pltpu.make_async_copy(s_hbm.at[:, cols], s_ref.at[:, cols], s_sem.at[n]))
        s_copies[n].start()
    half = SUBLANES // 2
    sub = lax.broadcasted_iota(jnp.int32, (SUBLANES, w_hbm.shape[2]), 0)
    top = sub < half
    w_copy.wait()
    rows = []
    for parity in range(2):
        for e in range(parity, chan_count, 2):
            base = (me ^ e) * beams_local
            for tile in range(beams_local // SUBLANES):
                start = pl.multiple_of(base + tile * SUBLANES, SUBLANES)
                wr = w_ref[0, pl.ds(start, SUBLANES), :]
                wi = w_ref[1, pl.ds(start, SUBLANES), :]
                wr_s = pltpu.roll(wr, half, 0)
                wi_s = pltpu.roll(wi, half, 0)
                first = [jnp.where(top, wr, wi_s), jnp.where(top, -wi, wr_s)]
                second = [jnp.where(top, wr_s, wi), jnp.where(top, -wi_s, wr)]
                rows.append(jnp.concatenate(first, 1))
                rows.append(jnp.concatenate(second, 1))
    weights = halves(jnp.concatenate(rows, 0))
    ref_copy.wait()
    for c in range(2):
        for n in range(tiles_ref.shape[1]):
            tiles_ref[c, n : n + 1, :] = ref_ref[c : c + 1, n * LANES : (n + 1) * LANES]
    mid = weights[0].shape[0] // 2
    for n in range(CHUNKS):
        cols = slice(n * width, (n + 1) * width)
        s_copies[n].wait()
        product = dot_split(weights, halves(s_ref[:, cols]))
        kept_ref[:, cols] = product[:mid]
        sent_ref[:, cols] = product[mid:]


def beam_call(steering, survey, ref, chan_count, beams_local):
    depth, length = survey.shape
    rows = chan_count * beams_local
    tiles = (2, length // LANES, LANES)
    out = jax.ShapeDtypeStruct((rows, length), jnp.float32)
    hbm, vmem = pl.BlockSpec(memory_space=pltpu.HBM), pl.BlockSpec(memory_space=pltpu.VMEM)
    return pl.pallas_call(
        functools.partial(beam_kernel, chan_count, beams_local),
        in_specs=[hbm] * 3,
        out_specs=[vmem] * 3,
        out_shape=[
            out,
            out,
            jax.ShapeDtypeStruct(tiles, jnp.float32),
        ],
        scratch_shapes=[
            pltpu.VMEM(steering.shape, jnp.float32),
            pltpu.VMEM(survey.shape, jnp.float32),
            pltpu.VMEM(ref.shape, jnp.float32),
            pltpu.SemaphoreType.DMA,
            pltpu.SemaphoreType.DMA((CHUNKS,)),
            pltpu.SemaphoreType.DMA,
        ],
        compiler_params=params(),
        cost_estimate=cost(2.2),
        name="beams",
    )(*(pltpu.with_memory_space_constraint(x, pltpu.HBM) for x in (steering, survey, ref)))


def sum_kernel(count, *refs):
    kept_ref, sent_ref = refs[-2:]
    for n in range(kept_ref.shape[0]):
        for offset, out_ref in ((0, kept_ref), (1, sent_ref)):
            total = refs[0][2 * n + offset]
            for ref in refs[1:count]:
                total = total + ref[2 * n + offset]
            out_ref[n] = total


def sum_call(parts):
    shape = (parts[0].shape[0] // 2,) + parts[0].shape[1:]
    out = jax.ShapeDtypeStruct(shape, jnp.float32)
    vmem = pl.BlockSpec(memory_space=pltpu.VMEM)
    return pl.pallas_call(
        functools.partial(sum_kernel, len(parts)),
        in_specs=[vmem] * len(parts),
        out_specs=[vmem, vmem],
        out_shape=[out, out],
        compiler_params=params(),
        cost_estimate=cost(0.1),
        name="halves_summed",
    )(*parts)


def join_kernel(first_ref, second_ref, *refs):
    out_ref = refs[-1]
    count = first_ref.shape[0]
    out_ref[:count] = first_ref[...]
    out_ref[count:] = second_ref[...]


def join_call(first, second, *after):
    vmem = pl.BlockSpec(memory_space=pltpu.VMEM)
    return pl.pallas_call(
        join_kernel,
        in_specs=[vmem, vmem] + [pl.BlockSpec(memory_space=pl.ANY)] * len(after),
        out_shape=jax.ShapeDtypeStruct((2 * first.shape[0],) + first.shape[1:], jnp.float32),
        compiler_params=params(),
        cost_estimate=cost(1.0),
        name="reference_joined",
    )(first, second, *after)


def spread_line(line, keep):
    for g in range(0, LANES, 2 * SUBLANES):
        tiled = jnp.broadcast_to(line, (2 * SUBLANES, line.shape[1]))
        for h, value in enumerate(halves(pltpu.roll(tiled, g, 1, stride=1, stride_axis=0)[:, LANES:])):
            keep(h, g, value)


def table_kernel(tiles_ref, out_ref):
    for c in range(2):
        line = jnp.concatenate([tiles_ref[c, n : n + 1, :] for n in range(tiles_ref.shape[1])], 1)

        def keep(h, g, value):
            out_ref[h, c, g : g + 2 * SUBLANES] = value

        spread_line(line, keep)


def table_call(tiles):
    shape = (2, 2, LANES, LANES * (tiles.shape[1] - 1))
    return pl.pallas_call(
        table_kernel,
        out_shape=jax.ShapeDtypeStruct(shape, jnp.bfloat16),
        compiler_params=params(),
        cost_estimate=cost(0.7),
        name="shifted_reference",
    )(tiles)


def lag_kernel(groups, part_count, *refs):
    y_refs, refs = refs[:part_count], refs[part_count:]
    table_ref, tiles_ref, *round_refs, _, out_hbm, out_ref, out_sem, first_ref = refs
    copies = []

    me = lax.axis_index("tm")
    for c in range(2):
        tails = [ref[ref.shape[0] - 1, c, ref.shape[2] - EDGE :, :] for ref in round_refs]
        before = jnp.where(me % 2 == 1, tails[0], jnp.where(me > 0, tails[-1], 0.0))
        line = jnp.concatenate([before[n : n + 1] for n in range(EDGE)] + [tiles_ref[c, 0:1, :]], 1)

        def keep(h, g, value):
            first_ref[h, c, g : g + 2 * SUBLANES] = value

        spread_line(line, keep)

    def table_tile(h, n):
        parts = []
        for c in range(2):
            known = first_ref.shape[3] // LANES
            ref, at = (first_ref, n) if n < known else (table_ref, n - known)
            parts.append(ref[h, c, :, at * LANES : (at + 1) * LANES])
        return jnp.concatenate(parts, 1)

    def send(start, count):
        part = (slice(None), pl.ds(start, count))
        copies.append(pltpu.make_async_copy(out_ref.at[part], out_hbm.at[part], out_sem.at[len(copies)]))
        copies[-1].start()

    y = y_refs[0][...]
    for y_ref in y_refs[1:]:
        y = y + y_ref[...]
    rows, length = y.shape
    blocks = length // BLOCK_LEN
    turned = jnp.concatenate(
        [pltpu.roll(y[r : r + SUBLANES], SUBLANES // 2, 0) for r in range(0, rows, SUBLANES)], 0
    )
    turned = turned * row_sign(turned.shape)
    y_high, y_low = halves(y)
    t_high, t_low = halves(turned)

    def half_block(q, b):
        cols = slice(q * BLOCK_LEN + b * LANES, q * BLOCK_LEN + (b + 1) * LANES)
        return [jnp.concatenate([x[:, cols], t[:, cols]], 1) for x, t in ((y_high, t_high), (y_low, t_low))]

    def products(stack, n, count):
        high, low = (jnp.concatenate([table_tile(h, n + i) for i in range(count)], 0) for h in range(2))
        by_high = dot_nt(jnp.concatenate([part for pair in stack for part in pair], 0), high)
        by_low = dot_nt(jnp.concatenate([pair[0] for pair in stack], 0), low)
        return [
            by_high[2 * i * rows : (2 * i + 1) * rows]
            + (by_high[(2 * i + 1) * rows : 2 * (i + 1) * rows] + by_low[i * rows : (i + 1) * rows])
            for i in range(len(stack))
        ]

    taps_sum = None
    (far,) = products([half_block(0, 0)], 0, 1)
    for q in range(blocks):
        stack = [half_block(q, 0), half_block(q, 1)]
        if q + 1 < blocks:
            stack.append(half_block(q + 1, 0))
        first, second, *after = products(stack, 2 * q + 1, 2)
        product = jnp.concatenate([first[:, :LANES] + second[:, LANES:], second[:, :LANES] + far], 1)
        if after:
            far = after[0][:, LANES:]
        taps = product[:, :LANES]
        taps_sum = taps if taps_sum is None else taps_sum + taps
        for h in range(LAGS // LANES):
            lanes = slice(h * LANES, (h + 1) * LANES)
            tiles = [product[r : r + SUBLANES, lanes] for r in range(0, rows, SUBLANES)]
            for j, tile in enumerate(swap_groups(tiles, groups)):
                out_ref[h * groups + j, q] = tile
        if q % 2:
            send(q - 1, 2)
    left = lax.broadcasted_iota(jnp.int32, (SUBLANES, LANES), 1) < TAPS
    for i in range(groups // 2):
        a = taps_sum[i * SUBLANES : (i + 1) * SUBLANES]
        other = i + groups // 2
        b = taps_sum[other * SUBLANES : (other + 1) * SUBLANES]
        tile = jnp.where(left, a, pltpu.roll(b, LANES - TAPS, 1))
        for owner in range(out_ref.shape[0]):
            out_ref[owner, blocks + i] = tile
    send(blocks, groups // 2)
    for copy in copies:
        copy.wait()


def lag_call(ys, table, tiles, rounds, after, groups, owners):
    blocks = ys[0].shape[1] // BLOCK_LEN
    shape = (owners, blocks + groups // 2, SUBLANES, LANES)
    vmem = pl.BlockSpec(memory_space=pltpu.VMEM)
    return pl.pallas_call(
        functools.partial(lag_kernel, groups, len(ys)),
        in_specs=[vmem] * (len(ys) + 2 + len(rounds)) + [pl.BlockSpec(memory_space=pl.ANY)],
        out_specs=pl.BlockSpec(memory_space=pltpu.HBM),
        out_shape=jax.ShapeDtypeStruct(shape, jnp.float32),
        scratch_shapes=[
            pltpu.VMEM(shape, jnp.float32),
            pltpu.SemaphoreType.DMA((blocks // 2 + 1,)),
            pltpu.VMEM((2, 2, LANES, 2 * LANES), jnp.bfloat16),
        ],
        compiler_params=params(),
        cost_estimate=cost(2.1),
        name="lag_products",
    )(*ys, table, tiles, *rounds, after)


BATCH = 4


def own_kernel(lags_local, *refs):
    *part_refs, _, out_ref, line_ref, tail_ref, span_ref, late_ref, taps_a, lags_a, taps_b, lags_b = refs
    me = lax.axis_index("tm")
    part_rows = part_refs[0].shape[2]
    owners = sum(part_ref.shape[0] for part_ref in part_refs)
    samples = owners * part_rows * LANES
    steps = samples // BLOCK_LEN // BATCH
    total_rows = span_ref.shape[1]
    block_rows = BLOCK_LEN // LANES

    span_ref[...] = jnp.zeros_like(span_ref)
    n = 0
    for part_ref in part_refs:
        for i in range(part_ref.shape[0]):
            block = lax.rem(me - (n // 2) * 2 + owners, owners) ^ (n % 2)
            span_ref[:, pl.ds(EDGE + block * part_rows, part_rows), :] = part_ref[i]
            n += 1
    late_rows = (me * lags_local) // LANES
    late_lanes = lax.rem(me * lags_local, LANES)
    turned = [pltpu.roll(span_ref[c], late_lanes, 1) for c in range(2)]
    before = [pltpu.roll(x, 1, 0) for x in turned]
    lanes = lax.broadcasted_iota(jnp.int32, (total_rows, LANES), 1)
    for c in range(2):
        late_ref[c] = pltpu.roll(jnp.where(lanes < late_lanes, before[c], turned[c]), late_rows, 0)

    def line_of(ref, c, first, count):
        return jnp.concatenate([ref[c, pl.ds(first + n, 1), :] for n in range(count)], 1)

    def shifted(line, by):
        tiled = jnp.broadcast_to(line, (2 * SUBLANES, line.shape[1]))
        return pltpu.roll(tiled, by, 1, stride=1, stride_axis=0)[:, LANES:]

    def keep(ref, row, value):
        high, low = halves(value)
        half = ref.shape[0] // 2
        ref[row : row + 2 * SUBLANES, :] = high
        ref[half + row : half + row + 2 * SUBLANES, :] = low

    def build(n, taps_ref, lags_ref):
        first = EDGE - 1 + n * BATCH * block_rows
        count = BATCH * block_rows + 1
        lines = [line_of(span_ref, c, first, count) for c in range(2)]
        for c in range(2):
            for g in range(0, TAPS, 2 * SUBLANES):
                keep(taps_ref, c * TAPS + g, shifted(lines[c], g))
            late = line_of(late_ref, c, first, count)
            for g in range(0, lags_local, 2 * SUBLANES):
                keep(lags_ref, c * lags_local + g, shifted(late, g))
        pad = jnp.zeros((2 * SUBLANES - 2, BATCH * BLOCK_LEN), jnp.float32)
        keep(lags_ref, 2 * lags_local, jnp.concatenate([line[:, LANES:] for line in lines] + [pad], 0))

    turn = lane_sign((lags_local, LANES))

    def use(n, taps_ref, lags_ref):
        count = lags_ref.shape[0] // 2
        for b in range(BATCH):
            cols = slice(b * BLOCK_LEN, (b + 1) * BLOCK_LEN)
            product = dot_nt(lags_ref[:, cols], taps_ref[:, cols])
            product = product[:count, :LANES] + (product[:count, LANES:] + product[count:, :LANES])
            by_real = product[:lags_local]
            by_imag = product[lags_local : 2 * lags_local]
            rows = pl.ds(pl.multiple_of((n * BATCH + b) * lags_local, lags_local), lags_local)
            high, low = halves(by_real + turn * pltpu.roll(by_imag, TAPS, 1))
            out_ref[0, rows, :] = high
            out_ref[1, rows, :] = low
            line_ref[...] += product[2 * lags_local : 2 * lags_local + SUBLANES]

    line_ref[...] = jnp.zeros_like(line_ref)
    build(0, taps_a, lags_a)

    def pair(m, carry):
        build(2 * m + 1, taps_b, lags_b)
        use(2 * m, taps_a, lags_a)
        build(jnp.minimum(2 * m + 2, steps - 1), taps_a, lags_a)
        use(2 * m + 1, taps_b, lags_b)
        return carry

    lax.fori_loop(0, steps // 2, pair, 0)
    tail = []
    for c in range(2):
        line = line_of(span_ref, c, EDGE + owners * part_rows - 1, 2)
        tail += [shifted(line, g) for g in range(0, TAPS, 2 * SUBLANES)]
    tail = jnp.concatenate(tail, 0)
    tail_ref[...] = dot_nt(tail, tail, HIGHEST)


def own_call(parts, lags_local, after):
    part_rows = parts[0].shape[2]
    span_rows = part_rows * sum(part.shape[0] for part in parts)
    rows = span_rows * LANES // BLOCK_LEN * lags_local
    held_rows = -(-(span_rows + 2 * EDGE) // SUBLANES) * SUBLANES
    width = BATCH * BLOCK_LEN
    taps = pltpu.VMEM((4 * TAPS, width), jnp.bfloat16)
    lags = pltpu.VMEM((4 * lags_local + 4 * SUBLANES, width), jnp.bfloat16)
    span = pltpu.VMEM((2, held_rows, LANES), jnp.float32)
    return pl.pallas_call(
        functools.partial(own_kernel, lags_local),
        in_specs=[pl.BlockSpec(memory_space=pltpu.VMEM)] * len(parts) + [pl.BlockSpec(memory_space=pl.ANY)],
        out_shape=[
            jax.ShapeDtypeStruct((2, rows, 2 * TAPS), jnp.bfloat16),
            jax.ShapeDtypeStruct((SUBLANES, 2 * TAPS), jnp.float32),
            jax.ShapeDtypeStruct((2 * TAPS, 2 * TAPS), jnp.float32),
        ],
        scratch_shapes=[span, span, taps, lags, taps, lags],
        compiler_params=params(),
        cost_estimate=cost(6.2),
        name="reference_products",
    )(*parts, after)


def as_factor(a):
    return jnp.concatenate([a, -lane_sign(a.shape) * pltpu.roll(a, a.shape[0], 1)], 0)


def solver_kernel(line_ref, tail_ref, gram_ref, solver_ref):
    total = line_ref[...]
    line = total[0:1] + lane_sign((1, LANES)) * pltpu.roll(total[1:2], TAPS, 1)
    low = lax.broadcasted_iota(jnp.int32, (1, LANES), 1) < TAPS
    line_r = jnp.where(low, line, 0.0)
    line_i = jnp.where(low, pltpu.roll(line, TAPS, 1), 0.0)
    cols = lax.broadcasted_iota(jnp.int32, (TAPS, TAPS), 1)
    rows = lax.broadcasted_iota(jnp.int32, (TAPS, TAPS), 0)
    above = cols > rows

    def upper(x):
        spread = pltpu.roll(jnp.broadcast_to(x, (TAPS, LANES)), 0, 1, stride=1, stride_axis=0)
        return spread[:, :TAPS]

    up_r = upper(line_r)
    up_i = jnp.where(above, upper(line_i), 0.0)
    strict_r = jnp.where(above, up_r, 0.0)
    diag_r = jnp.where(cols == rows, up_r, 0.0)
    tails = tail_ref[...]
    gram_r = strict_r + strict_r.T + diag_r - (tails[:TAPS, :TAPS] + tails[TAPS:, TAPS:])
    gram_i = up_i - up_i.T - (tails[:TAPS, TAPS:] - tails[TAPS:, :TAPS])
    gram = jnp.concatenate([gram_r, gram_i], 1)
    gram_halves = halves(as_factor(gram))
    gram_ref[0], gram_ref[1] = gram_halves
    one = (
        lax.broadcasted_iota(jnp.int32, gram.shape, 0) == lax.broadcasted_iota(jnp.int32, gram.shape, 1)
    ).astype(jnp.float32)
    bound = jnp.max(jnp.sum(jnp.abs(gram), axis=1, keepdims=True), axis=0, keepdims=True)

    def again(state):
        count, left, _ = state
        return (count < 60) & (left > 1e-3)

    def newton(state):
        count, _, x = state
        x_halves = halves(x)
        seen = dot_split(x_halves, gram_halves)
        left = jnp.max(jnp.abs(seen - one))
        x = 2.0 * x - dot_split(halves(seen), halves(as_factor(x)))
        return count + 1, left, x

    start = (jnp.int32(0), jnp.float32(1.0), one * (1.0 / bound))
    _, _, inverse = lax.while_loop(again, newton, start)
    solver_ref[0], solver_ref[1] = halves(as_factor(inverse))


def solver_call(line, tail):
    out = jax.ShapeDtypeStruct((2,) + tail.shape, jnp.bfloat16)
    return pl.pallas_call(
        solver_kernel,
        out_shape=[out, out],
        compiler_params=params(),
        cost_estimate=cost(2.0),
        name="gram_inverse",
    )(line, tail)


def doppler_table(block_count, scale):
    phase = (np.arange(block_count)[:, None] * np.arange(DOPPLER)[None, :] % DOPPLER) * (2.0 * math.pi / DOPPLER)
    cosine, sine = np.cos(phase), np.sin(phase)
    upper = np.concatenate([cosine, -sine], 1)
    lower = np.concatenate([sine, cosine], 1)
    return (np.concatenate([upper, lower], 0) * scale).astype(np.float32)


def map_kernel(groups, got_ref, own_ref, gram_ref, solver_ref, wave_ref, out_hbm, held_ref, out_ref, out_sem):
    owners, pieces = got_ref.shape[:2]
    blocks = pieces - groups // 2
    lags_local = LANES // groups
    total = owners * blocks
    left = lax.broadcasted_iota(jnp.int32, (SUBLANES, LANES), 1) < TAPS
    sign = row_sign((SUBLANES, LANES))
    rows = [None] * groups
    for i in range(groups // 2):
        tile = got_ref[0, blocks + i]
        for owner in range(1, owners):
            tile = tile + got_ref[owner, blocks + i]
        swapped = pltpu.roll(tile, TAPS, 1)
        for part, here, there in ((i, tile, swapped), (i + groups // 2, swapped, tile)):
            other = -sign * pltpu.roll(there, SUBLANES // 2, 0)
            rows[part] = jnp.where(left, here, other)
    cross = jnp.concatenate(rows, 0)
    solver = (solver_ref[0], solver_ref[1])
    taps = dot_split(halves(cross), solver)
    rest = cross - dot_split(halves(taps), (gram_ref[0], gram_ref[1]))
    taps = taps + dot_split(halves(rest), solver)
    taps_high, taps_low = halves(taps)
    taps_both = jnp.concatenate([taps_high, taps_low], 1)
    for q in range(0, total, 2 * groups):
        own = slice(q * lags_local, (q + 2 * groups) * lags_local)
        own_high = own_ref[0, own, :]
        clutter = dot_nt(taps_both, jnp.concatenate([own_high, own_high], 1)) + dot_nt(taps_high, own_ref[1, own, :])
        for h in range(2):
            lanes = slice(h * LANES, (h + 1) * LANES)
            tiles = [clutter[r : r + SUBLANES, lanes] for r in range(0, groups * SUBLANES, SUBLANES)]
            for j, tile in enumerate(swap_groups(tiles, groups)):
                at = q + h * groups + j
                held_ref[at * SUBLANES : (at + 1) * SUBLANES, :] = got_ref[at // blocks, at % blocks] - tile
    half = SUBLANES // 2
    wave = (wave_ref[0], wave_ref[1])
    copies = []
    for first in range(0, half, 2):
        lagged = []
        for g in (first, first + 1):
            parts = [held_ref[pl.ds(c * half + g, total, stride=SUBLANES), :] for c in range(2)]
            lagged.append(jnp.concatenate(parts, 0).T)
        spectrum = dot_split(halves(jnp.concatenate(lagged, 0)), wave)
        for n in range(2 * groups):
            beam = half * (n % groups) + first + n // groups
            for c in range(2):
                out_ref[beam, c] = spectrum[n * lags_local : (n + 1) * lags_local, c * DOPPLER : (c + 1) * DOPPLER]
            copies.append(pltpu.make_async_copy(out_ref.at[beam], out_hbm.at[beam], out_sem.at[beam]))
            copies[-1].start()
    for copy in copies:
        copy.wait()


def map_call(got, own, gram, solver, wave, groups, beams_local):
    total = got.shape[0] * (got.shape[1] - groups // 2)
    lags_local = LANES // groups
    shape = (beams_local, 2, lags_local, DOPPLER)
    return pl.pallas_call(
        functools.partial(map_kernel, groups),
        in_specs=[pl.BlockSpec(memory_space=pltpu.VMEM)] * 5,
        out_specs=pl.BlockSpec(memory_space=pltpu.HBM),
        out_shape=jax.ShapeDtypeStruct(shape, jnp.float32),
        scratch_shapes=[
            pltpu.VMEM((total * SUBLANES, LANES), jnp.float32),
            pltpu.VMEM(shape, jnp.float32),
            pltpu.SemaphoreType.DMA((beams_local,)),
        ],
        compiler_params=params(),
        cost_estimate=cost(2.5),
        name="range_doppler",
    )(got, own, gram, solver, wave)


def swap(x, axis, by):
    pairs = [(i, i ^ by) for i in range(lax.axis_size(axis))]
    return lax.ppermute(x, axis, pairs)


def tiled_device(ref_signal, surveillance, steering):
    chan_count, tm_count = lax.axis_size("chan"), lax.axis_size("tm")
    channels, length = surveillance.shape[1:]
    beams_local = steering.shape[1] // chan_count
    lags_local = LAGS // tm_count
    groups = LANES // lags_local
    samples = length * tm_count

    survey = surveillance.reshape(2 * channels, length)
    kept, moved, tiles = beam_call(steering, survey, ref_signal, chan_count, beams_local)
    near = swap(tiles[None], "tm", 1)
    shape = (chan_count // 2, 2 * beams_local, length)
    kept, got = kept.reshape(shape), swap(moved, "chan", 1).reshape(shape)
    by = 2
    while by < chan_count:
        kept, moved = sum_call([kept, got])
        got = swap(moved, "chan", by)
        by *= 2
    rounds = [near]
    joined = join_call(tiles[None], near, moved)
    while True:
        count = joined.shape[0]
        rounds.append(lax.ppermute(joined, "tm", [(i, (i + count) % tm_count) for i in range(tm_count)]))
        if count * 2 == tm_count:
            break
        joined = join_call(joined, rounds[-1])
    table = table_call(tiles)
    pieces = lag_call([kept[0], got[0]], table, tiles, rounds[:2], joined, groups, tm_count)
    got = lax.all_to_all(pieces, "tm", 0, 0, tiled=True)
    own, line, tail = own_call([tiles[None]] + rounds, lags_local, pieces)
    gram, solver = solver_call(line, tail)
    wave = doppler_table(samples // BLOCK_LEN, 0.125 / math.sqrt(samples))
    high = wave.astype(jnp.bfloat16)
    wave = np.stack([high, (wave - high.astype(np.float32)).astype(jnp.bfloat16)])
    return map_call(got, own, gram, solver, jnp.asarray(wave), groups, beams_local)


def lag_table(ref_ext, offset, lags):
    window = lax.dynamic_slice_in_dim(ref_ext, offset, BLOCK_LEN + LAGS, 1)
    span = BLOCK_LEN + LAGS
    tiled = jnp.tile(jnp.pad(window, ((0, 0), (0, 1))), (1, lags))[:, : lags * span]
    return tiled.reshape(2, lags, span)[:, :, LAGS:]


def times_conj(a, b):
    real = jnp.einsum("...t,lt->...l", a[..., 0, :], b[0], precision=HIGHEST) + jnp.einsum(
        "...t,lt->...l", a[..., 1, :], b[1], precision=HIGHEST
    )
    imag = jnp.einsum("...t,lt->...l", a[..., 1, :], b[0], precision=HIGHEST) - jnp.einsum(
        "...t,lt->...l", a[..., 0, :], b[1], precision=HIGHEST
    )
    return jnp.stack([real, imag], -2)


def plain_device(ref_signal, surveillance, steering):
    chan_count, tm_count = lax.axis_size("chan"), lax.axis_size("tm")
    length = surveillance.shape[2]
    beams = steering.shape[1]
    lags_local = LAGS // tm_count
    samples = length * tm_count
    local_blocks = length // BLOCK_LEN
    here = lax.axis_index("tm")

    w_real, w_imag = steering
    real = jnp.dot(w_real, surveillance[0], precision=HIGHEST) - jnp.dot(w_imag, surveillance[1], precision=HIGHEST)
    imag = jnp.dot(w_imag, surveillance[0], precision=HIGHEST) + jnp.dot(w_real, surveillance[1], precision=HIGHEST)
    beam = lax.psum_scatter(jnp.stack([real, imag], 1), "chan", scatter_dimension=0, tiled=True)
    ref_all = lax.all_gather(ref_signal, "tm", axis=1, tiled=True)
    ref_ext = jnp.pad(ref_all, ((0, 0), (LAGS, 0)))

    def beam_step(carry, q):
        offset = q * BLOCK_LEN
        table = lag_table(ref_ext, here * length + offset, LAGS)
        segment = lax.dynamic_slice_in_dim(beam, offset, BLOCK_LEN, 2)
        return carry, times_conj(segment, table)

    _, products = lax.scan(beam_step, None, jnp.arange(local_blocks, dtype=jnp.int32))
    cross = lax.psum(products[..., :TAPS].sum(0), "tm")
    got = lax.all_to_all(products, "tm", 3, 0, tiled=True)

    def own_step(gram, q):
        offset = q * BLOCK_LEN
        table = lag_table(ref_ext, offset, LAGS)
        taps = table[:, :TAPS].transpose(1, 0, 2)
        mine = lax.dynamic_slice_in_dim(table, here * lags_local, lags_local, 1)
        return gram + times_conj(taps, table[:, :TAPS]), times_conj(taps, mine)

    start = jnp.zeros((TAPS, 2, TAPS), jnp.float32)
    gram, own = lax.scan(own_step, start, jnp.arange(samples // BLOCK_LEN, dtype=jnp.int32))
    g_real, g_imag = gram[:, 0].T, gram[:, 1].T
    system = jnp.concatenate([jnp.concatenate([g_real, -g_imag], 1), jnp.concatenate([g_imag, g_real], 1)], 0)
    right = jnp.concatenate([cross[:, 0].T, cross[:, 1].T], 0)
    solved = jax.scipy.linalg.cho_solve((jnp.linalg.cholesky(system), True), right)
    b_real, b_imag = solved[:TAPS].T, solved[TAPS:].T
    mixing = jnp.concatenate([jnp.stack([b_real, b_imag], 1), jnp.stack([-b_imag, b_real], 1)], 2)
    stacked = jnp.concatenate([own[:, :, 0], own[:, :, 1]], 1)
    lagged = got - jnp.einsum("mck,qkl->qmcl", mixing, stacked, precision=HIGHEST)
    wave = jnp.asarray(doppler_table(samples // BLOCK_LEN, 0.125 / math.sqrt(samples)))
    wave = wave.reshape(2, samples // BLOCK_LEN, 2, DOPPLER)
    return jnp.einsum("qmcl,cqdk->mdlk", lagged, wave, precision=HIGHEST)


def on_device(ref_signal, surveillance, steering):
    chan_count, tm_count = lax.axis_size("chan"), lax.axis_size("tm")
    beams_local = steering.shape[1] // chan_count
    lags_local = LAGS // tm_count
    fills = (
        LANES % lags_local == 0
        and lags_local % (2 * SUBLANES) == 0
        and beams_local * lags_local == LANES * SUBLANES // 2
        and chan_count > 1
        and chan_count & (chan_count - 1) == 0
        and tm_count > 2
        and tm_count & (tm_count - 1) == 0
        and 2 * surveillance.shape[1] % LANES == 0
        and surveillance.shape[2] % (2 * BATCH * BLOCK_LEN) == 0
    )
    device = tiled_device if fills else plain_device
    return device(ref_signal, surveillance, steering)


def solution(mesh):
    placed = (P(None, "tm"), P(None, "chan", "tm"), P(None, None, "chan"))
    return jax.shard_map(
        on_device,
        mesh=mesh,
        in_specs=placed,
        out_specs=P("chan", None, "tm", None),
        check_vma=False,
    )
```

```python
import functools
import math

import jax
import jax.numpy as jnp
import numpy as np
from jax import lax
from jax.experimental import pallas as pl
from jax.experimental.pallas import tpu as pltpu
from jax.sharding import PartitionSpec as P

LAGS = 256
DOPPLER = 256
TAPS = 64
BLOCK_LEN = 256
LANES = 128
SUBLANES = 8
EDGE = 2

HIGHEST = lax.Precision.HIGHEST
VMEM_BYTES = 48 * 1024 * 1024


def params():
    return pltpu.CompilerParams(vmem_limit_bytes=VMEM_BYTES)


def cost(us):
    return pl.CostEstimate(flops=int(us * 1.15e9), bytes_accessed=0, transcendentals=0)


def halves(x):
    high = x.astype(jnp.bfloat16)
    return high, (x - high.astype(jnp.float32)).astype(jnp.bfloat16)


def dot_nt(a, b, precision=None):
    return lax.dot_general(
        a, b, (((1,), (1,)), ((), ())), precision=precision, preferred_element_type=jnp.float32
    )


def dot_split(a, b):
    (a_high, a_low), (b_high, b_low) = a, b
    left = jnp.concatenate([a_high, a_low], 1)
    right = jnp.concatenate([b_high, b_high], 0)
    return jnp.dot(left, right, preferred_element_type=jnp.float32) + jnp.dot(
        a_high, b_low, preferred_element_type=jnp.float32
    )


def row_sign(shape):
    rows = lax.broadcasted_iota(jnp.int32, shape, 0)
    return jnp.where(rows % SUBLANES < SUBLANES // 2, 1.0, -1.0).astype(jnp.float32)


def lane_sign(shape):
    lanes = lax.broadcasted_iota(jnp.int32, shape, 1)
    return jnp.where(lanes % LANES < LANES // 2, 1.0, -1.0).astype(jnp.float32)


def swap_groups(rows, groups):
    width = LANES // groups
    lane_group = lax.broadcasted_iota(jnp.int32, rows[0].shape, 1) // width
    outs = []
    for j in range(groups):
        out = rows[j]
        for i in range(groups):
            if i != j:
                moved = pltpu.roll(rows[i], (width * (i - j)) % LANES, 1)
                out = jnp.where(lane_group == i, moved, out)
        outs.append(out)
    return outs


CHUNKS = 4


def beam_kernel(
    chan_count, beams_local, w_hbm, s_hbm, ref_hbm, kept_ref, sent_ref, tiles_ref,
    w_ref, s_ref, ref_ref, w_sem, s_sem, ref_sem,
):
    me = lax.axis_index("chan")
    length = s_hbm.shape[1]
    width = length // CHUNKS
    w_copy = pltpu.make_async_copy(w_hbm, w_ref, w_sem)
    w_copy.start()
    ref_copy = pltpu.make_async_copy(ref_hbm, ref_ref, ref_sem)
    ref_copy.start()
    s_copies = []
    for n in range(CHUNKS):
        cols = pl.ds(n * width, width)
        s_copies.append(pltpu.make_async_copy(s_hbm.at[:, cols], s_ref.at[:, cols], s_sem.at[n]))
        s_copies[n].start()
    half = SUBLANES // 2
    sub = lax.broadcasted_iota(jnp.int32, (SUBLANES, w_hbm.shape[2]), 0)
    top = sub < half
    w_copy.wait()
    rows = []
    for parity in range(2):
        for e in range(parity, chan_count, 2):
            base = (me ^ e) * beams_local
            for tile in range(beams_local // SUBLANES):
                start = pl.multiple_of(base + tile * SUBLANES, SUBLANES)
                wr = w_ref[0, pl.ds(start, SUBLANES), :]
                wi = w_ref[1, pl.ds(start, SUBLANES), :]
                wr_s = pltpu.roll(wr, half, 0)
                wi_s = pltpu.roll(wi, half, 0)
                first = [jnp.where(top, wr, wi_s), jnp.where(top, -wi, wr_s)]
                second = [jnp.where(top, wr_s, wi), jnp.where(top, -wi_s, wr)]
                rows.append(jnp.concatenate(first, 1))
                rows.append(jnp.concatenate(second, 1))
    weights = halves(jnp.concatenate(rows, 0))
    ref_copy.wait()
    for c in range(2):
        for n in range(tiles_ref.shape[1]):
            tiles_ref[c, n : n + 1, :] = ref_ref[c : c + 1, n * LANES : (n + 1) * LANES]
    mid = weights[0].shape[0] // 2
    for n in range(CHUNKS):
        cols = slice(n * width, (n + 1) * width)
        s_copies[n].wait()
        product = dot_split(weights, halves(s_ref[:, cols]))
        kept_ref[:, cols] = product[:mid]
        sent_ref[:, cols] = product[mid:]


def beam_call(steering, survey, ref, chan_count, beams_local):
    depth, length = survey.shape
    rows = chan_count * beams_local
    tiles = (2, length // LANES, LANES)
    out = jax.ShapeDtypeStruct((rows, length), jnp.float32)
    hbm, vmem = pl.BlockSpec(memory_space=pltpu.HBM), pl.BlockSpec(memory_space=pltpu.VMEM)
    return pl.pallas_call(
        functools.partial(beam_kernel, chan_count, beams_local),
        in_specs=[hbm] * 3,
        out_specs=[vmem] * 3,
        out_shape=[
            out,
            out,
            jax.ShapeDtypeStruct(tiles, jnp.float32),
        ],
        scratch_shapes=[
            pltpu.VMEM(steering.shape, jnp.float32),
            pltpu.VMEM(survey.shape, jnp.float32),
            pltpu.VMEM(ref.shape, jnp.float32),
            pltpu.SemaphoreType.DMA,
            pltpu.SemaphoreType.DMA((CHUNKS,)),
            pltpu.SemaphoreType.DMA,
        ],
        compiler_params=params(),
        cost_estimate=cost(2.2),
        name="beams",
    )(*(pltpu.with_memory_space_constraint(x, pltpu.HBM) for x in (steering, survey, ref)))


def sum_kernel(count, *refs):
    kept_ref, sent_ref = refs[-2:]
    for n in range(kept_ref.shape[0]):
        for offset, out_ref in ((0, kept_ref), (1, sent_ref)):
            total = refs[0][2 * n + offset]
            for ref in refs[1:count]:
                total = total + ref[2 * n + offset]
            out_ref[n] = total


def sum_call(parts):
    shape = (parts[0].shape[0] // 2,) + parts[0].shape[1:]
    out = jax.ShapeDtypeStruct(shape, jnp.float32)
    vmem = pl.BlockSpec(memory_space=pltpu.VMEM)
    return pl.pallas_call(
        functools.partial(sum_kernel, len(parts)),
        in_specs=[vmem] * len(parts),
        out_specs=[vmem, vmem],
        out_shape=[out, out],
        compiler_params=params(),
        cost_estimate=cost(0.1),
        name="halves_summed",
    )(*parts)


def join_kernel(first_ref, second_ref, *refs):
    out_ref = refs[-1]
    count = first_ref.shape[0]
    out_ref[:count] = first_ref[...]
    out_ref[count:] = second_ref[...]


def join_call(first, second, *after):
    vmem = pl.BlockSpec(memory_space=pltpu.VMEM)
    return pl.pallas_call(
        join_kernel,
        in_specs=[vmem, vmem] + [pl.BlockSpec(memory_space=pl.ANY)] * len(after),
        out_shape=jax.ShapeDtypeStruct((2 * first.shape[0],) + first.shape[1:], jnp.float32),
        compiler_params=params(),
        cost_estimate=cost(1.0),
        name="reference_joined",
    )(first, second, *after)


def spread_line(line, keep):
    for g in range(0, LANES, 2 * SUBLANES):
        tiled = jnp.broadcast_to(line, (2 * SUBLANES, line.shape[1]))
        for h, value in enumerate(halves(pltpu.roll(tiled, g, 1, stride=1, stride_axis=0)[:, LANES:])):
            keep(h, g, value)


def table_kernel(tiles_ref, out_ref):
    for c in range(2):
        line = jnp.concatenate([tiles_ref[c, n : n + 1, :] for n in range(tiles_ref.shape[1])], 1)

        def keep(h, g, value):
            out_ref[h, c, g : g + 2 * SUBLANES] = value

        spread_line(line, keep)


def table_call(tiles):
    shape = (2, 2, LANES, LANES * (tiles.shape[1] - 1))
    return pl.pallas_call(
        table_kernel,
        out_shape=jax.ShapeDtypeStruct(shape, jnp.bfloat16),
        compiler_params=params(),
        cost_estimate=cost(0.7),
        name="shifted_reference",
    )(tiles)


def lag_kernel(groups, part_count, *refs):
    y_refs, refs = refs[:part_count], refs[part_count:]
    table_ref, tiles_ref, *round_refs, _, out_hbm, out_ref, out_sem, first_ref = refs
    copies = []

    me = lax.axis_index("tm")
    for c in range(2):
        tails = [ref[ref.shape[0] - 1, c, ref.shape[2] - EDGE :, :] for ref in round_refs]
        before = jnp.where(me % 2 == 1, tails[0], jnp.where(me > 0, tails[-1], 0.0))
        line = jnp.concatenate([before[n : n + 1] for n in range(EDGE)] + [tiles_ref[c, 0:1, :]], 1)

        def keep(h, g, value):
            first_ref[h, c, g : g + 2 * SUBLANES] = value

        spread_line(line, keep)

    def table_tile(h, n):
        parts = []
        for c in range(2):
            known = first_ref.shape[3] // LANES
            ref, at = (first_ref, n) if n < known else (table_ref, n - known)
            parts.append(ref[h, c, :, at * LANES : (at + 1) * LANES])
        return jnp.concatenate(parts, 1)

    def send(start, count):
        part = (slice(None), pl.ds(start, count))
        copies.append(pltpu.make_async_copy(out_ref.at[part], out_hbm.at[part], out_sem.at[len(copies)]))
        copies[-1].start()

    y = y_refs[0][...]
    for y_ref in y_refs[1:]:
        y = y + y_ref[...]
    rows, length = y.shape
    blocks = length // BLOCK_LEN
    turned = jnp.concatenate(
        [pltpu.roll(y[r : r + SUBLANES], SUBLANES // 2, 0) for r in range(0, rows, SUBLANES)], 0
    )
    turned = turned * row_sign(turned.shape)
    y_high, y_low = halves(y)
    t_high, t_low = halves(turned)

    def half_block(q, b):
        cols = slice(q * BLOCK_LEN + b * LANES, q * BLOCK_LEN + (b + 1) * LANES)
        return [jnp.concatenate([x[:, cols], t[:, cols]], 1) for x, t in ((y_high, t_high), (y_low, t_low))]

    def products(stack, n, count):
        high, low = (jnp.concatenate([table_tile(h, n + i) for i in range(count)], 0) for h in range(2))
        by_high = dot_nt(jnp.concatenate([part for pair in stack for part in pair], 0), high)
        by_low = dot_nt(jnp.concatenate([pair[0] for pair in stack], 0), low)
        return [
            by_high[2 * i * rows : (2 * i + 1) * rows]
            + (by_high[(2 * i + 1) * rows : 2 * (i + 1) * rows] + by_low[i * rows : (i + 1) * rows])
            for i in range(len(stack))
        ]

    taps_sum = None
    (far,) = products([half_block(0, 0)], 0, 1)
    for q in range(blocks):
        stack = [half_block(q, 0), half_block(q, 1)]
        if q + 1 < blocks:
            stack.append(half_block(q + 1, 0))
        first, second, *after = products(stack, 2 * q + 1, 2)
        product = jnp.concatenate([first[:, :LANES] + second[:, LANES:], second[:, :LANES] + far], 1)
        if after:
            far = after[0][:, LANES:]
        taps = product[:, :LANES]
        taps_sum = taps if taps_sum is None else taps_sum + taps
        for h in range(LAGS // LANES):
            lanes = slice(h * LANES, (h + 1) * LANES)
            tiles = [product[r : r + SUBLANES, lanes] for r in range(0, rows, SUBLANES)]
            for j, tile in enumerate(swap_groups(tiles, groups)):
                out_ref[h * groups + j, q] = tile
        if q % 2:
            send(q - 1, 2)
    left = lax.broadcasted_iota(jnp.int32, (SUBLANES, LANES), 1) < TAPS
    for i in range(groups // 2):
        a = taps_sum[i * SUBLANES : (i + 1) * SUBLANES]
        other = i + groups // 2
        b = taps_sum[other * SUBLANES : (other + 1) * SUBLANES]
        tile = jnp.where(left, a, pltpu.roll(b, LANES - TAPS, 1))
        for owner in range(out_ref.shape[0]):
            out_ref[owner, blocks + i] = tile
    send(blocks, groups // 2)
    for copy in copies:
        copy.wait()


def lag_call(ys, table, tiles, rounds, after, groups, owners):
    blocks = ys[0].shape[1] // BLOCK_LEN
    shape = (owners, blocks + groups // 2, SUBLANES, LANES)
    vmem = pl.BlockSpec(memory_space=pltpu.VMEM)
    return pl.pallas_call(
        functools.partial(lag_kernel, groups, len(ys)),
        in_specs=[vmem] * (len(ys) + 2 + len(rounds)) + [pl.BlockSpec(memory_space=pl.ANY)],
        out_specs=pl.BlockSpec(memory_space=pltpu.HBM),
        out_shape=jax.ShapeDtypeStruct(shape, jnp.float32),
        scratch_shapes=[
            pltpu.VMEM(shape, jnp.float32),
            pltpu.SemaphoreType.DMA((blocks // 2 + 1,)),
            pltpu.VMEM((2, 2, LANES, 2 * LANES), jnp.bfloat16),
        ],
        compiler_params=params(),
        cost_estimate=cost(2.1),
        name="lag_products",
    )(*ys, table, tiles, *rounds, after)


BATCH = 4


def own_kernel(lags_local, *refs):
    *part_refs, _, out_ref, line_ref, tail_ref, span_ref, late_ref, taps_a, lags_a, taps_b, lags_b = refs
    me = lax.axis_index("tm")
    part_rows = part_refs[0].shape[2]
    owners = sum(part_ref.shape[0] for part_ref in part_refs)
    samples = owners * part_rows * LANES
    steps = samples // BLOCK_LEN // BATCH
    total_rows = span_ref.shape[1]
    block_rows = BLOCK_LEN // LANES

    span_ref[...] = jnp.zeros_like(span_ref)
    n = 0
    for part_ref in part_refs:
        for i in range(part_ref.shape[0]):
            block = lax.rem(me - (n // 2) * 2 + owners, owners) ^ (n % 2)
            span_ref[:, pl.ds(EDGE + block * part_rows, part_rows), :] = part_ref[i]
            n += 1
    late_rows = (me * lags_local) // LANES
    late_lanes = lax.rem(me * lags_local, LANES)
    turned = [pltpu.roll(span_ref[c], late_lanes, 1) for c in range(2)]
    before = [pltpu.roll(x, 1, 0) for x in turned]
    lanes = lax.broadcasted_iota(jnp.int32, (total_rows, LANES), 1)
    for c in range(2):
        late_ref[c] = pltpu.roll(jnp.where(lanes < late_lanes, before[c], turned[c]), late_rows, 0)

    def line_of(ref, c, first, count):
        return jnp.concatenate([ref[c, pl.ds(first + n, 1), :] for n in range(count)], 1)

    def shifted(line, by):
        tiled = jnp.broadcast_to(line, (2 * SUBLANES, line.shape[1]))
        return pltpu.roll(tiled, by, 1, stride=1, stride_axis=0)[:, LANES:]

    def keep(ref, row, value):
        high, low = halves(value)
        half = ref.shape[0] // 2
        ref[row : row + 2 * SUBLANES, :] = high
        ref[half + row : half + row + 2 * SUBLANES, :] = low

    def build(n, taps_ref, lags_ref):
        first = EDGE - 1 + n * BATCH * block_rows
        count = BATCH * block_rows + 1
        lines = [line_of(span_ref, c, first, count) for c in range(2)]
        for c in range(2):
            for g in range(0, TAPS, 2 * SUBLANES):
                keep(taps_ref, c * TAPS + g, shifted(lines[c], g))
            late = line_of(late_ref, c, first, count)
            for g in range(0, lags_local, 2 * SUBLANES):
                keep(lags_ref, c * lags_local + g, shifted(late, g))
        pad = jnp.zeros((2 * SUBLANES - 2, BATCH * BLOCK_LEN), jnp.float32)
        keep(lags_ref, 2 * lags_local, jnp.concatenate([line[:, LANES:] for line in lines] + [pad], 0))

    turn = lane_sign((lags_local, LANES))

    def use(n, taps_ref, lags_ref):
        count = lags_ref.shape[0] // 2
        for b in range(BATCH):
            cols = slice(b * BLOCK_LEN, (b + 1) * BLOCK_LEN)
            product = dot_nt(lags_ref[:, cols], taps_ref[:, cols])
            product = product[:count, :LANES] + (product[:count, LANES:] + product[count:, :LANES])
            by_real = product[:lags_local]
            by_imag = product[lags_local : 2 * lags_local]
            rows = pl.ds(pl.multiple_of((n * BATCH + b) * lags_local, lags_local), lags_local)
            high, low = halves(by_real + turn * pltpu.roll(by_imag, TAPS, 1))
            out_ref[0, rows, :] = high
            out_ref[1, rows, :] = low
            line_ref[...] += product[2 * lags_local : 2 * lags_local + SUBLANES]

    line_ref[...] = jnp.zeros_like(line_ref)
    build(0, taps_a, lags_a)

    def pair(m, carry):
        build(2 * m + 1, taps_b, lags_b)
        use(2 * m, taps_a, lags_a)
        build(jnp.minimum(2 * m + 2, steps - 1), taps_a, lags_a)
        use(2 * m + 1, taps_b, lags_b)
        return carry

    lax.fori_loop(0, steps // 2, pair, 0)
    tail = []
    for c in range(2):
        line = line_of(span_ref, c, EDGE + owners * part_rows - 1, 2)
        tail += [shifted(line, g) for g in range(0, TAPS, 2 * SUBLANES)]
    tail = jnp.concatenate(tail, 0)
    tail_ref[...] = dot_nt(tail, tail, HIGHEST)


def own_call(parts, lags_local, after):
    part_rows = parts[0].shape[2]
    span_rows = part_rows * sum(part.shape[0] for part in parts)
    rows = span_rows * LANES // BLOCK_LEN * lags_local
    held_rows = -(-(span_rows + 2 * EDGE) // SUBLANES) * SUBLANES
    width = BATCH * BLOCK_LEN
    taps = pltpu.VMEM((4 * TAPS, width), jnp.bfloat16)
    lags = pltpu.VMEM((4 * lags_local + 4 * SUBLANES, width), jnp.bfloat16)
    span = pltpu.VMEM((2, held_rows, LANES), jnp.float32)
    return pl.pallas_call(
        functools.partial(own_kernel, lags_local),
        in_specs=[pl.BlockSpec(memory_space=pltpu.VMEM)] * len(parts) + [pl.BlockSpec(memory_space=pl.ANY)],
        out_shape=[
            jax.ShapeDtypeStruct((2, rows, 2 * TAPS), jnp.bfloat16),
            jax.ShapeDtypeStruct((SUBLANES, 2 * TAPS), jnp.float32),
            jax.ShapeDtypeStruct((2 * TAPS, 2 * TAPS), jnp.float32),
        ],
        scratch_shapes=[span, span, taps, lags, taps, lags],
        compiler_params=params(),
        cost_estimate=cost(6.2),
        name="reference_products",
    )(*parts, after)


def as_factor(a):
    return jnp.concatenate([a, -lane_sign(a.shape) * pltpu.roll(a, a.shape[0], 1)], 0)


def solver_kernel(line_ref, tail_ref, gram_ref, solver_ref):
    total = line_ref[...]
    line = total[0:1] + lane_sign((1, LANES)) * pltpu.roll(total[1:2], TAPS, 1)
    low = lax.broadcasted_iota(jnp.int32, (1, LANES), 1) < TAPS
    line_r = jnp.where(low, line, 0.0)
    line_i = jnp.where(low, pltpu.roll(line, TAPS, 1), 0.0)
    cols = lax.broadcasted_iota(jnp.int32, (TAPS, TAPS), 1)
    rows = lax.broadcasted_iota(jnp.int32, (TAPS, TAPS), 0)
    above = cols > rows

    def upper(x):
        spread = pltpu.roll(jnp.broadcast_to(x, (TAPS, LANES)), 0, 1, stride=1, stride_axis=0)
        return spread[:, :TAPS]

    up_r = upper(line_r)
    up_i = jnp.where(above, upper(line_i), 0.0)
    strict_r = jnp.where(above, up_r, 0.0)
    diag_r = jnp.where(cols == rows, up_r, 0.0)
    tails = tail_ref[...]
    gram_r = strict_r + strict_r.T + diag_r - (tails[:TAPS, :TAPS] + tails[TAPS:, TAPS:])
    gram_i = up_i - up_i.T - (tails[:TAPS, TAPS:] - tails[TAPS:, :TAPS])
    gram = jnp.concatenate([gram_r, gram_i], 1)
    gram_halves = halves(as_factor(gram))
    gram_ref[0], gram_ref[1] = gram_halves
    one = (
        lax.broadcasted_iota(jnp.int32, gram.shape, 0) == lax.broadcasted_iota(jnp.int32, gram.shape, 1)
    ).astype(jnp.float32)
    bound = jnp.max(jnp.sum(jnp.abs(gram), axis=1, keepdims=True), axis=0, keepdims=True)

    def again(state):
        count, left, _ = state
        return (count < 60) & (left > 1e-3)

    def newton(state):
        count, _, x = state
        x_halves = halves(x)
        seen = dot_split(x_halves, gram_halves)
        left = jnp.max(jnp.abs(seen - one))
        x = 2.0 * x - dot_split(halves(seen), halves(as_factor(x)))
        return count + 1, left, x

    start = (jnp.int32(0), jnp.float32(1.0), one * (1.0 / bound))
    _, _, inverse = lax.while_loop(again, newton, start)
    solver_ref[0], solver_ref[1] = halves(as_factor(inverse))


def solver_call(line, tail):
    out = jax.ShapeDtypeStruct((2,) + tail.shape, jnp.bfloat16)
    return pl.pallas_call(
        solver_kernel,
        out_shape=[out, out],
        compiler_params=params(),
        cost_estimate=cost(2.0),
        name="gram_inverse",
    )(line, tail)


def doppler_table(block_count, scale):
    phase = (np.arange(block_count)[:, None] * np.arange(DOPPLER)[None, :] % DOPPLER) * (2.0 * math.pi / DOPPLER)
    cosine, sine = np.cos(phase), np.sin(phase)
    upper = np.concatenate([cosine, -sine], 1)
    lower = np.concatenate([sine, cosine], 1)
    return (np.concatenate([upper, lower], 0) * scale).astype(np.float32)


def map_kernel(groups, got_ref, own_ref, gram_ref, solver_ref, wave_ref, out_hbm, held_ref, out_ref, out_sem):
    owners, pieces = got_ref.shape[:2]
    blocks = pieces - groups // 2
    lags_local = LANES // groups
    total = owners * blocks
    left = lax.broadcasted_iota(jnp.int32, (SUBLANES, LANES), 1) < TAPS
    sign = row_sign((SUBLANES, LANES))
    rows = [None] * groups
    for i in range(groups // 2):
        tile = got_ref[0, blocks + i]
        for owner in range(1, owners):
            tile = tile + got_ref[owner, blocks + i]
        swapped = pltpu.roll(tile, TAPS, 1)
        for part, here, there in ((i, tile, swapped), (i + groups // 2, swapped, tile)):
            other = -sign * pltpu.roll(there, SUBLANES // 2, 0)
            rows[part] = jnp.where(left, here, other)
    cross = jnp.concatenate(rows, 0)
    solver = (solver_ref[0], solver_ref[1])
    taps = dot_split(halves(cross), solver)
    rest = cross - dot_split(halves(taps), (gram_ref[0], gram_ref[1]))
    taps = taps + dot_split(halves(rest), solver)
    taps_high, taps_low = halves(taps)
    taps_both = jnp.concatenate([taps_high, taps_low], 0)
    count = taps.shape[0]
    for q in range(0, total, 2 * groups):
        own = slice(q * lags_local, (q + 2 * groups) * lags_local)
        by_high = dot_nt(taps_both, own_ref[0, own, :])
        clutter = by_high[:count] + (by_high[count:] + dot_nt(taps_high, own_ref[1, own, :]))
        for h in range(2):
            lanes = slice(h * LANES, (h + 1) * LANES)
            tiles = [clutter[r : r + SUBLANES, lanes] for r in range(0, groups * SUBLANES, SUBLANES)]
            for j, tile in enumerate(swap_groups(tiles, groups)):
                at = q + h * groups + j
                held_ref[at * SUBLANES : (at + 1) * SUBLANES, :] = got_ref[at // blocks, at % blocks] - tile
    half = SUBLANES // 2
    wave = (wave_ref[0], wave_ref[1])
    copies = []
    for first in range(0, half, 2):
        lagged = []
        for g in (first, first + 1):
            parts = [held_ref[pl.ds(c * half + g, total, stride=SUBLANES), :] for c in range(2)]
            lagged.append(jnp.concatenate(parts, 0).T)
        spectrum = dot_split(halves(jnp.concatenate(lagged, 0)), wave)
        for n in range(2 * groups):
            for c in range(2):
                out_ref[n % groups, first + n // groups, c] = spectrum[
                    n * lags_local : (n + 1) * lags_local, c * DOPPLER : (c + 1) * DOPPLER
                ]
        part = (slice(None), pl.ds(first, 2))
        copies.append(pltpu.make_async_copy(out_ref.at[part], out_hbm.at[part], out_sem.at[first // 2]))
        copies[-1].start()
    for copy in copies:
        copy.wait()


def map_call(got, own, gram, solver, wave, groups, beams_local):
    total = got.shape[0] * (got.shape[1] - groups // 2)
    lags_local = LANES // groups
    half = SUBLANES // 2
    shape = (beams_local // half, half, 2, lags_local, DOPPLER)
    out = pl.pallas_call(
        functools.partial(map_kernel, groups),
        in_specs=[pl.BlockSpec(memory_space=pltpu.VMEM)] * 5,
        out_specs=pl.BlockSpec(memory_space=pltpu.HBM),
        out_shape=jax.ShapeDtypeStruct(shape, jnp.float32),
        scratch_shapes=[
            pltpu.VMEM((total * SUBLANES, LANES), jnp.float32),
            pltpu.VMEM(shape, jnp.float32),
            pltpu.SemaphoreType.DMA((half // 2,)),
        ],
        compiler_params=params(),
        cost_estimate=cost(2.5),
        name="range_doppler",
    )(got, own, gram, solver, wave)
    return out.reshape((beams_local,) + shape[2:])


def swap(x, axis, by):
    pairs = [(i, i ^ by) for i in range(lax.axis_size(axis))]
    return lax.ppermute(x, axis, pairs)


def tiled_device(ref_signal, surveillance, steering):
    chan_count, tm_count = lax.axis_size("chan"), lax.axis_size("tm")
    channels, length = surveillance.shape[1:]
    beams_local = steering.shape[1] // chan_count
    lags_local = LAGS // tm_count
    groups = LANES // lags_local
    samples = length * tm_count

    survey = surveillance.reshape(2 * channels, length)
    kept, moved, tiles = beam_call(steering, survey, ref_signal, chan_count, beams_local)
    near = swap(tiles[None], "tm", 1)
    shape = (chan_count // 2, 2 * beams_local, length)
    kept, got = kept.reshape(shape), swap(moved, "chan", 1).reshape(shape)
    by = 2
    while by < chan_count:
        kept, moved = sum_call([kept, got])
        got = swap(moved, "chan", by)
        by *= 2
    rounds = [near]
    joined = join_call(tiles[None], near, moved)
    while True:
        count = joined.shape[0]
        rounds.append(lax.ppermute(joined, "tm", [(i, (i + count) % tm_count) for i in range(tm_count)]))
        if count * 2 == tm_count:
            break
        joined = join_call(joined, rounds[-1])
    table = table_call(tiles)
    pieces = lag_call([kept[0], got[0]], table, tiles, rounds[:2], joined, groups, tm_count)
    got = lax.all_to_all(pieces, "tm", 0, 0, tiled=True)
    own, line, tail = own_call([tiles[None]] + rounds, lags_local, pieces)
    gram, solver = solver_call(line, tail)
    wave = doppler_table(samples // BLOCK_LEN, 0.125 / math.sqrt(samples))
    high = wave.astype(jnp.bfloat16)
    wave = np.stack([high, (wave - high.astype(np.float32)).astype(jnp.bfloat16)])
    return map_call(got, own, gram, solver, jnp.asarray(wave), groups, beams_local)


def lag_table(ref_ext, offset, lags):
    window = lax.dynamic_slice_in_dim(ref_ext, offset, BLOCK_LEN + LAGS, 1)
    span = BLOCK_LEN + LAGS
    tiled = jnp.tile(jnp.pad(window, ((0, 0), (0, 1))), (1, lags))[:, : lags * span]
    return tiled.reshape(2, lags, span)[:, :, LAGS:]


def times_conj(a, b):
    real = jnp.einsum("...t,lt->...l", a[..., 0, :], b[0], precision=HIGHEST) + jnp.einsum(
        "...t,lt->...l", a[..., 1, :], b[1], precision=HIGHEST
    )
    imag = jnp.einsum("...t,lt->...l", a[..., 1, :], b[0], precision=HIGHEST) - jnp.einsum(
        "...t,lt->...l", a[..., 0, :], b[1], precision=HIGHEST
    )
    return jnp.stack([real, imag], -2)


def plain_device(ref_signal, surveillance, steering):
    chan_count, tm_count = lax.axis_size("chan"), lax.axis_size("tm")
    length = surveillance.shape[2]
    beams = steering.shape[1]
    lags_local = LAGS // tm_count
    samples = length * tm_count
    local_blocks = length // BLOCK_LEN
    here = lax.axis_index("tm")

    w_real, w_imag = steering
    real = jnp.dot(w_real, surveillance[0], precision=HIGHEST) - jnp.dot(w_imag, surveillance[1], precision=HIGHEST)
    imag = jnp.dot(w_imag, surveillance[0], precision=HIGHEST) + jnp.dot(w_real, surveillance[1], precision=HIGHEST)
    beam = lax.psum_scatter(jnp.stack([real, imag], 1), "chan", scatter_dimension=0, tiled=True)
    ref_all = lax.all_gather(ref_signal, "tm", axis=1, tiled=True)
    ref_ext = jnp.pad(ref_all, ((0, 0), (LAGS, 0)))

    def beam_step(carry, q):
        offset = q * BLOCK_LEN
        table = lag_table(ref_ext, here * length + offset, LAGS)
        segment = lax.dynamic_slice_in_dim(beam, offset, BLOCK_LEN, 2)
        return carry, times_conj(segment, table)

    _, products = lax.scan(beam_step, None, jnp.arange(local_blocks, dtype=jnp.int32))
    cross = lax.psum(products[..., :TAPS].sum(0), "tm")
    got = lax.all_to_all(products, "tm", 3, 0, tiled=True)

    def own_step(gram, q):
        offset = q * BLOCK_LEN
        table = lag_table(ref_ext, offset, LAGS)
        taps = table[:, :TAPS].transpose(1, 0, 2)
        mine = lax.dynamic_slice_in_dim(table, here * lags_local, lags_local, 1)
        return gram + times_conj(taps, table[:, :TAPS]), times_conj(taps, mine)

    start = jnp.zeros((TAPS, 2, TAPS), jnp.float32)
    gram, own = lax.scan(own_step, start, jnp.arange(samples // BLOCK_LEN, dtype=jnp.int32))
    g_real, g_imag = gram[:, 0].T, gram[:, 1].T
    system = jnp.concatenate([jnp.concatenate([g_real, -g_imag], 1), jnp.concatenate([g_imag, g_real], 1)], 0)
    right = jnp.concatenate([cross[:, 0].T, cross[:, 1].T], 0)
    solved = jax.scipy.linalg.cho_solve((jnp.linalg.cholesky(system), True), right)
    b_real, b_imag = solved[:TAPS].T, solved[TAPS:].T
    mixing = jnp.concatenate([jnp.stack([b_real, b_imag], 1), jnp.stack([-b_imag, b_real], 1)], 2)
    stacked = jnp.concatenate([own[:, :, 0], own[:, :, 1]], 1)
    lagged = got - jnp.einsum("mck,qkl->qmcl", mixing, stacked, precision=HIGHEST)
    wave = jnp.asarray(doppler_table(samples // BLOCK_LEN, 0.125 / math.sqrt(samples)))
    wave = wave.reshape(2, samples // BLOCK_LEN, 2, DOPPLER)
    return jnp.einsum("qmcl,cqdk->mdlk", lagged, wave, precision=HIGHEST)


def on_device(ref_signal, surveillance, steering):
    chan_count, tm_count = lax.axis_size("chan"), lax.axis_size("tm")
    beams_local = steering.shape[1] // chan_count
    lags_local = LAGS // tm_count
    fills = (
        LANES % lags_local == 0
        and lags_local % (2 * SUBLANES) == 0
        and beams_local * lags_local == LANES * SUBLANES // 2
        and chan_count > 1
        and chan_count & (chan_count - 1) == 0
        and tm_count > 2
        and tm_count & (tm_count - 1) == 0
        and 2 * surveillance.shape[1] % LANES == 0
        and surveillance.shape[2] % (2 * BATCH * BLOCK_LEN) == 0
    )
    device = tiled_device if fills else plain_device
    return device(ref_signal, surveillance, steering)


def solution(mesh):
    placed = (P(None, "tm"), P(None, "chan", "tm"), P(None, None, "chan"))
    return jax.shard_map(
        on_device,
        mesh=mesh,
        in_specs=placed,
        out_specs=P("chan", None, "tm", None),
        check_vma=False,
    )
```

```python
import functools
import math

import jax
import jax.numpy as jnp
import numpy as np
from jax import lax
from jax.experimental import pallas as pl
from jax.experimental.pallas import tpu as pltpu
from jax.sharding import PartitionSpec as P

LAGS = 256
DOPPLER = 256
TAPS = 64
BLOCK_LEN = 256
LANES = 128
SUBLANES = 8
EDGE = 2

HIGHEST = lax.Precision.HIGHEST
VMEM_BYTES = 48 * 1024 * 1024


def params():
    return pltpu.CompilerParams(vmem_limit_bytes=VMEM_BYTES)


def cost(us):
    return pl.CostEstimate(flops=int(us * 1.15e9), bytes_accessed=0, transcendentals=0)


def halves(x):
    high = x.astype(jnp.bfloat16)
    return high, (x - high.astype(jnp.float32)).astype(jnp.bfloat16)


def dot_nt(a, b, precision=None):
    return lax.dot_general(
        a, b, (((1,), (1,)), ((), ())), precision=precision, preferred_element_type=jnp.float32
    )


def dot_split(a, b):
    (a_high, a_low), (b_high, b_low) = a, b
    left = jnp.concatenate([a_high, a_low], 1)
    right = jnp.concatenate([b_high, b_high], 0)
    return jnp.dot(left, right, preferred_element_type=jnp.float32) + jnp.dot(
        a_high, b_low, preferred_element_type=jnp.float32
    )


def row_sign(shape):
    rows = lax.broadcasted_iota(jnp.int32, shape, 0)
    return jnp.where(rows % SUBLANES < SUBLANES // 2, 1.0, -1.0).astype(jnp.float32)


def lane_sign(shape):
    lanes = lax.broadcasted_iota(jnp.int32, shape, 1)
    return jnp.where(lanes % LANES < LANES // 2, 1.0, -1.0).astype(jnp.float32)


def swap_groups(rows, groups):
    width = LANES // groups
    lane_group = lax.broadcasted_iota(jnp.int32, rows[0].shape, 1) // width
    outs = []
    for j in range(groups):
        out = rows[j]
        for i in range(groups):
            if i != j:
                moved = pltpu.roll(rows[i], (width * (i - j)) % LANES, 1)
                out = jnp.where(lane_group == i, moved, out)
        outs.append(out)
    return outs


CHUNKS = 2


def beam_kernel(
    chan_count, beams_local, w_hbm, s_hbm, ref_hbm, kept_ref, sent_ref, tiles_ref,
    w_ref, s_ref, ref_ref, w_sem, s_sem, ref_sem,
):
    me = lax.axis_index("chan")
    length = s_hbm.shape[1]
    width = length // CHUNKS
    w_copy = pltpu.make_async_copy(w_hbm, w_ref, w_sem)
    w_copy.start()
    ref_copy = pltpu.make_async_copy(ref_hbm, ref_ref, ref_sem)
    ref_copy.start()
    s_copies = []
    for n in range(CHUNKS):
        cols = pl.ds(n * width, width)
        s_copies.append(pltpu.make_async_copy(s_hbm.at[:, cols], s_ref.at[:, cols], s_sem.at[n]))
        s_copies[n].start()
    half = SUBLANES // 2
    sub = lax.broadcasted_iota(jnp.int32, (SUBLANES, w_hbm.shape[2]), 0)
    top = sub < half
    w_copy.wait()
    rows = []
    for parity in range(2):
        for e in range(parity, chan_count, 2):
            base = (me ^ e) * beams_local
            for tile in range(beams_local // SUBLANES):
                start = pl.multiple_of(base + tile * SUBLANES, SUBLANES)
                wr = w_ref[0, pl.ds(start, SUBLANES), :]
                wi = w_ref[1, pl.ds(start, SUBLANES), :]
                wr_s = pltpu.roll(wr, half, 0)
                wi_s = pltpu.roll(wi, half, 0)
                first = [jnp.where(top, wr, wi_s), jnp.where(top, -wi, wr_s)]
                second = [jnp.where(top, wr_s, wi), jnp.where(top, -wi_s, wr)]
                rows.append(jnp.concatenate(first, 1))
                rows.append(jnp.concatenate(second, 1))
    weights = jnp.concatenate(halves(jnp.concatenate(rows, 0)), 0)
    count = weights.shape[0] // 2
    ref_copy.wait()
    for c in range(2):
        for n in range(tiles_ref.shape[1]):
            tiles_ref[c, n : n + 1, :] = ref_ref[c : c + 1, n * LANES : (n + 1) * LANES]
    mid = count // 2
    for n in range(CHUNKS):
        cols = slice(n * width, (n + 1) * width)
        s_copies[n].wait()
        high, low = halves(s_ref[:, cols])
        by_high = jnp.dot(weights, high, preferred_element_type=jnp.float32)
        by_low = jnp.dot(weights[:count], low, preferred_element_type=jnp.float32)
        product = by_high[:count] + (by_high[count:] + by_low)
        kept_ref[:, cols] = product[:mid]
        sent_ref[:, cols] = product[mid:]


def beam_call(steering, survey, ref, chan_count, beams_local):
    depth, length = survey.shape
    rows = chan_count * beams_local
    tiles = (2, length // LANES, LANES)
    out = jax.ShapeDtypeStruct((rows, length), jnp.float32)
    hbm, vmem = pl.BlockSpec(memory_space=pltpu.HBM), pl.BlockSpec(memory_space=pltpu.VMEM)
    return pl.pallas_call(
        functools.partial(beam_kernel, chan_count, beams_local),
        in_specs=[hbm] * 3,
        out_specs=[vmem] * 3,
        out_shape=[
            out,
            out,
            jax.ShapeDtypeStruct(tiles, jnp.float32),
        ],
        scratch_shapes=[
            pltpu.VMEM(steering.shape, jnp.float32),
            pltpu.VMEM(survey.shape, jnp.float32),
            pltpu.VMEM(ref.shape, jnp.float32),
            pltpu.SemaphoreType.DMA,
            pltpu.SemaphoreType.DMA((CHUNKS,)),
            pltpu.SemaphoreType.DMA,
        ],
        compiler_params=params(),
        cost_estimate=cost(2.2),
        name="beams",
    )(*(pltpu.with_memory_space_constraint(x, pltpu.HBM) for x in (steering, survey, ref)))


def sum_kernel(count, *refs):
    kept_ref, sent_ref = refs[-2:]
    for n in range(kept_ref.shape[0]):
        for offset, out_ref in ((0, kept_ref), (1, sent_ref)):
            total = refs[0][2 * n + offset]
            for ref in refs[1:count]:
                total = total + ref[2 * n + offset]
            out_ref[n] = total


def sum_call(parts):
    shape = (parts[0].shape[0] // 2,) + parts[0].shape[1:]
    out = jax.ShapeDtypeStruct(shape, jnp.float32)
    vmem = pl.BlockSpec(memory_space=pltpu.VMEM)
    return pl.pallas_call(
        functools.partial(sum_kernel, len(parts)),
        in_specs=[vmem] * len(parts),
        out_specs=[vmem, vmem],
        out_shape=[out, out],
        compiler_params=params(),
        cost_estimate=cost(0.1),
        name="halves_summed",
    )(*parts)


def join_kernel(first_ref, second_ref, *refs):
    out_ref = refs[-1]
    count = first_ref.shape[0]
    out_ref[:count] = first_ref[...]
    out_ref[count:] = second_ref[...]


def join_call(first, second, *after):
    vmem = pl.BlockSpec(memory_space=pltpu.VMEM)
    return pl.pallas_call(
        join_kernel,
        in_specs=[vmem, vmem] + [pl.BlockSpec(memory_space=pl.ANY)] * len(after),
        out_shape=jax.ShapeDtypeStruct((2 * first.shape[0],) + first.shape[1:], jnp.float32),
        compiler_params=params(),
        cost_estimate=cost(1.0),
        name="reference_joined",
    )(first, second, *after)


def spread_line(line, keep):
    for g in range(0, LANES, 2 * SUBLANES):
        tiled = jnp.broadcast_to(line, (2 * SUBLANES, line.shape[1]))
        for h, value in enumerate(halves(pltpu.roll(tiled, g, 1, stride=1, stride_axis=0)[:, LANES:])):
            keep(h, g, value)


def table_kernel(tiles_ref, out_ref):
    for c in range(2):
        line = jnp.concatenate([tiles_ref[c, n : n + 1, :] for n in range(tiles_ref.shape[1])], 1)

        def keep(h, g, value):
            out_ref[h, c, g : g + 2 * SUBLANES] = value

        spread_line(line, keep)


def table_call(tiles):
    shape = (2, 2, LANES, LANES * (tiles.shape[1] - 1))
    return pl.pallas_call(
        table_kernel,
        out_shape=jax.ShapeDtypeStruct(shape, jnp.bfloat16),
        compiler_params=params(),
        cost_estimate=cost(0.7),
        name="shifted_reference",
    )(tiles)


def lag_kernel(groups, part_count, *refs):
    y_refs, refs = refs[:part_count], refs[part_count:]
    table_ref, tiles_ref, *round_refs, _, out_hbm, out_ref, out_sem, first_ref = refs
    copies = []

    me = lax.axis_index("tm")
    for c in range(2):
        tails = [ref[ref.shape[0] - 1, c, ref.shape[2] - EDGE :, :] for ref in round_refs]
        before = jnp.where(me % 2 == 1, tails[0], jnp.where(me > 0, tails[-1], 0.0))
        line = jnp.concatenate([before[n : n + 1] for n in range(EDGE)] + [tiles_ref[c, 0:1, :]], 1)

        def keep(h, g, value):
            first_ref[h, c, g : g + 2 * SUBLANES] = value

        spread_line(line, keep)

    def table_tile(h, n):
        parts = []
        for c in range(2):
            known = first_ref.shape[3] // LANES
            ref, at = (first_ref, n) if n < known else (table_ref, n - known)
            parts.append(ref[h, c, :, at * LANES : (at + 1) * LANES])
        return jnp.concatenate(parts, 1)

    def send(start, count):
        part = (slice(None), pl.ds(start, count))
        copies.append(pltpu.make_async_copy(out_ref.at[part], out_hbm.at[part], out_sem.at[len(copies)]))
        copies[-1].start()

    y = y_refs[0][...]
    for y_ref in y_refs[1:]:
        y = y + y_ref[...]
    rows, length = y.shape
    blocks = length // BLOCK_LEN
    turned = jnp.concatenate(
        [pltpu.roll(y[r : r + SUBLANES], SUBLANES // 2, 0) for r in range(0, rows, SUBLANES)], 0
    )
    turned = turned * row_sign(turned.shape)
    y_high, y_low = halves(y)
    t_high, t_low = halves(turned)

    def half_block(q, b):
        cols = slice(q * BLOCK_LEN + b * LANES, q * BLOCK_LEN + (b + 1) * LANES)
        return [jnp.concatenate([x[:, cols], t[:, cols]], 1) for x, t in ((y_high, t_high), (y_low, t_low))]

    def products(stack, n, count):
        high, low = (jnp.concatenate([table_tile(h, n + i) for i in range(count)], 0) for h in range(2))
        by_high = dot_nt(jnp.concatenate([part for pair in stack for part in pair], 0), high)
        by_low = dot_nt(jnp.concatenate([pair[0] for pair in stack], 0), low)
        return [
            by_high[2 * i * rows : (2 * i + 1) * rows]
            + (by_high[(2 * i + 1) * rows : 2 * (i + 1) * rows] + by_low[i * rows : (i + 1) * rows])
            for i in range(len(stack))
        ]

    taps_sum = None
    (far,) = products([half_block(0, 0)], 0, 1)
    for q in range(blocks):
        stack = [half_block(q, 0), half_block(q, 1)]
        if q + 1 < blocks:
            stack.append(half_block(q + 1, 0))
        first, second, *after = products(stack, 2 * q + 1, 2)
        product = jnp.concatenate([first[:, :LANES] + second[:, LANES:], second[:, :LANES] + far], 1)
        if after:
            far = after[0][:, LANES:]
        taps = product[:, :LANES]
        taps_sum = taps if taps_sum is None else taps_sum + taps
        for h in range(LAGS // LANES):
            lanes = slice(h * LANES, (h + 1) * LANES)
            tiles = [product[r : r + SUBLANES, lanes] for r in range(0, rows, SUBLANES)]
            for j, tile in enumerate(swap_groups(tiles, groups)):
                out_ref[h * groups + j, q] = tile
        if q % 2:
            send(q - 1, 2)
    left = lax.broadcasted_iota(jnp.int32, (SUBLANES, LANES), 1) < TAPS
    for i in range(groups // 2):
        a = taps_sum[i * SUBLANES : (i + 1) * SUBLANES]
        other = i + groups // 2
        b = taps_sum[other * SUBLANES : (other + 1) * SUBLANES]
        tile = jnp.where(left, a, pltpu.roll(b, LANES - TAPS, 1))
        for owner in range(out_ref.shape[0]):
            out_ref[owner, blocks + i] = tile
    send(blocks, groups // 2)
    for copy in copies:
        copy.wait()


def lag_call(ys, table, tiles, rounds, after, groups, owners):
    blocks = ys[0].shape[1] // BLOCK_LEN
    shape = (owners, blocks + groups // 2, SUBLANES, LANES)
    vmem = pl.BlockSpec(memory_space=pltpu.VMEM)
    return pl.pallas_call(
        functools.partial(lag_kernel, groups, len(ys)),
        in_specs=[vmem] * (len(ys) + 2 + len(rounds)) + [pl.BlockSpec(memory_space=pl.ANY)],
        out_specs=pl.BlockSpec(memory_space=pltpu.HBM),
        out_shape=jax.ShapeDtypeStruct(shape, jnp.float32),
        scratch_shapes=[
            pltpu.VMEM(shape, jnp.float32),
            pltpu.SemaphoreType.DMA((blocks // 2 + 1,)),
            pltpu.VMEM((2, 2, LANES, 2 * LANES), jnp.bfloat16),
        ],
        compiler_params=params(),
        cost_estimate=cost(2.1),
        name="lag_products",
    )(*ys, table, tiles, *rounds, after)


BATCH = 4


def own_kernel(lags_local, *refs):
    *part_refs, _, out_ref, line_ref, tail_ref, span_ref, late_ref, taps_a, lags_a, taps_b, lags_b = refs
    me = lax.axis_index("tm")
    part_rows = part_refs[0].shape[2]
    owners = sum(part_ref.shape[0] for part_ref in part_refs)
    samples = owners * part_rows * LANES
    steps = samples // BLOCK_LEN // BATCH
    total_rows = span_ref.shape[1]
    block_rows = BLOCK_LEN // LANES

    span_ref[...] = jnp.zeros_like(span_ref)
    n = 0
    for part_ref in part_refs:
        for i in range(part_ref.shape[0]):
            block = lax.rem(me - (n // 2) * 2 + owners, owners) ^ (n % 2)
            span_ref[:, pl.ds(EDGE + block * part_rows, part_rows), :] = part_ref[i]
            n += 1
    late_rows = (me * lags_local) // LANES
    late_lanes = lax.rem(me * lags_local, LANES)
    turned = [pltpu.roll(span_ref[c], late_lanes, 1) for c in range(2)]
    before = [pltpu.roll(x, 1, 0) for x in turned]
    lanes = lax.broadcasted_iota(jnp.int32, (total_rows, LANES), 1)
    for c in range(2):
        late_ref[c] = pltpu.roll(jnp.where(lanes < late_lanes, before[c], turned[c]), late_rows, 0)

    def line_of(ref, c, first, count):
        return jnp.concatenate([ref[c, pl.ds(first + n, 1), :] for n in range(count)], 1)

    def shifted(line, by):
        tiled = jnp.broadcast_to(line, (2 * SUBLANES, line.shape[1]))
        return pltpu.roll(tiled, by, 1, stride=1, stride_axis=0)[:, LANES:]

    def keep(ref, row, value):
        high, low = halves(value)
        half = ref.shape[0] // 2
        ref[row : row + 2 * SUBLANES, :] = high
        ref[half + row : half + row + 2 * SUBLANES, :] = low

    def build(n, taps_ref, lags_ref):
        first = EDGE - 1 + n * BATCH * block_rows
        count = BATCH * block_rows + 1
        lines = [line_of(span_ref, c, first, count) for c in range(2)]
        for c in range(2):
            for g in range(0, TAPS, 2 * SUBLANES):
                keep(taps_ref, c * TAPS + g, shifted(lines[c], g))
            late = line_of(late_ref, c, first, count)
            for g in range(0, lags_local, 2 * SUBLANES):
                keep(lags_ref, c * lags_local + g, shifted(late, g))
        pad = jnp.zeros((2 * SUBLANES - 2, BATCH * BLOCK_LEN), jnp.float32)
        keep(lags_ref, 2 * lags_local, jnp.concatenate([line[:, LANES:] for line in lines] + [pad], 0))

    turn = lane_sign((lags_local, LANES))

    def use(n, taps_ref, lags_ref):
        count = lags_ref.shape[0] // 2
        for b in range(BATCH):
            cols = slice(b * BLOCK_LEN, (b + 1) * BLOCK_LEN)
            product = dot_nt(lags_ref[:, cols], taps_ref[:, cols])
            product = product[:count, :LANES] + (product[:count, LANES:] + product[count:, :LANES])
            by_real = product[:lags_local]
            by_imag = product[lags_local : 2 * lags_local]
            rows = pl.ds(pl.multiple_of((n * BATCH + b) * lags_local, lags_local), lags_local)
            high, low = halves(by_real + turn * pltpu.roll(by_imag, TAPS, 1))
            out_ref[0, rows, :] = high
            out_ref[1, rows, :] = low
            line_ref[...] += product[2 * lags_local : 2 * lags_local + SUBLANES]

    line_ref[...] = jnp.zeros_like(line_ref)
    build(0, taps_a, lags_a)

    def pair(m, carry):
        build(2 * m + 1, taps_b, lags_b)
        use(2 * m, taps_a, lags_a)
        build(jnp.minimum(2 * m + 2, steps - 1), taps_a, lags_a)
        use(2 * m + 1, taps_b, lags_b)
        return carry

    lax.fori_loop(0, steps // 2, pair, 0)
    tail = []
    for c in range(2):
        line = line_of(span_ref, c, EDGE + owners * part_rows - 1, 2)
        tail += [shifted(line, g) for g in range(0, TAPS, 2 * SUBLANES)]
    tail = jnp.concatenate(tail, 0)
    tail_ref[...] = dot_nt(tail, tail, HIGHEST)


def own_call(parts, lags_local, after):
    part_rows = parts[0].shape[2]
    span_rows = part_rows * sum(part.shape[0] for part in parts)
    rows = span_rows * LANES // BLOCK_LEN * lags_local
    held_rows = -(-(span_rows + 2 * EDGE) // SUBLANES) * SUBLANES
    width = BATCH * BLOCK_LEN
    taps = pltpu.VMEM((4 * TAPS, width), jnp.bfloat16)
    lags = pltpu.VMEM((4 * lags_local + 4 * SUBLANES, width), jnp.bfloat16)
    span = pltpu.VMEM((2, held_rows, LANES), jnp.float32)
    return pl.pallas_call(
        functools.partial(own_kernel, lags_local),
        in_specs=[pl.BlockSpec(memory_space=pltpu.VMEM)] * len(parts) + [pl.BlockSpec(memory_space=pl.ANY)],
        out_shape=[
            jax.ShapeDtypeStruct((2, rows, 2 * TAPS), jnp.bfloat16),
            jax.ShapeDtypeStruct((SUBLANES, 2 * TAPS), jnp.float32),
            jax.ShapeDtypeStruct((2 * TAPS, 2 * TAPS), jnp.float32),
        ],
        scratch_shapes=[span, span, taps, lags, taps, lags],
        compiler_params=params(),
        cost_estimate=cost(6.2),
        name="reference_products",
    )(*parts, after)


def as_factor(a):
    return jnp.concatenate([a, -lane_sign(a.shape) * pltpu.roll(a, a.shape[0], 1)], 0)


def solver_kernel(line_ref, tail_ref, gram_ref, solver_ref):
    total = line_ref[...]
    line = total[0:1] + lane_sign((1, LANES)) * pltpu.roll(total[1:2], TAPS, 1)
    low = lax.broadcasted_iota(jnp.int32, (1, LANES), 1) < TAPS
    line_r = jnp.where(low, line, 0.0)
    line_i = jnp.where(low, pltpu.roll(line, TAPS, 1), 0.0)
    cols = lax.broadcasted_iota(jnp.int32, (TAPS, TAPS), 1)
    rows = lax.broadcasted_iota(jnp.int32, (TAPS, TAPS), 0)
    above = cols > rows

    def upper(x):
        spread = pltpu.roll(jnp.broadcast_to(x, (TAPS, LANES)), 0, 1, stride=1, stride_axis=0)
        return spread[:, :TAPS]

    up_r = upper(line_r)
    up_i = jnp.where(above, upper(line_i), 0.0)
    strict_r = jnp.where(above, up_r, 0.0)
    diag_r = jnp.where(cols == rows, up_r, 0.0)
    tails = tail_ref[...]
    gram_r = strict_r + strict_r.T + diag_r - (tails[:TAPS, :TAPS] + tails[TAPS:, TAPS:])
    gram_i = up_i - up_i.T - (tails[:TAPS, TAPS:] - tails[TAPS:, :TAPS])
    gram = jnp.concatenate([gram_r, gram_i], 1)
    gram_halves = halves(as_factor(gram))
    gram_ref[0], gram_ref[1] = gram_halves
    one = (
        lax.broadcasted_iota(jnp.int32, gram.shape, 0) == lax.broadcasted_iota(jnp.int32, gram.shape, 1)
    ).astype(jnp.float32)
    bound = jnp.max(jnp.sum(jnp.abs(gram), axis=1, keepdims=True), axis=0, keepdims=True)

    def again(state):
        count, left, _ = state
        return (count < 60) & (left > 1e-3)

    def newton(state):
        count, _, x = state
        x_halves = halves(x)
        seen = dot_split(x_halves, gram_halves)
        left = jnp.max(jnp.abs(seen - one))
        x = 2.0 * x - dot_split(halves(seen), halves(as_factor(x)))
        return count + 1, left, x

    start = (jnp.int32(0), jnp.float32(1.0), one * (1.0 / bound))
    _, _, inverse = lax.while_loop(again, newton, start)
    solver_ref[0], solver_ref[1] = halves(as_factor(inverse))


def solver_call(line, tail):
    out = jax.ShapeDtypeStruct((2,) + tail.shape, jnp.bfloat16)
    return pl.pallas_call(
        solver_kernel,
        out_shape=[out, out],
        compiler_params=params(),
        cost_estimate=cost(2.0),
        name="gram_inverse",
    )(line, tail)


def doppler_table(block_count, scale):
    phase = (np.arange(block_count)[:, None] * np.arange(DOPPLER)[None, :] % DOPPLER) * (2.0 * math.pi / DOPPLER)
    cosine, sine = np.cos(phase), np.sin(phase)
    upper = np.concatenate([cosine, -sine], 1)
    lower = np.concatenate([sine, cosine], 1)
    return (np.concatenate([upper, lower], 0) * scale).astype(np.float32)


def map_kernel(groups, got_ref, own_ref, gram_ref, solver_ref, wave_ref, out_hbm, held_ref, out_ref, out_sem):
    owners, pieces = got_ref.shape[:2]
    blocks = pieces - groups // 2
    lags_local = LANES // groups
    total = owners * blocks
    left = lax.broadcasted_iota(jnp.int32, (SUBLANES, LANES), 1) < TAPS
    sign = row_sign((SUBLANES, LANES))
    rows = [None] * groups
    for i in range(groups // 2):
        tile = got_ref[0, blocks + i]
        for owner in range(1, owners):
            tile = tile + got_ref[owner, blocks + i]
        swapped = pltpu.roll(tile, TAPS, 1)
        for part, here, there in ((i, tile, swapped), (i + groups // 2, swapped, tile)):
            other = -sign * pltpu.roll(there, SUBLANES // 2, 0)
            rows[part] = jnp.where(left, here, other)
    cross = jnp.concatenate(rows, 0)
    solver = (solver_ref[0], solver_ref[1])
    taps = dot_split(halves(cross), solver)
    rest = cross - dot_split(halves(taps), (gram_ref[0], gram_ref[1]))
    taps = taps + dot_split(halves(rest), solver)
    taps_high, taps_low = halves(taps)
    taps_both = jnp.concatenate([taps_high, taps_low], 0)
    count = taps.shape[0]
    for q in range(0, total, 2 * groups):
        own = slice(q * lags_local, (q + 2 * groups) * lags_local)
        by_high = dot_nt(taps_both, own_ref[0, own, :])
        clutter = by_high[:count] + (by_high[count:] + dot_nt(taps_high, own_ref[1, own, :]))
        for h in range(2):
            lanes = slice(h * LANES, (h + 1) * LANES)
            tiles = [clutter[r : r + SUBLANES, lanes] for r in range(0, groups * SUBLANES, SUBLANES)]
            for j, tile in enumerate(swap_groups(tiles, groups)):
                at = q + h * groups + j
                held_ref[at * SUBLANES : (at + 1) * SUBLANES, :] = got_ref[at // blocks, at % blocks] - tile
    half = SUBLANES // 2
    wave = (wave_ref[0], wave_ref[1])
    copies = []
    for g in range(half):
        parts = [held_ref[pl.ds(c * half + g, total, stride=SUBLANES), :] for c in range(2)]
        spectrum = dot_split(halves(jnp.concatenate(parts, 0).T), wave)
        for i in range(groups):
            for c in range(2):
                out_ref[i, g, c] = spectrum[i * lags_local : (i + 1) * lags_local, c * DOPPLER : (c + 1) * DOPPLER]
        part = (slice(None), pl.ds(g, 1))
        copies.append(pltpu.make_async_copy(out_ref.at[part], out_hbm.at[part], out_sem.at[g]))
        copies[-1].start()
    for copy in copies:
        copy.wait()


def map_call(got, own, gram, solver, wave, groups, beams_local):
    total = got.shape[0] * (got.shape[1] - groups // 2)
    lags_local = LANES // groups
    half = SUBLANES // 2
    shape = (beams_local // half, half, 2, lags_local, DOPPLER)
    out = pl.pallas_call(
        functools.partial(map_kernel, groups),
        in_specs=[pl.BlockSpec(memory_space=pltpu.VMEM)] * 5,
        out_specs=pl.BlockSpec(memory_space=pltpu.HBM),
        out_shape=jax.ShapeDtypeStruct(shape, jnp.float32),
        scratch_shapes=[
            pltpu.VMEM((total * SUBLANES, LANES), jnp.float32),
            pltpu.VMEM(shape, jnp.float32),
            pltpu.SemaphoreType.DMA((half,)),
        ],
        compiler_params=params(),
        cost_estimate=cost(2.5),
        name="range_doppler",
    )(got, own, gram, solver, wave)
    return out.reshape((beams_local,) + shape[2:])


def swap(x, axis, by):
    pairs = [(i, i ^ by) for i in range(lax.axis_size(axis))]
    return lax.ppermute(x, axis, pairs)


def tiled_device(ref_signal, surveillance, steering):
    chan_count, tm_count = lax.axis_size("chan"), lax.axis_size("tm")
    channels, length = surveillance.shape[1:]
    beams_local = steering.shape[1] // chan_count
    lags_local = LAGS // tm_count
    groups = LANES // lags_local
    samples = length * tm_count

    survey = surveillance.reshape(2 * channels, length)
    kept, moved, tiles = beam_call(steering, survey, ref_signal, chan_count, beams_local)
    near = swap(tiles[None], "tm", 1)
    shape = (chan_count // 2, 2 * beams_local, length)
    kept, got = kept.reshape(shape), swap(moved, "chan", 1).reshape(shape)
    by = 2
    while by < chan_count:
        kept, moved = sum_call([kept, got])
        got = swap(moved, "chan", by)
        by *= 2
    rounds = [near]
    joined = join_call(tiles[None], near, moved)
    while True:
        count = joined.shape[0]
        rounds.append(lax.ppermute(joined, "tm", [(i, (i + count) % tm_count) for i in range(tm_count)]))
        if count * 2 == tm_count:
            break
        joined = join_call(joined, rounds[-1])
    table = table_call(tiles)
    pieces = lag_call([kept[0], got[0]], table, tiles, rounds[:2], joined, groups, tm_count)
    got = lax.all_to_all(pieces, "tm", 0, 0, tiled=True)
    own, line, tail = own_call([tiles[None]] + rounds, lags_local, pieces)
    gram, solver = solver_call(line, tail)
    wave = doppler_table(samples // BLOCK_LEN, 0.125 / math.sqrt(samples))
    high = wave.astype(jnp.bfloat16)
    wave = np.stack([high, (wave - high.astype(np.float32)).astype(jnp.bfloat16)])
    return map_call(got, own, gram, solver, jnp.asarray(wave), groups, beams_local)


def lag_table(ref_ext, offset, lags):
    window = lax.dynamic_slice_in_dim(ref_ext, offset, BLOCK_LEN + LAGS, 1)
    span = BLOCK_LEN + LAGS
    tiled = jnp.tile(jnp.pad(window, ((0, 0), (0, 1))), (1, lags))[:, : lags * span]
    return tiled.reshape(2, lags, span)[:, :, LAGS:]


def times_conj(a, b):
    real = jnp.einsum("...t,lt->...l", a[..., 0, :], b[0], precision=HIGHEST) + jnp.einsum(
        "...t,lt->...l", a[..., 1, :], b[1], precision=HIGHEST
    )
    imag = jnp.einsum("...t,lt->...l", a[..., 1, :], b[0], precision=HIGHEST) - jnp.einsum(
        "...t,lt->...l", a[..., 0, :], b[1], precision=HIGHEST
    )
    return jnp.stack([real, imag], -2)


def plain_device(ref_signal, surveillance, steering):
    chan_count, tm_count = lax.axis_size("chan"), lax.axis_size("tm")
    length = surveillance.shape[2]
    beams = steering.shape[1]
    lags_local = LAGS // tm_count
    samples = length * tm_count
    local_blocks = length // BLOCK_LEN
    here = lax.axis_index("tm")

    w_real, w_imag = steering
    real = jnp.dot(w_real, surveillance[0], precision=HIGHEST) - jnp.dot(w_imag, surveillance[1], precision=HIGHEST)
    imag = jnp.dot(w_imag, surveillance[0], precision=HIGHEST) + jnp.dot(w_real, surveillance[1], precision=HIGHEST)
    beam = lax.psum_scatter(jnp.stack([real, imag], 1), "chan", scatter_dimension=0, tiled=True)
    ref_all = lax.all_gather(ref_signal, "tm", axis=1, tiled=True)
    ref_ext = jnp.pad(ref_all, ((0, 0), (LAGS, 0)))

    def beam_step(carry, q):
        offset = q * BLOCK_LEN
        table = lag_table(ref_ext, here * length + offset, LAGS)
        segment = lax.dynamic_slice_in_dim(beam, offset, BLOCK_LEN, 2)
        return carry, times_conj(segment, table)

    _, products = lax.scan(beam_step, None, jnp.arange(local_blocks, dtype=jnp.int32))
    cross = lax.psum(products[..., :TAPS].sum(0), "tm")
    got = lax.all_to_all(products, "tm", 3, 0, tiled=True)

    def own_step(gram, q):
        offset = q * BLOCK_LEN
        table = lag_table(ref_ext, offset, LAGS)
        taps = table[:, :TAPS].transpose(1, 0, 2)
        mine = lax.dynamic_slice_in_dim(table, here * lags_local, lags_local, 1)
        return gram + times_conj(taps, table[:, :TAPS]), times_conj(taps, mine)

    start = jnp.zeros((TAPS, 2, TAPS), jnp.float32)
    gram, own = lax.scan(own_step, start, jnp.arange(samples // BLOCK_LEN, dtype=jnp.int32))
    g_real, g_imag = gram[:, 0].T, gram[:, 1].T
    system = jnp.concatenate([jnp.concatenate([g_real, -g_imag], 1), jnp.concatenate([g_imag, g_real], 1)], 0)
    right = jnp.concatenate([cross[:, 0].T, cross[:, 1].T], 0)
    solved = jax.scipy.linalg.cho_solve((jnp.linalg.cholesky(system), True), right)
    b_real, b_imag = solved[:TAPS].T, solved[TAPS:].T
    mixing = jnp.concatenate([jnp.stack([b_real, b_imag], 1), jnp.stack([-b_imag, b_real], 1)], 2)
    stacked = jnp.concatenate([own[:, :, 0], own[:, :, 1]], 1)
    lagged = got - jnp.einsum("mck,qkl->qmcl", mixing, stacked, precision=HIGHEST)
    wave = jnp.asarray(doppler_table(samples // BLOCK_LEN, 0.125 / math.sqrt(samples)))
    wave = wave.reshape(2, samples // BLOCK_LEN, 2, DOPPLER)
    return jnp.einsum("qmcl,cqdk->mdlk", lagged, wave, precision=HIGHEST)


def on_device(ref_signal, surveillance, steering):
    chan_count, tm_count = lax.axis_size("chan"), lax.axis_size("tm")
    beams_local = steering.shape[1] // chan_count
    lags_local = LAGS // tm_count
    fills = (
        LANES % lags_local == 0
        and lags_local % (2 * SUBLANES) == 0
        and beams_local * lags_local == LANES * SUBLANES // 2
        and chan_count > 1
        and chan_count & (chan_count - 1) == 0
        and tm_count > 2
        and tm_count & (tm_count - 1) == 0
        and 2 * surveillance.shape[1] % LANES == 0
        and surveillance.shape[2] % (2 * BATCH * BLOCK_LEN) == 0
    )
    device = tiled_device if fills else plain_device
    return device(ref_signal, surveillance, steering)


def solution(mesh):
    placed = (P(None, "tm"), P(None, "chan", "tm"), P(None, None, "chan"))
    return jax.shard_map(
        on_device,
        mesh=mesh,
        in_specs=placed,
        out_specs=P("chan", None, "tm", None),
        check_vma=False,
    )
```

```python
import functools
import math

import jax
import jax.numpy as jnp
import numpy as np
from jax import lax
from jax.experimental import pallas as pl
from jax.experimental.pallas import tpu as pltpu
from jax.sharding import PartitionSpec as P

LAGS = 256
DOPPLER = 256
TAPS = 64
BLOCK_LEN = 256
LANES = 128
SUBLANES = 8
EDGE = 2

HIGHEST = lax.Precision.HIGHEST
VMEM_BYTES = 48 * 1024 * 1024


def params():
    return pltpu.CompilerParams(vmem_limit_bytes=VMEM_BYTES)


def cost(us):
    return pl.CostEstimate(flops=int(us * 1.15e9), bytes_accessed=0, transcendentals=0)


def halves(x):
    high = x.astype(jnp.bfloat16)
    return high, (x - high.astype(jnp.float32)).astype(jnp.bfloat16)


def dot_nt(a, b, precision=None):
    return lax.dot_general(
        a, b, (((1,), (1,)), ((), ())), precision=precision, preferred_element_type=jnp.float32
    )


def dot_split(a, b):
    (a_high, a_low), (b_high, b_low) = a, b
    left = jnp.concatenate([a_high, a_low], 1)
    right = jnp.concatenate([b_high, b_high], 0)
    return jnp.dot(left, right, preferred_element_type=jnp.float32) + jnp.dot(
        a_high, b_low, preferred_element_type=jnp.float32
    )


def row_sign(shape):
    rows = lax.broadcasted_iota(jnp.int32, shape, 0)
    return jnp.where(rows % SUBLANES < SUBLANES // 2, 1.0, -1.0).astype(jnp.float32)


def lane_sign(shape):
    lanes = lax.broadcasted_iota(jnp.int32, shape, 1)
    return jnp.where(lanes % LANES < LANES // 2, 1.0, -1.0).astype(jnp.float32)


def swap_groups(rows, groups):
    width = LANES // groups
    lane_group = lax.broadcasted_iota(jnp.int32, rows[0].shape, 1) // width
    outs = []
    for j in range(groups):
        out = rows[j]
        for i in range(groups):
            if i != j:
                moved = pltpu.roll(rows[i], (width * (i - j)) % LANES, 1)
                out = jnp.where(lane_group == i, moved, out)
        outs.append(out)
    return outs


CHUNKS = 4


def beam_kernel(
    chan_count, beams_local, w_hbm, s_hbm, ref_hbm, kept_ref, sent_ref, tiles_ref,
    w_ref, s_ref, ref_ref, w_sem, s_sem, ref_sem,
):
    me = lax.axis_index("chan")
    length = s_hbm.shape[1]
    width = length // CHUNKS
    w_copy = pltpu.make_async_copy(w_hbm, w_ref, w_sem)
    w_copy.start()
    ref_copy = pltpu.make_async_copy(ref_hbm, ref_ref, ref_sem)
    ref_copy.start()
    s_copies = []
    for n in range(CHUNKS):
        cols = pl.ds(n * width, width)
        s_copies.append(pltpu.make_async_copy(s_hbm.at[:, cols], s_ref.at[:, cols], s_sem.at[n]))
        s_copies[n].start()
    half = SUBLANES // 2
    sub = lax.broadcasted_iota(jnp.int32, (SUBLANES, w_hbm.shape[2]), 0)
    top = sub < half
    w_copy.wait()
    rows = []
    for parity in range(2):
        for e in range(parity, chan_count, 2):
            base = (me ^ e) * beams_local
            for tile in range(beams_local // SUBLANES):
                start = pl.multiple_of(base + tile * SUBLANES, SUBLANES)
                wr = w_ref[0, pl.ds(start, SUBLANES), :]
                wi = w_ref[1, pl.ds(start, SUBLANES), :]
                wr_s = pltpu.roll(wr, half, 0)
                wi_s = pltpu.roll(wi, half, 0)
                first = [jnp.where(top, wr, wi_s), jnp.where(top, -wi, wr_s)]
                second = [jnp.where(top, wr_s, wi), jnp.where(top, -wi_s, wr)]
                rows.append(jnp.concatenate(first, 1))
                rows.append(jnp.concatenate(second, 1))
    weights = jnp.concatenate(halves(jnp.concatenate(rows, 0)), 0)
    count = weights.shape[0] // 2
    ref_copy.wait()
    for c in range(2):
        for n in range(tiles_ref.shape[1]):
            tiles_ref[c, n : n + 1, :] = ref_ref[c : c + 1, n * LANES : (n + 1) * LANES]
    mid = count // 2
    for n in range(CHUNKS):
        cols = slice(n * width, (n + 1) * width)
        s_copies[n].wait()
        high, low = halves(s_ref[:, cols])
        by_high = jnp.dot(weights, high, preferred_element_type=jnp.float32)
        by_low = jnp.dot(weights[:count], low, preferred_element_type=jnp.float32)
        product = by_high[:count] + (by_high[count:] + by_low)
        kept_ref[:, cols] = product[:mid]
        sent_ref[:, cols] = product[mid:]


def beam_call(steering, survey, ref, chan_count, beams_local):
    depth, length = survey.shape
    rows = chan_count * beams_local
    tiles = (2, length // LANES, LANES)
    out = jax.ShapeDtypeStruct((rows, length), jnp.float32)
    hbm, vmem = pl.BlockSpec(memory_space=pltpu.HBM), pl.BlockSpec(memory_space=pltpu.VMEM)
    return pl.pallas_call(
        functools.partial(beam_kernel, chan_count, beams_local),
        in_specs=[hbm] * 3,
        out_specs=[vmem] * 3,
        out_shape=[
            out,
            out,
            jax.ShapeDtypeStruct(tiles, jnp.float32),
        ],
        scratch_shapes=[
            pltpu.VMEM(steering.shape, jnp.float32),
            pltpu.VMEM(survey.shape, jnp.float32),
            pltpu.VMEM(ref.shape, jnp.float32),
            pltpu.SemaphoreType.DMA,
            pltpu.SemaphoreType.DMA((CHUNKS,)),
            pltpu.SemaphoreType.DMA,
        ],
        compiler_params=params(),
        cost_estimate=cost(2.2),
        name="beams",
    )(*(pltpu.with_memory_space_constraint(x, pltpu.HBM) for x in (steering, survey, ref)))


def sum_kernel(count, *refs):
    kept_ref, sent_ref = refs[-2:]
    for n in range(kept_ref.shape[0]):
        for offset, out_ref in ((0, kept_ref), (1, sent_ref)):
            total = refs[0][2 * n + offset]
            for ref in refs[1:count]:
                total = total + ref[2 * n + offset]
            out_ref[n] = total


def sum_call(parts):
    shape = (parts[0].shape[0] // 2,) + parts[0].shape[1:]
    out = jax.ShapeDtypeStruct(shape, jnp.float32)
    vmem = pl.BlockSpec(memory_space=pltpu.VMEM)
    return pl.pallas_call(
        functools.partial(sum_kernel, len(parts)),
        in_specs=[vmem] * len(parts),
        out_specs=[vmem, vmem],
        out_shape=[out, out],
        compiler_params=params(),
        cost_estimate=cost(0.1),
        name="halves_summed",
    )(*parts)


def join_kernel(first_ref, second_ref, *refs):
    out_ref = refs[-1]
    count = first_ref.shape[0]
    out_ref[:count] = first_ref[...]
    out_ref[count:] = second_ref[...]


def join_call(first, second, *after):
    vmem = pl.BlockSpec(memory_space=pltpu.VMEM)
    return pl.pallas_call(
        join_kernel,
        in_specs=[vmem, vmem] + [pl.BlockSpec(memory_space=pl.ANY)] * len(after),
        out_shape=jax.ShapeDtypeStruct((2 * first.shape[0],) + first.shape[1:], jnp.float32),
        compiler_params=params(),
        cost_estimate=cost(1.0),
        name="reference_joined",
    )(first, second, *after)


def spread_line(line, keep):
    for g in range(0, LANES, 2 * SUBLANES):
        tiled = jnp.broadcast_to(line, (2 * SUBLANES, line.shape[1]))
        for h, value in enumerate(halves(pltpu.roll(tiled, g, 1, stride=1, stride_axis=0)[:, LANES:])):
            keep(h, g, value)


def table_kernel(tiles_ref, out_ref):
    for c in range(2):
        line = jnp.concatenate([tiles_ref[c, n : n + 1, :] for n in range(tiles_ref.shape[1])], 1)

        def keep(h, g, value):
            out_ref[h, c, g : g + 2 * SUBLANES] = value

        spread_line(line, keep)


def table_call(tiles):
    shape = (2, 2, LANES, LANES * (tiles.shape[1] - 1))
    return pl.pallas_call(
        table_kernel,
        out_shape=jax.ShapeDtypeStruct(shape, jnp.bfloat16),
        compiler_params=params(),
        cost_estimate=cost(0.7),
        name="shifted_reference",
    )(tiles)


def lag_kernel(groups, part_count, *refs):
    y_refs, refs = refs[:part_count], refs[part_count:]
    table_ref, tiles_ref, *round_refs, _, out_hbm, out_ref, out_sem, first_ref = refs
    copies = []

    me = lax.axis_index("tm")
    for c in range(2):
        tails = [ref[ref.shape[0] - 1, c, ref.shape[2] - EDGE :, :] for ref in round_refs]
        before = jnp.where(me % 2 == 1, tails[0], jnp.where(me > 0, tails[-1], 0.0))
        line = jnp.concatenate([before[n : n + 1] for n in range(EDGE)] + [tiles_ref[c, 0:1, :]], 1)

        def keep(h, g, value):
            first_ref[h, c, g : g + 2 * SUBLANES] = value

        spread_line(line, keep)

    def table_tile(h, n):
        parts = []
        for c in range(2):
            known = first_ref.shape[3] // LANES
            ref, at = (first_ref, n) if n < known else (table_ref, n - known)
            parts.append(ref[h, c, :, at * LANES : (at + 1) * LANES])
        return jnp.concatenate(parts, 1)

    def send(start, count):
        part = (slice(None), pl.ds(start, count))
        copies.append(pltpu.make_async_copy(out_ref.at[part], out_hbm.at[part], out_sem.at[len(copies)]))
        copies[-1].start()

    y = y_refs[0][...]
    for y_ref in y_refs[1:]:
        y = y + y_ref[...]
    rows, length = y.shape
    blocks = length // BLOCK_LEN
    turned = jnp.concatenate(
        [pltpu.roll(y[r : r + SUBLANES], SUBLANES // 2, 0) for r in range(0, rows, SUBLANES)], 0
    )
    turned = turned * row_sign(turned.shape)
    y_high, y_low = halves(y)
    t_high, t_low = halves(turned)

    def half_block(q, b):
        cols = slice(q * BLOCK_LEN + b * LANES, q * BLOCK_LEN + (b + 1) * LANES)
        return [jnp.concatenate([x[:, cols], t[:, cols]], 1) for x, t in ((y_high, t_high), (y_low, t_low))]

    def products(stack, n, count):
        high, low = (jnp.concatenate([table_tile(h, n + i) for i in range(count)], 0) for h in range(2))
        by_high = dot_nt(jnp.concatenate([part for pair in stack for part in pair], 0), high)
        by_low = dot_nt(jnp.concatenate([pair[0] for pair in stack], 0), low)
        return [
            by_high[2 * i * rows : (2 * i + 1) * rows]
            + (by_high[(2 * i + 1) * rows : 2 * (i + 1) * rows] + by_low[i * rows : (i + 1) * rows])
            for i in range(len(stack))
        ]

    taps_sum = None
    (far,) = products([half_block(0, 0)], 0, 1)
    for q in range(blocks):
        stack = [half_block(q, 0), half_block(q, 1)]
        if q + 1 < blocks:
            stack.append(half_block(q + 1, 0))
        first, second, *after = products(stack, 2 * q + 1, 2)
        product = jnp.concatenate([first[:, :LANES] + second[:, LANES:], second[:, :LANES] + far], 1)
        if after:
            far = after[0][:, LANES:]
        taps = product[:, :LANES]
        taps_sum = taps if taps_sum is None else taps_sum + taps
        for h in range(LAGS // LANES):
            lanes = slice(h * LANES, (h + 1) * LANES)
            tiles = [product[r : r + SUBLANES, lanes] for r in range(0, rows, SUBLANES)]
            for j, tile in enumerate(swap_groups(tiles, groups)):
                out_ref[h * groups + j, q] = tile
        if q % 2:
            send(q - 1, 2)
    left = lax.broadcasted_iota(jnp.int32, (SUBLANES, LANES), 1) < TAPS
    for i in range(groups // 2):
        a = taps_sum[i * SUBLANES : (i + 1) * SUBLANES]
        other = i + groups // 2
        b = taps_sum[other * SUBLANES : (other + 1) * SUBLANES]
        tile = jnp.where(left, a, pltpu.roll(b, LANES - TAPS, 1))
        for owner in range(out_ref.shape[0]):
            out_ref[owner, blocks + i] = tile
    send(blocks, groups // 2)
    for copy in copies:
        copy.wait()


def lag_call(ys, table, tiles, rounds, after, groups, owners):
    blocks = ys[0].shape[1] // BLOCK_LEN
    shape = (owners, blocks + groups // 2, SUBLANES, LANES)
    vmem = pl.BlockSpec(memory_space=pltpu.VMEM)
    return pl.pallas_call(
        functools.partial(lag_kernel, groups, len(ys)),
        in_specs=[vmem] * (len(ys) + 2 + len(rounds)) + [pl.BlockSpec(memory_space=pl.ANY)],
        out_specs=pl.BlockSpec(memory_space=pltpu.HBM),
        out_shape=jax.ShapeDtypeStruct(shape, jnp.float32),
        scratch_shapes=[
            pltpu.VMEM(shape, jnp.float32),
            pltpu.SemaphoreType.DMA((blocks // 2 + 1,)),
            pltpu.VMEM((2, 2, LANES, 2 * LANES), jnp.bfloat16),
        ],
        compiler_params=params(),
        cost_estimate=cost(2.1),
        name="lag_products",
    )(*ys, table, tiles, *rounds, after)


BATCH = 4


def own_kernel(lags_local, *refs):
    *part_refs, _, out_ref, line_ref, tail_ref, span_ref, late_ref, taps_a, lags_a, taps_b, lags_b = refs
    me = lax.axis_index("tm")
    part_rows = part_refs[0].shape[2]
    owners = sum(part_ref.shape[0] for part_ref in part_refs)
    samples = owners * part_rows * LANES
    steps = samples // BLOCK_LEN // BATCH
    total_rows = span_ref.shape[1]
    block_rows = BLOCK_LEN // LANES

    span_ref[...] = jnp.zeros_like(span_ref)
    n = 0
    for part_ref in part_refs:
        for i in range(part_ref.shape[0]):
            block = lax.rem(me - (n // 2) * 2 + owners, owners) ^ (n % 2)
            span_ref[:, pl.ds(EDGE + block * part_rows, part_rows), :] = part_ref[i]
            n += 1
    late_rows = (me * lags_local) // LANES
    late_lanes = lax.rem(me * lags_local, LANES)
    turned = [pltpu.roll(span_ref[c], late_lanes, 1) for c in range(2)]
    before = [pltpu.roll(x, 1, 0) for x in turned]
    lanes = lax.broadcasted_iota(jnp.int32, (total_rows, LANES), 1)
    for c in range(2):
        late_ref[c] = pltpu.roll(jnp.where(lanes < late_lanes, before[c], turned[c]), late_rows, 0)

    def line_of(ref, c, first, count):
        return jnp.concatenate([ref[c, pl.ds(first + n, 1), :] for n in range(count)], 1)

    def shifted(line, by):
        tiled = jnp.broadcast_to(line, (2 * SUBLANES, line.shape[1]))
        return pltpu.roll(tiled, by, 1, stride=1, stride_axis=0)[:, LANES:]

    def keep(ref, row, value):
        high, low = halves(value)
        half = ref.shape[0] // 2
        ref[row : row + 2 * SUBLANES, :] = high
        ref[half + row : half + row + 2 * SUBLANES, :] = low

    def build(n, taps_ref, lags_ref):
        first = EDGE - 1 + n * BATCH * block_rows
        count = BATCH * block_rows + 1
        lines = [line_of(span_ref, c, first, count) for c in range(2)]
        for c in range(2):
            for g in range(0, TAPS, 2 * SUBLANES):
                keep(taps_ref, c * TAPS + g, shifted(lines[c], g))
            late = line_of(late_ref, c, first, count)
            for g in range(0, lags_local, 2 * SUBLANES):
                keep(lags_ref, c * lags_local + g, shifted(late, g))
        pad = jnp.zeros((2 * SUBLANES - 2, BATCH * BLOCK_LEN), jnp.float32)
        keep(lags_ref, 2 * lags_local, jnp.concatenate([line[:, LANES:] for line in lines] + [pad], 0))

    turn = lane_sign((lags_local, LANES))

    def use(n, taps_ref, lags_ref):
        count = lags_ref.shape[0] // 2
        for b in range(BATCH):
            cols = slice(b * BLOCK_LEN, (b + 1) * BLOCK_LEN)
            product = dot_nt(lags_ref[:, cols], taps_ref[:, cols])
            product = product[:count, :LANES] + (product[:count, LANES:] + product[count:, :LANES])
            by_real = product[:lags_local]
            by_imag = product[lags_local : 2 * lags_local]
            rows = pl.ds(pl.multiple_of((n * BATCH + b) * lags_local, lags_local), lags_local)
            high, low = halves(by_real + turn * pltpu.roll(by_imag, TAPS, 1))
            out_ref[0, rows, :] = high
            out_ref[1, rows, :] = low
            line_ref[...] += product[2 * lags_local : 2 * lags_local + SUBLANES]

    line_ref[...] = jnp.zeros_like(line_ref)
    build(0, taps_a, lags_a)

    def pair(m, carry):
        build(2 * m + 1, taps_b, lags_b)
        use(2 * m, taps_a, lags_a)
        build(jnp.minimum(2 * m + 2, steps - 1), taps_a, lags_a)
        use(2 * m + 1, taps_b, lags_b)
        return carry

    lax.fori_loop(0, steps // 2, pair, 0)
    tail = []
    for c in range(2):
        line = line_of(span_ref, c, EDGE + owners * part_rows - 1, 2)
        tail += [shifted(line, g) for g in range(0, TAPS, 2 * SUBLANES)]
    tail = jnp.concatenate(tail, 0)
    tail_ref[...] = dot_nt(tail, tail, HIGHEST)


def own_call(parts, lags_local, after):
    part_rows = parts[0].shape[2]
    span_rows = part_rows * sum(part.shape[0] for part in parts)
    rows = span_rows * LANES // BLOCK_LEN * lags_local
    held_rows = -(-(span_rows + 2 * EDGE) // SUBLANES) * SUBLANES
    width = BATCH * BLOCK_LEN
    taps = pltpu.VMEM((4 * TAPS, width), jnp.bfloat16)
    lags = pltpu.VMEM((4 * lags_local + 4 * SUBLANES, width), jnp.bfloat16)
    span = pltpu.VMEM((2, held_rows, LANES), jnp.float32)
    return pl.pallas_call(
        functools.partial(own_kernel, lags_local),
        in_specs=[pl.BlockSpec(memory_space=pltpu.VMEM)] * len(parts) + [pl.BlockSpec(memory_space=pl.ANY)],
        out_shape=[
            jax.ShapeDtypeStruct((2, rows, 2 * TAPS), jnp.bfloat16),
            jax.ShapeDtypeStruct((SUBLANES, 2 * TAPS), jnp.float32),
            jax.ShapeDtypeStruct((2 * TAPS, 2 * TAPS), jnp.float32),
        ],
        scratch_shapes=[span, span, taps, lags, taps, lags],
        compiler_params=params(),
        cost_estimate=cost(6.2),
        name="reference_products",
    )(*parts, after)


def as_factor(a):
    return jnp.concatenate([a, -lane_sign(a.shape) * pltpu.roll(a, a.shape[0], 1)], 0)


def solver_kernel(line_ref, tail_ref, gram_ref, solver_ref):
    total = line_ref[...]
    line = total[0:1] + lane_sign((1, LANES)) * pltpu.roll(total[1:2], TAPS, 1)
    low = lax.broadcasted_iota(jnp.int32, (1, LANES), 1) < TAPS
    line_r = jnp.where(low, line, 0.0)
    line_i = jnp.where(low, pltpu.roll(line, TAPS, 1), 0.0)
    cols = lax.broadcasted_iota(jnp.int32, (TAPS, TAPS), 1)
    rows = lax.broadcasted_iota(jnp.int32, (TAPS, TAPS), 0)
    above = cols > rows

    def upper(x):
        spread = pltpu.roll(jnp.broadcast_to(x, (TAPS, LANES)), 0, 1, stride=1, stride_axis=0)
        return spread[:, :TAPS]

    up_r = upper(line_r)
    up_i = jnp.where(above, upper(line_i), 0.0)
    strict_r = jnp.where(above, up_r, 0.0)
    diag_r = jnp.where(cols == rows, up_r, 0.0)
    tails = tail_ref[...]
    gram_r = strict_r + strict_r.T + diag_r - (tails[:TAPS, :TAPS] + tails[TAPS:, TAPS:])
    gram_i = up_i - up_i.T - (tails[:TAPS, TAPS:] - tails[TAPS:, :TAPS])
    gram = jnp.concatenate([gram_r, gram_i], 1)
    gram_halves = halves(as_factor(gram))
    gram_ref[0], gram_ref[1] = gram_halves
    one = (
        lax.broadcasted_iota(jnp.int32, gram.shape, 0) == lax.broadcasted_iota(jnp.int32, gram.shape, 1)
    ).astype(jnp.float32)
    bound = jnp.max(jnp.sum(jnp.abs(gram), axis=1, keepdims=True), axis=0, keepdims=True)

    def again(state):
        count, left, _ = state
        return (count < 60) & (left > 1e-3)

    def newton(state):
        count, _, x = state
        x_halves = halves(x)
        seen = dot_split(x_halves, gram_halves)
        left = jnp.max(jnp.abs(seen - one))
        x = 2.0 * x - dot_split(halves(seen), halves(as_factor(x)))
        return count + 1, left, x

    start = (jnp.int32(0), jnp.float32(1.0), one * (1.0 / bound))
    _, _, inverse = lax.while_loop(again, newton, start)
    solver_ref[0], solver_ref[1] = halves(as_factor(inverse))


def solver_call(line, tail):
    out = jax.ShapeDtypeStruct((2,) + tail.shape, jnp.bfloat16)
    return pl.pallas_call(
        solver_kernel,
        out_shape=[out, out],
        compiler_params=params(),
        cost_estimate=cost(2.0),
        name="gram_inverse",
    )(line, tail)


def doppler_table(block_count, scale):
    phase = (np.arange(block_count)[:, None] * np.arange(DOPPLER)[None, :] % DOPPLER) * (2.0 * math.pi / DOPPLER)
    cosine, sine = np.cos(phase), np.sin(phase)
    upper = np.concatenate([cosine, -sine], 1)
    lower = np.concatenate([sine, cosine], 1)
    return (np.concatenate([upper, lower], 0) * scale).astype(np.float32)


def map_kernel(groups, got_ref, own_ref, gram_ref, solver_ref, wave_ref, out_hbm, held_ref, out_ref, out_sem):
    owners, pieces = got_ref.shape[:2]
    blocks = pieces - groups // 2
    lags_local = LANES // groups
    total = owners * blocks
    left = lax.broadcasted_iota(jnp.int32, (SUBLANES, LANES), 1) < TAPS
    sign = row_sign((SUBLANES, LANES))
    rows = [None] * groups
    for i in range(groups // 2):
        tile = got_ref[0, blocks + i]
        for owner in range(1, owners):
            tile = tile + got_ref[owner, blocks + i]
        swapped = pltpu.roll(tile, TAPS, 1)
        for part, here, there in ((i, tile, swapped), (i + groups // 2, swapped, tile)):
            other = -sign * pltpu.roll(there, SUBLANES // 2, 0)
            rows[part] = jnp.where(left, here, other)
    cross = jnp.concatenate(rows, 0)
    solver = (solver_ref[0], solver_ref[1])
    taps = dot_split(halves(cross), solver)
    rest = cross - dot_split(halves(taps), (gram_ref[0], gram_ref[1]))
    taps = taps + dot_split(halves(rest), solver)
    taps_high, taps_low = halves(taps)
    taps_both = jnp.concatenate([taps_high, taps_low], 0)
    count = taps.shape[0]
    for q in range(0, total, 2 * groups):
        own = slice(q * lags_local, (q + 2 * groups) * lags_local)
        by_high = dot_nt(taps_both, own_ref[0, own, :])
        clutter = by_high[:count] + (by_high[count:] + dot_nt(taps_high, own_ref[1, own, :]))
        for h in range(2):
            lanes = slice(h * LANES, (h + 1) * LANES)
            tiles = [clutter[r : r + SUBLANES, lanes] for r in range(0, groups * SUBLANES, SUBLANES)]
            for j, tile in enumerate(swap_groups(tiles, groups)):
                at = q + h * groups + j
                held_ref[at * SUBLANES : (at + 1) * SUBLANES, :] = got_ref[at // blocks, at % blocks] - tile
    half = SUBLANES // 2
    copies = []
    for g in range(half):
        parts = [held_ref[pl.ds(c * half + g, total, stride=SUBLANES), :] for c in range(2)]
        high, low = halves(jnp.concatenate(parts, 0).T)
        by_high = jnp.dot(jnp.concatenate([high, low], 0), wave_ref[0], preferred_element_type=jnp.float32)
        by_low = jnp.dot(high, wave_ref[1], preferred_element_type=jnp.float32)
        spectrum = by_high[:LANES] + (by_high[LANES:] + by_low)
        for i in range(groups):
            for c in range(2):
                out_ref[i, g, c] = spectrum[i * lags_local : (i + 1) * lags_local, c * DOPPLER : (c + 1) * DOPPLER]
        part = (slice(None), pl.ds(g, 1))
        copies.append(pltpu.make_async_copy(out_ref.at[part], out_hbm.at[part], out_sem.at[g]))
        copies[-1].start()
    for copy in copies:
        copy.wait()


def map_call(got, own, gram, solver, wave, groups, beams_local):
    total = got.shape[0] * (got.shape[1] - groups // 2)
    lags_local = LANES // groups
    half = SUBLANES // 2
    shape = (beams_local // half, half, 2, lags_local, DOPPLER)
    out = pl.pallas_call(
        functools.partial(map_kernel, groups),
        in_specs=[pl.BlockSpec(memory_space=pltpu.VMEM)] * 5,
        out_specs=pl.BlockSpec(memory_space=pltpu.HBM),
        out_shape=jax.ShapeDtypeStruct(shape, jnp.float32),
        scratch_shapes=[
            pltpu.VMEM((total * SUBLANES, LANES), jnp.float32),
            pltpu.VMEM(shape, jnp.float32),
            pltpu.SemaphoreType.DMA((half,)),
        ],
        compiler_params=params(),
        cost_estimate=cost(2.5),
        name="range_doppler",
    )(got, own, gram, solver, wave)
    return out.reshape((beams_local,) + shape[2:])


def swap(x, axis, by):
    pairs = [(i, i ^ by) for i in range(lax.axis_size(axis))]
    return lax.ppermute(x, axis, pairs)


def tiled_device(ref_signal, surveillance, steering):
    chan_count, tm_count = lax.axis_size("chan"), lax.axis_size("tm")
    channels, length = surveillance.shape[1:]
    beams_local = steering.shape[1] // chan_count
    lags_local = LAGS // tm_count
    groups = LANES // lags_local
    samples = length * tm_count

    survey = surveillance.reshape(2 * channels, length)
    kept, moved, tiles = beam_call(steering, survey, ref_signal, chan_count, beams_local)
    near = swap(tiles[None], "tm", 1)
    shape = (chan_count // 2, 2 * beams_local, length)
    kept, got = kept.reshape(shape), swap(moved, "chan", 1).reshape(shape)
    by = 2
    while by < chan_count:
        kept, moved = sum_call([kept, got])
        got = swap(moved, "chan", by)
        by *= 2
    rounds = [near]
    joined = join_call(tiles[None], near, moved)
    while True:
        count = joined.shape[0]
        rounds.append(lax.ppermute(joined, "tm", [(i, (i + count) % tm_count) for i in range(tm_count)]))
        if count * 2 == tm_count:
            break
        joined = join_call(joined, rounds[-1])
    table = table_call(tiles)
    pieces = lag_call([kept[0], got[0]], table, tiles, rounds[:2], joined, groups, tm_count)
    got = lax.all_to_all(pieces, "tm", 0, 0, tiled=True)
    own, line, tail = own_call([tiles[None]] + rounds, lags_local, pieces)
    gram, solver = solver_call(line, tail)
    wave = doppler_table(samples // BLOCK_LEN, 0.125 / math.sqrt(samples))
    high = wave.astype(jnp.bfloat16)
    wave = np.stack([high, (wave - high.astype(np.float32)).astype(jnp.bfloat16)])
    return map_call(got, own, gram, solver, jnp.asarray(wave), groups, beams_local)


def lag_table(ref_ext, offset, lags):
    window = lax.dynamic_slice_in_dim(ref_ext, offset, BLOCK_LEN + LAGS, 1)
    span = BLOCK_LEN + LAGS
    tiled = jnp.tile(jnp.pad(window, ((0, 0), (0, 1))), (1, lags))[:, : lags * span]
    return tiled.reshape(2, lags, span)[:, :, LAGS:]


def times_conj(a, b):
    real = jnp.einsum("...t,lt->...l", a[..., 0, :], b[0], precision=HIGHEST) + jnp.einsum(
        "...t,lt->...l", a[..., 1, :], b[1], precision=HIGHEST
    )
    imag = jnp.einsum("...t,lt->...l", a[..., 1, :], b[0], precision=HIGHEST) - jnp.einsum(
        "...t,lt->...l", a[..., 0, :], b[1], precision=HIGHEST
    )
    return jnp.stack([real, imag], -2)


def plain_device(ref_signal, surveillance, steering):
    chan_count, tm_count = lax.axis_size("chan"), lax.axis_size("tm")
    length = surveillance.shape[2]
    beams = steering.shape[1]
    lags_local = LAGS // tm_count
    samples = length * tm_count
    local_blocks = length // BLOCK_LEN
    here = lax.axis_index("tm")

    w_real, w_imag = steering
    real = jnp.dot(w_real, surveillance[0], precision=HIGHEST) - jnp.dot(w_imag, surveillance[1], precision=HIGHEST)
    imag = jnp.dot(w_imag, surveillance[0], precision=HIGHEST) + jnp.dot(w_real, surveillance[1], precision=HIGHEST)
    beam = lax.psum_scatter(jnp.stack([real, imag], 1), "chan", scatter_dimension=0, tiled=True)
    ref_all = lax.all_gather(ref_signal, "tm", axis=1, tiled=True)
    ref_ext = jnp.pad(ref_all, ((0, 0), (LAGS, 0)))

    def beam_step(carry, q):
        offset = q * BLOCK_LEN
        table = lag_table(ref_ext, here * length + offset, LAGS)
        segment = lax.dynamic_slice_in_dim(beam, offset, BLOCK_LEN, 2)
        return carry, times_conj(segment, table)

    _, products = lax.scan(beam_step, None, jnp.arange(local_blocks, dtype=jnp.int32))
    cross = lax.psum(products[..., :TAPS].sum(0), "tm")
    got = lax.all_to_all(products, "tm", 3, 0, tiled=True)

    def own_step(gram, q):
        offset = q * BLOCK_LEN
        table = lag_table(ref_ext, offset, LAGS)
        taps = table[:, :TAPS].transpose(1, 0, 2)
        mine = lax.dynamic_slice_in_dim(table, here * lags_local, lags_local, 1)
        return gram + times_conj(taps, table[:, :TAPS]), times_conj(taps, mine)

    start = jnp.zeros((TAPS, 2, TAPS), jnp.float32)
    gram, own = lax.scan(own_step, start, jnp.arange(samples // BLOCK_LEN, dtype=jnp.int32))
    g_real, g_imag = gram[:, 0].T, gram[:, 1].T
    system = jnp.concatenate([jnp.concatenate([g_real, -g_imag], 1), jnp.concatenate([g_imag, g_real], 1)], 0)
    right = jnp.concatenate([cross[:, 0].T, cross[:, 1].T], 0)
    solved = jax.scipy.linalg.cho_solve((jnp.linalg.cholesky(system), True), right)
    b_real, b_imag = solved[:TAPS].T, solved[TAPS:].T
    mixing = jnp.concatenate([jnp.stack([b_real, b_imag], 1), jnp.stack([-b_imag, b_real], 1)], 2)
    stacked = jnp.concatenate([own[:, :, 0], own[:, :, 1]], 1)
    lagged = got - jnp.einsum("mck,qkl->qmcl", mixing, stacked, precision=HIGHEST)
    wave = jnp.asarray(doppler_table(samples // BLOCK_LEN, 0.125 / math.sqrt(samples)))
    wave = wave.reshape(2, samples // BLOCK_LEN, 2, DOPPLER)
    return jnp.einsum("qmcl,cqdk->mdlk", lagged, wave, precision=HIGHEST)


def on_device(ref_signal, surveillance, steering):
    chan_count, tm_count = lax.axis_size("chan"), lax.axis_size("tm")
    beams_local = steering.shape[1] // chan_count
    lags_local = LAGS // tm_count
    fills = (
        LANES % lags_local == 0
        and lags_local % (2 * SUBLANES) == 0
        and beams_local * lags_local == LANES * SUBLANES // 2
        and chan_count > 1
        and chan_count & (chan_count - 1) == 0
        and tm_count > 2
        and tm_count & (tm_count - 1) == 0
        and 2 * surveillance.shape[1] % LANES == 0
        and surveillance.shape[2] % (2 * BATCH * BLOCK_LEN) == 0
    )
    device = tiled_device if fills else plain_device
    return device(ref_signal, surveillance, steering)


def solution(mesh):
    placed = (P(None, "tm"), P(None, "chan", "tm"), P(None, None, "chan"))
    return jax.shard_map(
        on_device,
        mesh=mesh,
        in_specs=placed,
        out_specs=P("chan", None, "tm", None),
        check_vma=False,
    )
```

```python
import functools
import math

import jax
import jax.numpy as jnp
import numpy as np
from jax import lax
from jax.experimental import pallas as pl
from jax.experimental.pallas import tpu as pltpu
from jax.sharding import PartitionSpec as P

LAGS = 256
DOPPLER = 256
TAPS = 64
BLOCK_LEN = 256
LANES = 128
SUBLANES = 8
EDGE = 2

HIGHEST = lax.Precision.HIGHEST
VMEM_BYTES = 48 * 1024 * 1024


def params():
    return pltpu.CompilerParams(vmem_limit_bytes=VMEM_BYTES)


def cost(us):
    return pl.CostEstimate(flops=int(us * 1.15e9), bytes_accessed=0, transcendentals=0)


def halves(x):
    high = x.astype(jnp.bfloat16)
    return high, (x - high.astype(jnp.float32)).astype(jnp.bfloat16)


def dot_nt(a, b, precision=None):
    return lax.dot_general(
        a, b, (((1,), (1,)), ((), ())), precision=precision, preferred_element_type=jnp.float32
    )


def dot_split(a, b):
    (a_high, a_low), (b_high, b_low) = a, b
    left = jnp.concatenate([a_high, a_low], 1)
    right = jnp.concatenate([b_high, b_high], 0)
    return jnp.dot(left, right, preferred_element_type=jnp.float32) + jnp.dot(
        a_high, b_low, preferred_element_type=jnp.float32
    )


def row_sign(shape):
    rows = lax.broadcasted_iota(jnp.int32, shape, 0)
    return jnp.where(rows % SUBLANES < SUBLANES // 2, 1.0, -1.0).astype(jnp.float32)


def lane_sign(shape):
    lanes = lax.broadcasted_iota(jnp.int32, shape, 1)
    return jnp.where(lanes % LANES < LANES // 2, 1.0, -1.0).astype(jnp.float32)


def swap_groups(rows, groups):
    width = LANES // groups
    lane_group = lax.broadcasted_iota(jnp.int32, rows[0].shape, 1) // width
    outs = []
    for j in range(groups):
        out = rows[j]
        for i in range(groups):
            if i != j:
                moved = pltpu.roll(rows[i], (width * (i - j)) % LANES, 1)
                out = jnp.where(lane_group == i, moved, out)
        outs.append(out)
    return outs


COPIES = 4


def beam_kernel(
    chan_count, beams_local, w_hbm, s_hbm, ref_hbm, kept_ref, sent_ref, tiles_ref,
    w_ref, s_ref, ref_ref, w_sem, s_sem, ref_sem,
):
    me = lax.axis_index("chan")
    depth = s_hbm.shape[0] // COPIES
    w_copy = pltpu.make_async_copy(w_hbm, w_ref, w_sem)
    w_copy.start()
    ref_copy = pltpu.make_async_copy(ref_hbm, ref_ref, ref_sem)
    ref_copy.start()
    s_copies = []
    for n in range(COPIES):
        part = pl.ds(n * depth, depth)
        s_copies.append(pltpu.make_async_copy(s_hbm.at[part], s_ref.at[part], s_sem.at[n]))
        s_copies[n].start()
    half = SUBLANES // 2
    sub = lax.broadcasted_iota(jnp.int32, (SUBLANES, w_hbm.shape[2]), 0)
    top = sub < half
    w_copy.wait()
    rows = []
    for parity in range(2):
        for e in range(parity, chan_count, 2):
            base = (me ^ e) * beams_local
            for tile in range(beams_local // SUBLANES):
                start = pl.multiple_of(base + tile * SUBLANES, SUBLANES)
                wr = w_ref[0, pl.ds(start, SUBLANES), :]
                wi = w_ref[1, pl.ds(start, SUBLANES), :]
                wr_s = pltpu.roll(wr, half, 0)
                wi_s = pltpu.roll(wi, half, 0)
                first = [jnp.where(top, wr, wi_s), jnp.where(top, -wi, wr_s)]
                second = [jnp.where(top, wr_s, wi), jnp.where(top, -wi_s, wr)]
                rows.append(jnp.concatenate(first, 1))
                rows.append(jnp.concatenate(second, 1))
    weights = jnp.concatenate(halves(jnp.concatenate(rows, 0)), 0)
    count = weights.shape[0] // 2
    ref_copy.wait()
    for c in range(2):
        for n in range(tiles_ref.shape[1]):
            tiles_ref[c, n : n + 1, :] = ref_ref[c : c + 1, n * LANES : (n + 1) * LANES]
    mid = count // 2
    for copy in s_copies:
        copy.wait()
    high, low = halves(s_ref[...])
    by_high = jnp.dot(weights, high, preferred_element_type=jnp.float32)
    by_low = jnp.dot(weights[:count], low, preferred_element_type=jnp.float32)
    product = by_high[:count] + (by_high[count:] + by_low)
    kept_ref[...] = product[:mid]
    sent_ref[...] = product[mid:]


def beam_call(steering, survey, ref, chan_count, beams_local):
    depth, length = survey.shape
    rows = chan_count * beams_local
    tiles = (2, length // LANES, LANES)
    out = jax.ShapeDtypeStruct((rows, length), jnp.float32)
    hbm, vmem = pl.BlockSpec(memory_space=pltpu.HBM), pl.BlockSpec(memory_space=pltpu.VMEM)
    return pl.pallas_call(
        functools.partial(beam_kernel, chan_count, beams_local),
        in_specs=[hbm] * 3,
        out_specs=[vmem] * 3,
        out_shape=[
            out,
            out,
            jax.ShapeDtypeStruct(tiles, jnp.float32),
        ],
        scratch_shapes=[
            pltpu.VMEM(steering.shape, jnp.float32),
            pltpu.VMEM(survey.shape, jnp.float32),
            pltpu.VMEM(ref.shape, jnp.float32),
            pltpu.SemaphoreType.DMA,
            pltpu.SemaphoreType.DMA((COPIES,)),
            pltpu.SemaphoreType.DMA,
        ],
        compiler_params=params(),
        cost_estimate=cost(2.2),
        name="beams",
    )(*(pltpu.with_memory_space_constraint(x, pltpu.HBM) for x in (steering, survey, ref)))


def sum_kernel(count, *refs):
    kept_ref, sent_ref = refs[-2:]
    for n in range(kept_ref.shape[0]):
        for offset, out_ref in ((0, kept_ref), (1, sent_ref)):
            total = refs[0][2 * n + offset]
            for ref in refs[1:count]:
                total = total + ref[2 * n + offset]
            out_ref[n] = total


def sum_call(parts):
    shape = (parts[0].shape[0] // 2,) + parts[0].shape[1:]
    out = jax.ShapeDtypeStruct(shape, jnp.float32)
    vmem = pl.BlockSpec(memory_space=pltpu.VMEM)
    return pl.pallas_call(
        functools.partial(sum_kernel, len(parts)),
        in_specs=[vmem] * len(parts),
        out_specs=[vmem, vmem],
        out_shape=[out, out],
        compiler_params=params(),
        cost_estimate=cost(0.1),
        name="halves_summed",
    )(*parts)


def join_kernel(first_ref, second_ref, *refs):
    out_ref = refs[-1]
    count = first_ref.shape[0]
    out_ref[:count] = first_ref[...]
    out_ref[count:] = second_ref[...]


def join_call(first, second, *after):
    vmem = pl.BlockSpec(memory_space=pltpu.VMEM)
    return pl.pallas_call(
        join_kernel,
        in_specs=[vmem, vmem] + [pl.BlockSpec(memory_space=pl.ANY)] * len(after),
        out_shape=jax.ShapeDtypeStruct((2 * first.shape[0],) + first.shape[1:], jnp.float32),
        compiler_params=params(),
        cost_estimate=cost(1.0),
        name="reference_joined",
    )(first, second, *after)


def spread_line(line, keep):
    for g in range(0, LANES, 2 * SUBLANES):
        tiled = jnp.broadcast_to(line, (2 * SUBLANES, line.shape[1]))
        for h, value in enumerate(halves(pltpu.roll(tiled, g, 1, stride=1, stride_axis=0)[:, LANES:])):
            keep(h, g, value)


def table_kernel(tiles_ref, out_ref):
    for c in range(2):
        line = jnp.concatenate([tiles_ref[c, n : n + 1, :] for n in range(tiles_ref.shape[1])], 1)

        def keep(h, g, value):
            out_ref[h, c, g : g + 2 * SUBLANES] = value

        spread_line(line, keep)


def table_call(tiles):
    shape = (2, 2, LANES, LANES * (tiles.shape[1] - 1))
    return pl.pallas_call(
        table_kernel,
        out_shape=jax.ShapeDtypeStruct(shape, jnp.bfloat16),
        compiler_params=params(),
        cost_estimate=cost(0.7),
        name="shifted_reference",
    )(tiles)


def lag_kernel(groups, part_count, *refs):
    y_refs, refs = refs[:part_count], refs[part_count:]
    table_ref, tiles_ref, *round_refs, _, out_hbm, out_ref, out_sem, first_ref = refs
    copies = []

    me = lax.axis_index("tm")
    for c in range(2):
        tails = [ref[ref.shape[0] - 1, c, ref.shape[2] - EDGE :, :] for ref in round_refs]
        before = jnp.where(me % 2 == 1, tails[0], jnp.where(me > 0, tails[-1], 0.0))
        line = jnp.concatenate([before[n : n + 1] for n in range(EDGE)] + [tiles_ref[c, 0:1, :]], 1)

        def keep(h, g, value):
            first_ref[h, c, g : g + 2 * SUBLANES] = value

        spread_line(line, keep)

    def table_tile(h, n):
        parts = []
        for c in range(2):
            known = first_ref.shape[3] // LANES
            ref, at = (first_ref, n) if n < known else (table_ref, n - known)
            parts.append(ref[h, c, :, at * LANES : (at + 1) * LANES])
        return jnp.concatenate(parts, 1)

    def send(start, count):
        part = (slice(None), pl.ds(start, count))
        copies.append(pltpu.make_async_copy(out_ref.at[part], out_hbm.at[part], out_sem.at[len(copies)]))
        copies[-1].start()

    y = y_refs[0][...]
    for y_ref in y_refs[1:]:
        y = y + y_ref[...]
    rows, length = y.shape
    blocks = length // BLOCK_LEN
    turned = jnp.concatenate(
        [pltpu.roll(y[r : r + SUBLANES], SUBLANES // 2, 0) for r in range(0, rows, SUBLANES)], 0
    )
    turned = turned * row_sign(turned.shape)
    y_high, y_low = halves(y)
    t_high, t_low = halves(turned)

    def half_block(q, b):
        cols = slice(q * BLOCK_LEN + b * LANES, q * BLOCK_LEN + (b + 1) * LANES)
        return [jnp.concatenate([x[:, cols], t[:, cols]], 1) for x, t in ((y_high, t_high), (y_low, t_low))]

    def products(stack, n, count):
        high, low = (jnp.concatenate([table_tile(h, n + i) for i in range(count)], 0) for h in range(2))
        by_high = dot_nt(jnp.concatenate([part for pair in stack for part in pair], 0), high)
        by_low = dot_nt(jnp.concatenate([pair[0] for pair in stack], 0), low)
        return [
            by_high[2 * i * rows : (2 * i + 1) * rows]
            + (by_high[(2 * i + 1) * rows : 2 * (i + 1) * rows] + by_low[i * rows : (i + 1) * rows])
            for i in range(len(stack))
        ]

    taps_sum = None
    (far,) = products([half_block(0, 0)], 0, 1)
    for q in range(blocks):
        stack = [half_block(q, 0), half_block(q, 1)]
        if q + 1 < blocks:
            stack.append(half_block(q + 1, 0))
        first, second, *after = products(stack, 2 * q + 1, 2)
        product = jnp.concatenate([first[:, :LANES] + second[:, LANES:], second[:, :LANES] + far], 1)
        if after:
            far = after[0][:, LANES:]
        taps = product[:, :LANES]
        taps_sum = taps if taps_sum is None else taps_sum + taps
        for h in range(LAGS // LANES):
            lanes = slice(h * LANES, (h + 1) * LANES)
            tiles = [product[r : r + SUBLANES, lanes] for r in range(0, rows, SUBLANES)]
            for j, tile in enumerate(swap_groups(tiles, groups)):
                out_ref[h * groups + j, q] = tile
        if q + 1 == blocks // 2:
            send(0, blocks // 2)
    left = lax.broadcasted_iota(jnp.int32, (SUBLANES, LANES), 1) < TAPS
    for i in range(groups // 2):
        a = taps_sum[i * SUBLANES : (i + 1) * SUBLANES]
        other = i + groups // 2
        b = taps_sum[other * SUBLANES : (other + 1) * SUBLANES]
        tile = jnp.where(left, a, pltpu.roll(b, LANES - TAPS, 1))
        for owner in range(out_ref.shape[0]):
            out_ref[owner, blocks + i] = tile
    send(blocks // 2, blocks - blocks // 2 + groups // 2)
    for copy in copies:
        copy.wait()


def lag_call(ys, table, tiles, rounds, after, groups, owners):
    blocks = ys[0].shape[1] // BLOCK_LEN
    shape = (owners, blocks + groups // 2, SUBLANES, LANES)
    vmem = pl.BlockSpec(memory_space=pltpu.VMEM)
    return pl.pallas_call(
        functools.partial(lag_kernel, groups, len(ys)),
        in_specs=[vmem] * (len(ys) + 2 + len(rounds)) + [pl.BlockSpec(memory_space=pl.ANY)],
        out_specs=pl.BlockSpec(memory_space=pltpu.HBM),
        out_shape=jax.ShapeDtypeStruct(shape, jnp.float32),
        scratch_shapes=[
            pltpu.VMEM(shape, jnp.float32),
            pltpu.SemaphoreType.DMA((2,)),
            pltpu.VMEM((2, 2, LANES, 2 * LANES), jnp.bfloat16),
        ],
        compiler_params=params(),
        cost_estimate=cost(2.1),
        name="lag_products",
    )(*ys, table, tiles, *rounds, after)


BATCH = 4


def own_kernel(lags_local, *refs):
    *part_refs, _, out_ref, line_ref, tail_ref, span_ref, late_ref, taps_a, lags_a, taps_b, lags_b = refs
    me = lax.axis_index("tm")
    part_rows = part_refs[0].shape[2]
    owners = sum(part_ref.shape[0] for part_ref in part_refs)
    samples = owners * part_rows * LANES
    steps = samples // BLOCK_LEN // BATCH
    total_rows = span_ref.shape[1]
    block_rows = BLOCK_LEN // LANES

    span_ref[...] = jnp.zeros_like(span_ref)
    n = 0
    for part_ref in part_refs:
        for i in range(part_ref.shape[0]):
            block = lax.rem(me - (n // 2) * 2 + owners, owners) ^ (n % 2)
            span_ref[:, pl.ds(EDGE + block * part_rows, part_rows), :] = part_ref[i]
            n += 1
    late_rows = (me * lags_local) // LANES
    late_lanes = lax.rem(me * lags_local, LANES)
    turned = [pltpu.roll(span_ref[c], late_lanes, 1) for c in range(2)]
    before = [pltpu.roll(x, 1, 0) for x in turned]
    lanes = lax.broadcasted_iota(jnp.int32, (total_rows, LANES), 1)
    for c in range(2):
        late_ref[c] = pltpu.roll(jnp.where(lanes < late_lanes, before[c], turned[c]), late_rows, 0)

    def line_of(ref, c, first, count):
        return jnp.concatenate([ref[c, pl.ds(first + n, 1), :] for n in range(count)], 1)

    def shifted(line, by):
        tiled = jnp.broadcast_to(line, (2 * SUBLANES, line.shape[1]))
        return pltpu.roll(tiled, by, 1, stride=1, stride_axis=0)[:, LANES:]

    def keep(ref, row, value):
        high, low = halves(value)
        half = ref.shape[0] // 2
        ref[row : row + 2 * SUBLANES, :] = high
        ref[half + row : half + row + 2 * SUBLANES, :] = low

    def build(n, taps_ref, lags_ref):
        first = EDGE - 1 + n * BATCH * block_rows
        count = BATCH * block_rows + 1
        lines = [line_of(span_ref, c, first, count) for c in range(2)]
        for c in range(2):
            for g in range(0, TAPS, 2 * SUBLANES):
                keep(taps_ref, c * TAPS + g, shifted(lines[c], g))
            late = line_of(late_ref, c, first, count)
            for g in range(0, lags_local, 2 * SUBLANES):
                keep(lags_ref, c * lags_local + g, shifted(late, g))
        pad = jnp.zeros((2 * SUBLANES - 2, BATCH * BLOCK_LEN), jnp.float32)
        keep(lags_ref, 2 * lags_local, jnp.concatenate([line[:, LANES:] for line in lines] + [pad], 0))

    turn = lane_sign((lags_local, LANES))

    def use(n, taps_ref, lags_ref):
        count = lags_ref.shape[0] // 2
        for b in range(BATCH):
            cols = slice(b * BLOCK_LEN, (b + 1) * BLOCK_LEN)
            product = dot_nt(lags_ref[:, cols], taps_ref[:, cols])
            product = product[:count, :LANES] + (product[:count, LANES:] + product[count:, :LANES])
            by_real = product[:lags_local]
            by_imag = product[lags_local : 2 * lags_local]
            rows = pl.ds(pl.multiple_of((n * BATCH + b) * lags_local, lags_local), lags_local)
            high, low = halves(by_real + turn * pltpu.roll(by_imag, TAPS, 1))
            out_ref[0, rows, :] = high
            out_ref[1, rows, :] = low
            line_ref[...] += product[2 * lags_local : 2 * lags_local + SUBLANES]

    line_ref[...] = jnp.zeros_like(line_ref)
    build(0, taps_a, lags_a)

    def pair(m, carry):
        build(2 * m + 1, taps_b, lags_b)
        use(2 * m, taps_a, lags_a)
        build(jnp.minimum(2 * m + 2, steps - 1), taps_a, lags_a)
        use(2 * m + 1, taps_b, lags_b)
        return carry

    lax.fori_loop(0, steps // 2, pair, 0)
    tail = []
    for c in range(2):
        line = line_of(span_ref, c, EDGE + owners * part_rows - 1, 2)
        tail += [shifted(line, g) for g in range(0, TAPS, 2 * SUBLANES)]
    tail = jnp.concatenate(tail, 0)
    tail_ref[...] = dot_nt(tail, tail, HIGHEST)


def own_call(parts, lags_local, after):
    part_rows = parts[0].shape[2]
    span_rows = part_rows * sum(part.shape[0] for part in parts)
    rows = span_rows * LANES // BLOCK_LEN * lags_local
    held_rows = -(-(span_rows + 2 * EDGE) // SUBLANES) * SUBLANES
    width = BATCH * BLOCK_LEN
    taps = pltpu.VMEM((4 * TAPS, width), jnp.bfloat16)
    lags = pltpu.VMEM((4 * lags_local + 4 * SUBLANES, width), jnp.bfloat16)
    span = pltpu.VMEM((2, held_rows, LANES), jnp.float32)
    return pl.pallas_call(
        functools.partial(own_kernel, lags_local),
        in_specs=[pl.BlockSpec(memory_space=pltpu.VMEM)] * len(parts) + [pl.BlockSpec(memory_space=pl.ANY)],
        out_shape=[
            jax.ShapeDtypeStruct((2, rows, 2 * TAPS), jnp.bfloat16),
            jax.ShapeDtypeStruct((SUBLANES, 2 * TAPS), jnp.float32),
            jax.ShapeDtypeStruct((2 * TAPS, 2 * TAPS), jnp.float32),
        ],
        scratch_shapes=[span, span, taps, lags, taps, lags],
        compiler_params=params(),
        cost_estimate=cost(6.2),
        name="reference_products",
    )(*parts, after)


def as_factor(a):
    return jnp.concatenate([a, -lane_sign(a.shape) * pltpu.roll(a, a.shape[0], 1)], 0)


def solver_kernel(line_ref, tail_ref, gram_ref, solver_ref):
    total = line_ref[...]
    line = total[0:1] + lane_sign((1, LANES)) * pltpu.roll(total[1:2], TAPS, 1)
    low = lax.broadcasted_iota(jnp.int32, (1, LANES), 1) < TAPS
    line_r = jnp.where(low, line, 0.0)
    line_i = jnp.where(low, pltpu.roll(line, TAPS, 1), 0.0)
    cols = lax.broadcasted_iota(jnp.int32, (TAPS, TAPS), 1)
    rows = lax.broadcasted_iota(jnp.int32, (TAPS, TAPS), 0)
    above = cols > rows

    def upper(x):
        spread = pltpu.roll(jnp.broadcast_to(x, (TAPS, LANES)), 0, 1, stride=1, stride_axis=0)
        return spread[:, :TAPS]

    up_r = upper(line_r)
    up_i = jnp.where(above, upper(line_i), 0.0)
    strict_r = jnp.where(above, up_r, 0.0)
    diag_r = jnp.where(cols == rows, up_r, 0.0)
    tails = tail_ref[...]
    gram_r = strict_r + strict_r.T + diag_r - (tails[:TAPS, :TAPS] + tails[TAPS:, TAPS:])
    gram_i = up_i - up_i.T - (tails[:TAPS, TAPS:] - tails[TAPS:, :TAPS])
    gram = jnp.concatenate([gram_r, gram_i], 1)
    gram_halves = halves(as_factor(gram))
    gram_ref[0], gram_ref[1] = gram_halves
    one = (
        lax.broadcasted_iota(jnp.int32, gram.shape, 0) == lax.broadcasted_iota(jnp.int32, gram.shape, 1)
    ).astype(jnp.float32)
    bound = jnp.max(jnp.sum(jnp.abs(gram), axis=1, keepdims=True), axis=0, keepdims=True)

    def again(state):
        count, left, _ = state
        return (count < 60) & (left > 1e-3)

    def newton(state):
        count, _, x = state
        x_halves = halves(x)
        seen = dot_split(x_halves, gram_halves)
        left = jnp.max(jnp.abs(seen - one))
        x = 2.0 * x - dot_split(halves(seen), halves(as_factor(x)))
        return count + 1, left, x

    start = (jnp.int32(0), jnp.float32(1.0), one * (1.0 / bound))
    _, _, inverse = lax.while_loop(again, newton, start)
    solver_ref[0], solver_ref[1] = halves(as_factor(inverse))


def solver_call(line, tail):
    out = jax.ShapeDtypeStruct((2,) + tail.shape, jnp.bfloat16)
    return pl.pallas_call(
        solver_kernel,
        out_shape=[out, out],
        compiler_params=params(),
        cost_estimate=cost(2.0),
        name="gram_inverse",
    )(line, tail)


def doppler_table(block_count, scale):
    phase = (np.arange(block_count)[:, None] * np.arange(DOPPLER)[None, :] % DOPPLER) * (2.0 * math.pi / DOPPLER)
    cosine, sine = np.cos(phase), np.sin(phase)
    upper = np.concatenate([cosine, -sine], 1)
    lower = np.concatenate([sine, cosine], 1)
    return (np.concatenate([upper, lower], 0) * scale).astype(np.float32)


def map_kernel(groups, got_ref, own_ref, gram_ref, solver_ref, wave_ref, out_hbm, held_ref, out_ref, out_sem):
    owners, pieces = got_ref.shape[:2]
    blocks = pieces - groups // 2
    lags_local = LANES // groups
    total = owners * blocks
    left = lax.broadcasted_iota(jnp.int32, (SUBLANES, LANES), 1) < TAPS
    sign = row_sign((SUBLANES, LANES))
    rows = [None] * groups
    for i in range(groups // 2):
        tile = got_ref[0, blocks + i]
        for owner in range(1, owners):
            tile = tile + got_ref[owner, blocks + i]
        swapped = pltpu.roll(tile, TAPS, 1)
        for part, here, there in ((i, tile, swapped), (i + groups // 2, swapped, tile)):
            other = -sign * pltpu.roll(there, SUBLANES // 2, 0)
            rows[part] = jnp.where(left, here, other)
    cross = jnp.concatenate(rows, 0)
    solver = (solver_ref[0], solver_ref[1])
    taps = dot_split(halves(cross), solver)
    rest = cross - dot_split(halves(taps), (gram_ref[0], gram_ref[1]))
    taps = taps + dot_split(halves(rest), solver)
    taps_high, taps_low = halves(taps)
    taps_both = jnp.concatenate([taps_high, taps_low], 0)
    count = taps.shape[0]
    for q in range(0, total, 2 * groups):
        own = slice(q * lags_local, (q + 2 * groups) * lags_local)
        by_high = dot_nt(taps_both, own_ref[0, own, :])
        clutter = by_high[:count] + (by_high[count:] + dot_nt(taps_high, own_ref[1, own, :]))
        for h in range(2):
            lanes = slice(h * LANES, (h + 1) * LANES)
            tiles = [clutter[r : r + SUBLANES, lanes] for r in range(0, groups * SUBLANES, SUBLANES)]
            for j, tile in enumerate(swap_groups(tiles, groups)):
                at = q + h * groups + j
                held_ref[at * SUBLANES : (at + 1) * SUBLANES, :] = got_ref[at // blocks, at % blocks] - tile
    half = SUBLANES // 2
    wave = (wave_ref[0], wave_ref[1])
    copies = []
    for g in range(half):
        parts = [held_ref[pl.ds(c * half + g, total, stride=SUBLANES), :] for c in range(2)]
        spectrum = dot_split(halves(jnp.concatenate(parts, 0).T), wave)
        for i in range(groups):
            for c in range(2):
                out_ref[i, g, c] = spectrum[i * lags_local : (i + 1) * lags_local, c * DOPPLER : (c + 1) * DOPPLER]
        part = (slice(None), pl.ds(g, 1))
        copies.append(pltpu.make_async_copy(out_ref.at[part], out_hbm.at[part], out_sem.at[g]))
        copies[-1].start()
    for copy in copies:
        copy.wait()


def map_call(got, own, gram, solver, wave, groups, beams_local):
    total = got.shape[0] * (got.shape[1] - groups // 2)
    lags_local = LANES // groups
    half = SUBLANES // 2
    shape = (beams_local // half, half, 2, lags_local, DOPPLER)
    out = pl.pallas_call(
        functools.partial(map_kernel, groups),
        in_specs=[pl.BlockSpec(memory_space=pltpu.VMEM)] * 5,
        out_specs=pl.BlockSpec(memory_space=pltpu.HBM),
        out_shape=jax.ShapeDtypeStruct(shape, jnp.float32),
        scratch_shapes=[
            pltpu.VMEM((total * SUBLANES, LANES), jnp.float32),
            pltpu.VMEM(shape, jnp.float32),
            pltpu.SemaphoreType.DMA((half,)),
        ],
        compiler_params=params(),
        cost_estimate=cost(2.5),
        name="range_doppler",
    )(got, own, gram, solver, wave)
    return out.reshape((beams_local,) + shape[2:])


def swap(x, axis, by):
    pairs = [(i, i ^ by) for i in range(lax.axis_size(axis))]
    return lax.ppermute(x, axis, pairs)


def tiled_device(ref_signal, surveillance, steering):
    chan_count, tm_count = lax.axis_size("chan"), lax.axis_size("tm")
    channels, length = surveillance.shape[1:]
    beams_local = steering.shape[1] // chan_count
    lags_local = LAGS // tm_count
    groups = LANES // lags_local
    samples = length * tm_count

    survey = surveillance.reshape(2 * channels, length)
    kept, moved, tiles = beam_call(steering, survey, ref_signal, chan_count, beams_local)
    near = swap(tiles[None], "tm", 1)
    shape = (chan_count // 2, 2 * beams_local, length)
    kept, got = kept.reshape(shape), swap(moved, "chan", 1).reshape(shape)
    by = 2
    while by < chan_count:
        kept, moved = sum_call([kept, got])
        got = swap(moved, "chan", by)
        by *= 2
    rounds = [near]
    joined = join_call(tiles[None], near, moved)
    while True:
        count = joined.shape[0]
        rounds.append(lax.ppermute(joined, "tm", [(i, (i + count) % tm_count) for i in range(tm_count)]))
        if count * 2 == tm_count:
            break
        joined = join_call(joined, rounds[-1])
    table = table_call(tiles)
    pieces = lag_call([kept[0], got[0]], table, tiles, rounds[:2], joined, groups, tm_count)
    got = lax.all_to_all(pieces, "tm", 0, 0, tiled=True)
    own, line, tail = own_call([tiles[None]] + rounds, lags_local, pieces)
    gram, solver = solver_call(line, tail)
    wave = doppler_table(samples // BLOCK_LEN, 0.125 / math.sqrt(samples))
    high = wave.astype(jnp.bfloat16)
    wave = np.stack([high, (wave - high.astype(np.float32)).astype(jnp.bfloat16)])
    return map_call(got, own, gram, solver, jnp.asarray(wave), groups, beams_local)


def lag_table(ref_ext, offset, lags):
    window = lax.dynamic_slice_in_dim(ref_ext, offset, BLOCK_LEN + LAGS, 1)
    span = BLOCK_LEN + LAGS
    tiled = jnp.tile(jnp.pad(window, ((0, 0), (0, 1))), (1, lags))[:, : lags * span]
    return tiled.reshape(2, lags, span)[:, :, LAGS:]


def times_conj(a, b):
    real = jnp.einsum("...t,lt->...l", a[..., 0, :], b[0], precision=HIGHEST) + jnp.einsum(
        "...t,lt->...l", a[..., 1, :], b[1], precision=HIGHEST
    )
    imag = jnp.einsum("...t,lt->...l", a[..., 1, :], b[0], precision=HIGHEST) - jnp.einsum(
        "...t,lt->...l", a[..., 0, :], b[1], precision=HIGHEST
    )
    return jnp.stack([real, imag], -2)


def plain_device(ref_signal, surveillance, steering):
    chan_count, tm_count = lax.axis_size("chan"), lax.axis_size("tm")
    length = surveillance.shape[2]
    beams = steering.shape[1]
    lags_local = LAGS // tm_count
    samples = length * tm_count
    local_blocks = length // BLOCK_LEN
    here = lax.axis_index("tm")

    w_real, w_imag = steering
    real = jnp.dot(w_real, surveillance[0], precision=HIGHEST) - jnp.dot(w_imag, surveillance[1], precision=HIGHEST)
    imag = jnp.dot(w_imag, surveillance[0], precision=HIGHEST) + jnp.dot(w_real, surveillance[1], precision=HIGHEST)
    beam = lax.psum_scatter(jnp.stack([real, imag], 1), "chan", scatter_dimension=0, tiled=True)
    ref_all = lax.all_gather(ref_signal, "tm", axis=1, tiled=True)
    ref_ext = jnp.pad(ref_all, ((0, 0), (LAGS, 0)))

    def beam_step(carry, q):
        offset = q * BLOCK_LEN
        table = lag_table(ref_ext, here * length + offset, LAGS)
        segment = lax.dynamic_slice_in_dim(beam, offset, BLOCK_LEN, 2)
        return carry, times_conj(segment, table)

    _, products = lax.scan(beam_step, None, jnp.arange(local_blocks, dtype=jnp.int32))
    cross = lax.psum(products[..., :TAPS].sum(0), "tm")
    got = lax.all_to_all(products, "tm", 3, 0, tiled=True)

    def own_step(gram, q):
        offset = q * BLOCK_LEN
        table = lag_table(ref_ext, offset, LAGS)
        taps = table[:, :TAPS].transpose(1, 0, 2)
        mine = lax.dynamic_slice_in_dim(table, here * lags_local, lags_local, 1)
        return gram + times_conj(taps, table[:, :TAPS]), times_conj(taps, mine)

    start = jnp.zeros((TAPS, 2, TAPS), jnp.float32)
    gram, own = lax.scan(own_step, start, jnp.arange(samples // BLOCK_LEN, dtype=jnp.int32))
    g_real, g_imag = gram[:, 0].T, gram[:, 1].T
    system = jnp.concatenate([jnp.concatenate([g_real, -g_imag], 1), jnp.concatenate([g_imag, g_real], 1)], 0)
    right = jnp.concatenate([cross[:, 0].T, cross[:, 1].T], 0)
    solved = jax.scipy.linalg.cho_solve((jnp.linalg.cholesky(system), True), right)
    b_real, b_imag = solved[:TAPS].T, solved[TAPS:].T
    mixing = jnp.concatenate([jnp.stack([b_real, b_imag], 1), jnp.stack([-b_imag, b_real], 1)], 2)
    stacked = jnp.concatenate([own[:, :, 0], own[:, :, 1]], 1)
    lagged = got - jnp.einsum("mck,qkl->qmcl", mixing, stacked, precision=HIGHEST)
    wave = jnp.asarray(doppler_table(samples // BLOCK_LEN, 0.125 / math.sqrt(samples)))
    wave = wave.reshape(2, samples // BLOCK_LEN, 2, DOPPLER)
    return jnp.einsum("qmcl,cqdk->mdlk", lagged, wave, precision=HIGHEST)


def on_device(ref_signal, surveillance, steering):
    chan_count, tm_count = lax.axis_size("chan"), lax.axis_size("tm")
    beams_local = steering.shape[1] // chan_count
    lags_local = LAGS // tm_count
    fills = (
        LANES % lags_local == 0
        and lags_local % (2 * SUBLANES) == 0
        and beams_local * lags_local == LANES * SUBLANES // 2
        and chan_count > 1
        and chan_count & (chan_count - 1) == 0
        and tm_count > 2
        and tm_count & (tm_count - 1) == 0
        and 2 * surveillance.shape[1] % LANES == 0
        and surveillance.shape[2] % (2 * BATCH * BLOCK_LEN) == 0
    )
    device = tiled_device if fills else plain_device
    return device(ref_signal, surveillance, steering)


def solution(mesh):
    placed = (P(None, "tm"), P(None, "chan", "tm"), P(None, None, "chan"))
    return jax.shard_map(
        on_device,
        mesh=mesh,
        in_specs=placed,
        out_specs=P("chan", None, "tm", None),
        check_vma=False,
    )
```

```python
import functools
import math

import jax
import jax.numpy as jnp
import numpy as np
from jax import lax
from jax.experimental import pallas as pl
from jax.experimental.pallas import tpu as pltpu
from jax.sharding import PartitionSpec as P

LAGS = 256
DOPPLER = 256
TAPS = 64
BLOCK_LEN = 256
LANES = 128
SUBLANES = 8
EDGE = 2

HIGHEST = lax.Precision.HIGHEST
VMEM_BYTES = 48 * 1024 * 1024


def params():
    return pltpu.CompilerParams(vmem_limit_bytes=VMEM_BYTES)


def cost(us):
    return pl.CostEstimate(flops=int(us * 1.15e9), bytes_accessed=0, transcendentals=0)


def halves(x):
    high = x.astype(jnp.bfloat16)
    return high, (x - high.astype(jnp.float32)).astype(jnp.bfloat16)


def dot_nt(a, b, precision=None):
    return lax.dot_general(
        a, b, (((1,), (1,)), ((), ())), precision=precision, preferred_element_type=jnp.float32
    )


def dot_split(a, b):
    (a_high, a_low), (b_high, b_low) = a, b
    left = jnp.concatenate([a_high, a_low], 1)
    right = jnp.concatenate([b_high, b_high], 0)
    return jnp.dot(left, right, preferred_element_type=jnp.float32) + jnp.dot(
        a_high, b_low, preferred_element_type=jnp.float32
    )


def row_sign(shape):
    rows = lax.broadcasted_iota(jnp.int32, shape, 0)
    return jnp.where(rows % SUBLANES < SUBLANES // 2, 1.0, -1.0).astype(jnp.float32)


def lane_sign(shape):
    lanes = lax.broadcasted_iota(jnp.int32, shape, 1)
    return jnp.where(lanes % LANES < LANES // 2, 1.0, -1.0).astype(jnp.float32)


def swap_groups(rows, groups):
    width = LANES // groups
    lane_group = lax.broadcasted_iota(jnp.int32, rows[0].shape, 1) // width
    outs = []
    for j in range(groups):
        out = rows[j]
        for i in range(groups):
            if i != j:
                moved = pltpu.roll(rows[i], (width * (i - j)) % LANES, 1)
                out = jnp.where(lane_group == i, moved, out)
        outs.append(out)
    return outs


COPIES = 4


def beam_kernel(
    chan_count, beams_local, w_hbm, s_hbm, ref_hbm, kept_ref, sent_ref, tiles_ref,
    w_ref, s_ref, ref_ref, w_sem, s_sem, ref_sem,
):
    me = lax.axis_index("chan")
    depth = s_hbm.shape[0] // COPIES
    w_copy = pltpu.make_async_copy(w_hbm, w_ref, w_sem)
    w_copy.start()
    ref_copy = pltpu.make_async_copy(ref_hbm, ref_ref, ref_sem)
    ref_copy.start()
    s_copies = []
    for n in range(COPIES):
        part = pl.ds(n * depth, depth)
        s_copies.append(pltpu.make_async_copy(s_hbm.at[part], s_ref.at[part], s_sem.at[n]))
        s_copies[n].start()
    half = SUBLANES // 2
    sub = lax.broadcasted_iota(jnp.int32, (SUBLANES, w_hbm.shape[2]), 0)
    top = sub < half
    w_copy.wait()
    rows = []
    for parity in range(2):
        for e in range(parity, chan_count, 2):
            base = (me ^ e) * beams_local
            for tile in range(beams_local // SUBLANES):
                start = pl.multiple_of(base + tile * SUBLANES, SUBLANES)
                wr = w_ref[0, pl.ds(start, SUBLANES), :]
                wi = w_ref[1, pl.ds(start, SUBLANES), :]
                wr_s = pltpu.roll(wr, half, 0)
                wi_s = pltpu.roll(wi, half, 0)
                first = [jnp.where(top, wr, wi_s), jnp.where(top, -wi, wr_s)]
                second = [jnp.where(top, wr_s, wi), jnp.where(top, -wi_s, wr)]
                rows.append(jnp.concatenate(first, 1))
                rows.append(jnp.concatenate(second, 1))
    weights = jnp.concatenate(halves(jnp.concatenate(rows, 0)), 0)
    count = weights.shape[0] // 2
    ref_copy.wait()
    for c in range(2):
        for n in range(tiles_ref.shape[1]):
            tiles_ref[c, n : n + 1, :] = ref_ref[c : c + 1, n * LANES : (n + 1) * LANES]
    mid = count // 2
    for copy in s_copies:
        copy.wait()
    high, low = halves(s_ref[...])
    by_high = jnp.dot(weights, high, preferred_element_type=jnp.float32)
    by_low = jnp.dot(weights[:count], low, preferred_element_type=jnp.float32)
    product = by_high[:count] + (by_high[count:] + by_low)
    kept_ref[...] = product[:mid]
    sent_ref[...] = product[mid:]


def beam_call(steering, survey, ref, chan_count, beams_local):
    depth, length = survey.shape
    rows = chan_count * beams_local
    tiles = (2, length // LANES, LANES)
    out = jax.ShapeDtypeStruct((rows, length), jnp.float32)
    hbm, vmem = pl.BlockSpec(memory_space=pltpu.HBM), pl.BlockSpec(memory_space=pltpu.VMEM)
    return pl.pallas_call(
        functools.partial(beam_kernel, chan_count, beams_local),
        in_specs=[hbm] * 3,
        out_specs=[vmem] * 3,
        out_shape=[
            out,
            out,
            jax.ShapeDtypeStruct(tiles, jnp.float32),
        ],
        scratch_shapes=[
            pltpu.VMEM(steering.shape, jnp.float32),
            pltpu.VMEM(survey.shape, jnp.float32),
            pltpu.VMEM(ref.shape, jnp.float32),
            pltpu.SemaphoreType.DMA,
            pltpu.SemaphoreType.DMA((COPIES,)),
            pltpu.SemaphoreType.DMA,
        ],
        compiler_params=params(),
        cost_estimate=cost(2.2),
        name="beams",
    )(*(pltpu.with_memory_space_constraint(x, pltpu.HBM) for x in (steering, survey, ref)))


def sum_kernel(count, *refs):
    kept_ref, sent_ref = refs[-2:]
    for n in range(kept_ref.shape[0]):
        for offset, out_ref in ((0, kept_ref), (1, sent_ref)):
            total = refs[0][2 * n + offset]
            for ref in refs[1:count]:
                total = total + ref[2 * n + offset]
            out_ref[n] = total


def sum_call(parts):
    shape = (parts[0].shape[0] // 2,) + parts[0].shape[1:]
    out = jax.ShapeDtypeStruct(shape, jnp.float32)
    vmem = pl.BlockSpec(memory_space=pltpu.VMEM)
    return pl.pallas_call(
        functools.partial(sum_kernel, len(parts)),
        in_specs=[vmem] * len(parts),
        out_specs=[vmem, vmem],
        out_shape=[out, out],
        compiler_params=params(),
        cost_estimate=cost(0.1),
        name="halves_summed",
    )(*parts)


def join_kernel(first_ref, second_ref, *refs):
    out_ref = refs[-1]
    count = first_ref.shape[0]
    out_ref[:count] = first_ref[...]
    out_ref[count:] = second_ref[...]


def join_call(first, second, *after):
    vmem = pl.BlockSpec(memory_space=pltpu.VMEM)
    return pl.pallas_call(
        join_kernel,
        in_specs=[vmem, vmem] + [pl.BlockSpec(memory_space=pl.ANY)] * len(after),
        out_shape=jax.ShapeDtypeStruct((2 * first.shape[0],) + first.shape[1:], jnp.float32),
        compiler_params=params(),
        cost_estimate=cost(1.0),
        name="reference_joined",
    )(first, second, *after)


def spread_line(line, keep):
    for g in range(0, LANES, 2 * SUBLANES):
        tiled = jnp.broadcast_to(line, (2 * SUBLANES, line.shape[1]))
        for h, value in enumerate(halves(pltpu.roll(tiled, g, 1, stride=1, stride_axis=0)[:, LANES:])):
            keep(h, g, value)


def table_kernel(tiles_ref, out_ref):
    for c in range(2):
        line = jnp.concatenate([tiles_ref[c, n : n + 1, :] for n in range(tiles_ref.shape[1])], 1)

        def keep(h, g, value):
            out_ref[h, c, g : g + 2 * SUBLANES] = value

        spread_line(line, keep)


def table_call(tiles):
    shape = (2, 2, LANES, LANES * (tiles.shape[1] - 1))
    return pl.pallas_call(
        table_kernel,
        out_shape=jax.ShapeDtypeStruct(shape, jnp.bfloat16),
        compiler_params=params(),
        cost_estimate=cost(0.7),
        name="shifted_reference",
    )(tiles)


def first_kernel(tiles_ref, *refs):
    *round_refs, out_ref = refs
    me = lax.axis_index("tm")
    for c in range(2):
        tails = [ref[ref.shape[0] - 1, c, ref.shape[2] - EDGE :, :] for ref in round_refs]
        before = jnp.where(me % 2 == 1, tails[0], jnp.where(me > 0, tails[-1], 0.0))
        line = jnp.concatenate([before[n : n + 1] for n in range(EDGE)] + [tiles_ref[c, 0:1, :]], 1)

        def keep(h, g, value):
            out_ref[h, c, g : g + 2 * SUBLANES] = value

        spread_line(line, keep)


def first_call(tiles, rounds):
    return pl.pallas_call(
        first_kernel,
        out_shape=jax.ShapeDtypeStruct((2, 2, LANES, 2 * LANES), jnp.bfloat16),
        compiler_params=params(),
        cost_estimate=cost(0.1),
        name="shifted_first",
    )(tiles, *rounds)


def lag_kernel(groups, part_count, *refs):
    y_refs, refs = refs[:part_count], refs[part_count:]
    table_ref, first_ref, _, out_hbm, out_ref, out_sem = refs
    copies = []

    def table_tile(h, n):
        parts = []
        for c in range(2):
            known = first_ref.shape[3] // LANES
            ref, at = (first_ref, n) if n < known else (table_ref, n - known)
            parts.append(ref[h, c, :, at * LANES : (at + 1) * LANES])
        return jnp.concatenate(parts, 1)

    def send(start, count):
        part = (slice(None), pl.ds(start, count))
        copies.append(pltpu.make_async_copy(out_ref.at[part], out_hbm.at[part], out_sem.at[len(copies)]))
        copies[-1].start()

    y = y_refs[0][...]
    for y_ref in y_refs[1:]:
        y = y + y_ref[...]
    rows, length = y.shape
    blocks = length // BLOCK_LEN
    turned = jnp.concatenate(
        [pltpu.roll(y[r : r + SUBLANES], SUBLANES // 2, 0) for r in range(0, rows, SUBLANES)], 0
    )
    turned = turned * row_sign(turned.shape)
    y_high, y_low = halves(y)
    t_high, t_low = halves(turned)

    def half_block(q, b):
        cols = slice(q * BLOCK_LEN + b * LANES, q * BLOCK_LEN + (b + 1) * LANES)
        return [jnp.concatenate([x[:, cols], t[:, cols]], 1) for x, t in ((y_high, t_high), (y_low, t_low))]

    def products(stack, n, count):
        high, low = (jnp.concatenate([table_tile(h, n + i) for i in range(count)], 0) for h in range(2))
        by_high = dot_nt(jnp.concatenate([part for pair in stack for part in pair], 0), high)
        by_low = dot_nt(jnp.concatenate([pair[0] for pair in stack], 0), low)
        return [
            by_high[2 * i * rows : (2 * i + 1) * rows]
            + (by_high[(2 * i + 1) * rows : 2 * (i + 1) * rows] + by_low[i * rows : (i + 1) * rows])
            for i in range(len(stack))
        ]

    taps_sum = None
    (far,) = products([half_block(0, 0)], 0, 1)
    for q in range(blocks):
        stack = [half_block(q, 0), half_block(q, 1)]
        if q + 1 < blocks:
            stack.append(half_block(q + 1, 0))
        first, second, *after = products(stack, 2 * q + 1, 2)
        product = jnp.concatenate([first[:, :LANES] + second[:, LANES:], second[:, :LANES] + far], 1)
        if after:
            far = after[0][:, LANES:]
        taps = product[:, :LANES]
        taps_sum = taps if taps_sum is None else taps_sum + taps
        for h in range(LAGS // LANES):
            lanes = slice(h * LANES, (h + 1) * LANES)
            tiles = [product[r : r + SUBLANES, lanes] for r in range(0, rows, SUBLANES)]
            for j, tile in enumerate(swap_groups(tiles, groups)):
                out_ref[h * groups + j, q] = tile
        if q + 1 == blocks // 2:
            send(0, blocks // 2)
    left = lax.broadcasted_iota(jnp.int32, (SUBLANES, LANES), 1) < TAPS
    for i in range(groups // 2):
        a = taps_sum[i * SUBLANES : (i + 1) * SUBLANES]
        other = i + groups // 2
        b = taps_sum[other * SUBLANES : (other + 1) * SUBLANES]
        tile = jnp.where(left, a, pltpu.roll(b, LANES - TAPS, 1))
        for owner in range(out_ref.shape[0]):
            out_ref[owner, blocks + i] = tile
    send(blocks // 2, blocks - blocks // 2 + groups // 2)
    for copy in copies:
        copy.wait()


def lag_call(ys, table, first, after, groups, owners):
    blocks = ys[0].shape[1] // BLOCK_LEN
    shape = (owners, blocks + groups // 2, SUBLANES, LANES)
    vmem = pl.BlockSpec(memory_space=pltpu.VMEM)
    return pl.pallas_call(
        functools.partial(lag_kernel, groups, len(ys)),
        in_specs=[vmem] * (len(ys) + 2) + [pl.BlockSpec(memory_space=pl.ANY)],
        out_specs=pl.BlockSpec(memory_space=pltpu.HBM),
        out_shape=jax.ShapeDtypeStruct(shape, jnp.float32),
        scratch_shapes=[
            pltpu.VMEM(shape, jnp.float32),
            pltpu.SemaphoreType.DMA((2,)),
        ],
        compiler_params=params(),
        cost_estimate=cost(2.1),
        name="lag_products",
    )(*ys, table, first, after)


BATCH = 4


def own_kernel(lags_local, *refs):
    *part_refs, _, out_ref, line_ref, tail_ref, span_ref, late_ref, taps_a, lags_a, taps_b, lags_b = refs
    me = lax.axis_index("tm")
    part_rows = part_refs[0].shape[2]
    owners = sum(part_ref.shape[0] for part_ref in part_refs)
    samples = owners * part_rows * LANES
    steps = samples // BLOCK_LEN // BATCH
    total_rows = span_ref.shape[1]
    block_rows = BLOCK_LEN // LANES

    span_ref[...] = jnp.zeros_like(span_ref)
    n = 0
    for part_ref in part_refs:
        for i in range(part_ref.shape[0]):
            block = lax.rem(me - (n // 2) * 2 + owners, owners) ^ (n % 2)
            span_ref[:, pl.ds(EDGE + block * part_rows, part_rows), :] = part_ref[i]
            n += 1
    late_rows = (me * lags_local) // LANES
    late_lanes = lax.rem(me * lags_local, LANES)
    turned = [pltpu.roll(span_ref[c], late_lanes, 1) for c in range(2)]
    before = [pltpu.roll(x, 1, 0) for x in turned]
    lanes = lax.broadcasted_iota(jnp.int32, (total_rows, LANES), 1)
    for c in range(2):
        late_ref[c] = pltpu.roll(jnp.where(lanes < late_lanes, before[c], turned[c]), late_rows, 0)

    def line_of(ref, c, first, count):
        return jnp.concatenate([ref[c, pl.ds(first + n, 1), :] for n in range(count)], 1)

    def shifted(line, by):
        tiled = jnp.broadcast_to(line, (2 * SUBLANES, line.shape[1]))
        return pltpu.roll(tiled, by, 1, stride=1, stride_axis=0)[:, LANES:]

    def keep(ref, row, value):
        high, low = halves(value)
        half = ref.shape[0] // 2
        ref[row : row + 2 * SUBLANES, :] = high
        ref[half + row : half + row + 2 * SUBLANES, :] = low

    def build(n, taps_ref, lags_ref):
        first = EDGE - 1 + n * BATCH * block_rows
        count = BATCH * block_rows + 1
        lines = [line_of(span_ref, c, first, count) for c in range(2)]
        for c in range(2):
            for g in range(0, TAPS, 2 * SUBLANES):
                keep(taps_ref, c * TAPS + g, shifted(lines[c], g))
            late = line_of(late_ref, c, first, count)
            for g in range(0, lags_local, 2 * SUBLANES):
                keep(lags_ref, c * lags_local + g, shifted(late, g))
        pad = jnp.zeros((2 * SUBLANES - 2, BATCH * BLOCK_LEN), jnp.float32)
        keep(lags_ref, 2 * lags_local, jnp.concatenate([line[:, LANES:] for line in lines] + [pad], 0))

    turn = lane_sign((lags_local, LANES))

    def use(n, taps_ref, lags_ref):
        count = lags_ref.shape[0] // 2
        for b in range(BATCH):
            cols = slice(b * BLOCK_LEN, (b + 1) * BLOCK_LEN)
            product = dot_nt(lags_ref[:, cols], taps_ref[:, cols])
            product = product[:count, :LANES] + (product[:count, LANES:] + product[count:, :LANES])
            by_real = product[:lags_local]
            by_imag = product[lags_local : 2 * lags_local]
            rows = pl.ds(pl.multiple_of((n * BATCH + b) * lags_local, lags_local), lags_local)
            high, low = halves(by_real + turn * pltpu.roll(by_imag, TAPS, 1))
            out_ref[0, rows, :] = high
            out_ref[1, rows, :] = low
            line_ref[...] += product[2 * lags_local : 2 * lags_local + SUBLANES]

    line_ref[...] = jnp.zeros_like(line_ref)
    build(0, taps_a, lags_a)

    def pair(m, carry):
        build(2 * m + 1, taps_b, lags_b)
        use(2 * m, taps_a, lags_a)
        build(jnp.minimum(2 * m + 2, steps - 1), taps_a, lags_a)
        use(2 * m + 1, taps_b, lags_b)
        return carry

    lax.fori_loop(0, steps // 2, pair, 0)
    tail = []
    for c in range(2):
        line = line_of(span_ref, c, EDGE + owners * part_rows - 1, 2)
        tail += [shifted(line, g) for g in range(0, TAPS, 2 * SUBLANES)]
    tail = jnp.concatenate(tail, 0)
    tail_ref[...] = dot_nt(tail, tail, HIGHEST)


def own_call(parts, lags_local, after):
    part_rows = parts[0].shape[2]
    span_rows = part_rows * sum(part.shape[0] for part in parts)
    rows = span_rows * LANES // BLOCK_LEN * lags_local
    held_rows = -(-(span_rows + 2 * EDGE) // SUBLANES) * SUBLANES
    width = BATCH * BLOCK_LEN
    taps = pltpu.VMEM((4 * TAPS, width), jnp.bfloat16)
    lags = pltpu.VMEM((4 * lags_local + 4 * SUBLANES, width), jnp.bfloat16)
    span = pltpu.VMEM((2, held_rows, LANES), jnp.float32)
    return pl.pallas_call(
        functools.partial(own_kernel, lags_local),
        in_specs=[pl.BlockSpec(memory_space=pltpu.VMEM)] * len(parts) + [pl.BlockSpec(memory_space=pl.ANY)],
        out_shape=[
            jax.ShapeDtypeStruct((2, rows, 2 * TAPS), jnp.bfloat16),
            jax.ShapeDtypeStruct((SUBLANES, 2 * TAPS), jnp.float32),
            jax.ShapeDtypeStruct((2 * TAPS, 2 * TAPS), jnp.float32),
        ],
        scratch_shapes=[span, span, taps, lags, taps, lags],
        compiler_params=params(),
        cost_estimate=cost(6.2),
        name="reference_products",
    )(*parts, after)


def as_factor(a):
    return jnp.concatenate([a, -lane_sign(a.shape) * pltpu.roll(a, a.shape[0], 1)], 0)


def solver_kernel(line_ref, tail_ref, solver_ref):
    total = line_ref[...]
    line = total[0:1] + lane_sign((1, LANES)) * pltpu.roll(total[1:2], TAPS, 1)
    low = lax.broadcasted_iota(jnp.int32, (1, LANES), 1) < TAPS
    line_r = jnp.where(low, line, 0.0)
    line_i = jnp.where(low, pltpu.roll(line, TAPS, 1), 0.0)
    cols = lax.broadcasted_iota(jnp.int32, (TAPS, TAPS), 1)
    rows = lax.broadcasted_iota(jnp.int32, (TAPS, TAPS), 0)
    above = cols > rows

    def upper(x):
        spread = pltpu.roll(jnp.broadcast_to(x, (TAPS, LANES)), 0, 1, stride=1, stride_axis=0)
        return spread[:, :TAPS]

    up_r = upper(line_r)
    up_i = jnp.where(above, upper(line_i), 0.0)
    strict_r = jnp.where(above, up_r, 0.0)
    diag_r = jnp.where(cols == rows, up_r, 0.0)
    tails = tail_ref[...]
    gram_r = strict_r + strict_r.T + diag_r - (tails[:TAPS, :TAPS] + tails[TAPS:, TAPS:])
    gram_i = up_i - up_i.T - (tails[:TAPS, TAPS:] - tails[TAPS:, :TAPS])
    gram = jnp.concatenate([gram_r, gram_i], 1)
    gram_factor = as_factor(gram)
    gram_halves = halves(gram_factor)
    one = (
        lax.broadcasted_iota(jnp.int32, gram.shape, 0) == lax.broadcasted_iota(jnp.int32, gram.shape, 1)
    ).astype(jnp.float32)
    bound = jnp.max(jnp.sum(jnp.abs(gram), axis=1, keepdims=True), axis=0, keepdims=True)

    def again(state):
        count, left, _ = state
        return (count < 60) & (left > 1e-3)

    def newton(state):
        count, _, x = state
        x_halves = halves(x)
        seen = dot_split(x_halves, gram_halves)
        left = jnp.max(jnp.abs(seen - one))
        x = 2.0 * x - dot_split(halves(seen), halves(as_factor(x)))
        return count + 1, left, x

    start = (jnp.int32(0), jnp.float32(1.0), one * (1.0 / bound))
    _, _, inverse = lax.while_loop(again, newton, start)
    seen = jnp.dot(inverse, gram_factor, precision=HIGHEST, preferred_element_type=jnp.float32)
    inverse = inverse + jnp.dot(
        one - seen, as_factor(inverse), precision=HIGHEST, preferred_element_type=jnp.float32
    )
    solver_ref[...] = as_factor(inverse)


def solver_call(line, tail):
    return pl.pallas_call(
        solver_kernel,
        out_shape=jax.ShapeDtypeStruct(tail.shape, jnp.float32),
        compiler_params=params(),
        cost_estimate=cost(2.0),
        name="gram_inverse",
    )(line, tail)


def doppler_table(block_count, scale):
    phase = (np.arange(block_count)[:, None] * np.arange(DOPPLER)[None, :] % DOPPLER) * (2.0 * math.pi / DOPPLER)
    cosine, sine = np.cos(phase), np.sin(phase)
    upper = np.concatenate([cosine, -sine], 1)
    lower = np.concatenate([sine, cosine], 1)
    return (np.concatenate([upper, lower], 0) * scale).astype(np.float32)


def map_kernel(groups, got_ref, own_ref, solver_ref, wave_ref, out_hbm, held_ref, out_ref, out_sem):
    owners, pieces = got_ref.shape[:2]
    blocks = pieces - groups // 2
    lags_local = LANES // groups
    total = owners * blocks
    left = lax.broadcasted_iota(jnp.int32, (SUBLANES, LANES), 1) < TAPS
    sign = row_sign((SUBLANES, LANES))
    rows = [None] * groups
    for i in range(groups // 2):
        tile = got_ref[0, blocks + i]
        for owner in range(1, owners):
            tile = tile + got_ref[owner, blocks + i]
        swapped = pltpu.roll(tile, TAPS, 1)
        for part, here, there in ((i, tile, swapped), (i + groups // 2, swapped, tile)):
            other = -sign * pltpu.roll(there, SUBLANES // 2, 0)
            rows[part] = jnp.where(left, here, other)
    cross = jnp.concatenate(rows, 0)
    taps = jnp.dot(cross, solver_ref[...], precision=HIGHEST, preferred_element_type=jnp.float32)
    taps_high, taps_low = halves(taps)
    taps_both = jnp.concatenate([taps_high, taps_low], 0)
    count = taps.shape[0]
    for q in range(0, total, 2 * groups):
        own = slice(q * lags_local, (q + 2 * groups) * lags_local)
        by_high = dot_nt(taps_both, own_ref[0, own, :])
        clutter = by_high[:count] + (by_high[count:] + dot_nt(taps_high, own_ref[1, own, :]))
        for h in range(2):
            lanes = slice(h * LANES, (h + 1) * LANES)
            tiles = [clutter[r : r + SUBLANES, lanes] for r in range(0, groups * SUBLANES, SUBLANES)]
            for j, tile in enumerate(swap_groups(tiles, groups)):
                at = q + h * groups + j
                held_ref[at * SUBLANES : (at + 1) * SUBLANES, :] = got_ref[at // blocks, at % blocks] - tile
    half = SUBLANES // 2
    wave = (wave_ref[0], wave_ref[1])
    copies = []
    for g in range(half):
        parts = [held_ref[pl.ds(c * half + g, total, stride=SUBLANES), :] for c in range(2)]
        spectrum = dot_split(halves(jnp.concatenate(parts, 0).T), wave)
        for i in range(groups):
            for c in range(2):
                out_ref[i, g, c] = spectrum[i * lags_local : (i + 1) * lags_local, c * DOPPLER : (c + 1) * DOPPLER]
        part = (slice(None), pl.ds(g, 1))
        copies.append(pltpu.make_async_copy(out_ref.at[part], out_hbm.at[part], out_sem.at[g]))
        copies[-1].start()
    for copy in copies:
        copy.wait()


def map_call(got, own, solver, wave, groups, beams_local):
    total = got.shape[0] * (got.shape[1] - groups // 2)
    lags_local = LANES // groups
    half = SUBLANES // 2
    shape = (beams_local // half, half, 2, lags_local, DOPPLER)
    out = pl.pallas_call(
        functools.partial(map_kernel, groups),
        in_specs=[pl.BlockSpec(memory_space=pltpu.VMEM)] * 4,
        out_specs=pl.BlockSpec(memory_space=pltpu.HBM),
        out_shape=jax.ShapeDtypeStruct(shape, jnp.float32),
        scratch_shapes=[
            pltpu.VMEM((total * SUBLANES, LANES), jnp.float32),
            pltpu.VMEM(shape, jnp.float32),
            pltpu.SemaphoreType.DMA((half,)),
        ],
        compiler_params=params(),
        cost_estimate=cost(2.5),
        name="range_doppler",
    )(got, own, solver, wave)
    return out.reshape((beams_local,) + shape[2:])


def swap(x, axis, by):
    pairs = [(i, i ^ by) for i in range(lax.axis_size(axis))]
    return lax.ppermute(x, axis, pairs)


def tiled_device(ref_signal, surveillance, steering):
    chan_count, tm_count = lax.axis_size("chan"), lax.axis_size("tm")
    channels, length = surveillance.shape[1:]
    beams_local = steering.shape[1] // chan_count
    lags_local = LAGS // tm_count
    groups = LANES // lags_local
    samples = length * tm_count

    survey = surveillance.reshape(2 * channels, length)
    kept, moved, tiles = beam_call(steering, survey, ref_signal, chan_count, beams_local)
    near = swap(tiles[None], "tm", 1)
    shape = (chan_count // 2, 2 * beams_local, length)
    kept, got = kept.reshape(shape), swap(moved, "chan", 1).reshape(shape)
    by = 2
    while by < chan_count:
        kept, moved = sum_call([kept, got])
        got = swap(moved, "chan", by)
        by *= 2
    rounds = [near]
    joined = join_call(tiles[None], near, moved)
    while True:
        count = joined.shape[0]
        rounds.append(lax.ppermute(joined, "tm", [(i, (i + count) % tm_count) for i in range(tm_count)]))
        if count * 2 == tm_count:
            break
        joined = join_call(joined, rounds[-1])
    table = table_call(tiles)
    first = first_call(tiles, rounds[:2])
    pieces = lag_call([kept[0], got[0]], table, first, joined, groups, tm_count)
    got = lax.all_to_all(pieces, "tm", 0, 0, tiled=True)
    own, line, tail = own_call([tiles[None]] + rounds, lags_local, pieces)
    solver = solver_call(line, tail)
    wave = doppler_table(samples // BLOCK_LEN, 0.125 / math.sqrt(samples))
    high = wave.astype(jnp.bfloat16)
    wave = np.stack([high, (wave - high.astype(np.float32)).astype(jnp.bfloat16)])
    return map_call(got, own, solver, jnp.asarray(wave), groups, beams_local)


def lag_table(ref_ext, offset, lags):
    window = lax.dynamic_slice_in_dim(ref_ext, offset, BLOCK_LEN + LAGS, 1)
    span = BLOCK_LEN + LAGS
    tiled = jnp.tile(jnp.pad(window, ((0, 0), (0, 1))), (1, lags))[:, : lags * span]
    return tiled.reshape(2, lags, span)[:, :, LAGS:]


def times_conj(a, b):
    real = jnp.einsum("...t,lt->...l", a[..., 0, :], b[0], precision=HIGHEST) + jnp.einsum(
        "...t,lt->...l", a[..., 1, :], b[1], precision=HIGHEST
    )
    imag = jnp.einsum("...t,lt->...l", a[..., 1, :], b[0], precision=HIGHEST) - jnp.einsum(
        "...t,lt->...l", a[..., 0, :], b[1], precision=HIGHEST
    )
    return jnp.stack([real, imag], -2)


def plain_device(ref_signal, surveillance, steering):
    chan_count, tm_count = lax.axis_size("chan"), lax.axis_size("tm")
    length = surveillance.shape[2]
    beams = steering.shape[1]
    lags_local = LAGS // tm_count
    samples = length * tm_count
    local_blocks = length // BLOCK_LEN
    here = lax.axis_index("tm")

    w_real, w_imag = steering
    real = jnp.dot(w_real, surveillance[0], precision=HIGHEST) - jnp.dot(w_imag, surveillance[1], precision=HIGHEST)
    imag = jnp.dot(w_imag, surveillance[0], precision=HIGHEST) + jnp.dot(w_real, surveillance[1], precision=HIGHEST)
    beam = lax.psum_scatter(jnp.stack([real, imag], 1), "chan", scatter_dimension=0, tiled=True)
    ref_all = lax.all_gather(ref_signal, "tm", axis=1, tiled=True)
    ref_ext = jnp.pad(ref_all, ((0, 0), (LAGS, 0)))

    def beam_step(carry, q):
        offset = q * BLOCK_LEN
        table = lag_table(ref_ext, here * length + offset, LAGS)
        segment = lax.dynamic_slice_in_dim(beam, offset, BLOCK_LEN, 2)
        return carry, times_conj(segment, table)

    _, products = lax.scan(beam_step, None, jnp.arange(local_blocks, dtype=jnp.int32))
    cross = lax.psum(products[..., :TAPS].sum(0), "tm")
    got = lax.all_to_all(products, "tm", 3, 0, tiled=True)

    def own_step(gram, q):
        offset = q * BLOCK_LEN
        table = lag_table(ref_ext, offset, LAGS)
        taps = table[:, :TAPS].transpose(1, 0, 2)
        mine = lax.dynamic_slice_in_dim(table, here * lags_local, lags_local, 1)
        return gram + times_conj(taps, table[:, :TAPS]), times_conj(taps, mine)

    start = jnp.zeros((TAPS, 2, TAPS), jnp.float32)
    gram, own = lax.scan(own_step, start, jnp.arange(samples // BLOCK_LEN, dtype=jnp.int32))
    g_real, g_imag = gram[:, 0].T, gram[:, 1].T
    system = jnp.concatenate([jnp.concatenate([g_real, -g_imag], 1), jnp.concatenate([g_imag, g_real], 1)], 0)
    right = jnp.concatenate([cross[:, 0].T, cross[:, 1].T], 0)
    solved = jax.scipy.linalg.cho_solve((jnp.linalg.cholesky(system), True), right)
    b_real, b_imag = solved[:TAPS].T, solved[TAPS:].T
    mixing = jnp.concatenate([jnp.stack([b_real, b_imag], 1), jnp.stack([-b_imag, b_real], 1)], 2)
    stacked = jnp.concatenate([own[:, :, 0], own[:, :, 1]], 1)
    lagged = got - jnp.einsum("mck,qkl->qmcl", mixing, stacked, precision=HIGHEST)
    wave = jnp.asarray(doppler_table(samples // BLOCK_LEN, 0.125 / math.sqrt(samples)))
    wave = wave.reshape(2, samples // BLOCK_LEN, 2, DOPPLER)
    return jnp.einsum("qmcl,cqdk->mdlk", lagged, wave, precision=HIGHEST)


def on_device(ref_signal, surveillance, steering):
    chan_count, tm_count = lax.axis_size("chan"), lax.axis_size("tm")
    beams_local = steering.shape[1] // chan_count
    lags_local = LAGS // tm_count
    fills = (
        LANES % lags_local == 0
        and lags_local % (2 * SUBLANES) == 0
        and beams_local * lags_local == LANES * SUBLANES // 2
        and chan_count > 1
        and chan_count & (chan_count - 1) == 0
        and tm_count > 2
        and tm_count & (tm_count - 1) == 0
        and 2 * surveillance.shape[1] % LANES == 0
        and surveillance.shape[2] % (2 * BATCH * BLOCK_LEN) == 0
    )
    device = tiled_device if fills else plain_device
    return device(ref_signal, surveillance, steering)


def solution(mesh):
    placed = (P(None, "tm"), P(None, "chan", "tm"), P(None, None, "chan"))
    return jax.shard_map(
        on_device,
        mesh=mesh,
        in_specs=placed,
        out_specs=P("chan", None, "tm", None),
        check_vma=False,
    )
```

```python
import functools
import math

import jax
import jax.numpy as jnp
import numpy as np
from jax import lax
from jax.experimental import pallas as pl
from jax.experimental.pallas import tpu as pltpu
from jax.sharding import PartitionSpec as P

LAGS = 256
DOPPLER = 256
TAPS = 64
BLOCK_LEN = 256
LANES = 128
SUBLANES = 8
EDGE = 2

HIGHEST = lax.Precision.HIGHEST
VMEM_BYTES = 48 * 1024 * 1024


def params():
    return pltpu.CompilerParams(vmem_limit_bytes=VMEM_BYTES)


def cost(us):
    return pl.CostEstimate(flops=int(us * 1.15e9), bytes_accessed=0, transcendentals=0)


def halves(x):
    high = x.astype(jnp.bfloat16)
    return high, (x - high.astype(jnp.float32)).astype(jnp.bfloat16)


def dot_nt(a, b, precision=None):
    return lax.dot_general(
        a, b, (((1,), (1,)), ((), ())), precision=precision, preferred_element_type=jnp.float32
    )


def dot_split(a, b):
    (a_high, a_low), (b_high, b_low) = a, b
    left = jnp.concatenate([a_high, a_low], 1)
    right = jnp.concatenate([b_high, b_high], 0)
    return jnp.dot(left, right, preferred_element_type=jnp.float32) + jnp.dot(
        a_high, b_low, preferred_element_type=jnp.float32
    )


def row_sign(shape):
    rows = lax.broadcasted_iota(jnp.int32, shape, 0)
    return jnp.where(rows % SUBLANES < SUBLANES // 2, 1.0, -1.0).astype(jnp.float32)


def lane_sign(shape):
    lanes = lax.broadcasted_iota(jnp.int32, shape, 1)
    return jnp.where(lanes % LANES < LANES // 2, 1.0, -1.0).astype(jnp.float32)


def swap_groups(rows, groups):
    width = LANES // groups
    lane_group = lax.broadcasted_iota(jnp.int32, rows[0].shape, 1) // width
    outs = []
    for j in range(groups):
        out = rows[j]
        for i in range(groups):
            if i != j:
                moved = pltpu.roll(rows[i], (width * (i - j)) % LANES, 1)
                out = jnp.where(lane_group == i, moved, out)
        outs.append(out)
    return outs


COPIES = 8


def beam_kernel(
    chan_count, beams_local, w_hbm, s_hbm, ref_hbm, kept_ref, sent_ref, tiles_ref,
    w_ref, s_ref, ref_ref, w_sem, s_sem, ref_sem,
):
    me = lax.axis_index("chan")
    depth = s_hbm.shape[0] // COPIES
    w_copy = pltpu.make_async_copy(w_hbm, w_ref, w_sem)
    w_copy.start()
    ref_copy = pltpu.make_async_copy(ref_hbm, ref_ref, ref_sem)
    ref_copy.start()
    s_copies = []
    for n in range(COPIES):
        part = pl.ds(n * depth, depth)
        s_copies.append(pltpu.make_async_copy(s_hbm.at[part], s_ref.at[part], s_sem.at[n]))
        s_copies[n].start()
    half = SUBLANES // 2
    sub = lax.broadcasted_iota(jnp.int32, (SUBLANES, w_hbm.shape[2]), 0)
    top = sub < half
    w_copy.wait()
    rows = []
    for parity in range(2):
        for e in range(parity, chan_count, 2):
            base = (me ^ e) * beams_local
            for tile in range(beams_local // SUBLANES):
                start = pl.multiple_of(base + tile * SUBLANES, SUBLANES)
                wr = w_ref[0, pl.ds(start, SUBLANES), :]
                wi = w_ref[1, pl.ds(start, SUBLANES), :]
                wr_s = pltpu.roll(wr, half, 0)
                wi_s = pltpu.roll(wi, half, 0)
                first = [jnp.where(top, wr, wi_s), jnp.where(top, -wi, wr_s)]
                second = [jnp.where(top, wr_s, wi), jnp.where(top, -wi_s, wr)]
                rows.append(jnp.concatenate(first, 1))
                rows.append(jnp.concatenate(second, 1))
    weights = jnp.concatenate(halves(jnp.concatenate(rows, 0)), 0)
    count = weights.shape[0] // 2
    ref_copy.wait()
    for c in range(2):
        for n in range(tiles_ref.shape[1]):
            tiles_ref[c, n : n + 1, :] = ref_ref[c : c + 1, n * LANES : (n + 1) * LANES]
    mid = count // 2
    for copy in s_copies:
        copy.wait()
    high, low = halves(s_ref[...])
    by_high = jnp.dot(weights, high, preferred_element_type=jnp.float32)
    by_low = jnp.dot(weights[:count], low, preferred_element_type=jnp.float32)
    product = by_high[:count] + (by_high[count:] + by_low)
    kept_ref[...] = product[:mid]
    sent_ref[...] = product[mid:]


def beam_call(steering, survey, ref, chan_count, beams_local):
    depth, length = survey.shape
    rows = chan_count * beams_local
    tiles = (2, length // LANES, LANES)
    out = jax.ShapeDtypeStruct((rows, length), jnp.float32)
    hbm, vmem = pl.BlockSpec(memory_space=pltpu.HBM), pl.BlockSpec(memory_space=pltpu.VMEM)
    return pl.pallas_call(
        functools.partial(beam_kernel, chan_count, beams_local),
        in_specs=[hbm] * 3,
        out_specs=[vmem] * 3,
        out_shape=[
            out,
            out,
            jax.ShapeDtypeStruct(tiles, jnp.float32),
        ],
        scratch_shapes=[
            pltpu.VMEM(steering.shape, jnp.float32),
            pltpu.VMEM(survey.shape, jnp.float32),
            pltpu.VMEM(ref.shape, jnp.float32),
            pltpu.SemaphoreType.DMA,
            pltpu.SemaphoreType.DMA((COPIES,)),
            pltpu.SemaphoreType.DMA,
        ],
        compiler_params=params(),
        cost_estimate=cost(2.2),
        name="beams",
    )(*(pltpu.with_memory_space_constraint(x, pltpu.HBM) for x in (steering, survey, ref)))


def sum_kernel(count, *refs):
    kept_ref, sent_ref = refs[-2:]
    for n in range(kept_ref.shape[0]):
        for offset, out_ref in ((0, kept_ref), (1, sent_ref)):
            total = refs[0][2 * n + offset]
            for ref in refs[1:count]:
                total = total + ref[2 * n + offset]
            out_ref[n] = total


def sum_call(parts):
    shape = (parts[0].shape[0] // 2,) + parts[0].shape[1:]
    out = jax.ShapeDtypeStruct(shape, jnp.float32)
    vmem = pl.BlockSpec(memory_space=pltpu.VMEM)
    return pl.pallas_call(
        functools.partial(sum_kernel, len(parts)),
        in_specs=[vmem] * len(parts),
        out_specs=[vmem, vmem],
        out_shape=[out, out],
        compiler_params=params(),
        cost_estimate=cost(0.1),
        name="halves_summed",
    )(*parts)


def join_kernel(first_ref, second_ref, *refs):
    out_ref = refs[-1]
    count = first_ref.shape[0]
    out_ref[:count] = first_ref[...]
    out_ref[count:] = second_ref[...]


def join_call(first, second, *after):
    vmem = pl.BlockSpec(memory_space=pltpu.VMEM)
    return pl.pallas_call(
        join_kernel,
        in_specs=[vmem, vmem] + [pl.BlockSpec(memory_space=pl.ANY)] * len(after),
        out_shape=jax.ShapeDtypeStruct((2 * first.shape[0],) + first.shape[1:], jnp.float32),
        compiler_params=params(),
        cost_estimate=cost(1.0),
        name="reference_joined",
    )(first, second, *after)


def spread_line(line, keep):
    for g in range(0, LANES, 2 * SUBLANES):
        tiled = jnp.broadcast_to(line, (2 * SUBLANES, line.shape[1]))
        for h, value in enumerate(halves(pltpu.roll(tiled, g, 1, stride=1, stride_axis=0)[:, LANES:])):
            keep(h, g, value)


def table_kernel(tiles_ref, out_ref):
    for c in range(2):
        line = jnp.concatenate([tiles_ref[c, n : n + 1, :] for n in range(tiles_ref.shape[1])], 1)

        def keep(h, g, value):
            out_ref[h, c, g : g + 2 * SUBLANES] = value

        spread_line(line, keep)


def table_call(tiles):
    shape = (2, 2, LANES, LANES * (tiles.shape[1] - 1))
    return pl.pallas_call(
        table_kernel,
        out_shape=jax.ShapeDtypeStruct(shape, jnp.bfloat16),
        compiler_params=params(),
        cost_estimate=cost(0.7),
        name="shifted_reference",
    )(tiles)


def first_kernel(tiles_ref, *refs):
    *round_refs, out_ref = refs
    me = lax.axis_index("tm")
    for c in range(2):
        tails = [ref[ref.shape[0] - 1, c, ref.shape[2] - EDGE :, :] for ref in round_refs]
        before = jnp.where(me % 2 == 1, tails[0], jnp.where(me > 0, tails[-1], 0.0))
        line = jnp.concatenate([before[n : n + 1] for n in range(EDGE)] + [tiles_ref[c, 0:1, :]], 1)

        def keep(h, g, value):
            out_ref[h, c, g : g + 2 * SUBLANES] = value

        spread_line(line, keep)


def first_call(tiles, rounds):
    return pl.pallas_call(
        first_kernel,
        out_shape=jax.ShapeDtypeStruct((2, 2, LANES, 2 * LANES), jnp.bfloat16),
        compiler_params=params(),
        cost_estimate=cost(0.1),
        name="shifted_first",
    )(tiles, *rounds)


def lag_kernel(groups, part_count, *refs):
    y_refs, refs = refs[:part_count], refs[part_count:]
    table_ref, first_ref, _, out_hbm, out_ref, out_sem = refs
    copies = []

    def table_tile(h, n):
        parts = []
        for c in range(2):
            known = first_ref.shape[3] // LANES
            ref, at = (first_ref, n) if n < known else (table_ref, n - known)
            parts.append(ref[h, c, :, at * LANES : (at + 1) * LANES])
        return jnp.concatenate(parts, 1)

    def send(start, count):
        part = (slice(None), pl.ds(start, count))
        copies.append(pltpu.make_async_copy(out_ref.at[part], out_hbm.at[part], out_sem.at[len(copies)]))
        copies[-1].start()

    y = y_refs[0][...]
    for y_ref in y_refs[1:]:
        y = y + y_ref[...]
    rows, length = y.shape
    blocks = length // BLOCK_LEN
    turned = jnp.concatenate(
        [pltpu.roll(y[r : r + SUBLANES], SUBLANES // 2, 0) for r in range(0, rows, SUBLANES)], 0
    )
    turned = turned * row_sign(turned.shape)
    y_high, y_low = halves(y)
    t_high, t_low = halves(turned)

    def half_block(q, b):
        cols = slice(q * BLOCK_LEN + b * LANES, q * BLOCK_LEN + (b + 1) * LANES)
        return [jnp.concatenate([x[:, cols], t[:, cols]], 1) for x, t in ((y_high, t_high), (y_low, t_low))]

    def products(stack, n, count):
        high, low = (jnp.concatenate([table_tile(h, n + i) for i in range(count)], 0) for h in range(2))
        by_high = dot_nt(jnp.concatenate([part for pair in stack for part in pair], 0), high)
        by_low = dot_nt(jnp.concatenate([pair[0] for pair in stack], 0), low)
        return [
            by_high[2 * i * rows : (2 * i + 1) * rows]
            + (by_high[(2 * i + 1) * rows : 2 * (i + 1) * rows] + by_low[i * rows : (i + 1) * rows])
            for i in range(len(stack))
        ]

    taps_sum = None
    (far,) = products([half_block(0, 0)], 0, 1)
    for q in range(blocks):
        stack = [half_block(q, 0), half_block(q, 1)]
        if q + 1 < blocks:
            stack.append(half_block(q + 1, 0))
        first, second, *after = products(stack, 2 * q + 1, 2)
        product = jnp.concatenate([first[:, :LANES] + second[:, LANES:], second[:, :LANES] + far], 1)
        if after:
            far = after[0][:, LANES:]
        taps = product[:, :LANES]
        taps_sum = taps if taps_sum is None else taps_sum + taps
        for h in range(LAGS // LANES):
            lanes = slice(h * LANES, (h + 1) * LANES)
            tiles = [product[r : r + SUBLANES, lanes] for r in range(0, rows, SUBLANES)]
            for j, tile in enumerate(swap_groups(tiles, groups)):
                out_ref[h * groups + j, q] = tile
        if q + 1 == blocks - 2:
            send(0, q + 1)
    left = lax.broadcasted_iota(jnp.int32, (SUBLANES, LANES), 1) < TAPS
    for i in range(groups // 2):
        a = taps_sum[i * SUBLANES : (i + 1) * SUBLANES]
        other = i + groups // 2
        b = taps_sum[other * SUBLANES : (other + 1) * SUBLANES]
        tile = jnp.where(left, a, pltpu.roll(b, LANES - TAPS, 1))
        for owner in range(out_ref.shape[0]):
            out_ref[owner, blocks + i] = tile
    send(blocks - 2, 2 + groups // 2)
    for copy in copies:
        copy.wait()


def lag_call(ys, table, first, after, groups, owners):
    blocks = ys[0].shape[1] // BLOCK_LEN
    shape = (owners, blocks + groups // 2, SUBLANES, LANES)
    vmem = pl.BlockSpec(memory_space=pltpu.VMEM)
    return pl.pallas_call(
        functools.partial(lag_kernel, groups, len(ys)),
        in_specs=[vmem] * (len(ys) + 2) + [pl.BlockSpec(memory_space=pl.ANY)],
        out_specs=pl.BlockSpec(memory_space=pltpu.HBM),
        out_shape=jax.ShapeDtypeStruct(shape, jnp.float32),
        scratch_shapes=[
            pltpu.VMEM(shape, jnp.float32),
            pltpu.SemaphoreType.DMA((2,)),
        ],
        compiler_params=params(),
        cost_estimate=cost(2.1),
        name="lag_products",
    )(*ys, table, first, after)


BATCH = 4


def own_kernel(lags_local, *refs):
    *part_refs, _, out_ref, line_ref, tail_ref, span_ref, late_ref, taps_a, lags_a, taps_b, lags_b = refs
    me = lax.axis_index("tm")
    part_rows = part_refs[0].shape[2]
    owners = sum(part_ref.shape[0] for part_ref in part_refs)
    samples = owners * part_rows * LANES
    steps = samples // BLOCK_LEN // BATCH
    total_rows = span_ref.shape[1]
    block_rows = BLOCK_LEN // LANES

    span_ref[...] = jnp.zeros_like(span_ref)
    n = 0
    for part_ref in part_refs:
        for i in range(part_ref.shape[0]):
            block = lax.rem(me - (n // 2) * 2 + owners, owners) ^ (n % 2)
            span_ref[:, pl.ds(EDGE + block * part_rows, part_rows), :] = part_ref[i]
            n += 1
    late_rows = (me * lags_local) // LANES
    late_lanes = lax.rem(me * lags_local, LANES)
    turned = [pltpu.roll(span_ref[c], late_lanes, 1) for c in range(2)]
    before = [pltpu.roll(x, 1, 0) for x in turned]
    lanes = lax.broadcasted_iota(jnp.int32, (total_rows, LANES), 1)
    for c in range(2):
        late_ref[c] = pltpu.roll(jnp.where(lanes < late_lanes, before[c], turned[c]), late_rows, 0)

    def line_of(ref, c, first, count):
        return jnp.concatenate([ref[c, pl.ds(first + n, 1), :] for n in range(count)], 1)

    def shifted(line, by):
        tiled = jnp.broadcast_to(line, (2 * SUBLANES, line.shape[1]))
        return pltpu.roll(tiled, by, 1, stride=1, stride_axis=0)[:, LANES:]

    def keep(ref, row, value):
        high, low = halves(value)
        half = ref.shape[0] // 2
        ref[row : row + 2 * SUBLANES, :] = high
        ref[half + row : half + row + 2 * SUBLANES, :] = low

    def build(n, taps_ref, lags_ref):
        first = EDGE - 1 + n * BATCH * block_rows
        count = BATCH * block_rows + 1
        lines = [line_of(span_ref, c, first, count) for c in range(2)]
        for c in range(2):
            for g in range(0, TAPS, 2 * SUBLANES):
                keep(taps_ref, c * TAPS + g, shifted(lines[c], g))
            late = line_of(late_ref, c, first, count)
            for g in range(0, lags_local, 2 * SUBLANES):
                keep(lags_ref, c * lags_local + g, shifted(late, g))
        pad = jnp.zeros((2 * SUBLANES - 2, BATCH * BLOCK_LEN), jnp.float32)
        keep(lags_ref, 2 * lags_local, jnp.concatenate([line[:, LANES:] for line in lines] + [pad], 0))

    turn = lane_sign((lags_local, LANES))

    def use(n, taps_ref, lags_ref):
        count = lags_ref.shape[0] // 2
        for b in range(BATCH):
            cols = slice(b * BLOCK_LEN, (b + 1) * BLOCK_LEN)
            product = dot_nt(lags_ref[:, cols], taps_ref[:, cols])
            product = product[:count, :LANES] + (product[:count, LANES:] + product[count:, :LANES])
            by_real = product[:lags_local]
            by_imag = product[lags_local : 2 * lags_local]
            rows = pl.ds(pl.multiple_of((n * BATCH + b) * lags_local, lags_local), lags_local)
            high, low = halves(by_real + turn * pltpu.roll(by_imag, TAPS, 1))
            out_ref[0, rows, :] = high
            out_ref[1, rows, :] = low
            line_ref[...] += product[2 * lags_local : 2 * lags_local + SUBLANES]

    line_ref[...] = jnp.zeros_like(line_ref)
    build(0, taps_a, lags_a)

    def pair(m, carry):
        build(2 * m + 1, taps_b, lags_b)
        use(2 * m, taps_a, lags_a)
        build(jnp.minimum(2 * m + 2, steps - 1), taps_a, lags_a)
        use(2 * m + 1, taps_b, lags_b)
        return carry

    lax.fori_loop(0, steps // 2, pair, 0)
    tail = []
    for c in range(2):
        line = line_of(span_ref, c, EDGE + owners * part_rows - 1, 2)
        tail += [shifted(line, g) for g in range(0, TAPS, 2 * SUBLANES)]
    tail = jnp.concatenate(tail, 0)
    tail_ref[...] = dot_nt(tail, tail, HIGHEST)


def own_call(parts, lags_local, after):
    part_rows = parts[0].shape[2]
    span_rows = part_rows * sum(part.shape[0] for part in parts)
    rows = span_rows * LANES // BLOCK_LEN * lags_local
    held_rows = -(-(span_rows + 2 * EDGE) // SUBLANES) * SUBLANES
    width = BATCH * BLOCK_LEN
    taps = pltpu.VMEM((4 * TAPS, width), jnp.bfloat16)
    lags = pltpu.VMEM((4 * lags_local + 4 * SUBLANES, width), jnp.bfloat16)
    span = pltpu.VMEM((2, held_rows, LANES), jnp.float32)
    return pl.pallas_call(
        functools.partial(own_kernel, lags_local),
        in_specs=[pl.BlockSpec(memory_space=pltpu.VMEM)] * len(parts) + [pl.BlockSpec(memory_space=pl.ANY)],
        out_shape=[
            jax.ShapeDtypeStruct((2, rows, 2 * TAPS), jnp.bfloat16),
            jax.ShapeDtypeStruct((SUBLANES, 2 * TAPS), jnp.float32),
            jax.ShapeDtypeStruct((2 * TAPS, 2 * TAPS), jnp.float32),
        ],
        scratch_shapes=[span, span, taps, lags, taps, lags],
        compiler_params=params(),
        cost_estimate=cost(6.2),
        name="reference_products",
    )(*parts, after)


def as_factor(a):
    return jnp.concatenate([a, -lane_sign(a.shape) * pltpu.roll(a, a.shape[0], 1)], 0)


def solver_kernel(line_ref, tail_ref, solver_ref):
    total = line_ref[...]
    line = total[0:1] + lane_sign((1, LANES)) * pltpu.roll(total[1:2], TAPS, 1)
    low = lax.broadcasted_iota(jnp.int32, (1, LANES), 1) < TAPS
    line_r = jnp.where(low, line, 0.0)
    line_i = jnp.where(low, pltpu.roll(line, TAPS, 1), 0.0)
    cols = lax.broadcasted_iota(jnp.int32, (TAPS, TAPS), 1)
    rows = lax.broadcasted_iota(jnp.int32, (TAPS, TAPS), 0)
    above = cols > rows

    def upper(x):
        spread = pltpu.roll(jnp.broadcast_to(x, (TAPS, LANES)), 0, 1, stride=1, stride_axis=0)
        return spread[:, :TAPS]

    up_r = upper(line_r)
    up_i = jnp.where(above, upper(line_i), 0.0)
    strict_r = jnp.where(above, up_r, 0.0)
    diag_r = jnp.where(cols == rows, up_r, 0.0)
    tails = tail_ref[...]
    gram_r = strict_r + strict_r.T + diag_r - (tails[:TAPS, :TAPS] + tails[TAPS:, TAPS:])
    gram_i = up_i - up_i.T - (tails[:TAPS, TAPS:] - tails[TAPS:, :TAPS])
    gram = jnp.concatenate([gram_r, gram_i], 1)
    gram_factor = as_factor(gram)
    gram_halves = halves(gram_factor)
    one = (
        lax.broadcasted_iota(jnp.int32, gram.shape, 0) == lax.broadcasted_iota(jnp.int32, gram.shape, 1)
    ).astype(jnp.float32)
    bound = jnp.max(jnp.sum(jnp.abs(gram), axis=1, keepdims=True), axis=0, keepdims=True)

    def again(state):
        count, left, _ = state
        return (count < 60) & (left > 1e-3)

    def newton(state):
        count, _, x = state
        x_halves = halves(x)
        seen = dot_split(x_halves, gram_halves)
        left = jnp.max(jnp.abs(seen - one))
        x = 2.0 * x - dot_split(halves(seen), halves(as_factor(x)))
        return count + 1, left, x

    start = (jnp.int32(0), jnp.float32(1.0), one * (1.0 / bound))
    _, _, inverse = lax.while_loop(again, newton, start)
    seen = jnp.dot(inverse, gram_factor, precision=HIGHEST, preferred_element_type=jnp.float32)
    inverse = inverse + jnp.dot(
        one - seen, as_factor(inverse), precision=HIGHEST, preferred_element_type=jnp.float32
    )
    solver_ref[...] = as_factor(inverse)


def solver_call(line, tail):
    return pl.pallas_call(
        solver_kernel,
        out_shape=jax.ShapeDtypeStruct(tail.shape, jnp.float32),
        compiler_params=params(),
        cost_estimate=cost(2.0),
        name="gram_inverse",
    )(line, tail)


def doppler_table(block_count, scale):
    phase = (np.arange(block_count)[:, None] * np.arange(DOPPLER)[None, :] % DOPPLER) * (2.0 * math.pi / DOPPLER)
    cosine, sine = np.cos(phase), np.sin(phase)
    upper = np.concatenate([cosine, -sine], 1)
    lower = np.concatenate([sine, cosine], 1)
    return (np.concatenate([upper, lower], 0) * scale).astype(np.float32)


def map_kernel(groups, got_ref, own_ref, solver_ref, wave_ref, out_hbm, held_ref, out_ref, out_sem):
    owners, pieces = got_ref.shape[:2]
    blocks = pieces - groups // 2
    lags_local = LANES // groups
    total = owners * blocks
    left = lax.broadcasted_iota(jnp.int32, (SUBLANES, LANES), 1) < TAPS
    sign = row_sign((SUBLANES, LANES))
    rows = [None] * groups
    for i in range(groups // 2):
        tile = got_ref[0, blocks + i]
        for owner in range(1, owners):
            tile = tile + got_ref[owner, blocks + i]
        swapped = pltpu.roll(tile, TAPS, 1)
        for part, here, there in ((i, tile, swapped), (i + groups // 2, swapped, tile)):
            other = -sign * pltpu.roll(there, SUBLANES // 2, 0)
            rows[part] = jnp.where(left, here, other)
    cross = jnp.concatenate(rows, 0)
    taps = jnp.dot(cross, solver_ref[...], precision=HIGHEST, preferred_element_type=jnp.float32)
    taps_high, taps_low = halves(taps)
    taps_both = jnp.concatenate([taps_high, taps_low], 0)
    count = taps.shape[0]
    for q in range(0, total, 2 * groups):
        own = slice(q * lags_local, (q + 2 * groups) * lags_local)
        by_high = dot_nt(taps_both, own_ref[0, own, :])
        clutter = by_high[:count] + (by_high[count:] + dot_nt(taps_high, own_ref[1, own, :]))
        for h in range(2):
            lanes = slice(h * LANES, (h + 1) * LANES)
            tiles = [clutter[r : r + SUBLANES, lanes] for r in range(0, groups * SUBLANES, SUBLANES)]
            for j, tile in enumerate(swap_groups(tiles, groups)):
                at = q + h * groups + j
                held_ref[at * SUBLANES : (at + 1) * SUBLANES, :] = got_ref[at // blocks, at % blocks] - tile
    half = SUBLANES // 2
    wave = (wave_ref[0], wave_ref[1])
    copies = []
    for g in range(half):
        parts = [held_ref[pl.ds(c * half + g, total, stride=SUBLANES), :] for c in range(2)]
        spectrum = dot_split(halves(jnp.concatenate(parts, 0).T), wave)
        for i in range(groups):
            for c in range(2):
                out_ref[i, g, c] = spectrum[i * lags_local : (i + 1) * lags_local, c * DOPPLER : (c + 1) * DOPPLER]
        part = (slice(None), pl.ds(g, 1))
        copies.append(pltpu.make_async_copy(out_ref.at[part], out_hbm.at[part], out_sem.at[g]))
        copies[-1].start()
    for copy in copies:
        copy.wait()


def map_call(got, own, solver, wave, groups, beams_local):
    total = got.shape[0] * (got.shape[1] - groups // 2)
    lags_local = LANES // groups
    half = SUBLANES // 2
    shape = (beams_local // half, half, 2, lags_local, DOPPLER)
    out = pl.pallas_call(
        functools.partial(map_kernel, groups),
        in_specs=[pl.BlockSpec(memory_space=pltpu.VMEM)] * 4,
        out_specs=pl.BlockSpec(memory_space=pltpu.HBM),
        out_shape=jax.ShapeDtypeStruct(shape, jnp.float32),
        scratch_shapes=[
            pltpu.VMEM((total * SUBLANES, LANES), jnp.float32),
            pltpu.VMEM(shape, jnp.float32),
            pltpu.SemaphoreType.DMA((half,)),
        ],
        compiler_params=params(),
        cost_estimate=cost(2.5),
        name="range_doppler",
    )(got, own, solver, wave)
    return out.reshape((beams_local,) + shape[2:])


def swap(x, axis, by):
    pairs = [(i, i ^ by) for i in range(lax.axis_size(axis))]
    return lax.ppermute(x, axis, pairs)


def tiled_device(ref_signal, surveillance, steering):
    chan_count, tm_count = lax.axis_size("chan"), lax.axis_size("tm")
    channels, length = surveillance.shape[1:]
    beams_local = steering.shape[1] // chan_count
    lags_local = LAGS // tm_count
    groups = LANES // lags_local
    samples = length * tm_count

    survey = surveillance.reshape(2 * channels, length)
    kept, moved, tiles = beam_call(steering, survey, ref_signal, chan_count, beams_local)
    near = swap(tiles[None], "tm", 1)
    shape = (chan_count // 2, 2 * beams_local, length)
    kept, got = kept.reshape(shape), swap(moved, "chan", 1).reshape(shape)
    by = 2
    while by < chan_count:
        kept, moved = sum_call([kept, got])
        got = swap(moved, "chan", by)
        by *= 2
    rounds = [near]
    joined = join_call(tiles[None], near, moved)
    while True:
        count = joined.shape[0]
        rounds.append(lax.ppermute(joined, "tm", [(i, (i + count) % tm_count) for i in range(tm_count)]))
        if count * 2 == tm_count:
            break
        joined = join_call(joined, rounds[-1])
    table = table_call(tiles)
    first = first_call(tiles, rounds[:2])
    pieces = lag_call([kept[0], got[0]], table, first, joined, groups, tm_count)
    got = lax.all_to_all(pieces, "tm", 0, 0, tiled=True)
    own, line, tail = own_call([tiles[None]] + rounds, lags_local, pieces)
    solver = solver_call(line, tail)
    wave = doppler_table(samples // BLOCK_LEN, 0.125 / math.sqrt(samples))
    high = wave.astype(jnp.bfloat16)
    wave = np.stack([high, (wave - high.astype(np.float32)).astype(jnp.bfloat16)])
    return map_call(got, own, solver, jnp.asarray(wave), groups, beams_local)


def lag_table(ref_ext, offset, lags):
    window = lax.dynamic_slice_in_dim(ref_ext, offset, BLOCK_LEN + LAGS, 1)
    span = BLOCK_LEN + LAGS
    tiled = jnp.tile(jnp.pad(window, ((0, 0), (0, 1))), (1, lags))[:, : lags * span]
    return tiled.reshape(2, lags, span)[:, :, LAGS:]


def times_conj(a, b):
    real = jnp.einsum("...t,lt->...l", a[..., 0, :], b[0], precision=HIGHEST) + jnp.einsum(
        "...t,lt->...l", a[..., 1, :], b[1], precision=HIGHEST
    )
    imag = jnp.einsum("...t,lt->...l", a[..., 1, :], b[0], precision=HIGHEST) - jnp.einsum(
        "...t,lt->...l", a[..., 0, :], b[1], precision=HIGHEST
    )
    return jnp.stack([real, imag], -2)


def plain_device(ref_signal, surveillance, steering):
    chan_count, tm_count = lax.axis_size("chan"), lax.axis_size("tm")
    length = surveillance.shape[2]
    beams = steering.shape[1]
    lags_local = LAGS // tm_count
    samples = length * tm_count
    local_blocks = length // BLOCK_LEN
    here = lax.axis_index("tm")

    w_real, w_imag = steering
    real = jnp.dot(w_real, surveillance[0], precision=HIGHEST) - jnp.dot(w_imag, surveillance[1], precision=HIGHEST)
    imag = jnp.dot(w_imag, surveillance[0], precision=HIGHEST) + jnp.dot(w_real, surveillance[1], precision=HIGHEST)
    beam = lax.psum_scatter(jnp.stack([real, imag], 1), "chan", scatter_dimension=0, tiled=True)
    ref_all = lax.all_gather(ref_signal, "tm", axis=1, tiled=True)
    ref_ext = jnp.pad(ref_all, ((0, 0), (LAGS, 0)))

    def beam_step(carry, q):
        offset = q * BLOCK_LEN
        table = lag_table(ref_ext, here * length + offset, LAGS)
        segment = lax.dynamic_slice_in_dim(beam, offset, BLOCK_LEN, 2)
        return carry, times_conj(segment, table)

    _, products = lax.scan(beam_step, None, jnp.arange(local_blocks, dtype=jnp.int32))
    cross = lax.psum(products[..., :TAPS].sum(0), "tm")
    got = lax.all_to_all(products, "tm", 3, 0, tiled=True)

    def own_step(gram, q):
        offset = q * BLOCK_LEN
        table = lag_table(ref_ext, offset, LAGS)
        taps = table[:, :TAPS].transpose(1, 0, 2)
        mine = lax.dynamic_slice_in_dim(table, here * lags_local, lags_local, 1)
        return gram + times_conj(taps, table[:, :TAPS]), times_conj(taps, mine)

    start = jnp.zeros((TAPS, 2, TAPS), jnp.float32)
    gram, own = lax.scan(own_step, start, jnp.arange(samples // BLOCK_LEN, dtype=jnp.int32))
    g_real, g_imag = gram[:, 0].T, gram[:, 1].T
    system = jnp.concatenate([jnp.concatenate([g_real, -g_imag], 1), jnp.concatenate([g_imag, g_real], 1)], 0)
    right = jnp.concatenate([cross[:, 0].T, cross[:, 1].T], 0)
    solved = jax.scipy.linalg.cho_solve((jnp.linalg.cholesky(system), True), right)
    b_real, b_imag = solved[:TAPS].T, solved[TAPS:].T
    mixing = jnp.concatenate([jnp.stack([b_real, b_imag], 1), jnp.stack([-b_imag, b_real], 1)], 2)
    stacked = jnp.concatenate([own[:, :, 0], own[:, :, 1]], 1)
    lagged = got - jnp.einsum("mck,qkl->qmcl", mixing, stacked, precision=HIGHEST)
    wave = jnp.asarray(doppler_table(samples // BLOCK_LEN, 0.125 / math.sqrt(samples)))
    wave = wave.reshape(2, samples // BLOCK_LEN, 2, DOPPLER)
    return jnp.einsum("qmcl,cqdk->mdlk", lagged, wave, precision=HIGHEST)


def on_device(ref_signal, surveillance, steering):
    chan_count, tm_count = lax.axis_size("chan"), lax.axis_size("tm")
    beams_local = steering.shape[1] // chan_count
    lags_local = LAGS // tm_count
    fills = (
        LANES % lags_local == 0
        and lags_local % (2 * SUBLANES) == 0
        and beams_local * lags_local == LANES * SUBLANES // 2
        and chan_count > 1
        and chan_count & (chan_count - 1) == 0
        and tm_count > 2
        and tm_count & (tm_count - 1) == 0
        and 2 * surveillance.shape[1] % LANES == 0
        and surveillance.shape[2] % (2 * BATCH * BLOCK_LEN) == 0
    )
    device = tiled_device if fills else plain_device
    return device(ref_signal, surveillance, steering)


def solution(mesh):
    placed = (P(None, "tm"), P(None, "chan", "tm"), P(None, None, "chan"))
    return jax.shard_map(
        on_device,
        mesh=mesh,
        in_specs=placed,
        out_specs=P("chan", None, "tm", None),
        check_vma=False,
    )
```

```python
import functools
import math

import jax
import jax.numpy as jnp
import numpy as np
from jax import lax
from jax.experimental import pallas as pl
from jax.experimental.pallas import tpu as pltpu
from jax.sharding import PartitionSpec as P

LAGS = 256
DOPPLER = 256
TAPS = 64
BLOCK_LEN = 256
LANES = 128
SUBLANES = 8
EDGE = 2

HIGHEST = lax.Precision.HIGHEST
VMEM_BYTES = 48 * 1024 * 1024


def params():
    return pltpu.CompilerParams(vmem_limit_bytes=VMEM_BYTES)


def cost(us):
    return pl.CostEstimate(flops=int(us * 1.15e9), bytes_accessed=0, transcendentals=0)


def halves(x):
    high = x.astype(jnp.bfloat16)
    return high, (x - high.astype(jnp.float32)).astype(jnp.bfloat16)


def dot_nt(a, b, precision=None):
    return lax.dot_general(
        a, b, (((1,), (1,)), ((), ())), precision=precision, preferred_element_type=jnp.float32
    )


def dot_split(a, b):
    (a_high, a_low), (b_high, b_low) = a, b
    left = jnp.concatenate([a_high, a_low], 1)
    right = jnp.concatenate([b_high, b_high], 0)
    return jnp.dot(left, right, preferred_element_type=jnp.float32) + jnp.dot(
        a_high, b_low, preferred_element_type=jnp.float32
    )


def row_sign(shape):
    rows = lax.broadcasted_iota(jnp.int32, shape, 0)
    return jnp.where(rows % SUBLANES < SUBLANES // 2, 1.0, -1.0).astype(jnp.float32)


def lane_sign(shape):
    lanes = lax.broadcasted_iota(jnp.int32, shape, 1)
    return jnp.where(lanes % LANES < LANES // 2, 1.0, -1.0).astype(jnp.float32)


def swap_groups(rows, groups):
    width = LANES // groups
    lane_group = lax.broadcasted_iota(jnp.int32, rows[0].shape, 1) // width
    outs = []
    for j in range(groups):
        out = rows[j]
        for i in range(groups):
            if i != j:
                moved = pltpu.roll(rows[i], (width * (i - j)) % LANES, 1)
                out = jnp.where(lane_group == i, moved, out)
        outs.append(out)
    return outs


COPIES = 1


def beam_kernel(
    chan_count, beams_local, w_hbm, s_hbm, ref_hbm, kept_ref, sent_ref, tiles_ref,
    w_ref, s_ref, ref_ref, w_sem, s_sem, ref_sem,
):
    me = lax.axis_index("chan")
    depth = s_hbm.shape[0] // COPIES
    w_copy = pltpu.make_async_copy(w_hbm, w_ref, w_sem)
    w_copy.start()
    ref_copy = pltpu.make_async_copy(ref_hbm, ref_ref, ref_sem)
    ref_copy.start()
    s_copies = []
    for n in range(COPIES):
        part = pl.ds(n * depth, depth)
        s_copies.append(pltpu.make_async_copy(s_hbm.at[part], s_ref.at[part], s_sem.at[n]))
        s_copies[n].start()
    half = SUBLANES // 2
    sub = lax.broadcasted_iota(jnp.int32, (SUBLANES, w_hbm.shape[2]), 0)
    top = sub < half
    w_copy.wait()
    rows = []
    for parity in range(2):
        for e in range(parity, chan_count, 2):
            base = (me ^ e) * beams_local
            for tile in range(beams_local // SUBLANES):
                start = pl.multiple_of(base + tile * SUBLANES, SUBLANES)
                wr = w_ref[0, pl.ds(start, SUBLANES), :]
                wi = w_ref[1, pl.ds(start, SUBLANES), :]
                wr_s = pltpu.roll(wr, half, 0)
                wi_s = pltpu.roll(wi, half, 0)
                first = [jnp.where(top, wr, wi_s), jnp.where(top, -wi, wr_s)]
                second = [jnp.where(top, wr_s, wi), jnp.where(top, -wi_s, wr)]
                rows.append(jnp.concatenate(first, 1))
                rows.append(jnp.concatenate(second, 1))
    weights = jnp.concatenate(halves(jnp.concatenate(rows, 0)), 0)
    count = weights.shape[0] // 2
    ref_copy.wait()
    for c in range(2):
        for n in range(tiles_ref.shape[1]):
            tiles_ref[c, n : n + 1, :] = ref_ref[c : c + 1, n * LANES : (n + 1) * LANES]
    mid = count // 2
    for copy in s_copies:
        copy.wait()
    high, low = halves(s_ref[...])
    by_high = jnp.dot(weights, high, preferred_element_type=jnp.float32)
    by_low = jnp.dot(weights[:count], low, preferred_element_type=jnp.float32)
    product = by_high[:count] + (by_high[count:] + by_low)
    kept_ref[...] = product[:mid]
    sent_ref[...] = product[mid:]


def beam_call(steering, survey, ref, chan_count, beams_local):
    depth, length = survey.shape
    rows = chan_count * beams_local
    tiles = (2, length // LANES, LANES)
    out = jax.ShapeDtypeStruct((rows, length), jnp.float32)
    hbm, vmem = pl.BlockSpec(memory_space=pltpu.HBM), pl.BlockSpec(memory_space=pltpu.VMEM)
    return pl.pallas_call(
        functools.partial(beam_kernel, chan_count, beams_local),
        in_specs=[hbm] * 3,
        out_specs=[vmem] * 3,
        out_shape=[
            out,
            out,
            jax.ShapeDtypeStruct(tiles, jnp.float32),
        ],
        scratch_shapes=[
            pltpu.VMEM(steering.shape, jnp.float32),
            pltpu.VMEM(survey.shape, jnp.float32),
            pltpu.VMEM(ref.shape, jnp.float32),
            pltpu.SemaphoreType.DMA,
            pltpu.SemaphoreType.DMA((COPIES,)),
            pltpu.SemaphoreType.DMA,
        ],
        compiler_params=params(),
        cost_estimate=cost(2.2),
        name="beams",
    )(*(pltpu.with_memory_space_constraint(x, pltpu.HBM) for x in (steering, survey, ref)))


def sum_kernel(count, *refs):
    kept_ref, sent_ref = refs[-2:]
    for n in range(kept_ref.shape[0]):
        for offset, out_ref in ((0, kept_ref), (1, sent_ref)):
            total = refs[0][2 * n + offset]
            for ref in refs[1:count]:
                total = total + ref[2 * n + offset]
            out_ref[n] = total


def sum_call(parts):
    shape = (parts[0].shape[0] // 2,) + parts[0].shape[1:]
    out = jax.ShapeDtypeStruct(shape, jnp.float32)
    vmem = pl.BlockSpec(memory_space=pltpu.VMEM)
    return pl.pallas_call(
        functools.partial(sum_kernel, len(parts)),
        in_specs=[vmem] * len(parts),
        out_specs=[vmem, vmem],
        out_shape=[out, out],
        compiler_params=params(),
        cost_estimate=cost(0.1),
        name="halves_summed",
    )(*parts)


def join_kernel(first_ref, second_ref, *refs):
    out_ref = refs[-1]
    count = first_ref.shape[0]
    out_ref[:count] = first_ref[...]
    out_ref[count:] = second_ref[...]


def join_call(first, second, *after):
    vmem = pl.BlockSpec(memory_space=pltpu.VMEM)
    return pl.pallas_call(
        join_kernel,
        in_specs=[vmem, vmem] + [pl.BlockSpec(memory_space=pl.ANY)] * len(after),
        out_shape=jax.ShapeDtypeStruct((2 * first.shape[0],) + first.shape[1:], jnp.float32),
        compiler_params=params(),
        cost_estimate=cost(1.0),
        name="reference_joined",
    )(first, second, *after)


def spread_line(line, keep):
    for g in range(0, LANES, 2 * SUBLANES):
        tiled = jnp.broadcast_to(line, (2 * SUBLANES, line.shape[1]))
        for h, value in enumerate(halves(pltpu.roll(tiled, g, 1, stride=1, stride_axis=0)[:, LANES:])):
            keep(h, g, value)


def table_kernel(tiles_ref, out_ref):
    for c in range(2):
        line = jnp.concatenate([tiles_ref[c, n : n + 1, :] for n in range(tiles_ref.shape[1])], 1)

        def keep(h, g, value):
            out_ref[h, c, g : g + 2 * SUBLANES] = value

        spread_line(line, keep)


def table_call(tiles):
    shape = (2, 2, LANES, LANES * (tiles.shape[1] - 1))
    return pl.pallas_call(
        table_kernel,
        out_shape=jax.ShapeDtypeStruct(shape, jnp.bfloat16),
        compiler_params=params(),
        cost_estimate=cost(0.7),
        name="shifted_reference",
    )(tiles)


def first_kernel(tiles_ref, *refs):
    *round_refs, out_ref = refs
    me = lax.axis_index("tm")
    for c in range(2):
        tails = [ref[ref.shape[0] - 1, c, ref.shape[2] - EDGE :, :] for ref in round_refs]
        before = jnp.where(me % 2 == 1, tails[0], jnp.where(me > 0, tails[-1], 0.0))
        line = jnp.concatenate([before[n : n + 1] for n in range(EDGE)] + [tiles_ref[c, 0:1, :]], 1)

        def keep(h, g, value):
            out_ref[h, c, g : g + 2 * SUBLANES] = value

        spread_line(line, keep)


def first_call(tiles, rounds):
    return pl.pallas_call(
        first_kernel,
        out_shape=jax.ShapeDtypeStruct((2, 2, LANES, 2 * LANES), jnp.bfloat16),
        compiler_params=params(),
        cost_estimate=cost(0.1),
        name="shifted_first",
    )(tiles, *rounds)


def lag_kernel(groups, part_count, *refs):
    y_refs, refs = refs[:part_count], refs[part_count:]
    table_ref, first_ref, _, out_hbm, out_ref, out_sem = refs
    def table_tile(h, n):
        parts = []
        for c in range(2):
            known = first_ref.shape[3] // LANES
            ref, at = (first_ref, n) if n < known else (table_ref, n - known)
            parts.append(ref[h, c, :, at * LANES : (at + 1) * LANES])
        return jnp.concatenate(parts, 1)

    y = y_refs[0][...]
    for y_ref in y_refs[1:]:
        y = y + y_ref[...]
    rows, length = y.shape
    blocks = length // BLOCK_LEN
    turned = jnp.concatenate(
        [pltpu.roll(y[r : r + SUBLANES], SUBLANES // 2, 0) for r in range(0, rows, SUBLANES)], 0
    )
    turned = turned * row_sign(turned.shape)
    y_high, y_low = halves(y)
    t_high, t_low = halves(turned)

    def half_block(q, b):
        cols = slice(q * BLOCK_LEN + b * LANES, q * BLOCK_LEN + (b + 1) * LANES)
        return [jnp.concatenate([x[:, cols], t[:, cols]], 1) for x, t in ((y_high, t_high), (y_low, t_low))]

    def products(stack, n, count):
        high, low = (jnp.concatenate([table_tile(h, n + i) for i in range(count)], 0) for h in range(2))
        by_high = dot_nt(jnp.concatenate([part for pair in stack for part in pair], 0), high)
        by_low = dot_nt(jnp.concatenate([pair[0] for pair in stack], 0), low)
        return [
            by_high[2 * i * rows : (2 * i + 1) * rows]
            + (by_high[(2 * i + 1) * rows : 2 * (i + 1) * rows] + by_low[i * rows : (i + 1) * rows])
            for i in range(len(stack))
        ]

    taps_sum = None
    (far,) = products([half_block(0, 0)], 0, 1)
    for q in range(blocks):
        stack = [half_block(q, 0), half_block(q, 1)]
        if q + 1 < blocks:
            stack.append(half_block(q + 1, 0))
        first, second, *after = products(stack, 2 * q + 1, 2)
        product = jnp.concatenate([first[:, :LANES] + second[:, LANES:], second[:, :LANES] + far], 1)
        if after:
            far = after[0][:, LANES:]
        taps = product[:, :LANES]
        taps_sum = taps if taps_sum is None else taps_sum + taps
        for h in range(LAGS // LANES):
            lanes = slice(h * LANES, (h + 1) * LANES)
            tiles = [product[r : r + SUBLANES, lanes] for r in range(0, rows, SUBLANES)]
            for j, tile in enumerate(swap_groups(tiles, groups)):
                out_ref[h * groups + j, q] = tile
    left = lax.broadcasted_iota(jnp.int32, (SUBLANES, LANES), 1) < TAPS
    for i in range(groups // 2):
        a = taps_sum[i * SUBLANES : (i + 1) * SUBLANES]
        other = i + groups // 2
        b = taps_sum[other * SUBLANES : (other + 1) * SUBLANES]
        tile = jnp.where(left, a, pltpu.roll(b, LANES - TAPS, 1))
        for owner in range(out_ref.shape[0]):
            out_ref[owner, blocks + i] = tile
    copy = pltpu.make_async_copy(out_ref, out_hbm, out_sem)
    copy.start()
    copy.wait()


def lag_call(ys, table, first, after, groups, owners):
    blocks = ys[0].shape[1] // BLOCK_LEN
    shape = (owners, blocks + groups // 2, SUBLANES, LANES)
    vmem = pl.BlockSpec(memory_space=pltpu.VMEM)
    return pl.pallas_call(
        functools.partial(lag_kernel, groups, len(ys)),
        in_specs=[vmem] * (len(ys) + 2) + [pl.BlockSpec(memory_space=pl.ANY)],
        out_specs=pl.BlockSpec(memory_space=pltpu.HBM),
        out_shape=jax.ShapeDtypeStruct(shape, jnp.float32),
        scratch_shapes=[
            pltpu.VMEM(shape, jnp.float32),
            pltpu.SemaphoreType.DMA,
        ],
        compiler_params=params(),
        cost_estimate=cost(2.1),
        name="lag_products",
    )(*ys, table, first, after)


BATCH = 4


def own_kernel(lags_local, *refs):
    *part_refs, _, out_ref, line_ref, tail_ref, span_ref, late_ref, taps_a, lags_a, taps_b, lags_b = refs
    me = lax.axis_index("tm")
    part_rows = part_refs[0].shape[2]
    owners = sum(part_ref.shape[0] for part_ref in part_refs)
    samples = owners * part_rows * LANES
    steps = samples // BLOCK_LEN // BATCH
    total_rows = span_ref.shape[1]
    block_rows = BLOCK_LEN // LANES

    span_ref[...] = jnp.zeros_like(span_ref)
    n = 0
    for part_ref in part_refs:
        for i in range(part_ref.shape[0]):
            block = lax.rem(me - (n // 2) * 2 + owners, owners) ^ (n % 2)
            span_ref[:, pl.ds(EDGE + block * part_rows, part_rows), :] = part_ref[i]
            n += 1
    late_rows = (me * lags_local) // LANES
    late_lanes = lax.rem(me * lags_local, LANES)
    turned = [pltpu.roll(span_ref[c], late_lanes, 1) for c in range(2)]
    before = [pltpu.roll(x, 1, 0) for x in turned]
    lanes = lax.broadcasted_iota(jnp.int32, (total_rows, LANES), 1)
    for c in range(2):
        late_ref[c] = pltpu.roll(jnp.where(lanes < late_lanes, before[c], turned[c]), late_rows, 0)

    def line_of(ref, c, first, count):
        return jnp.concatenate([ref[c, pl.ds(first + n, 1), :] for n in range(count)], 1)

    def shifted(line, by):
        tiled = jnp.broadcast_to(line, (2 * SUBLANES, line.shape[1]))
        return pltpu.roll(tiled, by, 1, stride=1, stride_axis=0)[:, LANES:]

    def keep(ref, row, value):
        high, low = halves(value)
        half = ref.shape[0] // 2
        ref[row : row + 2 * SUBLANES, :] = high
        ref[half + row : half + row + 2 * SUBLANES, :] = low

    def build(n, taps_ref, lags_ref):
        first = EDGE - 1 + n * BATCH * block_rows
        count = BATCH * block_rows + 1
        lines = [line_of(span_ref, c, first, count) for c in range(2)]
        for c in range(2):
            for g in range(0, TAPS, 2 * SUBLANES):
                keep(taps_ref, c * TAPS + g, shifted(lines[c], g))
            late = line_of(late_ref, c, first, count)
            for g in range(0, lags_local, 2 * SUBLANES):
                keep(lags_ref, c * lags_local + g, shifted(late, g))
        pad = jnp.zeros((2 * SUBLANES - 2, BATCH * BLOCK_LEN), jnp.float32)
        keep(lags_ref, 2 * lags_local, jnp.concatenate([line[:, LANES:] for line in lines] + [pad], 0))

    turn = lane_sign((lags_local, LANES))

    def use(n, taps_ref, lags_ref):
        count = lags_ref.shape[0] // 2
        for b in range(BATCH):
            cols = slice(b * BLOCK_LEN, (b + 1) * BLOCK_LEN)
            product = dot_nt(lags_ref[:, cols], taps_ref[:, cols])
            product = product[:count, :LANES] + (product[:count, LANES:] + product[count:, :LANES])
            by_real = product[:lags_local]
            by_imag = product[lags_local : 2 * lags_local]
            rows = pl.ds(pl.multiple_of((n * BATCH + b) * lags_local, lags_local), lags_local)
            high, low = halves(by_real + turn * pltpu.roll(by_imag, TAPS, 1))
            out_ref[0, rows, :] = high
            out_ref[1, rows, :] = low
            line_ref[...] += product[2 * lags_local : 2 * lags_local + SUBLANES]

    line_ref[...] = jnp.zeros_like(line_ref)
    build(0, taps_a, lags_a)

    def pair(m, carry):
        build(2 * m + 1, taps_b, lags_b)
        use(2 * m, taps_a, lags_a)
        build(jnp.minimum(2 * m + 2, steps - 1), taps_a, lags_a)
        use(2 * m + 1, taps_b, lags_b)
        return carry

    lax.fori_loop(0, steps // 2, pair, 0)
    tail = []
    for c in range(2):
        line = line_of(span_ref, c, EDGE + owners * part_rows - 1, 2)
        tail += [shifted(line, g) for g in range(0, TAPS, 2 * SUBLANES)]
    tail = jnp.concatenate(tail, 0)
    tail_ref[...] = dot_nt(tail, tail, HIGHEST)


def own_call(parts, lags_local, after):
    part_rows = parts[0].shape[2]
    span_rows = part_rows * sum(part.shape[0] for part in parts)
    rows = span_rows * LANES // BLOCK_LEN * lags_local
    held_rows = -(-(span_rows + 2 * EDGE) // SUBLANES) * SUBLANES
    width = BATCH * BLOCK_LEN
    taps = pltpu.VMEM((4 * TAPS, width), jnp.bfloat16)
    lags = pltpu.VMEM((4 * lags_local + 4 * SUBLANES, width), jnp.bfloat16)
    span = pltpu.VMEM((2, held_rows, LANES), jnp.float32)
    return pl.pallas_call(
        functools.partial(own_kernel, lags_local),
        in_specs=[pl.BlockSpec(memory_space=pltpu.VMEM)] * len(parts) + [pl.BlockSpec(memory_space=pl.ANY)],
        out_shape=[
            jax.ShapeDtypeStruct((2, rows, 2 * TAPS), jnp.bfloat16),
            jax.ShapeDtypeStruct((SUBLANES, 2 * TAPS), jnp.float32),
            jax.ShapeDtypeStruct((2 * TAPS, 2 * TAPS), jnp.float32),
        ],
        scratch_shapes=[span, span, taps, lags, taps, lags],
        compiler_params=params(),
        cost_estimate=cost(6.2),
        name="reference_products",
    )(*parts, after)


def as_factor(a):
    return jnp.concatenate([a, -lane_sign(a.shape) * pltpu.roll(a, a.shape[0], 1)], 0)


def solver_kernel(line_ref, tail_ref, solver_ref):
    total = line_ref[...]
    line = total[0:1] + lane_sign((1, LANES)) * pltpu.roll(total[1:2], TAPS, 1)
    low = lax.broadcasted_iota(jnp.int32, (1, LANES), 1) < TAPS
    line_r = jnp.where(low, line, 0.0)
    line_i = jnp.where(low, pltpu.roll(line, TAPS, 1), 0.0)
    cols = lax.broadcasted_iota(jnp.int32, (TAPS, TAPS), 1)
    rows = lax.broadcasted_iota(jnp.int32, (TAPS, TAPS), 0)
    above = cols > rows

    def upper(x):
        spread = pltpu.roll(jnp.broadcast_to(x, (TAPS, LANES)), 0, 1, stride=1, stride_axis=0)
        return spread[:, :TAPS]

    up_r = upper(line_r)
    up_i = jnp.where(above, upper(line_i), 0.0)
    strict_r = jnp.where(above, up_r, 0.0)
    diag_r = jnp.where(cols == rows, up_r, 0.0)
    tails = tail_ref[...]
    gram_r = strict_r + strict_r.T + diag_r - (tails[:TAPS, :TAPS] + tails[TAPS:, TAPS:])
    gram_i = up_i - up_i.T - (tails[:TAPS, TAPS:] - tails[TAPS:, :TAPS])
    gram = jnp.concatenate([gram_r, gram_i], 1)
    gram_factor = as_factor(gram)
    gram_halves = halves(gram_factor)
    one = (
        lax.broadcasted_iota(jnp.int32, gram.shape, 0) == lax.broadcasted_iota(jnp.int32, gram.shape, 1)
    ).astype(jnp.float32)
    bound = jnp.max(jnp.sum(jnp.abs(gram), axis=1, keepdims=True), axis=0, keepdims=True)

    def again(state):
        count, left, _ = state
        return (count < 60) & (left > 1e-3)

    def newton(state):
        count, _, x = state
        x_halves = halves(x)
        seen = dot_split(x_halves, gram_halves)
        left = jnp.max(jnp.abs(seen - one))
        x = 2.0 * x - dot_split(halves(seen), halves(as_factor(x)))
        return count + 1, left, x

    start = (jnp.int32(0), jnp.float32(1.0), one * (1.0 / bound))
    _, _, inverse = lax.while_loop(again, newton, start)
    seen = jnp.dot(inverse, gram_factor, precision=HIGHEST, preferred_element_type=jnp.float32)
    inverse = inverse + jnp.dot(
        one - seen, as_factor(inverse), precision=HIGHEST, preferred_element_type=jnp.float32
    )
    solver_ref[...] = as_factor(inverse)


def solver_call(line, tail):
    return pl.pallas_call(
        solver_kernel,
        out_shape=jax.ShapeDtypeStruct(tail.shape, jnp.float32),
        compiler_params=params(),
        cost_estimate=cost(2.0),
        name="gram_inverse",
    )(line, tail)


def doppler_table(block_count, scale):
    phase = (np.arange(block_count)[:, None] * np.arange(DOPPLER)[None, :] % DOPPLER) * (2.0 * math.pi / DOPPLER)
    cosine, sine = np.cos(phase), np.sin(phase)
    upper = np.concatenate([cosine, -sine], 1)
    lower = np.concatenate([sine, cosine], 1)
    return (np.concatenate([upper, lower], 0) * scale).astype(np.float32)


def map_kernel(groups, got_ref, own_ref, solver_ref, wave_ref, out_hbm, held_ref, out_ref, out_sem):
    owners, pieces = got_ref.shape[:2]
    blocks = pieces - groups // 2
    lags_local = LANES // groups
    total = owners * blocks
    left = lax.broadcasted_iota(jnp.int32, (SUBLANES, LANES), 1) < TAPS
    sign = row_sign((SUBLANES, LANES))
    rows = [None] * groups
    for i in range(groups // 2):
        tile = got_ref[0, blocks + i]
        for owner in range(1, owners):
            tile = tile + got_ref[owner, blocks + i]
        swapped = pltpu.roll(tile, TAPS, 1)
        for part, here, there in ((i, tile, swapped), (i + groups // 2, swapped, tile)):
            other = -sign * pltpu.roll(there, SUBLANES // 2, 0)
            rows[part] = jnp.where(left, here, other)
    cross = jnp.concatenate(rows, 0)
    taps = jnp.dot(cross, solver_ref[...], precision=HIGHEST, preferred_element_type=jnp.float32)
    taps_high, taps_low = halves(taps)
    taps_both = jnp.concatenate([taps_high, taps_low], 0)
    count = taps.shape[0]
    for q in range(0, total, 2 * groups):
        own = slice(q * lags_local, (q + 2 * groups) * lags_local)
        by_high = dot_nt(taps_both, own_ref[0, own, :])
        clutter = by_high[:count] + (by_high[count:] + dot_nt(taps_high, own_ref[1, own, :]))
        for h in range(2):
            lanes = slice(h * LANES, (h + 1) * LANES)
            tiles = [clutter[r : r + SUBLANES, lanes] for r in range(0, groups * SUBLANES, SUBLANES)]
            for j, tile in enumerate(swap_groups(tiles, groups)):
                at = q + h * groups + j
                held_ref[at * SUBLANES : (at + 1) * SUBLANES, :] = got_ref[at // blocks, at % blocks] - tile
    half = SUBLANES // 2
    wave = (wave_ref[0], wave_ref[1])
    copies = []
    for g in range(half):
        parts = [held_ref[pl.ds(c * half + g, total, stride=SUBLANES), :] for c in range(2)]
        spectrum = dot_split(halves(jnp.concatenate(parts, 0).T), wave)
        for i in range(groups):
            for c in range(2):
                out_ref[i, g, c] = spectrum[i * lags_local : (i + 1) * lags_local, c * DOPPLER : (c + 1) * DOPPLER]
        part = (slice(None), pl.ds(g, 1))
        copies.append(pltpu.make_async_copy(out_ref.at[part], out_hbm.at[part], out_sem.at[g]))
        copies[-1].start()
    for copy in copies:
        copy.wait()


def map_call(got, own, solver, wave, groups, beams_local):
    total = got.shape[0] * (got.shape[1] - groups // 2)
    lags_local = LANES // groups
    half = SUBLANES // 2
    shape = (beams_local // half, half, 2, lags_local, DOPPLER)
    out = pl.pallas_call(
        functools.partial(map_kernel, groups),
        in_specs=[pl.BlockSpec(memory_space=pltpu.VMEM)] * 4,
        out_specs=pl.BlockSpec(memory_space=pltpu.HBM),
        out_shape=jax.ShapeDtypeStruct(shape, jnp.float32),
        scratch_shapes=[
            pltpu.VMEM((total * SUBLANES, LANES), jnp.float32),
            pltpu.VMEM(shape, jnp.float32),
            pltpu.SemaphoreType.DMA((half,)),
        ],
        compiler_params=params(),
        cost_estimate=cost(2.5),
        name="range_doppler",
    )(got, own, solver, wave)
    return out.reshape((beams_local,) + shape[2:])


def swap(x, axis, by):
    pairs = [(i, i ^ by) for i in range(lax.axis_size(axis))]
    return lax.ppermute(x, axis, pairs)


def tiled_device(ref_signal, surveillance, steering):
    chan_count, tm_count = lax.axis_size("chan"), lax.axis_size("tm")
    channels, length = surveillance.shape[1:]
    beams_local = steering.shape[1] // chan_count
    lags_local = LAGS // tm_count
    groups = LANES // lags_local
    samples = length * tm_count

    survey = surveillance.reshape(2 * channels, length)
    kept, moved, tiles = beam_call(steering, survey, ref_signal, chan_count, beams_local)
    near = swap(tiles[None], "tm", 1)
    shape = (chan_count // 2, 2 * beams_local, length)
    kept, got = kept.reshape(shape), swap(moved, "chan", 1).reshape(shape)
    by = 2
    while by < chan_count:
        kept, moved = sum_call([kept, got])
        got = swap(moved, "chan", by)
        by *= 2
    rounds = [near]
    joined = join_call(tiles[None], near, moved)
    while True:
        count = joined.shape[0]
        rounds.append(lax.ppermute(joined, "tm", [(i, (i + count) % tm_count) for i in range(tm_count)]))
        if count * 2 == tm_count:
            break
        joined = join_call(joined, rounds[-1])
    table = table_call(tiles)
    first = first_call(tiles, rounds[:2])
    pieces = lag_call([kept[0], got[0]], table, first, joined, groups, tm_count)
    got = lax.all_to_all(pieces, "tm", 0, 0, tiled=True)
    own, line, tail = own_call([tiles[None]] + rounds, lags_local, pieces)
    solver = solver_call(line, tail)
    wave = doppler_table(samples // BLOCK_LEN, 0.125 / math.sqrt(samples))
    high = wave.astype(jnp.bfloat16)
    wave = np.stack([high, (wave - high.astype(np.float32)).astype(jnp.bfloat16)])
    return map_call(got, own, solver, jnp.asarray(wave), groups, beams_local)


def lag_table(ref_ext, offset, lags):
    window = lax.dynamic_slice_in_dim(ref_ext, offset, BLOCK_LEN + LAGS, 1)
    span = BLOCK_LEN + LAGS
    tiled = jnp.tile(jnp.pad(window, ((0, 0), (0, 1))), (1, lags))[:, : lags * span]
    return tiled.reshape(2, lags, span)[:, :, LAGS:]


def times_conj(a, b):
    real = jnp.einsum("...t,lt->...l", a[..., 0, :], b[0], precision=HIGHEST) + jnp.einsum(
        "...t,lt->...l", a[..., 1, :], b[1], precision=HIGHEST
    )
    imag = jnp.einsum("...t,lt->...l", a[..., 1, :], b[0], precision=HIGHEST) - jnp.einsum(
        "...t,lt->...l", a[..., 0, :], b[1], precision=HIGHEST
    )
    return jnp.stack([real, imag], -2)


def plain_device(ref_signal, surveillance, steering):
    chan_count, tm_count = lax.axis_size("chan"), lax.axis_size("tm")
    length = surveillance.shape[2]
    beams = steering.shape[1]
    lags_local = LAGS // tm_count
    samples = length * tm_count
    local_blocks = length // BLOCK_LEN
    here = lax.axis_index("tm")

    w_real, w_imag = steering
    real = jnp.dot(w_real, surveillance[0], precision=HIGHEST) - jnp.dot(w_imag, surveillance[1], precision=HIGHEST)
    imag = jnp.dot(w_imag, surveillance[0], precision=HIGHEST) + jnp.dot(w_real, surveillance[1], precision=HIGHEST)
    beam = lax.psum_scatter(jnp.stack([real, imag], 1), "chan", scatter_dimension=0, tiled=True)
    ref_all = lax.all_gather(ref_signal, "tm", axis=1, tiled=True)
    ref_ext = jnp.pad(ref_all, ((0, 0), (LAGS, 0)))

    def beam_step(carry, q):
        offset = q * BLOCK_LEN
        table = lag_table(ref_ext, here * length + offset, LAGS)
        segment = lax.dynamic_slice_in_dim(beam, offset, BLOCK_LEN, 2)
        return carry, times_conj(segment, table)

    _, products = lax.scan(beam_step, None, jnp.arange(local_blocks, dtype=jnp.int32))
    cross = lax.psum(products[..., :TAPS].sum(0), "tm")
    got = lax.all_to_all(products, "tm", 3, 0, tiled=True)

    def own_step(gram, q):
        offset = q * BLOCK_LEN
        table = lag_table(ref_ext, offset, LAGS)
        taps = table[:, :TAPS].transpose(1, 0, 2)
        mine = lax.dynamic_slice_in_dim(table, here * lags_local, lags_local, 1)
        return gram + times_conj(taps, table[:, :TAPS]), times_conj(taps, mine)

    start = jnp.zeros((TAPS, 2, TAPS), jnp.float32)
    gram, own = lax.scan(own_step, start, jnp.arange(samples // BLOCK_LEN, dtype=jnp.int32))
    g_real, g_imag = gram[:, 0].T, gram[:, 1].T
    system = jnp.concatenate([jnp.concatenate([g_real, -g_imag], 1), jnp.concatenate([g_imag, g_real], 1)], 0)
    right = jnp.concatenate([cross[:, 0].T, cross[:, 1].T], 0)
    solved = jax.scipy.linalg.cho_solve((jnp.linalg.cholesky(system), True), right)
    b_real, b_imag = solved[:TAPS].T, solved[TAPS:].T
    mixing = jnp.concatenate([jnp.stack([b_real, b_imag], 1), jnp.stack([-b_imag, b_real], 1)], 2)
    stacked = jnp.concatenate([own[:, :, 0], own[:, :, 1]], 1)
    lagged = got - jnp.einsum("mck,qkl->qmcl", mixing, stacked, precision=HIGHEST)
    wave = jnp.asarray(doppler_table(samples // BLOCK_LEN, 0.125 / math.sqrt(samples)))
    wave = wave.reshape(2, samples // BLOCK_LEN, 2, DOPPLER)
    return jnp.einsum("qmcl,cqdk->mdlk", lagged, wave, precision=HIGHEST)


def on_device(ref_signal, surveillance, steering):
    chan_count, tm_count = lax.axis_size("chan"), lax.axis_size("tm")
    beams_local = steering.shape[1] // chan_count
    lags_local = LAGS // tm_count
    fills = (
        LANES % lags_local == 0
        and lags_local % (2 * SUBLANES) == 0
        and beams_local * lags_local == LANES * SUBLANES // 2
        and chan_count > 1
        and chan_count & (chan_count - 1) == 0
        and tm_count > 2
        and tm_count & (tm_count - 1) == 0
        and 2 * surveillance.shape[1] % LANES == 0
        and surveillance.shape[2] % (2 * BATCH * BLOCK_LEN) == 0
    )
    device = tiled_device if fills else plain_device
    return device(ref_signal, surveillance, steering)


def solution(mesh):
    placed = (P(None, "tm"), P(None, "chan", "tm"), P(None, None, "chan"))
    return jax.shard_map(
        on_device,
        mesh=mesh,
        in_specs=placed,
        out_specs=P("chan", None, "tm", None),
        check_vma=False,
    )
```

```python
import functools
import math

import jax
import jax.numpy as jnp
import numpy as np
from jax import lax
from jax.experimental import pallas as pl
from jax.experimental.pallas import tpu as pltpu
from jax.sharding import PartitionSpec as P

LAGS = 256
DOPPLER = 256
TAPS = 64
BLOCK_LEN = 256
LANES = 128
SUBLANES = 8
EDGE = 2

HIGHEST = lax.Precision.HIGHEST
VMEM_BYTES = 48 * 1024 * 1024


def params():
    return pltpu.CompilerParams(vmem_limit_bytes=VMEM_BYTES)


def cost(us):
    return pl.CostEstimate(flops=int(us * 1.15e9), bytes_accessed=0, transcendentals=0)


def halves(x):
    high = x.astype(jnp.bfloat16)
    return high, (x - high.astype(jnp.float32)).astype(jnp.bfloat16)


def thirds(x):
    high = x.astype(jnp.bfloat16)
    rest = x - high.astype(jnp.float32)
    return (high,) + halves(rest)


def dot_parts(a, b, across=False):
    rows = a[0].shape[0]
    by_size = {}
    for j, right in enumerate(b):
        left = a[: max(3 - j, 1)]
        left = left[0] if len(left) == 1 else jnp.concatenate(left, 0)
        contract = (((1,), (1 if across else 0,)), ((), ()))
        product = lax.dot_general(left, right, contract, preferred_element_type=jnp.float32)
        for i in range(product.shape[0] // rows):
            by_size.setdefault(i + j, []).append(product[i * rows : (i + 1) * rows])
    total = None
    for size in sorted(by_size, reverse=True):
        for term in by_size[size]:
            total = term if total is None else total + term
    return total


def dot_nt(a, b, precision=None):
    return lax.dot_general(
        a, b, (((1,), (1,)), ((), ())), precision=precision, preferred_element_type=jnp.float32
    )


def dot_split(a, b):
    (a_high, a_low), (b_high, b_low) = a, b
    left = jnp.concatenate([a_high, a_low], 1)
    right = jnp.concatenate([b_high, b_high], 0)
    return jnp.dot(left, right, preferred_element_type=jnp.float32) + jnp.dot(
        a_high, b_low, preferred_element_type=jnp.float32
    )


def row_sign(shape):
    rows = lax.broadcasted_iota(jnp.int32, shape, 0)
    return jnp.where(rows % SUBLANES < SUBLANES // 2, 1.0, -1.0).astype(jnp.float32)


def lane_sign(shape):
    lanes = lax.broadcasted_iota(jnp.int32, shape, 1)
    return jnp.where(lanes % LANES < LANES // 2, 1.0, -1.0).astype(jnp.float32)


def swap_groups(rows, groups):
    width = LANES // groups
    lane_group = lax.broadcasted_iota(jnp.int32, rows[0].shape, 1) // width
    outs = []
    for j in range(groups):
        out = rows[j]
        for i in range(groups):
            if i != j:
                moved = pltpu.roll(rows[i], (width * (i - j)) % LANES, 1)
                out = jnp.where(lane_group == i, moved, out)
        outs.append(out)
    return outs


COPIES = 4


def beam_kernel(
    chan_count, beams_local, w_hbm, s_hbm, ref_hbm, kept_ref, sent_ref, tiles_ref,
    w_ref, s_ref, ref_ref, w_sem, s_sem, ref_sem,
):
    me = lax.axis_index("chan")
    depth = s_hbm.shape[0] // COPIES
    w_copy = pltpu.make_async_copy(w_hbm, w_ref, w_sem)
    w_copy.start()
    ref_copy = pltpu.make_async_copy(ref_hbm, ref_ref, ref_sem)
    ref_copy.start()
    s_copies = []
    for n in range(COPIES):
        part = pl.ds(n * depth, depth)
        s_copies.append(pltpu.make_async_copy(s_hbm.at[part], s_ref.at[part], s_sem.at[n]))
        s_copies[n].start()
    half = SUBLANES // 2
    sub = lax.broadcasted_iota(jnp.int32, (SUBLANES, w_hbm.shape[2]), 0)
    top = sub < half
    w_copy.wait()
    rows = []
    for parity in range(2):
        for e in range(parity, chan_count, 2):
            base = (me ^ e) * beams_local
            for tile in range(beams_local // SUBLANES):
                start = pl.multiple_of(base + tile * SUBLANES, SUBLANES)
                wr = w_ref[0, pl.ds(start, SUBLANES), :]
                wi = w_ref[1, pl.ds(start, SUBLANES), :]
                wr_s = pltpu.roll(wr, half, 0)
                wi_s = pltpu.roll(wi, half, 0)
                first = [jnp.where(top, wr, wi_s), jnp.where(top, -wi, wr_s)]
                second = [jnp.where(top, wr_s, wi), jnp.where(top, -wi_s, wr)]
                rows.append(jnp.concatenate(first, 1))
                rows.append(jnp.concatenate(second, 1))
    weights = halves(jnp.concatenate(rows, 0))
    ref_copy.wait()
    for c in range(2):
        for n in range(tiles_ref.shape[1]):
            tiles_ref[c, n : n + 1, :] = ref_ref[c : c + 1, n * LANES : (n + 1) * LANES]
    for copy in s_copies:
        copy.wait()
    product = dot_parts(weights, thirds(s_ref[...]))
    mid = product.shape[0] // 2
    kept_ref[...] = product[:mid]
    sent_ref[...] = product[mid:]


def beam_call(steering, survey, ref, chan_count, beams_local):
    depth, length = survey.shape
    rows = chan_count * beams_local
    tiles = (2, length // LANES, LANES)
    out = jax.ShapeDtypeStruct((rows, length), jnp.float32)
    hbm, vmem = pl.BlockSpec(memory_space=pltpu.HBM), pl.BlockSpec(memory_space=pltpu.VMEM)
    return pl.pallas_call(
        functools.partial(beam_kernel, chan_count, beams_local),
        in_specs=[hbm] * 3,
        out_specs=[vmem] * 3,
        out_shape=[
            out,
            out,
            jax.ShapeDtypeStruct(tiles, jnp.float32),
        ],
        scratch_shapes=[
            pltpu.VMEM(steering.shape, jnp.float32),
            pltpu.VMEM(survey.shape, jnp.float32),
            pltpu.VMEM(ref.shape, jnp.float32),
            pltpu.SemaphoreType.DMA,
            pltpu.SemaphoreType.DMA((COPIES,)),
            pltpu.SemaphoreType.DMA,
        ],
        compiler_params=params(),
        cost_estimate=cost(2.2),
        name="beams",
    )(*(pltpu.with_memory_space_constraint(x, pltpu.HBM) for x in (steering, survey, ref)))


def sum_kernel(count, *refs):
    kept_ref, sent_ref = refs[-2:]
    for n in range(kept_ref.shape[0]):
        for offset, out_ref in ((0, kept_ref), (1, sent_ref)):
            total = refs[0][2 * n + offset]
            for ref in refs[1:count]:
                total = total + ref[2 * n + offset]
            out_ref[n] = total


def sum_call(parts):
    shape = (parts[0].shape[0] // 2,) + parts[0].shape[1:]
    out = jax.ShapeDtypeStruct(shape, jnp.float32)
    vmem = pl.BlockSpec(memory_space=pltpu.VMEM)
    return pl.pallas_call(
        functools.partial(sum_kernel, len(parts)),
        in_specs=[vmem] * len(parts),
        out_specs=[vmem, vmem],
        out_shape=[out, out],
        compiler_params=params(),
        cost_estimate=cost(0.1),
        name="halves_summed",
    )(*parts)


def join_kernel(first_ref, second_ref, *refs):
    out_ref = refs[-1]
    count = first_ref.shape[0]
    out_ref[:count] = first_ref[...]
    out_ref[count:] = second_ref[...]


def join_call(first, second, *after):
    vmem = pl.BlockSpec(memory_space=pltpu.VMEM)
    return pl.pallas_call(
        join_kernel,
        in_specs=[vmem, vmem] + [pl.BlockSpec(memory_space=pl.ANY)] * len(after),
        out_shape=jax.ShapeDtypeStruct((2 * first.shape[0],) + first.shape[1:], jnp.float32),
        compiler_params=params(),
        cost_estimate=cost(1.0),
        name="reference_joined",
    )(first, second, *after)


def spread_line(line, keep):
    for g in range(0, LANES, 2 * SUBLANES):
        tiled = jnp.broadcast_to(line, (2 * SUBLANES, line.shape[1]))
        for h, value in enumerate(halves(pltpu.roll(tiled, g, 1, stride=1, stride_axis=0)[:, LANES:])):
            keep(h, g, value)


def table_kernel(tiles_ref, out_ref):
    for c in range(2):
        line = jnp.concatenate([tiles_ref[c, n : n + 1, :] for n in range(tiles_ref.shape[1])], 1)

        def keep(h, g, value):
            out_ref[h, c, g : g + 2 * SUBLANES] = value

        spread_line(line, keep)


def table_call(tiles):
    shape = (2, 2, LANES, LANES * (tiles.shape[1] - 1))
    return pl.pallas_call(
        table_kernel,
        out_shape=jax.ShapeDtypeStruct(shape, jnp.bfloat16),
        compiler_params=params(),
        cost_estimate=cost(0.7),
        name="shifted_reference",
    )(tiles)


def first_kernel(tiles_ref, *refs):
    *round_refs, out_ref = refs
    me = lax.axis_index("tm")
    for c in range(2):
        tails = [ref[ref.shape[0] - 1, c, ref.shape[2] - EDGE :, :] for ref in round_refs]
        before = jnp.where(me % 2 == 1, tails[0], jnp.where(me > 0, tails[-1], 0.0))
        line = jnp.concatenate([before[n : n + 1] for n in range(EDGE)] + [tiles_ref[c, 0:1, :]], 1)

        def keep(h, g, value):
            out_ref[h, c, g : g + 2 * SUBLANES] = value

        spread_line(line, keep)


def first_call(tiles, rounds):
    return pl.pallas_call(
        first_kernel,
        out_shape=jax.ShapeDtypeStruct((2, 2, LANES, 2 * LANES), jnp.bfloat16),
        compiler_params=params(),
        cost_estimate=cost(0.1),
        name="shifted_first",
    )(tiles, *rounds)


def lag_kernel(groups, part_count, *refs):
    y_refs, refs = refs[:part_count], refs[part_count:]
    table_ref, first_ref, _, out_hbm, out_ref, out_sem = refs
    copies = []

    def table_tile(h, n):
        parts = []
        for c in range(2):
            known = first_ref.shape[3] // LANES
            ref, at = (first_ref, n) if n < known else (table_ref, n - known)
            parts.append(ref[h, c, :, at * LANES : (at + 1) * LANES])
        return jnp.concatenate(parts, 1)

    def send(start, count):
        part = (slice(None), pl.ds(start, count))
        copies.append(pltpu.make_async_copy(out_ref.at[part], out_hbm.at[part], out_sem.at[len(copies)]))
        copies[-1].start()

    y = y_refs[0][...]
    for y_ref in y_refs[1:]:
        y = y + y_ref[...]
    rows, length = y.shape
    blocks = length // BLOCK_LEN
    turned = jnp.concatenate(
        [pltpu.roll(y[r : r + SUBLANES], SUBLANES // 2, 0) for r in range(0, rows, SUBLANES)], 0
    )
    turned = turned * row_sign(turned.shape)
    y_parts, t_parts = thirds(y), thirds(turned)

    def half_block(q, b):
        cols = slice(q * BLOCK_LEN + b * LANES, q * BLOCK_LEN + (b + 1) * LANES)
        return [jnp.concatenate([x[:, cols], t[:, cols]], 1) for x, t in zip(y_parts, t_parts)]

    def products(stack, n, count):
        tiles = [jnp.concatenate([table_tile(h, n + i) for i in range(count)], 0) for h in range(2)]
        product = dot_parts([jnp.concatenate(part, 0) for part in zip(*stack)], tiles, True)
        return [product[i * rows : (i + 1) * rows] for i in range(len(stack))]

    taps_sum = None
    (far,) = products([half_block(0, 0)], 0, 1)
    for q in range(blocks):
        stack = [half_block(q, 0), half_block(q, 1)]
        if q + 1 < blocks:
            stack.append(half_block(q + 1, 0))
        first, second, *after = products(stack, 2 * q + 1, 2)
        product = jnp.concatenate([first[:, :LANES] + second[:, LANES:], second[:, :LANES] + far], 1)
        if after:
            far = after[0][:, LANES:]
        taps = product[:, :LANES]
        taps_sum = taps if taps_sum is None else taps_sum + taps
        for h in range(LAGS // LANES):
            lanes = slice(h * LANES, (h + 1) * LANES)
            tiles = [product[r : r + SUBLANES, lanes] for r in range(0, rows, SUBLANES)]
            for j, tile in enumerate(swap_groups(tiles, groups)):
                out_ref[h * groups + j, q] = tile
        if q + 1 == blocks // 2:
            send(0, blocks // 2)
    left = lax.broadcasted_iota(jnp.int32, (SUBLANES, LANES), 1) < TAPS
    for i in range(groups // 2):
        a = taps_sum[i * SUBLANES : (i + 1) * SUBLANES]
        other = i + groups // 2
        b = taps_sum[other * SUBLANES : (other + 1) * SUBLANES]
        tile = jnp.where(left, a, pltpu.roll(b, LANES - TAPS, 1))
        for owner in range(out_ref.shape[0]):
            out_ref[owner, blocks + i] = tile
    send(blocks // 2, blocks - blocks // 2 + groups // 2)
    for copy in copies:
        copy.wait()


def lag_call(ys, table, first, after, groups, owners):
    blocks = ys[0].shape[1] // BLOCK_LEN
    shape = (owners, blocks + groups // 2, SUBLANES, LANES)
    vmem = pl.BlockSpec(memory_space=pltpu.VMEM)
    return pl.pallas_call(
        functools.partial(lag_kernel, groups, len(ys)),
        in_specs=[vmem] * (len(ys) + 2) + [pl.BlockSpec(memory_space=pl.ANY)],
        out_specs=pl.BlockSpec(memory_space=pltpu.HBM),
        out_shape=jax.ShapeDtypeStruct(shape, jnp.float32),
        scratch_shapes=[
            pltpu.VMEM(shape, jnp.float32),
            pltpu.SemaphoreType.DMA((2,)),
        ],
        compiler_params=params(),
        cost_estimate=cost(2.1),
        name="lag_products",
    )(*ys, table, first, after)


BATCH = 4


def own_kernel(lags_local, *refs):
    *part_refs, _, out_ref, line_ref, tail_ref, span_ref, late_ref, taps_a, lags_a, taps_b, lags_b = refs
    me = lax.axis_index("tm")
    part_rows = part_refs[0].shape[2]
    owners = sum(part_ref.shape[0] for part_ref in part_refs)
    samples = owners * part_rows * LANES
    steps = samples // BLOCK_LEN // BATCH
    total_rows = span_ref.shape[1]
    block_rows = BLOCK_LEN // LANES

    span_ref[...] = jnp.zeros_like(span_ref)
    n = 0
    for part_ref in part_refs:
        for i in range(part_ref.shape[0]):
            block = lax.rem(me - (n // 2) * 2 + owners, owners) ^ (n % 2)
            span_ref[:, pl.ds(EDGE + block * part_rows, part_rows), :] = part_ref[i]
            n += 1
    late_rows = (me * lags_local) // LANES
    late_lanes = lax.rem(me * lags_local, LANES)
    turned = [pltpu.roll(span_ref[c], late_lanes, 1) for c in range(2)]
    before = [pltpu.roll(x, 1, 0) for x in turned]
    lanes = lax.broadcasted_iota(jnp.int32, (total_rows, LANES), 1)
    for c in range(2):
        late_ref[c] = pltpu.roll(jnp.where(lanes < late_lanes, before[c], turned[c]), late_rows, 0)

    def line_of(ref, c, first, count):
        return jnp.concatenate([ref[c, pl.ds(first + n, 1), :] for n in range(count)], 1)

    def shifted(line, by):
        tiled = jnp.broadcast_to(line, (2 * SUBLANES, line.shape[1]))
        return pltpu.roll(tiled, by, 1, stride=1, stride_axis=0)[:, LANES:]

    def keep(ref, row, parts):
        step = ref.shape[0] // len(parts)
        for n, part in enumerate(parts):
            ref[n * step + row : n * step + row + 2 * SUBLANES, :] = part

    def build(n, taps_ref, lags_ref):
        first = EDGE - 1 + n * BATCH * block_rows
        count = BATCH * block_rows + 1
        lines = [line_of(span_ref, c, first, count) for c in range(2)]
        for c in range(2):
            for g in range(0, TAPS, 2 * SUBLANES):
                keep(taps_ref, c * TAPS + g, thirds(shifted(lines[c], g)))
            late = line_of(late_ref, c, first, count)
            for g in range(0, lags_local, 2 * SUBLANES):
                keep(lags_ref, c * lags_local + g, halves(shifted(late, g)))
        pad = jnp.zeros((2 * SUBLANES - 2, BATCH * BLOCK_LEN), jnp.float32)
        keep(lags_ref, 2 * lags_local, halves(jnp.concatenate([line[:, LANES:] for line in lines] + [pad], 0)))

    turn = lane_sign((lags_local, LANES))

    def use(n, taps_ref, lags_ref):
        count = lags_ref.shape[0] // 2
        for b in range(BATCH):
            cols = slice(b * BLOCK_LEN, (b + 1) * BLOCK_LEN)
            product = dot_nt(lags_ref[:, cols], taps_ref[: 2 * LANES, cols])
            least = dot_nt(lags_ref[:count, cols], taps_ref[2 * LANES :, cols]) + product[count:, LANES:]
            product = product[:count, :LANES] + ((product[:count, LANES:] + product[count:, :LANES]) + least)
            by_real = product[:lags_local]
            by_imag = product[lags_local : 2 * lags_local]
            rows = pl.ds(pl.multiple_of((n * BATCH + b) * lags_local, lags_local), lags_local)
            for part, value in enumerate(thirds(by_real + turn * pltpu.roll(by_imag, TAPS, 1))):
                out_ref[part, rows, :] = value
            line_ref[...] += product[2 * lags_local : 2 * lags_local + SUBLANES]

    line_ref[...] = jnp.zeros_like(line_ref)
    build(0, taps_a, lags_a)

    def pair(m, carry):
        build(2 * m + 1, taps_b, lags_b)
        use(2 * m, taps_a, lags_a)
        build(jnp.minimum(2 * m + 2, steps - 1), taps_a, lags_a)
        use(2 * m + 1, taps_b, lags_b)
        return carry

    lax.fori_loop(0, steps // 2, pair, 0)
    tail = []
    for c in range(2):
        line = line_of(span_ref, c, EDGE + owners * part_rows - 1, 2)
        tail += [shifted(line, g) for g in range(0, TAPS, 2 * SUBLANES)]
    tail = jnp.concatenate(tail, 0)
    tail_ref[...] = dot_nt(tail, tail, HIGHEST)


def own_call(parts, lags_local, after):
    part_rows = parts[0].shape[2]
    span_rows = part_rows * sum(part.shape[0] for part in parts)
    rows = span_rows * LANES // BLOCK_LEN * lags_local
    held_rows = -(-(span_rows + 2 * EDGE) // SUBLANES) * SUBLANES
    width = BATCH * BLOCK_LEN
    taps = pltpu.VMEM((6 * TAPS, width), jnp.bfloat16)
    lags = pltpu.VMEM((4 * lags_local + 4 * SUBLANES, width), jnp.bfloat16)
    span = pltpu.VMEM((2, held_rows, LANES), jnp.float32)
    return pl.pallas_call(
        functools.partial(own_kernel, lags_local),
        in_specs=[pl.BlockSpec(memory_space=pltpu.VMEM)] * len(parts) + [pl.BlockSpec(memory_space=pl.ANY)],
        out_shape=[
            jax.ShapeDtypeStruct((3, rows, 2 * TAPS), jnp.bfloat16),
            jax.ShapeDtypeStruct((SUBLANES, 2 * TAPS), jnp.float32),
            jax.ShapeDtypeStruct((2 * TAPS, 2 * TAPS), jnp.float32),
        ],
        scratch_shapes=[span, span, taps, lags, taps, lags],
        compiler_params=params(),
        cost_estimate=cost(6.2),
        name="reference_products",
    )(*parts, after)


def as_factor(a):
    return jnp.concatenate([a, -lane_sign(a.shape) * pltpu.roll(a, a.shape[0], 1)], 0)


def solver_kernel(line_ref, tail_ref, gram_ref, solver_ref):
    total = line_ref[...]
    line = total[0:1] + lane_sign((1, LANES)) * pltpu.roll(total[1:2], TAPS, 1)
    low = lax.broadcasted_iota(jnp.int32, (1, LANES), 1) < TAPS
    line_r = jnp.where(low, line, 0.0)
    line_i = jnp.where(low, pltpu.roll(line, TAPS, 1), 0.0)
    cols = lax.broadcasted_iota(jnp.int32, (TAPS, TAPS), 1)
    rows = lax.broadcasted_iota(jnp.int32, (TAPS, TAPS), 0)
    above = cols > rows

    def upper(x):
        spread = pltpu.roll(jnp.broadcast_to(x, (TAPS, LANES)), 0, 1, stride=1, stride_axis=0)
        return spread[:, :TAPS]

    up_r = upper(line_r)
    up_i = jnp.where(above, upper(line_i), 0.0)
    strict_r = jnp.where(above, up_r, 0.0)
    diag_r = jnp.where(cols == rows, up_r, 0.0)
    tails = tail_ref[...]
    gram_r = strict_r + strict_r.T + diag_r - (tails[:TAPS, :TAPS] + tails[TAPS:, TAPS:])
    gram_i = up_i - up_i.T - (tails[:TAPS, TAPS:] - tails[TAPS:, :TAPS])
    gram = jnp.concatenate([gram_r, gram_i], 1)
    gram_factor = as_factor(gram)
    gram_ref[...] = gram_factor
    gram_halves = halves(gram_factor)
    one = (
        lax.broadcasted_iota(jnp.int32, gram.shape, 0) == lax.broadcasted_iota(jnp.int32, gram.shape, 1)
    ).astype(jnp.float32)
    bound = jnp.max(jnp.sum(jnp.abs(gram), axis=1, keepdims=True), axis=0, keepdims=True)

    def again(state):
        count, left, _ = state
        return (count < 60) & (left > 1e-3)

    def newton(state):
        count, _, x = state
        x_halves = halves(x)
        seen = dot_split(x_halves, gram_halves)
        left = jnp.max(jnp.abs(seen - one))
        x = 2.0 * x - dot_split(halves(seen), halves(as_factor(x)))
        return count + 1, left, x

    start = (jnp.int32(0), jnp.float32(1.0), one * (1.0 / bound))
    _, _, inverse = lax.while_loop(again, newton, start)
    seen = jnp.dot(inverse, gram_factor, precision=HIGHEST, preferred_element_type=jnp.float32)
    inverse = inverse + jnp.dot(
        one - seen, as_factor(inverse), precision=HIGHEST, preferred_element_type=jnp.float32
    )
    solver_ref[...] = as_factor(inverse)


def solver_call(line, tail):
    return pl.pallas_call(
        solver_kernel,
        out_shape=[jax.ShapeDtypeStruct(tail.shape, jnp.float32)] * 2,
        compiler_params=params(),
        cost_estimate=cost(2.0),
        name="gram_inverse",
    )(line, tail)


def doppler_table(block_count, scale):
    phase = (np.arange(block_count)[:, None] * np.arange(DOPPLER)[None, :] % DOPPLER) * (2.0 * math.pi / DOPPLER)
    cosine, sine = np.cos(phase), np.sin(phase)
    upper = np.concatenate([cosine, -sine], 1)
    lower = np.concatenate([sine, cosine], 1)
    return (np.concatenate([upper, lower], 0) * scale).astype(np.float32)


def map_kernel(groups, got_ref, own_ref, gram_ref, solver_ref, wave_ref, out_hbm, held_ref, out_ref, out_sem):
    owners, pieces = got_ref.shape[:2]
    blocks = pieces - groups // 2
    lags_local = LANES // groups
    total = owners * blocks
    left = lax.broadcasted_iota(jnp.int32, (SUBLANES, LANES), 1) < TAPS
    sign = row_sign((SUBLANES, LANES))
    rows = [None] * groups
    for i in range(groups // 2):
        tile = got_ref[0, blocks + i]
        for owner in range(1, owners):
            tile = tile + got_ref[owner, blocks + i]
        swapped = pltpu.roll(tile, TAPS, 1)
        for part, here, there in ((i, tile, swapped), (i + groups // 2, swapped, tile)):
            other = -sign * pltpu.roll(there, SUBLANES // 2, 0)
            rows[part] = jnp.where(left, here, other)
    cross = jnp.concatenate(rows, 0)

    def exact(x, ref):
        return jnp.dot(x, ref[...], precision=HIGHEST, preferred_element_type=jnp.float32)

    taps = exact(cross, solver_ref)
    taps = taps + exact(cross - exact(taps, gram_ref), solver_ref)
    taps = thirds(taps)
    for q in range(0, total, 2 * groups):
        own = slice(q * lags_local, (q + 2 * groups) * lags_local)
        clutter = dot_parts(taps, [own_ref[part, own, :] for part in range(3)], True)
        for h in range(2):
            lanes = slice(h * LANES, (h + 1) * LANES)
            tiles = [clutter[r : r + SUBLANES, lanes] for r in range(0, groups * SUBLANES, SUBLANES)]
            for j, tile in enumerate(swap_groups(tiles, groups)):
                at = q + h * groups + j
                held_ref[at * SUBLANES : (at + 1) * SUBLANES, :] = got_ref[at // blocks, at % blocks] - tile
    half = SUBLANES // 2
    wave = (wave_ref[0], wave_ref[1])
    copies = []
    for g in range(half):
        parts = [held_ref[pl.ds(c * half + g, total, stride=SUBLANES), :] for c in range(2)]
        spectrum = dot_split(halves(jnp.concatenate(parts, 0).T), wave)
        for i in range(groups):
            for c in range(2):
                out_ref[i, g, c] = spectrum[i * lags_local : (i + 1) * lags_local, c * DOPPLER : (c + 1) * DOPPLER]
        part = (slice(None), pl.ds(g, 1))
        copies.append(pltpu.make_async_copy(out_ref.at[part], out_hbm.at[part], out_sem.at[g]))
        copies[-1].start()
    for copy in copies:
        copy.wait()


def map_call(got, own, gram, solver, wave, groups, beams_local):
    total = got.shape[0] * (got.shape[1] - groups // 2)
    lags_local = LANES // groups
    half = SUBLANES // 2
    shape = (beams_local // half, half, 2, lags_local, DOPPLER)
    out = pl.pallas_call(
        functools.partial(map_kernel, groups),
        in_specs=[pl.BlockSpec(memory_space=pltpu.VMEM)] * 5,
        out_specs=pl.BlockSpec(memory_space=pltpu.HBM),
        out_shape=jax.ShapeDtypeStruct(shape, jnp.float32),
        scratch_shapes=[
            pltpu.VMEM((total * SUBLANES, LANES), jnp.float32),
            pltpu.VMEM(shape, jnp.float32),
            pltpu.SemaphoreType.DMA((half,)),
        ],
        compiler_params=params(),
        cost_estimate=cost(2.5),
        name="range_doppler",
    )(got, own, gram, solver, wave)
    return out.reshape((beams_local,) + shape[2:])


def swap(x, axis, by):
    pairs = [(i, i ^ by) for i in range(lax.axis_size(axis))]
    return lax.ppermute(x, axis, pairs)


def tiled_device(ref_signal, surveillance, steering):
    chan_count, tm_count = lax.axis_size("chan"), lax.axis_size("tm")
    channels, length = surveillance.shape[1:]
    beams_local = steering.shape[1] // chan_count
    lags_local = LAGS // tm_count
    groups = LANES // lags_local
    samples = length * tm_count

    survey = surveillance.reshape(2 * channels, length)
    kept, moved, tiles = beam_call(steering, survey, ref_signal, chan_count, beams_local)
    near = swap(tiles[None], "tm", 1)
    shape = (chan_count // 2, 2 * beams_local, length)
    kept, got = kept.reshape(shape), swap(moved, "chan", 1).reshape(shape)
    by = 2
    while by < chan_count:
        kept, moved = sum_call([kept, got])
        got = swap(moved, "chan", by)
        by *= 2
    rounds = [near]
    joined = join_call(tiles[None], near, moved)
    while True:
        count = joined.shape[0]
        rounds.append(lax.ppermute(joined, "tm", [(i, (i + count) % tm_count) for i in range(tm_count)]))
        if count * 2 == tm_count:
            break
        joined = join_call(joined, rounds[-1])
    table = table_call(tiles)
    first = first_call(tiles, rounds[:2])
    pieces = lag_call([kept[0], got[0]], table, first, joined, groups, tm_count)
    got = lax.all_to_all(pieces, "tm", 0, 0, tiled=True)
    own, line, tail = own_call([tiles[None]] + rounds, lags_local, pieces)
    gram, solver = solver_call(line, tail)
    wave = doppler_table(samples // BLOCK_LEN, 0.125 / math.sqrt(samples))
    high = wave.astype(jnp.bfloat16)
    wave = np.stack([high, (wave - high.astype(np.float32)).astype(jnp.bfloat16)])
    return map_call(got, own, gram, solver, jnp.asarray(wave), groups, beams_local)


def lag_table(ref_ext, offset, lags):
    window = lax.dynamic_slice_in_dim(ref_ext, offset, BLOCK_LEN + LAGS, 1)
    span = BLOCK_LEN + LAGS
    tiled = jnp.tile(jnp.pad(window, ((0, 0), (0, 1))), (1, lags))[:, : lags * span]
    return tiled.reshape(2, lags, span)[:, :, LAGS:]


def times_conj(a, b):
    real = jnp.einsum("...t,lt->...l", a[..., 0, :], b[0], precision=HIGHEST) + jnp.einsum(
        "...t,lt->...l", a[..., 1, :], b[1], precision=HIGHEST
    )
    imag = jnp.einsum("...t,lt->...l", a[..., 1, :], b[0], precision=HIGHEST) - jnp.einsum(
        "...t,lt->...l", a[..., 0, :], b[1], precision=HIGHEST
    )
    return jnp.stack([real, imag], -2)


def plain_device(ref_signal, surveillance, steering):
    chan_count, tm_count = lax.axis_size("chan"), lax.axis_size("tm")
    length = surveillance.shape[2]
    beams = steering.shape[1]
    lags_local = LAGS // tm_count
    samples = length * tm_count
    local_blocks = length // BLOCK_LEN
    here = lax.axis_index("tm")

    w_real, w_imag = steering
    real = jnp.dot(w_real, surveillance[0], precision=HIGHEST) - jnp.dot(w_imag, surveillance[1], precision=HIGHEST)
    imag = jnp.dot(w_imag, surveillance[0], precision=HIGHEST) + jnp.dot(w_real, surveillance[1], precision=HIGHEST)
    beam = lax.psum_scatter(jnp.stack([real, imag], 1), "chan", scatter_dimension=0, tiled=True)
    ref_all = lax.all_gather(ref_signal, "tm", axis=1, tiled=True)
    ref_ext = jnp.pad(ref_all, ((0, 0), (LAGS, 0)))

    def beam_step(carry, q):
        offset = q * BLOCK_LEN
        table = lag_table(ref_ext, here * length + offset, LAGS)
        segment = lax.dynamic_slice_in_dim(beam, offset, BLOCK_LEN, 2)
        return carry, times_conj(segment, table)

    _, products = lax.scan(beam_step, None, jnp.arange(local_blocks, dtype=jnp.int32))
    cross = lax.psum(products[..., :TAPS].sum(0), "tm")
    got = lax.all_to_all(products, "tm", 3, 0, tiled=True)

    def own_step(gram, q):
        offset = q * BLOCK_LEN
        table = lag_table(ref_ext, offset, LAGS)
        taps = table[:, :TAPS].transpose(1, 0, 2)
        mine = lax.dynamic_slice_in_dim(table, here * lags_local, lags_local, 1)
        return gram + times_conj(taps, table[:, :TAPS]), times_conj(taps, mine)

    start = jnp.zeros((TAPS, 2, TAPS), jnp.float32)
    gram, own = lax.scan(own_step, start, jnp.arange(samples // BLOCK_LEN, dtype=jnp.int32))
    g_real, g_imag = gram[:, 0].T, gram[:, 1].T
    system = jnp.concatenate([jnp.concatenate([g_real, -g_imag], 1), jnp.concatenate([g_imag, g_real], 1)], 0)
    right = jnp.concatenate([cross[:, 0].T, cross[:, 1].T], 0)
    solved = jax.scipy.linalg.cho_solve((jnp.linalg.cholesky(system), True), right)
    b_real, b_imag = solved[:TAPS].T, solved[TAPS:].T
    mixing = jnp.concatenate([jnp.stack([b_real, b_imag], 1), jnp.stack([-b_imag, b_real], 1)], 2)
    stacked = jnp.concatenate([own[:, :, 0], own[:, :, 1]], 1)
    lagged = got - jnp.einsum("mck,qkl->qmcl", mixing, stacked, precision=HIGHEST)
    wave = jnp.asarray(doppler_table(samples // BLOCK_LEN, 0.125 / math.sqrt(samples)))
    wave = wave.reshape(2, samples // BLOCK_LEN, 2, DOPPLER)
    return jnp.einsum("qmcl,cqdk->mdlk", lagged, wave, precision=HIGHEST)


def on_device(ref_signal, surveillance, steering):
    chan_count, tm_count = lax.axis_size("chan"), lax.axis_size("tm")
    beams_local = steering.shape[1] // chan_count
    lags_local = LAGS // tm_count
    fills = (
        LANES % lags_local == 0
        and lags_local % (2 * SUBLANES) == 0
        and beams_local * lags_local == LANES * SUBLANES // 2
        and chan_count > 1
        and chan_count & (chan_count - 1) == 0
        and tm_count > 2
        and tm_count & (tm_count - 1) == 0
        and 2 * surveillance.shape[1] % LANES == 0
        and surveillance.shape[2] % (2 * BATCH * BLOCK_LEN) == 0
    )
    device = tiled_device if fills else plain_device
    return device(ref_signal, surveillance, steering)


def solution(mesh):
    placed = (P(None, "tm"), P(None, "chan", "tm"), P(None, None, "chan"))
    return jax.shard_map(
        on_device,
        mesh=mesh,
        in_specs=placed,
        out_specs=P("chan", None, "tm", None),
        check_vma=False,
    )
```

```python
import functools
import math

import jax
import jax.numpy as jnp
import numpy as np
from jax import lax
from jax.experimental import pallas as pl
from jax.experimental.pallas import tpu as pltpu
from jax.sharding import PartitionSpec as P

LAGS = 256
DOPPLER = 256
TAPS = 64
BLOCK_LEN = 256
LANES = 128
SUBLANES = 8
EDGE = 2

HIGHEST = lax.Precision.HIGHEST
VMEM_BYTES = 48 * 1024 * 1024


def params():
    return pltpu.CompilerParams(vmem_limit_bytes=VMEM_BYTES)


def cost(us):
    return pl.CostEstimate(flops=int(us * 1.15e9), bytes_accessed=0, transcendentals=0)


def halves(x):
    high = x.astype(jnp.bfloat16)
    return high, (x - high.astype(jnp.float32)).astype(jnp.bfloat16)


def thirds(x):
    high = x.astype(jnp.bfloat16)
    rest = x - high.astype(jnp.float32)
    return (high,) + halves(rest)


def dot_parts(a, b, across=False):
    rows = a[0].shape[0]
    by_size = {}
    for j, right in enumerate(b):
        left = a[: max(3 - j, 1)]
        left = left[0] if len(left) == 1 else jnp.concatenate(left, 0)
        contract = (((1,), (1 if across else 0,)), ((), ()))
        product = lax.dot_general(left, right, contract, preferred_element_type=jnp.float32)
        for i in range(product.shape[0] // rows):
            by_size.setdefault(i + j, []).append(product[i * rows : (i + 1) * rows])
    total = None
    for size in sorted(by_size, reverse=True):
        for term in by_size[size]:
            total = term if total is None else total + term
    return total


def dot_nt(a, b, precision=None):
    return lax.dot_general(
        a, b, (((1,), (1,)), ((), ())), precision=precision, preferred_element_type=jnp.float32
    )


def dot_split(a, b):
    (a_high, a_low), (b_high, b_low) = a, b
    left = jnp.concatenate([a_high, a_low], 1)
    right = jnp.concatenate([b_high, b_high], 0)
    return jnp.dot(left, right, preferred_element_type=jnp.float32) + jnp.dot(
        a_high, b_low, preferred_element_type=jnp.float32
    )


def row_sign(shape):
    rows = lax.broadcasted_iota(jnp.int32, shape, 0)
    return jnp.where(rows % SUBLANES < SUBLANES // 2, 1.0, -1.0).astype(jnp.float32)


def lane_sign(shape):
    lanes = lax.broadcasted_iota(jnp.int32, shape, 1)
    return jnp.where(lanes % LANES < LANES // 2, 1.0, -1.0).astype(jnp.float32)


def swap_groups(rows, groups):
    width = LANES // groups
    lane_group = lax.broadcasted_iota(jnp.int32, rows[0].shape, 1) // width
    outs = []
    for j in range(groups):
        out = rows[j]
        for i in range(groups):
            if i != j:
                moved = pltpu.roll(rows[i], (width * (i - j)) % LANES, 1)
                out = jnp.where(lane_group == i, moved, out)
        outs.append(out)
    return outs


COPIES = 4


def beam_kernel(
    chan_count, beams_local, w_hbm, s_hbm, ref_hbm, kept_ref, sent_ref, tiles_ref,
    w_ref, s_ref, ref_ref, w_sem, s_sem, ref_sem,
):
    me = lax.axis_index("chan")
    depth = s_hbm.shape[0] // COPIES
    w_copy = pltpu.make_async_copy(w_hbm, w_ref, w_sem)
    w_copy.start()
    ref_copy = pltpu.make_async_copy(ref_hbm, ref_ref, ref_sem)
    ref_copy.start()
    s_copies = []
    for n in range(COPIES):
        part = pl.ds(n * depth, depth)
        s_copies.append(pltpu.make_async_copy(s_hbm.at[part], s_ref.at[part], s_sem.at[n]))
        s_copies[n].start()
    half = SUBLANES // 2
    sub = lax.broadcasted_iota(jnp.int32, (SUBLANES, w_hbm.shape[2]), 0)
    top = sub < half
    w_copy.wait()
    rows = []
    for parity in range(2):
        for e in range(parity, chan_count, 2):
            base = (me ^ e) * beams_local
            for tile in range(beams_local // SUBLANES):
                start = pl.multiple_of(base + tile * SUBLANES, SUBLANES)
                wr = w_ref[0, pl.ds(start, SUBLANES), :]
                wi = w_ref[1, pl.ds(start, SUBLANES), :]
                wr_s = pltpu.roll(wr, half, 0)
                wi_s = pltpu.roll(wi, half, 0)
                first = [jnp.where(top, wr, wi_s), jnp.where(top, -wi, wr_s)]
                second = [jnp.where(top, wr_s, wi), jnp.where(top, -wi_s, wr)]
                rows.append(jnp.concatenate(first, 1))
                rows.append(jnp.concatenate(second, 1))
    weights = halves(jnp.concatenate(rows, 0))
    ref_copy.wait()
    for c in range(2):
        for n in range(tiles_ref.shape[1]):
            tiles_ref[c, n : n + 1, :] = ref_ref[c : c + 1, n * LANES : (n + 1) * LANES]
    for copy in s_copies:
        copy.wait()
    product = dot_parts(weights, thirds(s_ref[...]))
    mid = product.shape[0] // 2
    kept_ref[...] = product[:mid]
    sent_ref[...] = product[mid:]


def beam_call(steering, survey, ref, chan_count, beams_local):
    depth, length = survey.shape
    rows = chan_count * beams_local
    tiles = (2, length // LANES, LANES)
    out = jax.ShapeDtypeStruct((rows, length), jnp.float32)
    hbm, vmem = pl.BlockSpec(memory_space=pltpu.HBM), pl.BlockSpec(memory_space=pltpu.VMEM)
    return pl.pallas_call(
        functools.partial(beam_kernel, chan_count, beams_local),
        in_specs=[hbm] * 3,
        out_specs=[vmem] * 3,
        out_shape=[
            out,
            out,
            jax.ShapeDtypeStruct(tiles, jnp.float32),
        ],
        scratch_shapes=[
            pltpu.VMEM(steering.shape, jnp.float32),
            pltpu.VMEM(survey.shape, jnp.float32),
            pltpu.VMEM(ref.shape, jnp.float32),
            pltpu.SemaphoreType.DMA,
            pltpu.SemaphoreType.DMA((COPIES,)),
            pltpu.SemaphoreType.DMA,
        ],
        compiler_params=params(),
        cost_estimate=cost(2.2),
        name="beams",
    )(*(pltpu.with_memory_space_constraint(x, pltpu.HBM) for x in (steering, survey, ref)))


def sum_kernel(count, *refs):
    kept_ref, sent_ref = refs[-2:]
    for n in range(kept_ref.shape[0]):
        for offset, out_ref in ((0, kept_ref), (1, sent_ref)):
            total = refs[0][2 * n + offset]
            for ref in refs[1:count]:
                total = total + ref[2 * n + offset]
            out_ref[n] = total


def sum_call(parts):
    shape = (parts[0].shape[0] // 2,) + parts[0].shape[1:]
    out = jax.ShapeDtypeStruct(shape, jnp.float32)
    vmem = pl.BlockSpec(memory_space=pltpu.VMEM)
    return pl.pallas_call(
        functools.partial(sum_kernel, len(parts)),
        in_specs=[vmem] * len(parts),
        out_specs=[vmem, vmem],
        out_shape=[out, out],
        compiler_params=params(),
        cost_estimate=cost(0.1),
        name="halves_summed",
    )(*parts)


def join_kernel(first_ref, second_ref, *refs):
    out_ref = refs[-1]
    count = first_ref.shape[0]
    out_ref[:count] = first_ref[...]
    out_ref[count:] = second_ref[...]


def join_call(first, second, *after):
    vmem = pl.BlockSpec(memory_space=pltpu.VMEM)
    return pl.pallas_call(
        join_kernel,
        in_specs=[vmem, vmem] + [pl.BlockSpec(memory_space=pl.ANY)] * len(after),
        out_shape=jax.ShapeDtypeStruct((2 * first.shape[0],) + first.shape[1:], jnp.float32),
        compiler_params=params(),
        cost_estimate=cost(1.0),
        name="reference_joined",
    )(first, second, *after)


def spread_line(line, keep):
    for g in range(0, LANES, 2 * SUBLANES):
        tiled = jnp.broadcast_to(line, (2 * SUBLANES, line.shape[1]))
        for h, value in enumerate(halves(pltpu.roll(tiled, g, 1, stride=1, stride_axis=0)[:, LANES:])):
            keep(h, g, value)


def table_kernel(tiles_ref, out_ref):
    for c in range(2):
        line = jnp.concatenate([tiles_ref[c, n : n + 1, :] for n in range(tiles_ref.shape[1])], 1)

        def keep(h, g, value):
            out_ref[h, c, g : g + 2 * SUBLANES] = value

        spread_line(line, keep)


def table_call(tiles):
    shape = (2, 2, LANES, LANES * (tiles.shape[1] - 1))
    return pl.pallas_call(
        table_kernel,
        out_shape=jax.ShapeDtypeStruct(shape, jnp.bfloat16),
        compiler_params=params(),
        cost_estimate=cost(0.7),
        name="shifted_reference",
    )(tiles)


def first_kernel(tiles_ref, *refs):
    *round_refs, out_ref = refs
    me = lax.axis_index("tm")
    for c in range(2):
        tails = [ref[ref.shape[0] - 1, c, ref.shape[2] - EDGE :, :] for ref in round_refs]
        before = jnp.where(me % 2 == 1, tails[0], jnp.where(me > 0, tails[-1], 0.0))
        line = jnp.concatenate([before[n : n + 1] for n in range(EDGE)] + [tiles_ref[c, 0:1, :]], 1)

        def keep(h, g, value):
            out_ref[h, c, g : g + 2 * SUBLANES] = value

        spread_line(line, keep)


def first_call(tiles, rounds):
    return pl.pallas_call(
        first_kernel,
        out_shape=jax.ShapeDtypeStruct((2, 2, LANES, 2 * LANES), jnp.bfloat16),
        compiler_params=params(),
        cost_estimate=cost(0.1),
        name="shifted_first",
    )(tiles, *rounds)


def lag_kernel(groups, part_count, *refs):
    y_refs, refs = refs[:part_count], refs[part_count:]
    table_ref, first_ref, _, out_hbm, out_ref, out_sem = refs
    copies = []

    def table_tile(h, n):
        parts = []
        for c in range(2):
            known = first_ref.shape[3] // LANES
            ref, at = (first_ref, n) if n < known else (table_ref, n - known)
            parts.append(ref[h, c, :, at * LANES : (at + 1) * LANES])
        return jnp.concatenate(parts, 1)

    def send(start, count):
        part = (slice(None), pl.ds(start, count))
        copies.append(pltpu.make_async_copy(out_ref.at[part], out_hbm.at[part], out_sem.at[len(copies)]))
        copies[-1].start()

    y = y_refs[0][...]
    for y_ref in y_refs[1:]:
        y = y + y_ref[...]
    rows, length = y.shape
    blocks = length // BLOCK_LEN
    turned = jnp.concatenate(
        [pltpu.roll(y[r : r + SUBLANES], SUBLANES // 2, 0) for r in range(0, rows, SUBLANES)], 0
    )
    turned = turned * row_sign(turned.shape)
    y_parts, t_parts = thirds(y), thirds(turned)

    def half_block(q, b):
        cols = slice(q * BLOCK_LEN + b * LANES, q * BLOCK_LEN + (b + 1) * LANES)
        return [jnp.concatenate([x[:, cols], t[:, cols]], 1) for x, t in zip(y_parts, t_parts)]

    def products(stack, n, count):
        tiles = [jnp.concatenate([table_tile(h, n + i) for i in range(count)], 0) for h in range(2)]
        product = dot_parts([jnp.concatenate(part, 0) for part in zip(*stack)], tiles, True)
        return [product[i * rows : (i + 1) * rows] for i in range(len(stack))]

    taps_sum = None
    (far,) = products([half_block(0, 0)], 0, 1)
    for q in range(blocks):
        stack = [half_block(q, 0), half_block(q, 1)]
        if q + 1 < blocks:
            stack.append(half_block(q + 1, 0))
        first, second, *after = products(stack, 2 * q + 1, 2)
        product = jnp.concatenate([first[:, :LANES] + second[:, LANES:], second[:, :LANES] + far], 1)
        if after:
            far = after[0][:, LANES:]
        taps = product[:, :LANES]
        taps_sum = taps if taps_sum is None else taps_sum + taps
        for h in range(LAGS // LANES):
            lanes = slice(h * LANES, (h + 1) * LANES)
            tiles = [product[r : r + SUBLANES, lanes] for r in range(0, rows, SUBLANES)]
            for j, tile in enumerate(swap_groups(tiles, groups)):
                out_ref[h * groups + j, q] = tile
        if q + 1 == blocks // 2:
            send(0, blocks // 2)
    left = lax.broadcasted_iota(jnp.int32, (SUBLANES, LANES), 1) < TAPS
    for i in range(groups // 2):
        a = taps_sum[i * SUBLANES : (i + 1) * SUBLANES]
        other = i + groups // 2
        b = taps_sum[other * SUBLANES : (other + 1) * SUBLANES]
        tile = jnp.where(left, a, pltpu.roll(b, LANES - TAPS, 1))
        for owner in range(out_ref.shape[0]):
            out_ref[owner, blocks + i] = tile
    send(blocks // 2, blocks - blocks // 2 + groups // 2)
    for copy in copies:
        copy.wait()


def lag_call(ys, table, first, after, groups, owners):
    blocks = ys[0].shape[1] // BLOCK_LEN
    shape = (owners, blocks + groups // 2, SUBLANES, LANES)
    vmem = pl.BlockSpec(memory_space=pltpu.VMEM)
    return pl.pallas_call(
        functools.partial(lag_kernel, groups, len(ys)),
        in_specs=[vmem] * (len(ys) + 2) + [pl.BlockSpec(memory_space=pl.ANY)],
        out_specs=pl.BlockSpec(memory_space=pltpu.HBM),
        out_shape=jax.ShapeDtypeStruct(shape, jnp.float32),
        scratch_shapes=[
            pltpu.VMEM(shape, jnp.float32),
            pltpu.SemaphoreType.DMA((2,)),
        ],
        compiler_params=params(),
        cost_estimate=cost(2.1),
        name="lag_products",
    )(*ys, table, first, after)


BATCH = 4


def own_kernel(lags_local, *refs):
    *part_refs, _, out_ref, line_ref, tail_ref, span_ref, late_ref, taps_a, lags_a, taps_b, lags_b = refs
    me = lax.axis_index("tm")
    part_rows = part_refs[0].shape[2]
    owners = sum(part_ref.shape[0] for part_ref in part_refs)
    samples = owners * part_rows * LANES
    steps = samples // BLOCK_LEN // BATCH
    total_rows = span_ref.shape[1]
    block_rows = BLOCK_LEN // LANES

    span_ref[...] = jnp.zeros_like(span_ref)
    n = 0
    for part_ref in part_refs:
        for i in range(part_ref.shape[0]):
            block = lax.rem(me - (n // 2) * 2 + owners, owners) ^ (n % 2)
            span_ref[:, pl.ds(EDGE + block * part_rows, part_rows), :] = part_ref[i]
            n += 1
    late_rows = (me * lags_local) // LANES
    late_lanes = lax.rem(me * lags_local, LANES)
    turned = [pltpu.roll(span_ref[c], late_lanes, 1) for c in range(2)]
    before = [pltpu.roll(x, 1, 0) for x in turned]
    lanes = lax.broadcasted_iota(jnp.int32, (total_rows, LANES), 1)
    for c in range(2):
        late_ref[c] = pltpu.roll(jnp.where(lanes < late_lanes, before[c], turned[c]), late_rows, 0)

    def line_of(ref, c, first, count):
        return jnp.concatenate([ref[c, pl.ds(first + n, 1), :] for n in range(count)], 1)

    def shifted(line, by):
        tiled = jnp.broadcast_to(line, (2 * SUBLANES, line.shape[1]))
        return pltpu.roll(tiled, by, 1, stride=1, stride_axis=0)[:, LANES:]

    def keep(ref, row, parts):
        step = ref.shape[0] // len(parts)
        for n, part in enumerate(parts):
            ref[n * step + row : n * step + row + 2 * SUBLANES, :] = part

    def build(n, taps_ref, lags_ref):
        first = EDGE - 1 + n * BATCH * block_rows
        count = BATCH * block_rows + 1
        lines = [line_of(span_ref, c, first, count) for c in range(2)]
        for c in range(2):
            for g in range(0, TAPS, 2 * SUBLANES):
                keep(taps_ref, c * TAPS + g, thirds(shifted(lines[c], g)))
            late = line_of(late_ref, c, first, count)
            for g in range(0, lags_local, 2 * SUBLANES):
                keep(lags_ref, c * lags_local + g, halves(shifted(late, g)))
        pad = jnp.zeros((2 * SUBLANES - 2, BATCH * BLOCK_LEN), jnp.float32)
        keep(lags_ref, 2 * lags_local, halves(jnp.concatenate([line[:, LANES:] for line in lines] + [pad], 0)))

    turn = lane_sign((lags_local, LANES))

    def use(n, taps_ref, lags_ref):
        count = lags_ref.shape[0] // 2
        for b in range(BATCH):
            cols = slice(b * BLOCK_LEN, (b + 1) * BLOCK_LEN)
            product = dot_nt(lags_ref[:, cols], taps_ref[: 2 * LANES, cols])
            least = dot_nt(lags_ref[:count, cols], taps_ref[2 * LANES :, cols]) + product[count:, LANES:]
            product = product[:count, :LANES] + ((product[:count, LANES:] + product[count:, :LANES]) + least)
            by_real = product[:lags_local]
            by_imag = product[lags_local : 2 * lags_local]
            rows = pl.ds(pl.multiple_of((n * BATCH + b) * lags_local, lags_local), lags_local)
            for part, value in enumerate(thirds(by_real + turn * pltpu.roll(by_imag, TAPS, 1))):
                out_ref[part, rows, :] = value
            line_ref[...] += product[2 * lags_local : 2 * lags_local + SUBLANES]

    line_ref[...] = jnp.zeros_like(line_ref)
    build(0, taps_a, lags_a)

    def pair(m, carry):
        build(2 * m + 1, taps_b, lags_b)
        use(2 * m, taps_a, lags_a)
        build(jnp.minimum(2 * m + 2, steps - 1), taps_a, lags_a)
        use(2 * m + 1, taps_b, lags_b)
        return carry

    lax.fori_loop(0, steps // 2, pair, 0)
    tail = []
    for c in range(2):
        line = line_of(span_ref, c, EDGE + owners * part_rows - 1, 2)
        tail += [shifted(line, g) for g in range(0, TAPS, 2 * SUBLANES)]
    tail = jnp.concatenate(tail, 0)
    tail_ref[...] = dot_nt(tail, tail, HIGHEST)


def own_call(parts, lags_local, after):
    part_rows = parts[0].shape[2]
    span_rows = part_rows * sum(part.shape[0] for part in parts)
    rows = span_rows * LANES // BLOCK_LEN * lags_local
    held_rows = -(-(span_rows + 2 * EDGE) // SUBLANES) * SUBLANES
    width = BATCH * BLOCK_LEN
    taps = pltpu.VMEM((6 * TAPS, width), jnp.bfloat16)
    lags = pltpu.VMEM((4 * lags_local + 4 * SUBLANES, width), jnp.bfloat16)
    span = pltpu.VMEM((2, held_rows, LANES), jnp.float32)
    return pl.pallas_call(
        functools.partial(own_kernel, lags_local),
        in_specs=[pl.BlockSpec(memory_space=pltpu.VMEM)] * len(parts) + [pl.BlockSpec(memory_space=pl.ANY)],
        out_shape=[
            jax.ShapeDtypeStruct((3, rows, 2 * TAPS), jnp.bfloat16),
            jax.ShapeDtypeStruct((SUBLANES, 2 * TAPS), jnp.float32),
            jax.ShapeDtypeStruct((2 * TAPS, 2 * TAPS), jnp.float32),
        ],
        scratch_shapes=[span, span, taps, lags, taps, lags],
        compiler_params=params(),
        cost_estimate=cost(6.2),
        name="reference_products",
    )(*parts, after)


def as_factor(a):
    return jnp.concatenate([a, -lane_sign(a.shape) * pltpu.roll(a, a.shape[0], 1)], 0)


def solver_kernel(line_ref, tail_ref, gram_ref, solver_ref):
    total = line_ref[...]
    line = total[0:1] + lane_sign((1, LANES)) * pltpu.roll(total[1:2], TAPS, 1)
    low = lax.broadcasted_iota(jnp.int32, (1, LANES), 1) < TAPS
    line_r = jnp.where(low, line, 0.0)
    line_i = jnp.where(low, pltpu.roll(line, TAPS, 1), 0.0)
    cols = lax.broadcasted_iota(jnp.int32, (TAPS, TAPS), 1)
    rows = lax.broadcasted_iota(jnp.int32, (TAPS, TAPS), 0)
    above = cols > rows

    def upper(x):
        spread = pltpu.roll(jnp.broadcast_to(x, (TAPS, LANES)), 0, 1, stride=1, stride_axis=0)
        return spread[:, :TAPS]

    up_r = upper(line_r)
    up_i = jnp.where(above, upper(line_i), 0.0)
    strict_r = jnp.where(above, up_r, 0.0)
    diag_r = jnp.where(cols == rows, up_r, 0.0)
    tails = tail_ref[...]
    gram_r = strict_r + strict_r.T + diag_r - (tails[:TAPS, :TAPS] + tails[TAPS:, TAPS:])
    gram_i = up_i - up_i.T - (tails[:TAPS, TAPS:] - tails[TAPS:, :TAPS])
    gram = jnp.concatenate([gram_r, gram_i], 1)
    gram_factor = as_factor(gram)
    for part, value in enumerate(thirds(gram_factor)):
        gram_ref[part] = value
    gram_halves = halves(gram_factor)
    one = (
        lax.broadcasted_iota(jnp.int32, gram.shape, 0) == lax.broadcasted_iota(jnp.int32, gram.shape, 1)
    ).astype(jnp.float32)
    bound = jnp.max(jnp.sum(jnp.abs(gram), axis=1, keepdims=True), axis=0, keepdims=True)

    def again(state):
        count, left, _ = state
        return (count < 60) & (left > 1e-3)

    def newton(state):
        count, _, x = state
        x_halves = halves(x)
        seen = dot_split(x_halves, gram_halves)
        left = jnp.max(jnp.abs(seen - one))
        x = 2.0 * x - dot_split(halves(seen), halves(as_factor(x)))
        return count + 1, left, x

    start = (jnp.int32(0), jnp.float32(1.0), one * (1.0 / bound))
    _, _, inverse = lax.while_loop(again, newton, start)
    seen = jnp.dot(inverse, gram_factor, precision=HIGHEST, preferred_element_type=jnp.float32)
    inverse = inverse + jnp.dot(
        one - seen, as_factor(inverse), precision=HIGHEST, preferred_element_type=jnp.float32
    )
    for part, value in enumerate(thirds(as_factor(inverse))):
        solver_ref[part] = value


def solver_call(line, tail):
    return pl.pallas_call(
        solver_kernel,
        out_shape=[jax.ShapeDtypeStruct((3,) + tail.shape, jnp.bfloat16)] * 2,
        compiler_params=params(),
        cost_estimate=cost(2.0),
        name="gram_inverse",
    )(line, tail)


def doppler_table(block_count, scale):
    phase = (np.arange(block_count)[:, None] * np.arange(DOPPLER)[None, :] % DOPPLER) * (2.0 * math.pi / DOPPLER)
    cosine, sine = np.cos(phase), np.sin(phase)
    upper = np.concatenate([cosine, -sine], 1)
    lower = np.concatenate([sine, cosine], 1)
    return (np.concatenate([upper, lower], 0) * scale).astype(np.float32)


def map_kernel(groups, got_ref, own_ref, gram_ref, solver_ref, wave_ref, out_hbm, held_ref, out_ref, out_sem):
    owners, pieces = got_ref.shape[:2]
    blocks = pieces - groups // 2
    lags_local = LANES // groups
    total = owners * blocks
    left = lax.broadcasted_iota(jnp.int32, (SUBLANES, LANES), 1) < TAPS
    sign = row_sign((SUBLANES, LANES))
    rows = [None] * groups
    for i in range(groups // 2):
        tile = got_ref[0, blocks + i]
        for owner in range(1, owners):
            tile = tile + got_ref[owner, blocks + i]
        swapped = pltpu.roll(tile, TAPS, 1)
        for part, here, there in ((i, tile, swapped), (i + groups // 2, swapped, tile)):
            other = -sign * pltpu.roll(there, SUBLANES // 2, 0)
            rows[part] = jnp.where(left, here, other)
    cross = jnp.concatenate(rows, 0)

    def exact(x, ref):
        return dot_parts(thirds(x), [ref[part] for part in range(3)])

    taps = exact(cross, solver_ref)
    taps = taps + exact(cross - exact(taps, gram_ref), solver_ref)
    taps = thirds(taps)
    for q in range(0, total, 2 * groups):
        own = slice(q * lags_local, (q + 2 * groups) * lags_local)
        clutter = dot_parts(taps, [own_ref[part, own, :] for part in range(3)], True)
        for h in range(2):
            lanes = slice(h * LANES, (h + 1) * LANES)
            tiles = [clutter[r : r + SUBLANES, lanes] for r in range(0, groups * SUBLANES, SUBLANES)]
            for j, tile in enumerate(swap_groups(tiles, groups)):
                at = q + h * groups + j
                held_ref[at * SUBLANES : (at + 1) * SUBLANES, :] = got_ref[at // blocks, at % blocks] - tile
    half = SUBLANES // 2
    wave = (wave_ref[0], wave_ref[1])
    copies = []
    for g in range(half):
        parts = [held_ref[pl.ds(c * half + g, total, stride=SUBLANES), :] for c in range(2)]
        spectrum = dot_split(halves(jnp.concatenate(parts, 0).T), wave)
        for i in range(groups):
            for c in range(2):
                out_ref[i, g, c] = spectrum[i * lags_local : (i + 1) * lags_local, c * DOPPLER : (c + 1) * DOPPLER]
        part = (slice(None), pl.ds(g, 1))
        copies.append(pltpu.make_async_copy(out_ref.at[part], out_hbm.at[part], out_sem.at[g]))
        copies[-1].start()
    for copy in copies:
        copy.wait()


def map_call(got, own, gram, solver, wave, groups, beams_local):
    total = got.shape[0] * (got.shape[1] - groups // 2)
    lags_local = LANES // groups
    half = SUBLANES // 2
    shape = (beams_local // half, half, 2, lags_local, DOPPLER)
    out = pl.pallas_call(
        functools.partial(map_kernel, groups),
        in_specs=[pl.BlockSpec(memory_space=pltpu.VMEM)] * 5,
        out_specs=pl.BlockSpec(memory_space=pltpu.HBM),
        out_shape=jax.ShapeDtypeStruct(shape, jnp.float32),
        scratch_shapes=[
            pltpu.VMEM((total * SUBLANES, LANES), jnp.float32),
            pltpu.VMEM(shape, jnp.float32),
            pltpu.SemaphoreType.DMA((half,)),
        ],
        compiler_params=params(),
        cost_estimate=cost(2.5),
        name="range_doppler",
    )(got, own, gram, solver, wave)
    return out.reshape((beams_local,) + shape[2:])


def swap(x, axis, by):
    pairs = [(i, i ^ by) for i in range(lax.axis_size(axis))]
    return lax.ppermute(x, axis, pairs)


def tiled_device(ref_signal, surveillance, steering):
    chan_count, tm_count = lax.axis_size("chan"), lax.axis_size("tm")
    channels, length = surveillance.shape[1:]
    beams_local = steering.shape[1] // chan_count
    lags_local = LAGS // tm_count
    groups = LANES // lags_local
    samples = length * tm_count

    survey = surveillance.reshape(2 * channels, length)
    kept, moved, tiles = beam_call(steering, survey, ref_signal, chan_count, beams_local)
    near = swap(tiles[None], "tm", 1)
    shape = (chan_count // 2, 2 * beams_local, length)
    kept, got = kept.reshape(shape), swap(moved, "chan", 1).reshape(shape)
    by = 2
    while by < chan_count:
        kept, moved = sum_call([kept, got])
        got = swap(moved, "chan", by)
        by *= 2
    rounds = [near]
    joined = join_call(tiles[None], near, moved)
    while True:
        count = joined.shape[0]
        rounds.append(lax.ppermute(joined, "tm", [(i, (i + count) % tm_count) for i in range(tm_count)]))
        if count * 2 == tm_count:
            break
        joined = join_call(joined, rounds[-1])
    table = table_call(tiles)
    first = first_call(tiles, rounds[:2])
    pieces = lag_call([kept[0], got[0]], table, first, joined, groups, tm_count)
    got = lax.all_to_all(pieces, "tm", 0, 0, tiled=True)
    own, line, tail = own_call([tiles[None]] + rounds, lags_local, pieces)
    gram, solver = solver_call(line, tail)
    wave = doppler_table(samples // BLOCK_LEN, 0.125 / math.sqrt(samples))
    high = wave.astype(jnp.bfloat16)
    wave = np.stack([high, (wave - high.astype(np.float32)).astype(jnp.bfloat16)])
    return map_call(got, own, gram, solver, jnp.asarray(wave), groups, beams_local)


def lag_table(ref_ext, offset, lags):
    window = lax.dynamic_slice_in_dim(ref_ext, offset, BLOCK_LEN + LAGS, 1)
    span = BLOCK_LEN + LAGS
    tiled = jnp.tile(jnp.pad(window, ((0, 0), (0, 1))), (1, lags))[:, : lags * span]
    return tiled.reshape(2, lags, span)[:, :, LAGS:]


def times_conj(a, b):
    real = jnp.einsum("...t,lt->...l", a[..., 0, :], b[0], precision=HIGHEST) + jnp.einsum(
        "...t,lt->...l", a[..., 1, :], b[1], precision=HIGHEST
    )
    imag = jnp.einsum("...t,lt->...l", a[..., 1, :], b[0], precision=HIGHEST) - jnp.einsum(
        "...t,lt->...l", a[..., 0, :], b[1], precision=HIGHEST
    )
    return jnp.stack([real, imag], -2)


def plain_device(ref_signal, surveillance, steering):
    chan_count, tm_count = lax.axis_size("chan"), lax.axis_size("tm")
    length = surveillance.shape[2]
    beams = steering.shape[1]
    lags_local = LAGS // tm_count
    samples = length * tm_count
    local_blocks = length // BLOCK_LEN
    here = lax.axis_index("tm")

    w_real, w_imag = steering
    real = jnp.dot(w_real, surveillance[0], precision=HIGHEST) - jnp.dot(w_imag, surveillance[1], precision=HIGHEST)
    imag = jnp.dot(w_imag, surveillance[0], precision=HIGHEST) + jnp.dot(w_real, surveillance[1], precision=HIGHEST)
    beam = lax.psum_scatter(jnp.stack([real, imag], 1), "chan", scatter_dimension=0, tiled=True)
    ref_all = lax.all_gather(ref_signal, "tm", axis=1, tiled=True)
    ref_ext = jnp.pad(ref_all, ((0, 0), (LAGS, 0)))

    def beam_step(carry, q):
        offset = q * BLOCK_LEN
        table = lag_table(ref_ext, here * length + offset, LAGS)
        segment = lax.dynamic_slice_in_dim(beam, offset, BLOCK_LEN, 2)
        return carry, times_conj(segment, table)

    _, products = lax.scan(beam_step, None, jnp.arange(local_blocks, dtype=jnp.int32))
    cross = lax.psum(products[..., :TAPS].sum(0), "tm")
    got = lax.all_to_all(products, "tm", 3, 0, tiled=True)

    def own_step(gram, q):
        offset = q * BLOCK_LEN
        table = lag_table(ref_ext, offset, LAGS)
        taps = table[:, :TAPS].transpose(1, 0, 2)
        mine = lax.dynamic_slice_in_dim(table, here * lags_local, lags_local, 1)
        return gram + times_conj(taps, table[:, :TAPS]), times_conj(taps, mine)

    start = jnp.zeros((TAPS, 2, TAPS), jnp.float32)
    gram, own = lax.scan(own_step, start, jnp.arange(samples // BLOCK_LEN, dtype=jnp.int32))
    g_real, g_imag = gram[:, 0].T, gram[:, 1].T
    system = jnp.concatenate([jnp.concatenate([g_real, -g_imag], 1), jnp.concatenate([g_imag, g_real], 1)], 0)
    right = jnp.concatenate([cross[:, 0].T, cross[:, 1].T], 0)
    solved = jax.scipy.linalg.cho_solve((jnp.linalg.cholesky(system), True), right)
    b_real, b_imag = solved[:TAPS].T, solved[TAPS:].T
    mixing = jnp.concatenate([jnp.stack([b_real, b_imag], 1), jnp.stack([-b_imag, b_real], 1)], 2)
    stacked = jnp.concatenate([own[:, :, 0], own[:, :, 1]], 1)
    lagged = got - jnp.einsum("mck,qkl->qmcl", mixing, stacked, precision=HIGHEST)
    wave = jnp.asarray(doppler_table(samples // BLOCK_LEN, 0.125 / math.sqrt(samples)))
    wave = wave.reshape(2, samples // BLOCK_LEN, 2, DOPPLER)
    return jnp.einsum("qmcl,cqdk->mdlk", lagged, wave, precision=HIGHEST)


def on_device(ref_signal, surveillance, steering):
    chan_count, tm_count = lax.axis_size("chan"), lax.axis_size("tm")
    beams_local = steering.shape[1] // chan_count
    lags_local = LAGS // tm_count
    fills = (
        LANES % lags_local == 0
        and lags_local % (2 * SUBLANES) == 0
        and beams_local * lags_local == LANES * SUBLANES // 2
        and chan_count > 1
        and chan_count & (chan_count - 1) == 0
        and tm_count > 2
        and tm_count & (tm_count - 1) == 0
        and 2 * surveillance.shape[1] % LANES == 0
        and surveillance.shape[2] % (2 * BATCH * BLOCK_LEN) == 0
    )
    device = tiled_device if fills else plain_device
    return device(ref_signal, surveillance, steering)


def solution(mesh):
    placed = (P(None, "tm"), P(None, "chan", "tm"), P(None, None, "chan"))
    return jax.shard_map(
        on_device,
        mesh=mesh,
        in_specs=placed,
        out_specs=P("chan", None, "tm", None),
        check_vma=False,
    )
```

```python
import functools
import math

import jax
import jax.numpy as jnp
import numpy as np
from jax import lax
from jax.experimental import pallas as pl
from jax.experimental.pallas import tpu as pltpu
from jax.sharding import PartitionSpec as P

LAGS = 256
DOPPLER = 256
TAPS = 64
BLOCK_LEN = 256
LANES = 128
SUBLANES = 8
EDGE = 2

HIGHEST = lax.Precision.HIGHEST
VMEM_BYTES = 48 * 1024 * 1024


def params():
    return pltpu.CompilerParams(vmem_limit_bytes=VMEM_BYTES)


def cost(us):
    return pl.CostEstimate(flops=int(us * 1.15e9), bytes_accessed=0, transcendentals=0)


def halves(x):
    high = x.astype(jnp.bfloat16)
    return high, (x - high.astype(jnp.float32)).astype(jnp.bfloat16)


def thirds(x):
    high = x.astype(jnp.bfloat16)
    rest = x - high.astype(jnp.float32)
    return (high,) + halves(rest)


PART_PAIRS = ((2, 0), (1, 1), (0, 2), (1, 0), (0, 1), (0, 0))


def dot_parts(a, b, across=False):
    rows = a[0].shape[0]
    by_size = {}
    for j, right in enumerate(b):
        left = a[: max(3 - j, 1)]
        left = left[0] if len(left) == 1 else jnp.concatenate(left, 0)
        contract = (((1,), (1 if across else 0,)), ((), ()))
        product = lax.dot_general(left, right, contract, preferred_element_type=jnp.float32)
        for i in range(product.shape[0] // rows):
            by_size.setdefault(i + j, []).append(product[i * rows : (i + 1) * rows])
    total = None
    for size in sorted(by_size, reverse=True):
        for term in by_size[size]:
            total = term if total is None else total + term
    return total


def dot_nt(a, b, precision=None):
    return lax.dot_general(
        a, b, (((1,), (1,)), ((), ())), precision=precision, preferred_element_type=jnp.float32
    )


def dot_split(a, b):
    (a_high, a_low), (b_high, b_low) = a, b
    left = jnp.concatenate([a_high, a_low], 1)
    right = jnp.concatenate([b_high, b_high], 0)
    return jnp.dot(left, right, preferred_element_type=jnp.float32) + jnp.dot(
        a_high, b_low, preferred_element_type=jnp.float32
    )


def row_sign(shape):
    rows = lax.broadcasted_iota(jnp.int32, shape, 0)
    return jnp.where(rows % SUBLANES < SUBLANES // 2, 1.0, -1.0).astype(jnp.float32)


def lane_sign(shape):
    lanes = lax.broadcasted_iota(jnp.int32, shape, 1)
    return jnp.where(lanes % LANES < LANES // 2, 1.0, -1.0).astype(jnp.float32)


def swap_groups(rows, groups):
    width = LANES // groups
    lane_group = lax.broadcasted_iota(jnp.int32, rows[0].shape, 1) // width
    outs = []
    for j in range(groups):
        out = rows[j]
        for i in range(groups):
            if i != j:
                moved = pltpu.roll(rows[i], (width * (i - j)) % LANES, 1)
                out = jnp.where(lane_group == i, moved, out)
        outs.append(out)
    return outs


COPIES = 4


def beam_kernel(
    chan_count, beams_local, w_hbm, s_hbm, ref_hbm, kept_ref, sent_ref, tiles_ref,
    w_ref, s_ref, ref_ref, w_sem, s_sem, ref_sem,
):
    me = lax.axis_index("chan")
    depth = s_hbm.shape[0] // COPIES
    w_copy = pltpu.make_async_copy(w_hbm, w_ref, w_sem)
    w_copy.start()
    ref_copy = pltpu.make_async_copy(ref_hbm, ref_ref, ref_sem)
    ref_copy.start()
    s_copies = []
    for n in range(COPIES):
        part = pl.ds(n * depth, depth)
        s_copies.append(pltpu.make_async_copy(s_hbm.at[part], s_ref.at[part], s_sem.at[n]))
        s_copies[n].start()
    half = SUBLANES // 2
    sub = lax.broadcasted_iota(jnp.int32, (SUBLANES, w_hbm.shape[2]), 0)
    top = sub < half
    w_copy.wait()
    rows = []
    for parity in range(2):
        for e in range(parity, chan_count, 2):
            base = (me ^ e) * beams_local
            for tile in range(beams_local // SUBLANES):
                start = pl.multiple_of(base + tile * SUBLANES, SUBLANES)
                wr = w_ref[0, pl.ds(start, SUBLANES), :]
                wi = w_ref[1, pl.ds(start, SUBLANES), :]
                wr_s = pltpu.roll(wr, half, 0)
                wi_s = pltpu.roll(wi, half, 0)
                first = [jnp.where(top, wr, wi_s), jnp.where(top, -wi, wr_s)]
                second = [jnp.where(top, wr_s, wi), jnp.where(top, -wi_s, wr)]
                rows.append(jnp.concatenate(first, 1))
                rows.append(jnp.concatenate(second, 1))
    weights = halves(jnp.concatenate(rows, 0))
    ref_copy.wait()
    for c in range(2):
        for n in range(tiles_ref.shape[1]):
            tiles_ref[c, n : n + 1, :] = ref_ref[c : c + 1, n * LANES : (n + 1) * LANES]
    for copy in s_copies:
        copy.wait()
    product = dot_parts(weights, thirds(s_ref[...]))
    mid = product.shape[0] // 2
    kept_ref[...] = product[:mid]
    sent_ref[...] = product[mid:]


def beam_call(steering, survey, ref, chan_count, beams_local):
    depth, length = survey.shape
    rows = chan_count * beams_local
    tiles = (2, length // LANES, LANES)
    out = jax.ShapeDtypeStruct((rows, length), jnp.float32)
    hbm, vmem = pl.BlockSpec(memory_space=pltpu.HBM), pl.BlockSpec(memory_space=pltpu.VMEM)
    return pl.pallas_call(
        functools.partial(beam_kernel, chan_count, beams_local),
        in_specs=[hbm] * 3,
        out_specs=[vmem] * 3,
        out_shape=[
            out,
            out,
            jax.ShapeDtypeStruct(tiles, jnp.float32),
        ],
        scratch_shapes=[
            pltpu.VMEM(steering.shape, jnp.float32),
            pltpu.VMEM(survey.shape, jnp.float32),
            pltpu.VMEM(ref.shape, jnp.float32),
            pltpu.SemaphoreType.DMA,
            pltpu.SemaphoreType.DMA((COPIES,)),
            pltpu.SemaphoreType.DMA,
        ],
        compiler_params=params(),
        cost_estimate=cost(2.2),
        name="beams",
    )(*(pltpu.with_memory_space_constraint(x, pltpu.HBM) for x in (steering, survey, ref)))


def sum_kernel(count, *refs):
    kept_ref, sent_ref = refs[-2:]
    for n in range(kept_ref.shape[0]):
        for offset, out_ref in ((0, kept_ref), (1, sent_ref)):
            total = refs[0][2 * n + offset]
            for ref in refs[1:count]:
                total = total + ref[2 * n + offset]
            out_ref[n] = total


def sum_call(parts):
    shape = (parts[0].shape[0] // 2,) + parts[0].shape[1:]
    out = jax.ShapeDtypeStruct(shape, jnp.float32)
    vmem = pl.BlockSpec(memory_space=pltpu.VMEM)
    return pl.pallas_call(
        functools.partial(sum_kernel, len(parts)),
        in_specs=[vmem] * len(parts),
        out_specs=[vmem, vmem],
        out_shape=[out, out],
        compiler_params=params(),
        cost_estimate=cost(0.1),
        name="halves_summed",
    )(*parts)


def join_kernel(first_ref, second_ref, *refs):
    out_ref = refs[-1]
    count = first_ref.shape[0]
    out_ref[:count] = first_ref[...]
    out_ref[count:] = second_ref[...]


def join_call(first, second, *after):
    vmem = pl.BlockSpec(memory_space=pltpu.VMEM)
    return pl.pallas_call(
        join_kernel,
        in_specs=[vmem, vmem] + [pl.BlockSpec(memory_space=pl.ANY)] * len(after),
        out_shape=jax.ShapeDtypeStruct((2 * first.shape[0],) + first.shape[1:], jnp.float32),
        compiler_params=params(),
        cost_estimate=cost(1.0),
        name="reference_joined",
    )(first, second, *after)


def spread_line(line, keep):
    for g in range(0, LANES, 2 * SUBLANES):
        tiled = jnp.broadcast_to(line, (2 * SUBLANES, line.shape[1]))
        for h, value in enumerate(halves(pltpu.roll(tiled, g, 1, stride=1, stride_axis=0)[:, LANES:])):
            keep(h, g, value)


def table_kernel(tiles_ref, out_ref):
    for c in range(2):
        line = jnp.concatenate([tiles_ref[c, n : n + 1, :] for n in range(tiles_ref.shape[1])], 1)

        def keep(h, g, value):
            out_ref[h, c, g : g + 2 * SUBLANES] = value

        spread_line(line, keep)


def table_call(tiles):
    shape = (2, 2, LANES, LANES * (tiles.shape[1] - 1))
    return pl.pallas_call(
        table_kernel,
        out_shape=jax.ShapeDtypeStruct(shape, jnp.bfloat16),
        compiler_params=params(),
        cost_estimate=cost(0.7),
        name="shifted_reference",
    )(tiles)


def first_kernel(tiles_ref, *refs):
    *round_refs, out_ref = refs
    me = lax.axis_index("tm")
    for c in range(2):
        tails = [ref[ref.shape[0] - 1, c, ref.shape[2] - EDGE :, :] for ref in round_refs]
        before = jnp.where(me % 2 == 1, tails[0], jnp.where(me > 0, tails[-1], 0.0))
        line = jnp.concatenate([before[n : n + 1] for n in range(EDGE)] + [tiles_ref[c, 0:1, :]], 1)

        def keep(h, g, value):
            out_ref[h, c, g : g + 2 * SUBLANES] = value

        spread_line(line, keep)


def first_call(tiles, rounds):
    return pl.pallas_call(
        first_kernel,
        out_shape=jax.ShapeDtypeStruct((2, 2, LANES, 2 * LANES), jnp.bfloat16),
        compiler_params=params(),
        cost_estimate=cost(0.1),
        name="shifted_first",
    )(tiles, *rounds)


def lag_kernel(groups, part_count, *refs):
    y_refs, refs = refs[:part_count], refs[part_count:]
    table_ref, first_ref, _, out_hbm, out_ref, out_sem = refs
    copies = []

    def table_tile(h, n):
        parts = []
        for c in range(2):
            known = first_ref.shape[3] // LANES
            ref, at = (first_ref, n) if n < known else (table_ref, n - known)
            parts.append(ref[h, c, :, at * LANES : (at + 1) * LANES])
        return jnp.concatenate(parts, 1)

    def send(start, count):
        part = (slice(None), pl.ds(start, count))
        copies.append(pltpu.make_async_copy(out_ref.at[part], out_hbm.at[part], out_sem.at[len(copies)]))
        copies[-1].start()

    y = y_refs[0][...]
    for y_ref in y_refs[1:]:
        y = y + y_ref[...]
    rows, length = y.shape
    blocks = length // BLOCK_LEN
    turned = jnp.concatenate(
        [pltpu.roll(y[r : r + SUBLANES], SUBLANES // 2, 0) for r in range(0, rows, SUBLANES)], 0
    )
    turned = turned * row_sign(turned.shape)
    y_parts, t_parts = thirds(y), thirds(turned)

    def half_block(q, b):
        cols = slice(q * BLOCK_LEN + b * LANES, q * BLOCK_LEN + (b + 1) * LANES)
        return [jnp.concatenate([x[:, cols], t[:, cols]], 1) for x, t in zip(y_parts, t_parts)]

    def products(stack, n, count):
        tiles = [jnp.concatenate([table_tile(h, n + i) for i in range(count)], 0) for h in range(2)]
        product = dot_parts([jnp.concatenate(part, 0) for part in zip(*stack)], tiles, True)
        return [product[i * rows : (i + 1) * rows] for i in range(len(stack))]

    taps_sum = None
    (far,) = products([half_block(0, 0)], 0, 1)
    for q in range(blocks):
        stack = [half_block(q, 0), half_block(q, 1)]
        if q + 1 < blocks:
            stack.append(half_block(q + 1, 0))
        first, second, *after = products(stack, 2 * q + 1, 2)
        product = jnp.concatenate([first[:, :LANES] + second[:, LANES:], second[:, :LANES] + far], 1)
        if after:
            far = after[0][:, LANES:]
        taps = product[:, :LANES]
        taps_sum = taps if taps_sum is None else taps_sum + taps
        for h in range(LAGS // LANES):
            lanes = slice(h * LANES, (h + 1) * LANES)
            tiles = [product[r : r + SUBLANES, lanes] for r in range(0, rows, SUBLANES)]
            for j, tile in enumerate(swap_groups(tiles, groups)):
                out_ref[h * groups + j, q] = tile
        if q + 1 == blocks // 2:
            send(0, blocks // 2)
    left = lax.broadcasted_iota(jnp.int32, (SUBLANES, LANES), 1) < TAPS
    for i in range(groups // 2):
        a = taps_sum[i * SUBLANES : (i + 1) * SUBLANES]
        other = i + groups // 2
        b = taps_sum[other * SUBLANES : (other + 1) * SUBLANES]
        tile = jnp.where(left, a, pltpu.roll(b, LANES - TAPS, 1))
        for owner in range(out_ref.shape[0]):
            out_ref[owner, blocks + i] = tile
    send(blocks // 2, blocks - blocks // 2 + groups // 2)
    for copy in copies:
        copy.wait()


def lag_call(ys, table, first, after, groups, owners):
    blocks = ys[0].shape[1] // BLOCK_LEN
    shape = (owners, blocks + groups // 2, SUBLANES, LANES)
    vmem = pl.BlockSpec(memory_space=pltpu.VMEM)
    return pl.pallas_call(
        functools.partial(lag_kernel, groups, len(ys)),
        in_specs=[vmem] * (len(ys) + 2) + [pl.BlockSpec(memory_space=pl.ANY)],
        out_specs=pl.BlockSpec(memory_space=pltpu.HBM),
        out_shape=jax.ShapeDtypeStruct(shape, jnp.float32),
        scratch_shapes=[
            pltpu.VMEM(shape, jnp.float32),
            pltpu.SemaphoreType.DMA((2,)),
        ],
        compiler_params=params(),
        cost_estimate=cost(2.1),
        name="lag_products",
    )(*ys, table, first, after)


BATCH = 4


def own_kernel(lags_local, *refs):
    *part_refs, _, out_ref, line_ref, tail_ref, span_ref, late_ref, taps_a, lags_a, taps_b, lags_b = refs
    me = lax.axis_index("tm")
    part_rows = part_refs[0].shape[2]
    owners = sum(part_ref.shape[0] for part_ref in part_refs)
    samples = owners * part_rows * LANES
    steps = samples // BLOCK_LEN // BATCH
    total_rows = span_ref.shape[1]
    block_rows = BLOCK_LEN // LANES

    span_ref[...] = jnp.zeros_like(span_ref)
    n = 0
    for part_ref in part_refs:
        for i in range(part_ref.shape[0]):
            block = lax.rem(me - (n // 2) * 2 + owners, owners) ^ (n % 2)
            span_ref[:, pl.ds(EDGE + block * part_rows, part_rows), :] = part_ref[i]
            n += 1
    late_rows = (me * lags_local) // LANES
    late_lanes = lax.rem(me * lags_local, LANES)
    turned = [pltpu.roll(span_ref[c], late_lanes, 1) for c in range(2)]
    before = [pltpu.roll(x, 1, 0) for x in turned]
    lanes = lax.broadcasted_iota(jnp.int32, (total_rows, LANES), 1)
    for c in range(2):
        late_ref[c] = pltpu.roll(jnp.where(lanes < late_lanes, before[c], turned[c]), late_rows, 0)

    def line_of(ref, c, first, count):
        return jnp.concatenate([ref[c, pl.ds(first + n, 1), :] for n in range(count)], 1)

    def shifted(line, by):
        tiled = jnp.broadcast_to(line, (2 * SUBLANES, line.shape[1]))
        return pltpu.roll(tiled, by, 1, stride=1, stride_axis=0)[:, LANES:]

    def keep(ref, row, parts):
        step = ref.shape[0] // len(parts)
        for n, part in enumerate(parts):
            ref[n * step + row : n * step + row + 2 * SUBLANES, :] = part

    def build(n, taps_ref, lags_ref):
        first = EDGE - 1 + n * BATCH * block_rows
        count = BATCH * block_rows + 1
        lines = [line_of(span_ref, c, first, count) for c in range(2)]
        for c in range(2):
            for g in range(0, TAPS, 2 * SUBLANES):
                keep(taps_ref, c * TAPS + g, thirds(shifted(lines[c], g)))
            late = line_of(late_ref, c, first, count)
            for g in range(0, lags_local, 2 * SUBLANES):
                keep(lags_ref, c * lags_local + g, halves(shifted(late, g)))
        pad = jnp.zeros((2 * SUBLANES - 2, BATCH * BLOCK_LEN), jnp.float32)
        keep(lags_ref, 2 * lags_local, halves(jnp.concatenate([line[:, LANES:] for line in lines] + [pad], 0)))

    turn = lane_sign((lags_local, LANES))

    def use(n, taps_ref, lags_ref):
        count = lags_ref.shape[0] // 2
        for b in range(BATCH):
            cols = slice(b * BLOCK_LEN, (b + 1) * BLOCK_LEN)
            product = dot_nt(lags_ref[:, cols], taps_ref[: 2 * LANES, cols])
            least = dot_nt(lags_ref[:count, cols], taps_ref[2 * LANES :, cols]) + product[count:, LANES:]
            product = product[:count, :LANES] + ((product[:count, LANES:] + product[count:, :LANES]) + least)
            by_real = product[:lags_local]
            by_imag = product[lags_local : 2 * lags_local]
            rows = pl.ds(pl.multiple_of((n * BATCH + b) * lags_local, lags_local), lags_local)
            for part, value in enumerate(thirds(by_real + turn * pltpu.roll(by_imag, TAPS, 1))):
                out_ref[part, rows, :] = value
            line_ref[...] += product[2 * lags_local : 2 * lags_local + SUBLANES]

    line_ref[...] = jnp.zeros_like(line_ref)
    build(0, taps_a, lags_a)

    def pair(m, carry):
        build(2 * m + 1, taps_b, lags_b)
        use(2 * m, taps_a, lags_a)
        build(jnp.minimum(2 * m + 2, steps - 1), taps_a, lags_a)
        use(2 * m + 1, taps_b, lags_b)
        return carry

    lax.fori_loop(0, steps // 2, pair, 0)
    tail = []
    for c in range(2):
        line = line_of(span_ref, c, EDGE + owners * part_rows - 1, 2)
        tail += [shifted(line, g) for g in range(0, TAPS, 2 * SUBLANES)]
    tail = jnp.concatenate(tail, 0)
    tail_ref[...] = dot_nt(tail, tail, HIGHEST)


def own_call(parts, lags_local, after):
    part_rows = parts[0].shape[2]
    span_rows = part_rows * sum(part.shape[0] for part in parts)
    rows = span_rows * LANES // BLOCK_LEN * lags_local
    held_rows = -(-(span_rows + 2 * EDGE) // SUBLANES) * SUBLANES
    width = BATCH * BLOCK_LEN
    taps = pltpu.VMEM((6 * TAPS, width), jnp.bfloat16)
    lags = pltpu.VMEM((4 * lags_local + 4 * SUBLANES, width), jnp.bfloat16)
    span = pltpu.VMEM((2, held_rows, LANES), jnp.float32)
    return pl.pallas_call(
        functools.partial(own_kernel, lags_local),
        in_specs=[pl.BlockSpec(memory_space=pltpu.VMEM)] * len(parts) + [pl.BlockSpec(memory_space=pl.ANY)],
        out_shape=[
            jax.ShapeDtypeStruct((3, rows, 2 * TAPS), jnp.bfloat16),
            jax.ShapeDtypeStruct((SUBLANES, 2 * TAPS), jnp.float32),
            jax.ShapeDtypeStruct((2 * TAPS, 2 * TAPS), jnp.float32),
        ],
        scratch_shapes=[span, span, taps, lags, taps, lags],
        compiler_params=params(),
        cost_estimate=cost(6.2),
        name="reference_products",
    )(*parts, after)


def as_factor(a):
    return jnp.concatenate([a, -lane_sign(a.shape) * pltpu.roll(a, a.shape[0], 1)], 0)


def solver_kernel(line_ref, tail_ref, gram_ref, solver_ref):
    total = line_ref[...]
    line = total[0:1] + lane_sign((1, LANES)) * pltpu.roll(total[1:2], TAPS, 1)
    low = lax.broadcasted_iota(jnp.int32, (1, LANES), 1) < TAPS
    line_r = jnp.where(low, line, 0.0)
    line_i = jnp.where(low, pltpu.roll(line, TAPS, 1), 0.0)
    cols = lax.broadcasted_iota(jnp.int32, (TAPS, TAPS), 1)
    rows = lax.broadcasted_iota(jnp.int32, (TAPS, TAPS), 0)
    above = cols > rows

    def stack(ref, value):
        parts = thirds(value)
        for n, (_, part) in enumerate(PART_PAIRS):
            ref[n * value.shape[0] : (n + 1) * value.shape[0], :] = parts[part]

    def upper(x):
        spread = pltpu.roll(jnp.broadcast_to(x, (TAPS, LANES)), 0, 1, stride=1, stride_axis=0)
        return spread[:, :TAPS]

    up_r = upper(line_r)
    up_i = jnp.where(above, upper(line_i), 0.0)
    strict_r = jnp.where(above, up_r, 0.0)
    diag_r = jnp.where(cols == rows, up_r, 0.0)
    tails = tail_ref[...]
    gram_r = strict_r + strict_r.T + diag_r - (tails[:TAPS, :TAPS] + tails[TAPS:, TAPS:])
    gram_i = up_i - up_i.T - (tails[:TAPS, TAPS:] - tails[TAPS:, :TAPS])
    gram = jnp.concatenate([gram_r, gram_i], 1)
    gram_factor = as_factor(gram)
    stack(gram_ref, gram_factor)
    gram_halves = halves(gram_factor)
    one = (
        lax.broadcasted_iota(jnp.int32, gram.shape, 0) == lax.broadcasted_iota(jnp.int32, gram.shape, 1)
    ).astype(jnp.float32)
    bound = jnp.max(jnp.sum(jnp.abs(gram), axis=1, keepdims=True), axis=0, keepdims=True)

    def again(state):
        count, left, _ = state
        return (count < 60) & (left > 1e-3)

    def newton(state):
        count, _, x = state
        x_halves = halves(x)
        seen = dot_split(x_halves, gram_halves)
        left = jnp.max(jnp.abs(seen - one))
        x = 2.0 * x - dot_split(halves(seen), halves(as_factor(x)))
        return count + 1, left, x

    start = (jnp.int32(0), jnp.float32(1.0), one * (1.0 / bound))
    _, _, inverse = lax.while_loop(again, newton, start)
    seen = jnp.dot(inverse, gram_factor, precision=HIGHEST, preferred_element_type=jnp.float32)
    inverse = inverse + jnp.dot(
        one - seen, as_factor(inverse), precision=HIGHEST, preferred_element_type=jnp.float32
    )
    stack(solver_ref, as_factor(inverse))


def solver_call(line, tail):
    return pl.pallas_call(
        solver_kernel,
        out_shape=[jax.ShapeDtypeStruct((len(PART_PAIRS) * tail.shape[0], tail.shape[1]), jnp.bfloat16)] * 2,
        compiler_params=params(),
        cost_estimate=cost(2.0),
        name="gram_inverse",
    )(line, tail)


def doppler_table(block_count, scale):
    phase = (np.arange(block_count)[:, None] * np.arange(DOPPLER)[None, :] % DOPPLER) * (2.0 * math.pi / DOPPLER)
    cosine, sine = np.cos(phase), np.sin(phase)
    upper = np.concatenate([cosine, -sine], 1)
    lower = np.concatenate([sine, cosine], 1)
    return (np.concatenate([upper, lower], 0) * scale).astype(np.float32)


def map_kernel(groups, got_ref, own_ref, gram_ref, solver_ref, wave_ref, out_hbm, held_ref, out_ref, out_sem):
    owners, pieces = got_ref.shape[:2]
    blocks = pieces - groups // 2
    lags_local = LANES // groups
    total = owners * blocks
    left = lax.broadcasted_iota(jnp.int32, (SUBLANES, LANES), 1) < TAPS
    sign = row_sign((SUBLANES, LANES))
    rows = [None] * groups
    for i in range(groups // 2):
        tile = got_ref[0, blocks + i]
        for owner in range(1, owners):
            tile = tile + got_ref[owner, blocks + i]
        swapped = pltpu.roll(tile, TAPS, 1)
        for part, here, there in ((i, tile, swapped), (i + groups // 2, swapped, tile)):
            other = -sign * pltpu.roll(there, SUBLANES // 2, 0)
            rows[part] = jnp.where(left, here, other)
    cross = jnp.concatenate(rows, 0)

    def exact(x, ref):
        parts = thirds(x)
        return jnp.dot(
            jnp.concatenate([parts[part] for part, _ in PART_PAIRS], 1), ref[...], preferred_element_type=jnp.float32
        )

    taps = exact(cross, solver_ref)
    taps = taps + exact(cross - exact(taps, gram_ref), solver_ref)
    taps = thirds(taps)
    for q in range(0, total, 2 * groups):
        own = slice(q * lags_local, (q + 2 * groups) * lags_local)
        clutter = dot_parts(taps, [own_ref[part, own, :] for part in range(3)], True)
        for h in range(2):
            lanes = slice(h * LANES, (h + 1) * LANES)
            tiles = [clutter[r : r + SUBLANES, lanes] for r in range(0, groups * SUBLANES, SUBLANES)]
            for j, tile in enumerate(swap_groups(tiles, groups)):
                at = q + h * groups + j
                held_ref[at * SUBLANES : (at + 1) * SUBLANES, :] = got_ref[at // blocks, at % blocks] - tile
    half = SUBLANES // 2
    wave = (wave_ref[0], wave_ref[1])
    copies = []
    for g in range(half):
        parts = [held_ref[pl.ds(c * half + g, total, stride=SUBLANES), :] for c in range(2)]
        spectrum = dot_split(halves(jnp.concatenate(parts, 0).T), wave)
        for i in range(groups):
            for c in range(2):
                out_ref[i, g, c] = spectrum[i * lags_local : (i + 1) * lags_local, c * DOPPLER : (c + 1) * DOPPLER]
        part = (slice(None), pl.ds(g, 1))
        copies.append(pltpu.make_async_copy(out_ref.at[part], out_hbm.at[part], out_sem.at[g]))
        copies[-1].start()
    for copy in copies:
        copy.wait()


def map_call(got, own, gram, solver, wave, groups, beams_local):
    total = got.shape[0] * (got.shape[1] - groups // 2)
    lags_local = LANES // groups
    half = SUBLANES // 2
    shape = (beams_local // half, half, 2, lags_local, DOPPLER)
    out = pl.pallas_call(
        functools.partial(map_kernel, groups),
        in_specs=[pl.BlockSpec(memory_space=pltpu.VMEM)] * 5,
        out_specs=pl.BlockSpec(memory_space=pltpu.HBM),
        out_shape=jax.ShapeDtypeStruct(shape, jnp.float32),
        scratch_shapes=[
            pltpu.VMEM((total * SUBLANES, LANES), jnp.float32),
            pltpu.VMEM(shape, jnp.float32),
            pltpu.SemaphoreType.DMA((half,)),
        ],
        compiler_params=params(),
        cost_estimate=cost(2.5),
        name="range_doppler",
    )(got, own, gram, solver, wave)
    return out.reshape((beams_local,) + shape[2:])


def swap(x, axis, by):
    pairs = [(i, i ^ by) for i in range(lax.axis_size(axis))]
    return lax.ppermute(x, axis, pairs)


def tiled_device(ref_signal, surveillance, steering):
    chan_count, tm_count = lax.axis_size("chan"), lax.axis_size("tm")
    channels, length = surveillance.shape[1:]
    beams_local = steering.shape[1] // chan_count
    lags_local = LAGS // tm_count
    groups = LANES // lags_local
    samples = length * tm_count

    survey = surveillance.reshape(2 * channels, length)
    kept, moved, tiles = beam_call(steering, survey, ref_signal, chan_count, beams_local)
    near = swap(tiles[None], "tm", 1)
    shape = (chan_count // 2, 2 * beams_local, length)
    kept, got = kept.reshape(shape), swap(moved, "chan", 1).reshape(shape)
    by = 2
    while by < chan_count:
        kept, moved = sum_call([kept, got])
        got = swap(moved, "chan", by)
        by *= 2
    rounds = [near]
    joined = join_call(tiles[None], near, moved)
    while True:
        count = joined.shape[0]
        rounds.append(lax.ppermute(joined, "tm", [(i, (i + count) % tm_count) for i in range(tm_count)]))
        if count * 2 == tm_count:
            break
        joined = join_call(joined, rounds[-1])
    table = table_call(tiles)
    first = first_call(tiles, rounds[:2])
    pieces = lag_call([kept[0], got[0]], table, first, joined, groups, tm_count)
    got = lax.all_to_all(pieces, "tm", 0, 0, tiled=True)
    own, line, tail = own_call([tiles[None]] + rounds, lags_local, pieces)
    gram, solver = solver_call(line, tail)
    wave = doppler_table(samples // BLOCK_LEN, 0.125 / math.sqrt(samples))
    high = wave.astype(jnp.bfloat16)
    wave = np.stack([high, (wave - high.astype(np.float32)).astype(jnp.bfloat16)])
    return map_call(got, own, gram, solver, jnp.asarray(wave), groups, beams_local)


def lag_table(ref_ext, offset, lags):
    window = lax.dynamic_slice_in_dim(ref_ext, offset, BLOCK_LEN + LAGS, 1)
    span = BLOCK_LEN + LAGS
    tiled = jnp.tile(jnp.pad(window, ((0, 0), (0, 1))), (1, lags))[:, : lags * span]
    return tiled.reshape(2, lags, span)[:, :, LAGS:]


def times_conj(a, b):
    real = jnp.einsum("...t,lt->...l", a[..., 0, :], b[0], precision=HIGHEST) + jnp.einsum(
        "...t,lt->...l", a[..., 1, :], b[1], precision=HIGHEST
    )
    imag = jnp.einsum("...t,lt->...l", a[..., 1, :], b[0], precision=HIGHEST) - jnp.einsum(
        "...t,lt->...l", a[..., 0, :], b[1], precision=HIGHEST
    )
    return jnp.stack([real, imag], -2)


def plain_device(ref_signal, surveillance, steering):
    chan_count, tm_count = lax.axis_size("chan"), lax.axis_size("tm")
    length = surveillance.shape[2]
    beams = steering.shape[1]
    lags_local = LAGS // tm_count
    samples = length * tm_count
    local_blocks = length // BLOCK_LEN
    here = lax.axis_index("tm")

    w_real, w_imag = steering
    real = jnp.dot(w_real, surveillance[0], precision=HIGHEST) - jnp.dot(w_imag, surveillance[1], precision=HIGHEST)
    imag = jnp.dot(w_imag, surveillance[0], precision=HIGHEST) + jnp.dot(w_real, surveillance[1], precision=HIGHEST)
    beam = lax.psum_scatter(jnp.stack([real, imag], 1), "chan", scatter_dimension=0, tiled=True)
    ref_all = lax.all_gather(ref_signal, "tm", axis=1, tiled=True)
    ref_ext = jnp.pad(ref_all, ((0, 0), (LAGS, 0)))

    def beam_step(carry, q):
        offset = q * BLOCK_LEN
        table = lag_table(ref_ext, here * length + offset, LAGS)
        segment = lax.dynamic_slice_in_dim(beam, offset, BLOCK_LEN, 2)
        return carry, times_conj(segment, table)

    _, products = lax.scan(beam_step, None, jnp.arange(local_blocks, dtype=jnp.int32))
    cross = lax.psum(products[..., :TAPS].sum(0), "tm")
    got = lax.all_to_all(products, "tm", 3, 0, tiled=True)

    def own_step(gram, q):
        offset = q * BLOCK_LEN
        table = lag_table(ref_ext, offset, LAGS)
        taps = table[:, :TAPS].transpose(1, 0, 2)
        mine = lax.dynamic_slice_in_dim(table, here * lags_local, lags_local, 1)
        return gram + times_conj(taps, table[:, :TAPS]), times_conj(taps, mine)

    start = jnp.zeros((TAPS, 2, TAPS), jnp.float32)
    gram, own = lax.scan(own_step, start, jnp.arange(samples // BLOCK_LEN, dtype=jnp.int32))
    g_real, g_imag = gram[:, 0].T, gram[:, 1].T
    system = jnp.concatenate([jnp.concatenate([g_real, -g_imag], 1), jnp.concatenate([g_imag, g_real], 1)], 0)
    right = jnp.concatenate([cross[:, 0].T, cross[:, 1].T], 0)
    solved = jax.scipy.linalg.cho_solve((jnp.linalg.cholesky(system), True), right)
    b_real, b_imag = solved[:TAPS].T, solved[TAPS:].T
    mixing = jnp.concatenate([jnp.stack([b_real, b_imag], 1), jnp.stack([-b_imag, b_real], 1)], 2)
    stacked = jnp.concatenate([own[:, :, 0], own[:, :, 1]], 1)
    lagged = got - jnp.einsum("mck,qkl->qmcl", mixing, stacked, precision=HIGHEST)
    wave = jnp.asarray(doppler_table(samples // BLOCK_LEN, 0.125 / math.sqrt(samples)))
    wave = wave.reshape(2, samples // BLOCK_LEN, 2, DOPPLER)
    return jnp.einsum("qmcl,cqdk->mdlk", lagged, wave, precision=HIGHEST)


def on_device(ref_signal, surveillance, steering):
    chan_count, tm_count = lax.axis_size("chan"), lax.axis_size("tm")
    beams_local = steering.shape[1] // chan_count
    lags_local = LAGS // tm_count
    fills = (
        LANES % lags_local == 0
        and lags_local % (2 * SUBLANES) == 0
        and beams_local * lags_local == LANES * SUBLANES // 2
        and chan_count > 1
        and chan_count & (chan_count - 1) == 0
        and tm_count > 2
        and tm_count & (tm_count - 1) == 0
        and 2 * surveillance.shape[1] % LANES == 0
        and surveillance.shape[2] % (2 * BATCH * BLOCK_LEN) == 0
    )
    device = tiled_device if fills else plain_device
    return device(ref_signal, surveillance, steering)


def solution(mesh):
    placed = (P(None, "tm"), P(None, "chan", "tm"), P(None, None, "chan"))
    return jax.shard_map(
        on_device,
        mesh=mesh,
        in_specs=placed,
        out_specs=P("chan", None, "tm", None),
        check_vma=False,
    )
```

```python
import functools
import math

import jax
import jax.numpy as jnp
import numpy as np
from jax import lax
from jax.experimental import pallas as pl
from jax.experimental.pallas import tpu as pltpu
from jax.sharding import PartitionSpec as P

LAGS = 256
DOPPLER = 256
TAPS = 64
BLOCK_LEN = 256
LANES = 128
SUBLANES = 8
EDGE = 2

HIGHEST = lax.Precision.HIGHEST
VMEM_BYTES = 48 * 1024 * 1024


def params():
    return pltpu.CompilerParams(vmem_limit_bytes=VMEM_BYTES)


def cost(us):
    return pl.CostEstimate(flops=int(us * 1.15e9), bytes_accessed=0, transcendentals=0)


def halves(x):
    high = x.astype(jnp.bfloat16)
    return high, (x - high.astype(jnp.float32)).astype(jnp.bfloat16)


def thirds(x):
    high = x.astype(jnp.bfloat16)
    rest = x - high.astype(jnp.float32)
    return (high,) + halves(rest)


PART_PAIRS = ((2, 0), (1, 1), (0, 2), (1, 0), (0, 1), (0, 0))


def dot_parts(a, b, across=False):
    rows = a[0].shape[0]
    by_size = {}
    for j, right in enumerate(b):
        left = a[: max(3 - j, 1)]
        left = left[0] if len(left) == 1 else jnp.concatenate(left, 0)
        contract = (((1,), (1 if across else 0,)), ((), ()))
        product = lax.dot_general(left, right, contract, preferred_element_type=jnp.float32)
        for i in range(product.shape[0] // rows):
            by_size.setdefault(i + j, []).append(product[i * rows : (i + 1) * rows])
    total = None
    for size in sorted(by_size, reverse=True):
        for term in by_size[size]:
            total = term if total is None else total + term
    return total


def dot_nt(a, b, precision=None):
    return lax.dot_general(
        a, b, (((1,), (1,)), ((), ())), precision=precision, preferred_element_type=jnp.float32
    )


def dot_split(a, b):
    (a_high, a_low), (b_high, b_low) = a, b
    left = jnp.concatenate([a_high, a_low], 1)
    right = jnp.concatenate([b_high, b_high], 0)
    return jnp.dot(left, right, preferred_element_type=jnp.float32) + jnp.dot(
        a_high, b_low, preferred_element_type=jnp.float32
    )


def row_sign(shape):
    rows = lax.broadcasted_iota(jnp.int32, shape, 0)
    return jnp.where(rows % SUBLANES < SUBLANES // 2, 1.0, -1.0).astype(jnp.float32)


def lane_sign(shape):
    lanes = lax.broadcasted_iota(jnp.int32, shape, 1)
    return jnp.where(lanes % LANES < LANES // 2, 1.0, -1.0).astype(jnp.float32)


def swap_groups(rows, groups):
    width = LANES // groups
    lane_group = lax.broadcasted_iota(jnp.int32, rows[0].shape, 1) // width
    outs = []
    for j in range(groups):
        out = rows[j]
        for i in range(groups):
            if i != j:
                moved = pltpu.roll(rows[i], (width * (i - j)) % LANES, 1)
                out = jnp.where(lane_group == i, moved, out)
        outs.append(out)
    return outs


COPIES = 2


def beam_kernel(
    chan_count, beams_local, w_hbm, s_hbm, ref_hbm, kept_ref, sent_ref, tiles_ref,
    w_ref, s_ref, ref_ref, w_sem, s_sem, ref_sem,
):
    me = lax.axis_index("chan")
    depth = s_hbm.shape[0] // COPIES
    w_copy = pltpu.make_async_copy(w_hbm, w_ref, w_sem)
    w_copy.start()
    ref_copy = pltpu.make_async_copy(ref_hbm, ref_ref, ref_sem)
    ref_copy.start()
    s_copies = []
    for n in range(COPIES):
        part = pl.ds(n * depth, depth)
        s_copies.append(pltpu.make_async_copy(s_hbm.at[part], s_ref.at[part], s_sem.at[n]))
        s_copies[n].start()
    half = SUBLANES // 2
    sub = lax.broadcasted_iota(jnp.int32, (SUBLANES, w_hbm.shape[2]), 0)
    top = sub < half
    w_copy.wait()
    rows = []
    for parity in range(2):
        for e in range(parity, chan_count, 2):
            base = (me ^ e) * beams_local
            for tile in range(beams_local // SUBLANES):
                start = pl.multiple_of(base + tile * SUBLANES, SUBLANES)
                wr = w_ref[0, pl.ds(start, SUBLANES), :]
                wi = w_ref[1, pl.ds(start, SUBLANES), :]
                wr_s = pltpu.roll(wr, half, 0)
                wi_s = pltpu.roll(wi, half, 0)
                first = [jnp.where(top, wr, wi_s), jnp.where(top, -wi, wr_s)]
                second = [jnp.where(top, wr_s, wi), jnp.where(top, -wi_s, wr)]
                rows.append(jnp.concatenate(first, 1))
                rows.append(jnp.concatenate(second, 1))
    weights = halves(jnp.concatenate(rows, 0))
    ref_copy.wait()
    for c in range(2):
        for n in range(tiles_ref.shape[1]):
            tiles_ref[c, n : n + 1, :] = ref_ref[c : c + 1, n * LANES : (n + 1) * LANES]
    for copy in s_copies:
        copy.wait()
    product = dot_parts(weights, thirds(s_ref[...]))
    mid = product.shape[0] // 2
    kept_ref[...] = product[:mid]
    sent_ref[...] = product[mid:]


def beam_call(steering, survey, ref, chan_count, beams_local):
    depth, length = survey.shape
    rows = chan_count * beams_local
    tiles = (2, length // LANES, LANES)
    out = jax.ShapeDtypeStruct((rows, length), jnp.float32)
    hbm, vmem = pl.BlockSpec(memory_space=pltpu.HBM), pl.BlockSpec(memory_space=pltpu.VMEM)
    return pl.pallas_call(
        functools.partial(beam_kernel, chan_count, beams_local),
        in_specs=[hbm] * 3,
        out_specs=[vmem] * 3,
        out_shape=[
            out,
            out,
            jax.ShapeDtypeStruct(tiles, jnp.float32),
        ],
        scratch_shapes=[
            pltpu.VMEM(steering.shape, jnp.float32),
            pltpu.VMEM(survey.shape, jnp.float32),
            pltpu.VMEM(ref.shape, jnp.float32),
            pltpu.SemaphoreType.DMA,
            pltpu.SemaphoreType.DMA((COPIES,)),
            pltpu.SemaphoreType.DMA,
        ],
        compiler_params=params(),
        cost_estimate=cost(2.2),
        name="beams",
    )(*(pltpu.with_memory_space_constraint(x, pltpu.HBM) for x in (steering, survey, ref)))


def sum_kernel(count, *refs):
    kept_ref, sent_ref = refs[-2:]
    for n in range(kept_ref.shape[0]):
        for offset, out_ref in ((0, kept_ref), (1, sent_ref)):
            total = refs[0][2 * n + offset]
            for ref in refs[1:count]:
                total = total + ref[2 * n + offset]
            out_ref[n] = total


def sum_call(parts):
    shape = (parts[0].shape[0] // 2,) + parts[0].shape[1:]
    out = jax.ShapeDtypeStruct(shape, jnp.float32)
    vmem = pl.BlockSpec(memory_space=pltpu.VMEM)
    return pl.pallas_call(
        functools.partial(sum_kernel, len(parts)),
        in_specs=[vmem] * len(parts),
        out_specs=[vmem, vmem],
        out_shape=[out, out],
        compiler_params=params(),
        cost_estimate=cost(0.1),
        name="halves_summed",
    )(*parts)


def join_kernel(first_ref, second_ref, *refs):
    out_ref = refs[-1]
    count = first_ref.shape[0]
    out_ref[:count] = first_ref[...]
    out_ref[count:] = second_ref[...]


def join_call(first, second, *after):
    vmem = pl.BlockSpec(memory_space=pltpu.VMEM)
    return pl.pallas_call(
        join_kernel,
        in_specs=[vmem, vmem] + [pl.BlockSpec(memory_space=pl.ANY)] * len(after),
        out_shape=jax.ShapeDtypeStruct((2 * first.shape[0],) + first.shape[1:], jnp.float32),
        compiler_params=params(),
        cost_estimate=cost(1.0),
        name="reference_joined",
    )(first, second, *after)


def spread_line(line, keep):
    for g in range(0, LANES, 2 * SUBLANES):
        tiled = jnp.broadcast_to(line, (2 * SUBLANES, line.shape[1]))
        for h, value in enumerate(halves(pltpu.roll(tiled, g, 1, stride=1, stride_axis=0)[:, LANES:])):
            keep(h, g, value)


def table_kernel(tiles_ref, out_ref):
    for c in range(2):
        line = jnp.concatenate([tiles_ref[c, n : n + 1, :] for n in range(tiles_ref.shape[1])], 1)

        def keep(h, g, value):
            out_ref[h, c, g : g + 2 * SUBLANES] = value

        spread_line(line, keep)


def table_call(tiles):
    shape = (2, 2, LANES, LANES * (tiles.shape[1] - 1))
    return pl.pallas_call(
        table_kernel,
        out_shape=jax.ShapeDtypeStruct(shape, jnp.bfloat16),
        compiler_params=params(),
        cost_estimate=cost(0.7),
        name="shifted_reference",
    )(tiles)


def first_kernel(tiles_ref, *refs):
    *round_refs, out_ref = refs
    me = lax.axis_index("tm")
    for c in range(2):
        tails = [ref[ref.shape[0] - 1, c, ref.shape[2] - EDGE :, :] for ref in round_refs]
        before = jnp.where(me % 2 == 1, tails[0], jnp.where(me > 0, tails[-1], 0.0))
        line = jnp.concatenate([before[n : n + 1] for n in range(EDGE)] + [tiles_ref[c, 0:1, :]], 1)

        def keep(h, g, value):
            out_ref[h, c, g : g + 2 * SUBLANES] = value

        spread_line(line, keep)


def first_call(tiles, rounds):
    return pl.pallas_call(
        first_kernel,
        out_shape=jax.ShapeDtypeStruct((2, 2, LANES, 2 * LANES), jnp.bfloat16),
        compiler_params=params(),
        cost_estimate=cost(0.1),
        name="shifted_first",
    )(tiles, *rounds)


def lag_kernel(groups, part_count, *refs):
    y_refs, refs = refs[:part_count], refs[part_count:]
    table_ref, first_ref, _, out_hbm, out_ref, out_sem = refs
    copies = []

    def table_tile(h, n):
        parts = []
        for c in range(2):
            known = first_ref.shape[3] // LANES
            ref, at = (first_ref, n) if n < known else (table_ref, n - known)
            parts.append(ref[h, c, :, at * LANES : (at + 1) * LANES])
        return jnp.concatenate(parts, 1)

    def send(start, count):
        part = (slice(None), pl.ds(start, count))
        copies.append(pltpu.make_async_copy(out_ref.at[part], out_hbm.at[part], out_sem.at[len(copies)]))
        copies[-1].start()

    y = y_refs[0][...]
    for y_ref in y_refs[1:]:
        y = y + y_ref[...]
    rows, length = y.shape
    blocks = length // BLOCK_LEN
    turned = jnp.concatenate(
        [pltpu.roll(y[r : r + SUBLANES], SUBLANES // 2, 0) for r in range(0, rows, SUBLANES)], 0
    )
    turned = turned * row_sign(turned.shape)
    y_parts, t_parts = thirds(y), thirds(turned)

    def half_block(q, b):
        cols = slice(q * BLOCK_LEN + b * LANES, q * BLOCK_LEN + (b + 1) * LANES)
        return [jnp.concatenate([x[:, cols], t[:, cols]], 1) for x, t in zip(y_parts, t_parts)]

    def products(stack, n, count):
        tiles = [jnp.concatenate([table_tile(h, n + i) for i in range(count)], 0) for h in range(2)]
        product = dot_parts([jnp.concatenate(part, 0) for part in zip(*stack)], tiles, True)
        return [product[i * rows : (i + 1) * rows] for i in range(len(stack))]

    taps_sum = None
    (far,) = products([half_block(0, 0)], 0, 1)
    for q in range(blocks):
        stack = [half_block(q, 0), half_block(q, 1)]
        if q + 1 < blocks:
            stack.append(half_block(q + 1, 0))
        first, second, *after = products(stack, 2 * q + 1, 2)
        product = jnp.concatenate([first[:, :LANES] + second[:, LANES:], second[:, :LANES] + far], 1)
        if after:
            far = after[0][:, LANES:]
        taps = product[:, :LANES]
        taps_sum = taps if taps_sum is None else taps_sum + taps
        for h in range(LAGS // LANES):
            lanes = slice(h * LANES, (h + 1) * LANES)
            tiles = [product[r : r + SUBLANES, lanes] for r in range(0, rows, SUBLANES)]
            for j, tile in enumerate(swap_groups(tiles, groups)):
                out_ref[h * groups + j, q] = tile
        if q + 1 == blocks // 2:
            send(0, blocks // 2)
    left = lax.broadcasted_iota(jnp.int32, (SUBLANES, LANES), 1) < TAPS
    for i in range(groups // 2):
        a = taps_sum[i * SUBLANES : (i + 1) * SUBLANES]
        other = i + groups // 2
        b = taps_sum[other * SUBLANES : (other + 1) * SUBLANES]
        tile = jnp.where(left, a, pltpu.roll(b, LANES - TAPS, 1))
        for owner in range(out_ref.shape[0]):
            out_ref[owner, blocks + i] = tile
    send(blocks // 2, blocks - blocks // 2 + groups // 2)
    for copy in copies:
        copy.wait()


def lag_call(ys, table, first, after, groups, owners):
    blocks = ys[0].shape[1] // BLOCK_LEN
    shape = (owners, blocks + groups // 2, SUBLANES, LANES)
    vmem = pl.BlockSpec(memory_space=pltpu.VMEM)
    return pl.pallas_call(
        functools.partial(lag_kernel, groups, len(ys)),
        in_specs=[vmem] * (len(ys) + 2) + [pl.BlockSpec(memory_space=pl.ANY)],
        out_specs=pl.BlockSpec(memory_space=pltpu.HBM),
        out_shape=jax.ShapeDtypeStruct(shape, jnp.float32),
        scratch_shapes=[
            pltpu.VMEM(shape, jnp.float32),
            pltpu.SemaphoreType.DMA((2,)),
        ],
        compiler_params=params(),
        cost_estimate=cost(2.1),
        name="lag_products",
    )(*ys, table, first, after)


BATCH = 4


def own_kernel(lags_local, *refs):
    *part_refs, _, out_ref, line_ref, tail_ref, span_ref, late_ref, taps_a, lags_a, taps_b, lags_b = refs
    me = lax.axis_index("tm")
    part_rows = part_refs[0].shape[2]
    owners = sum(part_ref.shape[0] for part_ref in part_refs)
    samples = owners * part_rows * LANES
    steps = samples // BLOCK_LEN // BATCH
    total_rows = span_ref.shape[1]
    block_rows = BLOCK_LEN // LANES

    span_ref[...] = jnp.zeros_like(span_ref)
    n = 0
    for part_ref in part_refs:
        for i in range(part_ref.shape[0]):
            block = lax.rem(me - (n // 2) * 2 + owners, owners) ^ (n % 2)
            span_ref[:, pl.ds(EDGE + block * part_rows, part_rows), :] = part_ref[i]
            n += 1
    late_rows = (me * lags_local) // LANES
    late_lanes = lax.rem(me * lags_local, LANES)
    turned = [pltpu.roll(span_ref[c], late_lanes, 1) for c in range(2)]
    before = [pltpu.roll(x, 1, 0) for x in turned]
    lanes = lax.broadcasted_iota(jnp.int32, (total_rows, LANES), 1)
    for c in range(2):
        late_ref[c] = pltpu.roll(jnp.where(lanes < late_lanes, before[c], turned[c]), late_rows, 0)

    def line_of(ref, c, first, count):
        return jnp.concatenate([ref[c, pl.ds(first + n, 1), :] for n in range(count)], 1)

    def shifted(line, by):
        tiled = jnp.broadcast_to(line, (2 * SUBLANES, line.shape[1]))
        return pltpu.roll(tiled, by, 1, stride=1, stride_axis=0)[:, LANES:]

    def keep(ref, row, parts):
        step = ref.shape[0] // len(parts)
        for n, part in enumerate(parts):
            ref[n * step + row : n * step + row + 2 * SUBLANES, :] = part

    def build(n, taps_ref, lags_ref):
        first = EDGE - 1 + n * BATCH * block_rows
        count = BATCH * block_rows + 1
        lines = [line_of(span_ref, c, first, count) for c in range(2)]
        for c in range(2):
            for g in range(0, TAPS, 2 * SUBLANES):
                keep(taps_ref, c * TAPS + g, thirds(shifted(lines[c], g)))
            late = line_of(late_ref, c, first, count)
            for g in range(0, lags_local, 2 * SUBLANES):
                keep(lags_ref, c * lags_local + g, halves(shifted(late, g)))
        pad = jnp.zeros((2 * SUBLANES - 2, BATCH * BLOCK_LEN), jnp.float32)
        keep(lags_ref, 2 * lags_local, halves(jnp.concatenate([line[:, LANES:] for line in lines] + [pad], 0)))

    turn = lane_sign((lags_local, LANES))

    def use(n, taps_ref, lags_ref):
        count = lags_ref.shape[0] // 2
        for b in range(BATCH):
            cols = slice(b * BLOCK_LEN, (b + 1) * BLOCK_LEN)
            product = dot_nt(lags_ref[:, cols], taps_ref[: 2 * LANES, cols])
            least = dot_nt(lags_ref[:count, cols], taps_ref[2 * LANES :, cols]) + product[count:, LANES:]
            product = product[:count, :LANES] + ((product[:count, LANES:] + product[count:, :LANES]) + least)
            by_real = product[:lags_local]
            by_imag = product[lags_local : 2 * lags_local]
            rows = pl.ds(pl.multiple_of((n * BATCH + b) * lags_local, lags_local), lags_local)
            for part, value in enumerate(thirds(by_real + turn * pltpu.roll(by_imag, TAPS, 1))):
                out_ref[part, rows, :] = value
            line_ref[...] += product[2 * lags_local : 2 * lags_local + SUBLANES]

    line_ref[...] = jnp.zeros_like(line_ref)
    build(0, taps_a, lags_a)

    def pair(m, carry):
        build(2 * m + 1, taps_b, lags_b)
        use(2 * m, taps_a, lags_a)
        build(jnp.minimum(2 * m + 2, steps - 1), taps_a, lags_a)
        use(2 * m + 1, taps_b, lags_b)
        return carry

    lax.fori_loop(0, steps // 2, pair, 0)
    tail = []
    for c in range(2):
        line = line_of(span_ref, c, EDGE + owners * part_rows - 1, 2)
        tail += [shifted(line, g) for g in range(0, TAPS, 2 * SUBLANES)]
    tail = jnp.concatenate(tail, 0)
    tail_ref[...] = dot_nt(tail, tail, HIGHEST)


def own_call(parts, lags_local, after):
    part_rows = parts[0].shape[2]
    span_rows = part_rows * sum(part.shape[0] for part in parts)
    rows = span_rows * LANES // BLOCK_LEN * lags_local
    held_rows = -(-(span_rows + 2 * EDGE) // SUBLANES) * SUBLANES
    width = BATCH * BLOCK_LEN
    taps = pltpu.VMEM((6 * TAPS, width), jnp.bfloat16)
    lags = pltpu.VMEM((4 * lags_local + 4 * SUBLANES, width), jnp.bfloat16)
    span = pltpu.VMEM((2, held_rows, LANES), jnp.float32)
    return pl.pallas_call(
        functools.partial(own_kernel, lags_local),
        in_specs=[pl.BlockSpec(memory_space=pltpu.VMEM)] * len(parts) + [pl.BlockSpec(memory_space=pl.ANY)],
        out_shape=[
            jax.ShapeDtypeStruct((3, rows, 2 * TAPS), jnp.bfloat16),
            jax.ShapeDtypeStruct((SUBLANES, 2 * TAPS), jnp.float32),
            jax.ShapeDtypeStruct((2 * TAPS, 2 * TAPS), jnp.float32),
        ],
        scratch_shapes=[span, span, taps, lags, taps, lags],
        compiler_params=params(),
        cost_estimate=cost(6.2),
        name="reference_products",
    )(*parts, after)


def as_factor(a):
    return jnp.concatenate([a, -lane_sign(a.shape) * pltpu.roll(a, a.shape[0], 1)], 0)


def solver_kernel(line_ref, tail_ref, gram_ref, solver_ref):
    total = line_ref[...]
    line = total[0:1] + lane_sign((1, LANES)) * pltpu.roll(total[1:2], TAPS, 1)
    low = lax.broadcasted_iota(jnp.int32, (1, LANES), 1) < TAPS
    line_r = jnp.where(low, line, 0.0)
    line_i = jnp.where(low, pltpu.roll(line, TAPS, 1), 0.0)
    cols = lax.broadcasted_iota(jnp.int32, (TAPS, TAPS), 1)
    rows = lax.broadcasted_iota(jnp.int32, (TAPS, TAPS), 0)
    above = cols > rows

    def stack(ref, value):
        parts = thirds(value)
        for n, (_, part) in enumerate(PART_PAIRS):
            ref[n * value.shape[0] : (n + 1) * value.shape[0], :] = parts[part]

    def upper(x):
        spread = pltpu.roll(jnp.broadcast_to(x, (TAPS, LANES)), 0, 1, stride=1, stride_axis=0)
        return spread[:, :TAPS]

    up_r = upper(line_r)
    up_i = jnp.where(above, upper(line_i), 0.0)
    strict_r = jnp.where(above, up_r, 0.0)
    diag_r = jnp.where(cols == rows, up_r, 0.0)
    tails = tail_ref[...]
    gram_r = strict_r + strict_r.T + diag_r - (tails[:TAPS, :TAPS] + tails[TAPS:, TAPS:])
    gram_i = up_i - up_i.T - (tails[:TAPS, TAPS:] - tails[TAPS:, :TAPS])
    gram = jnp.concatenate([gram_r, gram_i], 1)
    gram_factor = as_factor(gram)
    stack(gram_ref, gram_factor)
    gram_halves = halves(gram_factor)
    one = (
        lax.broadcasted_iota(jnp.int32, gram.shape, 0) == lax.broadcasted_iota(jnp.int32, gram.shape, 1)
    ).astype(jnp.float32)
    bound = jnp.max(jnp.sum(jnp.abs(gram), axis=1, keepdims=True), axis=0, keepdims=True)

    def again(state):
        count, left, _ = state
        return (count < 60) & (left > 1e-3)

    def newton(state):
        count, _, x = state
        x_halves = halves(x)
        seen = dot_split(x_halves, gram_halves)
        left = jnp.max(jnp.abs(seen - one))
        x = 2.0 * x - dot_split(halves(seen), halves(as_factor(x)))
        return count + 1, left, x

    start = (jnp.int32(0), jnp.float32(1.0), one * (1.0 / bound))
    _, _, inverse = lax.while_loop(again, newton, start)
    seen = jnp.dot(inverse, gram_factor, precision=HIGHEST, preferred_element_type=jnp.float32)
    inverse = inverse + jnp.dot(
        one - seen, as_factor(inverse), precision=HIGHEST, preferred_element_type=jnp.float32
    )
    stack(solver_ref, as_factor(inverse))


def solver_call(line, tail):
    return pl.pallas_call(
        solver_kernel,
        out_shape=[jax.ShapeDtypeStruct((len(PART_PAIRS) * tail.shape[0], tail.shape[1]), jnp.bfloat16)] * 2,
        compiler_params=params(),
        cost_estimate=cost(2.0),
        name="gram_inverse",
    )(line, tail)


def doppler_table(block_count, scale):
    phase = (np.arange(block_count)[:, None] * np.arange(DOPPLER)[None, :] % DOPPLER) * (2.0 * math.pi / DOPPLER)
    cosine, sine = np.cos(phase), np.sin(phase)
    upper = np.concatenate([cosine, -sine], 1)
    lower = np.concatenate([sine, cosine], 1)
    return (np.concatenate([upper, lower], 0) * scale).astype(np.float32)


def map_kernel(groups, got_ref, own_ref, gram_ref, solver_ref, wave_ref, out_hbm, held_ref, out_ref, out_sem):
    owners, pieces = got_ref.shape[:2]
    blocks = pieces - groups // 2
    lags_local = LANES // groups
    total = owners * blocks
    left = lax.broadcasted_iota(jnp.int32, (SUBLANES, LANES), 1) < TAPS
    sign = row_sign((SUBLANES, LANES))
    rows = [None] * groups
    for i in range(groups // 2):
        tile = got_ref[0, blocks + i]
        for owner in range(1, owners):
            tile = tile + got_ref[owner, blocks + i]
        swapped = pltpu.roll(tile, TAPS, 1)
        for part, here, there in ((i, tile, swapped), (i + groups // 2, swapped, tile)):
            other = -sign * pltpu.roll(there, SUBLANES // 2, 0)
            rows[part] = jnp.where(left, here, other)
    cross = jnp.concatenate(rows, 0)

    def exact(x, ref):
        parts = thirds(x)
        return jnp.dot(
            jnp.concatenate([parts[part] for part, _ in PART_PAIRS], 1), ref[...], preferred_element_type=jnp.float32
        )

    taps = exact(cross, solver_ref)
    taps = taps + exact(cross - exact(taps, gram_ref), solver_ref)
    taps = thirds(taps)
    for q in range(0, total, 2 * groups):
        own = slice(q * lags_local, (q + 2 * groups) * lags_local)
        clutter = dot_parts(taps, [own_ref[part, own, :] for part in range(3)], True)
        for h in range(2):
            lanes = slice(h * LANES, (h + 1) * LANES)
            tiles = [clutter[r : r + SUBLANES, lanes] for r in range(0, groups * SUBLANES, SUBLANES)]
            for j, tile in enumerate(swap_groups(tiles, groups)):
                at = q + h * groups + j
                held_ref[at * SUBLANES : (at + 1) * SUBLANES, :] = got_ref[at // blocks, at % blocks] - tile
    half = SUBLANES // 2
    wave = (wave_ref[0], wave_ref[1])
    copies = []
    for g in range(half):
        parts = [held_ref[pl.ds(c * half + g, total, stride=SUBLANES), :] for c in range(2)]
        spectrum = dot_split(halves(jnp.concatenate(parts, 0).T), wave)
        for i in range(groups):
            for c in range(2):
                out_ref[i, g, c] = spectrum[i * lags_local : (i + 1) * lags_local, c * DOPPLER : (c + 1) * DOPPLER]
        part = (slice(None), pl.ds(g, 1))
        copies.append(pltpu.make_async_copy(out_ref.at[part], out_hbm.at[part], out_sem.at[g]))
        copies[-1].start()
    for copy in copies:
        copy.wait()


def map_call(got, own, gram, solver, wave, groups, beams_local):
    total = got.shape[0] * (got.shape[1] - groups // 2)
    lags_local = LANES // groups
    half = SUBLANES // 2
    shape = (beams_local // half, half, 2, lags_local, DOPPLER)
    out = pl.pallas_call(
        functools.partial(map_kernel, groups),
        in_specs=[pl.BlockSpec(memory_space=pltpu.VMEM)] * 5,
        out_specs=pl.BlockSpec(memory_space=pltpu.HBM),
        out_shape=jax.ShapeDtypeStruct(shape, jnp.float32),
        scratch_shapes=[
            pltpu.VMEM((total * SUBLANES, LANES), jnp.float32),
            pltpu.VMEM(shape, jnp.float32),
            pltpu.SemaphoreType.DMA((half,)),
        ],
        compiler_params=params(),
        cost_estimate=cost(2.5),
        name="range_doppler",
    )(got, own, gram, solver, wave)
    return out.reshape((beams_local,) + shape[2:])


def swap(x, axis, by):
    pairs = [(i, i ^ by) for i in range(lax.axis_size(axis))]
    return lax.ppermute(x, axis, pairs)


def tiled_device(ref_signal, surveillance, steering):
    chan_count, tm_count = lax.axis_size("chan"), lax.axis_size("tm")
    channels, length = surveillance.shape[1:]
    beams_local = steering.shape[1] // chan_count
    lags_local = LAGS // tm_count
    groups = LANES // lags_local
    samples = length * tm_count

    survey = surveillance.reshape(2 * channels, length)
    kept, moved, tiles = beam_call(steering, survey, ref_signal, chan_count, beams_local)
    near = swap(tiles[None], "tm", 1)
    shape = (chan_count // 2, 2 * beams_local, length)
    kept, got = kept.reshape(shape), swap(moved, "chan", 1).reshape(shape)
    by = 2
    while by < chan_count:
        kept, moved = sum_call([kept, got])
        got = swap(moved, "chan", by)
        by *= 2
    rounds = [near]
    joined = join_call(tiles[None], near, moved)
    while True:
        count = joined.shape[0]
        rounds.append(lax.ppermute(joined, "tm", [(i, (i + count) % tm_count) for i in range(tm_count)]))
        if count * 2 == tm_count:
            break
        joined = join_call(joined, rounds[-1])
    table = table_call(tiles)
    first = first_call(tiles, rounds[:2])
    pieces = lag_call([kept[0], got[0]], table, first, joined, groups, tm_count)
    got = lax.all_to_all(pieces, "tm", 0, 0, tiled=True)
    own, line, tail = own_call([tiles[None]] + rounds, lags_local, pieces)
    gram, solver = solver_call(line, tail)
    wave = doppler_table(samples // BLOCK_LEN, 0.125 / math.sqrt(samples))
    high = wave.astype(jnp.bfloat16)
    wave = np.stack([high, (wave - high.astype(np.float32)).astype(jnp.bfloat16)])
    return map_call(got, own, gram, solver, jnp.asarray(wave), groups, beams_local)


def lag_table(ref_ext, offset, lags):
    window = lax.dynamic_slice_in_dim(ref_ext, offset, BLOCK_LEN + LAGS, 1)
    span = BLOCK_LEN + LAGS
    tiled = jnp.tile(jnp.pad(window, ((0, 0), (0, 1))), (1, lags))[:, : lags * span]
    return tiled.reshape(2, lags, span)[:, :, LAGS:]


def times_conj(a, b):
    real = jnp.einsum("...t,lt->...l", a[..., 0, :], b[0], precision=HIGHEST) + jnp.einsum(
        "...t,lt->...l", a[..., 1, :], b[1], precision=HIGHEST
    )
    imag = jnp.einsum("...t,lt->...l", a[..., 1, :], b[0], precision=HIGHEST) - jnp.einsum(
        "...t,lt->...l", a[..., 0, :], b[1], precision=HIGHEST
    )
    return jnp.stack([real, imag], -2)


def plain_device(ref_signal, surveillance, steering):
    chan_count, tm_count = lax.axis_size("chan"), lax.axis_size("tm")
    length = surveillance.shape[2]
    beams = steering.shape[1]
    lags_local = LAGS // tm_count
    samples = length * tm_count
    local_blocks = length // BLOCK_LEN
    here = lax.axis_index("tm")

    w_real, w_imag = steering
    real = jnp.dot(w_real, surveillance[0], precision=HIGHEST) - jnp.dot(w_imag, surveillance[1], precision=HIGHEST)
    imag = jnp.dot(w_imag, surveillance[0], precision=HIGHEST) + jnp.dot(w_real, surveillance[1], precision=HIGHEST)
    beam = lax.psum_scatter(jnp.stack([real, imag], 1), "chan", scatter_dimension=0, tiled=True)
    ref_all = lax.all_gather(ref_signal, "tm", axis=1, tiled=True)
    ref_ext = jnp.pad(ref_all, ((0, 0), (LAGS, 0)))

    def beam_step(carry, q):
        offset = q * BLOCK_LEN
        table = lag_table(ref_ext, here * length + offset, LAGS)
        segment = lax.dynamic_slice_in_dim(beam, offset, BLOCK_LEN, 2)
        return carry, times_conj(segment, table)

    _, products = lax.scan(beam_step, None, jnp.arange(local_blocks, dtype=jnp.int32))
    cross = lax.psum(products[..., :TAPS].sum(0), "tm")
    got = lax.all_to_all(products, "tm", 3, 0, tiled=True)

    def own_step(gram, q):
        offset = q * BLOCK_LEN
        table = lag_table(ref_ext, offset, LAGS)
        taps = table[:, :TAPS].transpose(1, 0, 2)
        mine = lax.dynamic_slice_in_dim(table, here * lags_local, lags_local, 1)
        return gram + times_conj(taps, table[:, :TAPS]), times_conj(taps, mine)

    start = jnp.zeros((TAPS, 2, TAPS), jnp.float32)
    gram, own = lax.scan(own_step, start, jnp.arange(samples // BLOCK_LEN, dtype=jnp.int32))
    g_real, g_imag = gram[:, 0].T, gram[:, 1].T
    system = jnp.concatenate([jnp.concatenate([g_real, -g_imag], 1), jnp.concatenate([g_imag, g_real], 1)], 0)
    right = jnp.concatenate([cross[:, 0].T, cross[:, 1].T], 0)
    solved = jax.scipy.linalg.cho_solve((jnp.linalg.cholesky(system), True), right)
    b_real, b_imag = solved[:TAPS].T, solved[TAPS:].T
    mixing = jnp.concatenate([jnp.stack([b_real, b_imag], 1), jnp.stack([-b_imag, b_real], 1)], 2)
    stacked = jnp.concatenate([own[:, :, 0], own[:, :, 1]], 1)
    lagged = got - jnp.einsum("mck,qkl->qmcl", mixing, stacked, precision=HIGHEST)
    wave = jnp.asarray(doppler_table(samples // BLOCK_LEN, 0.125 / math.sqrt(samples)))
    wave = wave.reshape(2, samples // BLOCK_LEN, 2, DOPPLER)
    return jnp.einsum("qmcl,cqdk->mdlk", lagged, wave, precision=HIGHEST)


def on_device(ref_signal, surveillance, steering):
    chan_count, tm_count = lax.axis_size("chan"), lax.axis_size("tm")
    beams_local = steering.shape[1] // chan_count
    lags_local = LAGS // tm_count
    fills = (
        LANES % lags_local == 0
        and lags_local % (2 * SUBLANES) == 0
        and beams_local * lags_local == LANES * SUBLANES // 2
        and chan_count > 1
        and chan_count & (chan_count - 1) == 0
        and tm_count > 2
        and tm_count & (tm_count - 1) == 0
        and 2 * surveillance.shape[1] % LANES == 0
        and surveillance.shape[2] % (2 * BATCH * BLOCK_LEN) == 0
    )
    device = tiled_device if fills else plain_device
    return device(ref_signal, surveillance, steering)


def solution(mesh):
    placed = (P(None, "tm"), P(None, "chan", "tm"), P(None, None, "chan"))
    return jax.shard_map(
        on_device,
        mesh=mesh,
        in_specs=placed,
        out_specs=P("chan", None, "tm", None),
        check_vma=False,
    )
```

```python
import functools
import math

import jax
import jax.numpy as jnp
import numpy as np
from jax import lax
from jax.experimental import pallas as pl
from jax.experimental.pallas import tpu as pltpu
from jax.sharding import PartitionSpec as P

LAGS = 256
DOPPLER = 256
TAPS = 64
BLOCK_LEN = 256
LANES = 128
SUBLANES = 8
EDGE = 2

HIGHEST = lax.Precision.HIGHEST
VMEM_BYTES = 48 * 1024 * 1024


def params():
    return pltpu.CompilerParams(vmem_limit_bytes=VMEM_BYTES)


def cost(us):
    return pl.CostEstimate(flops=int(us * 1.15e9), bytes_accessed=0, transcendentals=0)


def halves(x):
    high = x.astype(jnp.bfloat16)
    return high, (x - high.astype(jnp.float32)).astype(jnp.bfloat16)


def thirds(x):
    high = x.astype(jnp.bfloat16)
    rest = x - high.astype(jnp.float32)
    return (high,) + halves(rest)


PART_PAIRS = ((2, 0), (1, 1), (0, 2), (1, 0), (0, 1), (0, 0))


def dot_parts(a, b, across=False):
    rows = a[0].shape[0]
    by_size = {}
    for j, right in enumerate(b):
        left = a[: max(3 - j, 1)]
        left = left[0] if len(left) == 1 else jnp.concatenate(left, 0)
        contract = (((1,), (1 if across else 0,)), ((), ()))
        product = lax.dot_general(left, right, contract, preferred_element_type=jnp.float32)
        for i in range(product.shape[0] // rows):
            by_size.setdefault(i + j, []).append(product[i * rows : (i + 1) * rows])
    total = None
    for size in sorted(by_size, reverse=True):
        for term in by_size[size]:
            total = term if total is None else total + term
    return total


def dot_nt(a, b, precision=None):
    return lax.dot_general(
        a, b, (((1,), (1,)), ((), ())), precision=precision, preferred_element_type=jnp.float32
    )


def dot_split(a, b):
    (a_high, a_low), (b_high, b_low) = a, b
    left = jnp.concatenate([a_high, a_low], 1)
    right = jnp.concatenate([b_high, b_high], 0)
    return jnp.dot(left, right, preferred_element_type=jnp.float32) + jnp.dot(
        a_high, b_low, preferred_element_type=jnp.float32
    )


def row_sign(shape):
    rows = lax.broadcasted_iota(jnp.int32, shape, 0)
    return jnp.where(rows % SUBLANES < SUBLANES // 2, 1.0, -1.0).astype(jnp.float32)


def lane_sign(shape):
    lanes = lax.broadcasted_iota(jnp.int32, shape, 1)
    return jnp.where(lanes % LANES < LANES // 2, 1.0, -1.0).astype(jnp.float32)


def swap_groups(rows, groups):
    width = LANES // groups
    lane_group = lax.broadcasted_iota(jnp.int32, rows[0].shape, 1) // width
    outs = []
    for j in range(groups):
        out = rows[j]
        for i in range(groups):
            if i != j:
                moved = pltpu.roll(rows[i], (width * (i - j)) % LANES, 1)
                out = jnp.where(lane_group == i, moved, out)
        outs.append(out)
    return outs


COPIES = 2


def beam_kernel(
    chan_count, beams_local, w_hbm, s_hbm, ref_hbm, kept_ref, sent_ref, tiles_ref,
    w_ref, s_ref, ref_ref, w_sem, s_sem, ref_sem,
):
    me = lax.axis_index("chan")
    depth = s_hbm.shape[0] // COPIES
    w_copy = pltpu.make_async_copy(w_hbm, w_ref, w_sem)
    w_copy.start()
    ref_copy = pltpu.make_async_copy(ref_hbm, ref_ref, ref_sem)
    ref_copy.start()
    s_copies = []
    for n in range(COPIES):
        part = pl.ds(n * depth, depth)
        s_copies.append(pltpu.make_async_copy(s_hbm.at[part], s_ref.at[part], s_sem.at[n]))
        s_copies[n].start()
    half = SUBLANES // 2
    sub = lax.broadcasted_iota(jnp.int32, (SUBLANES, w_hbm.shape[2]), 0)
    top = sub < half
    w_copy.wait()
    rows = []
    for parity in range(2):
        for e in range(parity, chan_count, 2):
            base = (me ^ e) * beams_local
            for tile in range(beams_local // SUBLANES):
                start = pl.multiple_of(base + tile * SUBLANES, SUBLANES)
                wr = w_ref[0, pl.ds(start, SUBLANES), :]
                wi = w_ref[1, pl.ds(start, SUBLANES), :]
                wr_s = pltpu.roll(wr, half, 0)
                wi_s = pltpu.roll(wi, half, 0)
                first = [jnp.where(top, wr, wi_s), jnp.where(top, -wi, wr_s)]
                second = [jnp.where(top, wr_s, wi), jnp.where(top, -wi_s, wr)]
                rows.append(jnp.concatenate(first, 1))
                rows.append(jnp.concatenate(second, 1))
    weights = halves(jnp.concatenate(rows, 0))
    ref_copy.wait()
    for c in range(2):
        for n in range(tiles_ref.shape[1]):
            tiles_ref[c, n : n + 1, :] = ref_ref[c : c + 1, n * LANES : (n + 1) * LANES]
    for copy in s_copies:
        copy.wait()
    high, mid, low = thirds(s_ref[...])
    twice = jnp.concatenate([jnp.concatenate([part, part], 1) for part in weights], 0)
    product = jnp.dot(twice, jnp.concatenate([high, mid], 0), preferred_element_type=jnp.float32)
    least = jnp.dot(weights[0], low, preferred_element_type=jnp.float32)
    count = least.shape[0]
    product = product[:count] + (product[count:] + least)
    mid = product.shape[0] // 2
    kept_ref[...] = product[:mid]
    sent_ref[...] = product[mid:]


def beam_call(steering, survey, ref, chan_count, beams_local):
    depth, length = survey.shape
    rows = chan_count * beams_local
    tiles = (2, length // LANES, LANES)
    out = jax.ShapeDtypeStruct((rows, length), jnp.float32)
    hbm, vmem = pl.BlockSpec(memory_space=pltpu.HBM), pl.BlockSpec(memory_space=pltpu.VMEM)
    return pl.pallas_call(
        functools.partial(beam_kernel, chan_count, beams_local),
        in_specs=[hbm] * 3,
        out_specs=[vmem] * 3,
        out_shape=[
            out,
            out,
            jax.ShapeDtypeStruct(tiles, jnp.float32),
        ],
        scratch_shapes=[
            pltpu.VMEM(steering.shape, jnp.float32),
            pltpu.VMEM(survey.shape, jnp.float32),
            pltpu.VMEM(ref.shape, jnp.float32),
            pltpu.SemaphoreType.DMA,
            pltpu.SemaphoreType.DMA((COPIES,)),
            pltpu.SemaphoreType.DMA,
        ],
        compiler_params=params(),
        cost_estimate=cost(2.2),
        name="beams",
    )(*(pltpu.with_memory_space_constraint(x, pltpu.HBM) for x in (steering, survey, ref)))


def sum_kernel(count, *refs):
    kept_ref, sent_ref = refs[-2:]
    for n in range(kept_ref.shape[0]):
        for offset, out_ref in ((0, kept_ref), (1, sent_ref)):
            total = refs[0][2 * n + offset]
            for ref in refs[1:count]:
                total = total + ref[2 * n + offset]
            out_ref[n] = total


def sum_call(parts):
    shape = (parts[0].shape[0] // 2,) + parts[0].shape[1:]
    out = jax.ShapeDtypeStruct(shape, jnp.float32)
    vmem = pl.BlockSpec(memory_space=pltpu.VMEM)
    return pl.pallas_call(
        functools.partial(sum_kernel, len(parts)),
        in_specs=[vmem] * len(parts),
        out_specs=[vmem, vmem],
        out_shape=[out, out],
        compiler_params=params(),
        cost_estimate=cost(0.1),
        name="halves_summed",
    )(*parts)


def join_kernel(first_ref, second_ref, *refs):
    out_ref = refs[-1]
    count = first_ref.shape[0]
    out_ref[:count] = first_ref[...]
    out_ref[count:] = second_ref[...]


def join_call(first, second, *after):
    vmem = pl.BlockSpec(memory_space=pltpu.VMEM)
    return pl.pallas_call(
        join_kernel,
        in_specs=[vmem, vmem] + [pl.BlockSpec(memory_space=pl.ANY)] * len(after),
        out_shape=jax.ShapeDtypeStruct((2 * first.shape[0],) + first.shape[1:], jnp.float32),
        compiler_params=params(),
        cost_estimate=cost(1.0),
        name="reference_joined",
    )(first, second, *after)


def spread_line(line, keep):
    for g in range(0, LANES, 2 * SUBLANES):
        tiled = jnp.broadcast_to(line, (2 * SUBLANES, line.shape[1]))
        for h, value in enumerate(halves(pltpu.roll(tiled, g, 1, stride=1, stride_axis=0)[:, LANES:])):
            keep(h, g, value)


def table_kernel(tiles_ref, out_ref):
    for c in range(2):
        line = jnp.concatenate([tiles_ref[c, n : n + 1, :] for n in range(tiles_ref.shape[1])], 1)

        def keep(h, g, value):
            out_ref[h, c, g : g + 2 * SUBLANES] = value

        spread_line(line, keep)


def table_call(tiles):
    shape = (2, 2, LANES, LANES * (tiles.shape[1] - 1))
    return pl.pallas_call(
        table_kernel,
        out_shape=jax.ShapeDtypeStruct(shape, jnp.bfloat16),
        compiler_params=params(),
        cost_estimate=cost(0.7),
        name="shifted_reference",
    )(tiles)


def first_kernel(tiles_ref, *refs):
    *round_refs, out_ref = refs
    me = lax.axis_index("tm")
    for c in range(2):
        tails = [ref[ref.shape[0] - 1, c, ref.shape[2] - EDGE :, :] for ref in round_refs]
        before = jnp.where(me % 2 == 1, tails[0], jnp.where(me > 0, tails[-1], 0.0))
        line = jnp.concatenate([before[n : n + 1] for n in range(EDGE)] + [tiles_ref[c, 0:1, :]], 1)

        def keep(h, g, value):
            out_ref[h, c, g : g + 2 * SUBLANES] = value

        spread_line(line, keep)


def first_call(tiles, rounds):
    return pl.pallas_call(
        first_kernel,
        out_shape=jax.ShapeDtypeStruct((2, 2, LANES, 2 * LANES), jnp.bfloat16),
        compiler_params=params(),
        cost_estimate=cost(0.1),
        name="shifted_first",
    )(tiles, *rounds)


def lag_kernel(groups, part_count, *refs):
    y_refs, refs = refs[:part_count], refs[part_count:]
    table_ref, first_ref, _, out_hbm, out_ref, out_sem = refs
    copies = []

    def table_tile(h, n):
        parts = []
        for c in range(2):
            known = first_ref.shape[3] // LANES
            ref, at = (first_ref, n) if n < known else (table_ref, n - known)
            parts.append(ref[h, c, :, at * LANES : (at + 1) * LANES])
        return jnp.concatenate(parts, 1)

    def send(start, count):
        part = (slice(None), pl.ds(start, count))
        copies.append(pltpu.make_async_copy(out_ref.at[part], out_hbm.at[part], out_sem.at[len(copies)]))
        copies[-1].start()

    y = y_refs[0][...]
    for y_ref in y_refs[1:]:
        y = y + y_ref[...]
    rows, length = y.shape
    blocks = length // BLOCK_LEN
    turned = jnp.concatenate(
        [pltpu.roll(y[r : r + SUBLANES], SUBLANES // 2, 0) for r in range(0, rows, SUBLANES)], 0
    )
    turned = turned * row_sign(turned.shape)
    y_parts, t_parts = thirds(y), thirds(turned)

    def half_block(q, b):
        cols = slice(q * BLOCK_LEN + b * LANES, q * BLOCK_LEN + (b + 1) * LANES)
        return [jnp.concatenate([x[:, cols], t[:, cols]], 1) for x, t in zip(y_parts, t_parts)]

    def products(stack, n, count):
        tiles = [jnp.concatenate([table_tile(h, n + i) for i in range(count)], 0) for h in range(2)]
        product = dot_parts([jnp.concatenate(part, 0) for part in zip(*stack)], tiles, True)
        return [product[i * rows : (i + 1) * rows] for i in range(len(stack))]

    taps_sum = None
    (far,) = products([half_block(0, 0)], 0, 1)
    for q in range(blocks):
        stack = [half_block(q, 0), half_block(q, 1)]
        if q + 1 < blocks:
            stack.append(half_block(q + 1, 0))
        first, second, *after = products(stack, 2 * q + 1, 2)
        product = jnp.concatenate([first[:, :LANES] + second[:, LANES:], second[:, :LANES] + far], 1)
        if after:
            far = after[0][:, LANES:]
        taps = product[:, :LANES]
        taps_sum = taps if taps_sum is None else taps_sum + taps
        for h in range(LAGS // LANES):
            lanes = slice(h * LANES, (h + 1) * LANES)
            tiles = [product[r : r + SUBLANES, lanes] for r in range(0, rows, SUBLANES)]
            for j, tile in enumerate(swap_groups(tiles, groups)):
                out_ref[h * groups + j, q] = tile
        if q + 1 == blocks // 2:
            send(0, blocks // 2)
    left = lax.broadcasted_iota(jnp.int32, (SUBLANES, LANES), 1) < TAPS
    for i in range(groups // 2):
        a = taps_sum[i * SUBLANES : (i + 1) * SUBLANES]
        other = i + groups // 2
        b = taps_sum[other * SUBLANES : (other + 1) * SUBLANES]
        tile = jnp.where(left, a, pltpu.roll(b, LANES - TAPS, 1))
        for owner in range(out_ref.shape[0]):
            out_ref[owner, blocks + i] = tile
    send(blocks // 2, blocks - blocks // 2 + groups // 2)
    for copy in copies:
        copy.wait()


def lag_call(ys, table, first, after, groups, owners):
    blocks = ys[0].shape[1] // BLOCK_LEN
    shape = (owners, blocks + groups // 2, SUBLANES, LANES)
    vmem = pl.BlockSpec(memory_space=pltpu.VMEM)
    return pl.pallas_call(
        functools.partial(lag_kernel, groups, len(ys)),
        in_specs=[vmem] * (len(ys) + 2) + [pl.BlockSpec(memory_space=pl.ANY)],
        out_specs=pl.BlockSpec(memory_space=pltpu.HBM),
        out_shape=jax.ShapeDtypeStruct(shape, jnp.float32),
        scratch_shapes=[
            pltpu.VMEM(shape, jnp.float32),
            pltpu.SemaphoreType.DMA((2,)),
        ],
        compiler_params=params(),
        cost_estimate=cost(2.1),
        name="lag_products",
    )(*ys, table, first, after)


BATCH = 4


def own_kernel(lags_local, *refs):
    *part_refs, _, out_ref, line_ref, tail_ref, span_ref, late_ref, taps_a, lags_a, taps_b, lags_b = refs
    me = lax.axis_index("tm")
    part_rows = part_refs[0].shape[2]
    owners = sum(part_ref.shape[0] for part_ref in part_refs)
    samples = owners * part_rows * LANES
    steps = samples // BLOCK_LEN // BATCH
    total_rows = span_ref.shape[1]
    block_rows = BLOCK_LEN // LANES

    span_ref[...] = jnp.zeros_like(span_ref)
    n = 0
    for part_ref in part_refs:
        for i in range(part_ref.shape[0]):
            block = lax.rem(me - (n // 2) * 2 + owners, owners) ^ (n % 2)
            span_ref[:, pl.ds(EDGE + block * part_rows, part_rows), :] = part_ref[i]
            n += 1
    late_rows = (me * lags_local) // LANES
    late_lanes = lax.rem(me * lags_local, LANES)
    turned = [pltpu.roll(span_ref[c], late_lanes, 1) for c in range(2)]
    before = [pltpu.roll(x, 1, 0) for x in turned]
    lanes = lax.broadcasted_iota(jnp.int32, (total_rows, LANES), 1)
    for c in range(2):
        late_ref[c] = pltpu.roll(jnp.where(lanes < late_lanes, before[c], turned[c]), late_rows, 0)

    def line_of(ref, c, first, count):
        return jnp.concatenate([ref[c, pl.ds(first + n, 1), :] for n in range(count)], 1)

    def shifted(line, by):
        tiled = jnp.broadcast_to(line, (2 * SUBLANES, line.shape[1]))
        return pltpu.roll(tiled, by, 1, stride=1, stride_axis=0)[:, LANES:]

    def keep(ref, row, parts):
        step = ref.shape[0] // len(parts)
        for n, part in enumerate(parts):
            ref[n * step + row : n * step + row + 2 * SUBLANES, :] = part

    def build(n, taps_ref, lags_ref):
        first = EDGE - 1 + n * BATCH * block_rows
        count = BATCH * block_rows + 1
        lines = [line_of(span_ref, c, first, count) for c in range(2)]
        for c in range(2):
            for g in range(0, TAPS, 2 * SUBLANES):
                keep(taps_ref, c * TAPS + g, thirds(shifted(lines[c], g)))
            late = line_of(late_ref, c, first, count)
            for g in range(0, lags_local, 2 * SUBLANES):
                keep(lags_ref, c * lags_local + g, halves(shifted(late, g)))
        pad = jnp.zeros((2 * SUBLANES - 2, BATCH * BLOCK_LEN), jnp.float32)
        keep(lags_ref, 2 * lags_local, halves(jnp.concatenate([line[:, LANES:] for line in lines] + [pad], 0)))

    turn = lane_sign((lags_local, LANES))

    def use(n, taps_ref, lags_ref):
        count = lags_ref.shape[0] // 2
        for b in range(BATCH):
            cols = slice(b * BLOCK_LEN, (b + 1) * BLOCK_LEN)
            product = dot_nt(lags_ref[:, cols], taps_ref[: 2 * LANES, cols])
            least = dot_nt(lags_ref[:count, cols], taps_ref[2 * LANES :, cols]) + product[count:, LANES:]
            product = product[:count, :LANES] + ((product[:count, LANES:] + product[count:, :LANES]) + least)
            by_real = product[:lags_local]
            by_imag = product[lags_local : 2 * lags_local]
            rows = pl.ds(pl.multiple_of((n * BATCH + b) * lags_local, lags_local), lags_local)
            for part, value in enumerate(thirds(by_real + turn * pltpu.roll(by_imag, TAPS, 1))):
                out_ref[part, rows, :] = value
            line_ref[...] += product[2 * lags_local : 2 * lags_local + SUBLANES]

    line_ref[...] = jnp.zeros_like(line_ref)
    build(0, taps_a, lags_a)

    def pair(m, carry):
        build(2 * m + 1, taps_b, lags_b)
        use(2 * m, taps_a, lags_a)
        build(jnp.minimum(2 * m + 2, steps - 1), taps_a, lags_a)
        use(2 * m + 1, taps_b, lags_b)
        return carry

    lax.fori_loop(0, steps // 2, pair, 0)
    tail = []
    for c in range(2):
        line = line_of(span_ref, c, EDGE + owners * part_rows - 1, 2)
        tail += [shifted(line, g) for g in range(0, TAPS, 2 * SUBLANES)]
    tail = jnp.concatenate(tail, 0)
    tail_ref[...] = dot_nt(tail, tail, HIGHEST)


def own_call(parts, lags_local, after):
    part_rows = parts[0].shape[2]
    span_rows = part_rows * sum(part.shape[0] for part in parts)
    rows = span_rows * LANES // BLOCK_LEN * lags_local
    held_rows = -(-(span_rows + 2 * EDGE) // SUBLANES) * SUBLANES
    width = BATCH * BLOCK_LEN
    taps = pltpu.VMEM((6 * TAPS, width), jnp.bfloat16)
    lags = pltpu.VMEM((4 * lags_local + 4 * SUBLANES, width), jnp.bfloat16)
    span = pltpu.VMEM((2, held_rows, LANES), jnp.float32)
    return pl.pallas_call(
        functools.partial(own_kernel, lags_local),
        in_specs=[pl.BlockSpec(memory_space=pltpu.VMEM)] * len(parts) + [pl.BlockSpec(memory_space=pl.ANY)],
        out_shape=[
            jax.ShapeDtypeStruct((3, rows, 2 * TAPS), jnp.bfloat16),
            jax.ShapeDtypeStruct((SUBLANES, 2 * TAPS), jnp.float32),
            jax.ShapeDtypeStruct((2 * TAPS, 2 * TAPS), jnp.float32),
        ],
        scratch_shapes=[span, span, taps, lags, taps, lags],
        compiler_params=params(),
        cost_estimate=cost(6.2),
        name="reference_products",
    )(*parts, after)


def as_factor(a):
    return jnp.concatenate([a, -lane_sign(a.shape) * pltpu.roll(a, a.shape[0], 1)], 0)


def solver_kernel(line_ref, tail_ref, gram_ref, solver_ref):
    total = line_ref[...]
    line = total[0:1] + lane_sign((1, LANES)) * pltpu.roll(total[1:2], TAPS, 1)
    low = lax.broadcasted_iota(jnp.int32, (1, LANES), 1) < TAPS
    line_r = jnp.where(low, line, 0.0)
    line_i = jnp.where(low, pltpu.roll(line, TAPS, 1), 0.0)
    cols = lax.broadcasted_iota(jnp.int32, (TAPS, TAPS), 1)
    rows = lax.broadcasted_iota(jnp.int32, (TAPS, TAPS), 0)
    above = cols > rows

    def stack(ref, value):
        parts = thirds(value)
        for n, (_, part) in enumerate(PART_PAIRS):
            ref[n * value.shape[0] : (n + 1) * value.shape[0], :] = parts[part]

    def upper(x):
        spread = pltpu.roll(jnp.broadcast_to(x, (TAPS, LANES)), 0, 1, stride=1, stride_axis=0)
        return spread[:, :TAPS]

    up_r = upper(line_r)
    up_i = jnp.where(above, upper(line_i), 0.0)
    strict_r = jnp.where(above, up_r, 0.0)
    diag_r = jnp.where(cols == rows, up_r, 0.0)
    tails = tail_ref[...]
    gram_r = strict_r + strict_r.T + diag_r - (tails[:TAPS, :TAPS] + tails[TAPS:, TAPS:])
    gram_i = up_i - up_i.T - (tails[:TAPS, TAPS:] - tails[TAPS:, :TAPS])
    gram = jnp.concatenate([gram_r, gram_i], 1)
    gram_factor = as_factor(gram)
    stack(gram_ref, gram_factor)
    gram_halves = halves(gram_factor)
    one = (
        lax.broadcasted_iota(jnp.int32, gram.shape, 0) == lax.broadcasted_iota(jnp.int32, gram.shape, 1)
    ).astype(jnp.float32)
    bound = jnp.max(jnp.sum(jnp.abs(gram), axis=1, keepdims=True), axis=0, keepdims=True)

    def again(state):
        count, left, _ = state
        return (count < 60) & (left > 1e-3)

    def newton(state):
        count, _, x = state
        x_halves = halves(x)
        seen = dot_split(x_halves, gram_halves)
        left = jnp.max(jnp.abs(seen - one))
        x = 2.0 * x - dot_split(halves(seen), halves(as_factor(x)))
        return count + 1, left, x

    start = (jnp.int32(0), jnp.float32(1.0), one * (1.0 / bound))
    _, _, inverse = lax.while_loop(again, newton, start)
    seen = jnp.dot(inverse, gram_factor, precision=HIGHEST, preferred_element_type=jnp.float32)
    inverse = inverse + jnp.dot(
        one - seen, as_factor(inverse), precision=HIGHEST, preferred_element_type=jnp.float32
    )
    stack(solver_ref, as_factor(inverse))


def solver_call(line, tail):
    return pl.pallas_call(
        solver_kernel,
        out_shape=[jax.ShapeDtypeStruct((len(PART_PAIRS) * tail.shape[0], tail.shape[1]), jnp.bfloat16)] * 2,
        compiler_params=params(),
        cost_estimate=cost(2.0),
        name="gram_inverse",
    )(line, tail)


def doppler_table(block_count, scale):
    phase = (np.arange(block_count)[:, None] * np.arange(DOPPLER)[None, :] % DOPPLER) * (2.0 * math.pi / DOPPLER)
    cosine, sine = np.cos(phase), np.sin(phase)
    upper = np.concatenate([cosine, -sine], 1)
    lower = np.concatenate([sine, cosine], 1)
    return (np.concatenate([upper, lower], 0) * scale).astype(np.float32)


def map_kernel(groups, got_ref, own_ref, gram_ref, solver_ref, wave_ref, out_hbm, held_ref, out_ref, out_sem):
    owners, pieces = got_ref.shape[:2]
    blocks = pieces - groups // 2
    lags_local = LANES // groups
    total = owners * blocks
    left = lax.broadcasted_iota(jnp.int32, (SUBLANES, LANES), 1) < TAPS
    sign = row_sign((SUBLANES, LANES))
    rows = [None] * groups
    for i in range(groups // 2):
        tile = got_ref[0, blocks + i]
        for owner in range(1, owners):
            tile = tile + got_ref[owner, blocks + i]
        swapped = pltpu.roll(tile, TAPS, 1)
        for part, here, there in ((i, tile, swapped), (i + groups // 2, swapped, tile)):
            other = -sign * pltpu.roll(there, SUBLANES // 2, 0)
            rows[part] = jnp.where(left, here, other)
    cross = jnp.concatenate(rows, 0)

    def exact(x, ref):
        parts = thirds(x)
        return jnp.dot(
            jnp.concatenate([parts[part] for part, _ in PART_PAIRS], 1), ref[...], preferred_element_type=jnp.float32
        )

    taps = exact(cross, solver_ref)
    taps = taps + exact(cross - exact(taps, gram_ref), solver_ref)
    taps = thirds(taps)
    count = taps[0].shape[0]
    twice = [jnp.concatenate([part, part], 1) for part in taps[:2]]
    twice = jnp.concatenate(twice + [jnp.concatenate([taps[2], jnp.zeros_like(taps[2])], 1)], 0)
    for q in range(0, total, 2 * groups):
        own = slice(q * lags_local, (q + 2 * groups) * lags_local)
        by_part = dot_nt(twice, jnp.concatenate([own_ref[0, own, :], own_ref[1, own, :]], 1))
        least = by_part[2 * count :] + dot_nt(taps[0], own_ref[2, own, :])
        clutter = by_part[:count] + (by_part[count : 2 * count] + least)
        for h in range(2):
            lanes = slice(h * LANES, (h + 1) * LANES)
            tiles = [clutter[r : r + SUBLANES, lanes] for r in range(0, groups * SUBLANES, SUBLANES)]
            for j, tile in enumerate(swap_groups(tiles, groups)):
                at = q + h * groups + j
                held_ref[at * SUBLANES : (at + 1) * SUBLANES, :] = got_ref[at // blocks, at % blocks] - tile
    half = SUBLANES // 2
    wave = (wave_ref[0], wave_ref[1])
    copies = []
    for g in range(half):
        parts = [held_ref[pl.ds(c * half + g, total, stride=SUBLANES), :] for c in range(2)]
        spectrum = dot_split(halves(jnp.concatenate(parts, 0).T), wave)
        for i in range(groups):
            for c in range(2):
                out_ref[i, g, c] = spectrum[i * lags_local : (i + 1) * lags_local, c * DOPPLER : (c + 1) * DOPPLER]
        part = (slice(None), pl.ds(g, 1))
        copies.append(pltpu.make_async_copy(out_ref.at[part], out_hbm.at[part], out_sem.at[g]))
        copies[-1].start()
    for copy in copies:
        copy.wait()


def map_call(got, own, gram, solver, wave, groups, beams_local):
    total = got.shape[0] * (got.shape[1] - groups // 2)
    lags_local = LANES // groups
    half = SUBLANES // 2
    shape = (beams_local // half, half, 2, lags_local, DOPPLER)
    out = pl.pallas_call(
        functools.partial(map_kernel, groups),
        in_specs=[pl.BlockSpec(memory_space=pltpu.VMEM)] * 5,
        out_specs=pl.BlockSpec(memory_space=pltpu.HBM),
        out_shape=jax.ShapeDtypeStruct(shape, jnp.float32),
        scratch_shapes=[
            pltpu.VMEM((total * SUBLANES, LANES), jnp.float32),
            pltpu.VMEM(shape, jnp.float32),
            pltpu.SemaphoreType.DMA((half,)),
        ],
        compiler_params=params(),
        cost_estimate=cost(2.5),
        name="range_doppler",
    )(got, own, gram, solver, wave)
    return out.reshape((beams_local,) + shape[2:])


def swap(x, axis, by):
    pairs = [(i, i ^ by) for i in range(lax.axis_size(axis))]
    return lax.ppermute(x, axis, pairs)


def tiled_device(ref_signal, surveillance, steering):
    chan_count, tm_count = lax.axis_size("chan"), lax.axis_size("tm")
    channels, length = surveillance.shape[1:]
    beams_local = steering.shape[1] // chan_count
    lags_local = LAGS // tm_count
    groups = LANES // lags_local
    samples = length * tm_count

    survey = surveillance.reshape(2 * channels, length)
    kept, moved, tiles = beam_call(steering, survey, ref_signal, chan_count, beams_local)
    near = swap(tiles[None], "tm", 1)
    shape = (chan_count // 2, 2 * beams_local, length)
    kept, got = kept.reshape(shape), swap(moved, "chan", 1).reshape(shape)
    by = 2
    while by < chan_count:
        kept, moved = sum_call([kept, got])
        got = swap(moved, "chan", by)
        by *= 2
    rounds = [near]
    joined = join_call(tiles[None], near, moved)
    while True:
        count = joined.shape[0]
        rounds.append(lax.ppermute(joined, "tm", [(i, (i + count) % tm_count) for i in range(tm_count)]))
        if count * 2 == tm_count:
            break
        joined = join_call(joined, rounds[-1])
    table = table_call(tiles)
    first = first_call(tiles, rounds[:2])
    pieces = lag_call([kept[0], got[0]], table, first, joined, groups, tm_count)
    got = lax.all_to_all(pieces, "tm", 0, 0, tiled=True)
    own, line, tail = own_call([tiles[None]] + rounds, lags_local, pieces)
    gram, solver = solver_call(line, tail)
    wave = doppler_table(samples // BLOCK_LEN, 0.125 / math.sqrt(samples))
    high = wave.astype(jnp.bfloat16)
    wave = np.stack([high, (wave - high.astype(np.float32)).astype(jnp.bfloat16)])
    return map_call(got, own, gram, solver, jnp.asarray(wave), groups, beams_local)


def lag_table(ref_ext, offset, lags):
    window = lax.dynamic_slice_in_dim(ref_ext, offset, BLOCK_LEN + LAGS, 1)
    span = BLOCK_LEN + LAGS
    tiled = jnp.tile(jnp.pad(window, ((0, 0), (0, 1))), (1, lags))[:, : lags * span]
    return tiled.reshape(2, lags, span)[:, :, LAGS:]


def times_conj(a, b):
    real = jnp.einsum("...t,lt->...l", a[..., 0, :], b[0], precision=HIGHEST) + jnp.einsum(
        "...t,lt->...l", a[..., 1, :], b[1], precision=HIGHEST
    )
    imag = jnp.einsum("...t,lt->...l", a[..., 1, :], b[0], precision=HIGHEST) - jnp.einsum(
        "...t,lt->...l", a[..., 0, :], b[1], precision=HIGHEST
    )
    return jnp.stack([real, imag], -2)


def plain_device(ref_signal, surveillance, steering):
    chan_count, tm_count = lax.axis_size("chan"), lax.axis_size("tm")
    length = surveillance.shape[2]
    beams = steering.shape[1]
    lags_local = LAGS // tm_count
    samples = length * tm_count
    local_blocks = length // BLOCK_LEN
    here = lax.axis_index("tm")

    w_real, w_imag = steering
    real = jnp.dot(w_real, surveillance[0], precision=HIGHEST) - jnp.dot(w_imag, surveillance[1], precision=HIGHEST)
    imag = jnp.dot(w_imag, surveillance[0], precision=HIGHEST) + jnp.dot(w_real, surveillance[1], precision=HIGHEST)
    beam = lax.psum_scatter(jnp.stack([real, imag], 1), "chan", scatter_dimension=0, tiled=True)
    ref_all = lax.all_gather(ref_signal, "tm", axis=1, tiled=True)
    ref_ext = jnp.pad(ref_all, ((0, 0), (LAGS, 0)))

    def beam_step(carry, q):
        offset = q * BLOCK_LEN
        table = lag_table(ref_ext, here * length + offset, LAGS)
        segment = lax.dynamic_slice_in_dim(beam, offset, BLOCK_LEN, 2)
        return carry, times_conj(segment, table)

    _, products = lax.scan(beam_step, None, jnp.arange(local_blocks, dtype=jnp.int32))
    cross = lax.psum(products[..., :TAPS].sum(0), "tm")
    got = lax.all_to_all(products, "tm", 3, 0, tiled=True)

    def own_step(gram, q):
        offset = q * BLOCK_LEN
        table = lag_table(ref_ext, offset, LAGS)
        taps = table[:, :TAPS].transpose(1, 0, 2)
        mine = lax.dynamic_slice_in_dim(table, here * lags_local, lags_local, 1)
        return gram + times_conj(taps, table[:, :TAPS]), times_conj(taps, mine)

    start = jnp.zeros((TAPS, 2, TAPS), jnp.float32)
    gram, own = lax.scan(own_step, start, jnp.arange(samples // BLOCK_LEN, dtype=jnp.int32))
    g_real, g_imag = gram[:, 0].T, gram[:, 1].T
    system = jnp.concatenate([jnp.concatenate([g_real, -g_imag], 1), jnp.concatenate([g_imag, g_real], 1)], 0)
    right = jnp.concatenate([cross[:, 0].T, cross[:, 1].T], 0)
    solved = jax.scipy.linalg.cho_solve((jnp.linalg.cholesky(system), True), right)
    b_real, b_imag = solved[:TAPS].T, solved[TAPS:].T
    mixing = jnp.concatenate([jnp.stack([b_real, b_imag], 1), jnp.stack([-b_imag, b_real], 1)], 2)
    stacked = jnp.concatenate([own[:, :, 0], own[:, :, 1]], 1)
    lagged = got - jnp.einsum("mck,qkl->qmcl", mixing, stacked, precision=HIGHEST)
    wave = jnp.asarray(doppler_table(samples // BLOCK_LEN, 0.125 / math.sqrt(samples)))
    wave = wave.reshape(2, samples // BLOCK_LEN, 2, DOPPLER)
    return jnp.einsum("qmcl,cqdk->mdlk", lagged, wave, precision=HIGHEST)


def on_device(ref_signal, surveillance, steering):
    chan_count, tm_count = lax.axis_size("chan"), lax.axis_size("tm")
    beams_local = steering.shape[1] // chan_count
    lags_local = LAGS // tm_count
    fills = (
        LANES % lags_local == 0
        and lags_local % (2 * SUBLANES) == 0
        and beams_local * lags_local == LANES * SUBLANES // 2
        and chan_count > 1
        and chan_count & (chan_count - 1) == 0
        and tm_count > 2
        and tm_count & (tm_count - 1) == 0
        and 2 * surveillance.shape[1] % LANES == 0
        and surveillance.shape[2] % (2 * BATCH * BLOCK_LEN) == 0
    )
    device = tiled_device if fills else plain_device
    return device(ref_signal, surveillance, steering)


def solution(mesh):
    placed = (P(None, "tm"), P(None, "chan", "tm"), P(None, None, "chan"))
    return jax.shard_map(
        on_device,
        mesh=mesh,
        in_specs=placed,
        out_specs=P("chan", None, "tm", None),
        check_vma=False,
    )
```

```python
import functools
import math

import jax
import jax.numpy as jnp
import numpy as np
from jax import lax
from jax.experimental import pallas as pl
from jax.experimental.pallas import tpu as pltpu
from jax.sharding import PartitionSpec as P

LAGS = 256
DOPPLER = 256
TAPS = 64
BLOCK_LEN = 256
LANES = 128
SUBLANES = 8
EDGE = 2

HIGHEST = lax.Precision.HIGHEST
VMEM_BYTES = 48 * 1024 * 1024


def params():
    return pltpu.CompilerParams(vmem_limit_bytes=VMEM_BYTES)


def cost(us):
    return pl.CostEstimate(flops=int(us * 1.15e9), bytes_accessed=0, transcendentals=0)


def halves(x):
    high = x.astype(jnp.bfloat16)
    return high, (x - high.astype(jnp.float32)).astype(jnp.bfloat16)


def thirds(x):
    high = x.astype(jnp.bfloat16)
    rest = x - high.astype(jnp.float32)
    return (high,) + halves(rest)


PART_PAIRS = ((2, 0), (1, 1), (0, 2), (1, 0), (0, 1), (0, 0))


def dot_parts(a, b, across=False):
    rows = a[0].shape[0]
    by_size = {}
    for j, right in enumerate(b):
        left = a[: max(3 - j, 1)]
        left = left[0] if len(left) == 1 else jnp.concatenate(left, 0)
        contract = (((1,), (1 if across else 0,)), ((), ()))
        product = lax.dot_general(left, right, contract, preferred_element_type=jnp.float32)
        for i in range(product.shape[0] // rows):
            by_size.setdefault(i + j, []).append(product[i * rows : (i + 1) * rows])
    total = None
    for size in sorted(by_size, reverse=True):
        for term in by_size[size]:
            total = term if total is None else total + term
    return total


def dot_nt(a, b, precision=None):
    return lax.dot_general(
        a, b, (((1,), (1,)), ((), ())), precision=precision, preferred_element_type=jnp.float32
    )


def dot_split(a, b):
    (a_high, a_low), (b_high, b_low) = a, b
    left = jnp.concatenate([a_high, a_low], 1)
    right = jnp.concatenate([b_high, b_high], 0)
    return jnp.dot(left, right, preferred_element_type=jnp.float32) + jnp.dot(
        a_high, b_low, preferred_element_type=jnp.float32
    )


def row_sign(shape):
    rows = lax.broadcasted_iota(jnp.int32, shape, 0)
    return jnp.where(rows % SUBLANES < SUBLANES // 2, 1.0, -1.0).astype(jnp.float32)


def lane_sign(shape):
    lanes = lax.broadcasted_iota(jnp.int32, shape, 1)
    return jnp.where(lanes % LANES < LANES // 2, 1.0, -1.0).astype(jnp.float32)


def swap_groups(rows, groups):
    width = LANES // groups
    lane_group = lax.broadcasted_iota(jnp.int32, rows[0].shape, 1) // width
    outs = []
    for j in range(groups):
        out = rows[j]
        for i in range(groups):
            if i != j:
                moved = pltpu.roll(rows[i], (width * (i - j)) % LANES, 1)
                out = jnp.where(lane_group == i, moved, out)
        outs.append(out)
    return outs


COPIES = 2


def beam_kernel(
    chan_count, beams_local, w_hbm, s_hbm, ref_hbm, kept_ref, sent_ref, tiles_ref,
    w_ref, s_ref, ref_ref, w_sem, s_sem, ref_sem,
):
    me = lax.axis_index("chan")
    depth = s_hbm.shape[0] // COPIES
    w_copy = pltpu.make_async_copy(w_hbm, w_ref, w_sem)
    w_copy.start()
    ref_copy = pltpu.make_async_copy(ref_hbm, ref_ref, ref_sem)
    ref_copy.start()
    s_copies = []
    for n in range(COPIES):
        part = pl.ds(n * depth, depth)
        s_copies.append(pltpu.make_async_copy(s_hbm.at[part], s_ref.at[part], s_sem.at[n]))
        s_copies[n].start()
    half = SUBLANES // 2
    sub = lax.broadcasted_iota(jnp.int32, (SUBLANES, w_hbm.shape[2]), 0)
    top = sub < half
    w_copy.wait()
    rows = []
    for parity in range(2):
        for e in range(parity, chan_count, 2):
            base = (me ^ e) * beams_local
            for tile in range(beams_local // SUBLANES):
                start = pl.multiple_of(base + tile * SUBLANES, SUBLANES)
                wr = w_ref[0, pl.ds(start, SUBLANES), :]
                wi = w_ref[1, pl.ds(start, SUBLANES), :]
                wr_s = pltpu.roll(wr, half, 0)
                wi_s = pltpu.roll(wi, half, 0)
                first = [jnp.where(top, wr, wi_s), jnp.where(top, -wi, wr_s)]
                second = [jnp.where(top, wr_s, wi), jnp.where(top, -wi_s, wr)]
                rows.append(jnp.concatenate(first, 1))
                rows.append(jnp.concatenate(second, 1))
    weights = halves(jnp.concatenate(rows, 0))
    ref_copy.wait()
    for c in range(2):
        for n in range(tiles_ref.shape[1]):
            tiles_ref[c, n : n + 1, :] = ref_ref[c : c + 1, n * LANES : (n + 1) * LANES]
    for copy in s_copies:
        copy.wait()
    high, mid, low = thirds(s_ref[...])
    twice = jnp.concatenate([jnp.concatenate([part, part], 1) for part in weights], 0)
    product = jnp.dot(twice, jnp.concatenate([high, mid], 0), preferred_element_type=jnp.float32)
    least = jnp.dot(weights[0], low, preferred_element_type=jnp.float32)
    count = least.shape[0]
    product = product[:count] + (product[count:] + least)
    mid = product.shape[0] // 2
    kept_ref[...] = product[:mid]
    sent_ref[...] = product[mid:]


def beam_call(steering, survey, ref, chan_count, beams_local):
    depth, length = survey.shape
    rows = chan_count * beams_local
    tiles = (2, length // LANES, LANES)
    out = jax.ShapeDtypeStruct((rows, length), jnp.float32)
    hbm, vmem = pl.BlockSpec(memory_space=pltpu.HBM), pl.BlockSpec(memory_space=pltpu.VMEM)
    return pl.pallas_call(
        functools.partial(beam_kernel, chan_count, beams_local),
        in_specs=[hbm] * 3,
        out_specs=[vmem] * 3,
        out_shape=[
            out,
            out,
            jax.ShapeDtypeStruct(tiles, jnp.float32),
        ],
        scratch_shapes=[
            pltpu.VMEM(steering.shape, jnp.float32),
            pltpu.VMEM(survey.shape, jnp.float32),
            pltpu.VMEM(ref.shape, jnp.float32),
            pltpu.SemaphoreType.DMA,
            pltpu.SemaphoreType.DMA((COPIES,)),
            pltpu.SemaphoreType.DMA,
        ],
        compiler_params=params(),
        cost_estimate=cost(2.2),
        name="beams",
    )(*(pltpu.with_memory_space_constraint(x, pltpu.HBM) for x in (steering, survey, ref)))


def sum_kernel(count, *refs):
    kept_ref, sent_ref = refs[-2:]
    for n in range(kept_ref.shape[0]):
        for offset, out_ref in ((0, kept_ref), (1, sent_ref)):
            total = refs[0][2 * n + offset]
            for ref in refs[1:count]:
                total = total + ref[2 * n + offset]
            out_ref[n] = total


def sum_call(parts):
    shape = (parts[0].shape[0] // 2,) + parts[0].shape[1:]
    out = jax.ShapeDtypeStruct(shape, jnp.float32)
    vmem = pl.BlockSpec(memory_space=pltpu.VMEM)
    return pl.pallas_call(
        functools.partial(sum_kernel, len(parts)),
        in_specs=[vmem] * len(parts),
        out_specs=[vmem, vmem],
        out_shape=[out, out],
        compiler_params=params(),
        cost_estimate=cost(0.1),
        name="halves_summed",
    )(*parts)


def join_kernel(first_ref, second_ref, *refs):
    out_ref = refs[-1]
    count = first_ref.shape[0]
    out_ref[:count] = first_ref[...]
    out_ref[count:] = second_ref[...]


def join_call(first, second, *after):
    vmem = pl.BlockSpec(memory_space=pltpu.VMEM)
    return pl.pallas_call(
        join_kernel,
        in_specs=[vmem, vmem] + [pl.BlockSpec(memory_space=pl.ANY)] * len(after),
        out_shape=jax.ShapeDtypeStruct((2 * first.shape[0],) + first.shape[1:], jnp.float32),
        compiler_params=params(),
        cost_estimate=cost(1.0),
        name="reference_joined",
    )(first, second, *after)


def spread_line(line, keep):
    for g in range(0, LANES, 2 * SUBLANES):
        tiled = jnp.broadcast_to(line, (2 * SUBLANES, line.shape[1]))
        for h, value in enumerate(halves(pltpu.roll(tiled, g, 1, stride=1, stride_axis=0)[:, LANES:])):
            keep(h, g, value)


def table_kernel(tiles_ref, out_ref):
    for c in range(2):
        line = jnp.concatenate([tiles_ref[c, n : n + 1, :] for n in range(tiles_ref.shape[1])], 1)

        def keep(h, g, value):
            out_ref[h, c, g : g + 2 * SUBLANES] = value

        spread_line(line, keep)


def table_call(tiles):
    shape = (2, 2, LANES, LANES * (tiles.shape[1] - 1))
    return pl.pallas_call(
        table_kernel,
        out_shape=jax.ShapeDtypeStruct(shape, jnp.bfloat16),
        compiler_params=params(),
        cost_estimate=cost(0.7),
        name="shifted_reference",
    )(tiles)


def first_kernel(tiles_ref, *refs):
    *round_refs, out_ref = refs
    me = lax.axis_index("tm")
    for c in range(2):
        tails = [ref[ref.shape[0] - 1, c, ref.shape[2] - EDGE :, :] for ref in round_refs]
        before = jnp.where(me % 2 == 1, tails[0], jnp.where(me > 0, tails[-1], 0.0))
        line = jnp.concatenate([before[n : n + 1] for n in range(EDGE)] + [tiles_ref[c, 0:1, :]], 1)

        def keep(h, g, value):
            out_ref[h, c, g : g + 2 * SUBLANES] = value

        spread_line(line, keep)


def first_call(tiles, rounds):
    return pl.pallas_call(
        first_kernel,
        out_shape=jax.ShapeDtypeStruct((2, 2, LANES, 2 * LANES), jnp.bfloat16),
        compiler_params=params(),
        cost_estimate=cost(0.1),
        name="shifted_first",
    )(tiles, *rounds)


def lag_kernel(groups, part_count, *refs):
    y_refs, refs = refs[:part_count], refs[part_count:]
    table_ref, first_ref, _, out_hbm, out_ref, out_sem = refs
    copies = []

    def table_tile(h, n):
        parts = []
        for c in range(2):
            known = first_ref.shape[3] // LANES
            ref, at = (first_ref, n) if n < known else (table_ref, n - known)
            parts.append(ref[h, c, :, at * LANES : (at + 1) * LANES])
        return jnp.concatenate(parts, 1)

    def send(start, count):
        part = (slice(None), pl.ds(start, count))
        copies.append(pltpu.make_async_copy(out_ref.at[part], out_hbm.at[part], out_sem.at[len(copies)]))
        copies[-1].start()

    y = y_refs[0][...]
    for y_ref in y_refs[1:]:
        y = y + y_ref[...]
    rows, length = y.shape
    blocks = length // BLOCK_LEN
    turned = jnp.concatenate(
        [pltpu.roll(y[r : r + SUBLANES], SUBLANES // 2, 0) for r in range(0, rows, SUBLANES)], 0
    )
    turned = turned * row_sign(turned.shape)
    y_parts, t_parts = thirds(y), thirds(turned)

    def half_block(q, b):
        cols = slice(q * BLOCK_LEN + b * LANES, q * BLOCK_LEN + (b + 1) * LANES)
        return [jnp.concatenate([x[:, cols], t[:, cols]], 1) for x, t in zip(y_parts, t_parts)]

    def products(stack, n, count):
        tiles = [jnp.concatenate([table_tile(h, n + i) for i in range(count)], 0) for h in range(2)]
        product = dot_parts([jnp.concatenate(part, 0) for part in zip(*stack)], tiles, True)
        return [product[i * rows : (i + 1) * rows] for i in range(len(stack))]

    taps_sum = None
    (far,) = products([half_block(0, 0)], 0, 1)
    for q in range(blocks):
        stack = [half_block(q, 0), half_block(q, 1)]
        if q + 1 < blocks:
            stack.append(half_block(q + 1, 0))
        first, second, *after = products(stack, 2 * q + 1, 2)
        product = jnp.concatenate([first[:, :LANES] + second[:, LANES:], second[:, :LANES] + far], 1)
        if after:
            far = after[0][:, LANES:]
        taps = product[:, :LANES]
        taps_sum = taps if taps_sum is None else taps_sum + taps
        for h in range(LAGS // LANES):
            lanes = slice(h * LANES, (h + 1) * LANES)
            tiles = [product[r : r + SUBLANES, lanes] for r in range(0, rows, SUBLANES)]
            for j, tile in enumerate(swap_groups(tiles, groups)):
                out_ref[h * groups + j, q] = tile
        if q + 1 == blocks // 2:
            send(0, blocks // 2)
    left = lax.broadcasted_iota(jnp.int32, (SUBLANES, LANES), 1) < TAPS
    for i in range(groups // 2):
        a = taps_sum[i * SUBLANES : (i + 1) * SUBLANES]
        other = i + groups // 2
        b = taps_sum[other * SUBLANES : (other + 1) * SUBLANES]
        tile = jnp.where(left, a, pltpu.roll(b, LANES - TAPS, 1))
        for owner in range(out_ref.shape[0]):
            out_ref[owner, blocks + i] = tile
    send(blocks // 2, blocks - blocks // 2 + groups // 2)
    for copy in copies:
        copy.wait()


def lag_call(ys, table, first, after, groups, owners):
    blocks = ys[0].shape[1] // BLOCK_LEN
    shape = (owners, blocks + groups // 2, SUBLANES, LANES)
    vmem = pl.BlockSpec(memory_space=pltpu.VMEM)
    return pl.pallas_call(
        functools.partial(lag_kernel, groups, len(ys)),
        in_specs=[vmem] * (len(ys) + 2) + [pl.BlockSpec(memory_space=pl.ANY)],
        out_specs=pl.BlockSpec(memory_space=pltpu.HBM),
        out_shape=jax.ShapeDtypeStruct(shape, jnp.float32),
        scratch_shapes=[
            pltpu.VMEM(shape, jnp.float32),
            pltpu.SemaphoreType.DMA((2,)),
        ],
        compiler_params=params(),
        cost_estimate=cost(2.1),
        name="lag_products",
    )(*ys, table, first, after)


BATCH = 4


def own_kernel(lags_local, *refs):
    *part_refs, _, out_ref, line_ref, tail_ref, span_ref, late_ref, taps_a, lags_a, taps_b, lags_b = refs
    me = lax.axis_index("tm")
    part_rows = part_refs[0].shape[2]
    owners = sum(part_ref.shape[0] for part_ref in part_refs)
    samples = owners * part_rows * LANES
    steps = samples // BLOCK_LEN // BATCH
    total_rows = span_ref.shape[1]
    block_rows = BLOCK_LEN // LANES

    span_ref[...] = jnp.zeros_like(span_ref)
    n = 0
    for part_ref in part_refs:
        for i in range(part_ref.shape[0]):
            block = lax.rem(me - (n // 2) * 2 + owners, owners) ^ (n % 2)
            span_ref[:, pl.ds(EDGE + block * part_rows, part_rows), :] = part_ref[i]
            n += 1
    late_rows = (me * lags_local) // LANES
    late_lanes = lax.rem(me * lags_local, LANES)
    turned = [pltpu.roll(span_ref[c], late_lanes, 1) for c in range(2)]
    before = [pltpu.roll(x, 1, 0) for x in turned]
    lanes = lax.broadcasted_iota(jnp.int32, (total_rows, LANES), 1)
    for c in range(2):
        late_ref[c] = pltpu.roll(jnp.where(lanes < late_lanes, before[c], turned[c]), late_rows, 0)

    def line_of(ref, c, first, count):
        return jnp.concatenate([ref[c, pl.ds(first + n, 1), :] for n in range(count)], 1)

    def shifted(line, by):
        tiled = jnp.broadcast_to(line, (2 * SUBLANES, line.shape[1]))
        return pltpu.roll(tiled, by, 1, stride=1, stride_axis=0)[:, LANES:]

    def keep(ref, row, parts):
        step = ref.shape[0] // len(parts)
        for n, part in enumerate(parts):
            ref[n * step + row : n * step + row + 2 * SUBLANES, :] = part

    def build(n, taps_ref, lags_ref):
        first = EDGE - 1 + n * BATCH * block_rows
        count = BATCH * block_rows + 1
        lines = [line_of(span_ref, c, first, count) for c in range(2)]
        for c in range(2):
            for g in range(0, TAPS, 2 * SUBLANES):
                keep(taps_ref, c * TAPS + g, thirds(shifted(lines[c], g)))
            late = line_of(late_ref, c, first, count)
            for g in range(0, lags_local, 2 * SUBLANES):
                keep(lags_ref, c * lags_local + g, halves(shifted(late, g)))
        pad = jnp.zeros((2 * SUBLANES - 2, BATCH * BLOCK_LEN), jnp.float32)
        keep(lags_ref, 2 * lags_local, halves(jnp.concatenate([line[:, LANES:] for line in lines] + [pad], 0)))

    turn = lane_sign((lags_local, LANES))

    def use(n, taps_ref, lags_ref):
        count = lags_ref.shape[0] // 2
        for b in range(BATCH):
            cols = slice(b * BLOCK_LEN, (b + 1) * BLOCK_LEN)
            product = dot_nt(lags_ref[:, cols], taps_ref[: 2 * LANES, cols])
            least = dot_nt(lags_ref[:count, cols], taps_ref[2 * LANES :, cols]) + product[count:, LANES:]
            product = product[:count, :LANES] + ((product[:count, LANES:] + product[count:, :LANES]) + least)
            by_real = product[:lags_local]
            by_imag = product[lags_local : 2 * lags_local]
            rows = pl.ds(pl.multiple_of((n * BATCH + b) * lags_local, lags_local), lags_local)
            for part, value in enumerate(thirds(by_real + turn * pltpu.roll(by_imag, TAPS, 1))):
                out_ref[part, rows, :] = value
            line_ref[...] += product[2 * lags_local : 2 * lags_local + SUBLANES]

    line_ref[...] = jnp.zeros_like(line_ref)
    build(0, taps_a, lags_a)

    def pair(m, carry):
        build(2 * m + 1, taps_b, lags_b)
        use(2 * m, taps_a, lags_a)
        build(jnp.minimum(2 * m + 2, steps - 1), taps_a, lags_a)
        use(2 * m + 1, taps_b, lags_b)
        return carry

    lax.fori_loop(0, steps // 2, pair, 0)
    tail = []
    for c in range(2):
        line = line_of(span_ref, c, EDGE + owners * part_rows - 1, 2)
        tail += [shifted(line, g) for g in range(0, TAPS, 2 * SUBLANES)]
    tail = jnp.concatenate(tail, 0)
    tail_ref[...] = dot_nt(tail, tail, HIGHEST)


def own_call(parts, lags_local, after):
    part_rows = parts[0].shape[2]
    span_rows = part_rows * sum(part.shape[0] for part in parts)
    rows = span_rows * LANES // BLOCK_LEN * lags_local
    held_rows = -(-(span_rows + 2 * EDGE) // SUBLANES) * SUBLANES
    width = BATCH * BLOCK_LEN
    taps = pltpu.VMEM((6 * TAPS, width), jnp.bfloat16)
    lags = pltpu.VMEM((4 * lags_local + 4 * SUBLANES, width), jnp.bfloat16)
    span = pltpu.VMEM((2, held_rows, LANES), jnp.float32)
    return pl.pallas_call(
        functools.partial(own_kernel, lags_local),
        in_specs=[pl.BlockSpec(memory_space=pltpu.VMEM)] * len(parts) + [pl.BlockSpec(memory_space=pl.ANY)],
        out_shape=[
            jax.ShapeDtypeStruct((3, rows, 2 * TAPS), jnp.bfloat16),
            jax.ShapeDtypeStruct((SUBLANES, 2 * TAPS), jnp.float32),
            jax.ShapeDtypeStruct((2 * TAPS, 2 * TAPS), jnp.float32),
        ],
        scratch_shapes=[span, span, taps, lags, taps, lags],
        compiler_params=params(),
        cost_estimate=cost(6.2),
        name="reference_products",
    )(*parts, after)


def as_factor(a):
    return jnp.concatenate([a, -lane_sign(a.shape) * pltpu.roll(a, a.shape[0], 1)], 0)


def solver_kernel(line_ref, tail_ref, gram_ref, solver_ref):
    total = line_ref[...]
    line = total[0:1] + lane_sign((1, LANES)) * pltpu.roll(total[1:2], TAPS, 1)
    low = lax.broadcasted_iota(jnp.int32, (1, LANES), 1) < TAPS
    line_r = jnp.where(low, line, 0.0)
    line_i = jnp.where(low, pltpu.roll(line, TAPS, 1), 0.0)
    cols = lax.broadcasted_iota(jnp.int32, (TAPS, TAPS), 1)
    rows = lax.broadcasted_iota(jnp.int32, (TAPS, TAPS), 0)
    above = cols > rows

    def stack(ref, value):
        parts = thirds(value)
        for n, (_, part) in enumerate(PART_PAIRS):
            ref[n * value.shape[0] : (n + 1) * value.shape[0], :] = parts[part]

    def upper(x):
        spread = pltpu.roll(jnp.broadcast_to(x, (TAPS, LANES)), 0, 1, stride=1, stride_axis=0)
        return spread[:, :TAPS]

    up_r = upper(line_r)
    up_i = jnp.where(above, upper(line_i), 0.0)
    strict_r = jnp.where(above, up_r, 0.0)
    diag_r = jnp.where(cols == rows, up_r, 0.0)
    tails = tail_ref[...]
    gram_r = strict_r + strict_r.T + diag_r - (tails[:TAPS, :TAPS] + tails[TAPS:, TAPS:])
    gram_i = up_i - up_i.T - (tails[:TAPS, TAPS:] - tails[TAPS:, :TAPS])
    gram = jnp.concatenate([gram_r, gram_i], 1)
    gram_factor = as_factor(gram)
    stack(gram_ref, gram_factor)
    gram_halves = halves(gram_factor)
    one = (
        lax.broadcasted_iota(jnp.int32, gram.shape, 0) == lax.broadcasted_iota(jnp.int32, gram.shape, 1)
    ).astype(jnp.float32)
    bound = jnp.max(jnp.sum(jnp.abs(gram), axis=1, keepdims=True), axis=0, keepdims=True)

    def again(state):
        count, left, _ = state
        return (count < 60) & (left > 1e-3)

    def newton(state):
        count, _, x = state
        x_halves = halves(x)
        seen = dot_split(x_halves, gram_halves)
        left = jnp.max(jnp.abs(seen - one))
        x = 2.0 * x - dot_split(halves(seen), halves(as_factor(x)))
        return count + 1, left, x

    start = (jnp.int32(0), jnp.float32(1.0), one * (1.0 / bound))
    _, _, inverse = lax.while_loop(again, newton, start)
    seen = jnp.dot(inverse, gram_factor, precision=HIGHEST, preferred_element_type=jnp.float32)
    inverse = inverse + jnp.dot(
        one - seen, as_factor(inverse), precision=HIGHEST, preferred_element_type=jnp.float32
    )
    stack(solver_ref, as_factor(inverse))


def solver_call(line, tail):
    return pl.pallas_call(
        solver_kernel,
        out_shape=[jax.ShapeDtypeStruct((len(PART_PAIRS) * tail.shape[0], tail.shape[1]), jnp.bfloat16)] * 2,
        compiler_params=params(),
        cost_estimate=cost(2.0),
        name="gram_inverse",
    )(line, tail)


def doppler_table(block_count, scale):
    phase = (np.arange(block_count)[:, None] * np.arange(DOPPLER)[None, :] % DOPPLER) * (2.0 * math.pi / DOPPLER)
    cosine, sine = np.cos(phase), np.sin(phase)
    upper = np.concatenate([cosine, -sine], 1)
    lower = np.concatenate([sine, cosine], 1)
    return (np.concatenate([upper, lower], 0) * scale).astype(np.float32)


def map_kernel(groups, got_ref, own_ref, gram_ref, solver_ref, wave_ref, out_hbm, held_ref, out_ref, out_sem):
    owners, pieces = got_ref.shape[:2]
    blocks = pieces - groups // 2
    lags_local = LANES // groups
    total = owners * blocks
    left = lax.broadcasted_iota(jnp.int32, (SUBLANES, LANES), 1) < TAPS
    sign = row_sign((SUBLANES, LANES))
    rows = [None] * groups
    for i in range(groups // 2):
        tile = got_ref[0, blocks + i]
        for owner in range(1, owners):
            tile = tile + got_ref[owner, blocks + i]
        swapped = pltpu.roll(tile, TAPS, 1)
        for part, here, there in ((i, tile, swapped), (i + groups // 2, swapped, tile)):
            other = -sign * pltpu.roll(there, SUBLANES // 2, 0)
            rows[part] = jnp.where(left, here, other)
    cross = jnp.concatenate(rows, 0)

    def exact(x, ref):
        parts = thirds(x)
        return jnp.dot(
            jnp.concatenate([parts[part] for part, _ in PART_PAIRS], 1), ref[...], preferred_element_type=jnp.float32
        )

    taps = exact(cross, solver_ref)
    taps = taps + exact(cross - exact(taps, gram_ref), solver_ref)
    taps = thirds(taps)
    count = taps[0].shape[0]
    twice = [jnp.concatenate([part, part], 1) for part in taps[:2]]
    twice = jnp.concatenate(twice + [jnp.concatenate([taps[2], jnp.zeros_like(taps[2])], 1)], 0)
    for q in range(0, total, 2 * groups):
        own = slice(q * lags_local, (q + 2 * groups) * lags_local)
        by_part = dot_nt(twice, jnp.concatenate([own_ref[0, own, :], own_ref[1, own, :]], 1))
        least = by_part[2 * count :] + dot_nt(taps[0], own_ref[2, own, :])
        clutter = by_part[:count] + (by_part[count : 2 * count] + least)
        for h in range(2):
            lanes = slice(h * LANES, (h + 1) * LANES)
            tiles = [clutter[r : r + SUBLANES, lanes] for r in range(0, groups * SUBLANES, SUBLANES)]
            for j, tile in enumerate(swap_groups(tiles, groups)):
                at = q + h * groups + j
                held_ref[at * SUBLANES : (at + 1) * SUBLANES, :] = got_ref[at // blocks, at % blocks] - tile
    half = SUBLANES // 2
    copies = []
    for g in range(half):
        parts = [held_ref[pl.ds(c * half + g, total, stride=SUBLANES), :] for c in range(2)]
        high, low = halves(jnp.concatenate(parts, 0).T)
        spectrum = jnp.dot(jnp.concatenate([high, high], 1), wave_ref[...], preferred_element_type=jnp.float32)
        spectrum = spectrum + jnp.dot(low, wave_ref[: low.shape[1]], preferred_element_type=jnp.float32)
        for i in range(groups):
            for c in range(2):
                out_ref[i, g, c] = spectrum[i * lags_local : (i + 1) * lags_local, c * DOPPLER : (c + 1) * DOPPLER]
        part = (slice(None), pl.ds(g, 1))
        copies.append(pltpu.make_async_copy(out_ref.at[part], out_hbm.at[part], out_sem.at[g]))
        copies[-1].start()
    for copy in copies:
        copy.wait()


def map_call(got, own, gram, solver, wave, groups, beams_local):
    total = got.shape[0] * (got.shape[1] - groups // 2)
    lags_local = LANES // groups
    half = SUBLANES // 2
    shape = (beams_local // half, half, 2, lags_local, DOPPLER)
    out = pl.pallas_call(
        functools.partial(map_kernel, groups),
        in_specs=[pl.BlockSpec(memory_space=pltpu.VMEM)] * 5,
        out_specs=pl.BlockSpec(memory_space=pltpu.HBM),
        out_shape=jax.ShapeDtypeStruct(shape, jnp.float32),
        scratch_shapes=[
            pltpu.VMEM((total * SUBLANES, LANES), jnp.float32),
            pltpu.VMEM(shape, jnp.float32),
            pltpu.SemaphoreType.DMA((half,)),
        ],
        compiler_params=params(),
        cost_estimate=cost(2.5),
        name="range_doppler",
    )(got, own, gram, solver, wave)
    return out.reshape((beams_local,) + shape[2:])


def swap(x, axis, by):
    pairs = [(i, i ^ by) for i in range(lax.axis_size(axis))]
    return lax.ppermute(x, axis, pairs)


def tiled_device(ref_signal, surveillance, steering):
    chan_count, tm_count = lax.axis_size("chan"), lax.axis_size("tm")
    channels, length = surveillance.shape[1:]
    beams_local = steering.shape[1] // chan_count
    lags_local = LAGS // tm_count
    groups = LANES // lags_local
    samples = length * tm_count

    survey = surveillance.reshape(2 * channels, length)
    kept, moved, tiles = beam_call(steering, survey, ref_signal, chan_count, beams_local)
    near = swap(tiles[None], "tm", 1)
    shape = (chan_count // 2, 2 * beams_local, length)
    kept, got = kept.reshape(shape), swap(moved, "chan", 1).reshape(shape)
    by = 2
    while by < chan_count:
        kept, moved = sum_call([kept, got])
        got = swap(moved, "chan", by)
        by *= 2
    rounds = [near]
    joined = join_call(tiles[None], near, moved)
    while True:
        count = joined.shape[0]
        rounds.append(lax.ppermute(joined, "tm", [(i, (i + count) % tm_count) for i in range(tm_count)]))
        if count * 2 == tm_count:
            break
        joined = join_call(joined, rounds[-1])
    table = table_call(tiles)
    first = first_call(tiles, rounds[:2])
    pieces = lag_call([kept[0], got[0]], table, first, joined, groups, tm_count)
    got = lax.all_to_all(pieces, "tm", 0, 0, tiled=True)
    own, line, tail = own_call([tiles[None]] + rounds, lags_local, pieces)
    gram, solver = solver_call(line, tail)
    wave = doppler_table(samples // BLOCK_LEN, 0.125 / math.sqrt(samples))
    high = wave.astype(jnp.bfloat16)
    wave = np.concatenate([high, (wave - high.astype(np.float32)).astype(jnp.bfloat16)], 0)
    return map_call(got, own, gram, solver, jnp.asarray(wave), groups, beams_local)


def lag_table(ref_ext, offset, lags):
    window = lax.dynamic_slice_in_dim(ref_ext, offset, BLOCK_LEN + LAGS, 1)
    span = BLOCK_LEN + LAGS
    tiled = jnp.tile(jnp.pad(window, ((0, 0), (0, 1))), (1, lags))[:, : lags * span]
    return tiled.reshape(2, lags, span)[:, :, LAGS:]


def times_conj(a, b):
    real = jnp.einsum("...t,lt->...l", a[..., 0, :], b[0], precision=HIGHEST) + jnp.einsum(
        "...t,lt->...l", a[..., 1, :], b[1], precision=HIGHEST
    )
    imag = jnp.einsum("...t,lt->...l", a[..., 1, :], b[0], precision=HIGHEST) - jnp.einsum(
        "...t,lt->...l", a[..., 0, :], b[1], precision=HIGHEST
    )
    return jnp.stack([real, imag], -2)


def plain_device(ref_signal, surveillance, steering):
    chan_count, tm_count = lax.axis_size("chan"), lax.axis_size("tm")
    length = surveillance.shape[2]
    beams = steering.shape[1]
    lags_local = LAGS // tm_count
    samples = length * tm_count
    local_blocks = length // BLOCK_LEN
    here = lax.axis_index("tm")

    w_real, w_imag = steering
    real = jnp.dot(w_real, surveillance[0], precision=HIGHEST) - jnp.dot(w_imag, surveillance[1], precision=HIGHEST)
    imag = jnp.dot(w_imag, surveillance[0], precision=HIGHEST) + jnp.dot(w_real, surveillance[1], precision=HIGHEST)
    beam = lax.psum_scatter(jnp.stack([real, imag], 1), "chan", scatter_dimension=0, tiled=True)
    ref_all = lax.all_gather(ref_signal, "tm", axis=1, tiled=True)
    ref_ext = jnp.pad(ref_all, ((0, 0), (LAGS, 0)))

    def beam_step(carry, q):
        offset = q * BLOCK_LEN
        table = lag_table(ref_ext, here * length + offset, LAGS)
        segment = lax.dynamic_slice_in_dim(beam, offset, BLOCK_LEN, 2)
        return carry, times_conj(segment, table)

    _, products = lax.scan(beam_step, None, jnp.arange(local_blocks, dtype=jnp.int32))
    cross = lax.psum(products[..., :TAPS].sum(0), "tm")
    got = lax.all_to_all(products, "tm", 3, 0, tiled=True)

    def own_step(gram, q):
        offset = q * BLOCK_LEN
        table = lag_table(ref_ext, offset, LAGS)
        taps = table[:, :TAPS].transpose(1, 0, 2)
        mine = lax.dynamic_slice_in_dim(table, here * lags_local, lags_local, 1)
        return gram + times_conj(taps, table[:, :TAPS]), times_conj(taps, mine)

    start = jnp.zeros((TAPS, 2, TAPS), jnp.float32)
    gram, own = lax.scan(own_step, start, jnp.arange(samples // BLOCK_LEN, dtype=jnp.int32))
    g_real, g_imag = gram[:, 0].T, gram[:, 1].T
    system = jnp.concatenate([jnp.concatenate([g_real, -g_imag], 1), jnp.concatenate([g_imag, g_real], 1)], 0)
    right = jnp.concatenate([cross[:, 0].T, cross[:, 1].T], 0)
    solved = jax.scipy.linalg.cho_solve((jnp.linalg.cholesky(system), True), right)
    b_real, b_imag = solved[:TAPS].T, solved[TAPS:].T
    mixing = jnp.concatenate([jnp.stack([b_real, b_imag], 1), jnp.stack([-b_imag, b_real], 1)], 2)
    stacked = jnp.concatenate([own[:, :, 0], own[:, :, 1]], 1)
    lagged = got - jnp.einsum("mck,qkl->qmcl", mixing, stacked, precision=HIGHEST)
    wave = jnp.asarray(doppler_table(samples // BLOCK_LEN, 0.125 / math.sqrt(samples)))
    wave = wave.reshape(2, samples // BLOCK_LEN, 2, DOPPLER)
    return jnp.einsum("qmcl,cqdk->mdlk", lagged, wave, precision=HIGHEST)


def on_device(ref_signal, surveillance, steering):
    chan_count, tm_count = lax.axis_size("chan"), lax.axis_size("tm")
    beams_local = steering.shape[1] // chan_count
    lags_local = LAGS // tm_count
    fills = (
        LANES % lags_local == 0
        and lags_local % (2 * SUBLANES) == 0
        and beams_local * lags_local == LANES * SUBLANES // 2
        and chan_count > 1
        and chan_count & (chan_count - 1) == 0
        and tm_count > 2
        and tm_count & (tm_count - 1) == 0
        and 2 * surveillance.shape[1] % LANES == 0
        and surveillance.shape[2] % (2 * BATCH * BLOCK_LEN) == 0
    )
    device = tiled_device if fills else plain_device
    return device(ref_signal, surveillance, steering)


def solution(mesh):
    placed = (P(None, "tm"), P(None, "chan", "tm"), P(None, None, "chan"))
    return jax.shard_map(
        on_device,
        mesh=mesh,
        in_specs=placed,
        out_specs=P("chan", None, "tm", None),
        check_vma=False,
    )
```

```python
import functools
import math

import jax
import jax.numpy as jnp
import numpy as np
from jax import lax
from jax.experimental import pallas as pl
from jax.experimental.pallas import tpu as pltpu
from jax.sharding import PartitionSpec as P

LAGS = 256
DOPPLER = 256
TAPS = 64
BLOCK_LEN = 256
LANES = 128
SUBLANES = 8
EDGE = 2

HIGHEST = lax.Precision.HIGHEST
VMEM_BYTES = 48 * 1024 * 1024


def params():
    return pltpu.CompilerParams(vmem_limit_bytes=VMEM_BYTES)


def cost(us):
    return pl.CostEstimate(flops=int(us * 1.15e9), bytes_accessed=0, transcendentals=0)


def halves(x):
    high = x.astype(jnp.bfloat16)
    return high, (x - high.astype(jnp.float32)).astype(jnp.bfloat16)


def thirds(x):
    high = x.astype(jnp.bfloat16)
    rest = x - high.astype(jnp.float32)
    return (high,) + halves(rest)


PART_PAIRS = ((2, 0), (1, 1), (0, 2), (1, 0), (0, 1), (0, 0))


def dot_parts(a, b, across=False):
    rows = a[0].shape[0]
    by_size = {}
    for j, right in enumerate(b):
        left = a[: max(3 - j, 1)]
        left = left[0] if len(left) == 1 else jnp.concatenate(left, 0)
        contract = (((1,), (1 if across else 0,)), ((), ()))
        product = lax.dot_general(left, right, contract, preferred_element_type=jnp.float32)
        for i in range(product.shape[0] // rows):
            by_size.setdefault(i + j, []).append(product[i * rows : (i + 1) * rows])
    total = None
    for size in sorted(by_size, reverse=True):
        for term in by_size[size]:
            total = term if total is None else total + term
    return total


def dot_nt(a, b, precision=None):
    return lax.dot_general(
        a, b, (((1,), (1,)), ((), ())), precision=precision, preferred_element_type=jnp.float32
    )


def dot_split(a, b):
    (a_high, a_low), (b_high, b_low) = a, b
    left = jnp.concatenate([a_high, a_low], 1)
    right = jnp.concatenate([b_high, b_high], 0)
    return jnp.dot(left, right, preferred_element_type=jnp.float32) + jnp.dot(
        a_high, b_low, preferred_element_type=jnp.float32
    )


def row_sign(shape):
    rows = lax.broadcasted_iota(jnp.int32, shape, 0)
    return jnp.where(rows % SUBLANES < SUBLANES // 2, 1.0, -1.0).astype(jnp.float32)


def lane_sign(shape):
    lanes = lax.broadcasted_iota(jnp.int32, shape, 1)
    return jnp.where(lanes % LANES < LANES // 2, 1.0, -1.0).astype(jnp.float32)


def swap_groups(rows, groups):
    width = LANES // groups
    lane_group = lax.broadcasted_iota(jnp.int32, rows[0].shape, 1) // width
    outs = []
    for j in range(groups):
        out = rows[j]
        for i in range(groups):
            if i != j:
                moved = pltpu.roll(rows[i], (width * (i - j)) % LANES, 1)
                out = jnp.where(lane_group == i, moved, out)
        outs.append(out)
    return outs


COPIES = 2


def beam_kernel(
    chan_count, beams_local, w_hbm, s_hbm, ref_hbm, kept_ref, sent_ref, tiles_ref,
    w_ref, s_ref, ref_ref, w_sem, s_sem, ref_sem,
):
    me = lax.axis_index("chan")
    depth = s_hbm.shape[0] // COPIES
    w_copy = pltpu.make_async_copy(w_hbm, w_ref, w_sem)
    w_copy.start()
    ref_copy = pltpu.make_async_copy(ref_hbm, ref_ref, ref_sem)
    ref_copy.start()
    s_copies = []
    for n in range(COPIES):
        part = pl.ds(n * depth, depth)
        s_copies.append(pltpu.make_async_copy(s_hbm.at[part], s_ref.at[part], s_sem.at[n]))
        s_copies[n].start()
    half = SUBLANES // 2
    sub = lax.broadcasted_iota(jnp.int32, (SUBLANES, w_hbm.shape[2]), 0)
    top = sub < half
    w_copy.wait()
    rows = []
    for parity in range(2):
        for e in range(parity, chan_count, 2):
            base = (me ^ e) * beams_local
            for tile in range(beams_local // SUBLANES):
                start = pl.multiple_of(base + tile * SUBLANES, SUBLANES)
                wr = w_ref[0, pl.ds(start, SUBLANES), :]
                wi = w_ref[1, pl.ds(start, SUBLANES), :]
                wr_s = pltpu.roll(wr, half, 0)
                wi_s = pltpu.roll(wi, half, 0)
                first = [jnp.where(top, wr, wi_s), jnp.where(top, -wi, wr_s)]
                second = [jnp.where(top, wr_s, wi), jnp.where(top, -wi_s, wr)]
                rows.append(jnp.concatenate(first, 1))
                rows.append(jnp.concatenate(second, 1))
    weights = halves(jnp.concatenate(rows, 0))
    ref_copy.wait()
    for c in range(2):
        for n in range(tiles_ref.shape[1]):
            tiles_ref[c, n : n + 1, :] = ref_ref[c : c + 1, n * LANES : (n + 1) * LANES]
    for copy in s_copies:
        copy.wait()
    high, mid, low = thirds(s_ref[...])
    twice = jnp.concatenate([jnp.concatenate([part, part], 1) for part in weights], 0)
    product = jnp.dot(twice, jnp.concatenate([high, mid], 0), preferred_element_type=jnp.float32)
    least = jnp.dot(weights[0], low, preferred_element_type=jnp.float32)
    count = least.shape[0]
    product = product[:count] + (product[count:] + least)
    mid = product.shape[0] // 2
    kept_ref[...] = product[:mid]
    sent_ref[...] = product[mid:]


def beam_call(steering, survey, ref, chan_count, beams_local):
    depth, length = survey.shape
    rows = chan_count * beams_local
    tiles = (2, length // LANES, LANES)
    out = jax.ShapeDtypeStruct((rows, length), jnp.float32)
    hbm, vmem = pl.BlockSpec(memory_space=pltpu.HBM), pl.BlockSpec(memory_space=pltpu.VMEM)
    return pl.pallas_call(
        functools.partial(beam_kernel, chan_count, beams_local),
        in_specs=[hbm] * 3,
        out_specs=[vmem] * 3,
        out_shape=[
            out,
            out,
            jax.ShapeDtypeStruct(tiles, jnp.float32),
        ],
        scratch_shapes=[
            pltpu.VMEM(steering.shape, jnp.float32),
            pltpu.VMEM(survey.shape, jnp.float32),
            pltpu.VMEM(ref.shape, jnp.float32),
            pltpu.SemaphoreType.DMA,
            pltpu.SemaphoreType.DMA((COPIES,)),
            pltpu.SemaphoreType.DMA,
        ],
        compiler_params=params(),
        cost_estimate=cost(2.2),
        name="beams",
    )(*(pltpu.with_memory_space_constraint(x, pltpu.HBM) for x in (steering, survey, ref)))


def sum_kernel(count, *refs):
    kept_ref, sent_ref = refs[-2:]
    for n in range(kept_ref.shape[0]):
        for offset, out_ref in ((0, kept_ref), (1, sent_ref)):
            total = refs[0][2 * n + offset]
            for ref in refs[1:count]:
                total = total + ref[2 * n + offset]
            out_ref[n] = total


def sum_call(parts):
    shape = (parts[0].shape[0] // 2,) + parts[0].shape[1:]
    out = jax.ShapeDtypeStruct(shape, jnp.float32)
    vmem = pl.BlockSpec(memory_space=pltpu.VMEM)
    return pl.pallas_call(
        functools.partial(sum_kernel, len(parts)),
        in_specs=[vmem] * len(parts),
        out_specs=[vmem, vmem],
        out_shape=[out, out],
        compiler_params=params(),
        cost_estimate=cost(0.1),
        name="halves_summed",
    )(*parts)


def join_kernel(first_ref, second_ref, *refs):
    out_ref = refs[-1]
    count = first_ref.shape[0]
    out_ref[:count] = first_ref[...]
    out_ref[count:] = second_ref[...]


def join_call(first, second, *after):
    vmem = pl.BlockSpec(memory_space=pltpu.VMEM)
    return pl.pallas_call(
        join_kernel,
        in_specs=[vmem, vmem] + [pl.BlockSpec(memory_space=pl.ANY)] * len(after),
        out_shape=jax.ShapeDtypeStruct((2 * first.shape[0],) + first.shape[1:], jnp.float32),
        compiler_params=params(),
        cost_estimate=cost(1.0),
        name="reference_joined",
    )(first, second, *after)


def spread_line(line, keep):
    for g in range(0, LANES, 2 * SUBLANES):
        tiled = jnp.broadcast_to(line, (2 * SUBLANES, line.shape[1]))
        for h, value in enumerate(halves(pltpu.roll(tiled, g, 1, stride=1, stride_axis=0)[:, LANES:])):
            keep(h, g, value)


def table_kernel(tiles_ref, out_ref):
    for c in range(2):
        line = jnp.concatenate([tiles_ref[c, n : n + 1, :] for n in range(tiles_ref.shape[1])], 1)

        def keep(h, g, value):
            out_ref[h, c, g : g + 2 * SUBLANES] = value

        spread_line(line, keep)


def table_call(tiles):
    shape = (2, 2, LANES, LANES * (tiles.shape[1] - 1))
    return pl.pallas_call(
        table_kernel,
        out_shape=jax.ShapeDtypeStruct(shape, jnp.bfloat16),
        compiler_params=params(),
        cost_estimate=cost(0.7),
        name="shifted_reference",
    )(tiles)


def first_kernel(tiles_ref, *refs):
    *round_refs, out_ref = refs
    me = lax.axis_index("tm")
    for c in range(2):
        tails = [ref[ref.shape[0] - 1, c, ref.shape[2] - EDGE :, :] for ref in round_refs]
        before = jnp.where(me % 2 == 1, tails[0], jnp.where(me > 0, tails[-1], 0.0))
        line = jnp.concatenate([before[n : n + 1] for n in range(EDGE)] + [tiles_ref[c, 0:1, :]], 1)

        def keep(h, g, value):
            out_ref[h, c, g : g + 2 * SUBLANES] = value

        spread_line(line, keep)


def first_call(tiles, rounds):
    return pl.pallas_call(
        first_kernel,
        out_shape=jax.ShapeDtypeStruct((2, 2, LANES, 2 * LANES), jnp.bfloat16),
        compiler_params=params(),
        cost_estimate=cost(0.1),
        name="shifted_first",
    )(tiles, *rounds)


def lag_kernel(groups, part_count, *refs):
    y_refs, refs = refs[:part_count], refs[part_count:]
    table_ref, first_ref, _, out_hbm, out_ref, out_sem = refs
    copies = []

    def table_tile(h, n):
        parts = []
        for c in range(2):
            known = first_ref.shape[3] // LANES
            ref, at = (first_ref, n) if n < known else (table_ref, n - known)
            parts.append(ref[h, c, :, at * LANES : (at + 1) * LANES])
        return jnp.concatenate(parts, 1)

    def send(start, count):
        part = (slice(None), pl.ds(start, count))
        copies.append(pltpu.make_async_copy(out_ref.at[part], out_hbm.at[part], out_sem.at[len(copies)]))
        copies[-1].start()

    y = y_refs[0][...]
    for y_ref in y_refs[1:]:
        y = y + y_ref[...]
    rows, length = y.shape
    blocks = length // BLOCK_LEN
    turned = jnp.concatenate(
        [pltpu.roll(y[r : r + SUBLANES], SUBLANES // 2, 0) for r in range(0, rows, SUBLANES)], 0
    )
    turned = turned * row_sign(turned.shape)
    y_parts, t_parts = thirds(y), thirds(turned)

    def half_block(q, b):
        cols = slice(q * BLOCK_LEN + b * LANES, q * BLOCK_LEN + (b + 1) * LANES)
        return [jnp.concatenate([x[:, cols], t[:, cols]], 1) for x, t in zip(y_parts, t_parts)]

    def products(stack, n, count):
        tiles = [jnp.concatenate([table_tile(h, n + i) for i in range(count)], 0) for h in range(2)]
        product = dot_parts([jnp.concatenate(part, 0) for part in zip(*stack)], tiles, True)
        return [product[i * rows : (i + 1) * rows] for i in range(len(stack))]

    taps_sum = None
    (far,) = products([half_block(0, 0)], 0, 1)
    for q in range(blocks):
        stack = [half_block(q, 0), half_block(q, 1)]
        if q + 1 < blocks:
            stack.append(half_block(q + 1, 0))
        first, second, *after = products(stack, 2 * q + 1, 2)
        product = jnp.concatenate([first[:, :LANES] + second[:, LANES:], second[:, :LANES] + far], 1)
        if after:
            far = after[0][:, LANES:]
        taps = product[:, :LANES]
        taps_sum = taps if taps_sum is None else taps_sum + taps
        for h in range(LAGS // LANES):
            lanes = slice(h * LANES, (h + 1) * LANES)
            tiles = [product[r : r + SUBLANES, lanes] for r in range(0, rows, SUBLANES)]
            for j, tile in enumerate(swap_groups(tiles, groups)):
                out_ref[h * groups + j, q] = tile
        if q + 1 == blocks // 2:
            send(0, blocks // 2)
    left = lax.broadcasted_iota(jnp.int32, (SUBLANES, LANES), 1) < TAPS
    for i in range(groups // 2):
        a = taps_sum[i * SUBLANES : (i + 1) * SUBLANES]
        other = i + groups // 2
        b = taps_sum[other * SUBLANES : (other + 1) * SUBLANES]
        tile = jnp.where(left, a, pltpu.roll(b, LANES - TAPS, 1))
        for owner in range(out_ref.shape[0]):
            out_ref[owner, blocks + i] = tile
    send(blocks // 2, blocks - blocks // 2 + groups // 2)
    for copy in copies:
        copy.wait()


def lag_call(ys, table, first, after, groups, owners):
    blocks = ys[0].shape[1] // BLOCK_LEN
    shape = (owners, blocks + groups // 2, SUBLANES, LANES)
    vmem = pl.BlockSpec(memory_space=pltpu.VMEM)
    return pl.pallas_call(
        functools.partial(lag_kernel, groups, len(ys)),
        in_specs=[vmem] * (len(ys) + 2) + [pl.BlockSpec(memory_space=pl.ANY)],
        out_specs=pl.BlockSpec(memory_space=pltpu.HBM),
        out_shape=jax.ShapeDtypeStruct(shape, jnp.float32),
        scratch_shapes=[
            pltpu.VMEM(shape, jnp.float32),
            pltpu.SemaphoreType.DMA((2,)),
        ],
        compiler_params=params(),
        cost_estimate=cost(2.1),
        name="lag_products",
    )(*ys, table, first, after)


BATCH = 4


def own_kernel(lags_local, *refs):
    *part_refs, _, out_ref, line_ref, tail_ref, span_ref, late_ref, taps_a, lags_a, taps_b, lags_b = refs
    me = lax.axis_index("tm")
    part_rows = part_refs[0].shape[2]
    owners = sum(part_ref.shape[0] for part_ref in part_refs)
    samples = owners * part_rows * LANES
    steps = samples // BLOCK_LEN // BATCH
    total_rows = span_ref.shape[1]
    block_rows = BLOCK_LEN // LANES

    span_ref[...] = jnp.zeros_like(span_ref)
    n = 0
    for part_ref in part_refs:
        for i in range(part_ref.shape[0]):
            block = lax.rem(me - (n // 2) * 2 + owners, owners) ^ (n % 2)
            span_ref[:, pl.ds(EDGE + block * part_rows, part_rows), :] = part_ref[i]
            n += 1
    late_rows = (me * lags_local) // LANES
    late_lanes = lax.rem(me * lags_local, LANES)
    turned = [pltpu.roll(span_ref[c], late_lanes, 1) for c in range(2)]
    before = [pltpu.roll(x, 1, 0) for x in turned]
    lanes = lax.broadcasted_iota(jnp.int32, (total_rows, LANES), 1)
    for c in range(2):
        late_ref[c] = pltpu.roll(jnp.where(lanes < late_lanes, before[c], turned[c]), late_rows, 0)

    def line_of(ref, c, first, count):
        return jnp.concatenate([ref[c, pl.ds(first + n, 1), :] for n in range(count)], 1)

    def shifted(line, by):
        tiled = jnp.broadcast_to(line, (2 * SUBLANES, line.shape[1]))
        return pltpu.roll(tiled, by, 1, stride=1, stride_axis=0)[:, LANES:]

    def keep(ref, row, parts):
        step = ref.shape[0] // len(parts)
        for n, part in enumerate(parts):
            ref[n * step + row : n * step + row + 2 * SUBLANES, :] = part

    def build(n, taps_ref, lags_ref):
        first = EDGE - 1 + n * BATCH * block_rows
        count = BATCH * block_rows + 1
        lines = [line_of(span_ref, c, first, count) for c in range(2)]
        for c in range(2):
            for g in range(0, TAPS, 2 * SUBLANES):
                keep(taps_ref, c * TAPS + g, thirds(shifted(lines[c], g)))
            late = line_of(late_ref, c, first, count)
            for g in range(0, lags_local, 2 * SUBLANES):
                keep(lags_ref, c * lags_local + g, halves(shifted(late, g)))
        pad = jnp.zeros((2 * SUBLANES - 2, BATCH * BLOCK_LEN), jnp.float32)
        keep(lags_ref, 2 * lags_local, halves(jnp.concatenate([line[:, LANES:] for line in lines] + [pad], 0)))

    turn = lane_sign((lags_local, LANES))

    def use(n, taps_ref, lags_ref):
        count = lags_ref.shape[0] // 2
        for b in range(BATCH):
            cols = slice(b * BLOCK_LEN, (b + 1) * BLOCK_LEN)
            product = dot_nt(lags_ref[:, cols], taps_ref[: 2 * LANES, cols])
            least = dot_nt(lags_ref[:count, cols], taps_ref[2 * LANES :, cols]) + product[count:, LANES:]
            product = product[:count, :LANES] + ((product[:count, LANES:] + product[count:, :LANES]) + least)
            by_real = product[:lags_local]
            by_imag = product[lags_local : 2 * lags_local]
            rows = pl.ds(pl.multiple_of((n * BATCH + b) * lags_local, lags_local), lags_local)
            for part, value in enumerate(thirds(by_real + turn * pltpu.roll(by_imag, TAPS, 1))):
                out_ref[part, rows, :] = value
            line_ref[...] += product[2 * lags_local : 2 * lags_local + SUBLANES]

    line_ref[...] = jnp.zeros_like(line_ref)
    build(0, taps_a, lags_a)

    def pair(m, carry):
        build(2 * m + 1, taps_b, lags_b)
        use(2 * m, taps_a, lags_a)
        build(jnp.minimum(2 * m + 2, steps - 1), taps_a, lags_a)
        use(2 * m + 1, taps_b, lags_b)
        return carry

    lax.fori_loop(0, steps // 2, pair, 0)
    tail = []
    for c in range(2):
        line = line_of(span_ref, c, EDGE + owners * part_rows - 1, 2)
        tail += [shifted(line, g) for g in range(0, TAPS, 2 * SUBLANES)]
    tail = jnp.concatenate(tail, 0)
    tail_ref[...] = dot_nt(tail, tail, HIGHEST)


def own_call(parts, lags_local, after):
    part_rows = parts[0].shape[2]
    span_rows = part_rows * sum(part.shape[0] for part in parts)
    rows = span_rows * LANES // BLOCK_LEN * lags_local
    held_rows = -(-(span_rows + 2 * EDGE) // SUBLANES) * SUBLANES
    width = BATCH * BLOCK_LEN
    taps = pltpu.VMEM((6 * TAPS, width), jnp.bfloat16)
    lags = pltpu.VMEM((4 * lags_local + 4 * SUBLANES, width), jnp.bfloat16)
    span = pltpu.VMEM((2, held_rows, LANES), jnp.float32)
    return pl.pallas_call(
        functools.partial(own_kernel, lags_local),
        in_specs=[pl.BlockSpec(memory_space=pltpu.VMEM)] * len(parts) + [pl.BlockSpec(memory_space=pl.ANY)],
        out_shape=[
            jax.ShapeDtypeStruct((3, rows, 2 * TAPS), jnp.bfloat16),
            jax.ShapeDtypeStruct((SUBLANES, 2 * TAPS), jnp.float32),
            jax.ShapeDtypeStruct((2 * TAPS, 2 * TAPS), jnp.float32),
        ],
        scratch_shapes=[span, span, taps, lags, taps, lags],
        compiler_params=params(),
        cost_estimate=cost(6.2),
        name="reference_products",
    )(*parts, after)


def as_factor(a):
    return jnp.concatenate([a, -lane_sign(a.shape) * pltpu.roll(a, a.shape[0], 1)], 0)


def solver_kernel(line_ref, tail_ref, gram_ref, solver_ref):
    total = line_ref[...]
    line = total[0:1] + lane_sign((1, LANES)) * pltpu.roll(total[1:2], TAPS, 1)
    low = lax.broadcasted_iota(jnp.int32, (1, LANES), 1) < TAPS
    line_r = jnp.where(low, line, 0.0)
    line_i = jnp.where(low, pltpu.roll(line, TAPS, 1), 0.0)
    cols = lax.broadcasted_iota(jnp.int32, (TAPS, TAPS), 1)
    rows = lax.broadcasted_iota(jnp.int32, (TAPS, TAPS), 0)
    above = cols > rows

    def stack(ref, value):
        parts = thirds(value)
        for n, (_, part) in enumerate(PART_PAIRS):
            ref[n * value.shape[0] : (n + 1) * value.shape[0], :] = parts[part]

    def upper(x):
        spread = pltpu.roll(jnp.broadcast_to(x, (TAPS, LANES)), 0, 1, stride=1, stride_axis=0)
        return spread[:, :TAPS]

    up_r = upper(line_r)
    up_i = jnp.where(above, upper(line_i), 0.0)
    strict_r = jnp.where(above, up_r, 0.0)
    diag_r = jnp.where(cols == rows, up_r, 0.0)
    tails = tail_ref[...]
    gram_r = strict_r + strict_r.T + diag_r - (tails[:TAPS, :TAPS] + tails[TAPS:, TAPS:])
    gram_i = up_i - up_i.T - (tails[:TAPS, TAPS:] - tails[TAPS:, :TAPS])
    gram = jnp.concatenate([gram_r, gram_i], 1)
    gram_factor = as_factor(gram)
    stack(gram_ref, gram_factor)
    gram_halves = halves(gram_factor)
    one = (
        lax.broadcasted_iota(jnp.int32, gram.shape, 0) == lax.broadcasted_iota(jnp.int32, gram.shape, 1)
    ).astype(jnp.float32)
    bound = jnp.max(jnp.sum(jnp.abs(gram), axis=1, keepdims=True), axis=0, keepdims=True)

    def again(state):
        count, left, _ = state
        return (count < 60) & (left > 1e-3)

    def newton(state):
        count, _, x = state
        x_halves = halves(x)
        seen = dot_split(x_halves, gram_halves)
        left = jnp.max(jnp.abs(seen - one))
        x = 2.0 * x - dot_split(halves(seen), halves(as_factor(x)))
        return count + 1, left, x

    start = (jnp.int32(0), jnp.float32(1.0), one * (1.0 / bound))
    _, _, inverse = lax.while_loop(again, newton, start)
    seen = jnp.dot(inverse, gram_factor, precision=HIGHEST, preferred_element_type=jnp.float32)
    inverse = inverse + jnp.dot(
        one - seen, as_factor(inverse), precision=HIGHEST, preferred_element_type=jnp.float32
    )
    stack(solver_ref, as_factor(inverse))


def solver_call(line, tail):
    return pl.pallas_call(
        solver_kernel,
        out_shape=[jax.ShapeDtypeStruct((len(PART_PAIRS) * tail.shape[0], tail.shape[1]), jnp.bfloat16)] * 2,
        compiler_params=params(),
        cost_estimate=cost(2.0),
        name="gram_inverse",
    )(line, tail)


def doppler_table(block_count, scale):
    phase = (np.arange(block_count)[:, None] * np.arange(DOPPLER)[None, :] % DOPPLER) * (2.0 * math.pi / DOPPLER)
    cosine, sine = np.cos(phase), np.sin(phase)
    upper = np.concatenate([cosine, -sine], 1)
    lower = np.concatenate([sine, cosine], 1)
    return (np.concatenate([upper, lower], 0) * scale).astype(np.float32)


def map_kernel(groups, got_ref, own_ref, gram_ref, solver_ref, wave_ref, out_hbm, held_ref, out_ref, out_sem):
    owners, pieces = got_ref.shape[:2]
    blocks = pieces - groups // 2
    lags_local = LANES // groups
    total = owners * blocks
    left = lax.broadcasted_iota(jnp.int32, (SUBLANES, LANES), 1) < TAPS
    sign = row_sign((SUBLANES, LANES))
    rows = [None] * groups
    for i in range(groups // 2):
        tile = got_ref[0, blocks + i]
        for owner in range(1, owners):
            tile = tile + got_ref[owner, blocks + i]
        swapped = pltpu.roll(tile, TAPS, 1)
        for part, here, there in ((i, tile, swapped), (i + groups // 2, swapped, tile)):
            other = -sign * pltpu.roll(there, SUBLANES // 2, 0)
            rows[part] = jnp.where(left, here, other)
    cross = jnp.concatenate(rows, 0)

    def exact(x, ref):
        parts = thirds(x)
        return jnp.dot(
            jnp.concatenate([parts[part] for part, _ in PART_PAIRS], 1), ref[...], preferred_element_type=jnp.float32
        )

    taps = exact(cross, solver_ref)
    taps = taps + exact(cross - exact(taps, gram_ref), solver_ref)
    taps = thirds(taps)
    count = taps[0].shape[0]
    twice = [jnp.concatenate([part, part], 1) for part in taps[:2]]
    twice = jnp.concatenate(twice + [jnp.concatenate([taps[2], jnp.zeros_like(taps[2])], 1)], 0)
    for q in range(0, total, 2 * groups):
        own = slice(q * lags_local, (q + 2 * groups) * lags_local)
        by_part = dot_nt(twice, jnp.concatenate([own_ref[0, own, :], own_ref[1, own, :]], 1))
        least = by_part[2 * count :] + dot_nt(taps[0], own_ref[2, own, :])
        clutter = by_part[:count] + (by_part[count : 2 * count] + least)
        for h in range(2):
            lanes = slice(h * LANES, (h + 1) * LANES)
            tiles = [clutter[r : r + SUBLANES, lanes] for r in range(0, groups * SUBLANES, SUBLANES)]
            for j, tile in enumerate(swap_groups(tiles, groups)):
                at = q + h * groups + j
                held_ref[at * SUBLANES : (at + 1) * SUBLANES, :] = got_ref[at // blocks, at % blocks] - tile
    half = SUBLANES // 2
    copies = []
    for g in range(half):
        parts = [held_ref[pl.ds(c * half + g, total, stride=SUBLANES), :] for c in range(2)]
        high, low = halves(jnp.concatenate(parts, 0).T)
        left_rows = [jnp.concatenate([high, high], 1), jnp.concatenate([low, jnp.zeros_like(low)], 1)]
        by_part = jnp.dot(jnp.concatenate(left_rows, 0), wave_ref[...], preferred_element_type=jnp.float32)
        spectrum = by_part[:LANES] + by_part[LANES:]
        for i in range(groups):
            for c in range(2):
                out_ref[i, g, c] = spectrum[i * lags_local : (i + 1) * lags_local, c * DOPPLER : (c + 1) * DOPPLER]
        part = (slice(None), pl.ds(g, 1))
        copies.append(pltpu.make_async_copy(out_ref.at[part], out_hbm.at[part], out_sem.at[g]))
        copies[-1].start()
    for copy in copies:
        copy.wait()


def map_call(got, own, gram, solver, wave, groups, beams_local):
    total = got.shape[0] * (got.shape[1] - groups // 2)
    lags_local = LANES // groups
    half = SUBLANES // 2
    shape = (beams_local // half, half, 2, lags_local, DOPPLER)
    out = pl.pallas_call(
        functools.partial(map_kernel, groups),
        in_specs=[pl.BlockSpec(memory_space=pltpu.VMEM)] * 5,
        out_specs=pl.BlockSpec(memory_space=pltpu.HBM),
        out_shape=jax.ShapeDtypeStruct(shape, jnp.float32),
        scratch_shapes=[
            pltpu.VMEM((total * SUBLANES, LANES), jnp.float32),
            pltpu.VMEM(shape, jnp.float32),
            pltpu.SemaphoreType.DMA((half,)),
        ],
        compiler_params=params(),
        cost_estimate=cost(2.5),
        name="range_doppler",
    )(got, own, gram, solver, wave)
    return out.reshape((beams_local,) + shape[2:])


def swap(x, axis, by):
    pairs = [(i, i ^ by) for i in range(lax.axis_size(axis))]
    return lax.ppermute(x, axis, pairs)


def tiled_device(ref_signal, surveillance, steering):
    chan_count, tm_count = lax.axis_size("chan"), lax.axis_size("tm")
    channels, length = surveillance.shape[1:]
    beams_local = steering.shape[1] // chan_count
    lags_local = LAGS // tm_count
    groups = LANES // lags_local
    samples = length * tm_count

    survey = surveillance.reshape(2 * channels, length)
    kept, moved, tiles = beam_call(steering, survey, ref_signal, chan_count, beams_local)
    near = swap(tiles[None], "tm", 1)
    shape = (chan_count // 2, 2 * beams_local, length)
    kept, got = kept.reshape(shape), swap(moved, "chan", 1).reshape(shape)
    by = 2
    while by < chan_count:
        kept, moved = sum_call([kept, got])
        got = swap(moved, "chan", by)
        by *= 2
    rounds = [near]
    joined = join_call(tiles[None], near, moved)
    while True:
        count = joined.shape[0]
        rounds.append(lax.ppermute(joined, "tm", [(i, (i + count) % tm_count) for i in range(tm_count)]))
        if count * 2 == tm_count:
            break
        joined = join_call(joined, rounds[-1])
    table = table_call(tiles)
    first = first_call(tiles, rounds[:2])
    pieces = lag_call([kept[0], got[0]], table, first, joined, groups, tm_count)
    got = lax.all_to_all(pieces, "tm", 0, 0, tiled=True)
    own, line, tail = own_call([tiles[None]] + rounds, lags_local, pieces)
    gram, solver = solver_call(line, tail)
    wave = doppler_table(samples // BLOCK_LEN, 0.125 / math.sqrt(samples))
    high = wave.astype(jnp.bfloat16)
    wave = np.concatenate([high, (wave - high.astype(np.float32)).astype(jnp.bfloat16)], 0)
    return map_call(got, own, gram, solver, jnp.asarray(wave), groups, beams_local)


def lag_table(ref_ext, offset, lags):
    window = lax.dynamic_slice_in_dim(ref_ext, offset, BLOCK_LEN + LAGS, 1)
    span = BLOCK_LEN + LAGS
    tiled = jnp.tile(jnp.pad(window, ((0, 0), (0, 1))), (1, lags))[:, : lags * span]
    return tiled.reshape(2, lags, span)[:, :, LAGS:]


def times_conj(a, b):
    real = jnp.einsum("...t,lt->...l", a[..., 0, :], b[0], precision=HIGHEST) + jnp.einsum(
        "...t,lt->...l", a[..., 1, :], b[1], precision=HIGHEST
    )
    imag = jnp.einsum("...t,lt->...l", a[..., 1, :], b[0], precision=HIGHEST) - jnp.einsum(
        "...t,lt->...l", a[..., 0, :], b[1], precision=HIGHEST
    )
    return jnp.stack([real, imag], -2)


def plain_device(ref_signal, surveillance, steering):
    chan_count, tm_count = lax.axis_size("chan"), lax.axis_size("tm")
    length = surveillance.shape[2]
    beams = steering.shape[1]
    lags_local = LAGS // tm_count
    samples = length * tm_count
    local_blocks = length // BLOCK_LEN
    here = lax.axis_index("tm")

    w_real, w_imag = steering
    real = jnp.dot(w_real, surveillance[0], precision=HIGHEST) - jnp.dot(w_imag, surveillance[1], precision=HIGHEST)
    imag = jnp.dot(w_imag, surveillance[0], precision=HIGHEST) + jnp.dot(w_real, surveillance[1], precision=HIGHEST)
    beam = lax.psum_scatter(jnp.stack([real, imag], 1), "chan", scatter_dimension=0, tiled=True)
    ref_all = lax.all_gather(ref_signal, "tm", axis=1, tiled=True)
    ref_ext = jnp.pad(ref_all, ((0, 0), (LAGS, 0)))

    def beam_step(carry, q):
        offset = q * BLOCK_LEN
        table = lag_table(ref_ext, here * length + offset, LAGS)
        segment = lax.dynamic_slice_in_dim(beam, offset, BLOCK_LEN, 2)
        return carry, times_conj(segment, table)

    _, products = lax.scan(beam_step, None, jnp.arange(local_blocks, dtype=jnp.int32))
    cross = lax.psum(products[..., :TAPS].sum(0), "tm")
    got = lax.all_to_all(products, "tm", 3, 0, tiled=True)

    def own_step(gram, q):
        offset = q * BLOCK_LEN
        table = lag_table(ref_ext, offset, LAGS)
        taps = table[:, :TAPS].transpose(1, 0, 2)
        mine = lax.dynamic_slice_in_dim(table, here * lags_local, lags_local, 1)
        return gram + times_conj(taps, table[:, :TAPS]), times_conj(taps, mine)

    start = jnp.zeros((TAPS, 2, TAPS), jnp.float32)
    gram, own = lax.scan(own_step, start, jnp.arange(samples // BLOCK_LEN, dtype=jnp.int32))
    g_real, g_imag = gram[:, 0].T, gram[:, 1].T
    system = jnp.concatenate([jnp.concatenate([g_real, -g_imag], 1), jnp.concatenate([g_imag, g_real], 1)], 0)
    right = jnp.concatenate([cross[:, 0].T, cross[:, 1].T], 0)
    solved = jax.scipy.linalg.cho_solve((jnp.linalg.cholesky(system), True), right)
    b_real, b_imag = solved[:TAPS].T, solved[TAPS:].T
    mixing = jnp.concatenate([jnp.stack([b_real, b_imag], 1), jnp.stack([-b_imag, b_real], 1)], 2)
    stacked = jnp.concatenate([own[:, :, 0], own[:, :, 1]], 1)
    lagged = got - jnp.einsum("mck,qkl->qmcl", mixing, stacked, precision=HIGHEST)
    wave = jnp.asarray(doppler_table(samples // BLOCK_LEN, 0.125 / math.sqrt(samples)))
    wave = wave.reshape(2, samples // BLOCK_LEN, 2, DOPPLER)
    return jnp.einsum("qmcl,cqdk->mdlk", lagged, wave, precision=HIGHEST)


def on_device(ref_signal, surveillance, steering):
    chan_count, tm_count = lax.axis_size("chan"), lax.axis_size("tm")
    beams_local = steering.shape[1] // chan_count
    lags_local = LAGS // tm_count
    fills = (
        LANES % lags_local == 0
        and lags_local % (2 * SUBLANES) == 0
        and beams_local * lags_local == LANES * SUBLANES // 2
        and chan_count > 1
        and chan_count & (chan_count - 1) == 0
        and tm_count > 2
        and tm_count & (tm_count - 1) == 0
        and 2 * surveillance.shape[1] % LANES == 0
        and surveillance.shape[2] % (2 * BATCH * BLOCK_LEN) == 0
    )
    device = tiled_device if fills else plain_device
    return device(ref_signal, surveillance, steering)


def solution(mesh):
    placed = (P(None, "tm"), P(None, "chan", "tm"), P(None, None, "chan"))
    return jax.shard_map(
        on_device,
        mesh=mesh,
        in_specs=placed,
        out_specs=P("chan", None, "tm", None),
        check_vma=False,
    )
```
